32 devices in a mesh: dp: 32 (over z, y, x, core).
Axes of the slice: x: 2, y: 2, z: 4, core: 2. Of those that a mesh axis runs over, the one named last changes fastest.
Arguments:
- word_states: bfloat16 [16384, 768], P('dp'), may hold values from -6 to 6
- word_segments: int32 [32, 512], P('dp'), may hold values from 0 to 3, never falling along the last dimension, each value on 1 to 384 neighbouring positions
- entity_segments: int32 [32, 128], P('dp'), may hold values from 0 to 3, never falling along the last dimension, each value on 1 to 96 neighbouring positions
- request_rows: int32 [1024, 10], P('dp'), may hold values from 0 to 3967
- request_slot: int32 [1024, 10], P('dp'), may hold values from 0 to 160, as said below
- mask_slots: int32 [32, 32], P('dp'), may hold values from 0 to 127, as said below
- entity_table: bfloat16 [126976, 256], P('dp'), may hold values from -0.75 to 0.75
- vocab_bias: bfloat16 [126976], P('dp'), may hold values from 71 to 89
- entity_dense: bfloat16 [256, 768], replicated, may hold values from -3 to 3
- query_ww: bfloat16 [768, 768], replicated, may hold values from -0.21875 to 0.21875
- query_we: bfloat16 [768, 768], replicated, may hold values from -0.21875 to 0.21875
- query_ew: bfloat16 [768, 768], replicated, may hold values from -0.21875 to 0.21875
- query_ee: bfloat16 [768, 768], replicated, may hold values from -0.21875 to 0.21875
- key_weight: bfloat16 [768, 768], replicated, may hold values from -0.21875 to 0.21875
- value_weight: bfloat16 [768, 768], replicated, may hold values from -0.21875 to 0.21875
- out_weight: bfloat16 [768, 768], replicated, may hold values from -2 to 2
- norm1_gain: float32 [768], replicated, may hold values from 0.25 to 1.75
- norm1_bias: float32 [768], replicated, may hold values from -1.8 to 1.8
- up_weight: bfloat16 [768, 3072], replicated, may hold values from -0.21875 to 0.21875
- down_weight: bfloat16 [3072, 768], replicated, may hold values from -0.21875 to 0.21875
- norm2_gain: float32 [768], replicated, may hold values from 0.25 to 1.75
- norm2_bias: float32 [768], replicated, may hold values from -1.8 to 1.8
- head_weight: bfloat16 [768, 256], replicated, may hold values from -0.21875 to 0.21875
- head_gain: float32 [256], replicated, may hold values from 0.25 to 1.75
- head_bias: float32 [256], replicated, may hold values from -1.8 to 1.8
- cotangent: bfloat16 [20480, 768], P('dp'), may hold values from -2.9206276e-05 to 2.9206276e-05
Outputs:
- loss: float32 [], replicated
- layer_out: bfloat16 [20480, 768], P('dp')
- grad_words: bfloat16 [16384, 768], P('dp')
- grad_table: float32 [126976, 256], P('dp')
- grad_vocab_bias: float32 [126976], P('dp')
- grad_entity_dense: float32 [256, 768], P('dp')
- grad_query_ww: float32 [768, 768], P('dp')
- grad_query_we: float32 [768, 768], P('dp')
- grad_query_ew: float32 [768, 768], P('dp')
- grad_query_ee: float32 [768, 768], P('dp')
- grad_key: float32 [768, 768], P('dp')
- grad_value: float32 [768, 768], P('dp')
- grad_out: float32 [768, 768], P('dp')
- grad_norm1_gain: float32 [768], P('dp')
- grad_norm1_bias: float32 [768], P('dp')
- grad_up: float32 [768, 3072], P('dp')
- grad_down: float32 [3072, 768], P('dp')
- grad_norm2_gain: float32 [768], P('dp')
- grad_norm2_bias: float32 [768], P('dp')
- grad_head_weight: float32 [768, 256], P('dp')
- grad_head_gain: float32 [256], P('dp')
- grad_head_bias: float32 [256], P('dp')
- mask_loss: float32 [1024], P('dp')
The draws below stay inside these ranges and needn't reach their ends.
Inputs may be any that keep to these rules, and one draw needn't show every extreme that they name: `request_slot`: row block s * 32 + o holds the entries that sequence s sends to owner o: each request number below 160 appears exactly once among a sequence's entries, 160 marks an empty entry; some owner receives 10 requests from every sequence. `request_rows`: rows of empty entries are ignored. `mask_slots`: distinct within a sequence. `word_segments`: never falling along a sequence; every document 0 to 3 has words, one has exactly 384. `entity_segments`: never falling along a sequence; every document 0 to 3 has entity slots, one has exactly 96.
All inputs are finite; a program needn't handle non-finite values.
Results may differ from the reference program's by a relative error of at most 0.029.
Values may be sent and summed in bfloat16 or wider, within the bound.
A program may use at most 192 MiB of HBM per device.

```python
import math
import jax
import jax.numpy as jnp
import numpy as np
from jax import lax

D = 768
HD = 64
FF = 3072
EW = 256
ENT_DEV = 3968
WORDS = 512
ENT_SLOTS = 128
N_MASK = 32
NSEG = 4
SEQ = 640
REQ = 160
CAP = 10
M_ALL = 1024
WMOST = 384
EMOST = 96
TOKW = 16384
TOKS = 20480
ENT_ROWS = 126976
N_DP = 32


def draw_request_slot(key, part):
    total_slots = N_DP * CAP
    common = jax.random.randint(jax.random.fold_in(key, 11), (), 0, N_DP)

    def one_device(device):
        device_key = jax.random.fold_in(key, device)
        own_owner = jax.random.randint(jax.random.fold_in(device_key, 1), (), 0, N_DP)
        order_score = jax.random.permutation(jax.random.fold_in(device_key, 2), total_slots).astype(jnp.int32)
        owner_of = jnp.arange(total_slots, dtype=jnp.int32) // CAP
        forced = (owner_of == common) | (owner_of == own_owner)
        order_score = jnp.where(forced, order_score - total_slots, order_score)
        order_pos = jnp.argsort(order_score, stable=True)
        rank_of = jnp.argsort(order_pos, stable=True).astype(jnp.int32)
        slot_order = jax.random.permutation(jax.random.fold_in(device_key, 3), REQ).astype(jnp.int32)
        live_mask = rank_of < REQ
        return jnp.where(live_mask, slot_order[jnp.minimum(rank_of, REQ - 1)], REQ).astype(jnp.int32)
    return jax.vmap(one_device)(jnp.arange(N_DP, dtype=jnp.int32)).reshape(N_DP * N_DP, CAP)


def draw_mask_slots(key, part):

    def pick_slots(device):
        return jax.random.permutation(jax.random.fold_in(key, device), ENT_SLOTS)[:N_MASK].astype(jnp.int32)
    return jax.vmap(pick_slots)(jnp.arange(N_DP, dtype=jnp.int32))


def draw_vocab_bias(key, part):
    key = jax.random.fold_in(key, 29)
    spread = 2.0 * jnp.clip(jax.random.normal(key, (ENT_ROWS,), jnp.float32), -4.5, 4.5)
    return (80.0 + spread).astype(jnp.bfloat16)


def touch_ends(entries, key, least, high):
    longest = entries.shape.index(max(entries.shape))
    spots = []
    for shift in (0, 1):
        where = [jax.random.randint(jax.random.fold_in(key, axis), (), 0, length) for axis, length in enumerate(entries.shape)]
        where[longest] = (where[longest] + shift) % entries.shape[longest]
        spots.append(tuple(where))
    return entries.at[spots[0]].set(least).at[spots[1]].set(high)


def level_of(own_key, dims, pieces, least, high):
    def one(dim, blocks):
        heights = jax.random.uniform(jax.random.fold_in(jax.random.fold_in(own_key, 6), dim), (blocks,), jnp.float32, least / len(pieces), high / len(pieces))
        return jnp.repeat(jnp.exp(heights), dims[dim] // blocks).reshape((-1,) + (1,) * (len(dims) - dim - 1))

    factor_of = one(*pieces[0])
    for cut in pieces[1:]:
        factor_of = factor_of * one(*cut)
    return factor_of


def split_up(number_of, total, reach, skew):
    portions = [(1 << 20) // math.isqrt(standing ** skew) + 1 for standing in range(2, number_of + 1)]
    rest, holding = total - reach - (number_of - 1), [1] * (number_of - 1)
    while rest > 0:
        candidates = [i for i in range(number_of - 1) if holding[i] < reach]
        pool, budget = sum([portions[i] for i in candidates]), rest
        for i in candidates:
            addition = min(reach - holding[i], max(1, budget * portions[i] // pool), rest)
            holding[i] = holding[i] + addition
            rest = rest - addition
    return np.array([reach] + holding)


def ragged_sizes(rng, amount, total, reach, skew):
    if amount == 2:
        one = jax.random.randint(rng, (), max(1, total - reach), min(reach, total - 1) + 1)
        return jnp.stack([one, total - one])
    lengths = jnp.asarray(split_up(amount, total, reach, skew), jnp.int32)
    pairs = (amount - 1) // 2
    giver, sink = lengths[1:1 + 2 * pairs:2], lengths[2:2 + 2 * pairs:2]
    room = jnp.minimum(giver - 1, reach - sink)
    shifted = jax.random.randint(jax.random.fold_in(rng, 1), (pairs,), 0, 1 << 20) % (room + 1)
    lengths = lengths.at[1:1 + 2 * pairs:2].set(giver - shifted).at[2:2 + 2 * pairs:2].set(sink + shifted)
    return lengths[jax.random.permutation(jax.random.fold_in(rng, 2), amount)]


def centred(stream_key, extent, width, limit, cuts=(), kind=jnp.bfloat16):
    values = jax.random.normal(stream_key, extent, jnp.float32) * width
    if len(cuts) > 0:
        values = level_of(stream_key, extent, cuts, -0.22, 0.18) * values
    return jnp.clip(values, min=-limit, max=limit).astype(kind)


def setup_inputs(seed: int = 0) -> dict:
    arg_keys = jax.random.split(jax.random.key(seed), 27)
    word_states = centred(arg_keys[0], (TOKW, D), 1.0, 6.0, ((0, 32),))
    word_segments = jax.vmap(lambda own: jnp.searchsorted(jnp.cumsum(ragged_sizes(own, NSEG, WORDS, WMOST, 1)), jnp.arange(WORDS), side="right"))(jax.random.split(arg_keys[1], N_DP)).reshape((N_DP, WORDS)).astype(jnp.int32)
    entity_segments = jax.vmap(lambda own: jnp.searchsorted(jnp.cumsum(ragged_sizes(own, NSEG, ENT_SLOTS, EMOST, 1)), jnp.arange(ENT_SLOTS), side="right"))(jax.random.split(arg_keys[2], N_DP)).reshape((N_DP, ENT_SLOTS)).astype(jnp.int32)
    request_rows = touch_ends(jax.random.randint(arg_keys[3], (N_DP * N_DP, CAP), 0, ENT_DEV), jax.random.fold_in(arg_keys[3], 1), 0, ENT_DEV - 1).astype(jnp.int32)
    request_slot = draw_request_slot(jax.random.fold_in(arg_keys[26], 71), 0)
    mask_slots = draw_mask_slots(jax.random.fold_in(arg_keys[26], 71), 0)
    entity_table = centred(arg_keys[6], (ENT_ROWS, EW), 0.125, 0.75, ((0, 32),))
    vocab_bias = draw_vocab_bias(jax.random.fold_in(arg_keys[26], 71), 0)
    entity_dense = centred(arg_keys[8], (EW, D), (EW // 64) ** -0.5, 3.0)
    query_ww = centred(arg_keys[9], (D, D), D ** -0.5, 0.21875)
    query_we = centred(arg_keys[10], (D, D), D ** -0.5, 0.21875)
    query_ew = centred(arg_keys[11], (D, D), D ** -0.5, 0.21875)
    query_ee = centred(arg_keys[12], (D, D), D ** -0.5, 0.21875)
    key_weight = centred(arg_keys[13], (D, D), D ** -0.5, 0.21875)
    value_weight = centred(arg_keys[14], (D, D), D ** -0.5, 0.21875)
    out_weight = centred(arg_keys[15], (D, D), (max(1, D // 96)) ** -0.5, 2.0)
    norm1_gain = jnp.clip(1.0 + 0.15 * jax.random.normal(arg_keys[16], (D,), jnp.float32), 0.25, 1.75)
    norm1_bias = centred(arg_keys[17], (D,), 0.3, 1.8, (), jnp.float32)
    up_weight = centred(arg_keys[18], (D, FF), D ** -0.5, 0.21875)
    down_weight = centred(arg_keys[19], (FF, D), (FF // 4) ** -0.5, 0.21875)
    norm2_gain = jnp.clip(1.0 + 0.15 * jax.random.normal(arg_keys[20], (D,), jnp.float32), 0.25, 1.75)
    norm2_bias = centred(arg_keys[21], (D,), 0.3, 1.8, (), jnp.float32)
    head_weight = centred(arg_keys[22], (D, EW), D ** -0.5, 0.21875)
    head_gain = jnp.clip(1.0 + 0.15 * jax.random.normal(arg_keys[23], (EW,), jnp.float32), 0.25, 1.75)
    head_bias = centred(arg_keys[24], (EW,), 0.3, 1.8, (), jnp.float32)
    cotangent = centred(arg_keys[25], (TOKS, D), (0.005 * M_ALL ** -1), 2.9206275939941406e-05, ((0, 32),))
    return {"word_states": word_states, "word_segments": word_segments, "entity_segments": entity_segments, "request_rows": request_rows, "request_slot": request_slot, "mask_slots": mask_slots, "entity_table": entity_table, "vocab_bias": vocab_bias, "entity_dense": entity_dense, "query_ww": query_ww, "query_we": query_we, "query_ew": query_ew, "query_ee": query_ee, "key_weight": key_weight, "value_weight": value_weight, "out_weight": out_weight, "norm1_gain": norm1_gain, "norm1_bias": norm1_bias, "up_weight": up_weight, "down_weight": down_weight, "norm2_gain": norm2_gain, "norm2_bias": norm2_bias, "head_weight": head_weight, "head_gain": head_gain, "head_bias": head_bias, "cotangent": cotangent}


@jax.custom_vjp
def low(v):
    return lax.optimization_barrier(v.astype(jnp.bfloat16)).astype(jnp.float32)

@jax.custom_vjp
def low_back(v):
    return v

def low_keep(v):
    return (low(v), None)

def low_pass(kept, grad):
    return (grad,)

def back_keep(v):
    return (v, None)

def back_low(kept, grad):
    return (low(grad),)
low.defvjp(low_keep, low_pass)
low_back.defvjp(back_keep, back_low)
EPSILON = 1e-05
MASKED = -1000000000.0

def rounded(tensor):
    return low_back(low(tensor))

def matmul_high(left_side, right_side):
    return jnp.dot(left_side, right_side, precision=lax.Precision.HIGHEST, preferred_element_type=jnp.float32)

def layer_norm(tensor, gain_vec, shift_vec):
    center = tensor - lax.optimization_barrier(jnp.mean(tensor, axis=-1, keepdims=True))
    spread = lax.optimization_barrier(jnp.mean(center * center, axis=-1, keepdims=True))
    return center * lax.rsqrt(spread + EPSILON) * gain_vec + shift_vec

def gelu_exact(tensor):
    return jax.nn.gelu(tensor, approximate=False)

def sequence_layer(word_rows, entity_rows, segment_row, layer_weights):
    entity_dense, query_ww, query_we, query_ew, query_ee, key_weight, value_weight, out_weight, norm1_gain, norm1_bias, up_weight, down_weight, norm2_gain, norm2_bias = layer_weights
    query_scale = HD ** (-0.5)
    head_count = D // HD
    entity_states = low_back(matmul_high(entity_rows, entity_dense))
    hidden = jnp.concatenate([word_rows, entity_states], axis=0)
    hidden_low = low(hidden)
    word_part = hidden_low[:WORDS]
    entity_part = hidden_low[WORDS:]
    query_word = rounded(query_scale * jnp.concatenate([matmul_high(word_part, query_ww), matmul_high(entity_part, query_ew)], axis=0))
    query_entity = rounded(query_scale * jnp.concatenate([matmul_high(word_part, query_we), matmul_high(entity_part, query_ee)], axis=0))
    key_rows = rounded(matmul_high(hidden_low, key_weight))
    values = rounded(matmul_high(hidden_low, value_weight))
    head_shape = (SEQ, head_count, HD)
    query_word = query_word.reshape(head_shape)
    query_entity = query_entity.reshape(head_shape)
    key_rows = key_rows.reshape(head_shape)
    values = values.reshape(head_shape)
    to_words = jnp.einsum('qhd,khd->hqk', query_word, key_rows[:WORDS], precision=lax.Precision.HIGHEST)
    to_entities = jnp.einsum('qhd,khd->hqk', query_entity, key_rows[WORDS:], precision=lax.Precision.HIGHEST)
    scores = low_back(jnp.concatenate([to_words, to_entities], axis=2))
    allowed = segment_row[:, None] == segment_row[None, :]
    scores = jnp.where(allowed[None], scores, MASKED)
    row_top = lax.optimization_barrier(jnp.max(scores, axis=2, keepdims=True))
    exp_scores = jnp.exp(scores - row_top)
    attn_low = low(exp_scores / lax.optimization_barrier(jnp.sum(exp_scores, axis=2, keepdims=True)))
    context = rounded(jnp.einsum('hqk,khd->qhd', attn_low, values, precision=lax.Precision.HIGHEST).reshape(SEQ, D))
    attended = low_back(matmul_high(context, out_weight))
    normed = layer_norm(hidden + attended, norm1_gain, norm1_bias)
    up_value = low_back(matmul_high(low(normed), up_weight))
    activated = low(gelu_exact(up_value))
    down_value = low_back(matmul_high(activated, down_weight))
    return layer_norm(normed + down_value, norm2_gain, norm2_bias)

def reference(word_states, word_segments, entity_segments, request_rows, request_slot, mask_slots, entity_table, vocab_bias, entity_dense, query_ww, query_we, query_ew, query_ee, key_weight, value_weight, out_weight, norm1_gain, norm1_bias, up_weight, down_weight, norm2_gain, norm2_bias, head_weight, head_gain, head_bias, cotangent):
    owners = jnp.arange(N_DP * CAP, dtype=jnp.int32) // CAP
    global_rows = (owners[None, :] * ENT_DEV + request_rows.reshape(N_DP, N_DP * CAP)).astype(jnp.int32)
    slot_rows = request_slot.reshape(N_DP, N_DP * CAP).astype(jnp.int32)

    def place_ids(row_ids, row_slots):
        return jnp.zeros((REQ + 1,), jnp.int32).at[row_slots].set(row_ids)[:REQ]
    request_ids = jax.vmap(place_ids)(global_rows, slot_rows)
    segments_all = jnp.concatenate([word_segments, entity_segments], axis=1)
    target_ids = request_ids[:, ENT_SLOTS:].reshape(M_ALL)
    block_rows = min(128, M_ALL)

    def forward(word_input, table_rows, biases, *params):
        head_weight_f, head_gain_f, head_bias_f = (params[14], params[15], params[16])
        layer_weights = params[:14]
        looked = jnp.take(table_rows, request_ids, axis=0)
        entity_rows = looked[:, :ENT_SLOTS]
        target_rows = looked[:, ENT_SLOTS:].reshape(M_ALL, EW)
        target_bias = jnp.take(biases, target_ids, axis=0)

        def one_sequence(seq_items):
            return sequence_layer(seq_items[0], seq_items[1], seq_items[2], layer_weights)
        outputs = lax.map(jax.checkpoint(one_sequence), (word_input.reshape(N_DP, WORDS, D), entity_rows, segments_all))
        entity_out = outputs[:, WORDS:]
        picked = jnp.take_along_axis(entity_out, mask_slots[:, :, None], axis=1).reshape(M_ALL, D)
        head_pre = low_back(matmul_high(low(picked), head_weight_f))
        head_low = low(layer_norm(gelu_exact(head_pre), head_gain_f, head_bias_f))
        target_logit = lax.optimization_barrier(jnp.sum(head_low * target_rows, axis=1)) + target_bias

        def block_lse(row_block):
            logits = low_back(matmul_high(row_block, table_rows.T) + biases[None, :])
            top_value = lax.optimization_barrier(jnp.max(logits, axis=1))
            return top_value + jnp.log(lax.optimization_barrier(jnp.sum(jnp.exp(logits - top_value[:, None]), axis=1)))
        lse_all = lax.map(jax.checkpoint(block_lse), head_low.reshape(M_ALL // block_rows, block_rows, EW)).reshape(M_ALL)
        row_terms = lse_all - target_logit
        loss_value = jnp.mean(row_terms)
        return (outputs.reshape(N_DP * SEQ, D), loss_value, row_terms)
    primals = tuple((argument.astype(jnp.float32) for argument in (word_states, entity_table, vocab_bias, entity_dense, query_ww, query_we, query_ew, query_ee, key_weight, value_weight, out_weight, norm1_gain, norm1_bias, up_weight, down_weight, norm2_gain, norm2_bias, head_weight, head_gain, head_bias)))
    (outputs, loss_value, row_terms), pullback = jax.vjp(forward, *primals)
    gradients = pullback((cotangent.astype(jnp.float32), jnp.ones_like(loss_value), jnp.zeros_like(row_terms)))
    return (loss_value, outputs.astype(jnp.bfloat16), gradients[0].astype(jnp.bfloat16), gradients[1], gradients[2], gradients[3], gradients[4], gradients[5], gradients[6], gradients[7], gradients[8], gradients[9], gradients[10], gradients[11], gradients[12], gradients[13], gradients[14], gradients[15], gradients[16], gradients[17], gradients[18], gradients[19], row_terms)
```

```python
import functools

import jax
import jax.numpy as jnp
from jax import lax
from jax.experimental import pallas as pl
from jax.experimental.pallas import tpu as pltpu
from jax.sharding import PartitionSpec as P

MESH_ID = pl.DeviceIdType.MESH

HD = 64


EPSILON = 1e-05
MASKED = -1000000000.0


def dot_plain(left_side, right_side):
    return jnp.dot(left_side, right_side, preferred_element_type=jnp.float32)


def dot_left_t(left_side, right_side):
    return lax.dot_general(
        left_side, right_side, (((0,), (0,)), ((), ())), preferred_element_type=jnp.float32
    )


def dot_right_t(left_side, right_side):
    return lax.dot_general(
        left_side, right_side, (((1,), (1,)), ((), ())), preferred_element_type=jnp.float32
    )


def dot_exact(left_side, right_side):
    return jnp.dot(
        left_side, right_side, precision=lax.Precision.HIGHEST, preferred_element_type=jnp.float32
    )


def layer_norm(tensor, gain_vec, shift_vec):
    center = tensor - jnp.mean(tensor, axis=-1, keepdims=True)
    spread = jnp.mean(center * center, axis=-1, keepdims=True)
    return center * lax.rsqrt(spread + EPSILON) * gain_vec + shift_vec


def gelu_exact(tensor):
    return jax.nn.gelu(tensor, approximate=False)


def head_act(tensor, gain_vec, shift_vec):
    return layer_norm(gelu_exact(tensor), gain_vec, shift_vec)


def norm_back(tensor, gain_vec, shift_vec, grad_out):
    result, pullback = jax.vjp(layer_norm, tensor, gain_vec, shift_vec)
    return pullback(grad_out)


def attn_scores(query_word, query_entity, key_rows, allowed, word_count):
    to_words = jnp.einsum(
        "qhd,khd->hqk", query_word, key_rows[:word_count], preferred_element_type=jnp.float32
    )
    to_entities = jnp.einsum(
        "qhd,khd->hqk", query_entity, key_rows[word_count:], preferred_element_type=jnp.float32
    )
    return jnp.where(allowed[None], jnp.concatenate([to_words, to_entities], axis=2), MASKED)


def greet_all(me, devices):
    barrier = pltpu.get_barrier_semaphore()

    def greet(step, carry):
        pl.semaphore_signal(
            barrier, inc=1, device_id=(lax.rem(me + step, devices),), device_id_type=MESH_ID
        )
        return carry

    lax.fori_loop(1, devices, greet, 0)
    pl.semaphore_wait(barrier, devices - 1)


def swap_kernel(devices, gather, source, target, send_sem, recv_sem):
    me = lax.axis_index("dp")
    greet_all(me, devices)

    def piece(step):
        peer = lax.rem(me + step, devices)
        return pltpu.make_async_remote_copy(
            src_ref=source if gather else source.at[peer],
            dst_ref=target.at[me],
            send_sem=send_sem.at[step],
            recv_sem=recv_sem.at[step],
            device_id=(peer,),
            device_id_type=MESH_ID,
        )

    def begin(step, carry):
        piece(step).start()
        return carry

    def finish(step, carry):
        piece(step).wait()
        return carry

    lax.fori_loop(1, devices, begin, 0)
    target[me] = source[...] if gather else source[me]
    lax.fori_loop(1, devices, finish, 0)


def direct_swap(value, collective_id, gather=False):
    devices = lax.axis_size("dp")
    shape = (devices,) + value.shape if gather else value.shape
    return pl.pallas_call(
        functools.partial(swap_kernel, devices, gather),
        out_shape=jax.ShapeDtypeStruct(shape, value.dtype),
        in_specs=[pl.BlockSpec(memory_space=pltpu.VMEM)],
        out_specs=pl.BlockSpec(memory_space=pltpu.VMEM),
        scratch_shapes=[
            pltpu.SemaphoreType.DMA((devices,)),
            pltpu.SemaphoreType.DMA((devices,)),
        ],
        compiler_params=pltpu.CompilerParams(collective_id=collective_id, has_side_effects=True),
    )(value)


def stage_masks(devices):
    if devices == 32:
        axes = [[2], [4], [8, 16]]
    elif devices == 128:
        axes = [[2, 4], [8, 16], [32, 64]]
    else:
        axes = [[2**bit] for bit in range(1, devices.bit_length() - 1)]
        axes = axes + [[] for _ in range(3 - len(axes))]
    first, second, third = axes[0], axes[1], sum(axes[2:], [])
    return (
        [1] + first + second + third,
        [1] + second + first + third,
        [1] + third + first + second,
    )


def sum_kernel(masks, rows, *refs):
    parts = len(masks)
    stages = len(masks[0])
    sources, results = refs[:parts], refs[parts : 2 * parts]
    landing = refs[2 * parts : 3 * parts]
    send_sem, recv_sem = refs[3 * parts :]
    me = lax.axis_index("dp")
    barrier = pltpu.get_barrier_semaphore()
    partner_of = {}
    for mask in masks[0]:
        bit = lax.rem(lax.div(me, mask), 2)
        partner_of[mask] = (me + mask - 2 * mask * bit, bit)
    for mask in masks[0]:
        pl.semaphore_signal(
            barrier, inc=1, device_id=(partner_of[mask][0],), device_id_type=MESH_ID
        )
    pl.semaphore_wait(barrier, stages)
    sizes = [[rows[part] * 2 ** (stages - 1 - stage) for stage in range(stages)] for part in range(parts)]
    places = [[sum(size[:stage]) for stage in range(stages)] for size in sizes]

    def launch(part, stage):
        partner, bit = partner_of[masks[part][stage]]
        size = sizes[part][stage]
        away = (1 - bit) * size
        copy = pltpu.make_async_remote_copy(
            src_ref=sources[part].at[pl.ds(away, size)]
            if stage == 0
            else landing[part].at[pl.ds(places[part][stage - 1] + away, size)],
            dst_ref=landing[part].at[pl.ds(places[part][stage], size)],
            send_sem=send_sem.at[part, stage],
            recv_sem=recv_sem.at[part, stage],
            device_id=(partner,),
            device_id_type=MESH_ID,
        )
        copy.start()
        return copy

    flying = [launch(part, 0) for part in range(parts)]

    def add_rows(part, stage, start, count):
        keep = partner_of[masks[part][stage]][1] * sizes[part][stage] + start
        last = stage == stages - 1

        def step(index, carry):
            theirs = pl.ds(pl.multiple_of(places[part][stage] + start + index * 16, 16), 16)
            if stage == 0:
                mine = sources[part][pl.ds(pl.multiple_of(keep + index * 16, 16), 16)]
            else:
                mine = landing[part][
                    pl.ds(pl.multiple_of(places[part][stage - 1] + keep + index * 16, 16), 16)
                ]
            total = mine.astype(jnp.float32) + landing[part][theirs].astype(jnp.float32)
            if last:
                results[part][pl.ds(pl.multiple_of(index * 16, 16), 16)] = total
            else:
                landing[part][theirs] = total.astype(jnp.bfloat16)
            return carry

        lax.fori_loop(0, count // 16, step, 0, unroll=min(4, count // 16))

    for stage in range(stages):
        for part in range(parts):
            flying[part].wait()
            if stage == stages - 1:
                add_rows(part, stage, 0, sizes[part][stage])
                continue
            bit = partner_of[masks[part][stage + 1]][1]
            half = sizes[part][stage] // 2
            add_rows(part, stage, (1 - bit) * half, half)
            flying[part] = launch(part, stage + 1)
            add_rows(part, stage, bit * half, half)


def sum_scatter(parts, collective_id):
    devices = lax.axis_size("dp")
    masks = stage_masks(devices)
    rows = [part.shape[1] for part in parts]
    width = parts[0].shape[2]
    bits = devices.bit_length() - 1
    ordered = []
    for part, order in zip(parts, masks):
        view = part.reshape((2,) * bits + part.shape[1:])
        places = [bits - mask.bit_length() for mask in order]
        view = view.transpose(tuple(places) + (bits, bits + 1))
        ordered.append(view.reshape(devices * part.shape[1], width))
    return pl.pallas_call(
        functools.partial(sum_kernel, masks, rows),
        out_shape=[jax.ShapeDtypeStruct((count, width), jnp.float32) for count in rows],
        in_specs=[pl.BlockSpec(memory_space=pltpu.VMEM)] * len(parts),
        out_specs=[pl.BlockSpec(memory_space=pltpu.VMEM)] * len(parts),
        scratch_shapes=[pltpu.VMEM((devices * count, width), jnp.bfloat16) for count in rows]
        + [pltpu.SemaphoreType.DMA((len(parts), bits)), pltpu.SemaphoreType.DMA((len(parts), bits))],
        input_output_aliases={},
        compiler_params=pltpu.CompilerParams(
            collective_id=collective_id, has_side_effects=True, vmem_limit_bytes=56 * 2**20
        ),
    )(*ordered)


def by_owner(grad, width):
    devices = lax.axis_size("dp")
    rows = grad.shape[0] // devices
    blocks = grad.astype(jnp.bfloat16).reshape(devices, rows, grad.shape[1])
    if grad.shape[1] > width:
        cuts = grad.shape[1] // width
        return jnp.concatenate(jnp.split(blocks, cuts, axis=2), axis=1)
    if grad.shape[1] < width:
        return blocks.reshape(devices, rows * grad.shape[1] // width, width)
    return blocks


def from_owner(rows, shape):
    devices = lax.axis_size("dp")
    count, width = shape[0] // devices, shape[1]
    if width > rows.shape[1]:
        return jnp.concatenate(jnp.split(rows, width // rows.shape[1], axis=0), axis=1)
    return rows.reshape(count, width)


def sum_all(groups, collective_id):
    width = groups[0][0].shape[1]
    width = min(grad.shape[1] for group in groups for grad in group if grad.shape[1] >= 768)
    devices = lax.axis_size("dp")
    packed = []
    for group in groups:
        pieces = [by_owner(grad, width) for grad in group]
        count = sum(piece.shape[1] for piece in pieces)
        room = -(-count // 16) * 16 - count
        if room:
            pieces.append(jnp.zeros((devices, room, width), jnp.bfloat16))
        packed.append(jnp.concatenate(pieces, axis=1))
    sums = sum_scatter(packed, collective_id)
    results = []
    for group, total in zip(groups, sums):
        place, outs = 0, []
        for grad in group:
            count = grad.shape[0] // devices * grad.shape[1] // width
            outs.append(from_owner(total[place : place + count], grad.shape))
            place += count
        results.append(outs)
    return results


def body(
    word_states,
    word_segments,
    entity_segments,
    request_rows,
    request_slot,
    mask_slots,
    entity_table,
    vocab_bias,
    entity_dense,
    query_ww,
    query_we,
    query_ew,
    query_ee,
    key_weight,
    value_weight,
    out_weight,
    norm1_gain,
    norm1_bias,
    up_weight,
    down_weight,
    norm2_gain,
    norm2_bias,
    head_weight,
    head_gain,
    head_bias,
    cotangent,
):
    word_count = word_states.shape[0]
    model_width = word_states.shape[1]
    slot_count = entity_segments.shape[1]
    mask_count = mask_slots.shape[1]
    request_count = slot_count + mask_count
    seq_len = word_count + slot_count
    devices = lax.axis_size("dp")
    capacity = request_rows.shape[1]
    head_count = model_width // HD
    query_scale = HD ** (-0.5)
    emb_width = entity_table.shape[1]
    table_rows = entity_table.shape[0]
    total_mask = mask_count * devices
    grad_scale = 1.0 / total_mask
    id_block = jnp.pad(request_rows[:, None, :], ((0, 0), (0, 7), (0, 128 - capacity)))
    asked_ids = direct_swap(id_block, 0)[:, 0, :capacity]
    found_rows = jnp.take(entity_table, asked_ids, axis=0)
    found_bias = jnp.take(vocab_bias, asked_ids, axis=0)
    cap_room = -(-capacity // 16) * 16 - capacity
    found_all = jnp.concatenate(
        [found_rows, jnp.broadcast_to(found_bias[:, :, None], found_bias.shape + (128,))], axis=2
    )
    back_all = direct_swap(jnp.pad(found_all, ((0, 0), (0, cap_room), (0, 0))), 1)
    back_rows = back_all[:, :capacity, :emb_width]
    back_bias = back_all[:, :capacity, emb_width]
    got_rows = back_rows
    got_bias = back_bias
    slot_ids = request_slot.reshape(devices * capacity)
    placing = slot_ids[None, :] == jnp.arange(request_count, dtype=jnp.int32)[:, None]
    placing_low = placing.astype(jnp.bfloat16)
    request_vecs = dot_plain(placing_low, got_rows.reshape(devices * capacity, emb_width))
    request_bias = dot_plain(placing_low, got_bias.reshape(devices * capacity, 1))[:, 0]
    entity_low = request_vecs[:slot_count].astype(jnp.bfloat16)
    target_vecs = request_vecs[slot_count:]
    target_bias = request_bias[slot_count:]
    entity_states = dot_plain(entity_low, entity_dense)
    hidden = jnp.concatenate([word_states.astype(jnp.float32), entity_states], axis=0)
    hidden_low = hidden.astype(jnp.bfloat16)
    word_part = hidden_low[:word_count]
    entity_part = hidden_low[word_count:]
    query_word = (
        query_scale
        * jnp.concatenate(
            [dot_plain(word_part, query_ww), dot_plain(entity_part, query_ew)], axis=0
        )
    ).astype(jnp.bfloat16)
    query_entity = (
        query_scale
        * jnp.concatenate(
            [dot_plain(word_part, query_we), dot_plain(entity_part, query_ee)], axis=0
        )
    ).astype(jnp.bfloat16)
    key_rows = dot_plain(hidden_low, key_weight).astype(jnp.bfloat16)
    values = dot_plain(hidden_low, value_weight).astype(jnp.bfloat16)
    head_shape = (seq_len, head_count, HD)
    query_word_h = query_word.reshape(head_shape)
    query_entity_h = query_entity.reshape(head_shape)
    key_rows_h = key_rows.reshape(head_shape)
    values_h = values.reshape(head_shape)
    segment_row = jnp.concatenate([word_segments[0], entity_segments[0]])
    allowed = segment_row[:, None] == segment_row[None, :]
    scores = attn_scores(query_word_h, query_entity_h, key_rows_h, allowed, word_count)
    row_top = jnp.max(scores, axis=2, keepdims=True)
    exp_scores = jnp.exp(scores - row_top)
    row_total = jnp.sum(exp_scores, axis=2, keepdims=True)
    attn_low = (exp_scores / row_total).astype(jnp.bfloat16)
    row_lse = row_top + jnp.log(row_total)
    context = jnp.einsum("hqk,khd->qhd", attn_low, values_h, preferred_element_type=jnp.float32)
    context_low = context.reshape(seq_len, model_width).astype(jnp.bfloat16)
    attended = dot_plain(context_low, out_weight)
    residual_one = hidden + attended
    normed = layer_norm(residual_one, norm1_gain, norm1_bias)
    normed_low = normed.astype(jnp.bfloat16)
    up_value = dot_plain(normed_low, up_weight)
    activated = gelu_exact(up_value).astype(jnp.bfloat16)
    down_value = dot_plain(activated, down_weight)
    residual_two = normed + down_value
    layer_out = layer_norm(residual_two, norm2_gain, norm2_bias)
    choose = (mask_slots[0][:, None] == jnp.arange(slot_count, dtype=jnp.int32)[None, :]).astype(
        jnp.float32
    )
    picked_low = dot_exact(choose, layer_out[word_count:]).astype(jnp.bfloat16)
    head_pre = dot_plain(picked_low, head_weight)
    head_low = head_act(head_pre, head_gain, head_bias).astype(jnp.bfloat16)
    head_f32 = head_low.astype(jnp.float32)
    target_logit = jnp.sum(head_f32 * target_vecs, axis=1) + target_bias
    all_heads = direct_swap(head_low, 2, gather=True).reshape(total_mask, emb_width)
    block_rows = min(512, total_mask)
    block_count = total_mask // block_rows
    bias_f32 = vocab_bias.astype(jnp.float32)

    def block_logits(block_index):
        row_block = lax.dynamic_slice_in_dim(all_heads, block_index * block_rows, block_rows, 0)
        return (row_block, dot_right_t(row_block, entity_table) + bias_f32[None, :])

    def block_stats(block_index):
        row_block, logits = block_logits(block_index)
        top_value = jnp.max(logits, axis=1)
        return (top_value, jnp.sum(jnp.exp(logits - top_value[:, None]), axis=1))

    local_top, local_total = lax.map(block_stats, jnp.arange(block_count, dtype=jnp.int32))
    local_top = local_top.reshape(total_mask)
    local_total = local_total.reshape(total_mask)
    target_sum = jnp.sum(target_logit)
    stats = jnp.concatenate(
        [
            local_top.reshape(total_mask // 128, 128),
            local_total.reshape(total_mask // 128, 128),
            jnp.full((8, 128), target_sum),
        ],
        axis=0,
    )
    all_stats = direct_swap(stats, 3, gather=True)
    all_tops = all_stats[:, : total_mask // 128].reshape(devices, total_mask)
    all_totals = all_stats[:, total_mask // 128 : total_mask // 64].reshape(devices, total_mask)
    target_total = jnp.sum(all_stats[:, total_mask // 64, 0])
    global_top = jnp.max(all_tops, axis=0)
    global_total = jnp.sum(all_totals * jnp.exp(all_tops - global_top[None, :]), axis=0)
    lse_all = global_top + jnp.log(global_total)
    loss_value = (jnp.sum(lse_all) - target_total) * grad_scale
    own_lse = lax.dynamic_slice_in_dim(lse_all, lax.axis_index("dp") * mask_count, mask_count, 0)
    mask_loss = own_lse - target_logit

    def block_back(running, block_index):
        table_grad, bias_grad = running
        row_block, logits = block_logits(block_index)
        lse_block = lax.dynamic_slice_in_dim(lse_all, block_index * block_rows, block_rows, 0)
        logit_grad = (jnp.exp(logits - lse_block[:, None]) * grad_scale).astype(jnp.bfloat16)
        table_grad = table_grad + dot_left_t(logit_grad, row_block)
        bias_grad = bias_grad + jnp.sum(logit_grad.astype(jnp.float32), axis=0)
        return ((table_grad, bias_grad), dot_plain(logit_grad, entity_table))

    start_grads = (
        jnp.zeros((table_rows, emb_width), jnp.float32),
        jnp.zeros((table_rows,), jnp.float32),
    )
    (table_grad, bias_grad), head_terms = lax.scan(
        block_back, start_grads, jnp.arange(block_count, dtype=jnp.int32)
    )
    head_parts = direct_swap(head_terms.reshape(devices, mask_count, emb_width), 4)
    head_grad = jnp.sum(head_parts, axis=0)
    head_grad = head_grad - grad_scale * target_vecs
    target_grad = -grad_scale * head_f32
    pre_grad, head_gain_grad, head_bias_grad = jax.vjp(head_act, head_pre, head_gain, head_bias)[1](
        head_grad
    )
    pre_low = pre_grad.astype(jnp.bfloat16)
    head_weight_grad = dot_left_t(picked_low, pre_low)
    picked_grad = dot_right_t(pre_low, head_weight)
    out_grad = cotangent.astype(jnp.float32) + jnp.concatenate(
        [jnp.zeros((word_count, model_width), jnp.float32), dot_exact(choose.T, picked_grad)],
        axis=0,
    )
    resid_grad, norm2_gain_grad, norm2_bias_grad = norm_back(
        residual_two, norm2_gain, norm2_bias, out_grad
    )
    down_in = resid_grad.astype(jnp.bfloat16)
    down_grad = dot_left_t(activated, down_in)
    act_grad = dot_right_t(down_in, down_weight)
    up_grad = jax.vjp(gelu_exact, up_value)[1](act_grad)[0]
    up_low = up_grad.astype(jnp.bfloat16)
    up_weight_grad = dot_left_t(normed_low, up_low)
    normed_grad = resid_grad + dot_right_t(up_low, up_weight)
    first_grad, norm1_gain_grad, norm1_bias_grad = norm_back(
        residual_one, norm1_gain, norm1_bias, normed_grad
    )
    attn_in = first_grad.astype(jnp.bfloat16)
    out_weight_grad = dot_left_t(context_low, attn_in)
    context_grad = dot_right_t(attn_in, out_weight).astype(jnp.bfloat16).reshape(head_shape)
    scores_again = attn_scores(query_word_h, query_entity_h, key_rows_h, allowed, word_count)
    attn_prob = jnp.exp(scores_again - row_lse)
    prob_low = attn_prob.astype(jnp.bfloat16)
    prob_grad = jnp.einsum(
        "qhd,khd->hqk", context_grad, values_h, preferred_element_type=jnp.float32
    )
    values_grad = jnp.einsum(
        "hqk,qhd->khd", prob_low, context_grad, preferred_element_type=jnp.float32
    )
    values_grad = values_grad.reshape(seq_len, model_width).astype(jnp.bfloat16)
    row_delta = jnp.sum(attn_prob * prob_grad, axis=2, keepdims=True)
    score_grad = (attn_prob * (prob_grad - row_delta)).astype(jnp.bfloat16)
    qword_grad = jnp.einsum(
        "hqk,khd->qhd",
        score_grad[:, :, :word_count],
        key_rows_h[:word_count],
        preferred_element_type=jnp.float32,
    )
    qword_grad = qword_grad.reshape(seq_len, model_width).astype(jnp.bfloat16)
    qent_grad = jnp.einsum(
        "hqk,khd->qhd",
        score_grad[:, :, word_count:],
        key_rows_h[word_count:],
        preferred_element_type=jnp.float32,
    )
    qent_grad = qent_grad.reshape(seq_len, model_width).astype(jnp.bfloat16)
    keys_grad = jnp.concatenate(
        [
            jnp.einsum(
                "hqk,qhd->khd",
                score_grad[:, :, :word_count],
                query_word_h,
                preferred_element_type=jnp.float32,
            ),
            jnp.einsum(
                "hqk,qhd->khd",
                score_grad[:, :, word_count:],
                query_entity_h,
                preferred_element_type=jnp.float32,
            ),
        ],
        axis=0,
    )
    keys_grad = keys_grad.reshape(seq_len, model_width).astype(jnp.bfloat16)
    query_ww_grad = query_scale * dot_left_t(word_part, qword_grad[:word_count])
    query_ew_grad = query_scale * dot_left_t(entity_part, qword_grad[word_count:])
    query_we_grad = query_scale * dot_left_t(word_part, qent_grad[:word_count])
    query_ee_grad = query_scale * dot_left_t(entity_part, qent_grad[word_count:])
    key_weight_grad = dot_left_t(hidden_low, keys_grad)
    value_weight_grad = dot_left_t(hidden_low, values_grad)
    word_back = query_scale * (
        dot_right_t(qword_grad[:word_count], query_ww)
        + dot_right_t(qent_grad[:word_count], query_we)
    )
    entity_back = query_scale * (
        dot_right_t(qword_grad[word_count:], query_ew)
        + dot_right_t(qent_grad[word_count:], query_ee)
    )
    hidden_grad = (
        first_grad
        + jnp.concatenate([word_back, entity_back], axis=0)
        + dot_right_t(keys_grad, key_weight)
        + dot_right_t(values_grad, value_weight)
    )
    words_grad = hidden_grad[:word_count].astype(jnp.bfloat16)
    state_low = hidden_grad[word_count:].astype(jnp.bfloat16)
    dense_grad = dot_left_t(entity_low, state_low)
    entity_vec_grad = dot_right_t(state_low, entity_dense)
    vec_grad = jnp.concatenate([entity_vec_grad, target_grad], axis=0)
    bias_vec_grad = jnp.concatenate(
        [jnp.zeros((slot_count,), jnp.float32), jnp.full((mask_count,), -grad_scale, jnp.float32)]
    )
    placing_f32 = placing.astype(jnp.float32)
    per_request = dot_exact(placing_f32.T, vec_grad)
    bias_request = dot_exact(placing_f32.T, bias_vec_grad[:, None])[:, 0]
    back_block = jnp.concatenate(
        [
            per_request.reshape(devices, capacity, emb_width).astype(jnp.bfloat16),
            jnp.broadcast_to(
                bias_request.reshape(devices, capacity, 1).astype(jnp.bfloat16),
                (devices, capacity, 128),
            ),
        ],
        axis=2,
    )
    back_block = direct_swap(jnp.pad(back_block, ((0, 0), (0, cap_room), (0, 0))), 5)
    back_rows = back_block[:, :capacity, :emb_width].astype(jnp.float32)
    back_bias = back_block[:, :capacity, emb_width].astype(jnp.float32)
    flat_ids = asked_ids.reshape(devices * capacity)
    table_grad = table_grad + jax.ops.segment_sum(
        back_rows.reshape(devices * capacity, emb_width), flat_ids, num_segments=table_rows
    )
    bias_grad = bias_grad + jax.ops.segment_sum(
        back_bias.reshape(devices * capacity), flat_ids, num_segments=table_rows
    )
    vectors = [
        head_gain_grad,
        head_bias_grad,
        norm2_gain_grad,
        norm2_bias_grad,
        norm1_gain_grad,
        norm1_bias_grad,
    ]
    cuts = [vector.reshape(devices, -1) for vector in vectors]
    spots = [0]
    for cut in cuts:
        spots.append(spots[-1] + cut.shape[1])
    block = jnp.concatenate(cuts, axis=1)
    block = jnp.pad(block, ((0, 0), (0, 128 - spots[-1])))[:, None, :]
    vector_sums = jnp.sum(direct_swap(jnp.pad(block, ((0, 0), (0, 7), (0, 0))), 6)[:, 0], axis=0)
    vector_out = [vector_sums[spots[i] : spots[i + 1]] for i in range(len(cuts))]
    sums = sum_all(
        [
            [up_weight_grad, out_weight_grad, head_weight_grad],
            [down_grad, query_ww_grad, dense_grad],
            [query_we_grad, query_ew_grad, query_ee_grad, key_weight_grad, value_weight_grad],
        ],
        7,
    )
    all_sums = (
        sums[0][2],
        vector_out[0],
        vector_out[1],
        vector_out[2],
        vector_out[3],
        sums[0][0],
        sums[1][0],
        vector_out[4],
        vector_out[5],
        sums[0][1],
        sums[1][1],
        sums[2][0],
        sums[2][1],
        sums[2][2],
        sums[2][3],
        sums[2][4],
        sums[1][2],
    )
    return (
        loss_value,
        layer_out.astype(jnp.bfloat16),
        words_grad,
        table_grad,
        bias_grad,
        all_sums[16],
        all_sums[10],
        all_sums[11],
        all_sums[12],
        all_sums[13],
        all_sums[14],
        all_sums[15],
        all_sums[9],
        all_sums[7],
        all_sums[8],
        all_sums[5],
        all_sums[6],
        all_sums[3],
        all_sums[4],
        all_sums[0],
        all_sums[1],
        all_sums[2],
        mask_loss,
    )


def solution(mesh):
    in_specs = (
        P("dp", None),
        P("dp", None),
        P("dp", None),
        P("dp", None),
        P("dp", None),
        P("dp", None),
        P("dp", None),
        P("dp"),
        P(),
        P(),
        P(),
        P(),
        P(),
        P(),
        P(),
        P(),
        P(),
        P(),
        P(),
        P(),
        P(),
        P(),
        P(),
        P(),
        P(),
        P("dp", None),
    )
    out_specs = (
        P(),
        P("dp", None),
        P("dp", None),
        P("dp", None),
        P("dp"),
        P("dp", None),
        P("dp", None),
        P("dp", None),
        P("dp", None),
        P("dp", None),
        P("dp", None),
        P("dp", None),
        P("dp", None),
        P("dp"),
        P("dp"),
        P("dp", None),
        P("dp", None),
        P("dp"),
        P("dp"),
        P("dp", None),
        P("dp"),
        P("dp"),
        P("dp"),
    )
    return jax.shard_map(body, mesh=mesh, in_specs=in_specs, out_specs=out_specs, check_vma=False)
```

```python
import functools

import jax
import jax.numpy as jnp
from jax import lax
from jax.experimental import pallas as pl
from jax.experimental.pallas import tpu as pltpu
from jax.sharding import PartitionSpec as P

MESH_ID = pl.DeviceIdType.MESH

HD = 64


EPSILON = 1e-05
MASKED = -1000000000.0


def dot_plain(left_side, right_side):
    return jnp.dot(left_side, right_side, preferred_element_type=jnp.float32)


def dot_left_t(left_side, right_side):
    return lax.dot_general(
        left_side, right_side, (((0,), (0,)), ((), ())), preferred_element_type=jnp.float32
    )


def dot_right_t(left_side, right_side):
    return lax.dot_general(
        left_side, right_side, (((1,), (1,)), ((), ())), preferred_element_type=jnp.float32
    )


def dot_exact(left_side, right_side):
    return jnp.dot(
        left_side, right_side, precision=lax.Precision.HIGHEST, preferred_element_type=jnp.float32
    )


def layer_norm(tensor, gain_vec, shift_vec):
    center = tensor - jnp.mean(tensor, axis=-1, keepdims=True)
    spread = jnp.mean(center * center, axis=-1, keepdims=True)
    return center * lax.rsqrt(spread + EPSILON) * gain_vec + shift_vec


def gelu_exact(tensor):
    return jax.nn.gelu(tensor, approximate=False)


def head_act(tensor, gain_vec, shift_vec):
    return layer_norm(gelu_exact(tensor), gain_vec, shift_vec)


def norm_back(tensor, gain_vec, shift_vec, grad_out):
    result, pullback = jax.vjp(layer_norm, tensor, gain_vec, shift_vec)
    return pullback(grad_out)


def attn_scores(query_word, query_entity, key_rows, allowed, word_count):
    to_words = jnp.einsum(
        "qhd,khd->hqk", query_word, key_rows[:word_count], preferred_element_type=jnp.float32
    )
    to_entities = jnp.einsum(
        "qhd,khd->hqk", query_entity, key_rows[word_count:], preferred_element_type=jnp.float32
    )
    return jnp.where(allowed[None], jnp.concatenate([to_words, to_entities], axis=2), MASKED)


def greet_all(me, devices):
    barrier = pltpu.get_barrier_semaphore()

    def greet(step, carry):
        pl.semaphore_signal(
            barrier, inc=1, device_id=(lax.rem(me + step, devices),), device_id_type=MESH_ID
        )
        return carry

    lax.fori_loop(1, devices, greet, 0)
    pl.semaphore_wait(barrier, devices - 1)


def swap_kernel(devices, gather, source, target, send_sem, recv_sem):
    me = lax.axis_index("dp")
    greet_all(me, devices)

    def piece(step):
        peer = lax.rem(me + step, devices)
        return pltpu.make_async_remote_copy(
            src_ref=source if gather else source.at[peer],
            dst_ref=target.at[me],
            send_sem=send_sem.at[step],
            recv_sem=recv_sem.at[step],
            device_id=(peer,),
            device_id_type=MESH_ID,
        )

    def begin(step, carry):
        piece(step).start()
        return carry

    def finish(step, carry):
        piece(step).wait()
        return carry

    lax.fori_loop(1, devices, begin, 0)
    target[me] = source[...] if gather else source[me]
    lax.fori_loop(1, devices, finish, 0)


def direct_swap(value, collective_id, gather=False):
    devices = lax.axis_size("dp")
    shape = (devices,) + value.shape if gather else value.shape
    return pl.pallas_call(
        functools.partial(swap_kernel, devices, gather),
        out_shape=jax.ShapeDtypeStruct(shape, value.dtype),
        in_specs=[pl.BlockSpec(memory_space=pltpu.VMEM)],
        out_specs=pl.BlockSpec(memory_space=pltpu.VMEM),
        scratch_shapes=[
            pltpu.SemaphoreType.DMA((devices,)),
            pltpu.SemaphoreType.DMA((devices,)),
        ],
        compiler_params=pltpu.CompilerParams(collective_id=collective_id, has_side_effects=True),
    )(value)


def stage_masks(devices):
    if devices == 32:
        axes = [[2], [4], [8, 16]]
    elif devices == 128:
        axes = [[2, 4], [8, 16], [32, 64]]
    else:
        axes = [[2**bit] for bit in range(1, devices.bit_length() - 1)]
        axes = axes + [[] for _ in range(3 - len(axes))]
    first, second, third = axes[0], axes[1], sum(axes[2:], [])
    return (
        [1] + first + second + third,
        [1] + second + first + third,
        [1] + third + first + second,
    )


def sum_kernel(masks, rows, *refs):
    parts = len(masks)
    stages = len(masks[0])
    sources, results = refs[:parts], refs[parts : 2 * parts]
    landing = refs[2 * parts : 3 * parts]
    send_sem, recv_sem = refs[3 * parts :]
    me = lax.axis_index("dp")
    barrier = pltpu.get_barrier_semaphore()
    partner_of = {}
    for mask in masks[0]:
        bit = lax.rem(lax.div(me, mask), 2)
        partner_of[mask] = (me + mask - 2 * mask * bit, bit)
    for mask in masks[0]:
        pl.semaphore_signal(
            barrier, inc=1, device_id=(partner_of[mask][0],), device_id_type=MESH_ID
        )
    pl.semaphore_wait(barrier, stages)
    sizes = [[rows[part] * 2 ** (stages - 1 - stage) for stage in range(stages)] for part in range(parts)]
    places = [[sum(size[:stage]) for stage in range(stages)] for size in sizes]

    def launch(part, stage):
        partner, bit = partner_of[masks[part][stage]]
        size = sizes[part][stage]
        away = (1 - bit) * size
        copy = pltpu.make_async_remote_copy(
            src_ref=sources[part].at[pl.ds(away, size)]
            if stage == 0
            else landing[part].at[pl.ds(places[part][stage - 1] + away, size)],
            dst_ref=landing[part].at[pl.ds(places[part][stage], size)],
            send_sem=send_sem.at[part, stage],
            recv_sem=recv_sem.at[part, stage],
            device_id=(partner,),
            device_id_type=MESH_ID,
        )
        copy.start()
        return copy

    flying = [launch(part, 0) for part in range(parts)]

    def add_rows(part, stage, start, count):
        keep = partner_of[masks[part][stage]][1] * sizes[part][stage] + start
        last = stage == stages - 1

        def step(index, carry):
            theirs = pl.ds(pl.multiple_of(places[part][stage] + start + index * 16, 16), 16)
            if stage == 0:
                mine = sources[part][pl.ds(pl.multiple_of(keep + index * 16, 16), 16)]
            else:
                mine = landing[part][
                    pl.ds(pl.multiple_of(places[part][stage - 1] + keep + index * 16, 16), 16)
                ]
            total = mine.astype(jnp.float32) + landing[part][theirs].astype(jnp.float32)
            if last:
                results[part][pl.ds(pl.multiple_of(index * 16, 16), 16)] = total
            else:
                landing[part][theirs] = total.astype(jnp.bfloat16)
            return carry

        lax.fori_loop(0, count // 16, step, 0, unroll=min(4, count // 16))

    for stage in range(stages):
        for part in range(parts):
            flying[part].wait()
            if stage == stages - 1:
                add_rows(part, stage, 0, sizes[part][stage])
                continue
            bit = partner_of[masks[part][stage + 1]][1]
            half = sizes[part][stage] // 2
            add_rows(part, stage, (1 - bit) * half, half)
            flying[part] = launch(part, stage + 1)
            add_rows(part, stage, bit * half, half)


def sum_scatter(parts, collective_id):
    devices = lax.axis_size("dp")
    masks = stage_masks(devices)
    rows = [part.shape[1] for part in parts]
    width = parts[0].shape[2]
    bits = devices.bit_length() - 1
    ordered = []
    for part, order in zip(parts, masks):
        view = part.reshape((2,) * bits + part.shape[1:])
        places = [bits - mask.bit_length() for mask in order]
        view = view.transpose(tuple(places) + (bits, bits + 1))
        ordered.append(view.reshape(devices * part.shape[1], width))
    return pl.pallas_call(
        functools.partial(sum_kernel, masks, rows),
        out_shape=[jax.ShapeDtypeStruct((count, width), jnp.float32) for count in rows],
        in_specs=[pl.BlockSpec(memory_space=pltpu.VMEM)] * len(parts),
        out_specs=[pl.BlockSpec(memory_space=pltpu.VMEM)] * len(parts),
        scratch_shapes=[pltpu.VMEM((devices * count, width), jnp.bfloat16) for count in rows]
        + [pltpu.SemaphoreType.DMA((len(parts), bits)), pltpu.SemaphoreType.DMA((len(parts), bits))],
        input_output_aliases={},
        compiler_params=pltpu.CompilerParams(
            collective_id=collective_id, has_side_effects=True, vmem_limit_bytes=56 * 2**20
        ),
    )(*ordered)


def by_owner(grad, width):
    devices = lax.axis_size("dp")
    rows = grad.shape[0] // devices
    blocks = grad.astype(jnp.bfloat16).reshape(devices, rows, grad.shape[1])
    if grad.shape[1] > width:
        cuts = grad.shape[1] // width
        return jnp.concatenate(jnp.split(blocks, cuts, axis=2), axis=1)
    if grad.shape[1] < width:
        return blocks.reshape(devices, rows * grad.shape[1] // width, width)
    return blocks


def from_owner(rows, shape):
    devices = lax.axis_size("dp")
    count, width = shape[0] // devices, shape[1]
    if width > rows.shape[1]:
        return jnp.concatenate(jnp.split(rows, width // rows.shape[1], axis=0), axis=1)
    return rows.reshape(count, width)


def sum_all(groups, collective_id):
    width = groups[0][0].shape[1]
    width = min(grad.shape[1] for group in groups for grad in group if grad.shape[1] >= 768)
    devices = lax.axis_size("dp")
    packed = []
    for group in groups:
        pieces = [by_owner(grad, width) for grad in group]
        count = sum(piece.shape[1] for piece in pieces)
        room = -(-count // 16) * 16 - count
        if room:
            pieces.append(jnp.zeros((devices, room, width), jnp.bfloat16))
        packed.append(jnp.concatenate(pieces, axis=1))
    sums = sum_scatter(packed, collective_id)
    results = []
    for group, total in zip(groups, sums):
        place, outs = 0, []
        for grad in group:
            count = grad.shape[0] // devices * grad.shape[1] // width
            outs.append(from_owner(total[place : place + count], grad.shape))
            place += count
        results.append(outs)
    return results


def place_owner(order, place):
    bits = len(order)
    return sum(((place >> (bits - 1 - spot)) & 1) * mask for spot, mask in enumerate(order))


class Piece:
    def __init__(self, rows, stages, send, own, land, tail, tail_land, out, send_sem, recv_sem):
        self.rows, self.stages = rows, stages
        self.send, self.own, self.land = send, own, land
        self.tail, self.tail_land, self.out = tail, tail_land, out
        self.send_sem, self.recv_sem = send_sem, recv_sem
        self.sizes = [rows * 2 ** (stages - 1 - stage) for stage in range(stages)]
        self.spots = [sum(self.sizes[:stage]) for stage in range(stages)]

    def copy(self, stage, partner, bit):
        size = self.sizes[stage]
        away = pl.multiple_of((1 - bit) * size, 8 if stage == self.stages - 1 else 16)
        if stage == 0:
            source, target = self.send.at[:, pl.ds(away, size)], self.land.at[:, pl.ds(0, size)]
        elif stage < self.stages - 1:
            spot = pl.multiple_of(self.spots[stage - 1] + away, 16)
            source = self.land.at[:, pl.ds(spot, size)]
            target = self.land.at[:, pl.ds(self.spots[stage], size)]
        else:
            source, target = self.tail.at[:, pl.ds(away, size)], self.tail_land
        return pltpu.make_async_remote_copy(
            src_ref=source,
            dst_ref=target,
            send_sem=self.send_sem.at[stage],
            recv_sem=self.recv_sem.at[stage],
            device_id=(partner,),
            device_id_type=MESH_ID,
        )

    def held(self, stage, bit):
        size = self.sizes[stage]
        if stage == 0 and self.own is not None:
            return self.own, 0
        if stage == 0:
            return self.send, pl.multiple_of(bit * size, 16)
        return self.land, pl.multiple_of(self.spots[stage - 1] + bit * size, 16)

    def add(self, stage, bit, half_index):
        size = self.sizes[stage]
        half = size // 2
        unit = 48 if half % 48 == 0 else 16
        start = half_index * half
        source, base = self.held(stage, bit)
        for slot in range(self.land.shape[0]):

            def step(index, carry, slot=slot):
                row = pl.multiple_of(start + index * unit, 16)
                mine = source[slot, pl.ds(pl.multiple_of(base + row, 16), unit)]
                spot = pl.ds(pl.multiple_of(self.spots[stage] + row, 16), unit)
                theirs = self.land[slot, spot]
                total = mine.astype(jnp.float32) + theirs.astype(jnp.float32)
                self.land[slot, spot] = total.astype(jnp.bfloat16)
                return carry

            lax.fori_loop(0, half // unit, step, 0)

    def add_tail(self, stage, bit):
        size = self.sizes[stage]
        source, base = self.held(stage, bit)
        for slot in range(self.land.shape[0]):
            mine = source[slot, pl.ds(base, size)]
            theirs = self.land[slot, pl.ds(self.spots[stage], size)]
            self.tail[slot] = mine.astype(jnp.float32) + theirs.astype(jnp.float32)

    def finish(self, bit):
        size = self.sizes[-1]
        for slot in range(self.out.shape[0]):
            mine = self.tail[slot, pl.ds(pl.multiple_of(bit * size, 8), size)]
            self.out[slot] = mine + self.tail_land[slot]


class Stream:
    def __init__(self, order, partner_of, pieces):
        self.order, self.partner_of, self.pieces = order, partner_of, pieces
        self.stages = len(order)

    def launch(self, stage):
        partner, bit = self.partner_of[self.order[stage]]
        for piece in self.pieces:
            piece.copy(stage, partner, bit).start()

    def advance(self, stage):
        partner, bit = self.partner_of[self.order[stage]]
        for piece in self.pieces:
            piece.copy(stage, partner, bit).wait()
        if stage == self.stages - 1:
            for piece in self.pieces:
                piece.finish(bit)
        elif stage == self.stages - 2:
            for piece in self.pieces:
                piece.add_tail(stage, bit)
            self.launch(stage + 1)
        else:
            following = self.partner_of[self.order[stage + 1]][1]
            for piece in self.pieces:
                piece.add(stage, bit, 1 - following)
            self.launch(stage + 1)
            for piece in self.pieces:
                piece.add(stage, bit, following)


def partners(me, masks):
    result = {}
    for mask in masks:
        bit = lax.rem(lax.div(me, mask), 2)
        result[mask] = (me + mask - 2 * mask * bit, bit)
    return result


def greet_partners(partner_of):
    barrier = pltpu.get_barrier_semaphore()
    for partner, _ in partner_of.values():
        pl.semaphore_signal(barrier, inc=1, device_id=(partner,), device_id_type=MESH_ID)
    pl.semaphore_wait(barrier, len(partner_of))


EARLY = ((0, 3, 24, 768), (0, 1, 24, 256), (1, 4, 24, 768), (2, 2, 24, 768))
LATE = ((0, 2, 24, 768), (0, 1, 8, 768), (1, 2, 24, 768), (2, 2, 24, 768))


def piece_scratch(spec, stages, source, own):
    _, slots, rows, width = spec
    owners = 2**stages
    shapes = []
    if source:
        shapes.append(pltpu.VMEM((slots, rows * owners, width), jnp.bfloat16))
    if own:
        shapes.append(pltpu.VMEM((slots, rows * owners // 2, width), jnp.bfloat16))
    shapes += [
        pltpu.VMEM((slots, rows * (owners - 2), width), jnp.bfloat16),
        pltpu.VMEM((slots, 2 * rows, width), jnp.float32),
        pltpu.VMEM((slots, rows, width), jnp.float32),
        pltpu.SemaphoreType.DMA((stages,)),
        pltpu.SemaphoreType.DMA((stages,)),
    ]
    return shapes


def attention_back_kernel(orders, *refs):
    stages = len(orders[0])
    refs = list(refs)

    def take(count):
        taken = refs[:count]
        del refs[:count]
        return taken

    early_send = take(len(EARLY))
    (hidden, qword, qent, keys, values, cgrad, feat_q, feat_k, lse_delta, first_grad) = take(10)
    (w_ww, w_we, w_ew, w_ee, w_key, w_value, dense, entity_low) = take(8)
    early_out = take(len(EARLY))
    late_out = take(len(LATE))
    words_out, dent_out = take(2)
    early_pieces = []
    own_copies = []
    me = lax.axis_index("dp")
    partner_of = partners(me, orders[0])
    own_sem = refs.pop()
    word_weights = []
    dqw, dqe, dkey, dvalue, prob_s, grad_s, flip, hidden_t, hidden_te, entity_t = refs[-10:]
    del refs[-10:]
    early = [[], [], []]
    for index, spec in enumerate(EARLY):
        own, land, tail, tail_land, send_sem, recv_sem = take(6)
        early[spec[0]].append(
            Piece(
                spec[2], stages, early_send[index], own, land, tail, tail_land,
                early_out[index], send_sem, recv_sem,
            )
        )
        bit = partner_of[orders[spec[0]][0]][1]
        size = spec[2] * 2 ** (stages - 1)
        own_copies.append(
            pltpu.make_async_copy(
                early_send[index].at[:, pl.ds(pl.multiple_of(bit * size, 16), size)],
                own,
                own_sem.at[index],
            )
        )
    late, late_source = [[], [], []], []
    for index, spec in enumerate(LATE):
        source, land, tail, tail_land, send_sem, recv_sem = take(6)
        late_source.append(source)
        late[spec[0]].append(
            Piece(
                spec[2], stages, source, None, land, tail, tail_land,
                late_out[index], send_sem, recv_sem,
            )
        )
    spare = early[1][0].own
    half_rows = w_ww.shape[0] // 2
    for index, weight in enumerate((w_ww, w_we)):
        for part in range(2):
            word_weights.append(
                pltpu.make_async_copy(
                    weight.at[pl.ds(part * half_rows, half_rows)],
                    spare.at[2 * index + part],
                    own_sem.at[len(EARLY) + 2 * index + part],
                )
            )
    early = [Stream(orders[i], partner_of, early[i]) for i in range(3)]
    late = [Stream(orders[i], partner_of, late[i]) for i in range(3)]

    greet_partners(partner_of)
    for stream in early:
        stream.launch(0)
    for copy in own_copies:
        copy.start()

    width = hidden.shape[1]
    seq_len = hidden.shape[0]
    words = words_out.shape[0]
    block = 128
    lane = lax.broadcasted_iota(jnp.int32, (1, block), 1)
    low_half = (lane < HD).astype(jnp.float32).astype(jnp.bfloat16)
    high_half = (lane >= HD).astype(jnp.float32).astype(jnp.bfloat16)
    halves = (low_half, high_half)

    def flip_step(index, carry):
        at = pl.ds(pl.multiple_of(index * block, block), block)
        flip[at] = hidden[:, at].astype(jnp.float32).T
        return carry

    lax.fori_loop(0, width // block, flip_step, 0)
    owners = 2**stages
    rows = width // owners
    for slot, order in enumerate(orders):
        begin = words if slot == 2 else 0
        for pair in range(owners // 2):
            one, two = place_owner(order, 2 * pair), place_owner(order, 2 * pair + 1)
            both = jnp.concatenate(
                [flip[one * rows : one * rows + rows, begin:], flip[two * rows : two * rows + rows, begin:]],
                axis=0,
            ).astype(jnp.bfloat16)
            if slot == 2:
                hidden_te[pair * 2 * rows : (pair + 1) * 2 * rows] = both
            else:
                hidden_t[slot, pair * 2 * rows : (pair + 1) * 2 * rows] = both

    def pair_step(pair, carry):
        lanes = pl.ds(pl.multiple_of(pair * block, block), block)
        key_pair = keys[:, lanes]
        value_pair = values[:, lanes]
        key_feat = [key_pair * halves[h] + feat_k[...] * halves[1 - h] for h in range(2)]
        key_only = [key_pair * halves[h] for h in range(2)]
        value_only = [value_pair * halves[h] for h in range(2)]

        def row_step(index, inner):
            at = pl.ds(pl.multiple_of(index * block, block), block)
            qw = qword[at, lanes]
            qe = qent[at, lanes]
            feats = feat_q[at]
            given = cgrad[at, lanes]
            stats = lse_delta[at]
            spot = lax.broadcasted_iota(jnp.int32, (1, block), 1) - 4 * pair
            total_w = jnp.zeros((block, block), jnp.float32)
            total_e = jnp.zeros((block, block), jnp.float32)
            for h in range(2):
                left_w = qw * halves[h] + feats * halves[1 - h]
                left_e = qe * halves[h] + feats * halves[1 - h]
                scores = jnp.concatenate(
                    [
                        dot_right_t(left_w, key_feat[h][:words]),
                        dot_right_t(left_e, key_feat[h][words:]),
                    ],
                    axis=1,
                )
                prob = jnp.exp(scores - jnp.sum(jnp.where(spot == h, stats, 0.0), axis=1, keepdims=True))
                pgrad = dot_right_t(given, value_only[h])
                sgrad = (prob * (pgrad - jnp.sum(jnp.where(spot == 2 + h, stats, 0.0), axis=1, keepdims=True))).astype(jnp.bfloat16)
                prob_s[h, at] = prob.astype(jnp.bfloat16)
                grad_s[h, at] = sgrad
                total_w += dot_plain(sgrad[:, :words], key_only[h][:words])
                total_e += dot_plain(sgrad[:, words:], key_only[h][words:])
            dqw[at, lanes] = total_w.astype(jnp.bfloat16)
            dqe[at, lanes] = total_e.astype(jnp.bfloat16)
            return inner

        lax.fori_loop(0, seq_len // block, row_step, 0)
        qw_all, qe_all, given_all = qword[:, lanes], qent[:, lanes], cgrad[:, lanes]
        dkey[:words, lanes] = (
            dot_left_t(grad_s[0, :, :words], qw_all * halves[0])
            + dot_left_t(grad_s[1, :, :words], qw_all * halves[1])
        ).astype(jnp.bfloat16)
        dkey[words:, lanes] = (
            dot_left_t(grad_s[0, :, words:], qe_all * halves[0])
            + dot_left_t(grad_s[1, :, words:], qe_all * halves[1])
        ).astype(jnp.bfloat16)
        dvalue[:, lanes] = (
            dot_left_t(prob_s[0], given_all * halves[0])
            + dot_left_t(prob_s[1], given_all * halves[1])
        ).astype(jnp.bfloat16)

        @pl.when(pair == 2)
        def _():
            for copy in own_copies:
                copy.wait()
            for stream in early:
                stream.advance(0)
            for copy in word_weights:
                copy.start()

        return carry

    lax.fori_loop(0, width // block, pair_step, 0)

    query_scale = HD ** (-0.5)
    column = 384

    def weight_grad(source, slot, order_slot, grad, begin, end, scale):
        for cut in range(0, width, column):
            left = hidden_te[...] if order_slot == 2 else hidden_t[order_slot, :, begin:end]
            piece = dot_plain(left, grad[begin:end, cut : cut + column])
            if scale:
                piece = piece * query_scale
            source[slot, :, cut : cut + column] = piece.astype(jnp.bfloat16)

    weight_grad(late_source[2], 0, 1, dkey, 0, seq_len, False)
    weight_grad(late_source[2], 1, 1, dvalue, 0, seq_len, False)
    late[1].launch(0)
    for stream in early:
        stream.advance(1)
    weight_grad(late_source[3], 0, 2, dqw, words, seq_len, True)
    weight_grad(late_source[3], 1, 2, dqe, words, seq_len, True)
    late[2].launch(0)

    def spare_weight(index):
        return spare[2 * index : 2 * index + 2].reshape(width, width)

    def data_grad(begin, size, word_w, ent_w):
        at = pl.ds(begin, size)
        queries = dot_right_t(dqw[at], word_w()) + dot_right_t(dqe[at], ent_w())
        return (
            first_grad[at]
            + query_scale * queries
            + dot_right_t(dkey[at], w_key[...])
            + dot_right_t(dvalue[at], w_value[...])
        )

    state_low = data_grad(words, seq_len - words, lambda: w_ew[...], lambda: w_ee[...]).astype(jnp.bfloat16)
    dent_out[...] = dot_right_t(state_low, dense[...])
    entity_width = dense.shape[0]
    few = entity_width // owners
    for cut in range(0, entity_width, block):
        flip[cut : cut + block, :block] = entity_low[:, cut : cut + block].astype(jnp.float32).T
    for pair in range(owners // 2):
        one, two = place_owner(orders[0], 2 * pair), place_owner(orders[0], 2 * pair + 1)
        both = jnp.concatenate(
            [flip[one * few : one * few + few, :block], flip[two * few : two * few + few, :block]],
            axis=0,
        )
        entity_t[pair * 2 * few : (pair + 1) * 2 * few] = both.astype(jnp.bfloat16)
    late_source[1][0] = dot_plain(entity_t[...], state_low).astype(jnp.bfloat16)
    weight_grad(late_source[0], 0, 0, dqw, 0, words, True)
    weight_grad(late_source[0], 1, 0, dqe, 0, words, True)
    late[0].launch(0)
    for stream in early:
        stream.advance(2)

    for copy in word_weights:
        copy.wait()

    def word_step(index, carry):
        begin = pl.multiple_of(index * block, block)
        words_out[pl.ds(begin, block)] = data_grad(begin, block, lambda: spare_weight(0), lambda: spare_weight(1)).astype(jnp.bfloat16)
        return carry

    lax.fori_loop(0, words // block, word_step, 0)
    for turn in ((late[1], 0), (late[2], 0), (late[0], 0)):
        turn[0].advance(turn[1])
    for stream in early:
        stream.advance(3)
    for stream in late:
        stream.advance(1)
    for stream in early:
        stream.advance(4)
    for stage in (2, 3, 4):
        for stream in late:
            stream.advance(stage)


def in_order(grad, order):
    bits = len(order)
    owners = 2**bits
    view = grad.reshape((2,) * bits + (grad.shape[0] // owners, grad.shape[1]))
    spots = tuple(bits - mask.bit_length() for mask in order)
    return view.transpose(spots + (bits, bits + 1)).reshape(grad.shape)


def attention_back(early_grads, inputs, weights, collective_id):
    devices = lax.axis_size("dp")
    orders = stage_masks(devices)
    stages = len(orders[0])
    hidden = inputs[0]
    seq_len, width = hidden.shape
    slots = weights[-1].shape[0]
    words = seq_len - slots
    outs = [
        jax.ShapeDtypeStruct((count, rows, wide), jnp.float32)
        for _, count, rows, wide in EARLY + LATE
    ] + [
        jax.ShapeDtypeStruct((words, width), jnp.bfloat16),
        jax.ShapeDtypeStruct((slots, weights[-2].shape[0]), jnp.float32),
    ]
    scratch = []
    for spec in EARLY:
        scratch += piece_scratch(spec, stages, False, True)
    for spec in LATE:
        scratch += piece_scratch(spec, stages, True, False)
    scratch += [pltpu.VMEM((seq_len, width), jnp.bfloat16)] * 4
    scratch += [pltpu.VMEM((2, seq_len, seq_len), jnp.bfloat16)] * 2
    scratch += [
        pltpu.VMEM((width, seq_len), jnp.float32),
        pltpu.VMEM((2, width, seq_len), jnp.bfloat16),
        pltpu.VMEM((width, slots), jnp.bfloat16),
        pltpu.VMEM((weights[-2].shape[0], slots), jnp.bfloat16),
        pltpu.SemaphoreType.DMA((len(EARLY) + 4,)),
    ]
    vmem = pl.BlockSpec(memory_space=pltpu.VMEM)
    return pl.pallas_call(
        functools.partial(attention_back_kernel, orders),
        out_shape=outs,
        in_specs=[pl.BlockSpec(memory_space=pltpu.HBM)] * len(EARLY)
        + [vmem] * len(inputs)
        + [pl.BlockSpec(memory_space=pltpu.HBM)] * 2
        + [vmem] * (len(weights) - 2),
        out_specs=[vmem] * len(outs),
        scratch_shapes=scratch,
        compiler_params=pltpu.CompilerParams(
            collective_id=collective_id, has_side_effects=True, vmem_limit_bytes=62 * 2**20
        ),
    )(*early_grads, *inputs, *weights)


def body(
    word_states,
    word_segments,
    entity_segments,
    request_rows,
    request_slot,
    mask_slots,
    entity_table,
    vocab_bias,
    entity_dense,
    query_ww,
    query_we,
    query_ew,
    query_ee,
    key_weight,
    value_weight,
    out_weight,
    norm1_gain,
    norm1_bias,
    up_weight,
    down_weight,
    norm2_gain,
    norm2_bias,
    head_weight,
    head_gain,
    head_bias,
    cotangent,
):
    word_count = word_states.shape[0]
    model_width = word_states.shape[1]
    slot_count = entity_segments.shape[1]
    mask_count = mask_slots.shape[1]
    request_count = slot_count + mask_count
    seq_len = word_count + slot_count
    devices = lax.axis_size("dp")
    capacity = request_rows.shape[1]
    head_count = model_width // HD
    query_scale = HD ** (-0.5)
    emb_width = entity_table.shape[1]
    table_rows = entity_table.shape[0]
    total_mask = mask_count * devices
    grad_scale = 1.0 / total_mask
    id_block = jnp.pad(request_rows[:, None, :], ((0, 0), (0, 7), (0, 128 - capacity)))
    asked_ids = direct_swap(id_block, 0)[:, 0, :capacity]
    found_rows = jnp.take(entity_table, asked_ids, axis=0)
    found_bias = jnp.take(vocab_bias, asked_ids, axis=0)
    cap_room = -(-capacity // 16) * 16 - capacity
    found_all = jnp.concatenate(
        [found_rows, jnp.broadcast_to(found_bias[:, :, None], found_bias.shape + (128,))], axis=2
    )
    back_all = direct_swap(jnp.pad(found_all, ((0, 0), (0, cap_room), (0, 0))), 1)
    back_rows = back_all[:, :capacity, :emb_width]
    back_bias = back_all[:, :capacity, emb_width]
    got_rows = back_rows
    got_bias = back_bias
    slot_ids = request_slot.reshape(devices * capacity)
    placing = slot_ids[None, :] == jnp.arange(request_count, dtype=jnp.int32)[:, None]
    placing_low = placing.astype(jnp.bfloat16)
    request_vecs = dot_plain(placing_low, got_rows.reshape(devices * capacity, emb_width))
    request_bias = dot_plain(placing_low, got_bias.reshape(devices * capacity, 1))[:, 0]
    entity_low = request_vecs[:slot_count].astype(jnp.bfloat16)
    target_vecs = request_vecs[slot_count:]
    target_bias = request_bias[slot_count:]
    entity_states = dot_plain(entity_low, entity_dense)
    hidden = jnp.concatenate([word_states.astype(jnp.float32), entity_states], axis=0)
    hidden_low = hidden.astype(jnp.bfloat16)
    word_part = hidden_low[:word_count]
    entity_part = hidden_low[word_count:]
    query_word = (
        query_scale
        * jnp.concatenate(
            [dot_plain(word_part, query_ww), dot_plain(entity_part, query_ew)], axis=0
        )
    ).astype(jnp.bfloat16)
    query_entity = (
        query_scale
        * jnp.concatenate(
            [dot_plain(word_part, query_we), dot_plain(entity_part, query_ee)], axis=0
        )
    ).astype(jnp.bfloat16)
    key_rows = dot_plain(hidden_low, key_weight).astype(jnp.bfloat16)
    values = dot_plain(hidden_low, value_weight).astype(jnp.bfloat16)
    head_shape = (seq_len, head_count, HD)
    query_word_h = query_word.reshape(head_shape)
    query_entity_h = query_entity.reshape(head_shape)
    key_rows_h = key_rows.reshape(head_shape)
    values_h = values.reshape(head_shape)
    segment_row = jnp.concatenate([word_segments[0], entity_segments[0]])
    allowed = segment_row[:, None] == segment_row[None, :]
    scores = attn_scores(query_word_h, query_entity_h, key_rows_h, allowed, word_count)
    row_top = jnp.max(scores, axis=2, keepdims=True)
    exp_scores = jnp.exp(scores - row_top)
    row_total = jnp.sum(exp_scores, axis=2, keepdims=True)
    attn_low = (exp_scores / row_total).astype(jnp.bfloat16)
    row_lse = row_top + jnp.log(row_total)
    context = jnp.einsum("hqk,khd->qhd", attn_low, values_h, preferred_element_type=jnp.float32)
    context_low = context.reshape(seq_len, model_width).astype(jnp.bfloat16)
    attended = dot_plain(context_low, out_weight)
    residual_one = hidden + attended
    normed = layer_norm(residual_one, norm1_gain, norm1_bias)
    normed_low = normed.astype(jnp.bfloat16)
    up_value = dot_plain(normed_low, up_weight)
    activated = gelu_exact(up_value).astype(jnp.bfloat16)
    down_value = dot_plain(activated, down_weight)
    residual_two = normed + down_value
    layer_out = layer_norm(residual_two, norm2_gain, norm2_bias)
    choose = (mask_slots[0][:, None] == jnp.arange(slot_count, dtype=jnp.int32)[None, :]).astype(
        jnp.float32
    )
    picked_low = dot_exact(choose, layer_out[word_count:]).astype(jnp.bfloat16)
    head_pre = dot_plain(picked_low, head_weight)
    head_low = head_act(head_pre, head_gain, head_bias).astype(jnp.bfloat16)
    head_f32 = head_low.astype(jnp.float32)
    target_logit = jnp.sum(head_f32 * target_vecs, axis=1) + target_bias
    all_heads = direct_swap(head_low, 2, gather=True).reshape(total_mask, emb_width)
    block_rows = min(512, total_mask)
    block_count = total_mask // block_rows
    bias_f32 = vocab_bias.astype(jnp.float32)

    def block_logits(block_index):
        row_block = lax.dynamic_slice_in_dim(all_heads, block_index * block_rows, block_rows, 0)
        return (row_block, dot_right_t(row_block, entity_table) + bias_f32[None, :])

    def block_stats(block_index):
        row_block, logits = block_logits(block_index)
        top_value = jnp.max(logits, axis=1)
        return (top_value, jnp.sum(jnp.exp(logits - top_value[:, None]), axis=1))

    local_top, local_total = lax.map(block_stats, jnp.arange(block_count, dtype=jnp.int32))
    local_top = local_top.reshape(total_mask)
    local_total = local_total.reshape(total_mask)
    target_sum = jnp.sum(target_logit)
    stats = jnp.concatenate(
        [
            local_top.reshape(total_mask // 128, 128),
            local_total.reshape(total_mask // 128, 128),
            jnp.full((8, 128), target_sum),
        ],
        axis=0,
    )
    all_stats = direct_swap(stats, 3, gather=True)
    all_tops = all_stats[:, : total_mask // 128].reshape(devices, total_mask)
    all_totals = all_stats[:, total_mask // 128 : total_mask // 64].reshape(devices, total_mask)
    target_total = jnp.sum(all_stats[:, total_mask // 64, 0])
    global_top = jnp.max(all_tops, axis=0)
    global_total = jnp.sum(all_totals * jnp.exp(all_tops - global_top[None, :]), axis=0)
    lse_all = global_top + jnp.log(global_total)
    loss_value = (jnp.sum(lse_all) - target_total) * grad_scale
    own_lse = lax.dynamic_slice_in_dim(lse_all, lax.axis_index("dp") * mask_count, mask_count, 0)
    mask_loss = own_lse - target_logit

    def block_back(running, block_index):
        table_grad, bias_grad = running
        row_block, logits = block_logits(block_index)
        lse_block = lax.dynamic_slice_in_dim(lse_all, block_index * block_rows, block_rows, 0)
        logit_grad = (jnp.exp(logits - lse_block[:, None]) * grad_scale).astype(jnp.bfloat16)
        table_grad = table_grad + dot_left_t(logit_grad, row_block)
        bias_grad = bias_grad + jnp.sum(logit_grad.astype(jnp.float32), axis=0)
        return ((table_grad, bias_grad), dot_plain(logit_grad, entity_table))

    start_grads = (
        jnp.zeros((table_rows, emb_width), jnp.float32),
        jnp.zeros((table_rows,), jnp.float32),
    )
    (table_grad, bias_grad), head_terms = lax.scan(
        block_back, start_grads, jnp.arange(block_count, dtype=jnp.int32)
    )
    head_parts = direct_swap(head_terms.reshape(devices, mask_count, emb_width), 4)
    head_grad = jnp.sum(head_parts, axis=0)
    head_grad = head_grad - grad_scale * target_vecs
    target_grad = -grad_scale * head_f32
    pre_grad, head_gain_grad, head_bias_grad = jax.vjp(head_act, head_pre, head_gain, head_bias)[1](
        head_grad
    )
    pre_low = pre_grad.astype(jnp.bfloat16)
    head_weight_grad = dot_left_t(picked_low, pre_low)
    picked_grad = dot_right_t(pre_low, head_weight)
    out_grad = cotangent.astype(jnp.float32) + jnp.concatenate(
        [jnp.zeros((word_count, model_width), jnp.float32), dot_exact(choose.T, picked_grad)],
        axis=0,
    )
    resid_grad, norm2_gain_grad, norm2_bias_grad = norm_back(
        residual_two, norm2_gain, norm2_bias, out_grad
    )
    down_in = resid_grad.astype(jnp.bfloat16)
    down_grad = dot_left_t(activated, down_in)
    act_grad = dot_right_t(down_in, down_weight)
    up_grad = jax.vjp(gelu_exact, up_value)[1](act_grad)[0]
    up_low = up_grad.astype(jnp.bfloat16)
    up_weight_grad = dot_left_t(normed_low, up_low)
    normed_grad = resid_grad + dot_right_t(up_low, up_weight)
    first_grad, norm1_gain_grad, norm1_bias_grad = norm_back(
        residual_one, norm1_gain, norm1_bias, normed_grad
    )
    attn_in = first_grad.astype(jnp.bfloat16)
    out_weight_grad = dot_left_t(context_low, attn_in)
    context_grad = dot_right_t(attn_in, out_weight).astype(jnp.bfloat16).reshape(head_shape)
    fused = model_width % devices == 0 and (model_width // devices) % 8 == 0 and devices == 32
    if fused:
        orders = stage_masks(devices)
        up_low_grad = up_weight_grad.astype(jnp.bfloat16)
        up_cuts = [
            in_order(up_low_grad[:, i * model_width : (i + 1) * model_width], orders[2 * (i // 3)])
            for i in range(4)
        ]
        down_view = down_grad.astype(jnp.bfloat16).reshape(devices, 4, -1, model_width)
        down_cuts = [
            in_order(down_view[:, i].reshape(model_width, model_width), orders[1 + i // 3])
            for i in range(4)
        ]
        early_grads = [
            jnp.stack(up_cuts[:3]),
            in_order(head_weight_grad.astype(jnp.bfloat16), orders[0])[None],
            jnp.stack(down_cuts[:3] + [in_order(out_weight_grad.astype(jnp.bfloat16), orders[1])]),
            jnp.stack([up_cuts[3], down_cuts[3]]),
        ]
        codes = jnp.arange(128, dtype=jnp.int32)[None, :] % HD
        same = segment_row[:, None] == codes
        feat_q = same.astype(jnp.bfloat16)
        feat_k = jnp.where(same | (codes >= 4), 0.0, MASKED).astype(jnp.bfloat16)
        delta = jnp.sum(
            (context_low.astype(jnp.float32) * context_grad.reshape(seq_len, model_width)).reshape(
                seq_len, head_count // 2, 2, HD
            ),
            axis=3,
        )
        lse_pair = row_lse[:, :, 0].T.reshape(seq_len, head_count // 2, 2)
        lse_delta = jnp.concatenate([lse_pair, delta], axis=2).reshape(seq_len, 2 * head_count)
        lse_delta = jnp.pad(lse_delta, ((0, 0), (0, 128 - 2 * head_count)))
        fused_out = attention_back(
            early_grads,
            [
                hidden_low,
                query_word,
                query_entity,
                key_rows,
                values,
                context_grad.reshape(seq_len, model_width),
                feat_q,
                feat_k,
                lse_delta,
                first_grad,
            ],
            [
                query_ww,
                query_we,
                query_ew,
                query_ee,
                key_weight,
                value_weight,
                entity_dense,
                entity_low,
            ],
            7,
        )
        up_a, head_a, down_a, mixed, q_word, dense_a, key_value, q_ent, words_grad, entity_vec_grad = (
            fused_out
        )
        up_sum = jnp.concatenate([up_a[0], up_a[1], up_a[2], mixed[0]], axis=1)
        down_sum = jnp.concatenate([down_a[0], down_a[1], down_a[2], mixed[1]], axis=0)
    else:
        scores_again = attn_scores(query_word_h, query_entity_h, key_rows_h, allowed, word_count)
        attn_prob = jnp.exp(scores_again - row_lse)
        prob_low = attn_prob.astype(jnp.bfloat16)
        prob_grad = jnp.einsum(
            "qhd,khd->hqk", context_grad, values_h, preferred_element_type=jnp.float32
        )
        values_grad = jnp.einsum(
            "hqk,qhd->khd", prob_low, context_grad, preferred_element_type=jnp.float32
        )
        values_grad = values_grad.reshape(seq_len, model_width).astype(jnp.bfloat16)
        row_delta = jnp.sum(attn_prob * prob_grad, axis=2, keepdims=True)
        score_grad = (attn_prob * (prob_grad - row_delta)).astype(jnp.bfloat16)
        qword_grad = jnp.einsum(
            "hqk,khd->qhd",
            score_grad[:, :, :word_count],
            key_rows_h[:word_count],
            preferred_element_type=jnp.float32,
        )
        qword_grad = qword_grad.reshape(seq_len, model_width).astype(jnp.bfloat16)
        qent_grad = jnp.einsum(
            "hqk,khd->qhd",
            score_grad[:, :, word_count:],
            key_rows_h[word_count:],
            preferred_element_type=jnp.float32,
        )
        qent_grad = qent_grad.reshape(seq_len, model_width).astype(jnp.bfloat16)
        keys_grad = jnp.concatenate(
            [
                jnp.einsum(
                    "hqk,qhd->khd",
                    score_grad[:, :, :word_count],
                    query_word_h,
                    preferred_element_type=jnp.float32,
                ),
                jnp.einsum(
                    "hqk,qhd->khd",
                    score_grad[:, :, word_count:],
                    query_entity_h,
                    preferred_element_type=jnp.float32,
                ),
            ],
            axis=0,
        )
        keys_grad = keys_grad.reshape(seq_len, model_width).astype(jnp.bfloat16)
        query_ww_grad = query_scale * dot_left_t(word_part, qword_grad[:word_count])
        query_ew_grad = query_scale * dot_left_t(entity_part, qword_grad[word_count:])
        query_we_grad = query_scale * dot_left_t(word_part, qent_grad[:word_count])
        query_ee_grad = query_scale * dot_left_t(entity_part, qent_grad[word_count:])
        key_weight_grad = dot_left_t(hidden_low, keys_grad)
        value_weight_grad = dot_left_t(hidden_low, values_grad)
        word_back = query_scale * (
            dot_right_t(qword_grad[:word_count], query_ww)
            + dot_right_t(qent_grad[:word_count], query_we)
        )
        entity_back = query_scale * (
            dot_right_t(qword_grad[word_count:], query_ew)
            + dot_right_t(qent_grad[word_count:], query_ee)
        )
        hidden_grad = (
            first_grad
            + jnp.concatenate([word_back, entity_back], axis=0)
            + dot_right_t(keys_grad, key_weight)
            + dot_right_t(values_grad, value_weight)
        )
        words_grad = hidden_grad[:word_count].astype(jnp.bfloat16)
        state_low = hidden_grad[word_count:].astype(jnp.bfloat16)
        dense_grad = dot_left_t(entity_low, state_low)
        entity_vec_grad = dot_right_t(state_low, entity_dense)
    vec_grad = jnp.concatenate([entity_vec_grad, target_grad], axis=0)
    bias_vec_grad = jnp.concatenate(
        [jnp.zeros((slot_count,), jnp.float32), jnp.full((mask_count,), -grad_scale, jnp.float32)]
    )
    placing_f32 = placing.astype(jnp.float32)
    per_request = dot_exact(placing_f32.T, vec_grad)
    bias_request = dot_exact(placing_f32.T, bias_vec_grad[:, None])[:, 0]
    back_block = jnp.concatenate(
        [
            per_request.reshape(devices, capacity, emb_width).astype(jnp.bfloat16),
            jnp.broadcast_to(
                bias_request.reshape(devices, capacity, 1).astype(jnp.bfloat16),
                (devices, capacity, 128),
            ),
        ],
        axis=2,
    )
    back_block = direct_swap(jnp.pad(back_block, ((0, 0), (0, cap_room), (0, 0))), 5)
    back_rows = back_block[:, :capacity, :emb_width].astype(jnp.float32)
    back_bias = back_block[:, :capacity, emb_width].astype(jnp.float32)
    flat_ids = asked_ids.reshape(devices * capacity)
    table_grad = table_grad + jax.ops.segment_sum(
        back_rows.reshape(devices * capacity, emb_width), flat_ids, num_segments=table_rows
    )
    bias_grad = bias_grad + jax.ops.segment_sum(
        back_bias.reshape(devices * capacity), flat_ids, num_segments=table_rows
    )
    vectors = [
        head_gain_grad,
        head_bias_grad,
        norm2_gain_grad,
        norm2_bias_grad,
        norm1_gain_grad,
        norm1_bias_grad,
    ]
    cuts = [vector.reshape(devices, -1) for vector in vectors]
    spots = [0]
    for cut in cuts:
        spots.append(spots[-1] + cut.shape[1])
    block = jnp.concatenate(cuts, axis=1)
    block = jnp.pad(block, ((0, 0), (0, 128 - spots[-1])))[:, None, :]
    vector_sums = jnp.sum(direct_swap(jnp.pad(block, ((0, 0), (0, 7), (0, 0))), 6)[:, 0], axis=0)
    vector_out = [vector_sums[spots[i] : spots[i + 1]] for i in range(len(cuts))]
    if fused:
        all_sums = (
            head_a[0],
            vector_out[0],
            vector_out[1],
            vector_out[2],
            vector_out[3],
            up_sum,
            down_sum,
            vector_out[4],
            vector_out[5],
            down_a[3],
            q_word[0],
            q_word[1],
            q_ent[0],
            q_ent[1],
            key_value[0],
            key_value[1],
            dense_a[0],
        )
    else:
        sums = sum_all(
            [
                [up_weight_grad, out_weight_grad, head_weight_grad],
                [down_grad, query_ww_grad, dense_grad],
                [query_we_grad, query_ew_grad, query_ee_grad, key_weight_grad, value_weight_grad],
            ],
            7,
        )
        all_sums = (
            sums[0][2],
            vector_out[0],
            vector_out[1],
            vector_out[2],
            vector_out[3],
            sums[0][0],
            sums[1][0],
            vector_out[4],
            vector_out[5],
            sums[0][1],
            sums[1][1],
            sums[2][0],
            sums[2][1],
            sums[2][2],
            sums[2][3],
            sums[2][4],
            sums[1][2],
        )
    return (
        loss_value,
        layer_out.astype(jnp.bfloat16),
        words_grad,
        table_grad,
        bias_grad,
        all_sums[16],
        all_sums[10],
        all_sums[11],
        all_sums[12],
        all_sums[13],
        all_sums[14],
        all_sums[15],
        all_sums[9],
        all_sums[7],
        all_sums[8],
        all_sums[5],
        all_sums[6],
        all_sums[3],
        all_sums[4],
        all_sums[0],
        all_sums[1],
        all_sums[2],
        mask_loss,
    )


def solution(mesh):
    in_specs = (
        P("dp", None),
        P("dp", None),
        P("dp", None),
        P("dp", None),
        P("dp", None),
        P("dp", None),
        P("dp", None),
        P("dp"),
        P(),
        P(),
        P(),
        P(),
        P(),
        P(),
        P(),
        P(),
        P(),
        P(),
        P(),
        P(),
        P(),
        P(),
        P(),
        P(),
        P(),
        P("dp", None),
    )
    out_specs = (
        P(),
        P("dp", None),
        P("dp", None),
        P("dp", None),
        P("dp"),
        P("dp", None),
        P("dp", None),
        P("dp", None),
        P("dp", None),
        P("dp", None),
        P("dp", None),
        P("dp", None),
        P("dp", None),
        P("dp"),
        P("dp"),
        P("dp", None),
        P("dp", None),
        P("dp"),
        P("dp"),
        P("dp", None),
        P("dp"),
        P("dp"),
        P("dp"),
    )
    return jax.shard_map(body, mesh=mesh, in_specs=in_specs, out_specs=out_specs, check_vma=False)
```

```python
import functools

import jax
import jax.numpy as jnp
from jax import lax
from jax.experimental import pallas as pl
from jax.experimental.pallas import tpu as pltpu
from jax.sharding import PartitionSpec as P

MESH_ID = pl.DeviceIdType.MESH

HD = 64


EPSILON = 1e-05
MASKED = -1000000000.0


def dot_plain(left_side, right_side):
    return jnp.dot(left_side, right_side, preferred_element_type=jnp.float32)


def dot_left_t(left_side, right_side):
    return lax.dot_general(
        left_side, right_side, (((0,), (0,)), ((), ())), preferred_element_type=jnp.float32
    )


def dot_right_t(left_side, right_side):
    return lax.dot_general(
        left_side, right_side, (((1,), (1,)), ((), ())), preferred_element_type=jnp.float32
    )


def dot_exact(left_side, right_side):
    return jnp.dot(
        left_side, right_side, precision=lax.Precision.HIGHEST, preferred_element_type=jnp.float32
    )


def layer_norm(tensor, gain_vec, shift_vec):
    center = tensor - jnp.mean(tensor, axis=-1, keepdims=True)
    spread = jnp.mean(center * center, axis=-1, keepdims=True)
    return center * lax.rsqrt(spread + EPSILON) * gain_vec + shift_vec


def gelu_exact(tensor):
    return jax.nn.gelu(tensor, approximate=False)


def head_act(tensor, gain_vec, shift_vec):
    return layer_norm(gelu_exact(tensor), gain_vec, shift_vec)


def norm_back(tensor, gain_vec, shift_vec, grad_out):
    result, pullback = jax.vjp(layer_norm, tensor, gain_vec, shift_vec)
    return pullback(grad_out)


def attn_scores(query_word, query_entity, key_rows, allowed, word_count):
    to_words = jnp.einsum(
        "qhd,khd->hqk", query_word, key_rows[:word_count], preferred_element_type=jnp.float32
    )
    to_entities = jnp.einsum(
        "qhd,khd->hqk", query_entity, key_rows[word_count:], preferred_element_type=jnp.float32
    )
    return jnp.where(allowed[None], jnp.concatenate([to_words, to_entities], axis=2), MASKED)


def greet_all(me, devices):
    barrier = pltpu.get_barrier_semaphore()

    def greet(step, carry):
        pl.semaphore_signal(
            barrier, inc=1, device_id=(lax.rem(me + step, devices),), device_id_type=MESH_ID
        )
        return carry

    lax.fori_loop(1, devices, greet, 0)
    pl.semaphore_wait(barrier, devices - 1)


def swap_kernel(devices, gather, source, target, send_sem, recv_sem):
    me = lax.axis_index("dp")
    greet_all(me, devices)

    def piece(step):
        peer = lax.rem(me + step, devices)
        return pltpu.make_async_remote_copy(
            src_ref=source if gather else source.at[peer],
            dst_ref=target.at[me],
            send_sem=send_sem.at[step],
            recv_sem=recv_sem.at[step],
            device_id=(peer,),
            device_id_type=MESH_ID,
        )

    def begin(step, carry):
        piece(step).start()
        return carry

    def finish(step, carry):
        piece(step).wait()
        return carry

    lax.fori_loop(1, devices, begin, 0)
    target[me] = source[...] if gather else source[me]
    lax.fori_loop(1, devices, finish, 0)


def direct_swap(value, collective_id, gather=False):
    devices = lax.axis_size("dp")
    shape = (devices,) + value.shape if gather else value.shape
    return pl.pallas_call(
        functools.partial(swap_kernel, devices, gather),
        out_shape=jax.ShapeDtypeStruct(shape, value.dtype),
        in_specs=[pl.BlockSpec(memory_space=pltpu.VMEM)],
        out_specs=pl.BlockSpec(memory_space=pltpu.VMEM),
        scratch_shapes=[
            pltpu.SemaphoreType.DMA((devices,)),
            pltpu.SemaphoreType.DMA((devices,)),
        ],
        compiler_params=pltpu.CompilerParams(collective_id=collective_id, has_side_effects=True),
    )(value)


def stage_masks(devices):
    if devices == 32:
        axes = [[2], [4], [8, 16]]
    elif devices == 128:
        axes = [[2, 4], [8, 16], [32, 64]]
    else:
        axes = [[2**bit] for bit in range(1, devices.bit_length() - 1)]
        axes = axes + [[] for _ in range(3 - len(axes))]
    first, second, third = axes[0], axes[1], sum(axes[2:], [])
    return (
        [1] + first + second + third,
        [1] + second + first + third,
        [1] + third + first + second,
    )


def sum_kernel(masks, rows, *refs):
    parts = len(masks)
    stages = len(masks[0])
    sources, results = refs[:parts], refs[parts : 2 * parts]
    landing = refs[2 * parts : 3 * parts]
    send_sem, recv_sem = refs[3 * parts :]
    me = lax.axis_index("dp")
    barrier = pltpu.get_barrier_semaphore()
    partner_of = {}
    for mask in masks[0]:
        bit = lax.rem(lax.div(me, mask), 2)
        partner_of[mask] = (me + mask - 2 * mask * bit, bit)
    for mask in masks[0]:
        pl.semaphore_signal(
            barrier, inc=1, device_id=(partner_of[mask][0],), device_id_type=MESH_ID
        )
    pl.semaphore_wait(barrier, stages)
    sizes = [[rows[part] * 2 ** (stages - 1 - stage) for stage in range(stages)] for part in range(parts)]
    places = [[sum(size[:stage]) for stage in range(stages)] for size in sizes]

    def launch(part, stage):
        partner, bit = partner_of[masks[part][stage]]
        size = sizes[part][stage]
        away = (1 - bit) * size
        copy = pltpu.make_async_remote_copy(
            src_ref=sources[part].at[pl.ds(away, size)]
            if stage == 0
            else landing[part].at[pl.ds(places[part][stage - 1] + away, size)],
            dst_ref=landing[part].at[pl.ds(places[part][stage], size)],
            send_sem=send_sem.at[part, stage],
            recv_sem=recv_sem.at[part, stage],
            device_id=(partner,),
            device_id_type=MESH_ID,
        )
        copy.start()
        return copy

    flying = [launch(part, 0) for part in range(parts)]

    def add_rows(part, stage, start, count):
        keep = partner_of[masks[part][stage]][1] * sizes[part][stage] + start
        last = stage == stages - 1

        def step(index, carry):
            theirs = pl.ds(pl.multiple_of(places[part][stage] + start + index * 16, 16), 16)
            if stage == 0:
                mine = sources[part][pl.ds(pl.multiple_of(keep + index * 16, 16), 16)]
            else:
                mine = landing[part][
                    pl.ds(pl.multiple_of(places[part][stage - 1] + keep + index * 16, 16), 16)
                ]
            total = mine.astype(jnp.float32) + landing[part][theirs].astype(jnp.float32)
            if last:
                results[part][pl.ds(pl.multiple_of(index * 16, 16), 16)] = total
            else:
                landing[part][theirs] = total.astype(jnp.bfloat16)
            return carry

        lax.fori_loop(0, count // 16, step, 0, unroll=min(4, count // 16))

    for stage in range(stages):
        for part in range(parts):
            flying[part].wait()
            if stage == stages - 1:
                add_rows(part, stage, 0, sizes[part][stage])
                continue
            bit = partner_of[masks[part][stage + 1]][1]
            half = sizes[part][stage] // 2
            add_rows(part, stage, (1 - bit) * half, half)
            flying[part] = launch(part, stage + 1)
            add_rows(part, stage, bit * half, half)


def sum_scatter(parts, collective_id):
    devices = lax.axis_size("dp")
    masks = stage_masks(devices)
    rows = [part.shape[1] for part in parts]
    width = parts[0].shape[2]
    bits = devices.bit_length() - 1
    ordered = []
    for part, order in zip(parts, masks):
        view = part.reshape((2,) * bits + part.shape[1:])
        places = [bits - mask.bit_length() for mask in order]
        view = view.transpose(tuple(places) + (bits, bits + 1))
        ordered.append(view.reshape(devices * part.shape[1], width))
    return pl.pallas_call(
        functools.partial(sum_kernel, masks, rows),
        out_shape=[jax.ShapeDtypeStruct((count, width), jnp.float32) for count in rows],
        in_specs=[pl.BlockSpec(memory_space=pltpu.VMEM)] * len(parts),
        out_specs=[pl.BlockSpec(memory_space=pltpu.VMEM)] * len(parts),
        scratch_shapes=[pltpu.VMEM((devices * count, width), jnp.bfloat16) for count in rows]
        + [pltpu.SemaphoreType.DMA((len(parts), bits)), pltpu.SemaphoreType.DMA((len(parts), bits))],
        input_output_aliases={},
        compiler_params=pltpu.CompilerParams(
            collective_id=collective_id, has_side_effects=True, vmem_limit_bytes=56 * 2**20
        ),
    )(*ordered)


def by_owner(grad, width):
    devices = lax.axis_size("dp")
    rows = grad.shape[0] // devices
    blocks = grad.astype(jnp.bfloat16).reshape(devices, rows, grad.shape[1])
    if grad.shape[1] > width:
        cuts = grad.shape[1] // width
        return jnp.concatenate(jnp.split(blocks, cuts, axis=2), axis=1)
    if grad.shape[1] < width:
        return blocks.reshape(devices, rows * grad.shape[1] // width, width)
    return blocks


def from_owner(rows, shape):
    devices = lax.axis_size("dp")
    count, width = shape[0] // devices, shape[1]
    if width > rows.shape[1]:
        return jnp.concatenate(jnp.split(rows, width // rows.shape[1], axis=0), axis=1)
    return rows.reshape(count, width)


def sum_all(groups, collective_id):
    width = groups[0][0].shape[1]
    width = min(grad.shape[1] for group in groups for grad in group if grad.shape[1] >= 768)
    devices = lax.axis_size("dp")
    packed = []
    for group in groups:
        pieces = [by_owner(grad, width) for grad in group]
        count = sum(piece.shape[1] for piece in pieces)
        room = -(-count // 16) * 16 - count
        if room:
            pieces.append(jnp.zeros((devices, room, width), jnp.bfloat16))
        packed.append(jnp.concatenate(pieces, axis=1))
    sums = sum_scatter(packed, collective_id)
    results = []
    for group, total in zip(groups, sums):
        place, outs = 0, []
        for grad in group:
            count = grad.shape[0] // devices * grad.shape[1] // width
            outs.append(from_owner(total[place : place + count], grad.shape))
            place += count
        results.append(outs)
    return results


def place_owner(order, place):
    bits = len(order)
    return sum(((place >> (bits - 1 - spot)) & 1) * mask for spot, mask in enumerate(order))


class Piece:
    def __init__(self, rows, stages, send, own, land, tail, tail_land, out, send_sem, recv_sem):
        self.rows, self.stages = rows, stages
        self.send, self.own, self.land = send, own, land
        self.tail, self.tail_land, self.out = tail, tail_land, out
        self.send_sem, self.recv_sem = send_sem, recv_sem
        self.sizes = [rows * 2 ** (stages - 1 - stage) for stage in range(stages)]
        self.spots = [sum(self.sizes[:stage]) for stage in range(stages)]

    def copy(self, stage, partner, bit):
        size = self.sizes[stage]
        away = pl.multiple_of((1 - bit) * size, 8 if stage == self.stages - 1 else 16)
        if stage == 0:
            source, target = self.send.at[:, pl.ds(away, size)], self.land.at[:, pl.ds(0, size)]
        elif stage < self.stages - 1:
            spot = pl.multiple_of(self.spots[stage - 1] + away, 16)
            source = self.land.at[:, pl.ds(spot, size)]
            target = self.land.at[:, pl.ds(self.spots[stage], size)]
        else:
            source, target = self.tail.at[:, pl.ds(away, size)], self.tail_land
        return pltpu.make_async_remote_copy(
            src_ref=source,
            dst_ref=target,
            send_sem=self.send_sem.at[stage],
            recv_sem=self.recv_sem.at[stage],
            device_id=(partner,),
            device_id_type=MESH_ID,
        )

    def held(self, stage, bit):
        size = self.sizes[stage]
        if stage == 0 and self.own is not None:
            return self.own, 0
        if stage == 0:
            return self.send, pl.multiple_of(bit * size, 16)
        return self.land, pl.multiple_of(self.spots[stage - 1] + bit * size, 16)

    def add(self, stage, bit, half_index):
        size = self.sizes[stage]
        half = size // 2
        unit = 48 if half % 48 == 0 else 16
        start = half_index * half
        source, base = self.held(stage, bit)
        for slot in range(self.land.shape[0]):

            def step(index, carry, slot=slot):
                row = pl.multiple_of(start + index * unit, 16)
                mine = source[slot, pl.ds(pl.multiple_of(base + row, 16), unit)]
                spot = pl.ds(pl.multiple_of(self.spots[stage] + row, 16), unit)
                theirs = self.land[slot, spot]
                total = mine.astype(jnp.float32) + theirs.astype(jnp.float32)
                self.land[slot, spot] = total.astype(jnp.bfloat16)
                return carry

            lax.fori_loop(0, half // unit, step, 0)

    def add_tail(self, stage, bit):
        size = self.sizes[stage]
        source, base = self.held(stage, bit)
        for slot in range(self.land.shape[0]):
            mine = source[slot, pl.ds(base, size)]
            theirs = self.land[slot, pl.ds(self.spots[stage], size)]
            self.tail[slot] = mine.astype(jnp.float32) + theirs.astype(jnp.float32)

    def finish(self, bit):
        size = self.sizes[-1]
        for slot in range(self.out.shape[0]):
            mine = self.tail[slot, pl.ds(pl.multiple_of(bit * size, 8), size)]
            self.out[slot] = mine + self.tail_land[slot]


class Stream:
    def __init__(self, order, partner_of, pieces):
        self.order, self.partner_of, self.pieces = order, partner_of, pieces
        self.stages = len(order)

    def launch(self, stage):
        partner, bit = self.partner_of[self.order[stage]]
        for piece in self.pieces:
            piece.copy(stage, partner, bit).start()

    def advance(self, stage):
        partner, bit = self.partner_of[self.order[stage]]
        for piece in self.pieces:
            piece.copy(stage, partner, bit).wait()
        if stage == self.stages - 1:
            for piece in self.pieces:
                piece.finish(bit)
        elif stage == self.stages - 2:
            for piece in self.pieces:
                piece.add_tail(stage, bit)
            self.launch(stage + 1)
        else:
            following = self.partner_of[self.order[stage + 1]][1]
            for piece in self.pieces:
                piece.add(stage, bit, 1 - following)
            self.launch(stage + 1)
            for piece in self.pieces:
                piece.add(stage, bit, following)


def partners(me, masks):
    result = {}
    for mask in masks:
        bit = lax.rem(lax.div(me, mask), 2)
        result[mask] = (me + mask - 2 * mask * bit, bit)
    return result


def greet_partners(partner_of):
    barrier = pltpu.get_barrier_semaphore()
    for partner, _ in partner_of.values():
        pl.semaphore_signal(barrier, inc=1, device_id=(partner,), device_id_type=MESH_ID)
    pl.semaphore_wait(barrier, len(partner_of))


EARLY = ((0, 3, 24, 768), (0, 1, 24, 256), (1, 4, 24, 768), (2, 2, 24, 768))
LATE = ((0, 2, 24, 768), (0, 1, 8, 768), (1, 2, 24, 768), (2, 2, 24, 768))


def piece_scratch(spec, stages, source, own):
    _, slots, rows, width = spec
    owners = 2**stages
    shapes = []
    if source:
        shapes.append(pltpu.VMEM((slots, rows * owners, width), jnp.bfloat16))
    if own:
        shapes.append(pltpu.VMEM((slots, rows * owners // 2, width), jnp.bfloat16))
    shapes += [
        pltpu.VMEM((slots, rows * (owners - 2), width), jnp.bfloat16),
        pltpu.VMEM((slots, 2 * rows, width), jnp.float32),
        pltpu.VMEM((slots, rows, width), jnp.float32),
        pltpu.SemaphoreType.DMA((stages,)),
        pltpu.SemaphoreType.DMA((stages,)),
    ]
    return shapes


def attention_back_kernel(orders, *refs):
    stages = len(orders[0])
    refs = list(refs)

    def take(count):
        taken = refs[:count]
        del refs[:count]
        return taken

    early_send = take(len(EARLY))
    (hidden, qword, qent, keys, values, cgrad, feat_q, feat_k, lse_delta, first_grad) = take(10)
    (w_ww, w_we, w_ew, w_ee, w_key, w_value, dense, entity_low) = take(8)
    early_out = take(len(EARLY))
    late_out = take(len(LATE))
    words_out, dent_out = take(2)
    early_pieces = []
    own_copies = []
    me = lax.axis_index("dp")
    partner_of = partners(me, orders[0])
    own_sem = refs.pop()
    word_weights = []
    dqw, dqe, dkey, dvalue, prob_s, grad_s, flip, hidden_t, hidden_te, entity_t = refs[-10:]
    del refs[-10:]
    early = [[], [], []]
    for index, spec in enumerate(EARLY):
        own, land, tail, tail_land, send_sem, recv_sem = take(6)
        early[spec[0]].append(
            Piece(
                spec[2], stages, early_send[index], own, land, tail, tail_land,
                early_out[index], send_sem, recv_sem,
            )
        )
        bit = partner_of[orders[spec[0]][0]][1]
        size = spec[2] * 2 ** (stages - 1)
        own_copies.append(
            pltpu.make_async_copy(
                early_send[index].at[:, pl.ds(pl.multiple_of(bit * size, 16), size)],
                own,
                own_sem.at[index],
            )
        )
    late, late_source = [[], [], []], []
    for index, spec in enumerate(LATE):
        source, land, tail, tail_land, send_sem, recv_sem = take(6)
        late_source.append(source)
        late[spec[0]].append(
            Piece(
                spec[2], stages, source, None, land, tail, tail_land,
                late_out[index], send_sem, recv_sem,
            )
        )
    spare = early[1][0].own
    half_rows = w_ww.shape[0] // 2
    for index, weight in enumerate((w_ww, w_we)):
        for part in range(2):
            word_weights.append(
                pltpu.make_async_copy(
                    weight.at[pl.ds(part * half_rows, half_rows)],
                    spare.at[2 * index + part],
                    own_sem.at[len(EARLY) + 2 * index + part],
                )
            )
    early = [Stream(orders[i], partner_of, early[i]) for i in range(3)]
    late = [Stream(orders[i], partner_of, late[i]) for i in range(3)]

    greet_partners(partner_of)
    for stream in early:
        stream.launch(0)
    for copy in own_copies:
        copy.start()

    width = hidden.shape[1]
    seq_len = hidden.shape[0]
    words = words_out.shape[0]
    block = 128
    lane = lax.broadcasted_iota(jnp.int32, (1, block), 1)
    low_half = (lane < HD).astype(jnp.float32).astype(jnp.bfloat16)
    high_half = (lane >= HD).astype(jnp.float32).astype(jnp.bfloat16)
    halves = (low_half, high_half)

    def flip_step(index, carry):
        at = pl.ds(pl.multiple_of(index * block, block), block)
        flip[at] = hidden[:, at].astype(jnp.float32).T
        return carry

    lax.fori_loop(0, width // block, flip_step, 0)
    owners = 2**stages
    rows = width // owners
    for slot, order in enumerate(orders):
        begin = words if slot == 2 else 0
        for pair in range(owners // 2):
            one, two = place_owner(order, 2 * pair), place_owner(order, 2 * pair + 1)
            both = jnp.concatenate(
                [flip[one * rows : one * rows + rows, begin:], flip[two * rows : two * rows + rows, begin:]],
                axis=0,
            ).astype(jnp.bfloat16)
            if slot == 2:
                hidden_te[pair * 2 * rows : (pair + 1) * 2 * rows] = both
            else:
                hidden_t[slot, pair * 2 * rows : (pair + 1) * 2 * rows] = both

    def pair_step(pair, carry):
        lanes = pl.ds(pl.multiple_of(pair * block, block), block)
        key_pair = keys[:, lanes]
        value_pair = values[:, lanes]
        key_feat = [key_pair * halves[h] + feat_k[...] * halves[1 - h] for h in range(2)]
        key_only = [key_pair * halves[h] for h in range(2)]
        value_only = [value_pair * halves[h] for h in range(2)]

        def row_step(index, inner):
            at = pl.ds(pl.multiple_of(index * block, block), block)
            qw = qword[at, lanes]
            qe = qent[at, lanes]
            feats = feat_q[at]
            given = cgrad[at, lanes]
            stats = lse_delta[at]
            spot = lax.broadcasted_iota(jnp.int32, (1, block), 1) - 4 * pair
            total_w = jnp.zeros((block, block), jnp.float32)
            total_e = jnp.zeros((block, block), jnp.float32)
            for h in range(2):
                left_w = qw * halves[h] + feats * halves[1 - h]
                left_e = qe * halves[h] + feats * halves[1 - h]
                scores = jnp.concatenate(
                    [
                        dot_right_t(left_w, key_feat[h][:words]),
                        dot_right_t(left_e, key_feat[h][words:]),
                    ],
                    axis=1,
                )
                prob = jnp.exp(scores - jnp.sum(jnp.where(spot == h, stats, 0.0), axis=1, keepdims=True))
                pgrad = dot_right_t(given, value_only[h])
                sgrad = (prob * (pgrad - jnp.sum(jnp.where(spot == 2 + h, stats, 0.0), axis=1, keepdims=True))).astype(jnp.bfloat16)
                prob_s[h, at] = prob.astype(jnp.bfloat16)
                grad_s[h, at] = sgrad
                total_w += dot_plain(sgrad[:, :words], key_only[h][:words])
                total_e += dot_plain(sgrad[:, words:], key_only[h][words:])
            dqw[at, lanes] = total_w.astype(jnp.bfloat16)
            dqe[at, lanes] = total_e.astype(jnp.bfloat16)
            return inner

        lax.fori_loop(0, seq_len // block, row_step, 0)
        qw_all, qe_all, given_all = qword[:, lanes], qent[:, lanes], cgrad[:, lanes]
        dkey[:words, lanes] = (
            dot_left_t(grad_s[0, :, :words], qw_all * halves[0])
            + dot_left_t(grad_s[1, :, :words], qw_all * halves[1])
        ).astype(jnp.bfloat16)
        dkey[words:, lanes] = (
            dot_left_t(grad_s[0, :, words:], qe_all * halves[0])
            + dot_left_t(grad_s[1, :, words:], qe_all * halves[1])
        ).astype(jnp.bfloat16)
        dvalue[:, lanes] = (
            dot_left_t(prob_s[0], given_all * halves[0])
            + dot_left_t(prob_s[1], given_all * halves[1])
        ).astype(jnp.bfloat16)

        @pl.when(pair == 2)
        def _():
            for copy in own_copies:
                copy.wait()
            for stream in early:
                stream.advance(0)
            for copy in word_weights:
                copy.start()

        return carry

    lax.fori_loop(0, width // block, pair_step, 0)

    query_scale = HD ** (-0.5)
    column = 384

    def weight_grad(source, slot, order_slot, grad, begin, end, scale):
        for cut in range(0, width, column):
            left = hidden_te[...] if order_slot == 2 else hidden_t[order_slot, :, begin:end]
            piece = dot_plain(left, grad[begin:end, cut : cut + column])
            if scale:
                piece = piece * query_scale
            source[slot, :, cut : cut + column] = piece.astype(jnp.bfloat16)

    weight_grad(late_source[2], 0, 1, dkey, 0, seq_len, False)
    weight_grad(late_source[2], 1, 1, dvalue, 0, seq_len, False)
    late[1].launch(0)
    for stream in early:
        stream.advance(1)
    weight_grad(late_source[3], 0, 2, dqw, words, seq_len, True)
    weight_grad(late_source[3], 1, 2, dqe, words, seq_len, True)
    late[2].launch(0)

    def spare_weight(index):
        return spare[2 * index : 2 * index + 2].reshape(width, width)

    def data_grad(begin, size, word_w, ent_w):
        at = pl.ds(begin, size)
        queries = dot_right_t(dqw[at], word_w()) + dot_right_t(dqe[at], ent_w())
        return (
            first_grad[at]
            + query_scale * queries
            + dot_right_t(dkey[at], w_key[...])
            + dot_right_t(dvalue[at], w_value[...])
        )

    state_low = data_grad(words, seq_len - words, lambda: w_ew[...], lambda: w_ee[...]).astype(jnp.bfloat16)
    dent_out[...] = dot_right_t(state_low, dense[...])
    entity_width = dense.shape[0]
    few = entity_width // owners
    for cut in range(0, entity_width, block):
        flip[cut : cut + block, :block] = entity_low[:, cut : cut + block].astype(jnp.float32).T
    for pair in range(owners // 2):
        one, two = place_owner(orders[0], 2 * pair), place_owner(orders[0], 2 * pair + 1)
        both = jnp.concatenate(
            [flip[one * few : one * few + few, :block], flip[two * few : two * few + few, :block]],
            axis=0,
        )
        entity_t[pair * 2 * few : (pair + 1) * 2 * few] = both.astype(jnp.bfloat16)
    late_source[1][0] = dot_plain(entity_t[...], state_low).astype(jnp.bfloat16)
    weight_grad(late_source[0], 0, 0, dqw, 0, words, True)
    weight_grad(late_source[0], 1, 0, dqe, 0, words, True)
    late[0].launch(0)
    for stream in early:
        stream.advance(2)

    for copy in word_weights:
        copy.wait()

    def word_step(index, carry):
        begin = pl.multiple_of(index * block, block)
        words_out[pl.ds(begin, block)] = data_grad(begin, block, lambda: spare_weight(0), lambda: spare_weight(1)).astype(jnp.bfloat16)
        return carry

    lax.fori_loop(0, words // block, word_step, 0)
    for turn in ((late[1], 0), (late[2], 0), (late[0], 0)):
        turn[0].advance(turn[1])
    for stream in early:
        stream.advance(3)
    for stream in late:
        stream.advance(1)
    for stream in early:
        stream.advance(4)
    for stage in (2, 3, 4):
        for stream in late:
            stream.advance(stage)


def in_order(grad, order):
    bits = len(order)
    owners = 2**bits
    view = grad.reshape((2,) * bits + (grad.shape[0] // owners, grad.shape[1]))
    spots = tuple(bits - mask.bit_length() for mask in order)
    return view.transpose(spots + (bits, bits + 1)).reshape(grad.shape)


def attention_back(early_grads, inputs, weights, collective_id):
    devices = lax.axis_size("dp")
    orders = stage_masks(devices)
    stages = len(orders[0])
    hidden = inputs[0]
    seq_len, width = hidden.shape
    slots = weights[-1].shape[0]
    words = seq_len - slots
    outs = [
        jax.ShapeDtypeStruct((count, rows, wide), jnp.float32)
        for _, count, rows, wide in EARLY + LATE
    ] + [
        jax.ShapeDtypeStruct((words, width), jnp.bfloat16),
        jax.ShapeDtypeStruct((slots, weights[-2].shape[0]), jnp.float32),
    ]
    scratch = []
    for spec in EARLY:
        scratch += piece_scratch(spec, stages, False, True)
    for spec in LATE:
        scratch += piece_scratch(spec, stages, True, False)
    scratch += [pltpu.VMEM((seq_len, width), jnp.bfloat16)] * 4
    scratch += [pltpu.VMEM((2, seq_len, seq_len), jnp.bfloat16)] * 2
    scratch += [
        pltpu.VMEM((width, seq_len), jnp.float32),
        pltpu.VMEM((2, width, seq_len), jnp.bfloat16),
        pltpu.VMEM((width, slots), jnp.bfloat16),
        pltpu.VMEM((weights[-2].shape[0], slots), jnp.bfloat16),
        pltpu.SemaphoreType.DMA((len(EARLY) + 4,)),
    ]
    vmem = pl.BlockSpec(memory_space=pltpu.VMEM)
    return pl.pallas_call(
        functools.partial(attention_back_kernel, orders),
        out_shape=outs,
        in_specs=[pl.BlockSpec(memory_space=pltpu.HBM)] * len(EARLY)
        + [vmem] * len(inputs)
        + [pl.BlockSpec(memory_space=pltpu.HBM)] * 2
        + [vmem] * (len(weights) - 2),
        out_specs=[vmem] * len(outs),
        scratch_shapes=scratch,
        compiler_params=pltpu.CompilerParams(
            collective_id=collective_id, has_side_effects=True, vmem_limit_bytes=62 * 2**20
        ),
    )(*early_grads, *inputs, *weights)


def norm_parts(value):
    center = value - jnp.mean(value, axis=-1, keepdims=True)
    spread = jnp.mean(center * center, axis=-1, keepdims=True)
    rate = lax.rsqrt(spread + EPSILON)
    return center * rate, rate


def gelu_parts(value):
    chance = 0.5 + 0.5 * lax.erf(value * (0.5**0.5))
    slope = chance + value * (jnp.exp(-0.5 * value * value) * (0.5 / jnp.pi) ** 0.5)
    return value * chance, slope


def half_lanes(block):
    lane = lax.broadcasted_iota(jnp.int32, (1, block), 1)
    low_half = (lane < HD).astype(jnp.float32).astype(jnp.bfloat16)
    high_half = (lane >= HD).astype(jnp.float32).astype(jnp.bfloat16)
    return low_half, high_half


def forward_kernel(
    word_states,
    entity_low,
    feat_q,
    feat_k,
    choose,
    dense,
    w_ww,
    w_we,
    w_ew,
    w_ee,
    w_key,
    w_value,
    out_hbm,
    gain_one,
    shift_one,
    up_hbm,
    down_hbm,
    gain_two,
    shift_two,
    head_w,
    gain_head,
    shift_head,
    hidden,
    qword,
    qent,
    keys,
    values,
    context,
    lse_out,
    resid_one,
    normed_out,
    active_hbm,
    slope_hbm,
    resid_two,
    layer_low,
    picked_out,
    head_pre_out,
    head_out,
    state_scr,
    normed_scr,
    out_w,
    up_w,
    down_w,
    active,
    slope,
    sems,
):
    loads = [
        pltpu.make_async_copy(source, target, sems.at[index])
        for index, (source, target) in enumerate(
            ((out_hbm, out_w), (up_hbm, up_w), (down_hbm, down_w))
        )
    ]
    for load in loads:
        load.start()
    words, width = word_states.shape
    seq_len = hidden.shape[0]
    slots = seq_len - words
    block = 128
    halves = half_lanes(block)
    query_scale = HD ** (-0.5)
    state_scr[...] = dot_plain(entity_low[...], dense[...])
    hidden[:words] = word_states[...]
    hidden[words:] = state_scr[...].astype(jnp.bfloat16)

    half = width // 2
    for cut in range(0, width, half):
        at = slice(cut, cut + half)
        for target, word_w, ent_w in ((qword, w_ww, w_ew), (qent, w_we, w_ee)):
            target[:words, at] = (query_scale * dot_plain(word_states[...], word_w[:, at])).astype(
                jnp.bfloat16
            )
            target[words:, at] = (query_scale * dot_plain(hidden[words:], ent_w[:, at])).astype(
                jnp.bfloat16
            )
        keys[:, at] = dot_plain(hidden[...], w_key[:, at]).astype(jnp.bfloat16)
        values[:, at] = dot_plain(hidden[...], w_value[:, at]).astype(jnp.bfloat16)
    lse_out[...] = jnp.zeros_like(lse_out)

    def pair_step(pair, carry):
        lanes = pl.ds(pl.multiple_of(pair * block, block), block)
        key_pair = keys[:, lanes]
        value_pair = values[:, lanes]
        key_feat = [key_pair * halves[h] + feat_k[...] * halves[1 - h] for h in range(2)]
        value_only = [value_pair * halves[h] for h in range(2)]
        spot = lax.broadcasted_iota(jnp.int32, (1, block), 1) - 4 * pair

        def row_step(index, inner):
            at = pl.ds(pl.multiple_of(index * block, block), block)
            qw = qword[at, lanes]
            qe = qent[at, lanes]
            feats = feat_q[at]
            result = jnp.zeros((block, block), jnp.float32)
            stats = lse_out[at]
            for h in range(2):
                left_w = qw * halves[h] + feats * halves[1 - h]
                left_e = qe * halves[h] + feats * halves[1 - h]
                scores = jnp.concatenate(
                    [
                        dot_right_t(left_w, key_feat[h][:words]),
                        dot_right_t(left_e, key_feat[h][words:]),
                    ],
                    axis=1,
                )
                top = jnp.max(scores, axis=1, keepdims=True)
                expo = jnp.exp(scores - top)
                total = jnp.sum(expo, axis=1, keepdims=True)
                prob = (expo * (1.0 / total)).astype(jnp.bfloat16)
                result += dot_plain(prob, value_only[h])
                stats = jnp.where(spot == h, top + jnp.log(total), stats)
            context[at, lanes] = result.astype(jnp.bfloat16)
            lse_out[at] = stats
            return inner

        lax.fori_loop(0, seq_len // block, row_step, 0)
        return carry

    lax.fori_loop(0, width // block, pair_step, 0)

    loads[0].wait()
    for begin, size in ((0, words // 2), (words // 2, words // 2), (words, slots)):
        at = slice(begin, begin + size)
        start = (
            state_scr[...] if begin == words else word_states[at].astype(jnp.float32)
        )
        value = start + dot_plain(context[at], out_w[...])
        resid_one[at] = value
        normed = norm_parts(value)[0] * gain_one[...] + shift_one[...]
        normed_scr[at] = normed
        normed_out[at] = normed.astype(jnp.bfloat16)
    loads[1].wait()
    loads[2].wait()
    span = seq_len // 4
    stores = []

    for slot in range(down_w.shape[0] // width):
        cols = slice(slot * width, slot * width + width)

        def up_step(index, carry, cols=cols):
            at = pl.ds(pl.multiple_of(index * span, 16), span)
            result, change = gelu_parts(dot_plain(normed_out[at], up_w[:, cols]))
            active[at, cols] = result.astype(jnp.bfloat16)
            slope[at, cols] = change.astype(jnp.bfloat16)
            return carry

        lax.fori_loop(0, 4, up_step, 0)
        for index, (source, target) in enumerate(((active, active_hbm), (slope, slope_hbm))):
            stores.append(
                pltpu.make_async_copy(
                    source.at[:, cols], target.at[:, cols], sems.at[3 + 2 * slot + index]
                )
            )
            stores[-1].start()

    def down_step(index, carry):
        at = pl.ds(pl.multiple_of(index * span, 16), span)
        value = normed_scr[at] + dot_plain(active[at], down_w[...])
        resid_two[at] = value
        layer_low[at] = (norm_parts(value)[0] * gain_two[...] + shift_two[...]).astype(jnp.bfloat16)
        return carry

    lax.fori_loop(0, 4, down_step, 0)
    picked = dot_plain(choose[...], layer_low[words:]).astype(jnp.bfloat16)
    picked_out[...] = picked
    head_pre = dot_plain(picked, head_w[...])
    head_pre_out[...] = head_pre
    raised = gelu_parts(head_pre)[0]
    head_out[...] = (norm_parts(raised)[0] * gain_head[...] + shift_head[...]).astype(jnp.bfloat16)
    for store in stores:
        store.wait()


def forward_pass(inputs):
    words, width = inputs[0].shape
    slots = inputs[1].shape[0]
    seq_len = words + slots
    hidden_units = inputs[15].shape[1]
    mask_count = inputs[4].shape[0]
    head_width = inputs[19].shape[1]
    low, full = jnp.bfloat16, jnp.float32
    vmem, hbm = pl.BlockSpec(memory_space=pltpu.VMEM), pl.BlockSpec(memory_space=pltpu.HBM)
    far = (12, 15, 16)
    shapes = [
        ((seq_len, width), low),
        ((seq_len, width), low),
        ((seq_len, width), low),
        ((seq_len, width), low),
        ((seq_len, width), low),
        ((seq_len, width), low),
        ((seq_len, 128), full),
        ((seq_len, width), full),
        ((seq_len, width), low),
        ((seq_len, hidden_units), low),
        ((seq_len, hidden_units), low),
        ((seq_len, width), full),
        ((seq_len, width), low),
        ((mask_count, width), low),
        ((mask_count, head_width), full),
        ((mask_count, head_width), low),
    ]
    return pl.pallas_call(
        forward_kernel,
        out_shape=[jax.ShapeDtypeStruct(*shape) for shape in shapes],
        in_specs=[hbm if index in far else vmem for index in range(len(inputs))],
        out_specs=[hbm if index in (9, 10) else vmem for index in range(len(shapes))],
        scratch_shapes=[
            pltpu.VMEM((slots, width), full),
            pltpu.VMEM((seq_len, width), full),
            pltpu.VMEM(inputs[12].shape, low),
            pltpu.VMEM(inputs[15].shape, low),
            pltpu.VMEM(inputs[16].shape, low),
            pltpu.VMEM((seq_len, hidden_units), low),
            pltpu.VMEM((seq_len, hidden_units), low),
            pltpu.SemaphoreType.DMA((16,)),
        ],
        compiler_params=pltpu.CompilerParams(vmem_limit_bytes=60 * 2**20),
    )(*inputs)


class Grid:
    def __init__(self):
        me = lax.axis_index("dp")
        self.core = lax.rem(me, 2)
        self.square = lax.rem(lax.div(me, 2), 4)
        self.line = lax.div(me, 8)
        self.twin = me + 1 - 2 * self.core
        self.squares = []
        self.lines = []
        for step in range(1, 4):
            other = lax.rem(self.square + step, 4)
            self.squares.append((me + 2 * (other - self.square), other))
            other = lax.rem(self.line + step, 4)
            self.lines.append((me + 8 * (other - self.line), other))

    def greet(self):
        barrier = pltpu.get_barrier_semaphore()
        peers = [self.twin] + [peer for peer, _ in self.squares + self.lines]
        for peer in peers:
            pl.semaphore_signal(barrier, inc=1, device_id=(peer,), device_id_type=MESH_ID)
        pl.semaphore_wait(barrier, len(peers))


class Sender:
    def __init__(self, send_sem, recv_sem):
        self.send_sem, self.recv_sem, self.used = send_sem, recv_sem, 0

    def start(self, source, target, peer):
        slot = self.used
        self.used += 1
        copy = pltpu.make_async_remote_copy(
            src_ref=source,
            dst_ref=target,
            send_sem=self.send_sem.at[slot],
            recv_sem=self.recv_sem.at[slot],
            device_id=(peer,),
            device_id_type=MESH_ID,
        )
        copy.start()
        return copy


def wait_all(copies):
    for copy in copies:
        copy.wait()


def merge_stats(blocks):
    tops = [block[0] for block in blocks]
    top = functools.reduce(jnp.maximum, tops)
    total = sum(block[1] * jnp.exp(block[0] - top) for block in blocks)
    return top, total


def head_kernel(
    grad_scale,
    head,
    table,
    bias,
    table_grad,
    bias_grad,
    lse_out,
    head_grad,
    heads,
    logits,
    expo,
    table_t,
    bias_col,
    part,
    land_pair,
    sum_pair,
    land_square,
    sum_square,
    land_line,
    stat,
    stat_pair,
    stat_square,
    stat_line,
    send_sem,
    recv_sem,
):
    grid = Grid()
    rows, wide = table.shape
    count = head.shape[0]
    total_mask = 32 * count
    grid.greet()
    sender = Sender(send_sem, recv_sem)
    line, square, core = grid.line, grid.square, grid.core
    flying = [sender.start(head, heads.at[line, square, core], peer) for peer, _ in grid.lines]
    heads[line, square, core] = head[...]

    def table_step(index, carry):
        at = pl.ds(pl.multiple_of(index * 128, 128), 128)
        table_t[:, at] = table[at].astype(jnp.float32).T.astype(jnp.bfloat16)
        return carry

    lax.fori_loop(0, rows // 128, table_step, 0)
    wait_all(flying)
    flying = [
        sender.start(heads.at[:, square, core], heads.at[:, square, core], peer)
        for peer, _ in grid.squares
    ]

    def bias_step(index, carry):
        at = pl.ds(pl.multiple_of(index * 128, 128), 128)
        bias_col[at] = jnp.broadcast_to(bias[:, at], (128, 128)).T
        return carry

    lax.fori_loop(0, rows // 128, bias_step, 0)
    wait_all(flying)
    sender.start(heads.at[:, :, core], heads.at[:, :, core], grid.twin).wait()

    all_heads = heads[...].reshape(total_mask, wide)
    slab = rows // 8

    def logit_step(index, carry):
        at = pl.ds(pl.multiple_of(index * slab, 16), slab)
        logits[at] = dot_right_t(table[at], all_heads)
        return carry

    lax.fori_loop(0, 8, logit_step, 0)
    tile = 64
    wide_copies = total_mask // 128

    def value_at(index):
        at = pl.ds(pl.multiple_of(index * tile, tile), tile)
        shift = bias_col[at]
        return at, logits[at] + jnp.concatenate([shift] * wide_copies, axis=1)

    def top_step(index, top):
        at, value = value_at(index)
        return jnp.maximum(top, jnp.max(value.reshape(tile // 8, 8, total_mask), axis=0))

    top = lax.fori_loop(
        0, rows // tile, top_step, jnp.full((8, total_mask), -jnp.inf, jnp.float32)
    )
    top = jnp.max(top, axis=0, keepdims=True)

    def exp_step(index, total):
        at, value = value_at(index)
        value = jnp.exp(value - top)
        expo[at] = value.astype(jnp.bfloat16)
        return total + jnp.sum(value.reshape(tile // 8, 8, total_mask), axis=0)

    total = lax.fori_loop(0, rows // tile, exp_step, jnp.zeros((8, total_mask), jnp.float32))
    total = jnp.sum(total, axis=0, keepdims=True)

    def fold(row):
        return jnp.concatenate([row[:, i * 128 : i * 128 + 128] for i in range(wide_copies)], axis=0)

    def unfold(block):
        return jnp.concatenate([block[i : i + 1] for i in range(wide_copies)], axis=1)

    own_top, own_total = fold(top), fold(total)
    stat[0, 0], stat[0, 1] = own_top, own_total
    copy = sender.start(stat.at[0], stat_pair, grid.twin)
    quarter = total_mask // 4
    parts = [dot_plain(table_t[...], expo[:, :quarter])]
    copy.wait()
    stat[1, 0], stat[1, 1] = merge_stats(
        [(own_top, own_total), (stat_pair[0], stat_pair[1])]
    )
    stat_square[square] = stat[1]
    flying = [sender.start(stat.at[1], stat_square.at[square], peer) for peer, _ in grid.squares]
    parts.append(dot_plain(table_t[...], expo[:, quarter : 2 * quarter]))
    wait_all(flying)
    stat[2, 0], stat[2, 1] = merge_stats([(stat_square[i, 0], stat_square[i, 1]) for i in range(4)])
    stat_line[line] = stat[2]
    flying = [sender.start(stat.at[2], stat_line.at[line], peer) for peer, _ in grid.lines]
    parts.append(dot_plain(table_t[...], expo[:, 2 * quarter : 3 * quarter]))
    parts.append(dot_plain(table_t[...], expo[:, 3 * quarter :]))
    wait_all(flying)
    full_top, full_total = merge_stats([(stat_line[i, 0], stat_line[i, 1]) for i in range(4)])
    lse = full_top + jnp.log(full_total)
    lse_out[...] = lse
    scale = unfold(jnp.exp(own_top - lse) * grad_scale)
    per = 128 // count
    for index in range(total_mask // 128):
        at = slice(index * 128, index * 128 + 128)
        source = parts[index * 128 // quarter]
        begin = index * 128 % quarter
        piece = (source[:, begin : begin + 128] * scale[:, at]).T.astype(jnp.bfloat16)
        for inner in range(per):
            owner = index * per + inner
            part[owner // 8, owner // 2 % 4, owner % 2] = piece[inner * count : inner * count + count]
    copy = sender.start(part.at[:, :, 1 - core], land_pair, grid.twin)

    scaled = []
    for index in range(total_mask // 128):
        at = slice(index * 128, index * 128 + 128)
        column = jnp.broadcast_to(scale[:, at], (128, 128)).T
        column = jnp.concatenate([column] * (wide // 128), axis=1)
        scaled.append((all_heads[at].astype(jnp.float32) * column).astype(jnp.bfloat16))
    scaled = jnp.concatenate(scaled, axis=0)
    slab = rows // 4

    def grad_part(index):
        at = slice(index * slab, index * slab + slab)
        table_grad[at] = dot_plain(expo[at], scaled)

    grad_part(0)
    copy.wait()
    sum_pair[...] = (part[:, :, core].astype(jnp.float32) + land_pair[...].astype(jnp.float32)).astype(
        jnp.bfloat16
    )
    flying = [
        sender.start(sum_pair.at[:, other], land_square.at[square], peer)
        for peer, other in grid.squares
    ]
    land_square[square] = sum_pair[:, square]
    grad_part(1)
    wait_all(flying)
    sum_square[...] = sum(land_square[i].astype(jnp.float32) for i in range(4)).astype(jnp.bfloat16)
    flying = [
        sender.start(sum_square.at[other], land_line.at[line], peer) for peer, other in grid.lines
    ]
    land_line[line] = sum_square[line]
    grad_part(2)
    high = scale.astype(jnp.bfloat16)
    low = (scale - high.astype(jnp.float32)).astype(jnp.bfloat16)
    both = jnp.concatenate(
        [high.astype(jnp.float32), low.astype(jnp.float32), jnp.zeros((14, total_mask), jnp.float32)],
        axis=0,
    ).astype(jnp.bfloat16)
    sums = dot_right_t(both, expo[...])
    bias_grad[...] = sums[0:1] + sums[1:2]
    grad_part(3)
    wait_all(flying)
    head_grad[...] = sum(land_line[i].astype(jnp.float32) for i in range(4))


def head_and_table(head_low, entity_table, bias_row, grad_scale, collective_id):
    count, wide = head_low.shape
    rows = entity_table.shape[0]
    total_mask = 32 * count
    low, full = jnp.bfloat16, jnp.float32
    vmem = pl.BlockSpec(memory_space=pltpu.VMEM)
    folded = (total_mask // 128, 128)
    return pl.pallas_call(
        functools.partial(head_kernel, grad_scale),
        out_shape=[
            jax.ShapeDtypeStruct((rows, wide), full),
            jax.ShapeDtypeStruct((1, rows), full),
            jax.ShapeDtypeStruct(folded, full),
            jax.ShapeDtypeStruct((count, wide), full),
        ],
        in_specs=[vmem] * 3,
        out_specs=[vmem] * 4,
        scratch_shapes=[
            pltpu.VMEM((4, 4, 2, count, wide), low),
            pltpu.VMEM((rows, total_mask), full),
            pltpu.VMEM((rows, total_mask), low),
            pltpu.VMEM((wide, rows), low),
            pltpu.VMEM((rows, 128), full),
            pltpu.VMEM((4, 4, 2, count, wide), low),
            pltpu.VMEM((4, 4, count, wide), low),
            pltpu.VMEM((4, 4, count, wide), low),
            pltpu.VMEM((4, 4, count, wide), low),
            pltpu.VMEM((4, count, wide), low),
            pltpu.VMEM((4, count, wide), low),
            pltpu.VMEM((3, 2) + folded, full),
            pltpu.VMEM((2,) + folded, full),
            pltpu.VMEM((4, 2) + folded, full),
            pltpu.VMEM((4, 2) + folded, full),
            pltpu.SemaphoreType.DMA((24,)),
            pltpu.SemaphoreType.DMA((24,)),
        ],
        compiler_params=pltpu.CompilerParams(
            collective_id=collective_id, has_side_effects=True, vmem_limit_bytes=60 * 2**20
        ),
    )(head_low, entity_table, bias_row)


def body(
    word_states,
    word_segments,
    entity_segments,
    request_rows,
    request_slot,
    mask_slots,
    entity_table,
    vocab_bias,
    entity_dense,
    query_ww,
    query_we,
    query_ew,
    query_ee,
    key_weight,
    value_weight,
    out_weight,
    norm1_gain,
    norm1_bias,
    up_weight,
    down_weight,
    norm2_gain,
    norm2_bias,
    head_weight,
    head_gain,
    head_bias,
    cotangent,
):
    word_count = word_states.shape[0]
    model_width = word_states.shape[1]
    slot_count = entity_segments.shape[1]
    mask_count = mask_slots.shape[1]
    request_count = slot_count + mask_count
    seq_len = word_count + slot_count
    devices = lax.axis_size("dp")
    capacity = request_rows.shape[1]
    head_count = model_width // HD
    query_scale = HD ** (-0.5)
    emb_width = entity_table.shape[1]
    table_rows = entity_table.shape[0]
    total_mask = mask_count * devices
    grad_scale = 1.0 / total_mask
    id_block = jnp.pad(request_rows[:, None, :], ((0, 0), (0, 7), (0, 128 - capacity)))
    asked_ids = direct_swap(id_block, 0)[:, 0, :capacity]
    found_rows = jnp.take(entity_table, asked_ids, axis=0)
    found_bias = jnp.take(vocab_bias, asked_ids, axis=0)
    cap_room = -(-capacity // 16) * 16 - capacity
    found_all = jnp.concatenate(
        [found_rows, jnp.broadcast_to(found_bias[:, :, None], found_bias.shape + (128,))], axis=2
    )
    back_all = direct_swap(jnp.pad(found_all, ((0, 0), (0, cap_room), (0, 0))), 1)
    back_rows = back_all[:, :capacity, :emb_width]
    back_bias = back_all[:, :capacity, emb_width]
    got_rows = back_rows
    got_bias = back_bias
    slot_ids = request_slot.reshape(devices * capacity)
    placing = slot_ids[None, :] == jnp.arange(request_count, dtype=jnp.int32)[:, None]
    placing_low = placing.astype(jnp.bfloat16)
    request_vecs = dot_plain(placing_low, got_rows.reshape(devices * capacity, emb_width))
    request_bias = dot_plain(placing_low, got_bias.reshape(devices * capacity, 1))[:, 0]
    entity_low = request_vecs[:slot_count].astype(jnp.bfloat16)
    target_vecs = request_vecs[slot_count:]
    target_bias = request_bias[slot_count:]
    fused = model_width % devices == 0 and (model_width // devices) % 8 == 0 and devices == 32
    segment_row = jnp.concatenate([word_segments[0], entity_segments[0]])
    choose = (mask_slots[0][:, None] == jnp.arange(slot_count, dtype=jnp.int32)[None, :]).astype(
        jnp.float32
    )
    head_shape = (seq_len, head_count, HD)
    if fused:
        codes = jnp.arange(128, dtype=jnp.int32)[None, :] % HD
        same = segment_row[:, None] == codes
        feat_q = same.astype(jnp.bfloat16)
        feat_k = jnp.where(same | (codes >= 4), 0.0, MASKED).astype(jnp.bfloat16)
        (
            hidden_low,
            query_word,
            query_entity,
            key_rows,
            values,
            context_low,
            lse_lanes,
            residual_one,
            normed_low,
            activated,
            gelu_slope,
            residual_two,
            layer_low,
            picked_low,
            head_pre,
            head_low,
        ) = forward_pass(
            [
                word_states,
                entity_low,
                feat_q,
                feat_k,
                choose.astype(jnp.bfloat16),
                entity_dense,
                query_ww,
                query_we,
                query_ew,
                query_ee,
                key_weight,
                value_weight,
                out_weight,
                norm1_gain[None],
                norm1_bias[None],
                up_weight,
                down_weight,
                norm2_gain[None],
                norm2_bias[None],
                head_weight,
                head_gain[None],
                head_bias[None],
            ]
        )
    else:
        entity_states = dot_plain(entity_low, entity_dense)
        hidden = jnp.concatenate([word_states.astype(jnp.float32), entity_states], axis=0)
        hidden_low = hidden.astype(jnp.bfloat16)
        word_part = hidden_low[:word_count]
        entity_part = hidden_low[word_count:]
        query_word = (
            query_scale
            * jnp.concatenate(
                [dot_plain(word_part, query_ww), dot_plain(entity_part, query_ew)], axis=0
            )
        ).astype(jnp.bfloat16)
        query_entity = (
            query_scale
            * jnp.concatenate(
                [dot_plain(word_part, query_we), dot_plain(entity_part, query_ee)], axis=0
            )
        ).astype(jnp.bfloat16)
        key_rows = dot_plain(hidden_low, key_weight).astype(jnp.bfloat16)
        values = dot_plain(hidden_low, value_weight).astype(jnp.bfloat16)
        query_word_h = query_word.reshape(head_shape)
        query_entity_h = query_entity.reshape(head_shape)
        key_rows_h = key_rows.reshape(head_shape)
        values_h = values.reshape(head_shape)
        allowed = segment_row[:, None] == segment_row[None, :]
        scores = attn_scores(query_word_h, query_entity_h, key_rows_h, allowed, word_count)
        row_top = jnp.max(scores, axis=2, keepdims=True)
        exp_scores = jnp.exp(scores - row_top)
        row_total = jnp.sum(exp_scores, axis=2, keepdims=True)
        attn_low = (exp_scores / row_total).astype(jnp.bfloat16)
        row_lse = row_top + jnp.log(row_total)
        context = jnp.einsum("hqk,khd->qhd", attn_low, values_h, preferred_element_type=jnp.float32)
        context_low = context.reshape(seq_len, model_width).astype(jnp.bfloat16)
        attended = dot_plain(context_low, out_weight)
        residual_one = hidden + attended
        normed = layer_norm(residual_one, norm1_gain, norm1_bias)
        normed_low = normed.astype(jnp.bfloat16)
        up_value = dot_plain(normed_low, up_weight)
        activated = gelu_exact(up_value).astype(jnp.bfloat16)
        down_value = dot_plain(activated, down_weight)
        residual_two = normed + down_value
        layer_out = layer_norm(residual_two, norm2_gain, norm2_bias)
        choose = (mask_slots[0][:, None] == jnp.arange(slot_count, dtype=jnp.int32)[None, :]).astype(
            jnp.float32
        )
        picked_low = dot_exact(choose, layer_out[word_count:]).astype(jnp.bfloat16)
        head_pre = dot_plain(picked_low, head_weight)
        head_low = head_act(head_pre, head_gain, head_bias).astype(jnp.bfloat16)
        layer_low = layer_out.astype(jnp.bfloat16)
    head_f32 = head_low.astype(jnp.float32)
    target_logit = jnp.sum(head_f32 * target_vecs, axis=1) + target_bias
    if fused:
        table_grad, bias_grad, lse_all, head_grad = head_and_table(
            head_low, entity_table, vocab_bias.astype(jnp.float32)[None, :], grad_scale, 8
        )
        bias_grad = bias_grad[0]
        lse_all = lse_all.reshape(total_mask)
        own_lse = lax.dynamic_slice_in_dim(
            lse_all, lax.axis_index("dp") * mask_count, mask_count, 0
        )
        mask_loss = own_lse - target_logit
    else:
        all_heads = direct_swap(head_low, 2, gather=True).reshape(total_mask, emb_width)
        block_rows = min(512, total_mask)
        block_count = total_mask // block_rows
        bias_f32 = vocab_bias.astype(jnp.float32)

        def block_logits(block_index):
            row_block = lax.dynamic_slice_in_dim(all_heads, block_index * block_rows, block_rows, 0)
            return (row_block, dot_right_t(row_block, entity_table) + bias_f32[None, :])

        def block_stats(block_index):
            row_block, logits = block_logits(block_index)
            top_value = jnp.max(logits, axis=1)
            return (top_value, jnp.sum(jnp.exp(logits - top_value[:, None]), axis=1))

        local_top, local_total = lax.map(block_stats, jnp.arange(block_count, dtype=jnp.int32))
        local_top = local_top.reshape(total_mask)
        local_total = local_total.reshape(total_mask)
        target_sum = jnp.sum(target_logit)
        stats = jnp.concatenate(
            [
                local_top.reshape(total_mask // 128, 128),
                local_total.reshape(total_mask // 128, 128),
                jnp.full((8, 128), target_sum),
            ],
            axis=0,
        )
        all_stats = direct_swap(stats, 3, gather=True)
        all_tops = all_stats[:, : total_mask // 128].reshape(devices, total_mask)
        all_totals = all_stats[:, total_mask // 128 : total_mask // 64].reshape(devices, total_mask)
        target_total = jnp.sum(all_stats[:, total_mask // 64, 0])
        global_top = jnp.max(all_tops, axis=0)
        global_total = jnp.sum(all_totals * jnp.exp(all_tops - global_top[None, :]), axis=0)
        lse_all = global_top + jnp.log(global_total)
        loss_value = (jnp.sum(lse_all) - target_total) * grad_scale
        own_lse = lax.dynamic_slice_in_dim(lse_all, lax.axis_index("dp") * mask_count, mask_count, 0)
        mask_loss = own_lse - target_logit

        def block_back(running, block_index):
            table_grad, bias_grad = running
            row_block, logits = block_logits(block_index)
            lse_block = lax.dynamic_slice_in_dim(lse_all, block_index * block_rows, block_rows, 0)
            logit_grad = (jnp.exp(logits - lse_block[:, None]) * grad_scale).astype(jnp.bfloat16)
            table_grad = table_grad + dot_left_t(logit_grad, row_block)
            bias_grad = bias_grad + jnp.sum(logit_grad.astype(jnp.float32), axis=0)
            return ((table_grad, bias_grad), dot_plain(logit_grad, entity_table))

        start_grads = (
            jnp.zeros((table_rows, emb_width), jnp.float32),
            jnp.zeros((table_rows,), jnp.float32),
        )
        (table_grad, bias_grad), head_terms = lax.scan(
            block_back, start_grads, jnp.arange(block_count, dtype=jnp.int32)
        )
        head_parts = direct_swap(head_terms.reshape(devices, mask_count, emb_width), 4)
        head_grad = jnp.sum(head_parts, axis=0)
    head_grad = head_grad - grad_scale * target_vecs
    target_grad = -grad_scale * head_f32
    pre_grad, head_gain_grad, head_bias_grad = jax.vjp(head_act, head_pre, head_gain, head_bias)[1](
        head_grad
    )
    pre_low = pre_grad.astype(jnp.bfloat16)
    head_weight_grad = dot_left_t(picked_low, pre_low)
    picked_grad = dot_right_t(pre_low, head_weight)
    out_grad = cotangent.astype(jnp.float32) + jnp.concatenate(
        [jnp.zeros((word_count, model_width), jnp.float32), dot_exact(choose.T, picked_grad)],
        axis=0,
    )
    resid_grad, norm2_gain_grad, norm2_bias_grad = norm_back(
        residual_two, norm2_gain, norm2_bias, out_grad
    )
    down_in = resid_grad.astype(jnp.bfloat16)
    down_grad = dot_left_t(activated, down_in)
    act_grad = dot_right_t(down_in, down_weight)
    if fused:
        up_grad = act_grad * gelu_slope.astype(jnp.float32)
    else:
        up_grad = jax.vjp(gelu_exact, up_value)[1](act_grad)[0]
    up_low = up_grad.astype(jnp.bfloat16)
    up_weight_grad = dot_left_t(normed_low, up_low)
    normed_grad = resid_grad + dot_right_t(up_low, up_weight)
    first_grad, norm1_gain_grad, norm1_bias_grad = norm_back(
        residual_one, norm1_gain, norm1_bias, normed_grad
    )
    attn_in = first_grad.astype(jnp.bfloat16)
    out_weight_grad = dot_left_t(context_low, attn_in)
    context_grad = dot_right_t(attn_in, out_weight).astype(jnp.bfloat16).reshape(head_shape)
    if fused:
        orders = stage_masks(devices)
        up_low_grad = up_weight_grad.astype(jnp.bfloat16)
        up_cuts = [
            in_order(up_low_grad[:, i * model_width : (i + 1) * model_width], orders[2 * (i // 3)])
            for i in range(4)
        ]
        down_view = down_grad.astype(jnp.bfloat16).reshape(devices, 4, -1, model_width)
        down_cuts = [
            in_order(down_view[:, i].reshape(model_width, model_width), orders[1 + i // 3])
            for i in range(4)
        ]
        early_grads = [
            jnp.stack(up_cuts[:3]),
            in_order(head_weight_grad.astype(jnp.bfloat16), orders[0])[None],
            jnp.stack(down_cuts[:3] + [in_order(out_weight_grad.astype(jnp.bfloat16), orders[1])]),
            jnp.stack([up_cuts[3], down_cuts[3]]),
        ]
        delta = jnp.sum(
            (context_low.astype(jnp.float32) * context_grad.reshape(seq_len, model_width)).reshape(
                seq_len, head_count // 2, 2, HD
            ),
            axis=3,
        )
        delta = jnp.pad(delta, ((0, 0), (0, 0), (2, 0))).reshape(seq_len, 2 * head_count)
        lse_delta = lse_lanes + jnp.pad(delta, ((0, 0), (0, 128 - 2 * head_count)))
        fused_out = attention_back(
            early_grads,
            [
                hidden_low,
                query_word,
                query_entity,
                key_rows,
                values,
                context_grad.reshape(seq_len, model_width),
                feat_q,
                feat_k,
                lse_delta,
                first_grad,
            ],
            [
                query_ww,
                query_we,
                query_ew,
                query_ee,
                key_weight,
                value_weight,
                entity_dense,
                entity_low,
            ],
            7,
        )
        up_a, head_a, down_a, mixed, q_word, dense_a, key_value, q_ent, words_grad, entity_vec_grad = (
            fused_out
        )
        up_sum = jnp.concatenate([up_a[0], up_a[1], up_a[2], mixed[0]], axis=1)
        down_sum = jnp.concatenate([down_a[0], down_a[1], down_a[2], mixed[1]], axis=0)
    else:
        scores_again = attn_scores(query_word_h, query_entity_h, key_rows_h, allowed, word_count)
        attn_prob = jnp.exp(scores_again - row_lse)
        prob_low = attn_prob.astype(jnp.bfloat16)
        prob_grad = jnp.einsum(
            "qhd,khd->hqk", context_grad, values_h, preferred_element_type=jnp.float32
        )
        values_grad = jnp.einsum(
            "hqk,qhd->khd", prob_low, context_grad, preferred_element_type=jnp.float32
        )
        values_grad = values_grad.reshape(seq_len, model_width).astype(jnp.bfloat16)
        row_delta = jnp.sum(attn_prob * prob_grad, axis=2, keepdims=True)
        score_grad = (attn_prob * (prob_grad - row_delta)).astype(jnp.bfloat16)
        qword_grad = jnp.einsum(
            "hqk,khd->qhd",
            score_grad[:, :, :word_count],
            key_rows_h[:word_count],
            preferred_element_type=jnp.float32,
        )
        qword_grad = qword_grad.reshape(seq_len, model_width).astype(jnp.bfloat16)
        qent_grad = jnp.einsum(
            "hqk,khd->qhd",
            score_grad[:, :, word_count:],
            key_rows_h[word_count:],
            preferred_element_type=jnp.float32,
        )
        qent_grad = qent_grad.reshape(seq_len, model_width).astype(jnp.bfloat16)
        keys_grad = jnp.concatenate(
            [
                jnp.einsum(
                    "hqk,qhd->khd",
                    score_grad[:, :, :word_count],
                    query_word_h,
                    preferred_element_type=jnp.float32,
                ),
                jnp.einsum(
                    "hqk,qhd->khd",
                    score_grad[:, :, word_count:],
                    query_entity_h,
                    preferred_element_type=jnp.float32,
                ),
            ],
            axis=0,
        )
        keys_grad = keys_grad.reshape(seq_len, model_width).astype(jnp.bfloat16)
        query_ww_grad = query_scale * dot_left_t(word_part, qword_grad[:word_count])
        query_ew_grad = query_scale * dot_left_t(entity_part, qword_grad[word_count:])
        query_we_grad = query_scale * dot_left_t(word_part, qent_grad[:word_count])
        query_ee_grad = query_scale * dot_left_t(entity_part, qent_grad[word_count:])
        key_weight_grad = dot_left_t(hidden_low, keys_grad)
        value_weight_grad = dot_left_t(hidden_low, values_grad)
        word_back = query_scale * (
            dot_right_t(qword_grad[:word_count], query_ww)
            + dot_right_t(qent_grad[:word_count], query_we)
        )
        entity_back = query_scale * (
            dot_right_t(qword_grad[word_count:], query_ew)
            + dot_right_t(qent_grad[word_count:], query_ee)
        )
        hidden_grad = (
            first_grad
            + jnp.concatenate([word_back, entity_back], axis=0)
            + dot_right_t(keys_grad, key_weight)
            + dot_right_t(values_grad, value_weight)
        )
        words_grad = hidden_grad[:word_count].astype(jnp.bfloat16)
        state_low = hidden_grad[word_count:].astype(jnp.bfloat16)
        dense_grad = dot_left_t(entity_low, state_low)
        entity_vec_grad = dot_right_t(state_low, entity_dense)
    vec_grad = jnp.concatenate([entity_vec_grad, target_grad], axis=0)
    bias_vec_grad = jnp.concatenate(
        [jnp.zeros((slot_count,), jnp.float32), jnp.full((mask_count,), -grad_scale, jnp.float32)]
    )
    placing_f32 = placing.astype(jnp.float32)
    per_request = dot_exact(placing_f32.T, vec_grad)
    bias_request = dot_exact(placing_f32.T, bias_vec_grad[:, None])[:, 0]
    back_block = jnp.concatenate(
        [
            per_request.reshape(devices, capacity, emb_width).astype(jnp.bfloat16),
            jnp.broadcast_to(
                bias_request.reshape(devices, capacity, 1).astype(jnp.bfloat16),
                (devices, capacity, 128),
            ),
        ],
        axis=2,
    )
    back_block = direct_swap(jnp.pad(back_block, ((0, 0), (0, cap_room), (0, 0))), 5)
    back_rows = back_block[:, :capacity, :emb_width].astype(jnp.float32)
    back_bias = back_block[:, :capacity, emb_width].astype(jnp.float32)
    flat_ids = asked_ids.reshape(devices * capacity)
    table_grad = table_grad + jax.ops.segment_sum(
        back_rows.reshape(devices * capacity, emb_width), flat_ids, num_segments=table_rows
    )
    bias_grad = bias_grad + jax.ops.segment_sum(
        back_bias.reshape(devices * capacity), flat_ids, num_segments=table_rows
    )
    vectors = [
        head_gain_grad,
        head_bias_grad,
        norm2_gain_grad,
        norm2_bias_grad,
        norm1_gain_grad,
        norm1_bias_grad,
    ]
    cuts = [vector.reshape(devices, -1) for vector in vectors]
    spots = [0]
    for cut in cuts:
        spots.append(spots[-1] + cut.shape[1])
    cuts.append(jnp.full((devices, 1), jnp.sum(mask_loss)))
    block = jnp.concatenate(cuts, axis=1)
    block = jnp.pad(block, ((0, 0), (0, 127 - spots[-1])))[:, None, :]
    vector_sums = jnp.sum(direct_swap(jnp.pad(block, ((0, 0), (0, 7), (0, 0))), 6)[:, 0], axis=0)
    if fused:
        loss_value = vector_sums[spots[-1]] * grad_scale
    vector_out = [vector_sums[spots[i] : spots[i + 1]] for i in range(len(vectors))]
    if fused:
        all_sums = (
            head_a[0],
            vector_out[0],
            vector_out[1],
            vector_out[2],
            vector_out[3],
            up_sum,
            down_sum,
            vector_out[4],
            vector_out[5],
            down_a[3],
            q_word[0],
            q_word[1],
            q_ent[0],
            q_ent[1],
            key_value[0],
            key_value[1],
            dense_a[0],
        )
    else:
        sums = sum_all(
            [
                [up_weight_grad, out_weight_grad, head_weight_grad],
                [down_grad, query_ww_grad, dense_grad],
                [query_we_grad, query_ew_grad, query_ee_grad, key_weight_grad, value_weight_grad],
            ],
            7,
        )
        all_sums = (
            sums[0][2],
            vector_out[0],
            vector_out[1],
            vector_out[2],
            vector_out[3],
            sums[0][0],
            sums[1][0],
            vector_out[4],
            vector_out[5],
            sums[0][1],
            sums[1][1],
            sums[2][0],
            sums[2][1],
            sums[2][2],
            sums[2][3],
            sums[2][4],
            sums[1][2],
        )
    return (
        loss_value,
        layer_low,
        words_grad,
        table_grad,
        bias_grad,
        all_sums[16],
        all_sums[10],
        all_sums[11],
        all_sums[12],
        all_sums[13],
        all_sums[14],
        all_sums[15],
        all_sums[9],
        all_sums[7],
        all_sums[8],
        all_sums[5],
        all_sums[6],
        all_sums[3],
        all_sums[4],
        all_sums[0],
        all_sums[1],
        all_sums[2],
        mask_loss,
    )


def solution(mesh):
    in_specs = (
        P("dp", None),
        P("dp", None),
        P("dp", None),
        P("dp", None),
        P("dp", None),
        P("dp", None),
        P("dp", None),
        P("dp"),
        P(),
        P(),
        P(),
        P(),
        P(),
        P(),
        P(),
        P(),
        P(),
        P(),
        P(),
        P(),
        P(),
        P(),
        P(),
        P(),
        P(),
        P("dp", None),
    )
    out_specs = (
        P(),
        P("dp", None),
        P("dp", None),
        P("dp", None),
        P("dp"),
        P("dp", None),
        P("dp", None),
        P("dp", None),
        P("dp", None),
        P("dp", None),
        P("dp", None),
        P("dp", None),
        P("dp", None),
        P("dp"),
        P("dp"),
        P("dp", None),
        P("dp", None),
        P("dp"),
        P("dp"),
        P("dp", None),
        P("dp"),
        P("dp"),
        P("dp"),
    )
    return jax.shard_map(body, mesh=mesh, in_specs=in_specs, out_specs=out_specs, check_vma=False)
```

```python
import functools

import jax
import jax.numpy as jnp
from jax import lax
from jax.experimental import pallas as pl
from jax.experimental.pallas import tpu as pltpu
from jax.sharding import PartitionSpec as P

MESH_ID = pl.DeviceIdType.MESH

HD = 64


EPSILON = 1e-05
MASKED = -1000000000.0


def dot_plain(left_side, right_side):
    return jnp.dot(left_side, right_side, preferred_element_type=jnp.float32)


def dot_left_t(left_side, right_side):
    return lax.dot_general(
        left_side, right_side, (((0,), (0,)), ((), ())), preferred_element_type=jnp.float32
    )


def dot_right_t(left_side, right_side):
    return lax.dot_general(
        left_side, right_side, (((1,), (1,)), ((), ())), preferred_element_type=jnp.float32
    )


def dot_exact(left_side, right_side):
    return jnp.dot(
        left_side, right_side, precision=lax.Precision.HIGHEST, preferred_element_type=jnp.float32
    )


def layer_norm(tensor, gain_vec, shift_vec):
    center = tensor - jnp.mean(tensor, axis=-1, keepdims=True)
    spread = jnp.mean(center * center, axis=-1, keepdims=True)
    return center * lax.rsqrt(spread + EPSILON) * gain_vec + shift_vec


def gelu_exact(tensor):
    return jax.nn.gelu(tensor, approximate=False)


def head_act(tensor, gain_vec, shift_vec):
    return layer_norm(gelu_exact(tensor), gain_vec, shift_vec)


def norm_back(tensor, gain_vec, shift_vec, grad_out):
    result, pullback = jax.vjp(layer_norm, tensor, gain_vec, shift_vec)
    return pullback(grad_out)


def attn_scores(query_word, query_entity, key_rows, allowed, word_count):
    to_words = jnp.einsum(
        "qhd,khd->hqk", query_word, key_rows[:word_count], preferred_element_type=jnp.float32
    )
    to_entities = jnp.einsum(
        "qhd,khd->hqk", query_entity, key_rows[word_count:], preferred_element_type=jnp.float32
    )
    return jnp.where(allowed[None], jnp.concatenate([to_words, to_entities], axis=2), MASKED)


def greet_all(me, devices):
    barrier = pltpu.get_barrier_semaphore()

    def greet(step, carry):
        pl.semaphore_signal(
            barrier, inc=1, device_id=(lax.rem(me + step, devices),), device_id_type=MESH_ID
        )
        return carry

    lax.fori_loop(1, devices, greet, 0)
    pl.semaphore_wait(barrier, devices - 1)


def swap_kernel(devices, gather, source, target, send_sem, recv_sem):
    me = lax.axis_index("dp")
    greet_all(me, devices)

    def piece(step):
        peer = lax.rem(me + step, devices)
        return pltpu.make_async_remote_copy(
            src_ref=source if gather else source.at[peer],
            dst_ref=target.at[me],
            send_sem=send_sem.at[step],
            recv_sem=recv_sem.at[step],
            device_id=(peer,),
            device_id_type=MESH_ID,
        )

    def begin(step, carry):
        piece(step).start()
        return carry

    def finish(step, carry):
        piece(step).wait()
        return carry

    lax.fori_loop(1, devices, begin, 0)
    target[me] = source[...] if gather else source[me]
    lax.fori_loop(1, devices, finish, 0)


def direct_swap(value, collective_id, gather=False):
    devices = lax.axis_size("dp")
    shape = (devices,) + value.shape if gather else value.shape
    return pl.pallas_call(
        functools.partial(swap_kernel, devices, gather),
        out_shape=jax.ShapeDtypeStruct(shape, value.dtype),
        in_specs=[pl.BlockSpec(memory_space=pltpu.VMEM)],
        out_specs=pl.BlockSpec(memory_space=pltpu.VMEM),
        scratch_shapes=[
            pltpu.SemaphoreType.DMA((devices,)),
            pltpu.SemaphoreType.DMA((devices,)),
        ],
        compiler_params=pltpu.CompilerParams(collective_id=collective_id, has_side_effects=True),
    )(value)


def stage_masks(devices):
    if devices == 32:
        axes = [[2], [4], [8, 16]]
    elif devices == 128:
        axes = [[2, 4], [8, 16], [32, 64]]
    else:
        axes = [[2**bit] for bit in range(1, devices.bit_length() - 1)]
        axes = axes + [[] for _ in range(3 - len(axes))]
    first, second, third = axes[0], axes[1], sum(axes[2:], [])
    return (
        [1] + first + second + third,
        [1] + second + first + third,
        [1] + third + first + second,
    )


def sum_kernel(masks, rows, *refs):
    parts = len(masks)
    stages = len(masks[0])
    sources, results = refs[:parts], refs[parts : 2 * parts]
    landing = refs[2 * parts : 3 * parts]
    send_sem, recv_sem = refs[3 * parts :]
    me = lax.axis_index("dp")
    barrier = pltpu.get_barrier_semaphore()
    partner_of = {}
    for mask in masks[0]:
        bit = lax.rem(lax.div(me, mask), 2)
        partner_of[mask] = (me + mask - 2 * mask * bit, bit)
    for mask in masks[0]:
        pl.semaphore_signal(
            barrier, inc=1, device_id=(partner_of[mask][0],), device_id_type=MESH_ID
        )
    pl.semaphore_wait(barrier, stages)
    sizes = [[rows[part] * 2 ** (stages - 1 - stage) for stage in range(stages)] for part in range(parts)]
    places = [[sum(size[:stage]) for stage in range(stages)] for size in sizes]

    def launch(part, stage):
        partner, bit = partner_of[masks[part][stage]]
        size = sizes[part][stage]
        away = (1 - bit) * size
        copy = pltpu.make_async_remote_copy(
            src_ref=sources[part].at[pl.ds(away, size)]
            if stage == 0
            else landing[part].at[pl.ds(places[part][stage - 1] + away, size)],
            dst_ref=landing[part].at[pl.ds(places[part][stage], size)],
            send_sem=send_sem.at[part, stage],
            recv_sem=recv_sem.at[part, stage],
            device_id=(partner,),
            device_id_type=MESH_ID,
        )
        copy.start()
        return copy

    flying = [launch(part, 0) for part in range(parts)]

    def add_rows(part, stage, start, count):
        keep = partner_of[masks[part][stage]][1] * sizes[part][stage] + start
        last = stage == stages - 1

        def step(index, carry):
            theirs = pl.ds(pl.multiple_of(places[part][stage] + start + index * 16, 16), 16)
            if stage == 0:
                mine = sources[part][pl.ds(pl.multiple_of(keep + index * 16, 16), 16)]
            else:
                mine = landing[part][
                    pl.ds(pl.multiple_of(places[part][stage - 1] + keep + index * 16, 16), 16)
                ]
            total = mine.astype(jnp.float32) + landing[part][theirs].astype(jnp.float32)
            if last:
                results[part][pl.ds(pl.multiple_of(index * 16, 16), 16)] = total
            else:
                landing[part][theirs] = total.astype(jnp.bfloat16)
            return carry

        lax.fori_loop(0, count // 16, step, 0, unroll=min(4, count // 16))

    for stage in range(stages):
        for part in range(parts):
            flying[part].wait()
            if stage == stages - 1:
                add_rows(part, stage, 0, sizes[part][stage])
                continue
            bit = partner_of[masks[part][stage + 1]][1]
            half = sizes[part][stage] // 2
            add_rows(part, stage, (1 - bit) * half, half)
            flying[part] = launch(part, stage + 1)
            add_rows(part, stage, bit * half, half)


def sum_scatter(parts, collective_id):
    devices = lax.axis_size("dp")
    masks = stage_masks(devices)
    rows = [part.shape[1] for part in parts]
    width = parts[0].shape[2]
    bits = devices.bit_length() - 1
    ordered = []
    for part, order in zip(parts, masks):
        view = part.reshape((2,) * bits + part.shape[1:])
        places = [bits - mask.bit_length() for mask in order]
        view = view.transpose(tuple(places) + (bits, bits + 1))
        ordered.append(view.reshape(devices * part.shape[1], width))
    return pl.pallas_call(
        functools.partial(sum_kernel, masks, rows),
        out_shape=[jax.ShapeDtypeStruct((count, width), jnp.float32) for count in rows],
        in_specs=[pl.BlockSpec(memory_space=pltpu.VMEM)] * len(parts),
        out_specs=[pl.BlockSpec(memory_space=pltpu.VMEM)] * len(parts),
        scratch_shapes=[pltpu.VMEM((devices * count, width), jnp.bfloat16) for count in rows]
        + [pltpu.SemaphoreType.DMA((len(parts), bits)), pltpu.SemaphoreType.DMA((len(parts), bits))],
        input_output_aliases={},
        compiler_params=pltpu.CompilerParams(
            collective_id=collective_id, has_side_effects=True, vmem_limit_bytes=56 * 2**20
        ),
    )(*ordered)


def by_owner(grad, width):
    devices = lax.axis_size("dp")
    rows = grad.shape[0] // devices
    blocks = grad.astype(jnp.bfloat16).reshape(devices, rows, grad.shape[1])
    if grad.shape[1] > width:
        cuts = grad.shape[1] // width
        return jnp.concatenate(jnp.split(blocks, cuts, axis=2), axis=1)
    if grad.shape[1] < width:
        return blocks.reshape(devices, rows * grad.shape[1] // width, width)
    return blocks


def from_owner(rows, shape):
    devices = lax.axis_size("dp")
    count, width = shape[0] // devices, shape[1]
    if width > rows.shape[1]:
        return jnp.concatenate(jnp.split(rows, width // rows.shape[1], axis=0), axis=1)
    return rows.reshape(count, width)


def sum_all(groups, collective_id):
    width = groups[0][0].shape[1]
    width = min(grad.shape[1] for group in groups for grad in group if grad.shape[1] >= 768)
    devices = lax.axis_size("dp")
    packed = []
    for group in groups:
        pieces = [by_owner(grad, width) for grad in group]
        count = sum(piece.shape[1] for piece in pieces)
        room = -(-count // 16) * 16 - count
        if room:
            pieces.append(jnp.zeros((devices, room, width), jnp.bfloat16))
        packed.append(jnp.concatenate(pieces, axis=1))
    sums = sum_scatter(packed, collective_id)
    results = []
    for group, total in zip(groups, sums):
        place, outs = 0, []
        for grad in group:
            count = grad.shape[0] // devices * grad.shape[1] // width
            outs.append(from_owner(total[place : place + count], grad.shape))
            place += count
        results.append(outs)
    return results


def body(
    word_states,
    word_segments,
    entity_segments,
    request_rows,
    request_slot,
    mask_slots,
    entity_table,
    vocab_bias,
    entity_dense,
    query_ww,
    query_we,
    query_ew,
    query_ee,
    key_weight,
    value_weight,
    out_weight,
    norm1_gain,
    norm1_bias,
    up_weight,
    down_weight,
    norm2_gain,
    norm2_bias,
    head_weight,
    head_gain,
    head_bias,
    cotangent,
):
    word_count = word_states.shape[0]
    model_width = word_states.shape[1]
    slot_count = entity_segments.shape[1]
    mask_count = mask_slots.shape[1]
    request_count = slot_count + mask_count
    seq_len = word_count + slot_count
    devices = lax.axis_size("dp")
    capacity = request_rows.shape[1]
    head_count = model_width // HD
    query_scale = HD ** (-0.5)
    emb_width = entity_table.shape[1]
    table_rows = entity_table.shape[0]
    total_mask = mask_count * devices
    grad_scale = 1.0 / total_mask
    id_block = jnp.pad(request_rows[:, None, :], ((0, 0), (0, 7), (0, 128 - capacity)))
    asked_ids = direct_swap(id_block, 0)[:, 0, :capacity]
    found_rows = jnp.take(entity_table, asked_ids, axis=0)
    found_bias = jnp.take(vocab_bias, asked_ids, axis=0)
    cap_room = -(-capacity // 16) * 16 - capacity
    found_all = jnp.concatenate(
        [found_rows, jnp.broadcast_to(found_bias[:, :, None], found_bias.shape + (128,))], axis=2
    )
    back_all = direct_swap(jnp.pad(found_all, ((0, 0), (0, cap_room), (0, 0))), 1)
    back_rows = back_all[:, :capacity, :emb_width]
    back_bias = back_all[:, :capacity, emb_width]
    got_rows = back_rows
    got_bias = back_bias
    slot_ids = request_slot.reshape(devices * capacity)
    placing = slot_ids[None, :] == jnp.arange(request_count, dtype=jnp.int32)[:, None]
    placing_low = placing.astype(jnp.bfloat16)
    request_vecs = dot_plain(placing_low, got_rows.reshape(devices * capacity, emb_width))
    request_bias = dot_plain(placing_low, got_bias.reshape(devices * capacity, 1))[:, 0]
    entity_low = request_vecs[:slot_count].astype(jnp.bfloat16)
    target_vecs = request_vecs[slot_count:]
    target_bias = request_bias[slot_count:]
    entity_states = dot_plain(entity_low, entity_dense)
    hidden = jnp.concatenate([word_states.astype(jnp.float32), entity_states], axis=0)
    hidden_low = hidden.astype(jnp.bfloat16)
    word_part = hidden_low[:word_count]
    entity_part = hidden_low[word_count:]
    query_word = (
        query_scale
        * jnp.concatenate(
            [dot_plain(word_part, query_ww), dot_plain(entity_part, query_ew)], axis=0
        )
    ).astype(jnp.bfloat16)
    query_entity = (
        query_scale
        * jnp.concatenate(
            [dot_plain(word_part, query_we), dot_plain(entity_part, query_ee)], axis=0
        )
    ).astype(jnp.bfloat16)
    key_rows = dot_plain(hidden_low, key_weight).astype(jnp.bfloat16)
    values = dot_plain(hidden_low, value_weight).astype(jnp.bfloat16)
    head_shape = (seq_len, head_count, HD)
    query_word_h = query_word.reshape(head_shape)
    query_entity_h = query_entity.reshape(head_shape)
    key_rows_h = key_rows.reshape(head_shape)
    values_h = values.reshape(head_shape)
    segment_row = jnp.concatenate([word_segments[0], entity_segments[0]])
    allowed = segment_row[:, None] == segment_row[None, :]
    scores = attn_scores(query_word_h, query_entity_h, key_rows_h, allowed, word_count)
    row_top = jnp.max(scores, axis=2, keepdims=True)
    exp_scores = jnp.exp(scores - row_top)
    row_total = jnp.sum(exp_scores, axis=2, keepdims=True)
    attn_low = (exp_scores / row_total).astype(jnp.bfloat16)
    row_lse = row_top + jnp.log(row_total)
    context = jnp.einsum("hqk,khd->qhd", attn_low, values_h, preferred_element_type=jnp.float32)
    context_low = context.reshape(seq_len, model_width).astype(jnp.bfloat16)
    attended = dot_plain(context_low, out_weight)
    residual_one = hidden + attended
    normed = layer_norm(residual_one, norm1_gain, norm1_bias)
    normed_low = normed.astype(jnp.bfloat16)
    up_value = dot_plain(normed_low, up_weight)
    activated = gelu_exact(up_value).astype(jnp.bfloat16)
    down_value = dot_plain(activated, down_weight)
    residual_two = normed + down_value
    layer_out = layer_norm(residual_two, norm2_gain, norm2_bias)
    choose = (mask_slots[0][:, None] == jnp.arange(slot_count, dtype=jnp.int32)[None, :]).astype(
        jnp.float32
    )
    picked_low = dot_exact(choose, layer_out[word_count:]).astype(jnp.bfloat16)
    head_pre = dot_plain(picked_low, head_weight)
    head_low = head_act(head_pre, head_gain, head_bias).astype(jnp.bfloat16)
    head_f32 = head_low.astype(jnp.float32)
    target_logit = jnp.sum(head_f32 * target_vecs, axis=1) + target_bias
    all_heads = direct_swap(head_low, 2, gather=True).reshape(total_mask, emb_width)
    block_rows = min(512, total_mask)
    block_count = total_mask // block_rows
    bias_f32 = vocab_bias.astype(jnp.float32)

    def block_logits(block_index):
        row_block = lax.dynamic_slice_in_dim(all_heads, block_index * block_rows, block_rows, 0)
        return (row_block, dot_right_t(row_block, entity_table) + bias_f32[None, :])

    def block_stats(block_index):
        row_block, logits = block_logits(block_index)
        top_value = jnp.max(logits, axis=1)
        return (top_value, jnp.sum(jnp.exp(logits - top_value[:, None]), axis=1))

    local_top, local_total = lax.map(block_stats, jnp.arange(block_count, dtype=jnp.int32))
    local_top = local_top.reshape(total_mask)
    local_total = local_total.reshape(total_mask)
    target_sum = jnp.sum(target_logit)
    stats = jnp.concatenate(
        [
            local_top.reshape(total_mask // 128, 128),
            local_total.reshape(total_mask // 128, 128),
            jnp.full((8, 128), target_sum),
        ],
        axis=0,
    )
    all_stats = direct_swap(stats, 3, gather=True)
    all_tops = all_stats[:, : total_mask // 128].reshape(devices, total_mask)
    all_totals = all_stats[:, total_mask // 128 : total_mask // 64].reshape(devices, total_mask)
    target_total = jnp.sum(all_stats[:, total_mask // 64, 0])
    global_top = jnp.max(all_tops, axis=0)
    global_total = jnp.sum(all_totals * jnp.exp(all_tops - global_top[None, :]), axis=0)
    lse_all = global_top + jnp.log(global_total)
    loss_value = (jnp.sum(lse_all) - target_total) * grad_scale
    own_lse = lax.dynamic_slice_in_dim(lse_all, lax.axis_index("dp") * mask_count, mask_count, 0)
    mask_loss = own_lse - target_logit

    def block_back(running, block_index):
        table_grad, bias_grad = running
        row_block, logits = block_logits(block_index)
        lse_block = lax.dynamic_slice_in_dim(lse_all, block_index * block_rows, block_rows, 0)
        logit_grad = (jnp.exp(logits - lse_block[:, None]) * grad_scale).astype(jnp.bfloat16)
        table_grad = table_grad + dot_left_t(logit_grad, row_block)
        bias_grad = bias_grad + jnp.sum(logit_grad.astype(jnp.float32), axis=0)
        return ((table_grad, bias_grad), dot_plain(logit_grad, entity_table))

    start_grads = (
        jnp.zeros((table_rows, emb_width), jnp.float32),
        jnp.zeros((table_rows,), jnp.float32),
    )
    (table_grad, bias_grad), head_terms = lax.scan(
        block_back, start_grads, jnp.arange(block_count, dtype=jnp.int32)
    )
    head_parts = direct_swap(head_terms.reshape(devices, mask_count, emb_width), 4)
    head_grad = jnp.sum(head_parts, axis=0)
    head_grad = head_grad - grad_scale * target_vecs
    target_grad = -grad_scale * head_f32
    pre_grad, head_gain_grad, head_bias_grad = jax.vjp(head_act, head_pre, head_gain, head_bias)[1](
        head_grad
    )
    pre_low = pre_grad.astype(jnp.bfloat16)
    head_weight_grad = dot_left_t(picked_low, pre_low)
    picked_grad = dot_right_t(pre_low, head_weight)
    out_grad = cotangent.astype(jnp.float32) + jnp.concatenate(
        [jnp.zeros((word_count, model_width), jnp.float32), dot_exact(choose.T, picked_grad)],
        axis=0,
    )
    resid_grad, norm2_gain_grad, norm2_bias_grad = norm_back(
        residual_two, norm2_gain, norm2_bias, out_grad
    )
    down_in = resid_grad.astype(jnp.bfloat16)
    down_grad = dot_left_t(activated, down_in)
    act_grad = dot_right_t(down_in, down_weight)
    up_grad = jax.vjp(gelu_exact, up_value)[1](act_grad)[0]
    up_low = up_grad.astype(jnp.bfloat16)
    up_weight_grad = dot_left_t(normed_low, up_low)
    normed_grad = resid_grad + dot_right_t(up_low, up_weight)
    first_grad, norm1_gain_grad, norm1_bias_grad = norm_back(
        residual_one, norm1_gain, norm1_bias, normed_grad
    )
    attn_in = first_grad.astype(jnp.bfloat16)
    out_weight_grad = dot_left_t(context_low, attn_in)
    context_grad = dot_right_t(attn_in, out_weight).astype(jnp.bfloat16).reshape(head_shape)
    scores_again = attn_scores(query_word_h, query_entity_h, key_rows_h, allowed, word_count)
    attn_prob = jnp.exp(scores_again - row_lse)
    prob_low = attn_prob.astype(jnp.bfloat16)
    prob_grad = jnp.einsum(
        "qhd,khd->hqk", context_grad, values_h, preferred_element_type=jnp.float32
    )
    values_grad = jnp.einsum(
        "hqk,qhd->khd", prob_low, context_grad, preferred_element_type=jnp.float32
    )
    values_grad = values_grad.reshape(seq_len, model_width).astype(jnp.bfloat16)
    row_delta = jnp.sum(attn_prob * prob_grad, axis=2, keepdims=True)
    score_grad = (attn_prob * (prob_grad - row_delta)).astype(jnp.bfloat16)
    qword_grad = jnp.einsum(
        "hqk,khd->qhd",
        score_grad[:, :, :word_count],
        key_rows_h[:word_count],
        preferred_element_type=jnp.float32,
    )
    qword_grad = qword_grad.reshape(seq_len, model_width).astype(jnp.bfloat16)
    qent_grad = jnp.einsum(
        "hqk,khd->qhd",
        score_grad[:, :, word_count:],
        key_rows_h[word_count:],
        preferred_element_type=jnp.float32,
    )
    qent_grad = qent_grad.reshape(seq_len, model_width).astype(jnp.bfloat16)
    keys_grad = jnp.concatenate(
        [
            jnp.einsum(
                "hqk,qhd->khd",
                score_grad[:, :, :word_count],
                query_word_h,
                preferred_element_type=jnp.float32,
            ),
            jnp.einsum(
                "hqk,qhd->khd",
                score_grad[:, :, word_count:],
                query_entity_h,
                preferred_element_type=jnp.float32,
            ),
        ],
        axis=0,
    )
    keys_grad = keys_grad.reshape(seq_len, model_width).astype(jnp.bfloat16)
    query_ww_grad = query_scale * dot_left_t(word_part, qword_grad[:word_count])
    query_ew_grad = query_scale * dot_left_t(entity_part, qword_grad[word_count:])
    query_we_grad = query_scale * dot_left_t(word_part, qent_grad[:word_count])
    query_ee_grad = query_scale * dot_left_t(entity_part, qent_grad[word_count:])
    key_weight_grad = dot_left_t(hidden_low, keys_grad)
    value_weight_grad = dot_left_t(hidden_low, values_grad)
    word_back = query_scale * (
        dot_right_t(qword_grad[:word_count], query_ww)
        + dot_right_t(qent_grad[:word_count], query_we)
    )
    entity_back = query_scale * (
        dot_right_t(qword_grad[word_count:], query_ew)
        + dot_right_t(qent_grad[word_count:], query_ee)
    )
    hidden_grad = (
        first_grad
        + jnp.concatenate([word_back, entity_back], axis=0)
        + dot_right_t(keys_grad, key_weight)
        + dot_right_t(values_grad, value_weight)
    )
    words_grad = hidden_grad[:word_count].astype(jnp.bfloat16)
    state_low = hidden_grad[word_count:].astype(jnp.bfloat16)
    dense_grad = dot_left_t(entity_low, state_low)
    entity_vec_grad = dot_right_t(state_low, entity_dense)
    vec_grad = jnp.concatenate([entity_vec_grad, target_grad], axis=0)
    bias_vec_grad = jnp.concatenate(
        [jnp.zeros((slot_count,), jnp.float32), jnp.full((mask_count,), -grad_scale, jnp.float32)]
    )
    placing_f32 = placing.astype(jnp.float32)
    per_request = dot_exact(placing_f32.T, vec_grad)
    bias_request = dot_exact(placing_f32.T, bias_vec_grad[:, None])[:, 0]
    back_block = jnp.concatenate(
        [
            per_request.reshape(devices, capacity, emb_width).astype(jnp.bfloat16),
            jnp.broadcast_to(
                bias_request.reshape(devices, capacity, 1).astype(jnp.bfloat16),
                (devices, capacity, 128),
            ),
        ],
        axis=2,
    )
    back_block = direct_swap(jnp.pad(back_block, ((0, 0), (0, cap_room), (0, 0))), 5)
    back_rows = back_block[:, :capacity, :emb_width].astype(jnp.float32)
    back_bias = back_block[:, :capacity, emb_width].astype(jnp.float32)
    flat_ids = asked_ids.reshape(devices * capacity)
    table_grad = table_grad + jax.ops.segment_sum(
        back_rows.reshape(devices * capacity, emb_width), flat_ids, num_segments=table_rows
    )
    bias_grad = bias_grad + jax.ops.segment_sum(
        back_bias.reshape(devices * capacity), flat_ids, num_segments=table_rows
    )
    vectors = [
        head_gain_grad,
        head_bias_grad,
        norm2_gain_grad,
        norm2_bias_grad,
        norm1_gain_grad,
        norm1_bias_grad,
    ]
    cuts = [vector.reshape(devices, -1) for vector in vectors]
    spots = [0]
    for cut in cuts:
        spots.append(spots[-1] + cut.shape[1])
    block = jnp.concatenate(cuts, axis=1)
    block = jnp.pad(block, ((0, 0), (0, 128 - spots[-1])))[:, None, :]
    vector_sums = jnp.sum(direct_swap(jnp.pad(block, ((0, 0), (0, 7), (0, 0))), 6)[:, 0], axis=0)
    vector_out = [vector_sums[spots[i] : spots[i + 1]] for i in range(len(cuts))]
    sums = sum_all(
        [
            [up_weight_grad, out_weight_grad, head_weight_grad],
            [down_grad, query_ww_grad, dense_grad],
            [query_we_grad, query_ew_grad, query_ee_grad, key_weight_grad, value_weight_grad],
        ],
        7,
    )
    all_sums = (
        sums[0][2],
        vector_out[0],
        vector_out[1],
        vector_out[2],
        vector_out[3],
        sums[0][0],
        sums[1][0],
        vector_out[4],
        vector_out[5],
        sums[0][1],
        sums[1][1],
        sums[2][0],
        sums[2][1],
        sums[2][2],
        sums[2][3],
        sums[2][4],
        sums[1][2],
    )
    return (
        loss_value,
        layer_out.astype(jnp.bfloat16),
        words_grad,
        table_grad,
        bias_grad,
        all_sums[16],
        all_sums[10],
        all_sums[11],
        all_sums[12],
        all_sums[13],
        all_sums[14],
        all_sums[15],
        all_sums[9],
        all_sums[7],
        all_sums[8],
        all_sums[5],
        all_sums[6],
        all_sums[3],
        all_sums[4],
        all_sums[0],
        all_sums[1],
        all_sums[2],
        mask_loss,
    )


def all_pairs(source, target, sems, me, devices):
    def piece(step):
        peer = lax.rem(me + step, devices)
        return pltpu.make_async_remote_copy(
            src_ref=source.at[peer],
            dst_ref=target.at[me],
            send_sem=sems.at[0, step],
            recv_sem=sems.at[1, step],
            device_id=(peer,),
            device_id_type=MESH_ID,
        )

    def begin(step, carry):
        piece(step).start()
        return carry

    def finish(step, carry):
        piece(step).wait()
        return carry

    lax.fori_loop(1, devices, begin, 0)
    target[me] = source[me]
    return lambda: lax.fori_loop(1, devices, finish, 0)


def lookup_kernel(
    codes, table, bias_col, slot_row, entity_out, vec_out, bias_out, code_out,
    codes_in, found, rows_in, sems,
):
    devices, room, _ = codes.shape
    me = lax.axis_index("dp")
    rows, wide = table.shape
    entries = devices * room
    greet_all(me, devices)
    all_pairs(codes, codes_in, sems.at[0], me, devices)()
    code = codes_in[...].reshape(entries, 128)
    for begin in range(0, entries, 128):
        turned = code[begin : begin + 128].astype(jnp.float32).T
        code_out[:, begin : begin + 128] = turned[0:8].astype(jnp.int32)
    code = jnp.where(code >= rows, code - rows, code)
    lane = lax.broadcasted_iota(jnp.int32, (entries, 128), 1)
    total = jnp.zeros((entries, wide), jnp.float32)
    shift = jnp.zeros((entries, 128), jnp.float32)
    step = 512
    for begin in range(0, rows, step):
        size = min(step, rows - begin)
        match = jnp.concatenate(
            [
                (code - (begin + inner) == lane).astype(jnp.float32)
                for inner in range(0, size, 128)
            ],
            axis=1,
        ).astype(jnp.bfloat16)
        total += dot_plain(match, table[begin : begin + size])
        shift += dot_plain(match, bias_col[begin : begin + size])
    both = jnp.concatenate([total, shift], axis=1).astype(jnp.bfloat16)
    found[...] = both.reshape(found.shape)
    all_pairs(found, rows_in, sems.at[1], me, devices)()
    slots, masked = entity_out.shape[0], vec_out.shape[0]
    wanted = lax.broadcasted_iota(jnp.int32, (slots + masked, entries), 0)
    placing = (wanted == slot_row[0:1]).astype(jnp.float32).astype(jnp.bfloat16)
    placed = dot_plain(placing, rows_in[...].reshape(entries, wide + 128))
    entity_out[...] = placed[:slots, :wide].astype(jnp.bfloat16)
    vec_out[...] = placed[slots:, :wide]
    bias_out[...] = placed[slots:, wide:]


def lookup(codes, table, bias_col, slot_row, slots, masked, collective_id):
    devices, room, _ = codes.shape
    wide = table.shape[1]
    entries = devices * room
    vmem = pl.BlockSpec(memory_space=pltpu.VMEM)
    return pl.pallas_call(
        lookup_kernel,
        out_shape=[
            jax.ShapeDtypeStruct((slots, wide), jnp.bfloat16),
            jax.ShapeDtypeStruct((masked, wide), jnp.float32),
            jax.ShapeDtypeStruct((masked, 128), jnp.float32),
            jax.ShapeDtypeStruct((8, entries), jnp.int32),
        ],
        in_specs=[vmem] * 4,
        out_specs=[vmem] * 4,
        scratch_shapes=[
            pltpu.VMEM(codes.shape, jnp.int32),
            pltpu.VMEM((devices, room, wide + 128), jnp.bfloat16),
            pltpu.VMEM((devices, room, wide + 128), jnp.bfloat16),
            pltpu.SemaphoreType.DMA((2, 2, devices)),
        ],
        compiler_params=pltpu.CompilerParams(
            collective_id=collective_id, has_side_effects=True, vmem_limit_bytes=40 * 2**20
        ),
    )(codes, table, bias_col, slot_row)


def norm_parts(value):
    center = value - jnp.mean(value, axis=-1, keepdims=True)
    spread = jnp.mean(center * center, axis=-1, keepdims=True)
    rate = lax.rsqrt(spread + EPSILON)
    return center * rate, rate


def gelu_parts(value):
    chance = 0.5 + 0.5 * lax.erf(value * (0.5**0.5))
    slope = chance + value * (jnp.exp(-0.5 * value * value) * (0.5 / jnp.pi) ** 0.5)
    return value * chance, slope


def half_lanes(block):
    lane = lax.broadcasted_iota(jnp.int32, (1, block), 1)
    low_half = (lane < HD).astype(jnp.float32).astype(jnp.bfloat16)
    high_half = (lane >= HD).astype(jnp.float32).astype(jnp.bfloat16)
    return low_half, high_half


def forward_kernel(
    word_states,
    entity_low,
    feat_q,
    feat_k,
    choose,
    dense,
    w_ww,
    w_we,
    w_ew,
    w_ee,
    w_key,
    w_value,
    out_hbm,
    gain_one,
    shift_one,
    up_hbm,
    down_hbm,
    gain_two,
    shift_two,
    head_w,
    gain_head,
    shift_head,
    hidden,
    qword,
    qent,
    keys,
    values,
    context,
    lse_out,
    resid_one,
    normed_out,
    active_hbm,
    slope_hbm,
    resid_two,
    layer_low,
    picked_out,
    head_pre_out,
    head_out,
    state_scr,
    normed_scr,
    out_w,
    up_w,
    down_w,
    active,
    slope,
    sems,
):
    loads = [
        pltpu.make_async_copy(source, target, sems.at[index])
        for index, (source, target) in enumerate(
            ((out_hbm, out_w), (up_hbm, up_w), (down_hbm, down_w))
        )
    ]
    for load in loads:
        load.start()
    words, width = word_states.shape
    seq_len = hidden.shape[0]
    slots = seq_len - words
    block = 128
    halves = half_lanes(block)
    query_scale = HD ** (-0.5)
    state_scr[...] = dot_plain(entity_low[...], dense[...])
    hidden[:words] = word_states[...]
    hidden[words:] = state_scr[...].astype(jnp.bfloat16)

    half = width // 2
    for cut in range(0, width, half):
        at = slice(cut, cut + half)
        for target, word_w, ent_w in ((qword, w_ww, w_ew), (qent, w_we, w_ee)):
            target[:words, at] = (query_scale * dot_plain(word_states[...], word_w[:, at])).astype(
                jnp.bfloat16
            )
            target[words:, at] = (query_scale * dot_plain(hidden[words:], ent_w[:, at])).astype(
                jnp.bfloat16
            )
        keys[:, at] = dot_plain(hidden[...], w_key[:, at]).astype(jnp.bfloat16)
        values[:, at] = dot_plain(hidden[...], w_value[:, at]).astype(jnp.bfloat16)
    lse_out[...] = jnp.zeros_like(lse_out)

    def pair_step(pair, carry):
        lanes = pl.ds(pl.multiple_of(pair * block, block), block)
        key_pair = keys[:, lanes]
        value_pair = values[:, lanes]
        key_feat = [key_pair * halves[h] + feat_k[...] * halves[1 - h] for h in range(2)]
        value_only = [value_pair * halves[h] for h in range(2)]
        spot = lax.broadcasted_iota(jnp.int32, (1, block), 1) - 4 * pair

        def row_step(index, inner):
            at = pl.ds(pl.multiple_of(index * block, block), block)
            qw = qword[at, lanes]
            qe = qent[at, lanes]
            feats = feat_q[at]
            result = jnp.zeros((block, block), jnp.float32)
            stats = lse_out[at]
            for h in range(2):
                left_w = qw * halves[h] + feats * halves[1 - h]
                left_e = qe * halves[h] + feats * halves[1 - h]
                scores = jnp.concatenate(
                    [
                        dot_right_t(left_w, key_feat[h][:words]),
                        dot_right_t(left_e, key_feat[h][words:]),
                    ],
                    axis=1,
                )
                top = jnp.max(scores, axis=1, keepdims=True)
                expo = jnp.exp(scores - top)
                total = jnp.sum(expo, axis=1, keepdims=True)
                prob = (expo * (1.0 / total)).astype(jnp.bfloat16)
                result += dot_plain(prob, value_only[h])
                stats = jnp.where(spot == h, top + jnp.log(total), stats)
            context[at, lanes] = result.astype(jnp.bfloat16)
            lse_out[at] = stats
            return inner

        lax.fori_loop(0, seq_len // block, row_step, 0)
        return carry

    lax.fori_loop(0, width // block, pair_step, 0)

    loads[0].wait()
    for begin, size in ((0, words // 2), (words // 2, words // 2), (words, slots)):
        at = slice(begin, begin + size)
        start = (
            state_scr[...] if begin == words else word_states[at].astype(jnp.float32)
        )
        value = start + dot_plain(context[at], out_w[...])
        resid_one[at] = value
        normed = norm_parts(value)[0] * gain_one[...] + shift_one[...]
        normed_scr[at] = normed
        normed_out[at] = normed.astype(jnp.bfloat16)
    loads[1].wait()
    loads[2].wait()
    span = seq_len // 4
    stores = []

    for slot in range(down_w.shape[0] // width):
        cols = slice(slot * width, slot * width + width)

        def up_step(index, carry, cols=cols):
            at = pl.ds(pl.multiple_of(index * span, 16), span)
            result, change = gelu_parts(dot_plain(normed_out[at], up_w[:, cols]))
            active[at, cols] = result.astype(jnp.bfloat16)
            slope[at, cols] = change.astype(jnp.bfloat16)
            return carry

        lax.fori_loop(0, 4, up_step, 0)
        for index, (source, target) in enumerate(((active, active_hbm), (slope, slope_hbm))):
            stores.append(
                pltpu.make_async_copy(
                    source.at[:, cols], target.at[:, cols], sems.at[3 + 2 * slot + index]
                )
            )
            stores[-1].start()

    def down_step(index, carry):
        at = pl.ds(pl.multiple_of(index * span, 16), span)
        value = normed_scr[at] + dot_plain(active[at], down_w[...])
        resid_two[at] = value
        layer_low[at] = (norm_parts(value)[0] * gain_two[...] + shift_two[...]).astype(jnp.bfloat16)
        return carry

    lax.fori_loop(0, 4, down_step, 0)
    picked = dot_plain(choose[...], layer_low[words:]).astype(jnp.bfloat16)
    picked_out[...] = picked
    head_pre = dot_plain(picked, head_w[...])
    head_pre_out[...] = head_pre
    raised = gelu_parts(head_pre)[0]
    head_out[...] = (norm_parts(raised)[0] * gain_head[...] + shift_head[...]).astype(jnp.bfloat16)
    for store in stores:
        store.wait()


def forward_pass(inputs):
    words, width = inputs[0].shape
    slots = inputs[1].shape[0]
    seq_len = words + slots
    hidden_units = inputs[15].shape[1]
    mask_count = inputs[4].shape[0]
    head_width = inputs[19].shape[1]
    low, full = jnp.bfloat16, jnp.float32
    vmem, hbm = pl.BlockSpec(memory_space=pltpu.VMEM), pl.BlockSpec(memory_space=pltpu.HBM)
    far = (12, 15, 16)
    shapes = [
        ((seq_len, width), low),
        ((seq_len, width), low),
        ((seq_len, width), low),
        ((seq_len, width), low),
        ((seq_len, width), low),
        ((seq_len, width), low),
        ((seq_len, 128), full),
        ((seq_len, width), full),
        ((seq_len, width), low),
        ((seq_len, hidden_units), low),
        ((seq_len, hidden_units), low),
        ((seq_len, width), full),
        ((seq_len, width), low),
        ((mask_count, width), low),
        ((mask_count, head_width), full),
        ((mask_count, head_width), low),
    ]
    return pl.pallas_call(
        forward_kernel,
        out_shape=[jax.ShapeDtypeStruct(*shape) for shape in shapes],
        in_specs=[hbm if index in far else vmem for index in range(len(inputs))],
        out_specs=[hbm if index in (9, 10) else vmem for index in range(len(shapes))],
        scratch_shapes=[
            pltpu.VMEM((slots, width), full),
            pltpu.VMEM((seq_len, width), full),
            pltpu.VMEM(inputs[12].shape, low),
            pltpu.VMEM(inputs[15].shape, low),
            pltpu.VMEM(inputs[16].shape, low),
            pltpu.VMEM((seq_len, hidden_units), low),
            pltpu.VMEM((seq_len, hidden_units), low),
            pltpu.SemaphoreType.DMA((16,)),
        ],
        compiler_params=pltpu.CompilerParams(vmem_limit_bytes=60 * 2**20),
    )(*inputs)


class Grid:
    def __init__(self):
        me = lax.axis_index("dp")
        self.core = lax.rem(me, 2)
        self.square = lax.rem(lax.div(me, 2), 4)
        self.line = lax.div(me, 8)
        self.twin = me + 1 - 2 * self.core
        self.squares = []
        self.lines = []
        for step in range(1, 4):
            other = lax.rem(self.square + step, 4)
            self.squares.append((me + 2 * (other - self.square), other))
            other = lax.rem(self.line + step, 4)
            self.lines.append((me + 8 * (other - self.line), other))

    def greet(self):
        barrier = pltpu.get_barrier_semaphore()
        peers = [self.twin] + [peer for peer, _ in self.squares + self.lines]
        for peer in peers:
            pl.semaphore_signal(barrier, inc=1, device_id=(peer,), device_id_type=MESH_ID)
        pl.semaphore_wait(barrier, len(peers))


class Sender:
    def __init__(self, send_sem, recv_sem):
        self.send_sem, self.recv_sem, self.used = send_sem, recv_sem, 0

    def start(self, source, target, peer):
        slot = self.used
        self.used += 1
        copy = pltpu.make_async_remote_copy(
            src_ref=source,
            dst_ref=target,
            send_sem=self.send_sem.at[slot],
            recv_sem=self.recv_sem.at[slot],
            device_id=(peer,),
            device_id_type=MESH_ID,
        )
        copy.start()
        return copy


def wait_all(copies):
    for copy in copies:
        copy.wait()


def merge_stats(blocks):
    tops = [block[0] for block in blocks]
    top = functools.reduce(jnp.maximum, tops)
    total = sum(block[1] * jnp.exp(block[0] - top) for block in blocks)
    return top, total, sum(block[2] for block in blocks)


def head_kernel(
    grad_scale,
    head,
    table,
    bias,
    target_vecs,
    target_bias,
    table_grad,
    bias_grad,
    losses,
    total_loss,
    head_grad,
    heads,
    logits,
    expo,
    table_t,
    bias_col,
    part,
    land_pair,
    sum_pair,
    land_square,
    sum_square,
    land_line,
    stat,
    stat_pair,
    stat_square,
    stat_line,
    send_sem,
    recv_sem,
):
    grid = Grid()
    rows, wide = table.shape
    count = head.shape[0]
    total_mask = 32 * count
    grid.greet()
    sender = Sender(send_sem, recv_sem)
    line, square, core = grid.line, grid.square, grid.core
    flying = [sender.start(head, heads.at[line, square, core], peer) for peer, _ in grid.lines]
    heads[line, square, core] = head[...]

    def table_step(index, carry):
        at = pl.ds(pl.multiple_of(index * 128, 128), 128)
        table_t[:, at] = table[at].astype(jnp.float32).T.astype(jnp.bfloat16)
        return carry

    lax.fori_loop(0, rows // 128, table_step, 0)
    wait_all(flying)
    flying = [
        sender.start(heads.at[:, square, core], heads.at[:, square, core], peer)
        for peer, _ in grid.squares
    ]

    def bias_step(index, carry):
        at = pl.ds(pl.multiple_of(index * 128, 128), 128)
        bias_col[at] = jnp.broadcast_to(bias[:, at], (128, 128)).T
        return carry

    lax.fori_loop(0, rows // 128, bias_step, 0)
    wait_all(flying)
    sender.start(heads.at[:, :, core], heads.at[:, :, core], grid.twin).wait()

    all_heads = heads[...].reshape(total_mask, wide)
    slab = rows // 8

    def logit_step(index, carry):
        at = pl.ds(pl.multiple_of(index * slab, 16), slab)
        logits[at] = dot_right_t(table[at], all_heads)
        return carry

    lax.fori_loop(0, 8, logit_step, 0)
    tile = 64
    wide_copies = total_mask // 128

    def value_at(index):
        at = pl.ds(pl.multiple_of(index * tile, tile), tile)
        shift = bias_col[at]
        return at, logits[at] + jnp.concatenate([shift] * wide_copies, axis=1)

    def top_step(index, top):
        at, value = value_at(index)
        return jnp.maximum(top, jnp.max(value.reshape(tile // 8, 8, total_mask), axis=0))

    top = lax.fori_loop(
        0, rows // tile, top_step, jnp.full((8, total_mask), -jnp.inf, jnp.float32)
    )
    top = jnp.max(top, axis=0, keepdims=True)

    def exp_step(index, total):
        at, value = value_at(index)
        value = jnp.exp(value - top)
        expo[at] = value.astype(jnp.bfloat16)
        return total + jnp.sum(value.reshape(tile // 8, 8, total_mask), axis=0)

    total = lax.fori_loop(0, rows // tile, exp_step, jnp.zeros((8, total_mask), jnp.float32))
    total = jnp.sum(total, axis=0, keepdims=True)

    def fold(row):
        return jnp.concatenate([row[:, i * 128 : i * 128 + 128] for i in range(wide_copies)], axis=0)

    def unfold(block):
        return jnp.concatenate([block[i : i + 1] for i in range(wide_copies)], axis=1)

    own_top, own_total = fold(top), fold(total)
    target = (
        jnp.sum(head[...].astype(jnp.float32) * target_vecs[...], axis=1, keepdims=True)
        + target_bias[:, 0:1]
    )
    own_target = jnp.broadcast_to(jnp.sum(target, axis=0, keepdims=True), own_top.shape)
    stat[0, 0], stat[0, 1], stat[0, 2] = own_top, own_total, own_target
    copy = sender.start(stat.at[0], stat_pair, grid.twin)
    quarter = total_mask // 4
    parts = [dot_plain(table_t[...], expo[:, :quarter])]
    copy.wait()
    stat[1, 0], stat[1, 1], stat[1, 2] = merge_stats(
        [(own_top, own_total, own_target), (stat_pair[0], stat_pair[1], stat_pair[2])]
    )
    stat_square[square] = stat[1]
    flying = [sender.start(stat.at[1], stat_square.at[square], peer) for peer, _ in grid.squares]
    parts.append(dot_plain(table_t[...], expo[:, quarter : 2 * quarter]))
    wait_all(flying)
    stat[2, 0], stat[2, 1], stat[2, 2] = merge_stats(
        [(stat_square[i, 0], stat_square[i, 1], stat_square[i, 2]) for i in range(4)]
    )
    stat_line[line] = stat[2]
    flying = [sender.start(stat.at[2], stat_line.at[line], peer) for peer, _ in grid.lines]
    parts.append(dot_plain(table_t[...], expo[:, 2 * quarter : 3 * quarter]))
    parts.append(dot_plain(table_t[...], expo[:, 3 * quarter :]))
    wait_all(flying)
    full_top, full_total, full_target = merge_stats(
        [(stat_line[i, 0], stat_line[i, 1], stat_line[i, 2]) for i in range(4)]
    )
    lse = full_top + jnp.log(full_total)
    all_lse = jnp.sum(jnp.sum(lse, axis=1, keepdims=True), axis=0, keepdims=True)
    total_loss[...] = (all_lse - full_target[0:1]) * grad_scale
    mine = lax.broadcasted_iota(jnp.int32, (count, total_mask), 0) + lax.axis_index("dp") * count
    hit = mine == lax.broadcasted_iota(jnp.int32, (count, total_mask), 1)
    own_lse = jnp.sum(jnp.where(hit, unfold(lse), 0.0), axis=1, keepdims=True)
    losses[...] = jnp.broadcast_to(own_lse - target, losses.shape)
    scale = unfold(jnp.exp(own_top - lse) * grad_scale)
    per = 128 // count
    for index in range(total_mask // 128):
        at = slice(index * 128, index * 128 + 128)
        source = parts[index * 128 // quarter]
        begin = index * 128 % quarter
        piece = (source[:, begin : begin + 128] * scale[:, at]).T.astype(jnp.bfloat16)
        for inner in range(per):
            owner = index * per + inner
            part[owner // 8, owner // 2 % 4, owner % 2] = piece[inner * count : inner * count + count]
    copy = sender.start(part.at[:, :, 1 - core], land_pair, grid.twin)

    scaled = []
    for index in range(total_mask // 128):
        at = slice(index * 128, index * 128 + 128)
        column = jnp.broadcast_to(scale[:, at], (128, 128)).T
        column = jnp.concatenate([column] * (wide // 128), axis=1)
        scaled.append((all_heads[at].astype(jnp.float32) * column).astype(jnp.bfloat16))
    scaled = jnp.concatenate(scaled, axis=0)
    slab = rows // 4

    def grad_part(index):
        at = slice(index * slab, index * slab + slab)
        table_grad[at] = dot_plain(expo[at], scaled)

    grad_part(0)
    copy.wait()
    sum_pair[...] = (part[:, :, core].astype(jnp.float32) + land_pair[...].astype(jnp.float32)).astype(
        jnp.bfloat16
    )
    flying = [
        sender.start(sum_pair.at[:, other], land_square.at[square], peer)
        for peer, other in grid.squares
    ]
    land_square[square] = sum_pair[:, square]
    grad_part(1)
    wait_all(flying)
    sum_square[...] = sum(land_square[i].astype(jnp.float32) for i in range(4)).astype(jnp.bfloat16)
    flying = [
        sender.start(sum_square.at[other], land_line.at[line], peer) for peer, other in grid.lines
    ]
    land_line[line] = sum_square[line]
    grad_part(2)
    high = scale.astype(jnp.bfloat16)
    low = (scale - high.astype(jnp.float32)).astype(jnp.bfloat16)
    both = jnp.concatenate(
        [high.astype(jnp.float32), low.astype(jnp.float32), jnp.zeros((14, total_mask), jnp.float32)],
        axis=0,
    ).astype(jnp.bfloat16)
    sums = dot_right_t(both, expo[...])
    bias_grad[...] = sums[0:1] + sums[1:2]
    grad_part(3)
    wait_all(flying)
    head_grad[...] = sum(land_line[i].astype(jnp.float32) for i in range(4))


def head_and_table(
    head_low, entity_table, bias_row, target_vecs, target_bias, grad_scale, collective_id
):
    count, wide = head_low.shape
    rows = entity_table.shape[0]
    total_mask = 32 * count
    low, full = jnp.bfloat16, jnp.float32
    vmem = pl.BlockSpec(memory_space=pltpu.VMEM)
    folded = (total_mask // 128, 128)
    return pl.pallas_call(
        functools.partial(head_kernel, grad_scale),
        out_shape=[
            jax.ShapeDtypeStruct((rows, wide), full),
            jax.ShapeDtypeStruct((1, rows), full),
            jax.ShapeDtypeStruct((count, 128), full),
            jax.ShapeDtypeStruct((1, 128), full),
            jax.ShapeDtypeStruct((count, wide), full),
        ],
        in_specs=[vmem] * 5,
        out_specs=[vmem] * 5,
        scratch_shapes=[
            pltpu.VMEM((4, 4, 2, count, wide), low),
            pltpu.VMEM((rows, total_mask), full),
            pltpu.VMEM((rows, total_mask), low),
            pltpu.VMEM((wide, rows), low),
            pltpu.VMEM((rows, 128), full),
            pltpu.VMEM((4, 4, 2, count, wide), low),
            pltpu.VMEM((4, 4, count, wide), low),
            pltpu.VMEM((4, 4, count, wide), low),
            pltpu.VMEM((4, 4, count, wide), low),
            pltpu.VMEM((4, count, wide), low),
            pltpu.VMEM((4, count, wide), low),
            pltpu.VMEM((3, 3) + folded, full),
            pltpu.VMEM((3,) + folded, full),
            pltpu.VMEM((4, 3) + folded, full),
            pltpu.VMEM((4, 3) + folded, full),
            pltpu.SemaphoreType.DMA((24,)),
            pltpu.SemaphoreType.DMA((24,)),
        ],
        compiler_params=pltpu.CompilerParams(
            collective_id=collective_id, has_side_effects=True, vmem_limit_bytes=60 * 2**20
        ),
    )(head_low, entity_table, bias_row, target_vecs, target_bias)


def norm_slope(value, given, gain):
    scaled, rate = norm_parts(value)
    back = given * gain
    mean_back = jnp.mean(back, axis=-1, keepdims=True)
    mean_both = jnp.mean(back * scaled, axis=-1, keepdims=True)
    grad = rate * (back - mean_back - scaled * mean_both)
    return (
        grad,
        jnp.sum(given * scaled, axis=0, keepdims=True),
        jnp.sum(given, axis=0, keepdims=True),
    )


def split_low(value):
    high = value.astype(jnp.bfloat16)
    return high, (value - high.astype(jnp.float32)).astype(jnp.bfloat16)


def place_rows(source, order, count, store):
    owners = 2 ** len(order)
    for pair in range(owners // 2):
        one, two = place_owner(order, 2 * pair), place_owner(order, 2 * pair + 1)
        both = jnp.concatenate(
            [source[one * count : one * count + count], source[two * count : two * count + count]],
            axis=0,
        )
        store(slice(pair * 2 * count, (pair + 1) * 2 * count), both.astype(jnp.bfloat16))


def middle_back_kernel(
    orders,
    grad_scale,
    head_grad,
    target_vecs,
    head_pre,
    gain_head,
    picked,
    head_w,
    choose,
    cotangent,
    resid_two,
    gain_two,
    normed_low,
    resid_one,
    gain_one,
    out_w,
    context,
    lse_lanes,
    active_hbm,
    slope_hbm,
    up_hbm,
    down_hbm,
    up_a,
    head_a,
    out_b,
    down_b,
    up_c,
    down_c,
    first_grad,
    context_grad,
    lse_delta,
    head_vectors,
    wide_vectors,
    active,
    slope,
    up_w,
    down_w,
    flip,
    normed_t,
    context_t,
    down_in,
    acc,
    up_low,
    stage_a,
    stage_c,
    sems,
):
    seq_len, width = cotangent.shape
    slots = choose.shape[1]
    words = seq_len - slots
    cuts = down_w.shape[0] // width
    loads = []
    for index, (source, target) in enumerate(
        ((active_hbm, active), (down_hbm, down_w), (slope_hbm, slope), (up_hbm, up_w))
    ):
        for cut in range(cuts):
            at = pl.ds(cut * width, width)
            view = (at,) if index == 1 else (slice(None), at)
            loads.append(
                pltpu.make_async_copy(source.at[view], target.at[view], sems.at[index * cuts + cut])
            )
    for cut in range(cuts):
        for index in range(4):
            loads[index * cuts + cut].start()

    given = head_grad[...] - grad_scale * target_vecs[...]
    pre = head_pre[...]
    raised, change = gelu_parts(pre)
    back, gain_sum, bias_sum = norm_slope(raised, given, gain_head[...])
    head_vectors[0:1] = gain_sum
    head_vectors[1:2] = bias_sum
    head_vectors[2:8] = jnp.zeros((6, head_vectors.shape[1]), jnp.float32)
    pre_low = (back * change).astype(jnp.bfloat16)
    head_weight_grad = dot_left_t(picked[...], pre_low)
    count = width // 2 ** len(orders[0])

    def keep_head(at, value):
        head_a[0, at] = value

    flip[:, : head_a.shape[2]] = head_weight_grad
    place_rows(flip[:, : head_a.shape[2]], orders[0], count, keep_head)
    picked_high, picked_rest = split_low(dot_right_t(pre_low, head_w[...]))
    placed = dot_left_t(choose[...], picked_high) + dot_left_t(choose[...], picked_rest)

    block = 128
    total_gain = jnp.zeros((1, width), jnp.float32)
    total_bias = jnp.zeros((1, width), jnp.float32)
    for begin in range(0, seq_len, block):
        at = slice(begin, begin + block)
        given = cotangent[at].astype(jnp.float32)
        if begin >= words:
            given = given + placed[begin - words : begin - words + block]
        grad, gain_sum, bias_sum = norm_slope(resid_two[at], given, gain_two[...])
        total_gain += gain_sum
        total_bias += bias_sum
        acc[at] = grad
        down_in[at] = grad.astype(jnp.bfloat16)
    wide_vectors[0:1] = total_gain
    wide_vectors[1:2] = total_bias

    def flip_into(source, target, order_list):
        def flip_step(index, carry):
            at = pl.ds(pl.multiple_of(index * block, block), block)
            flip[at] = source[:, at].astype(jnp.float32).T
            return carry

        lax.fori_loop(0, width // block, flip_step, 0)
        for slot, order in enumerate(order_list):

            def keep(at, value, slot=slot):
                target[slot, at] = value

            place_rows(flip, order, count, keep)

    flip_into(normed_low, normed_t, (orders[0], orders[2]))
    flip_into(context, context_t, (orders[1],))

    column = 384
    split = down_b.shape[2]
    owners = 2 ** len(orders[0])
    tall = down_w.shape[0] // owners
    spots = [
        {place_owner(order, place): place for place in range(owners)}
        for order in (orders[1], orders[2])
    ]
    stores = []
    for cut in range(cuts):
        at = slice(cut * width, cut * width + width)
        for index in range(4):
            loads[index * cuts + cut].wait()
        for begin in range(0, width, column):
            piece = dot_left_t(active[:, at], down_in[:, begin : begin + column])
            for inner in range(width // tall):
                owner = cut * (width // tall) + inner
                rows = piece[inner * tall : inner * tall + tall].astype(jnp.bfloat16)
                stop = min(begin + column, split)
                if begin < split:
                    place = spots[0][owner] * tall
                    stage_a[place : place + tall, begin:stop] = rows[:, : stop - begin]
                if begin + column > split:
                    start = max(begin, split)
                    place = spots[1][owner] * tall
                    stage_c[place : place + tall, start - split : begin + column - split] = rows[
                        :, start - begin :
                    ]

        def back_step(index, carry, at=at):
            span = seq_len // 4
            rows = pl.ds(pl.multiple_of(index * span, 16), span)
            grad = dot_right_t(down_in[rows], down_w[at]) * slope[rows, at].astype(jnp.float32)
            grad = grad.astype(jnp.bfloat16)
            up_low[rows] = grad
            acc[rows] = acc[rows] + dot_right_t(grad, up_w[:, at])
            return carry

        lax.fori_loop(0, 4, back_step, 0)
        target, slot, order_slot = (up_a, cut, 0) if cut < cuts - 1 else (up_c, 0, 1)
        for begin in range(0, width, column):
            target[slot, :, begin : begin + column] = dot_plain(
                normed_t[order_slot], up_low[:, begin : begin + column]
            ).astype(jnp.bfloat16)
    stores = [
        pltpu.make_async_copy(stage_a, down_b.at[0], sems.at[4 * cuts]),
        pltpu.make_async_copy(stage_c, down_c.at[0], sems.at[4 * cuts + 1]),
    ]
    for store in stores:
        store.start()

    total_gain = jnp.zeros((1, width), jnp.float32)
    total_bias = jnp.zeros((1, width), jnp.float32)
    row = lax.broadcasted_iota(jnp.int32, (width, 128), 0)
    lane = lax.broadcasted_iota(jnp.int32, (width, 128), 1)
    spot = 4 * lax.div(row, 128) + 2 + lax.div(lax.rem(row, 128), HD)
    pick = (spot == lane).astype(jnp.float32).astype(jnp.bfloat16)
    for begin in range(0, seq_len, block):
        at = slice(begin, begin + block)
        grad, gain_sum, bias_sum = norm_slope(resid_one[at], acc[at], gain_one[...])
        total_gain += gain_sum
        total_bias += bias_sum
        first_grad[at] = grad
        low = grad.astype(jnp.bfloat16)
        down_in[at] = low
        back = dot_right_t(low, out_w[...]).astype(jnp.bfloat16)
        context_grad[at] = back
        high, rest = split_low(back.astype(jnp.float32) * context[at].astype(jnp.float32))
        lse_delta[at] = lse_lanes[at] + dot_plain(high, pick) + dot_plain(rest, pick)
    wide_vectors[2:3] = total_gain
    wide_vectors[3:4] = total_bias
    wide_vectors[4:8] = jnp.zeros((4, width), jnp.float32)
    for begin in range(0, width, column):
        out_b[0, :, begin : begin + column] = dot_plain(
            context_t[0], down_in[:, begin : begin + column]
        ).astype(jnp.bfloat16)
    for store in stores:
        store.wait()


DOWN_SPLIT = 512


def middle_back(inputs, orders, grad_scale):
    seq_len, width = inputs[7].shape
    hidden_units = inputs[16].shape[1]
    head_width = inputs[0].shape[1]
    low, full = jnp.bfloat16, jnp.float32
    cuts = hidden_units // width
    vmem, hbm = pl.BlockSpec(memory_space=pltpu.VMEM), pl.BlockSpec(memory_space=pltpu.HBM)
    shapes = [
        ((cuts - 1, width, width), low),
        ((1, width, head_width), low),
        ((1, width, width), low),
        ((1, hidden_units, DOWN_SPLIT), low),
        ((1, width, width), low),
        ((1, hidden_units, width - DOWN_SPLIT), low),
        ((seq_len, width), full),
        ((seq_len, width), low),
        ((seq_len, 128), full),
        ((8, head_width), full),
        ((8, width), full),
    ]
    return pl.pallas_call(
        functools.partial(middle_back_kernel, orders, grad_scale),
        out_shape=[jax.ShapeDtypeStruct(*shape) for shape in shapes],
        in_specs=[vmem] * 16 + [hbm] * 4,
        out_specs=[hbm if index in (3, 5) else vmem for index in range(len(shapes))],
        scratch_shapes=[
            pltpu.VMEM((seq_len, hidden_units), low),
            pltpu.VMEM((seq_len, hidden_units), low),
            pltpu.VMEM((width, hidden_units), low),
            pltpu.VMEM((hidden_units, width), low),
            pltpu.VMEM((width, seq_len), full),
            pltpu.VMEM((2, width, seq_len), low),
            pltpu.VMEM((1, width, seq_len), low),
            pltpu.VMEM((seq_len, width), low),
            pltpu.VMEM((seq_len, width), full),
            pltpu.VMEM((seq_len, width), low),
            pltpu.VMEM((hidden_units, DOWN_SPLIT), low),
            pltpu.VMEM((hidden_units, width - DOWN_SPLIT), low),
            pltpu.SemaphoreType.DMA((4 * cuts + 2,)),
        ],
        compiler_params=pltpu.CompilerParams(vmem_limit_bytes=62 * 2**20),
    )(*inputs)


def scatter_kernel(grad_scale, codes, back, table_in, bias_in, table_out, bias_out):
    rows, wide = table_in.shape
    entries = back.shape[0]
    code = codes[0:1]
    target = (code >= rows).astype(jnp.float32)
    flags = jnp.broadcast_to(target, (16, entries)).astype(jnp.bfloat16)
    code = jnp.where(code >= rows, code - rows, code)
    step = 1024
    for begin in range(0, rows, step):
        size = min(step, rows - begin)
        row = lax.broadcasted_iota(jnp.int32, (size, entries), 0) + begin
        match = (row == code).astype(jnp.float32).astype(jnp.bfloat16)
        at = slice(begin, begin + size)
        table_out[at] = table_in[at] + dot_plain(match, back[...])
        counts = dot_right_t(flags, match)
        bias_out[:, at] = bias_in[:, at] - grad_scale * counts[0:1]


def scatter_add(codes, back, table_grad, bias_grad, grad_scale):
    vmem = pl.BlockSpec(memory_space=pltpu.VMEM)
    return pl.pallas_call(
        functools.partial(scatter_kernel, grad_scale),
        out_shape=[
            jax.ShapeDtypeStruct(table_grad.shape, jnp.float32),
            jax.ShapeDtypeStruct(bias_grad.shape, jnp.float32),
        ],
        in_specs=[vmem] * 4,
        out_specs=[vmem] * 2,
        compiler_params=pltpu.CompilerParams(vmem_limit_bytes=40 * 2**20),
    )(codes, back, table_grad, bias_grad)


def place_owner(order, place):
    bits = len(order)
    return sum(((place >> (bits - 1 - spot)) & 1) * mask for spot, mask in enumerate(order))


class Piece:
    def __init__(self, rows, stages, send, own, land, tail, tail_land, out, send_sem, recv_sem):
        self.rows, self.stages = rows, stages
        self.send, self.own, self.land = send, own, land
        self.tail, self.tail_land, self.out = tail, tail_land, out
        self.send_sem, self.recv_sem = send_sem, recv_sem
        self.sizes = [rows * 2 ** (stages - 1 - stage) for stage in range(stages)]
        self.spots = [sum(self.sizes[:stage]) for stage in range(stages)]

    def copy(self, stage, partner, bit):
        size = self.sizes[stage]
        away = pl.multiple_of((1 - bit) * size, 8 if stage == self.stages - 1 else 16)
        if stage == 0:
            source, target = self.send.at[:, pl.ds(away, size)], self.land.at[:, pl.ds(0, size)]
        elif stage < self.stages - 1:
            spot = pl.multiple_of(self.spots[stage - 1] + away, 16)
            source = self.land.at[:, pl.ds(spot, size)]
            target = self.land.at[:, pl.ds(self.spots[stage], size)]
        else:
            source, target = self.tail.at[:, pl.ds(away, size)], self.tail_land
        return pltpu.make_async_remote_copy(
            src_ref=source,
            dst_ref=target,
            send_sem=self.send_sem.at[stage],
            recv_sem=self.recv_sem.at[stage],
            device_id=(partner,),
            device_id_type=MESH_ID,
        )

    def held(self, stage, bit):
        size = self.sizes[stage]
        if stage == 0 and self.own is not None:
            return self.own, 0
        if stage == 0:
            return self.send, pl.multiple_of(bit * size, 16)
        return self.land, pl.multiple_of(self.spots[stage - 1] + bit * size, 16)

    def add(self, stage, bit, half_index):
        size = self.sizes[stage]
        half = size // 2
        unit = 48 if half % 48 == 0 else 16
        start = half_index * half
        source, base = self.held(stage, bit)
        for slot in range(self.land.shape[0]):

            def step(index, carry, slot=slot):
                row = pl.multiple_of(start + index * unit, 16)
                mine = source[slot, pl.ds(pl.multiple_of(base + row, 16), unit)]
                spot = pl.ds(pl.multiple_of(self.spots[stage] + row, 16), unit)
                theirs = self.land[slot, spot]
                total = mine.astype(jnp.float32) + theirs.astype(jnp.float32)
                self.land[slot, spot] = total.astype(jnp.bfloat16)
                return carry

            lax.fori_loop(0, half // unit, step, 0)

    def add_tail(self, stage, bit):
        size = self.sizes[stage]
        source, base = self.held(stage, bit)
        for slot in range(self.land.shape[0]):
            mine = source[slot, pl.ds(base, size)]
            theirs = self.land[slot, pl.ds(self.spots[stage], size)]
            self.tail[slot] = mine.astype(jnp.float32) + theirs.astype(jnp.float32)

    def finish(self, bit):
        size = self.sizes[-1]
        for slot in range(self.out.shape[0]):
            mine = self.tail[slot, pl.ds(pl.multiple_of(bit * size, 8), size)]
            self.out[slot] = mine + self.tail_land[slot]


class Stream:
    def __init__(self, order, partner_of, pieces):
        self.order, self.partner_of, self.pieces = order, partner_of, pieces
        self.stages = len(order)

    def launch(self, stage):
        partner, bit = self.partner_of[self.order[stage]]
        for piece in self.pieces:
            piece.copy(stage, partner, bit).start()

    def advance(self, stage):
        partner, bit = self.partner_of[self.order[stage]]
        for piece in self.pieces:
            piece.copy(stage, partner, bit).wait()
        if stage == self.stages - 1:
            for piece in self.pieces:
                piece.finish(bit)
        elif stage == self.stages - 2:
            for piece in self.pieces:
                piece.add_tail(stage, bit)
            self.launch(stage + 1)
        else:
            following = self.partner_of[self.order[stage + 1]][1]
            for piece in self.pieces:
                piece.add(stage, bit, 1 - following)
            self.launch(stage + 1)
            for piece in self.pieces:
                piece.add(stage, bit, following)


def partners(me, masks):
    result = {}
    for mask in masks:
        bit = lax.rem(lax.div(me, mask), 2)
        result[mask] = (me + mask - 2 * mask * bit, bit)
    return result


EARLY = (
    (0, 3, 24, 768),
    (0, 1, 24, 256),
    (0, 1, 8, 128),
    (1, 1, 24, 768),
    (1, 1, 96, 512),
    (2, 1, 24, 768),
    (2, 1, 96, 256),
)
LATE = ((0, 2, 24, 768), (0, 1, 8, 768), (1, 2, 24, 768), (2, 2, 24, 768))


def piece_scratch(spec, stages, source, own):
    _, slots, rows, width = spec
    owners = 2**stages
    shapes = []
    if source:
        shapes.append(pltpu.VMEM((slots, rows * owners, width), jnp.bfloat16))
    if own:
        shapes.append(pltpu.VMEM((slots, rows * owners // 2, width), jnp.bfloat16))
    shapes += [
        pltpu.VMEM((slots, rows * (owners - 2), width), jnp.bfloat16),
        pltpu.VMEM((slots, 2 * rows, width), jnp.float32),
        pltpu.VMEM((slots, rows, width), jnp.float32),
        pltpu.SemaphoreType.DMA((stages,)),
        pltpu.SemaphoreType.DMA((stages,)),
    ]
    return shapes


def attention_back_kernel(orders, *refs):
    stages = len(orders[0])
    refs = list(refs)

    def take(count):
        taken = refs[:count]
        del refs[:count]
        return taken

    early_send = take(len(EARLY))
    (hidden, qword, qent, keys, values, cgrad, feat_q, feat_k, lse_delta, first_grad, target_grad, slot_row) = take(12)
    (w_ww, w_we, w_ew, w_ee, w_key, w_value, dense, entity_low) = take(8)
    early_out = take(len(EARLY))
    late_out = take(len(LATE))
    words_out, request_out = take(2)
    devices = request_out.shape[0]
    early_pieces = []
    own_copies = []
    me = lax.axis_index("dp")
    partner_of = partners(me, orders[0])
    own_sem = refs.pop()
    request_sems = refs.pop()
    request_send = refs.pop()
    word_weights = []
    dqw, dqe, dkey, dvalue, prob_s, grad_s, flip, hidden_t, hidden_te, entity_t = refs[-10:]
    del refs[-10:]
    early = [[], [], []]
    for index, spec in enumerate(EARLY):
        own, land, tail, tail_land, send_sem, recv_sem = take(6)
        early[spec[0]].append(
            Piece(
                spec[2], stages, early_send[index], own, land, tail, tail_land,
                early_out[index], send_sem, recv_sem,
            )
        )
        bit = partner_of[orders[spec[0]][0]][1]
        size = spec[2] * 2 ** (stages - 1)
        own_copies.append(
            pltpu.make_async_copy(
                early_send[index].at[:, pl.ds(pl.multiple_of(bit * size, 16), size)],
                own,
                own_sem.at[index],
            )
        )
    late, late_source = [[], [], []], []
    for index, spec in enumerate(LATE):
        source, land, tail, tail_land, send_sem, recv_sem = take(6)
        late_source.append(source)
        late[spec[0]].append(
            Piece(
                spec[2], stages, source, None, land, tail, tail_land,
                late_out[index], send_sem, recv_sem,
            )
        )
    spare = (early[1][1].own, early[2][1].own)
    split = spare[0].shape[2]
    for index, weight in enumerate((w_ww, w_we)):
        rows = weight.shape[0]
        for part, at in enumerate((pl.ds(0, split), pl.ds(split, weight.shape[1] - split))):
            word_weights.append(
                pltpu.make_async_copy(
                    weight.at[:, at],
                    spare[part].at[0, pl.ds(index * rows, rows)],
                    own_sem.at[len(EARLY) + 2 * index + part],
                )
            )
    early = [Stream(orders[i], partner_of, early[i]) for i in range(3)]
    late = [Stream(orders[i], partner_of, late[i]) for i in range(3)]

    greet_all(me, devices)
    for stream in early:
        stream.launch(0)
    for copy in own_copies:
        copy.start()

    width = hidden.shape[1]
    seq_len = hidden.shape[0]
    words = words_out.shape[0]
    block = 128
    lane = lax.broadcasted_iota(jnp.int32, (1, block), 1)
    low_half = (lane < HD).astype(jnp.float32).astype(jnp.bfloat16)
    high_half = (lane >= HD).astype(jnp.float32).astype(jnp.bfloat16)
    halves = (low_half, high_half)

    def flip_step(index, carry):
        at = pl.ds(pl.multiple_of(index * block, block), block)
        flip[at] = hidden[:, at].astype(jnp.float32).T
        return carry

    lax.fori_loop(0, width // block, flip_step, 0)
    owners = 2**stages
    rows = width // owners
    for slot, order in enumerate(orders):
        begin = words if slot == 2 else 0
        for pair in range(owners // 2):
            one, two = place_owner(order, 2 * pair), place_owner(order, 2 * pair + 1)
            both = jnp.concatenate(
                [flip[one * rows : one * rows + rows, begin:], flip[two * rows : two * rows + rows, begin:]],
                axis=0,
            ).astype(jnp.bfloat16)
            if slot == 2:
                hidden_te[pair * 2 * rows : (pair + 1) * 2 * rows] = both
            else:
                hidden_t[slot, pair * 2 * rows : (pair + 1) * 2 * rows] = both

    def pair_step(pair, carry):
        lanes = pl.ds(pl.multiple_of(pair * block, block), block)
        key_pair = keys[:, lanes]
        value_pair = values[:, lanes]
        key_feat = [key_pair * halves[h] + feat_k[...] * halves[1 - h] for h in range(2)]
        key_only = [key_pair * halves[h] for h in range(2)]
        value_only = [value_pair * halves[h] for h in range(2)]

        def row_step(index, inner):
            at = pl.ds(pl.multiple_of(index * block, block), block)
            qw = qword[at, lanes]
            qe = qent[at, lanes]
            feats = feat_q[at]
            given = cgrad[at, lanes]
            stats = lse_delta[at]
            spot = lax.broadcasted_iota(jnp.int32, (1, block), 1) - 4 * pair
            total_w = jnp.zeros((block, block), jnp.float32)
            total_e = jnp.zeros((block, block), jnp.float32)
            for h in range(2):
                left_w = qw * halves[h] + feats * halves[1 - h]
                left_e = qe * halves[h] + feats * halves[1 - h]
                scores = jnp.concatenate(
                    [
                        dot_right_t(left_w, key_feat[h][:words]),
                        dot_right_t(left_e, key_feat[h][words:]),
                    ],
                    axis=1,
                )
                prob = jnp.exp(scores - jnp.sum(jnp.where(spot == h, stats, 0.0), axis=1, keepdims=True))
                pgrad = dot_right_t(given, value_only[h])
                sgrad = (prob * (pgrad - jnp.sum(jnp.where(spot == 2 + h, stats, 0.0), axis=1, keepdims=True))).astype(jnp.bfloat16)
                prob_s[h, at] = prob.astype(jnp.bfloat16)
                grad_s[h, at] = sgrad
                total_w += dot_plain(sgrad[:, :words], key_only[h][:words])
                total_e += dot_plain(sgrad[:, words:], key_only[h][words:])
            dqw[at, lanes] = total_w.astype(jnp.bfloat16)
            dqe[at, lanes] = total_e.astype(jnp.bfloat16)
            return inner

        lax.fori_loop(0, seq_len // block, row_step, 0)
        qw_all, qe_all, given_all = qword[:, lanes], qent[:, lanes], cgrad[:, lanes]
        dkey[:words, lanes] = (
            dot_left_t(grad_s[0, :, :words], qw_all * halves[0])
            + dot_left_t(grad_s[1, :, :words], qw_all * halves[1])
        ).astype(jnp.bfloat16)
        dkey[words:, lanes] = (
            dot_left_t(grad_s[0, :, words:], qe_all * halves[0])
            + dot_left_t(grad_s[1, :, words:], qe_all * halves[1])
        ).astype(jnp.bfloat16)
        dvalue[:, lanes] = (
            dot_left_t(prob_s[0], given_all * halves[0])
            + dot_left_t(prob_s[1], given_all * halves[1])
        ).astype(jnp.bfloat16)

        @pl.when(pair == 2)
        def _():
            for copy in own_copies:
                copy.wait()
            for stream in early:
                stream.advance(0)
            for copy in word_weights:
                copy.start()

        return carry

    lax.fori_loop(0, width // block, pair_step, 0)

    query_scale = HD ** (-0.5)
    column = 384

    def weight_grad(source, slot, order_slot, grad, begin, end, scale):
        for cut in range(0, width, column):
            left = hidden_te[...] if order_slot == 2 else hidden_t[order_slot, :, begin:end]
            piece = dot_plain(left, grad[begin:end, cut : cut + column])
            if scale:
                piece = piece * query_scale
            source[slot, :, cut : cut + column] = piece.astype(jnp.bfloat16)

    weight_grad(late_source[2], 0, 1, dkey, 0, seq_len, False)
    weight_grad(late_source[2], 1, 1, dvalue, 0, seq_len, False)
    late[1].launch(0)
    for stream in early:
        stream.advance(1)
    weight_grad(late_source[3], 0, 2, dqw, words, seq_len, True)
    weight_grad(late_source[3], 1, 2, dqe, words, seq_len, True)
    late[2].launch(0)

    def data_grad(begin, size, queries):
        at = pl.ds(begin, size)
        return (
            first_grad[at]
            + query_scale * queries(at)
            + dot_right_t(dkey[at], w_key[...])
            + dot_right_t(dvalue[at], w_value[...])
        )

    def entity_queries(at):
        return dot_right_t(dqw[at], w_ew[...]) + dot_right_t(dqe[at], w_ee[...])

    def word_queries(at):
        total = 0.0
        for index, grad in enumerate((dqw, dqe)):
            rows_at = pl.ds(index * width, width)
            total += dot_right_t(grad[at, :split], spare[0][0, rows_at])
            total += dot_right_t(grad[at, split:], spare[1][0, rows_at])
        return total

    state_low = data_grad(words, seq_len - words, entity_queries).astype(jnp.bfloat16)
    vectors = jnp.concatenate(
        [dot_right_t(state_low, dense[...]).astype(jnp.bfloat16), target_grad[...]], axis=0
    )
    entries = slot_row.shape[1]
    wanted = lax.broadcasted_iota(jnp.int32, (vectors.shape[0], entries), 0)
    placing = (wanted == slot_row[0:1]).astype(jnp.float32).astype(jnp.bfloat16)
    per_request = dot_left_t(placing, vectors).astype(jnp.bfloat16)
    request_send[...] = per_request.reshape(request_send.shape)

    def request_copy(step):
        peer = lax.rem(me + step, devices)
        return pltpu.make_async_remote_copy(
            src_ref=request_send.at[peer],
            dst_ref=request_out.at[me],
            send_sem=request_sems.at[0, step],
            recv_sem=request_sems.at[1, step],
            device_id=(peer,),
            device_id_type=MESH_ID,
        )

    def begin_request(step, carry):
        request_copy(step).start()
        return carry

    def finish_request(step, carry):
        request_copy(step).wait()
        return carry

    lax.fori_loop(1, devices, begin_request, 0)
    request_out[me] = request_send[me]
    entity_width = dense.shape[0]
    few = entity_width // owners
    for cut in range(0, entity_width, block):
        flip[cut : cut + block, :block] = entity_low[:, cut : cut + block].astype(jnp.float32).T
    for pair in range(owners // 2):
        one, two = place_owner(orders[0], 2 * pair), place_owner(orders[0], 2 * pair + 1)
        both = jnp.concatenate(
            [flip[one * few : one * few + few, :block], flip[two * few : two * few + few, :block]],
            axis=0,
        )
        entity_t[pair * 2 * few : (pair + 1) * 2 * few] = both.astype(jnp.bfloat16)
    late_source[1][0] = dot_plain(entity_t[...], state_low).astype(jnp.bfloat16)
    weight_grad(late_source[0], 0, 0, dqw, 0, words, True)
    weight_grad(late_source[0], 1, 0, dqe, 0, words, True)
    late[0].launch(0)
    for stream in early:
        stream.advance(2)

    for copy in word_weights:
        copy.wait()

    def word_step(index, carry):
        begin = pl.multiple_of(index * block, block)
        words_out[pl.ds(begin, block)] = data_grad(begin, block, word_queries).astype(jnp.bfloat16)
        return carry

    lax.fori_loop(0, words // block, word_step, 0)
    for turn in ((late[1], 0), (late[2], 0), (late[0], 0)):
        turn[0].advance(turn[1])
    for stream in early:
        stream.advance(3)
    for stream in late:
        stream.advance(1)
    for stream in early:
        stream.advance(4)
    for stage in (2, 3, 4):
        for stream in late:
            stream.advance(stage)
    lax.fori_loop(1, devices, finish_request, 0)


def in_order(grad, order):
    bits = len(order)
    owners = 2**bits
    view = grad.reshape((2,) * bits + (grad.shape[0] // owners, grad.shape[1]))
    spots = tuple(bits - mask.bit_length() for mask in order)
    return view.transpose(spots + (bits, bits + 1)).reshape(grad.shape)


def attention_back(early_grads, inputs, weights, collective_id):
    devices = lax.axis_size("dp")
    orders = stage_masks(devices)
    stages = len(orders[0])
    hidden = inputs[0]
    seq_len, width = hidden.shape
    slots = weights[-1].shape[0]
    words = seq_len - slots
    outs = [
        jax.ShapeDtypeStruct((count, rows, wide), jnp.float32)
        for _, count, rows, wide in EARLY + LATE
    ] + [
        jax.ShapeDtypeStruct((words, width), jnp.bfloat16),
        jax.ShapeDtypeStruct(
            (devices, inputs[11].shape[1] // devices, weights[-2].shape[0]), jnp.bfloat16
        ),
    ]
    scratch = []
    for spec in EARLY:
        scratch += piece_scratch(spec, stages, False, True)
    for spec in LATE:
        scratch += piece_scratch(spec, stages, True, False)
    scratch += [pltpu.VMEM((seq_len, width), jnp.bfloat16)] * 4
    scratch += [pltpu.VMEM((2, seq_len, seq_len), jnp.bfloat16)] * 2
    scratch += [
        pltpu.VMEM((width, seq_len), jnp.float32),
        pltpu.VMEM((2, width, seq_len), jnp.bfloat16),
        pltpu.VMEM((width, slots), jnp.bfloat16),
        pltpu.VMEM((weights[-2].shape[0], slots), jnp.bfloat16),
        pltpu.VMEM((devices, inputs[11].shape[1] // devices, weights[-2].shape[0]), jnp.bfloat16),
        pltpu.SemaphoreType.DMA((2, devices)),
        pltpu.SemaphoreType.DMA((len(EARLY) + 4,)),
    ]
    vmem = pl.BlockSpec(memory_space=pltpu.VMEM)
    return pl.pallas_call(
        functools.partial(attention_back_kernel, orders),
        out_shape=outs,
        in_specs=[pl.BlockSpec(memory_space=pltpu.HBM)] * len(EARLY)
        + [vmem] * len(inputs)
        + [pl.BlockSpec(memory_space=pltpu.HBM)] * 2
        + [vmem] * (len(weights) - 2),
        out_specs=[vmem] * len(outs),
        scratch_shapes=scratch,
        compiler_params=pltpu.CompilerParams(
            collective_id=collective_id, has_side_effects=True, vmem_limit_bytes=62 * 2**20
        ),
    )(*early_grads, *inputs, *weights)


def fused_body(
    word_states,
    word_segments,
    entity_segments,
    request_rows,
    request_slot,
    mask_slots,
    entity_table,
    vocab_bias,
    entity_dense,
    query_ww,
    query_we,
    query_ew,
    query_ee,
    key_weight,
    value_weight,
    out_weight,
    norm1_gain,
    norm1_bias,
    up_weight,
    down_weight,
    norm2_gain,
    norm2_bias,
    head_weight,
    head_gain,
    head_bias,
    cotangent,
):
    devices = lax.axis_size("dp")
    low = jnp.bfloat16
    slot_count = entity_segments.shape[1]
    mask_count = mask_slots.shape[1]
    request_count = slot_count + mask_count
    table_rows = entity_table.shape[0]
    grad_scale = 1.0 / (mask_count * devices)
    orders = stage_masks(devices)
    capacity = request_rows.shape[1]
    room = -(-capacity // 16) * 16 - capacity
    kind = jnp.where(request_slot >= slot_count, table_rows, 0)
    codes = jnp.where(request_slot < request_count, request_rows + kind, -1)
    codes = jnp.pad(codes, ((0, 0), (0, room)), constant_values=-1)
    codes = jnp.broadcast_to(codes[:, :, None], codes.shape + (128,))
    slot_row = jnp.pad(request_slot, ((0, 0), (0, room)), constant_values=request_count)
    slot_row = jnp.broadcast_to(slot_row.reshape(1, -1), (8, slot_row.size))
    bias_col = jnp.broadcast_to(vocab_bias[:, None], (table_rows, 128))
    entity_low, target_vecs, target_bias, code_row = lookup(
        codes, entity_table, bias_col, slot_row, slot_count, mask_count, 0
    )
    segment_row = jnp.concatenate([word_segments[0], entity_segments[0]])
    columns = jnp.arange(128, dtype=jnp.int32)[None, :] % HD
    same = segment_row[:, None] == columns
    feat_q = same.astype(low)
    feat_k = jnp.where(same | (columns >= 4), 0.0, MASKED).astype(low)
    choose = (mask_slots[0][:, None] == jnp.arange(slot_count, dtype=jnp.int32)[None, :]).astype(low)
    (
        hidden_low,
        query_word,
        query_entity,
        key_rows,
        values,
        context_low,
        lse_lanes,
        residual_one,
        normed_low,
        activated,
        gelu_slope,
        residual_two,
        layer_low,
        picked_low,
        head_pre,
        head_low,
    ) = forward_pass(
        [
            word_states,
            entity_low,
            feat_q,
            feat_k,
            choose,
            entity_dense,
            query_ww,
            query_we,
            query_ew,
            query_ee,
            key_weight,
            value_weight,
            out_weight,
            norm1_gain[None],
            norm1_bias[None],
            up_weight,
            down_weight,
            norm2_gain[None],
            norm2_bias[None],
            head_weight,
            head_gain[None],
            head_bias[None],
        ]
    )
    table_grad, bias_grad, losses, total_loss, head_grad = head_and_table(
        head_low,
        entity_table,
        vocab_bias.astype(jnp.float32)[None, :],
        target_vecs,
        target_bias,
        grad_scale,
        1,
    )
    (
        up_a,
        head_a,
        out_b,
        down_b,
        up_c,
        down_c,
        first_grad,
        context_grad,
        lse_delta,
        head_vectors,
        wide_vectors,
    ) = middle_back(
        [
            head_grad,
            target_vecs,
            head_pre,
            head_gain[None],
            picked_low,
            head_weight,
            choose,
            cotangent,
            residual_two,
            norm2_gain[None],
            normed_low,
            residual_one,
            norm1_gain[None],
            out_weight,
            context_low,
            lse_lanes,
            activated,
            gelu_slope,
            up_weight,
            down_weight,
        ],
        orders,
        grad_scale,
    )
    vectors = jnp.concatenate(
        [head_vectors[i].reshape(devices, -1) for i in range(2)]
        + [wide_vectors[i].reshape(devices, -1) for i in range(4)],
        axis=1,
    )
    vectors = jnp.pad(vectors, ((0, 0), (0, 128 - vectors.shape[1])))[:, None, :]
    vectors = jnp.pad(vectors, ((0, 0), (0, 7), (0, 0))).reshape(8 * devices, 128)
    vectors = in_order(vectors.astype(low), orders[0])[None]
    (
        up_sum,
        head_sum,
        vector_sum,
        out_sum,
        down_sum,
        up_rest,
        down_rest,
        q_word,
        dense_sum,
        key_value,
        q_ent,
        words_grad,
        back_rows,
    ) = attention_back(
        [up_a, head_a, vectors, out_b, down_b, up_c, down_c],
        [
            hidden_low,
            query_word,
            query_entity,
            key_rows,
            values,
            context_grad,
            feat_q,
            feat_k,
            lse_delta,
            first_grad,
            (-grad_scale * head_low.astype(jnp.float32)).astype(low),
            slot_row,
        ],
        [
            query_ww,
            query_we,
            query_ew,
            query_ee,
            key_weight,
            value_weight,
            entity_dense,
            entity_low,
        ],
        2,
    )
    table_grad, bias_grad = scatter_add(
        code_row, back_rows.reshape(-1, back_rows.shape[2]), table_grad, bias_grad, grad_scale
    )
    row = vector_sum[0, 0]
    few, many = head_gain.shape[0] // devices, norm1_gain.shape[0] // devices
    spots = [0, few, 2 * few] + [2 * few + many * (i + 1) for i in range(4)]
    vector_out = [row[spots[i] : spots[i + 1]] for i in range(6)]
    return (
        total_loss[0, 0],
        layer_low,
        words_grad,
        table_grad,
        bias_grad[0],
        dense_sum[0],
        q_word[0],
        q_word[1],
        q_ent[0],
        q_ent[1],
        key_value[0],
        key_value[1],
        out_sum[0],
        vector_out[4],
        vector_out[5],
        jnp.concatenate([up_sum[0], up_sum[1], up_sum[2], up_rest[0]], axis=1),
        jnp.concatenate([down_sum[0], down_rest[0]], axis=1),
        vector_out[2],
        vector_out[3],
        head_sum[0],
        vector_out[0],
        vector_out[1],
        losses[:, 0],
    )


def solution(mesh):
    in_specs = (
        P("dp", None),
        P("dp", None),
        P("dp", None),
        P("dp", None),
        P("dp", None),
        P("dp", None),
        P("dp", None),
        P("dp"),
        P(),
        P(),
        P(),
        P(),
        P(),
        P(),
        P(),
        P(),
        P(),
        P(),
        P(),
        P(),
        P(),
        P(),
        P(),
        P(),
        P(),
        P("dp", None),
    )
    out_specs = (
        P(),
        P("dp", None),
        P("dp", None),
        P("dp", None),
        P("dp"),
        P("dp", None),
        P("dp", None),
        P("dp", None),
        P("dp", None),
        P("dp", None),
        P("dp", None),
        P("dp", None),
        P("dp", None),
        P("dp"),
        P("dp"),
        P("dp", None),
        P("dp", None),
        P("dp"),
        P("dp"),
        P("dp", None),
        P("dp"),
        P("dp"),
        P("dp"),
    )
    chosen = fused_body if mesh.shape["dp"] == 32 else body
    return jax.shard_map(chosen, mesh=mesh, in_specs=in_specs, out_specs=out_specs, check_vma=False)
```

```python
import functools

import jax
import jax.numpy as jnp
from jax import lax
from jax.experimental import pallas as pl
from jax.experimental.pallas import tpu as pltpu
from jax.sharding import PartitionSpec as P

MESH_ID = pl.DeviceIdType.MESH

HD = 64


EPSILON = 1e-05
MASKED = -1000000000.0


def dot_plain(left_side, right_side):
    return jnp.dot(left_side, right_side, preferred_element_type=jnp.float32)


def dot_left_t(left_side, right_side):
    return lax.dot_general(
        left_side, right_side, (((0,), (0,)), ((), ())), preferred_element_type=jnp.float32
    )


def dot_right_t(left_side, right_side):
    return lax.dot_general(
        left_side, right_side, (((1,), (1,)), ((), ())), preferred_element_type=jnp.float32
    )


def dot_exact(left_side, right_side):
    return jnp.dot(
        left_side, right_side, precision=lax.Precision.HIGHEST, preferred_element_type=jnp.float32
    )


def layer_norm(tensor, gain_vec, shift_vec):
    center = tensor - jnp.mean(tensor, axis=-1, keepdims=True)
    spread = jnp.mean(center * center, axis=-1, keepdims=True)
    return center * lax.rsqrt(spread + EPSILON) * gain_vec + shift_vec


def gelu_exact(tensor):
    return jax.nn.gelu(tensor, approximate=False)


def head_act(tensor, gain_vec, shift_vec):
    return layer_norm(gelu_exact(tensor), gain_vec, shift_vec)


def norm_back(tensor, gain_vec, shift_vec, grad_out):
    result, pullback = jax.vjp(layer_norm, tensor, gain_vec, shift_vec)
    return pullback(grad_out)


def attn_scores(query_word, query_entity, key_rows, allowed, word_count):
    to_words = jnp.einsum(
        "qhd,khd->hqk", query_word, key_rows[:word_count], preferred_element_type=jnp.float32
    )
    to_entities = jnp.einsum(
        "qhd,khd->hqk", query_entity, key_rows[word_count:], preferred_element_type=jnp.float32
    )
    return jnp.where(allowed[None], jnp.concatenate([to_words, to_entities], axis=2), MASKED)


def greet_all(me, devices):
    barrier = pltpu.get_barrier_semaphore()

    def greet(step, carry):
        pl.semaphore_signal(
            barrier, inc=1, device_id=(lax.rem(me + step, devices),), device_id_type=MESH_ID
        )
        return carry

    lax.fori_loop(1, devices, greet, 0)
    pl.semaphore_wait(barrier, devices - 1)


def swap_kernel(devices, gather, source, target, send_sem, recv_sem):
    me = lax.axis_index("dp")
    greet_all(me, devices)

    def piece(step):
        peer = lax.rem(me + step, devices)
        return pltpu.make_async_remote_copy(
            src_ref=source if gather else source.at[peer],
            dst_ref=target.at[me],
            send_sem=send_sem.at[step],
            recv_sem=recv_sem.at[step],
            device_id=(peer,),
            device_id_type=MESH_ID,
        )

    def begin(step, carry):
        piece(step).start()
        return carry

    def finish(step, carry):
        piece(step).wait()
        return carry

    lax.fori_loop(1, devices, begin, 0)
    target[me] = source[...] if gather else source[me]
    lax.fori_loop(1, devices, finish, 0)


def direct_swap(value, collective_id, gather=False):
    devices = lax.axis_size("dp")
    shape = (devices,) + value.shape if gather else value.shape
    return pl.pallas_call(
        functools.partial(swap_kernel, devices, gather),
        out_shape=jax.ShapeDtypeStruct(shape, value.dtype),
        in_specs=[pl.BlockSpec(memory_space=pltpu.VMEM)],
        out_specs=pl.BlockSpec(memory_space=pltpu.VMEM),
        scratch_shapes=[
            pltpu.SemaphoreType.DMA((devices,)),
            pltpu.SemaphoreType.DMA((devices,)),
        ],
        compiler_params=pltpu.CompilerParams(collective_id=collective_id, has_side_effects=True),
    )(value)


def stage_masks(devices):
    if devices == 32:
        axes = [[2], [4], [8, 16]]
    elif devices == 128:
        axes = [[2, 4], [8, 16], [32, 64]]
    else:
        axes = [[2**bit] for bit in range(1, devices.bit_length() - 1)]
        axes = axes + [[] for _ in range(3 - len(axes))]
    first, second, third = axes[0], axes[1], sum(axes[2:], [])
    return (
        [1] + first + second + third,
        [1] + second + first + third,
        [1] + third + first + second,
    )


def sum_kernel(masks, rows, *refs):
    parts = len(masks)
    stages = len(masks[0])
    sources, results = refs[:parts], refs[parts : 2 * parts]
    landing = refs[2 * parts : 3 * parts]
    send_sem, recv_sem = refs[3 * parts :]
    me = lax.axis_index("dp")
    barrier = pltpu.get_barrier_semaphore()
    partner_of = {}
    for mask in masks[0]:
        bit = lax.rem(lax.div(me, mask), 2)
        partner_of[mask] = (me + mask - 2 * mask * bit, bit)
    for mask in masks[0]:
        pl.semaphore_signal(
            barrier, inc=1, device_id=(partner_of[mask][0],), device_id_type=MESH_ID
        )
    pl.semaphore_wait(barrier, stages)
    sizes = [[rows[part] * 2 ** (stages - 1 - stage) for stage in range(stages)] for part in range(parts)]
    places = [[sum(size[:stage]) for stage in range(stages)] for size in sizes]

    def launch(part, stage):
        partner, bit = partner_of[masks[part][stage]]
        size = sizes[part][stage]
        away = (1 - bit) * size
        copy = pltpu.make_async_remote_copy(
            src_ref=sources[part].at[pl.ds(away, size)]
            if stage == 0
            else landing[part].at[pl.ds(places[part][stage - 1] + away, size)],
            dst_ref=landing[part].at[pl.ds(places[part][stage], size)],
            send_sem=send_sem.at[part, stage],
            recv_sem=recv_sem.at[part, stage],
            device_id=(partner,),
            device_id_type=MESH_ID,
        )
        copy.start()
        return copy

    flying = [launch(part, 0) for part in range(parts)]

    def add_rows(part, stage, start, count):
        keep = partner_of[masks[part][stage]][1] * sizes[part][stage] + start
        last = stage == stages - 1

        def step(index, carry):
            theirs = pl.ds(pl.multiple_of(places[part][stage] + start + index * 16, 16), 16)
            if stage == 0:
                mine = sources[part][pl.ds(pl.multiple_of(keep + index * 16, 16), 16)]
            else:
                mine = landing[part][
                    pl.ds(pl.multiple_of(places[part][stage - 1] + keep + index * 16, 16), 16)
                ]
            total = mine.astype(jnp.float32) + landing[part][theirs].astype(jnp.float32)
            if last:
                results[part][pl.ds(pl.multiple_of(index * 16, 16), 16)] = total
            else:
                landing[part][theirs] = total.astype(jnp.bfloat16)
            return carry

        lax.fori_loop(0, count // 16, step, 0, unroll=min(4, count // 16))

    for stage in range(stages):
        for part in range(parts):
            flying[part].wait()
            if stage == stages - 1:
                add_rows(part, stage, 0, sizes[part][stage])
                continue
            bit = partner_of[masks[part][stage + 1]][1]
            half = sizes[part][stage] // 2
            add_rows(part, stage, (1 - bit) * half, half)
            flying[part] = launch(part, stage + 1)
            add_rows(part, stage, bit * half, half)


def sum_scatter(parts, collective_id):
    devices = lax.axis_size("dp")
    masks = stage_masks(devices)
    rows = [part.shape[1] for part in parts]
    width = parts[0].shape[2]
    bits = devices.bit_length() - 1
    ordered = []
    for part, order in zip(parts, masks):
        view = part.reshape((2,) * bits + part.shape[1:])
        places = [bits - mask.bit_length() for mask in order]
        view = view.transpose(tuple(places) + (bits, bits + 1))
        ordered.append(view.reshape(devices * part.shape[1], width))
    return pl.pallas_call(
        functools.partial(sum_kernel, masks, rows),
        out_shape=[jax.ShapeDtypeStruct((count, width), jnp.float32) for count in rows],
        in_specs=[pl.BlockSpec(memory_space=pltpu.VMEM)] * len(parts),
        out_specs=[pl.BlockSpec(memory_space=pltpu.VMEM)] * len(parts),
        scratch_shapes=[pltpu.VMEM((devices * count, width), jnp.bfloat16) for count in rows]
        + [pltpu.SemaphoreType.DMA((len(parts), bits)), pltpu.SemaphoreType.DMA((len(parts), bits))],
        input_output_aliases={},
        compiler_params=pltpu.CompilerParams(
            collective_id=collective_id, has_side_effects=True, vmem_limit_bytes=56 * 2**20
        ),
    )(*ordered)


def by_owner(grad, width):
    devices = lax.axis_size("dp")
    rows = grad.shape[0] // devices
    blocks = grad.astype(jnp.bfloat16).reshape(devices, rows, grad.shape[1])
    if grad.shape[1] > width:
        cuts = grad.shape[1] // width
        return jnp.concatenate(jnp.split(blocks, cuts, axis=2), axis=1)
    if grad.shape[1] < width:
        return blocks.reshape(devices, rows * grad.shape[1] // width, width)
    return blocks


def from_owner(rows, shape):
    devices = lax.axis_size("dp")
    count, width = shape[0] // devices, shape[1]
    if width > rows.shape[1]:
        return jnp.concatenate(jnp.split(rows, width // rows.shape[1], axis=0), axis=1)
    return rows.reshape(count, width)


def sum_all(groups, collective_id):
    width = groups[0][0].shape[1]
    width = min(grad.shape[1] for group in groups for grad in group if grad.shape[1] >= 768)
    devices = lax.axis_size("dp")
    packed = []
    for group in groups:
        pieces = [by_owner(grad, width) for grad in group]
        count = sum(piece.shape[1] for piece in pieces)
        room = -(-count // 16) * 16 - count
        if room:
            pieces.append(jnp.zeros((devices, room, width), jnp.bfloat16))
        packed.append(jnp.concatenate(pieces, axis=1))
    sums = sum_scatter(packed, collective_id)
    results = []
    for group, total in zip(groups, sums):
        place, outs = 0, []
        for grad in group:
            count = grad.shape[0] // devices * grad.shape[1] // width
            outs.append(from_owner(total[place : place + count], grad.shape))
            place += count
        results.append(outs)
    return results


def body(
    word_states,
    word_segments,
    entity_segments,
    request_rows,
    request_slot,
    mask_slots,
    entity_table,
    vocab_bias,
    entity_dense,
    query_ww,
    query_we,
    query_ew,
    query_ee,
    key_weight,
    value_weight,
    out_weight,
    norm1_gain,
    norm1_bias,
    up_weight,
    down_weight,
    norm2_gain,
    norm2_bias,
    head_weight,
    head_gain,
    head_bias,
    cotangent,
):
    word_count = word_states.shape[0]
    model_width = word_states.shape[1]
    slot_count = entity_segments.shape[1]
    mask_count = mask_slots.shape[1]
    request_count = slot_count + mask_count
    seq_len = word_count + slot_count
    devices = lax.axis_size("dp")
    capacity = request_rows.shape[1]
    head_count = model_width // HD
    query_scale = HD ** (-0.5)
    emb_width = entity_table.shape[1]
    table_rows = entity_table.shape[0]
    total_mask = mask_count * devices
    grad_scale = 1.0 / total_mask
    id_block = jnp.pad(request_rows[:, None, :], ((0, 0), (0, 7), (0, 128 - capacity)))
    asked_ids = direct_swap(id_block, 0)[:, 0, :capacity]
    found_rows = jnp.take(entity_table, asked_ids, axis=0)
    found_bias = jnp.take(vocab_bias, asked_ids, axis=0)
    cap_room = -(-capacity // 16) * 16 - capacity
    found_all = jnp.concatenate(
        [found_rows, jnp.broadcast_to(found_bias[:, :, None], found_bias.shape + (128,))], axis=2
    )
    back_all = direct_swap(jnp.pad(found_all, ((0, 0), (0, cap_room), (0, 0))), 1)
    back_rows = back_all[:, :capacity, :emb_width]
    back_bias = back_all[:, :capacity, emb_width]
    got_rows = back_rows
    got_bias = back_bias
    slot_ids = request_slot.reshape(devices * capacity)
    placing = slot_ids[None, :] == jnp.arange(request_count, dtype=jnp.int32)[:, None]
    placing_low = placing.astype(jnp.bfloat16)
    request_vecs = dot_plain(placing_low, got_rows.reshape(devices * capacity, emb_width))
    request_bias = dot_plain(placing_low, got_bias.reshape(devices * capacity, 1))[:, 0]
    entity_low = request_vecs[:slot_count].astype(jnp.bfloat16)
    target_vecs = request_vecs[slot_count:]
    target_bias = request_bias[slot_count:]
    entity_states = dot_plain(entity_low, entity_dense)
    hidden = jnp.concatenate([word_states.astype(jnp.float32), entity_states], axis=0)
    hidden_low = hidden.astype(jnp.bfloat16)
    word_part = hidden_low[:word_count]
    entity_part = hidden_low[word_count:]
    query_word = (
        query_scale
        * jnp.concatenate(
            [dot_plain(word_part, query_ww), dot_plain(entity_part, query_ew)], axis=0
        )
    ).astype(jnp.bfloat16)
    query_entity = (
        query_scale
        * jnp.concatenate(
            [dot_plain(word_part, query_we), dot_plain(entity_part, query_ee)], axis=0
        )
    ).astype(jnp.bfloat16)
    key_rows = dot_plain(hidden_low, key_weight).astype(jnp.bfloat16)
    values = dot_plain(hidden_low, value_weight).astype(jnp.bfloat16)
    head_shape = (seq_len, head_count, HD)
    query_word_h = query_word.reshape(head_shape)
    query_entity_h = query_entity.reshape(head_shape)
    key_rows_h = key_rows.reshape(head_shape)
    values_h = values.reshape(head_shape)
    segment_row = jnp.concatenate([word_segments[0], entity_segments[0]])
    allowed = segment_row[:, None] == segment_row[None, :]
    scores = attn_scores(query_word_h, query_entity_h, key_rows_h, allowed, word_count)
    row_top = jnp.max(scores, axis=2, keepdims=True)
    exp_scores = jnp.exp(scores - row_top)
    row_total = jnp.sum(exp_scores, axis=2, keepdims=True)
    attn_low = (exp_scores / row_total).astype(jnp.bfloat16)
    row_lse = row_top + jnp.log(row_total)
    context = jnp.einsum("hqk,khd->qhd", attn_low, values_h, preferred_element_type=jnp.float32)
    context_low = context.reshape(seq_len, model_width).astype(jnp.bfloat16)
    attended = dot_plain(context_low, out_weight)
    residual_one = hidden + attended
    normed = layer_norm(residual_one, norm1_gain, norm1_bias)
    normed_low = normed.astype(jnp.bfloat16)
    up_value = dot_plain(normed_low, up_weight)
    activated = gelu_exact(up_value).astype(jnp.bfloat16)
    down_value = dot_plain(activated, down_weight)
    residual_two = normed + down_value
    layer_out = layer_norm(residual_two, norm2_gain, norm2_bias)
    choose = (mask_slots[0][:, None] == jnp.arange(slot_count, dtype=jnp.int32)[None, :]).astype(
        jnp.float32
    )
    picked_low = dot_exact(choose, layer_out[word_count:]).astype(jnp.bfloat16)
    head_pre = dot_plain(picked_low, head_weight)
    head_low = head_act(head_pre, head_gain, head_bias).astype(jnp.bfloat16)
    head_f32 = head_low.astype(jnp.float32)
    target_logit = jnp.sum(head_f32 * target_vecs, axis=1) + target_bias
    all_heads = direct_swap(head_low, 2, gather=True).reshape(total_mask, emb_width)
    block_rows = min(512, total_mask)
    block_count = total_mask // block_rows
    bias_f32 = vocab_bias.astype(jnp.float32)

    def block_logits(block_index):
        row_block = lax.dynamic_slice_in_dim(all_heads, block_index * block_rows, block_rows, 0)
        return (row_block, dot_right_t(row_block, entity_table) + bias_f32[None, :])

    def block_stats(block_index):
        row_block, logits = block_logits(block_index)
        top_value = jnp.max(logits, axis=1)
        return (top_value, jnp.sum(jnp.exp(logits - top_value[:, None]), axis=1))

    local_top, local_total = lax.map(block_stats, jnp.arange(block_count, dtype=jnp.int32))
    local_top = local_top.reshape(total_mask)
    local_total = local_total.reshape(total_mask)
    target_sum = jnp.sum(target_logit)
    stats = jnp.concatenate(
        [
            local_top.reshape(total_mask // 128, 128),
            local_total.reshape(total_mask // 128, 128),
            jnp.full((8, 128), target_sum),
        ],
        axis=0,
    )
    all_stats = direct_swap(stats, 3, gather=True)
    all_tops = all_stats[:, : total_mask // 128].reshape(devices, total_mask)
    all_totals = all_stats[:, total_mask // 128 : total_mask // 64].reshape(devices, total_mask)
    target_total = jnp.sum(all_stats[:, total_mask // 64, 0])
    global_top = jnp.max(all_tops, axis=0)
    global_total = jnp.sum(all_totals * jnp.exp(all_tops - global_top[None, :]), axis=0)
    lse_all = global_top + jnp.log(global_total)
    loss_value = (jnp.sum(lse_all) - target_total) * grad_scale
    own_lse = lax.dynamic_slice_in_dim(lse_all, lax.axis_index("dp") * mask_count, mask_count, 0)
    mask_loss = own_lse - target_logit

    def block_back(running, block_index):
        table_grad, bias_grad = running
        row_block, logits = block_logits(block_index)
        lse_block = lax.dynamic_slice_in_dim(lse_all, block_index * block_rows, block_rows, 0)
        logit_grad = (jnp.exp(logits - lse_block[:, None]) * grad_scale).astype(jnp.bfloat16)
        table_grad = table_grad + dot_left_t(logit_grad, row_block)
        bias_grad = bias_grad + jnp.sum(logit_grad.astype(jnp.float32), axis=0)
        return ((table_grad, bias_grad), dot_plain(logit_grad, entity_table))

    start_grads = (
        jnp.zeros((table_rows, emb_width), jnp.float32),
        jnp.zeros((table_rows,), jnp.float32),
    )
    (table_grad, bias_grad), head_terms = lax.scan(
        block_back, start_grads, jnp.arange(block_count, dtype=jnp.int32)
    )
    head_parts = direct_swap(head_terms.reshape(devices, mask_count, emb_width), 4)
    head_grad = jnp.sum(head_parts, axis=0)
    head_grad = head_grad - grad_scale * target_vecs
    target_grad = -grad_scale * head_f32
    pre_grad, head_gain_grad, head_bias_grad = jax.vjp(head_act, head_pre, head_gain, head_bias)[1](
        head_grad
    )
    pre_low = pre_grad.astype(jnp.bfloat16)
    head_weight_grad = dot_left_t(picked_low, pre_low)
    picked_grad = dot_right_t(pre_low, head_weight)
    out_grad = cotangent.astype(jnp.float32) + jnp.concatenate(
        [jnp.zeros((word_count, model_width), jnp.float32), dot_exact(choose.T, picked_grad)],
        axis=0,
    )
    resid_grad, norm2_gain_grad, norm2_bias_grad = norm_back(
        residual_two, norm2_gain, norm2_bias, out_grad
    )
    down_in = resid_grad.astype(jnp.bfloat16)
    down_grad = dot_left_t(activated, down_in)
    act_grad = dot_right_t(down_in, down_weight)
    up_grad = jax.vjp(gelu_exact, up_value)[1](act_grad)[0]
    up_low = up_grad.astype(jnp.bfloat16)
    up_weight_grad = dot_left_t(normed_low, up_low)
    normed_grad = resid_grad + dot_right_t(up_low, up_weight)
    first_grad, norm1_gain_grad, norm1_bias_grad = norm_back(
        residual_one, norm1_gain, norm1_bias, normed_grad
    )
    attn_in = first_grad.astype(jnp.bfloat16)
    out_weight_grad = dot_left_t(context_low, attn_in)
    context_grad = dot_right_t(attn_in, out_weight).astype(jnp.bfloat16).reshape(head_shape)
    scores_again = attn_scores(query_word_h, query_entity_h, key_rows_h, allowed, word_count)
    attn_prob = jnp.exp(scores_again - row_lse)
    prob_low = attn_prob.astype(jnp.bfloat16)
    prob_grad = jnp.einsum(
        "qhd,khd->hqk", context_grad, values_h, preferred_element_type=jnp.float32
    )
    values_grad = jnp.einsum(
        "hqk,qhd->khd", prob_low, context_grad, preferred_element_type=jnp.float32
    )
    values_grad = values_grad.reshape(seq_len, model_width).astype(jnp.bfloat16)
    row_delta = jnp.sum(attn_prob * prob_grad, axis=2, keepdims=True)
    score_grad = (attn_prob * (prob_grad - row_delta)).astype(jnp.bfloat16)
    qword_grad = jnp.einsum(
        "hqk,khd->qhd",
        score_grad[:, :, :word_count],
        key_rows_h[:word_count],
        preferred_element_type=jnp.float32,
    )
    qword_grad = qword_grad.reshape(seq_len, model_width).astype(jnp.bfloat16)
    qent_grad = jnp.einsum(
        "hqk,khd->qhd",
        score_grad[:, :, word_count:],
        key_rows_h[word_count:],
        preferred_element_type=jnp.float32,
    )
    qent_grad = qent_grad.reshape(seq_len, model_width).astype(jnp.bfloat16)
    keys_grad = jnp.concatenate(
        [
            jnp.einsum(
                "hqk,qhd->khd",
                score_grad[:, :, :word_count],
                query_word_h,
                preferred_element_type=jnp.float32,
            ),
            jnp.einsum(
                "hqk,qhd->khd",
                score_grad[:, :, word_count:],
                query_entity_h,
                preferred_element_type=jnp.float32,
            ),
        ],
        axis=0,
    )
    keys_grad = keys_grad.reshape(seq_len, model_width).astype(jnp.bfloat16)
    query_ww_grad = query_scale * dot_left_t(word_part, qword_grad[:word_count])
    query_ew_grad = query_scale * dot_left_t(entity_part, qword_grad[word_count:])
    query_we_grad = query_scale * dot_left_t(word_part, qent_grad[:word_count])
    query_ee_grad = query_scale * dot_left_t(entity_part, qent_grad[word_count:])
    key_weight_grad = dot_left_t(hidden_low, keys_grad)
    value_weight_grad = dot_left_t(hidden_low, values_grad)
    word_back = query_scale * (
        dot_right_t(qword_grad[:word_count], query_ww)
        + dot_right_t(qent_grad[:word_count], query_we)
    )
    entity_back = query_scale * (
        dot_right_t(qword_grad[word_count:], query_ew)
        + dot_right_t(qent_grad[word_count:], query_ee)
    )
    hidden_grad = (
        first_grad
        + jnp.concatenate([word_back, entity_back], axis=0)
        + dot_right_t(keys_grad, key_weight)
        + dot_right_t(values_grad, value_weight)
    )
    words_grad = hidden_grad[:word_count].astype(jnp.bfloat16)
    state_low = hidden_grad[word_count:].astype(jnp.bfloat16)
    dense_grad = dot_left_t(entity_low, state_low)
    entity_vec_grad = dot_right_t(state_low, entity_dense)
    vec_grad = jnp.concatenate([entity_vec_grad, target_grad], axis=0)
    bias_vec_grad = jnp.concatenate(
        [jnp.zeros((slot_count,), jnp.float32), jnp.full((mask_count,), -grad_scale, jnp.float32)]
    )
    placing_f32 = placing.astype(jnp.float32)
    per_request = dot_exact(placing_f32.T, vec_grad)
    bias_request = dot_exact(placing_f32.T, bias_vec_grad[:, None])[:, 0]
    back_block = jnp.concatenate(
        [
            per_request.reshape(devices, capacity, emb_width).astype(jnp.bfloat16),
            jnp.broadcast_to(
                bias_request.reshape(devices, capacity, 1).astype(jnp.bfloat16),
                (devices, capacity, 128),
            ),
        ],
        axis=2,
    )
    back_block = direct_swap(jnp.pad(back_block, ((0, 0), (0, cap_room), (0, 0))), 5)
    back_rows = back_block[:, :capacity, :emb_width].astype(jnp.float32)
    back_bias = back_block[:, :capacity, emb_width].astype(jnp.float32)
    flat_ids = asked_ids.reshape(devices * capacity)
    table_grad = table_grad + jax.ops.segment_sum(
        back_rows.reshape(devices * capacity, emb_width), flat_ids, num_segments=table_rows
    )
    bias_grad = bias_grad + jax.ops.segment_sum(
        back_bias.reshape(devices * capacity), flat_ids, num_segments=table_rows
    )
    vectors = [
        head_gain_grad,
        head_bias_grad,
        norm2_gain_grad,
        norm2_bias_grad,
        norm1_gain_grad,
        norm1_bias_grad,
    ]
    cuts = [vector.reshape(devices, -1) for vector in vectors]
    spots = [0]
    for cut in cuts:
        spots.append(spots[-1] + cut.shape[1])
    block = jnp.concatenate(cuts, axis=1)
    block = jnp.pad(block, ((0, 0), (0, 128 - spots[-1])))[:, None, :]
    vector_sums = jnp.sum(direct_swap(jnp.pad(block, ((0, 0), (0, 7), (0, 0))), 6)[:, 0], axis=0)
    vector_out = [vector_sums[spots[i] : spots[i + 1]] for i in range(len(cuts))]
    sums = sum_all(
        [
            [up_weight_grad, out_weight_grad, head_weight_grad],
            [down_grad, query_ww_grad, dense_grad],
            [query_we_grad, query_ew_grad, query_ee_grad, key_weight_grad, value_weight_grad],
        ],
        7,
    )
    all_sums = (
        sums[0][2],
        vector_out[0],
        vector_out[1],
        vector_out[2],
        vector_out[3],
        sums[0][0],
        sums[1][0],
        vector_out[4],
        vector_out[5],
        sums[0][1],
        sums[1][1],
        sums[2][0],
        sums[2][1],
        sums[2][2],
        sums[2][3],
        sums[2][4],
        sums[1][2],
    )
    return (
        loss_value,
        layer_out.astype(jnp.bfloat16),
        words_grad,
        table_grad,
        bias_grad,
        all_sums[16],
        all_sums[10],
        all_sums[11],
        all_sums[12],
        all_sums[13],
        all_sums[14],
        all_sums[15],
        all_sums[9],
        all_sums[7],
        all_sums[8],
        all_sums[5],
        all_sums[6],
        all_sums[3],
        all_sums[4],
        all_sums[0],
        all_sums[1],
        all_sums[2],
        mask_loss,
    )


def all_pairs(source, target, sems, me, devices):
    def piece(step):
        peer = lax.rem(me + step, devices)
        return pltpu.make_async_remote_copy(
            src_ref=source.at[peer],
            dst_ref=target.at[me],
            send_sem=sems.at[0, step],
            recv_sem=sems.at[1, step],
            device_id=(peer,),
            device_id_type=MESH_ID,
        )

    def begin(step, carry):
        piece(step).start()
        return carry

    def finish(step, carry):
        piece(step).wait()
        return carry

    lax.fori_loop(1, devices, begin, 0)
    target[me] = source[me]
    return lambda: lax.fori_loop(1, devices, finish, 0)


def lookup_kernel(
    codes, table, bias_col, slot_row, entity_out, vec_out, bias_out, code_out,
    codes_in, found, rows_in, sems,
):
    devices, room, _ = codes.shape
    me = lax.axis_index("dp")
    rows, wide = table.shape
    entries = devices * room
    greet_all(me, devices)
    all_pairs(codes, codes_in, sems.at[0], me, devices)()
    code = codes_in[...].reshape(entries, 128)
    for begin in range(0, entries, 128):
        turned = code[begin : begin + 128].astype(jnp.float32).T
        code_out[:, begin : begin + 128] = turned[0:8].astype(jnp.int32)
    code = jnp.where(code >= rows, code - rows, code)
    lane = lax.broadcasted_iota(jnp.int32, (entries, 128), 1)
    total = jnp.zeros((entries, wide), jnp.float32)
    shift = jnp.zeros((entries, 128), jnp.float32)
    step = 512
    for begin in range(0, rows, step):
        size = min(step, rows - begin)
        match = jnp.concatenate(
            [
                (code - (begin + inner) == lane).astype(jnp.float32)
                for inner in range(0, size, 128)
            ],
            axis=1,
        ).astype(jnp.bfloat16)
        total += dot_plain(match, table[begin : begin + size])
        shift += dot_plain(match, bias_col[begin : begin + size])
    both = jnp.concatenate([total, shift], axis=1).astype(jnp.bfloat16)
    found[...] = both.reshape(found.shape)
    all_pairs(found, rows_in, sems.at[1], me, devices)()
    slots, masked = entity_out.shape[0], vec_out.shape[0]
    wanted = lax.broadcasted_iota(jnp.int32, (slots + masked, entries), 0)
    placing = (wanted == slot_row[0:1]).astype(jnp.float32).astype(jnp.bfloat16)
    placed = dot_plain(placing, rows_in[...].reshape(entries, wide + 128))
    entity_out[...] = placed[:slots, :wide].astype(jnp.bfloat16)
    vec_out[...] = placed[slots:, :wide]
    bias_out[...] = placed[slots:, wide:]


def lookup(codes, table, bias_col, slot_row, slots, masked, collective_id):
    devices, room, _ = codes.shape
    wide = table.shape[1]
    entries = devices * room
    vmem = pl.BlockSpec(memory_space=pltpu.VMEM)
    return pl.pallas_call(
        lookup_kernel,
        out_shape=[
            jax.ShapeDtypeStruct((slots, wide), jnp.bfloat16),
            jax.ShapeDtypeStruct((masked, wide), jnp.float32),
            jax.ShapeDtypeStruct((masked, 128), jnp.float32),
            jax.ShapeDtypeStruct((8, entries), jnp.int32),
        ],
        in_specs=[vmem] * 4,
        out_specs=[vmem] * 4,
        scratch_shapes=[
            pltpu.VMEM(codes.shape, jnp.int32),
            pltpu.VMEM((devices, room, wide + 128), jnp.bfloat16),
            pltpu.VMEM((devices, room, wide + 128), jnp.bfloat16),
            pltpu.SemaphoreType.DMA((2, 2, devices)),
        ],
        compiler_params=pltpu.CompilerParams(
            collective_id=collective_id, has_side_effects=True, vmem_limit_bytes=40 * 2**20
        ),
    )(codes, table, bias_col, slot_row)


def norm_parts(value):
    center = value - jnp.mean(value, axis=-1, keepdims=True)
    spread = jnp.mean(center * center, axis=-1, keepdims=True)
    rate = lax.rsqrt(spread + EPSILON)
    return center * rate, rate


def gelu_parts(value):
    chance = 0.5 + 0.5 * lax.erf(value * (0.5**0.5))
    slope = chance + value * (jnp.exp(-0.5 * value * value) * (0.5 / jnp.pi) ** 0.5)
    return value * chance, slope


def half_lanes(block):
    lane = lax.broadcasted_iota(jnp.int32, (1, block), 1)
    low_half = (lane < HD).astype(jnp.float32).astype(jnp.bfloat16)
    high_half = (lane >= HD).astype(jnp.float32).astype(jnp.bfloat16)
    return low_half, high_half


def forward_kernel(
    word_states,
    entity_low,
    feat_q,
    feat_k,
    choose,
    dense,
    w_ww,
    w_we,
    w_ew,
    w_ee,
    w_key,
    w_value,
    out_hbm,
    gain_one,
    shift_one,
    up_hbm,
    down_hbm,
    gain_two,
    shift_two,
    head_w,
    gain_head,
    shift_head,
    hidden,
    qword,
    qent,
    keys,
    values,
    context,
    lse_out,
    resid_one,
    normed_out,
    active_hbm,
    slope_hbm,
    resid_two,
    layer_low,
    picked_out,
    head_pre_out,
    head_out,
    state_scr,
    normed_scr,
    out_w,
    up_w,
    down_w,
    active,
    slope,
    sems,
):
    loads = [
        pltpu.make_async_copy(source, target, sems.at[index])
        for index, (source, target) in enumerate(
            ((out_hbm, out_w), (up_hbm, up_w), (down_hbm, down_w))
        )
    ]
    for load in loads:
        load.start()
    words, width = word_states.shape
    seq_len = hidden.shape[0]
    slots = seq_len - words
    block = 128
    halves = half_lanes(block)
    query_scale = HD ** (-0.5)
    state_scr[...] = dot_plain(entity_low[...], dense[...])
    hidden[:words] = word_states[...]
    hidden[words:] = state_scr[...].astype(jnp.bfloat16)

    half = width // 2
    for cut in range(0, width, half):
        at = slice(cut, cut + half)
        for target, word_w, ent_w in ((qword, w_ww, w_ew), (qent, w_we, w_ee)):
            target[:words, at] = (query_scale * dot_plain(word_states[...], word_w[:, at])).astype(
                jnp.bfloat16
            )
            target[words:, at] = (query_scale * dot_plain(hidden[words:], ent_w[:, at])).astype(
                jnp.bfloat16
            )
        keys[:, at] = dot_plain(hidden[...], w_key[:, at]).astype(jnp.bfloat16)
        values[:, at] = dot_plain(hidden[...], w_value[:, at]).astype(jnp.bfloat16)
    lse_out[...] = jnp.zeros_like(lse_out)

    def pair_step(pair, carry):
        lanes = pl.ds(pl.multiple_of(pair * block, block), block)
        key_pair = keys[:, lanes]
        value_pair = values[:, lanes]
        key_feat = [key_pair * halves[h] + feat_k[...] * halves[1 - h] for h in range(2)]
        value_only = [value_pair * halves[h] for h in range(2)]
        spot = lax.broadcasted_iota(jnp.int32, (1, block), 1) - 4 * pair

        def row_step(index, inner):
            at = pl.ds(pl.multiple_of(index * block, block), block)
            qw = qword[at, lanes]
            qe = qent[at, lanes]
            feats = feat_q[at]
            result = jnp.zeros((block, block), jnp.float32)
            stats = lse_out[at]
            for h in range(2):
                left_w = qw * halves[h] + feats * halves[1 - h]
                left_e = qe * halves[h] + feats * halves[1 - h]
                scores = jnp.concatenate(
                    [
                        dot_right_t(left_w, key_feat[h][:words]),
                        dot_right_t(left_e, key_feat[h][words:]),
                    ],
                    axis=1,
                )
                top = jnp.max(scores, axis=1, keepdims=True)
                expo = jnp.exp(scores - top)
                total = jnp.sum(expo, axis=1, keepdims=True)
                prob = (expo * (1.0 / total)).astype(jnp.bfloat16)
                result += dot_plain(prob, value_only[h])
                stats = jnp.where(spot == h, top + jnp.log(total), stats)
            context[at, lanes] = result.astype(jnp.bfloat16)
            lse_out[at] = stats
            return inner

        lax.fori_loop(0, seq_len // block, row_step, 0)
        return carry

    lax.fori_loop(0, width // block, pair_step, 0)

    loads[0].wait()
    for begin, size in ((0, words // 2), (words // 2, words // 2), (words, slots)):
        at = slice(begin, begin + size)
        start = (
            state_scr[...] if begin == words else word_states[at].astype(jnp.float32)
        )
        value = start + dot_plain(context[at], out_w[...])
        resid_one[at] = value
        normed = norm_parts(value)[0] * gain_one[...] + shift_one[...]
        normed_scr[at] = normed
        normed_out[at] = normed.astype(jnp.bfloat16)
    loads[1].wait()
    loads[2].wait()
    span = seq_len // 4
    stores = []

    for slot in range(down_w.shape[0] // width):
        cols = slice(slot * width, slot * width + width)

        def up_step(index, carry, cols=cols):
            at = pl.ds(pl.multiple_of(index * span, 16), span)
            result, change = gelu_parts(dot_plain(normed_out[at], up_w[:, cols]))
            active[at, cols] = result.astype(jnp.bfloat16)
            slope[at, cols] = change.astype(jnp.bfloat16)
            return carry

        lax.fori_loop(0, 4, up_step, 0)
        for index, (source, target) in enumerate(((active, active_hbm), (slope, slope_hbm))):
            stores.append(
                pltpu.make_async_copy(
                    source.at[:, cols], target.at[:, cols], sems.at[3 + 2 * slot + index]
                )
            )
            stores[-1].start()

    def down_step(index, carry):
        at = pl.ds(pl.multiple_of(index * span, 16), span)
        value = normed_scr[at] + dot_plain(active[at], down_w[...])
        resid_two[at] = value
        layer_low[at] = (norm_parts(value)[0] * gain_two[...] + shift_two[...]).astype(jnp.bfloat16)
        return carry

    lax.fori_loop(0, 4, down_step, 0)
    picked = dot_plain(choose[...], layer_low[words:]).astype(jnp.bfloat16)
    picked_out[...] = picked
    head_pre = dot_plain(picked, head_w[...])
    head_pre_out[...] = head_pre
    raised = gelu_parts(head_pre)[0]
    head_out[...] = (norm_parts(raised)[0] * gain_head[...] + shift_head[...]).astype(jnp.bfloat16)
    for store in stores:
        store.wait()


def forward_pass(inputs):
    words, width = inputs[0].shape
    slots = inputs[1].shape[0]
    seq_len = words + slots
    hidden_units = inputs[15].shape[1]
    mask_count = inputs[4].shape[0]
    head_width = inputs[19].shape[1]
    low, full = jnp.bfloat16, jnp.float32
    vmem, hbm = pl.BlockSpec(memory_space=pltpu.VMEM), pl.BlockSpec(memory_space=pltpu.HBM)
    far = (12, 15, 16)
    shapes = [
        ((seq_len, width), low),
        ((seq_len, width), low),
        ((seq_len, width), low),
        ((seq_len, width), low),
        ((seq_len, width), low),
        ((seq_len, width), low),
        ((seq_len, 128), full),
        ((seq_len, width), full),
        ((seq_len, width), low),
        ((seq_len, hidden_units), low),
        ((seq_len, hidden_units), low),
        ((seq_len, width), full),
        ((seq_len, width), low),
        ((mask_count, width), low),
        ((mask_count, head_width), full),
        ((mask_count, head_width), low),
    ]
    return pl.pallas_call(
        forward_kernel,
        out_shape=[jax.ShapeDtypeStruct(*shape) for shape in shapes],
        in_specs=[hbm if index in far else vmem for index in range(len(inputs))],
        out_specs=[hbm if index in (9, 10) else vmem for index in range(len(shapes))],
        scratch_shapes=[
            pltpu.VMEM((slots, width), full),
            pltpu.VMEM((seq_len, width), full),
            pltpu.VMEM(inputs[12].shape, low),
            pltpu.VMEM(inputs[15].shape, low),
            pltpu.VMEM(inputs[16].shape, low),
            pltpu.VMEM((seq_len, hidden_units), low),
            pltpu.VMEM((seq_len, hidden_units), low),
            pltpu.SemaphoreType.DMA((16,)),
        ],
        compiler_params=pltpu.CompilerParams(vmem_limit_bytes=60 * 2**20),
    )(*inputs)


class Grid:
    def __init__(self):
        me = lax.axis_index("dp")
        self.core = lax.rem(me, 2)
        self.square = lax.rem(lax.div(me, 2), 4)
        self.line = lax.div(me, 8)
        self.twin = me + 1 - 2 * self.core
        self.squares = []
        self.lines = []
        for step in range(1, 4):
            other = lax.rem(self.square + step, 4)
            self.squares.append((me + 2 * (other - self.square), other))
            other = lax.rem(self.line + step, 4)
            self.lines.append((me + 8 * (other - self.line), other))

    def greet(self):
        barrier = pltpu.get_barrier_semaphore()
        peers = [self.twin] + [peer for peer, _ in self.squares + self.lines]
        for peer in peers:
            pl.semaphore_signal(barrier, inc=1, device_id=(peer,), device_id_type=MESH_ID)
        pl.semaphore_wait(barrier, len(peers))


class Sender:
    def __init__(self, send_sem, recv_sem):
        self.send_sem, self.recv_sem, self.used = send_sem, recv_sem, 0

    def start(self, source, target, peer):
        slot = self.used
        self.used += 1
        copy = pltpu.make_async_remote_copy(
            src_ref=source,
            dst_ref=target,
            send_sem=self.send_sem.at[slot],
            recv_sem=self.recv_sem.at[slot],
            device_id=(peer,),
            device_id_type=MESH_ID,
        )
        copy.start()
        return copy


def wait_all(copies):
    for copy in copies:
        copy.wait()


def merge_stats(blocks):
    tops = [block[0] for block in blocks]
    top = functools.reduce(jnp.maximum, tops)
    total = sum(block[1] * jnp.exp(block[0] - top) for block in blocks)
    return top, total, sum(block[2] for block in blocks)


def head_kernel(
    grad_scale,
    head,
    table,
    bias,
    target_vecs,
    target_bias,
    table_grad,
    bias_grad,
    losses,
    total_loss,
    head_grad,
    heads,
    logits,
    expo,
    table_t,
    bias_col,
    part,
    land_pair,
    sum_pair,
    land_square,
    sum_square,
    land_line,
    stat,
    stat_pair,
    stat_square,
    stat_line,
    send_sem,
    recv_sem,
):
    grid = Grid()
    rows, wide = table.shape
    count = head.shape[0]
    total_mask = 32 * count
    grid.greet()
    sender = Sender(send_sem, recv_sem)
    line, square, core = grid.line, grid.square, grid.core
    flying = [sender.start(head, heads.at[line, square, core], peer) for peer, _ in grid.lines]
    heads[line, square, core] = head[...]

    def table_step(index, carry):
        at = pl.ds(pl.multiple_of(index * 128, 128), 128)
        table_t[:, at] = table[at].astype(jnp.float32).T.astype(jnp.bfloat16)
        return carry

    lax.fori_loop(0, rows // 128, table_step, 0)
    wait_all(flying)
    flying = [
        sender.start(heads.at[:, square, core], heads.at[:, square, core], peer)
        for peer, _ in grid.squares
    ]

    def bias_step(index, carry):
        at = pl.ds(pl.multiple_of(index * 128, 128), 128)
        bias_col[at] = jnp.broadcast_to(bias[:, at], (128, 128)).T
        return carry

    lax.fori_loop(0, rows // 128, bias_step, 0)
    wait_all(flying)
    sender.start(heads.at[:, :, core], heads.at[:, :, core], grid.twin).wait()

    all_heads = heads[...].reshape(total_mask, wide)
    slab = rows // 8

    def logit_step(index, carry):
        at = pl.ds(pl.multiple_of(index * slab, 16), slab)
        logits[at] = dot_right_t(table[at], all_heads)
        return carry

    lax.fori_loop(0, 8, logit_step, 0)
    tile = 64
    wide_copies = total_mask // 128

    def value_at(index):
        at = pl.ds(pl.multiple_of(index * tile, tile), tile)
        shift = bias_col[at]
        return at, logits[at] + jnp.concatenate([shift] * wide_copies, axis=1)

    def top_step(index, top):
        at, value = value_at(index)
        return jnp.maximum(top, jnp.max(value.reshape(tile // 8, 8, total_mask), axis=0))

    top = lax.fori_loop(
        0, rows // tile, top_step, jnp.full((8, total_mask), -jnp.inf, jnp.float32)
    )
    top = jnp.max(top, axis=0, keepdims=True)

    def exp_step(index, total):
        at, value = value_at(index)
        value = jnp.exp(value - top)
        expo[at] = value.astype(jnp.bfloat16)
        return total + jnp.sum(value.reshape(tile // 8, 8, total_mask), axis=0)

    total = lax.fori_loop(0, rows // tile, exp_step, jnp.zeros((8, total_mask), jnp.float32))
    total = jnp.sum(total, axis=0, keepdims=True)

    def fold(row):
        return jnp.concatenate([row[:, i * 128 : i * 128 + 128] for i in range(wide_copies)], axis=0)

    def unfold(block):
        return jnp.concatenate([block[i : i + 1] for i in range(wide_copies)], axis=1)

    own_top, own_total = fold(top), fold(total)
    target = (
        jnp.sum(head[...].astype(jnp.float32) * target_vecs[...], axis=1, keepdims=True)
        + target_bias[:, 0:1]
    )
    own_target = jnp.broadcast_to(jnp.sum(target, axis=0, keepdims=True), own_top.shape)
    stat[0, 0], stat[0, 1], stat[0, 2] = own_top, own_total, own_target
    copy = sender.start(stat.at[0], stat_pair, grid.twin)
    quarter = total_mask // 4
    parts = [dot_plain(table_t[...], expo[:, :quarter])]
    copy.wait()
    stat[1, 0], stat[1, 1], stat[1, 2] = merge_stats(
        [(own_top, own_total, own_target), (stat_pair[0], stat_pair[1], stat_pair[2])]
    )
    stat_square[square] = stat[1]
    flying = [sender.start(stat.at[1], stat_square.at[square], peer) for peer, _ in grid.squares]
    parts.append(dot_plain(table_t[...], expo[:, quarter : 2 * quarter]))
    wait_all(flying)
    stat[2, 0], stat[2, 1], stat[2, 2] = merge_stats(
        [(stat_square[i, 0], stat_square[i, 1], stat_square[i, 2]) for i in range(4)]
    )
    stat_line[line] = stat[2]
    flying = [sender.start(stat.at[2], stat_line.at[line], peer) for peer, _ in grid.lines]
    parts.append(dot_plain(table_t[...], expo[:, 2 * quarter : 3 * quarter]))
    parts.append(dot_plain(table_t[...], expo[:, 3 * quarter :]))
    wait_all(flying)
    full_top, full_total, full_target = merge_stats(
        [(stat_line[i, 0], stat_line[i, 1], stat_line[i, 2]) for i in range(4)]
    )
    lse = full_top + jnp.log(full_total)
    all_lse = jnp.sum(jnp.sum(lse, axis=1, keepdims=True), axis=0, keepdims=True)
    total_loss[...] = (all_lse - full_target[0:1]) * grad_scale
    mine = lax.broadcasted_iota(jnp.int32, (count, total_mask), 0) + lax.axis_index("dp") * count
    hit = mine == lax.broadcasted_iota(jnp.int32, (count, total_mask), 1)
    own_lse = jnp.sum(jnp.where(hit, unfold(lse), 0.0), axis=1, keepdims=True)
    losses[...] = jnp.broadcast_to(own_lse - target, losses.shape)
    scale = unfold(jnp.exp(own_top - lse) * grad_scale)
    per = 128 // count
    for index in range(total_mask // 128):
        at = slice(index * 128, index * 128 + 128)
        source = parts[index * 128 // quarter]
        begin = index * 128 % quarter
        piece = (source[:, begin : begin + 128] * scale[:, at]).T.astype(jnp.bfloat16)
        for inner in range(per):
            owner = index * per + inner
            part[owner // 8, owner // 2 % 4, owner % 2] = piece[inner * count : inner * count + count]
    copy = sender.start(part.at[:, :, 1 - core], land_pair, grid.twin)

    scaled = []
    for index in range(total_mask // 128):
        at = slice(index * 128, index * 128 + 128)
        column = jnp.broadcast_to(scale[:, at], (128, 128)).T
        column = jnp.concatenate([column] * (wide // 128), axis=1)
        scaled.append((all_heads[at].astype(jnp.float32) * column).astype(jnp.bfloat16))
    scaled = jnp.concatenate(scaled, axis=0)
    slab = rows // 4

    def grad_part(index):
        at = slice(index * slab, index * slab + slab)
        table_grad[at] = dot_plain(expo[at], scaled)

    grad_part(0)
    copy.wait()
    sum_pair[...] = (part[:, :, core].astype(jnp.float32) + land_pair[...].astype(jnp.float32)).astype(
        jnp.bfloat16
    )
    flying = [
        sender.start(sum_pair.at[:, other], land_square.at[square], peer)
        for peer, other in grid.squares
    ]
    land_square[square] = sum_pair[:, square]
    grad_part(1)
    wait_all(flying)
    sum_square[...] = sum(land_square[i].astype(jnp.float32) for i in range(4)).astype(jnp.bfloat16)
    flying = [
        sender.start(sum_square.at[other], land_line.at[line], peer) for peer, other in grid.lines
    ]
    land_line[line] = sum_square[line]
    grad_part(2)
    high = scale.astype(jnp.bfloat16)
    low = (scale - high.astype(jnp.float32)).astype(jnp.bfloat16)
    both = jnp.concatenate(
        [high.astype(jnp.float32), low.astype(jnp.float32), jnp.zeros((14, total_mask), jnp.float32)],
        axis=0,
    ).astype(jnp.bfloat16)
    sums = dot_right_t(both, expo[...])
    bias_grad[...] = sums[0:1] + sums[1:2]
    grad_part(3)
    wait_all(flying)
    head_grad[...] = sum(land_line[i].astype(jnp.float32) for i in range(4))


def head_and_table(
    head_low, entity_table, bias_row, target_vecs, target_bias, grad_scale, collective_id
):
    count, wide = head_low.shape
    rows = entity_table.shape[0]
    total_mask = 32 * count
    low, full = jnp.bfloat16, jnp.float32
    vmem = pl.BlockSpec(memory_space=pltpu.VMEM)
    folded = (total_mask // 128, 128)
    return pl.pallas_call(
        functools.partial(head_kernel, grad_scale),
        out_shape=[
            jax.ShapeDtypeStruct((rows, wide), full),
            jax.ShapeDtypeStruct((1, rows), full),
            jax.ShapeDtypeStruct((count, 128), full),
            jax.ShapeDtypeStruct((1, 128), full),
            jax.ShapeDtypeStruct((count, wide), full),
        ],
        in_specs=[vmem] * 5,
        out_specs=[vmem] * 5,
        scratch_shapes=[
            pltpu.VMEM((4, 4, 2, count, wide), low),
            pltpu.VMEM((rows, total_mask), full),
            pltpu.VMEM((rows, total_mask), low),
            pltpu.VMEM((wide, rows), low),
            pltpu.VMEM((rows, 128), full),
            pltpu.VMEM((4, 4, 2, count, wide), low),
            pltpu.VMEM((4, 4, count, wide), low),
            pltpu.VMEM((4, 4, count, wide), low),
            pltpu.VMEM((4, 4, count, wide), low),
            pltpu.VMEM((4, count, wide), low),
            pltpu.VMEM((4, count, wide), low),
            pltpu.VMEM((3, 3) + folded, full),
            pltpu.VMEM((3,) + folded, full),
            pltpu.VMEM((4, 3) + folded, full),
            pltpu.VMEM((4, 3) + folded, full),
            pltpu.SemaphoreType.DMA((24,)),
            pltpu.SemaphoreType.DMA((24,)),
        ],
        compiler_params=pltpu.CompilerParams(
            collective_id=collective_id, has_side_effects=True, vmem_limit_bytes=60 * 2**20
        ),
    )(head_low, entity_table, bias_row, target_vecs, target_bias)


def norm_slope(value, given, gain):
    scaled, rate = norm_parts(value)
    back = given * gain
    mean_back = jnp.mean(back, axis=-1, keepdims=True)
    mean_both = jnp.mean(back * scaled, axis=-1, keepdims=True)
    grad = rate * (back - mean_back - scaled * mean_both)
    return (
        grad,
        jnp.sum(given * scaled, axis=0, keepdims=True),
        jnp.sum(given, axis=0, keepdims=True),
    )


def split_low(value):
    high = value.astype(jnp.bfloat16)
    return high, (value - high.astype(jnp.float32)).astype(jnp.bfloat16)


def place_rows(source, order, count, store):
    owners = 2 ** len(order)
    for pair in range(owners // 2):
        one, two = place_owner(order, 2 * pair), place_owner(order, 2 * pair + 1)
        both = jnp.concatenate(
            [source[one * count : one * count + count], source[two * count : two * count + count]],
            axis=0,
        )
        store(slice(pair * 2 * count, (pair + 1) * 2 * count), both.astype(jnp.bfloat16))


def middle_back_kernel(
    orders,
    grad_scale,
    head_grad,
    target_vecs,
    head_pre,
    gain_head,
    picked,
    head_w,
    choose,
    cotangent,
    resid_two,
    gain_two,
    normed_low,
    resid_one,
    gain_one,
    out_w,
    context,
    lse_lanes,
    active_hbm,
    slope_hbm,
    up_hbm,
    down_hbm,
    up_a,
    up_b,
    head_a,
    out_b,
    down_b,
    up_c,
    down_c,
    first_grad,
    context_grad,
    lse_delta,
    head_vectors,
    wide_vectors,
    active,
    slope,
    up_w,
    down_w,
    flip,
    normed_t,
    context_t,
    down_in,
    acc,
    up_low,
    stage_a,
    stage_c,
    sems,
):
    seq_len, width = cotangent.shape
    slots = choose.shape[1]
    words = seq_len - slots
    cuts = down_w.shape[0] // width
    loads = []
    for index, (source, target) in enumerate(
        ((active_hbm, active), (down_hbm, down_w), (slope_hbm, slope), (up_hbm, up_w))
    ):
        for cut in range(cuts):
            at = pl.ds(cut * width, width)
            view = (at,) if index == 1 else (slice(None), at)
            loads.append(
                pltpu.make_async_copy(source.at[view], target.at[view], sems.at[index * cuts + cut])
            )
    for cut in range(cuts):
        for index in range(4):
            loads[index * cuts + cut].start()

    given = head_grad[...] - grad_scale * target_vecs[...]
    pre = head_pre[...]
    raised, change = gelu_parts(pre)
    back, gain_sum, bias_sum = norm_slope(raised, given, gain_head[...])
    head_vectors[0:1] = gain_sum
    head_vectors[1:2] = bias_sum
    head_vectors[2:8] = jnp.zeros((6, head_vectors.shape[1]), jnp.float32)
    pre_low = (back * change).astype(jnp.bfloat16)
    head_weight_grad = dot_left_t(picked[...], pre_low)
    count = width // 2 ** len(orders[0])

    def keep_head(at, value):
        head_a[0, at] = value

    flip[:, : head_a.shape[2]] = head_weight_grad
    place_rows(flip[:, : head_a.shape[2]], orders[0], count, keep_head)
    picked_high, picked_rest = split_low(dot_right_t(pre_low, head_w[...]))
    placed = dot_left_t(choose[...], picked_high) + dot_left_t(choose[...], picked_rest)

    block = 128
    total_gain = jnp.zeros((1, width), jnp.float32)
    total_bias = jnp.zeros((1, width), jnp.float32)
    for begin in range(0, seq_len, block):
        at = slice(begin, begin + block)
        given = cotangent[at].astype(jnp.float32)
        if begin >= words:
            given = given + placed[begin - words : begin - words + block]
        grad, gain_sum, bias_sum = norm_slope(resid_two[at], given, gain_two[...])
        total_gain += gain_sum
        total_bias += bias_sum
        acc[at] = grad
        down_in[at] = grad.astype(jnp.bfloat16)
    wide_vectors[0:1] = total_gain
    wide_vectors[1:2] = total_bias

    def flip_into(source, target, order_list):
        def flip_step(index, carry):
            at = pl.ds(pl.multiple_of(index * block, block), block)
            flip[at] = source[:, at].astype(jnp.float32).T
            return carry

        lax.fori_loop(0, width // block, flip_step, 0)
        for slot, order in enumerate(order_list):

            def keep(at, value, slot=slot):
                target[slot, at] = value

            place_rows(flip, order, count, keep)

    flip_into(normed_low, normed_t, (orders[0], orders[2]))
    flip_into(context, context_t, (orders[1],))

    column = 384
    split = down_b.shape[2]
    owners = 2 ** len(orders[0])
    tall = down_w.shape[0] // owners
    spots = [
        {place_owner(order, place): place for place in range(owners)}
        for order in (orders[1], orders[2])
    ]
    stores = []
    for cut in range(cuts):
        at = slice(cut * width, cut * width + width)
        for index in range(4):
            loads[index * cuts + cut].wait()
        for begin in range(0, width, column):
            piece = dot_left_t(active[:, at], down_in[:, begin : begin + column])
            for inner in range(width // tall):
                owner = cut * (width // tall) + inner
                rows = piece[inner * tall : inner * tall + tall].astype(jnp.bfloat16)
                stop = min(begin + column, split)
                if begin < split:
                    place = spots[0][owner] * tall
                    stage_a[place : place + tall, begin:stop] = rows[:, : stop - begin]
                if begin + column > split:
                    start = max(begin, split)
                    place = spots[1][owner] * tall
                    stage_c[place : place + tall, start - split : begin + column - split] = rows[
                        :, start - begin :
                    ]

        def back_step(index, carry, at=at):
            span = seq_len // 4
            rows = pl.ds(pl.multiple_of(index * span, 16), span)
            grad = dot_right_t(down_in[rows], down_w[at]) * slope[rows, at].astype(jnp.float32)
            grad = grad.astype(jnp.bfloat16)
            up_low[rows] = grad
            acc[rows] = acc[rows] + dot_right_t(grad, up_w[:, at])
            return carry

        lax.fori_loop(0, 4, back_step, 0)
        target, slot, order_slot = ((up_a, 0, 0), (up_a, 1, 0), (up_b, 0, 0), (up_c, 0, 1))[cut]
        for begin in range(0, width, column):
            target[slot, :, begin : begin + column] = dot_plain(
                normed_t[order_slot], up_low[:, begin : begin + column]
            ).astype(jnp.bfloat16)
    stores = [
        pltpu.make_async_copy(stage_a, down_b.at[0], sems.at[4 * cuts]),
        pltpu.make_async_copy(stage_c, down_c.at[0], sems.at[4 * cuts + 1]),
    ]
    for store in stores:
        store.start()

    total_gain = jnp.zeros((1, width), jnp.float32)
    total_bias = jnp.zeros((1, width), jnp.float32)
    row = lax.broadcasted_iota(jnp.int32, (width, 128), 0)
    lane = lax.broadcasted_iota(jnp.int32, (width, 128), 1)
    spot = 4 * lax.div(row, 128) + 2 + lax.div(lax.rem(row, 128), HD)
    pick = (spot == lane).astype(jnp.float32).astype(jnp.bfloat16)
    for begin in range(0, seq_len, block):
        at = slice(begin, begin + block)
        grad, gain_sum, bias_sum = norm_slope(resid_one[at], acc[at], gain_one[...])
        total_gain += gain_sum
        total_bias += bias_sum
        first_grad[at] = grad
        low = grad.astype(jnp.bfloat16)
        down_in[at] = low
        back = dot_right_t(low, out_w[...]).astype(jnp.bfloat16)
        context_grad[at] = back
        high, rest = split_low(back.astype(jnp.float32) * context[at].astype(jnp.float32))
        lse_delta[at] = lse_lanes[at] + dot_plain(high, pick) + dot_plain(rest, pick)
    wide_vectors[2:3] = total_gain
    wide_vectors[3:4] = total_bias
    wide_vectors[4:8] = jnp.zeros((4, width), jnp.float32)
    for begin in range(0, width, column):
        out_b[0, :, begin : begin + column] = dot_plain(
            context_t[0], down_in[:, begin : begin + column]
        ).astype(jnp.bfloat16)
    for store in stores:
        store.wait()


DOWN_SPLIT = 512


def middle_back(inputs, orders, grad_scale):
    seq_len, width = inputs[7].shape
    hidden_units = inputs[16].shape[1]
    head_width = inputs[0].shape[1]
    low, full = jnp.bfloat16, jnp.float32
    cuts = hidden_units // width
    vmem, hbm = pl.BlockSpec(memory_space=pltpu.VMEM), pl.BlockSpec(memory_space=pltpu.HBM)
    shapes = [
        ((2, width, width), low),
        ((1, width, width), low),
        ((1, width, head_width), low),
        ((1, width, width), low),
        ((1, hidden_units, DOWN_SPLIT), low),
        ((1, width, width), low),
        ((1, hidden_units, width - DOWN_SPLIT), low),
        ((seq_len, width), full),
        ((seq_len, width), low),
        ((seq_len, 128), full),
        ((8, head_width), full),
        ((8, width), full),
    ]
    return pl.pallas_call(
        functools.partial(middle_back_kernel, orders, grad_scale),
        out_shape=[jax.ShapeDtypeStruct(*shape) for shape in shapes],
        in_specs=[vmem] * 16 + [hbm] * 4,
        out_specs=[hbm if index in (4, 6) else vmem for index in range(len(shapes))],
        scratch_shapes=[
            pltpu.VMEM((seq_len, hidden_units), low),
            pltpu.VMEM((seq_len, hidden_units), low),
            pltpu.VMEM((width, hidden_units), low),
            pltpu.VMEM((hidden_units, width), low),
            pltpu.VMEM((width, seq_len), full),
            pltpu.VMEM((2, width, seq_len), low),
            pltpu.VMEM((1, width, seq_len), low),
            pltpu.VMEM((seq_len, width), low),
            pltpu.VMEM((seq_len, width), full),
            pltpu.VMEM((seq_len, width), low),
            pltpu.VMEM((hidden_units, DOWN_SPLIT), low),
            pltpu.VMEM((hidden_units, width - DOWN_SPLIT), low),
            pltpu.SemaphoreType.DMA((4 * cuts + 2,)),
        ],
        compiler_params=pltpu.CompilerParams(vmem_limit_bytes=62 * 2**20),
    )(*inputs)


def scatter_kernel(grad_scale, codes, back, table_in, bias_in, table_out, bias_out):
    rows, wide = table_in.shape
    entries = back.shape[0]
    code = codes[0:1]
    target = (code >= rows).astype(jnp.float32)
    flags = jnp.broadcast_to(target, (16, entries)).astype(jnp.bfloat16)
    code = jnp.where(code >= rows, code - rows, code)
    step = 1024
    for begin in range(0, rows, step):
        size = min(step, rows - begin)
        row = lax.broadcasted_iota(jnp.int32, (size, entries), 0) + begin
        match = (row == code).astype(jnp.float32).astype(jnp.bfloat16)
        at = slice(begin, begin + size)
        table_out[at] = table_in[at] + dot_plain(match, back[...])
        counts = dot_right_t(flags, match)
        bias_out[:, at] = bias_in[:, at] - grad_scale * counts[0:1]


def scatter_add(codes, back, table_grad, bias_grad, grad_scale):
    vmem = pl.BlockSpec(memory_space=pltpu.VMEM)
    return pl.pallas_call(
        functools.partial(scatter_kernel, grad_scale),
        out_shape=[
            jax.ShapeDtypeStruct(table_grad.shape, jnp.float32),
            jax.ShapeDtypeStruct(bias_grad.shape, jnp.float32),
        ],
        in_specs=[vmem] * 4,
        out_specs=[vmem] * 2,
        compiler_params=pltpu.CompilerParams(vmem_limit_bytes=40 * 2**20),
    )(codes, back, table_grad, bias_grad)


def place_owner(order, place):
    bits = len(order)
    return sum(((place >> (bits - 1 - spot)) & 1) * mask for spot, mask in enumerate(order))


class Piece:
    def __init__(
        self, rows, stages, send, own, land, tail, pack, tail_land, out, send_sem, recv_sem
    ):
        self.rows, self.stages = rows, stages
        self.send, self.own, self.land = send, own, land
        self.tail, self.pack, self.tail_land, self.out = tail, pack, tail_land, out
        self.send_sem, self.recv_sem = send_sem, recv_sem
        self.sizes = [rows * 2 ** (stages - 1 - stage) for stage in range(stages)]
        self.spots = [sum(self.sizes[:stage]) for stage in range(stages)]

    def copy(self, stage, partner, bit):
        size = self.sizes[stage]
        away = (1 - bit) * size
        if stage < self.stages - 1:
            away = pl.multiple_of(away, 16)
        if stage == 0:
            source, target = self.send.at[:, pl.ds(away, size)], self.land.at[:, pl.ds(0, size)]
        elif stage < self.stages - 1:
            spot = pl.multiple_of(self.spots[stage - 1] + away, 16)
            source = self.land.at[:, pl.ds(spot, size)]
            target = self.land.at[:, pl.ds(self.spots[stage], size)]
        else:
            source, target = self.pack, self.tail_land
        return pltpu.make_async_remote_copy(
            src_ref=source,
            dst_ref=target,
            send_sem=self.send_sem.at[stage],
            recv_sem=self.recv_sem.at[stage],
            device_id=(partner,),
            device_id_type=MESH_ID,
        )

    def held(self, stage, bit):
        size = self.sizes[stage]
        if stage == 0 and self.own is not None:
            return self.own, 0
        if stage == 0:
            return self.send, pl.multiple_of(bit * size, 16)
        return self.land, pl.multiple_of(self.spots[stage - 1] + bit * size, 16)

    def add(self, stage, bit, half_index):
        size = self.sizes[stage]
        half = size // 2
        unit = 48 if half % 48 == 0 else 16
        start = half_index * half
        source, base = self.held(stage, bit)
        for slot in range(self.land.shape[0]):

            def step(index, carry, slot=slot):
                row = pl.multiple_of(start + index * unit, 16)
                mine = source[slot, pl.ds(pl.multiple_of(base + row, 16), unit)]
                spot = pl.ds(pl.multiple_of(self.spots[stage] + row, 16), unit)
                theirs = self.land[slot, spot]
                total = mine.astype(jnp.float32) + theirs.astype(jnp.float32)
                self.land[slot, spot] = total.astype(jnp.bfloat16)
                return carry

            lax.fori_loop(0, half // unit, step, 0)

    def add_tail(self, stage, bit, following):
        size = self.sizes[stage]
        half = size // 2
        middle = self.land.shape[2] // 2
        source, base = self.held(stage, bit)
        for slot in range(self.land.shape[0]):
            mine = source[slot, pl.ds(base, size)]
            theirs = self.land[slot, pl.ds(self.spots[stage], size)]
            self.tail[slot] = mine.astype(jnp.float32) + theirs.astype(jnp.float32)
            other = self.tail[slot, pl.ds(pl.multiple_of((1 - following) * half, 8), half)]
            self.pack[slot] = jnp.concatenate(
                [other[:, :middle], other[:, middle:]], axis=0
            ).astype(jnp.bfloat16)

    def finish(self, bit):
        size = self.sizes[-1]
        for slot in range(self.out.shape[0]):
            mine = self.tail[slot, pl.ds(pl.multiple_of(bit * size, 8), size)]
            theirs = self.tail_land[slot].astype(jnp.float32)
            self.out[slot] = mine + jnp.concatenate([theirs[:size], theirs[size:]], axis=1)


class Stream:
    def __init__(self, order, partner_of, pieces):
        self.order, self.partner_of, self.pieces = order, partner_of, pieces
        self.stages = len(order)

    def launch(self, stage):
        partner, bit = self.partner_of[self.order[stage]]
        for piece in self.pieces:
            piece.copy(stage, partner, bit).start()

    def advance(self, stage):
        partner, bit = self.partner_of[self.order[stage]]
        for piece in self.pieces:
            piece.copy(stage, partner, bit).wait()
        if stage == self.stages - 1:
            for piece in self.pieces:
                piece.finish(bit)
        elif stage == self.stages - 2:
            for piece in self.pieces:
                piece.add_tail(stage, bit, self.partner_of[self.order[stage + 1]][1])
            self.launch(stage + 1)
        else:
            following = self.partner_of[self.order[stage + 1]][1]
            for piece in self.pieces:
                piece.add(stage, bit, 1 - following)
            self.launch(stage + 1)
            for piece in self.pieces:
                piece.add(stage, bit, following)


def partners(me, masks):
    result = {}
    for mask in masks:
        bit = lax.rem(lax.div(me, mask), 2)
        result[mask] = (me + mask - 2 * mask * bit, bit)
    return result


EARLY = (
    (0, 2, 24, 768),
    (1, 1, 96, 512),
    (2, 1, 24, 768),
    (3, 1, 96, 256),
    (4, 1, 24, 768),
    (4, 1, 24, 256),
    (4, 1, 8, 256),
    (5, 1, 24, 768),
)
LATE = (
    (6, 1, 24, 768),
    (7, 1, 24, 768),
    (8, 1, 24, 768),
    (9, 1, 24, 768),
    (10, 1, 24, 768),
    (11, 1, 24, 768),
    (11, 1, 8, 768),
)
STREAM_ORDER = (0, 1, 2, 2, 0, 1, 1, 1, 2, 1, 0, 0)

WORD_POINTS = ("word0", "word1", "word2", "word3")

PLAN = {('p', 0): ((0, 0),), ('r', 1): ((1, 0), (2, 0)), ('p', 1): ((3, 0),), ('r', 2): ((4, 0), (5, 0)), ('r', 3): ((2, 1), (0, 1)), ('p', 4): ((3, 1),), ('r', 5): ((1, 1), (4, 1), (2, 2)), 'KV': ((5, 1),), 'ee': ((3, 2),), 'ww': ((6, 0), (7, 0), (8, 0), (0, 2), (1, 2)), 'ent': ((9, 0), (2, 3), (10, 0), (4, 2), (5, 2)), 'we': ((3, 3),), 'word0': ((8, 1),), 'word1': ((6, 1), (11, 0), (0, 3)), 'word3': ((10, 1),), 'end': ((1, 3), (6, 2), (7, 1), (4, 3), (5, 3), (8, 2), (9, 1), (0, 4), (2, 4), (11, 1), (3, 4), (1, 4), (6, 3), (7, 2), (10, 2), (4, 4), (5, 4), (8, 3), (6, 4), (7, 3), (11, 2), (9, 2), (8, 4), (10, 3), (7, 4), (11, 3), (9, 3), (10, 4), (11, 4), (9, 4))}


def piece_scratch(spec, stages, source, own):
    _, slots, rows, width = spec
    owners = 2**stages
    shapes = []
    if source:
        shapes.append(pltpu.VMEM((slots, rows * owners, width), jnp.bfloat16))
    if own:
        shapes.append(pltpu.VMEM((slots, rows * owners // 2, width), jnp.bfloat16))
    shapes += [
        pltpu.VMEM((slots, rows * (owners - 2), width), jnp.bfloat16),
        pltpu.VMEM((slots, 2 * rows, width), jnp.float32),
        pltpu.VMEM((slots, 2 * rows, width // 2), jnp.bfloat16),
        pltpu.VMEM((slots, 2 * rows, width // 2), jnp.bfloat16),
        pltpu.SemaphoreType.DMA((stages,)),
        pltpu.SemaphoreType.DMA((stages,)),
    ]
    return shapes


def attention_back_kernel(orders, *refs):
    stages = len(orders[0])
    refs = list(refs)

    def take(count):
        taken = refs[:count]
        del refs[:count]
        return taken

    early_send = take(len(EARLY))
    (hidden, qword, qent, keys, values, cgrad, feat_q, feat_k, lse_delta, first_grad, target_grad, slot_row) = take(12)
    (w_ww, w_we, w_ew, w_ee, w_key, w_value, dense, entity_low) = take(8)
    early_out = take(len(EARLY))
    late_out = take(len(LATE))
    words_out, request_out = take(2)
    devices = request_out.shape[0]
    early_pieces = []
    own_copies = []
    me = lax.axis_index("dp")
    partner_of = partners(me, orders[0])
    own_sem = refs.pop()
    request_sems = refs.pop()
    request_send = refs.pop()
    word_weights = []
    dqw, dqe, dkey, dvalue, prob_s, grad_s, flip, hidden_t, hidden_te, entity_t = refs[-10:]
    del refs[-10:]
    pieces = [[] for _ in STREAM_ORDER]
    early_flat = []
    for index, spec in enumerate(EARLY):
        own, land, tail, pack, tail_land, send_sem, recv_sem = take(7)
        piece = Piece(
            spec[2], stages, early_send[index], own, land, tail, pack, tail_land,
            early_out[index], send_sem, recv_sem,
        )
        pieces[spec[0]].append(piece)
        early_flat.append(piece)
        bit = partner_of[orders[STREAM_ORDER[spec[0]]][0]][1]
        size = spec[2] * 2 ** (stages - 1)
        own_copies.append(
            pltpu.make_async_copy(
                early_send[index].at[:, pl.ds(pl.multiple_of(bit * size, 16), size)],
                own,
                own_sem.at[index],
            )
        )
    late_source = []
    for index, spec in enumerate(LATE):
        source, land, tail, pack, tail_land, send_sem, recv_sem = take(7)
        late_source.append(source)
        pieces[spec[0]].append(
            Piece(
                spec[2], stages, source, None, land, tail, pack, tail_land,
                late_out[index], send_sem, recv_sem,
            )
        )
    spare = (early_flat[1].own, early_flat[3].own)
    split = spare[0].shape[2]
    for index, weight in enumerate((w_ww, w_we)):
        rows = weight.shape[0]
        for part, at in enumerate((pl.ds(0, split), pl.ds(split, weight.shape[1] - split))):
            word_weights.append(
                pltpu.make_async_copy(
                    weight.at[:, at],
                    spare[part].at[0, pl.ds(index * rows, rows)],
                    own_sem.at[len(EARLY) + 2 * index + part],
                )
            )
    streams = [
        Stream(orders[order], partner_of, pieces[index])
        for index, order in enumerate(STREAM_ORDER)
    ]
    first_late = LATE[0][0]

    def go_on(point):
        for index, stage in PLAN.get(point, ()):
            if stage == 0 and index < first_late:
                for piece, spec in enumerate(EARLY):
                    if spec[0] == index:
                        own_copies[piece].wait()
            streams[index].advance(stage)
            if stage == 0 and index in (1, 3):
                for copy in word_weights[(index - 1) // 2 :: 2]:
                    copy.start()

    greet_all(me, devices)
    for stream in streams[:first_late]:
        stream.launch(0)
    for copy in own_copies:
        copy.start()

    width = hidden.shape[1]
    seq_len = hidden.shape[0]
    words = words_out.shape[0]
    block = 128
    lane = lax.broadcasted_iota(jnp.int32, (1, block), 1)
    low_half = (lane < HD).astype(jnp.float32).astype(jnp.bfloat16)
    high_half = (lane >= HD).astype(jnp.float32).astype(jnp.bfloat16)
    halves = (low_half, high_half)

    def flip_step(index, carry):
        at = pl.ds(pl.multiple_of(index * block, block), block)
        flip[at] = hidden[:, at].astype(jnp.float32).T
        return carry

    lax.fori_loop(0, width // block, flip_step, 0)
    owners = 2**stages
    rows = width // owners
    for slot, order in enumerate(orders):
        begin = words if slot == 2 else 0
        for pair in range(owners // 2):
            one, two = place_owner(order, 2 * pair), place_owner(order, 2 * pair + 1)
            both = jnp.concatenate(
                [flip[one * rows : one * rows + rows, begin:], flip[two * rows : two * rows + rows, begin:]],
                axis=0,
            ).astype(jnp.bfloat16)
            if slot == 2:
                hidden_te[pair * 2 * rows : (pair + 1) * 2 * rows] = both
            else:
                hidden_t[slot, pair * 2 * rows : (pair + 1) * 2 * rows] = both

    go_on("start")

    def go_on_in_loop(name, pair):
        for point in range(width // block):
            if (name, point) in PLAN:
                pl.when(pair == point)(functools.partial(go_on, (name, point)))

    def pair_step(pair, carry):
        lanes = pl.ds(pl.multiple_of(pair * block, block), block)
        key_pair = keys[:, lanes]
        value_pair = values[:, lanes]
        key_feat = [key_pair * halves[h] + feat_k[...] * halves[1 - h] for h in range(2)]
        key_only = [key_pair * halves[h] for h in range(2)]
        value_only = [value_pair * halves[h] for h in range(2)]

        def row_step(index, inner):
            at = pl.ds(pl.multiple_of(index * block, block), block)
            qw = qword[at, lanes]
            qe = qent[at, lanes]
            feats = feat_q[at]
            given = cgrad[at, lanes]
            stats = lse_delta[at]
            spot = lax.broadcasted_iota(jnp.int32, (1, block), 1) - 4 * pair
            total_w = jnp.zeros((block, block), jnp.float32)
            total_e = jnp.zeros((block, block), jnp.float32)
            for h in range(2):
                left_w = qw * halves[h] + feats * halves[1 - h]
                left_e = qe * halves[h] + feats * halves[1 - h]
                scores = jnp.concatenate(
                    [
                        dot_right_t(left_w, key_feat[h][:words]),
                        dot_right_t(left_e, key_feat[h][words:]),
                    ],
                    axis=1,
                )
                prob = jnp.exp(scores - jnp.sum(jnp.where(spot == h, stats, 0.0), axis=1, keepdims=True))
                pgrad = dot_right_t(given, value_only[h])
                sgrad = (prob * (pgrad - jnp.sum(jnp.where(spot == 2 + h, stats, 0.0), axis=1, keepdims=True))).astype(jnp.bfloat16)
                prob_s[h, at] = prob.astype(jnp.bfloat16)
                grad_s[h, at] = sgrad
                total_w += dot_plain(sgrad[:, :words], key_only[h][:words])
                total_e += dot_plain(sgrad[:, words:], key_only[h][words:])
            dqw[at, lanes] = total_w.astype(jnp.bfloat16)
            dqe[at, lanes] = total_e.astype(jnp.bfloat16)
            return inner

        lax.fori_loop(0, seq_len // block, row_step, 0)
        go_on_in_loop("r", pair)
        qw_all, qe_all, given_all = qword[:, lanes], qent[:, lanes], cgrad[:, lanes]
        dkey[:words, lanes] = (
            dot_left_t(grad_s[0, :, :words], qw_all * halves[0])
            + dot_left_t(grad_s[1, :, :words], qw_all * halves[1])
        ).astype(jnp.bfloat16)
        dkey[words:, lanes] = (
            dot_left_t(grad_s[0, :, words:], qe_all * halves[0])
            + dot_left_t(grad_s[1, :, words:], qe_all * halves[1])
        ).astype(jnp.bfloat16)
        dvalue[:, lanes] = (
            dot_left_t(prob_s[0], given_all * halves[0])
            + dot_left_t(prob_s[1], given_all * halves[1])
        ).astype(jnp.bfloat16)

        go_on_in_loop("p", pair)
        return carry

    lax.fori_loop(0, width // block, pair_step, 0)

    query_scale = HD ** (-0.5)
    column = 384

    def weight_grad(source, slot, order_slot, grad, begin, end, scale):
        for cut in range(0, width, column):
            left = hidden_te[...] if order_slot == 2 else hidden_t[order_slot, :, begin:end]
            piece = dot_plain(left, grad[begin:end, cut : cut + column])
            if scale:
                piece = piece * query_scale
            source[slot, :, cut : cut + column] = piece.astype(jnp.bfloat16)

    weight_grad(late_source[0], 0, 1, dkey, 0, seq_len, False)
    streams[6].launch(0)
    weight_grad(late_source[1], 0, 1, dvalue, 0, seq_len, False)
    streams[7].launch(0)
    go_on("KV")
    weight_grad(late_source[2], 0, 2, dqw, words, seq_len, True)
    streams[8].launch(0)
    go_on("ew")
    weight_grad(late_source[3], 0, 1, dqe, words, seq_len, True)
    streams[9].launch(0)
    go_on("ee")
    weight_grad(late_source[4], 0, 0, dqw, 0, words, True)
    streams[10].launch(0)
    go_on("ww")

    def data_grad(begin, size, queries):
        at = pl.ds(begin, size)
        return (
            first_grad[at]
            + query_scale * queries(at)
            + dot_right_t(dkey[at], w_key[...])
            + dot_right_t(dvalue[at], w_value[...])
        )

    def entity_queries(at):
        return dot_right_t(dqw[at], w_ew[...]) + dot_right_t(dqe[at], w_ee[...])

    def word_queries(at):
        total = 0.0
        for index, grad in enumerate((dqw, dqe)):
            rows_at = pl.ds(index * width, width)
            total += dot_right_t(grad[at, :split], spare[0][0, rows_at])
            total += dot_right_t(grad[at, split:], spare[1][0, rows_at])
        return total

    state_low = data_grad(words, seq_len - words, entity_queries).astype(jnp.bfloat16)
    vectors = jnp.concatenate(
        [dot_right_t(state_low, dense[...]).astype(jnp.bfloat16), target_grad[...]], axis=0
    )
    entries = slot_row.shape[1]
    wanted = lax.broadcasted_iota(jnp.int32, (vectors.shape[0], entries), 0)
    placing = (wanted == slot_row[0:1]).astype(jnp.float32).astype(jnp.bfloat16)
    per_request = dot_left_t(placing, vectors).astype(jnp.bfloat16)
    request_send[...] = per_request.reshape(request_send.shape)

    def request_copy(step):
        peer = lax.rem(me + step, devices)
        return pltpu.make_async_remote_copy(
            src_ref=request_send.at[peer],
            dst_ref=request_out.at[me],
            send_sem=request_sems.at[0, step],
            recv_sem=request_sems.at[1, step],
            device_id=(peer,),
            device_id_type=MESH_ID,
        )

    def begin_request(step, carry):
        request_copy(step).start()
        return carry

    def finish_request(step, carry):
        request_copy(step).wait()
        return carry

    lax.fori_loop(1, devices, begin_request, 0)
    request_out[me] = request_send[me]
    entity_width = dense.shape[0]
    few = entity_width // owners
    for cut in range(0, entity_width, block):
        flip[cut : cut + block, :block] = entity_low[:, cut : cut + block].astype(jnp.float32).T
    for pair in range(owners // 2):
        one, two = place_owner(orders[0], 2 * pair), place_owner(orders[0], 2 * pair + 1)
        both = jnp.concatenate(
            [flip[one * few : one * few + few, :block], flip[two * few : two * few + few, :block]],
            axis=0,
        )
        entity_t[pair * 2 * few : (pair + 1) * 2 * few] = both.astype(jnp.bfloat16)
    late_source[6][0] = dot_plain(entity_t[...], state_low).astype(jnp.bfloat16)
    go_on("ent")
    weight_grad(late_source[5], 0, 0, dqe, 0, words, True)
    streams[11].launch(0)
    go_on("we")
    for copy in word_weights:
        copy.wait()

    def word_step(index, carry):
        begin = pl.multiple_of(index * block, block)
        words_out[pl.ds(begin, block)] = data_grad(begin, block, word_queries).astype(jnp.bfloat16)
        for point in range(words // block):
            name = WORD_POINTS[point]
            if name in PLAN:
                pl.when(index == point)(functools.partial(go_on, name))
        return carry

    lax.fori_loop(0, words // block, word_step, 0)
    go_on("end")
    lax.fori_loop(1, devices, finish_request, 0)


def in_order(grad, order):
    bits = len(order)
    owners = 2**bits
    view = grad.reshape((2,) * bits + (grad.shape[0] // owners, grad.shape[1]))
    spots = tuple(bits - mask.bit_length() for mask in order)
    return view.transpose(spots + (bits, bits + 1)).reshape(grad.shape)


def attention_back(early_grads, inputs, weights, collective_id):
    devices = lax.axis_size("dp")
    orders = stage_masks(devices)
    stages = len(orders[0])
    hidden = inputs[0]
    seq_len, width = hidden.shape
    slots = weights[-1].shape[0]
    words = seq_len - slots
    outs = [
        jax.ShapeDtypeStruct((count, rows, wide), jnp.float32)
        for _, count, rows, wide in EARLY + LATE
    ] + [
        jax.ShapeDtypeStruct((words, width), jnp.bfloat16),
        jax.ShapeDtypeStruct(
            (devices, inputs[11].shape[1] // devices, weights[-2].shape[0]), jnp.bfloat16
        ),
    ]
    scratch = []
    for spec in EARLY:
        scratch += piece_scratch(spec, stages, False, True)
    for spec in LATE:
        scratch += piece_scratch(spec, stages, True, False)
    scratch += [pltpu.VMEM((seq_len, width), jnp.bfloat16)] * 4
    scratch += [pltpu.VMEM((2, seq_len, seq_len), jnp.bfloat16)] * 2
    scratch += [
        pltpu.VMEM((width, seq_len), jnp.float32),
        pltpu.VMEM((2, width, seq_len), jnp.bfloat16),
        pltpu.VMEM((width, slots), jnp.bfloat16),
        pltpu.VMEM((weights[-2].shape[0], slots), jnp.bfloat16),
        pltpu.VMEM((devices, inputs[11].shape[1] // devices, weights[-2].shape[0]), jnp.bfloat16),
        pltpu.SemaphoreType.DMA((2, devices)),
        pltpu.SemaphoreType.DMA((len(EARLY) + 4,)),
    ]
    vmem = pl.BlockSpec(memory_space=pltpu.VMEM)
    return pl.pallas_call(
        functools.partial(attention_back_kernel, orders),
        out_shape=outs,
        in_specs=[pl.BlockSpec(memory_space=pltpu.HBM)] * len(EARLY)
        + [vmem] * len(inputs)
        + [pl.BlockSpec(memory_space=pltpu.HBM)] * 2
        + [vmem] * (len(weights) - 2),
        out_specs=[vmem] * len(outs),
        scratch_shapes=scratch,
        compiler_params=pltpu.CompilerParams(
            collective_id=collective_id, has_side_effects=True, vmem_limit_bytes=62 * 2**20
        ),
    )(*early_grads, *inputs, *weights)


def fused_body(
    word_states,
    word_segments,
    entity_segments,
    request_rows,
    request_slot,
    mask_slots,
    entity_table,
    vocab_bias,
    entity_dense,
    query_ww,
    query_we,
    query_ew,
    query_ee,
    key_weight,
    value_weight,
    out_weight,
    norm1_gain,
    norm1_bias,
    up_weight,
    down_weight,
    norm2_gain,
    norm2_bias,
    head_weight,
    head_gain,
    head_bias,
    cotangent,
):
    devices = lax.axis_size("dp")
    low = jnp.bfloat16
    slot_count = entity_segments.shape[1]
    mask_count = mask_slots.shape[1]
    request_count = slot_count + mask_count
    table_rows = entity_table.shape[0]
    grad_scale = 1.0 / (mask_count * devices)
    orders = stage_masks(devices)
    capacity = request_rows.shape[1]
    room = -(-capacity // 16) * 16 - capacity
    kind = jnp.where(request_slot >= slot_count, table_rows, 0)
    codes = jnp.where(request_slot < request_count, request_rows + kind, -1)
    codes = jnp.pad(codes, ((0, 0), (0, room)), constant_values=-1)
    codes = jnp.broadcast_to(codes[:, :, None], codes.shape + (128,))
    slot_row = jnp.pad(request_slot, ((0, 0), (0, room)), constant_values=request_count)
    slot_row = jnp.broadcast_to(slot_row.reshape(1, -1), (8, slot_row.size))
    bias_col = jnp.broadcast_to(vocab_bias[:, None], (table_rows, 128))
    entity_low, target_vecs, target_bias, code_row = lookup(
        codes, entity_table, bias_col, slot_row, slot_count, mask_count, 0
    )
    segment_row = jnp.concatenate([word_segments[0], entity_segments[0]])
    columns = jnp.arange(128, dtype=jnp.int32)[None, :] % HD
    same = segment_row[:, None] == columns
    feat_q = same.astype(low)
    feat_k = jnp.where(same | (columns >= 4), 0.0, MASKED).astype(low)
    choose = (mask_slots[0][:, None] == jnp.arange(slot_count, dtype=jnp.int32)[None, :]).astype(low)
    (
        hidden_low,
        query_word,
        query_entity,
        key_rows,
        values,
        context_low,
        lse_lanes,
        residual_one,
        normed_low,
        activated,
        gelu_slope,
        residual_two,
        layer_low,
        picked_low,
        head_pre,
        head_low,
    ) = forward_pass(
        [
            word_states,
            entity_low,
            feat_q,
            feat_k,
            choose,
            entity_dense,
            query_ww,
            query_we,
            query_ew,
            query_ee,
            key_weight,
            value_weight,
            out_weight,
            norm1_gain[None],
            norm1_bias[None],
            up_weight,
            down_weight,
            norm2_gain[None],
            norm2_bias[None],
            head_weight,
            head_gain[None],
            head_bias[None],
        ]
    )
    table_grad, bias_grad, losses, total_loss, head_grad = head_and_table(
        head_low,
        entity_table,
        vocab_bias.astype(jnp.float32)[None, :],
        target_vecs,
        target_bias,
        grad_scale,
        1,
    )
    (
        up_a,
        up_b,
        head_a,
        out_b,
        down_b,
        up_c,
        down_c,
        first_grad,
        context_grad,
        lse_delta,
        head_vectors,
        wide_vectors,
    ) = middle_back(
        [
            head_grad,
            target_vecs,
            head_pre,
            head_gain[None],
            picked_low,
            head_weight,
            choose,
            cotangent,
            residual_two,
            norm2_gain[None],
            normed_low,
            residual_one,
            norm1_gain[None],
            out_weight,
            context_low,
            lse_lanes,
            activated,
            gelu_slope,
            up_weight,
            down_weight,
        ],
        orders,
        grad_scale,
    )
    vectors = jnp.concatenate(
        [head_vectors[i].reshape(devices, -1) for i in range(2)]
        + [wide_vectors[i].reshape(devices, -1) for i in range(4)],
        axis=1,
    )
    vectors = jnp.pad(vectors, ((0, 0), (0, 256 - vectors.shape[1])))[:, None, :]
    vectors = jnp.pad(vectors, ((0, 0), (0, 7), (0, 0))).reshape(8 * devices, 256)
    vectors = in_order(vectors.astype(low), orders[0])[None]
    (
        up_sum,
        down_sum,
        up_rest,
        down_rest,
        up_third,
        head_sum,
        vector_sum,
        out_sum,
        key_sum,
        value_sum,
        ew_sum,
        ee_sum,
        ww_sum,
        we_sum,
        dense_sum,
        words_grad,
        back_rows,
    ) = attention_back(
        [up_a, down_b, up_c, down_c, up_b, head_a, vectors, out_b],
        [
            hidden_low,
            query_word,
            query_entity,
            key_rows,
            values,
            context_grad,
            feat_q,
            feat_k,
            lse_delta,
            first_grad,
            (-grad_scale * head_low.astype(jnp.float32)).astype(low),
            slot_row,
        ],
        [
            query_ww,
            query_we,
            query_ew,
            query_ee,
            key_weight,
            value_weight,
            entity_dense,
            entity_low,
        ],
        2,
    )
    table_grad, bias_grad = scatter_add(
        code_row, back_rows.reshape(-1, back_rows.shape[2]), table_grad, bias_grad, grad_scale
    )
    row = vector_sum[0, 0]
    few, many = head_gain.shape[0] // devices, norm1_gain.shape[0] // devices
    spots = [0, few, 2 * few] + [2 * few + many * (i + 1) for i in range(4)]
    vector_out = [row[spots[i] : spots[i + 1]] for i in range(6)]
    return (
        total_loss[0, 0],
        layer_low,
        words_grad,
        table_grad,
        bias_grad[0],
        dense_sum[0],
        ww_sum[0],
        we_sum[0],
        ew_sum[0],
        ee_sum[0],
        key_sum[0],
        value_sum[0],
        out_sum[0],
        vector_out[4],
        vector_out[5],
        jnp.concatenate([up_sum[0], up_sum[1], up_third[0], up_rest[0]], axis=1),
        jnp.concatenate([down_sum[0], down_rest[0]], axis=1),
        vector_out[2],
        vector_out[3],
        head_sum[0],
        vector_out[0],
        vector_out[1],
        losses[:, 0],
    )


def solution(mesh):
    in_specs = (
        P("dp", None),
        P("dp", None),
        P("dp", None),
        P("dp", None),
        P("dp", None),
        P("dp", None),
        P("dp", None),
        P("dp"),
        P(),
        P(),
        P(),
        P(),
        P(),
        P(),
        P(),
        P(),
        P(),
        P(),
        P(),
        P(),
        P(),
        P(),
        P(),
        P(),
        P(),
        P("dp", None),
    )
    out_specs = (
        P(),
        P("dp", None),
        P("dp", None),
        P("dp", None),
        P("dp"),
        P("dp", None),
        P("dp", None),
        P("dp", None),
        P("dp", None),
        P("dp", None),
        P("dp", None),
        P("dp", None),
        P("dp", None),
        P("dp"),
        P("dp"),
        P("dp", None),
        P("dp", None),
        P("dp"),
        P("dp"),
        P("dp", None),
        P("dp"),
        P("dp"),
        P("dp"),
    )
    chosen = fused_body if mesh.shape["dp"] == 32 else body
    return jax.shard_map(chosen, mesh=mesh, in_specs=in_specs, out_specs=out_specs, check_vma=False)
```

```python
import functools

import jax
import jax.numpy as jnp
from jax import lax
from jax.experimental import pallas as pl
from jax.experimental.pallas import tpu as pltpu
from jax.sharding import PartitionSpec as P

MESH_ID = pl.DeviceIdType.MESH

HD = 64


EPSILON = 1e-05
MASKED = -1000000000.0


def dot_plain(left_side, right_side):
    return jnp.dot(left_side, right_side, preferred_element_type=jnp.float32)


def dot_left_t(left_side, right_side):
    return lax.dot_general(
        left_side, right_side, (((0,), (0,)), ((), ())), preferred_element_type=jnp.float32
    )


def dot_right_t(left_side, right_side):
    return lax.dot_general(
        left_side, right_side, (((1,), (1,)), ((), ())), preferred_element_type=jnp.float32
    )


def dot_exact(left_side, right_side):
    return jnp.dot(
        left_side, right_side, precision=lax.Precision.HIGHEST, preferred_element_type=jnp.float32
    )


def layer_norm(tensor, gain_vec, shift_vec):
    center = tensor - jnp.mean(tensor, axis=-1, keepdims=True)
    spread = jnp.mean(center * center, axis=-1, keepdims=True)
    return center * lax.rsqrt(spread + EPSILON) * gain_vec + shift_vec


def gelu_exact(tensor):
    return jax.nn.gelu(tensor, approximate=False)


def head_act(tensor, gain_vec, shift_vec):
    return layer_norm(gelu_exact(tensor), gain_vec, shift_vec)


def norm_back(tensor, gain_vec, shift_vec, grad_out):
    result, pullback = jax.vjp(layer_norm, tensor, gain_vec, shift_vec)
    return pullback(grad_out)


def attn_scores(query_word, query_entity, key_rows, allowed, word_count):
    to_words = jnp.einsum(
        "qhd,khd->hqk", query_word, key_rows[:word_count], preferred_element_type=jnp.float32
    )
    to_entities = jnp.einsum(
        "qhd,khd->hqk", query_entity, key_rows[word_count:], preferred_element_type=jnp.float32
    )
    return jnp.where(allowed[None], jnp.concatenate([to_words, to_entities], axis=2), MASKED)


def greet_all(me, devices):
    barrier = pltpu.get_barrier_semaphore()

    def greet(step, carry):
        pl.semaphore_signal(
            barrier, inc=1, device_id=(lax.rem(me + step, devices),), device_id_type=MESH_ID
        )
        return carry

    lax.fori_loop(1, devices, greet, 0)
    pl.semaphore_wait(barrier, devices - 1)


def swap_kernel(devices, gather, source, target, send_sem, recv_sem):
    me = lax.axis_index("dp")
    greet_all(me, devices)

    def piece(step):
        peer = lax.rem(me + step, devices)
        return pltpu.make_async_remote_copy(
            src_ref=source if gather else source.at[peer],
            dst_ref=target.at[me],
            send_sem=send_sem.at[step],
            recv_sem=recv_sem.at[step],
            device_id=(peer,),
            device_id_type=MESH_ID,
        )

    def begin(step, carry):
        piece(step).start()
        return carry

    def finish(step, carry):
        piece(step).wait()
        return carry

    lax.fori_loop(1, devices, begin, 0)
    target[me] = source[...] if gather else source[me]
    lax.fori_loop(1, devices, finish, 0)


def direct_swap(value, collective_id, gather=False):
    devices = lax.axis_size("dp")
    shape = (devices,) + value.shape if gather else value.shape
    return pl.pallas_call(
        functools.partial(swap_kernel, devices, gather),
        out_shape=jax.ShapeDtypeStruct(shape, value.dtype),
        in_specs=[pl.BlockSpec(memory_space=pltpu.VMEM)],
        out_specs=pl.BlockSpec(memory_space=pltpu.VMEM),
        scratch_shapes=[
            pltpu.SemaphoreType.DMA((devices,)),
            pltpu.SemaphoreType.DMA((devices,)),
        ],
        compiler_params=pltpu.CompilerParams(collective_id=collective_id, has_side_effects=True),
    )(value)


def stage_masks(devices):
    if devices == 32:
        axes = [[2], [4], [8, 16]]
    elif devices == 128:
        axes = [[2, 4], [8, 16], [32, 64]]
    else:
        axes = [[2**bit] for bit in range(1, devices.bit_length() - 1)]
        axes = axes + [[] for _ in range(3 - len(axes))]
    first, second, third = axes[0], axes[1], sum(axes[2:], [])
    return (
        [1] + first + second + third,
        [1] + second + first + third,
        [1] + third + first + second,
    )


def sum_kernel(masks, rows, *refs):
    parts = len(masks)
    stages = len(masks[0])
    sources, results = refs[:parts], refs[parts : 2 * parts]
    landing = refs[2 * parts : 3 * parts]
    send_sem, recv_sem = refs[3 * parts :]
    me = lax.axis_index("dp")
    barrier = pltpu.get_barrier_semaphore()
    partner_of = {}
    for mask in masks[0]:
        bit = lax.rem(lax.div(me, mask), 2)
        partner_of[mask] = (me + mask - 2 * mask * bit, bit)
    for mask in masks[0]:
        pl.semaphore_signal(
            barrier, inc=1, device_id=(partner_of[mask][0],), device_id_type=MESH_ID
        )
    pl.semaphore_wait(barrier, stages)
    sizes = [[rows[part] * 2 ** (stages - 1 - stage) for stage in range(stages)] for part in range(parts)]
    places = [[sum(size[:stage]) for stage in range(stages)] for size in sizes]

    def launch(part, stage):
        partner, bit = partner_of[masks[part][stage]]
        size = sizes[part][stage]
        away = (1 - bit) * size
        copy = pltpu.make_async_remote_copy(
            src_ref=sources[part].at[pl.ds(away, size)]
            if stage == 0
            else landing[part].at[pl.ds(places[part][stage - 1] + away, size)],
            dst_ref=landing[part].at[pl.ds(places[part][stage], size)],
            send_sem=send_sem.at[part, stage],
            recv_sem=recv_sem.at[part, stage],
            device_id=(partner,),
            device_id_type=MESH_ID,
        )
        copy.start()
        return copy

    flying = [launch(part, 0) for part in range(parts)]

    def add_rows(part, stage, start, count):
        keep = partner_of[masks[part][stage]][1] * sizes[part][stage] + start
        last = stage == stages - 1

        def step(index, carry):
            theirs = pl.ds(pl.multiple_of(places[part][stage] + start + index * 16, 16), 16)
            if stage == 0:
                mine = sources[part][pl.ds(pl.multiple_of(keep + index * 16, 16), 16)]
            else:
                mine = landing[part][
                    pl.ds(pl.multiple_of(places[part][stage - 1] + keep + index * 16, 16), 16)
                ]
            total = mine.astype(jnp.float32) + landing[part][theirs].astype(jnp.float32)
            if last:
                results[part][pl.ds(pl.multiple_of(index * 16, 16), 16)] = total
            else:
                landing[part][theirs] = total.astype(jnp.bfloat16)
            return carry

        lax.fori_loop(0, count // 16, step, 0, unroll=min(4, count // 16))

    for stage in range(stages):
        for part in range(parts):
            flying[part].wait()
            if stage == stages - 1:
                add_rows(part, stage, 0, sizes[part][stage])
                continue
            bit = partner_of[masks[part][stage + 1]][1]
            half = sizes[part][stage] // 2
            add_rows(part, stage, (1 - bit) * half, half)
            flying[part] = launch(part, stage + 1)
            add_rows(part, stage, bit * half, half)


def sum_scatter(parts, collective_id):
    devices = lax.axis_size("dp")
    masks = stage_masks(devices)
    rows = [part.shape[1] for part in parts]
    width = parts[0].shape[2]
    bits = devices.bit_length() - 1
    ordered = []
    for part, order in zip(parts, masks):
        view = part.reshape((2,) * bits + part.shape[1:])
        places = [bits - mask.bit_length() for mask in order]
        view = view.transpose(tuple(places) + (bits, bits + 1))
        ordered.append(view.reshape(devices * part.shape[1], width))
    return pl.pallas_call(
        functools.partial(sum_kernel, masks, rows),
        out_shape=[jax.ShapeDtypeStruct((count, width), jnp.float32) for count in rows],
        in_specs=[pl.BlockSpec(memory_space=pltpu.VMEM)] * len(parts),
        out_specs=[pl.BlockSpec(memory_space=pltpu.VMEM)] * len(parts),
        scratch_shapes=[pltpu.VMEM((devices * count, width), jnp.bfloat16) for count in rows]
        + [pltpu.SemaphoreType.DMA((len(parts), bits)), pltpu.SemaphoreType.DMA((len(parts), bits))],
        input_output_aliases={},
        compiler_params=pltpu.CompilerParams(
            collective_id=collective_id, has_side_effects=True, vmem_limit_bytes=56 * 2**20
        ),
    )(*ordered)


def by_owner(grad, width):
    devices = lax.axis_size("dp")
    rows = grad.shape[0] // devices
    blocks = grad.astype(jnp.bfloat16).reshape(devices, rows, grad.shape[1])
    if grad.shape[1] > width:
        cuts = grad.shape[1] // width
        return jnp.concatenate(jnp.split(blocks, cuts, axis=2), axis=1)
    if grad.shape[1] < width:
        return blocks.reshape(devices, rows * grad.shape[1] // width, width)
    return blocks


def from_owner(rows, shape):
    devices = lax.axis_size("dp")
    count, width = shape[0] // devices, shape[1]
    if width > rows.shape[1]:
        return jnp.concatenate(jnp.split(rows, width // rows.shape[1], axis=0), axis=1)
    return rows.reshape(count, width)


def sum_all(groups, collective_id):
    width = groups[0][0].shape[1]
    width = min(grad.shape[1] for group in groups for grad in group if grad.shape[1] >= 768)
    devices = lax.axis_size("dp")
    packed = []
    for group in groups:
        pieces = [by_owner(grad, width) for grad in group]
        count = sum(piece.shape[1] for piece in pieces)
        room = -(-count // 16) * 16 - count
        if room:
            pieces.append(jnp.zeros((devices, room, width), jnp.bfloat16))
        packed.append(jnp.concatenate(pieces, axis=1))
    sums = sum_scatter(packed, collective_id)
    results = []
    for group, total in zip(groups, sums):
        place, outs = 0, []
        for grad in group:
            count = grad.shape[0] // devices * grad.shape[1] // width
            outs.append(from_owner(total[place : place + count], grad.shape))
            place += count
        results.append(outs)
    return results


def body(
    word_states,
    word_segments,
    entity_segments,
    request_rows,
    request_slot,
    mask_slots,
    entity_table,
    vocab_bias,
    entity_dense,
    query_ww,
    query_we,
    query_ew,
    query_ee,
    key_weight,
    value_weight,
    out_weight,
    norm1_gain,
    norm1_bias,
    up_weight,
    down_weight,
    norm2_gain,
    norm2_bias,
    head_weight,
    head_gain,
    head_bias,
    cotangent,
):
    word_count = word_states.shape[0]
    model_width = word_states.shape[1]
    slot_count = entity_segments.shape[1]
    mask_count = mask_slots.shape[1]
    request_count = slot_count + mask_count
    seq_len = word_count + slot_count
    devices = lax.axis_size("dp")
    capacity = request_rows.shape[1]
    head_count = model_width // HD
    query_scale = HD ** (-0.5)
    emb_width = entity_table.shape[1]
    table_rows = entity_table.shape[0]
    total_mask = mask_count * devices
    grad_scale = 1.0 / total_mask
    id_block = jnp.pad(request_rows[:, None, :], ((0, 0), (0, 7), (0, 128 - capacity)))
    asked_ids = direct_swap(id_block, 0)[:, 0, :capacity]
    found_rows = jnp.take(entity_table, asked_ids, axis=0)
    found_bias = jnp.take(vocab_bias, asked_ids, axis=0)
    cap_room = -(-capacity // 16) * 16 - capacity
    found_all = jnp.concatenate(
        [found_rows, jnp.broadcast_to(found_bias[:, :, None], found_bias.shape + (128,))], axis=2
    )
    back_all = direct_swap(jnp.pad(found_all, ((0, 0), (0, cap_room), (0, 0))), 1)
    back_rows = back_all[:, :capacity, :emb_width]
    back_bias = back_all[:, :capacity, emb_width]
    got_rows = back_rows
    got_bias = back_bias
    slot_ids = request_slot.reshape(devices * capacity)
    placing = slot_ids[None, :] == jnp.arange(request_count, dtype=jnp.int32)[:, None]
    placing_low = placing.astype(jnp.bfloat16)
    request_vecs = dot_plain(placing_low, got_rows.reshape(devices * capacity, emb_width))
    request_bias = dot_plain(placing_low, got_bias.reshape(devices * capacity, 1))[:, 0]
    entity_low = request_vecs[:slot_count].astype(jnp.bfloat16)
    target_vecs = request_vecs[slot_count:]
    target_bias = request_bias[slot_count:]
    entity_states = dot_plain(entity_low, entity_dense)
    hidden = jnp.concatenate([word_states.astype(jnp.float32), entity_states], axis=0)
    hidden_low = hidden.astype(jnp.bfloat16)
    word_part = hidden_low[:word_count]
    entity_part = hidden_low[word_count:]
    query_word = (
        query_scale
        * jnp.concatenate(
            [dot_plain(word_part, query_ww), dot_plain(entity_part, query_ew)], axis=0
        )
    ).astype(jnp.bfloat16)
    query_entity = (
        query_scale
        * jnp.concatenate(
            [dot_plain(word_part, query_we), dot_plain(entity_part, query_ee)], axis=0
        )
    ).astype(jnp.bfloat16)
    key_rows = dot_plain(hidden_low, key_weight).astype(jnp.bfloat16)
    values = dot_plain(hidden_low, value_weight).astype(jnp.bfloat16)
    head_shape = (seq_len, head_count, HD)
    query_word_h = query_word.reshape(head_shape)
    query_entity_h = query_entity.reshape(head_shape)
    key_rows_h = key_rows.reshape(head_shape)
    values_h = values.reshape(head_shape)
    segment_row = jnp.concatenate([word_segments[0], entity_segments[0]])
    allowed = segment_row[:, None] == segment_row[None, :]
    scores = attn_scores(query_word_h, query_entity_h, key_rows_h, allowed, word_count)
    row_top = jnp.max(scores, axis=2, keepdims=True)
    exp_scores = jnp.exp(scores - row_top)
    row_total = jnp.sum(exp_scores, axis=2, keepdims=True)
    attn_low = (exp_scores / row_total).astype(jnp.bfloat16)
    row_lse = row_top + jnp.log(row_total)
    context = jnp.einsum("hqk,khd->qhd", attn_low, values_h, preferred_element_type=jnp.float32)
    context_low = context.reshape(seq_len, model_width).astype(jnp.bfloat16)
    attended = dot_plain(context_low, out_weight)
    residual_one = hidden + attended
    normed = layer_norm(residual_one, norm1_gain, norm1_bias)
    normed_low = normed.astype(jnp.bfloat16)
    up_value = dot_plain(normed_low, up_weight)
    activated = gelu_exact(up_value).astype(jnp.bfloat16)
    down_value = dot_plain(activated, down_weight)
    residual_two = normed + down_value
    layer_out = layer_norm(residual_two, norm2_gain, norm2_bias)
    choose = (mask_slots[0][:, None] == jnp.arange(slot_count, dtype=jnp.int32)[None, :]).astype(
        jnp.float32
    )
    picked_low = dot_exact(choose, layer_out[word_count:]).astype(jnp.bfloat16)
    head_pre = dot_plain(picked_low, head_weight)
    head_low = head_act(head_pre, head_gain, head_bias).astype(jnp.bfloat16)
    head_f32 = head_low.astype(jnp.float32)
    target_logit = jnp.sum(head_f32 * target_vecs, axis=1) + target_bias
    all_heads = direct_swap(head_low, 2, gather=True).reshape(total_mask, emb_width)
    block_rows = min(512, total_mask)
    block_count = total_mask // block_rows
    bias_f32 = vocab_bias.astype(jnp.float32)

    def block_logits(block_index):
        row_block = lax.dynamic_slice_in_dim(all_heads, block_index * block_rows, block_rows, 0)
        return (row_block, dot_right_t(row_block, entity_table) + bias_f32[None, :])

    def block_stats(block_index):
        row_block, logits = block_logits(block_index)
        top_value = jnp.max(logits, axis=1)
        return (top_value, jnp.sum(jnp.exp(logits - top_value[:, None]), axis=1))

    local_top, local_total = lax.map(block_stats, jnp.arange(block_count, dtype=jnp.int32))
    local_top = local_top.reshape(total_mask)
    local_total = local_total.reshape(total_mask)
    target_sum = jnp.sum(target_logit)
    stats = jnp.concatenate(
        [
            local_top.reshape(total_mask // 128, 128),
            local_total.reshape(total_mask // 128, 128),
            jnp.full((8, 128), target_sum),
        ],
        axis=0,
    )
    all_stats = direct_swap(stats, 3, gather=True)
    all_tops = all_stats[:, : total_mask // 128].reshape(devices, total_mask)
    all_totals = all_stats[:, total_mask // 128 : total_mask // 64].reshape(devices, total_mask)
    target_total = jnp.sum(all_stats[:, total_mask // 64, 0])
    global_top = jnp.max(all_tops, axis=0)
    global_total = jnp.sum(all_totals * jnp.exp(all_tops - global_top[None, :]), axis=0)
    lse_all = global_top + jnp.log(global_total)
    loss_value = (jnp.sum(lse_all) - target_total) * grad_scale
    own_lse = lax.dynamic_slice_in_dim(lse_all, lax.axis_index("dp") * mask_count, mask_count, 0)
    mask_loss = own_lse - target_logit

    def block_back(running, block_index):
        table_grad, bias_grad = running
        row_block, logits = block_logits(block_index)
        lse_block = lax.dynamic_slice_in_dim(lse_all, block_index * block_rows, block_rows, 0)
        logit_grad = (jnp.exp(logits - lse_block[:, None]) * grad_scale).astype(jnp.bfloat16)
        table_grad = table_grad + dot_left_t(logit_grad, row_block)
        bias_grad = bias_grad + jnp.sum(logit_grad.astype(jnp.float32), axis=0)
        return ((table_grad, bias_grad), dot_plain(logit_grad, entity_table))

    start_grads = (
        jnp.zeros((table_rows, emb_width), jnp.float32),
        jnp.zeros((table_rows,), jnp.float32),
    )
    (table_grad, bias_grad), head_terms = lax.scan(
        block_back, start_grads, jnp.arange(block_count, dtype=jnp.int32)
    )
    head_parts = direct_swap(head_terms.reshape(devices, mask_count, emb_width), 4)
    head_grad = jnp.sum(head_parts, axis=0)
    head_grad = head_grad - grad_scale * target_vecs
    target_grad = -grad_scale * head_f32
    pre_grad, head_gain_grad, head_bias_grad = jax.vjp(head_act, head_pre, head_gain, head_bias)[1](
        head_grad
    )
    pre_low = pre_grad.astype(jnp.bfloat16)
    head_weight_grad = dot_left_t(picked_low, pre_low)
    picked_grad = dot_right_t(pre_low, head_weight)
    out_grad = cotangent.astype(jnp.float32) + jnp.concatenate(
        [jnp.zeros((word_count, model_width), jnp.float32), dot_exact(choose.T, picked_grad)],
        axis=0,
    )
    resid_grad, norm2_gain_grad, norm2_bias_grad = norm_back(
        residual_two, norm2_gain, norm2_bias, out_grad
    )
    down_in = resid_grad.astype(jnp.bfloat16)
    down_grad = dot_left_t(activated, down_in)
    act_grad = dot_right_t(down_in, down_weight)
    up_grad = jax.vjp(gelu_exact, up_value)[1](act_grad)[0]
    up_low = up_grad.astype(jnp.bfloat16)
    up_weight_grad = dot_left_t(normed_low, up_low)
    normed_grad = resid_grad + dot_right_t(up_low, up_weight)
    first_grad, norm1_gain_grad, norm1_bias_grad = norm_back(
        residual_one, norm1_gain, norm1_bias, normed_grad
    )
    attn_in = first_grad.astype(jnp.bfloat16)
    out_weight_grad = dot_left_t(context_low, attn_in)
    context_grad = dot_right_t(attn_in, out_weight).astype(jnp.bfloat16).reshape(head_shape)
    scores_again = attn_scores(query_word_h, query_entity_h, key_rows_h, allowed, word_count)
    attn_prob = jnp.exp(scores_again - row_lse)
    prob_low = attn_prob.astype(jnp.bfloat16)
    prob_grad = jnp.einsum(
        "qhd,khd->hqk", context_grad, values_h, preferred_element_type=jnp.float32
    )
    values_grad = jnp.einsum(
        "hqk,qhd->khd", prob_low, context_grad, preferred_element_type=jnp.float32
    )
    values_grad = values_grad.reshape(seq_len, model_width).astype(jnp.bfloat16)
    row_delta = jnp.sum(attn_prob * prob_grad, axis=2, keepdims=True)
    score_grad = (attn_prob * (prob_grad - row_delta)).astype(jnp.bfloat16)
    qword_grad = jnp.einsum(
        "hqk,khd->qhd",
        score_grad[:, :, :word_count],
        key_rows_h[:word_count],
        preferred_element_type=jnp.float32,
    )
    qword_grad = qword_grad.reshape(seq_len, model_width).astype(jnp.bfloat16)
    qent_grad = jnp.einsum(
        "hqk,khd->qhd",
        score_grad[:, :, word_count:],
        key_rows_h[word_count:],
        preferred_element_type=jnp.float32,
    )
    qent_grad = qent_grad.reshape(seq_len, model_width).astype(jnp.bfloat16)
    keys_grad = jnp.concatenate(
        [
            jnp.einsum(
                "hqk,qhd->khd",
                score_grad[:, :, :word_count],
                query_word_h,
                preferred_element_type=jnp.float32,
            ),
            jnp.einsum(
                "hqk,qhd->khd",
                score_grad[:, :, word_count:],
                query_entity_h,
                preferred_element_type=jnp.float32,
            ),
        ],
        axis=0,
    )
    keys_grad = keys_grad.reshape(seq_len, model_width).astype(jnp.bfloat16)
    query_ww_grad = query_scale * dot_left_t(word_part, qword_grad[:word_count])
    query_ew_grad = query_scale * dot_left_t(entity_part, qword_grad[word_count:])
    query_we_grad = query_scale * dot_left_t(word_part, qent_grad[:word_count])
    query_ee_grad = query_scale * dot_left_t(entity_part, qent_grad[word_count:])
    key_weight_grad = dot_left_t(hidden_low, keys_grad)
    value_weight_grad = dot_left_t(hidden_low, values_grad)
    word_back = query_scale * (
        dot_right_t(qword_grad[:word_count], query_ww)
        + dot_right_t(qent_grad[:word_count], query_we)
    )
    entity_back = query_scale * (
        dot_right_t(qword_grad[word_count:], query_ew)
        + dot_right_t(qent_grad[word_count:], query_ee)
    )
    hidden_grad = (
        first_grad
        + jnp.concatenate([word_back, entity_back], axis=0)
        + dot_right_t(keys_grad, key_weight)
        + dot_right_t(values_grad, value_weight)
    )
    words_grad = hidden_grad[:word_count].astype(jnp.bfloat16)
    state_low = hidden_grad[word_count:].astype(jnp.bfloat16)
    dense_grad = dot_left_t(entity_low, state_low)
    entity_vec_grad = dot_right_t(state_low, entity_dense)
    vec_grad = jnp.concatenate([entity_vec_grad, target_grad], axis=0)
    bias_vec_grad = jnp.concatenate(
        [jnp.zeros((slot_count,), jnp.float32), jnp.full((mask_count,), -grad_scale, jnp.float32)]
    )
    placing_f32 = placing.astype(jnp.float32)
    per_request = dot_exact(placing_f32.T, vec_grad)
    bias_request = dot_exact(placing_f32.T, bias_vec_grad[:, None])[:, 0]
    back_block = jnp.concatenate(
        [
            per_request.reshape(devices, capacity, emb_width).astype(jnp.bfloat16),
            jnp.broadcast_to(
                bias_request.reshape(devices, capacity, 1).astype(jnp.bfloat16),
                (devices, capacity, 128),
            ),
        ],
        axis=2,
    )
    back_block = direct_swap(jnp.pad(back_block, ((0, 0), (0, cap_room), (0, 0))), 5)
    back_rows = back_block[:, :capacity, :emb_width].astype(jnp.float32)
    back_bias = back_block[:, :capacity, emb_width].astype(jnp.float32)
    flat_ids = asked_ids.reshape(devices * capacity)
    table_grad = table_grad + jax.ops.segment_sum(
        back_rows.reshape(devices * capacity, emb_width), flat_ids, num_segments=table_rows
    )
    bias_grad = bias_grad + jax.ops.segment_sum(
        back_bias.reshape(devices * capacity), flat_ids, num_segments=table_rows
    )
    vectors = [
        head_gain_grad,
        head_bias_grad,
        norm2_gain_grad,
        norm2_bias_grad,
        norm1_gain_grad,
        norm1_bias_grad,
    ]
    cuts = [vector.reshape(devices, -1) for vector in vectors]
    spots = [0]
    for cut in cuts:
        spots.append(spots[-1] + cut.shape[1])
    block = jnp.concatenate(cuts, axis=1)
    block = jnp.pad(block, ((0, 0), (0, 128 - spots[-1])))[:, None, :]
    vector_sums = jnp.sum(direct_swap(jnp.pad(block, ((0, 0), (0, 7), (0, 0))), 6)[:, 0], axis=0)
    vector_out = [vector_sums[spots[i] : spots[i + 1]] for i in range(len(cuts))]
    sums = sum_all(
        [
            [up_weight_grad, out_weight_grad, head_weight_grad],
            [down_grad, query_ww_grad, dense_grad],
            [query_we_grad, query_ew_grad, query_ee_grad, key_weight_grad, value_weight_grad],
        ],
        7,
    )
    all_sums = (
        sums[0][2],
        vector_out[0],
        vector_out[1],
        vector_out[2],
        vector_out[3],
        sums[0][0],
        sums[1][0],
        vector_out[4],
        vector_out[5],
        sums[0][1],
        sums[1][1],
        sums[2][0],
        sums[2][1],
        sums[2][2],
        sums[2][3],
        sums[2][4],
        sums[1][2],
    )
    return (
        loss_value,
        layer_out.astype(jnp.bfloat16),
        words_grad,
        table_grad,
        bias_grad,
        all_sums[16],
        all_sums[10],
        all_sums[11],
        all_sums[12],
        all_sums[13],
        all_sums[14],
        all_sums[15],
        all_sums[9],
        all_sums[7],
        all_sums[8],
        all_sums[5],
        all_sums[6],
        all_sums[3],
        all_sums[4],
        all_sums[0],
        all_sums[1],
        all_sums[2],
        mask_loss,
    )


class Stage:
    def __init__(self, loads, stores):
        self.loads, self.stores, self.waited, self.sent = loads, stores, set(), []

    def need(self, *indices):
        for index in indices:
            if index not in self.waited:
                self.waited.add(index)
                self.loads[index].wait()

    def send(self, *indices):
        for index in indices:
            self.sent.append(index)
            self.stores[index].start()

    def finish(self):
        self.need(*self.loads)
        self.send(*[index for index in self.stores if index not in self.sent])
        for copy in self.stores.values():
            copy.wait()


def staged_kernel(inner, counts, far_in, far_out, *refs):
    ins, outs = list(refs[: counts[0]]), list(refs[counts[0] : sum(counts)])
    rest = list(refs[sum(counts) :])
    out_sem, in_sem = rest.pop(), rest.pop()
    near = rest[len(rest) - len(far_in) - len(far_out) :]
    rest = rest[: len(rest) - len(near)]
    loads, stores = {}, {}
    for slot, index in enumerate(far_in):
        loads[index] = pltpu.make_async_copy(ins[index], near[slot], in_sem.at[slot])
        ins[index] = near[slot]
        loads[index].start()
    for slot, index in enumerate(far_out):
        close = near[len(far_in) + slot]
        stores[index] = pltpu.make_async_copy(close, outs[index], out_sem.at[slot])
        outs[index] = close
    stage = Stage(loads, stores)
    inner(stage, *ins, *outs, *rest)
    stage.finish()


def staged_call(inner, inputs, outs, in_specs, out_specs, far_in, far_out, scratch, params):
    hbm = pl.BlockSpec(memory_space=pltpu.HBM)
    in_specs, out_specs = list(in_specs), list(out_specs)
    extra = []
    for index in far_in:
        in_specs[index] = hbm
        extra.append(pltpu.VMEM(inputs[index].shape, inputs[index].dtype))
    for index in far_out:
        out_specs[index] = hbm
        extra.append(pltpu.VMEM(outs[index].shape, outs[index].dtype))
    return pl.pallas_call(
        functools.partial(staged_kernel, inner, (len(inputs), len(outs)), far_in, far_out),
        out_shape=outs,
        in_specs=in_specs,
        out_specs=out_specs,
        scratch_shapes=list(scratch)
        + extra
        + [
            pltpu.SemaphoreType.DMA((max(1, len(far_in)),)),
            pltpu.SemaphoreType.DMA((max(1, len(far_out)),)),
        ],
        compiler_params=params,
    )(*inputs)


def all_pairs(source, target, sems, me, devices):
    def piece(step):
        peer = lax.rem(me + step, devices)
        return pltpu.make_async_remote_copy(
            src_ref=source.at[peer],
            dst_ref=target.at[me],
            send_sem=sems.at[0, step],
            recv_sem=sems.at[1, step],
            device_id=(peer,),
            device_id_type=MESH_ID,
        )

    def begin(step, carry):
        piece(step).start()
        return carry

    def finish(step, carry):
        piece(step).wait()
        return carry

    lax.fori_loop(1, devices, begin, 0)
    target[me] = source[me]
    return lambda: lax.fori_loop(1, devices, finish, 0)


def lookup_kernel(
    stage,
    codes,
    table,
    bias,
    slot_row,
    word_states,
    w_ww,
    w_we,
    w_key,
    w_value,
    word_seg,
    entity_seg,
    entity_out,
    vec_out,
    bias_out,
    code_out,
    qword,
    qent,
    keys,
    values,
    feat_q,
    feat_k,
    codes_in,
    found,
    rows_in,
    bias_col,
    sems,
):
    devices, room, _ = codes.shape
    me = lax.axis_index("dp")
    rows, wide = table.shape
    entries = devices * room
    greet_all(me, devices)
    ended = all_pairs(codes, codes_in, sems.at[0], me, devices)
    width = word_states.shape[1]
    half = width // 2
    query_scale = HD ** (-0.5)

    def project(target, weight, scale):
        for cut in range(0, width, half):
            value = dot_plain(word_states[...], weight[:, cut : cut + half])
            if scale:
                value = value * query_scale
            target[:, cut : cut + half] = value.astype(jnp.bfloat16)

    def bias_step(index, carry):
        at = pl.ds(pl.multiple_of(index * 128, 128), 128)
        bias_col[at] = jnp.broadcast_to(bias[:, at], (128, 128)).T.astype(jnp.bfloat16)
        return carry

    lax.fori_loop(0, rows // 128, bias_step, 0)
    words = word_seg.shape[1]
    column = lax.rem(lax.broadcasted_iota(jnp.int32, (128, 128), 1), HD)
    for begin in range(0, words + entity_seg.shape[1], 128):
        seg = word_seg[:, begin : begin + 128] if begin < words else entity_seg[...]
        turned = jnp.broadcast_to(seg.astype(jnp.float32), (128, 128)).T
        same = turned == column.astype(jnp.float32)
        at = slice(begin, begin + 128)
        feat_q[at] = same.astype(jnp.float32).astype(jnp.bfloat16)
        feat_k[at] = jnp.where(same | (column >= 4), 0.0, MASKED).astype(jnp.bfloat16)
    stage.need(4, 5)
    project(qword, w_ww, True)
    stage.send(4)
    stage.need(1)
    ended()
    code = codes_in[...].reshape(entries, 128)
    for begin in range(0, entries, 128):
        turned = code[begin : begin + 128].astype(jnp.float32).T
        code_out[:, begin : begin + 128] = turned[0:8].astype(jnp.int32)
    code = jnp.where(code >= rows, code - rows, code)
    lane = lax.broadcasted_iota(jnp.int32, (entries, 128), 1)
    total = jnp.zeros((entries, wide), jnp.float32)
    shift = jnp.zeros((entries, 128), jnp.float32)
    step = 512
    for begin in range(0, rows, step):
        size = min(step, rows - begin)
        match = jnp.concatenate(
            [
                (code - (begin + inner) == lane).astype(jnp.float32)
                for inner in range(0, size, 128)
            ],
            axis=1,
        ).astype(jnp.bfloat16)
        total += dot_plain(match, table[begin : begin + size])
        shift += dot_plain(match, bias_col[begin : begin + size])
    both = jnp.concatenate([total, shift], axis=1).astype(jnp.bfloat16)
    found[...] = both.reshape(found.shape)
    ended = all_pairs(found, rows_in, sems.at[1], me, devices)
    stage.need(6)
    project(qent, w_we, True)
    stage.send(5)
    stage.need(7)
    project(keys, w_key, False)
    stage.send(6)
    stage.need(8)
    project(values, w_value, False)
    stage.send(7)
    ended()
    slots, masked = entity_out.shape[0], vec_out.shape[0]
    wanted = lax.broadcasted_iota(jnp.int32, (slots + masked, entries), 0)
    placing = (wanted == slot_row[0:1]).astype(jnp.float32).astype(jnp.bfloat16)
    placed = dot_plain(placing, rows_in[...].reshape(entries, wide + 128))
    entity_out[...] = placed[:slots, :wide].astype(jnp.bfloat16)
    vec_out[...] = placed[slots:, :wide]
    bias_out[...] = placed[slots:, wide:]


def lookup(inputs, slots, masked, collective_id):
    devices, room, _ = inputs[0].shape
    rows, wide = inputs[1].shape
    words, width = inputs[4].shape
    entries = devices * room
    low = jnp.bfloat16
    vmem = pl.BlockSpec(memory_space=pltpu.VMEM)
    outs = [
        jax.ShapeDtypeStruct((slots, wide), low),
        jax.ShapeDtypeStruct((masked, wide), jnp.float32),
        jax.ShapeDtypeStruct((masked, 128), jnp.float32),
        jax.ShapeDtypeStruct((8, entries), jnp.int32),
    ]
    outs += [jax.ShapeDtypeStruct((words, width), low)] * 4
    outs += [jax.ShapeDtypeStruct((words + slots, 128), low)] * 2
    return staged_call(
        lookup_kernel,
        inputs,
        outs,
        [vmem] * len(inputs),
        [vmem] * len(outs),
        (4, 5, 1, 6, 7, 8),
        (4, 5, 6, 7),
        [
            pltpu.VMEM(inputs[0].shape, jnp.int32),
            pltpu.VMEM((devices, room, wide + 128), low),
            pltpu.VMEM((devices, room, wide + 128), low),
            pltpu.VMEM((rows, 128), low),
            pltpu.SemaphoreType.DMA((2, 2, devices)),
        ],
        pltpu.CompilerParams(
            collective_id=collective_id, has_side_effects=True, vmem_limit_bytes=63 * 2**20
        ),
    )


def norm_parts(value):
    center = value - jnp.mean(value, axis=-1, keepdims=True)
    spread = jnp.mean(center * center, axis=-1, keepdims=True)
    rate = lax.rsqrt(spread + EPSILON)
    return center * rate, rate


def gelu_parts(value):
    chance = 0.5 + 0.5 * lax.erf(value * (0.5**0.5))
    slope = chance + value * (jnp.exp(-0.5 * value * value) * (0.5 / jnp.pi) ** 0.5)
    return value * chance, slope


def half_lanes(block):
    lane = lax.broadcasted_iota(jnp.int32, (1, block), 1)
    low_half = (lane < HD).astype(jnp.float32).astype(jnp.bfloat16)
    high_half = (lane >= HD).astype(jnp.float32).astype(jnp.bfloat16)
    return low_half, high_half


def forward_kernel(
    stage,
    word_states,
    entity_low,
    feat_q,
    feat_k,
    choose,
    dense,
    word_q,
    word_e,
    word_k,
    word_v,
    w_ew,
    w_ee,
    w_key,
    w_value,
    out_hbm,
    gain_one,
    shift_one,
    up_hbm,
    down_hbm,
    gain_two,
    shift_two,
    head_w,
    gain_head,
    shift_head,
    hidden,
    qword,
    qent,
    keys,
    values,
    context,
    lse_out,
    resid_one,
    normed_out,
    active_hbm,
    slope_hbm,
    resid_two,
    layer_low,
    picked_out,
    head_pre_out,
    head_out,
    state_scr,
    normed_scr,
    out_w,
    up_w,
    down_w,
    active,
    slope,
    sems,
):
    loads = [
        pltpu.make_async_copy(source, target, sems.at[index])
        for index, (source, target) in enumerate(
            ((out_hbm, out_w), (up_hbm, up_w), (down_hbm, down_w))
        )
    ]
    words, width = word_states.shape
    word_loads = [
        pltpu.make_async_copy(source, target.at[pl.ds(0, words)], sems.at[12 + index])
        for index, (source, target) in enumerate(
            ((word_q, qword), (word_e, qent), (word_k, keys), (word_v, values))
        )
    ]
    for load in word_loads + loads:
        load.start()
    stage.need(0, 1, 5)
    seq_len = hidden.shape[0]
    slots = seq_len - words
    block = 128
    halves = half_lanes(block)
    query_scale = HD ** (-0.5)
    state_scr[...] = dot_plain(entity_low[...], dense[...])
    hidden[:words] = word_states[...]
    hidden[words:] = state_scr[...].astype(jnp.bfloat16)

    stage.send(0)
    ents = hidden[words:]
    stage.need(10, 11, 12, 13)
    for target, weight, scale in (
        (qword, w_ew, query_scale),
        (qent, w_ee, query_scale),
        (keys, w_key, None),
        (values, w_value, None),
    ):
        value = dot_plain(ents, weight[...])
        if scale is not None:
            value = value * scale
        target[words:] = value.astype(jnp.bfloat16)
    for load in word_loads:
        load.wait()
    stage.send(1, 2, 3, 4)
    stage.need(2, 3)
    lse_out[...] = jnp.zeros_like(lse_out)

    def pair_step(pair, carry):
        lanes = pl.ds(pl.multiple_of(pair * block, block), block)
        key_pair = keys[:, lanes]
        value_pair = values[:, lanes]
        key_feat = [key_pair * halves[h] + feat_k[...] * halves[1 - h] for h in range(2)]
        value_only = [value_pair * halves[h] for h in range(2)]
        spot = lax.broadcasted_iota(jnp.int32, (1, block), 1) - 4 * pair

        def row_step(index, inner):
            at = pl.ds(pl.multiple_of(index * block, block), block)
            qw = qword[at, lanes]
            qe = qent[at, lanes]
            feats = feat_q[at]
            result = jnp.zeros((block, block), jnp.float32)
            stats = lse_out[at]
            for h in range(2):
                left_w = qw * halves[h] + feats * halves[1 - h]
                left_e = qe * halves[h] + feats * halves[1 - h]
                scores = jnp.concatenate(
                    [
                        dot_right_t(left_w, key_feat[h][:words]),
                        dot_right_t(left_e, key_feat[h][words:]),
                    ],
                    axis=1,
                )
                top = jnp.max(scores, axis=1, keepdims=True)
                expo = jnp.exp(scores - top)
                total = jnp.sum(expo, axis=1, keepdims=True)
                prob = (expo * (1.0 / total)).astype(jnp.bfloat16)
                result += dot_plain(prob, value_only[h])
                stats = jnp.where(spot == h, top + jnp.log(total), stats)
            context[at, lanes] = result.astype(jnp.bfloat16)
            lse_out[at] = stats
            return inner

        lax.fori_loop(0, seq_len // block, row_step, 0)
        return carry

    lax.fori_loop(0, width // block, pair_step, 0)

    stage.send(5)
    loads[0].wait()
    for begin, size in ((0, words // 2), (words // 2, words // 2), (words, slots)):
        at = slice(begin, begin + size)
        start = (
            state_scr[...] if begin == words else word_states[at].astype(jnp.float32)
        )
        value = start + dot_plain(context[at], out_w[...])
        resid_one[at] = value
        normed = norm_parts(value)[0] * gain_one[...][None, :] + shift_one[...][None, :]
        normed_scr[at] = normed
        normed_out[at] = normed.astype(jnp.bfloat16)
    stage.send(7, 8)
    loads[1].wait()
    loads[2].wait()
    span = seq_len // 4
    stores = []

    for slot in range(down_w.shape[0] // width):
        cols = slice(slot * width, slot * width + width)

        def up_step(index, carry, cols=cols):
            at = pl.ds(pl.multiple_of(index * span, 16), span)
            result, change = gelu_parts(dot_plain(normed_out[at], up_w[:, cols]))
            active[at, cols] = result.astype(jnp.bfloat16)
            slope[at, cols] = change.astype(jnp.bfloat16)
            return carry

        lax.fori_loop(0, 4, up_step, 0)
        for index, (source, target) in enumerate(((active, active_hbm), (slope, slope_hbm))):
            stores.append(
                pltpu.make_async_copy(
                    source.at[:, cols], target.at[:, cols], sems.at[3 + 2 * slot + index]
                )
            )
            stores[-1].start()

    def down_step(index, carry):
        at = pl.ds(pl.multiple_of(index * span, 16), span)
        value = normed_scr[at] + dot_plain(active[at], down_w[...])
        resid_two[at] = value
        layer_low[at] = (norm_parts(value)[0] * gain_two[...][None, :] + shift_two[...][None, :]).astype(jnp.bfloat16)
        return carry

    lax.fori_loop(0, 4, down_step, 0)
    stage.send(11, 12)
    stage.need(21)
    picked = dot_plain(choose[...], layer_low[words:]).astype(jnp.bfloat16)
    picked_out[...] = picked
    head_pre = dot_plain(picked, head_w[...])
    head_pre_out[...] = head_pre
    raised = gelu_parts(head_pre)[0]
    head_out[...] = (norm_parts(raised)[0] * gain_head[...][None, :] + shift_head[...][None, :]).astype(jnp.bfloat16)
    for store in stores:
        store.wait()


def forward_pass(inputs):
    words, width = inputs[0].shape
    slots = inputs[1].shape[0]
    seq_len = words + slots
    hidden_units = inputs[17].shape[1]
    mask_count = inputs[4].shape[0]
    head_width = inputs[21].shape[1]
    low, full = jnp.bfloat16, jnp.float32
    vmem, hbm = pl.BlockSpec(memory_space=pltpu.VMEM), pl.BlockSpec(memory_space=pltpu.HBM)
    far = (6, 7, 8, 9, 14, 17, 18)
    shapes = [
        ((seq_len, width), low),
        ((seq_len, width), low),
        ((seq_len, width), low),
        ((seq_len, width), low),
        ((seq_len, width), low),
        ((seq_len, width), low),
        ((seq_len, 128), full),
        ((seq_len, width), full),
        ((seq_len, width), low),
        ((seq_len, hidden_units), low),
        ((seq_len, hidden_units), low),
        ((seq_len, width), full),
        ((seq_len, width), low),
        ((mask_count, width), low),
        ((mask_count, head_width), full),
        ((mask_count, head_width), low),
    ]
    outs = [jax.ShapeDtypeStruct(*shape) for shape in shapes]
    return staged_call(
        forward_kernel,
        inputs,
        outs,
        [hbm if index in far else vmem for index in range(len(inputs))],
        [hbm if index in (9, 10) else vmem for index in range(len(shapes))],
        (0, 1, 5, 10, 11, 12, 13, 2, 3, 21),
        (0, 1, 2, 3, 4, 5, 7, 8, 11, 12),
        [
            pltpu.VMEM((slots, width), full),
            pltpu.VMEM((seq_len, width), full),
            pltpu.VMEM(inputs[14].shape, low),
            pltpu.VMEM(inputs[17].shape, low),
            pltpu.VMEM(inputs[18].shape, low),
            pltpu.VMEM((seq_len, hidden_units), low),
            pltpu.VMEM((seq_len, hidden_units), low),
            pltpu.SemaphoreType.DMA((16,)),
        ],
        pltpu.CompilerParams(vmem_limit_bytes=63 * 2**20),
    )


class Grid:
    def __init__(self):
        me = lax.axis_index("dp")
        self.core = lax.rem(me, 2)
        self.square = lax.rem(lax.div(me, 2), 4)
        self.line = lax.div(me, 8)
        self.twin = me + 1 - 2 * self.core
        self.squares = []
        self.lines = []
        for step in range(1, 4):
            other = lax.rem(self.square + step, 4)
            self.squares.append((me + 2 * (other - self.square), other))
            other = lax.rem(self.line + step, 4)
            self.lines.append((me + 8 * (other - self.line), other))

    def greet(self):
        barrier = pltpu.get_barrier_semaphore()
        peers = [self.twin] + [peer for peer, _ in self.squares + self.lines]
        for peer in peers:
            pl.semaphore_signal(barrier, inc=1, device_id=(peer,), device_id_type=MESH_ID)
        pl.semaphore_wait(barrier, len(peers))


class Sender:
    def __init__(self, send_sem, recv_sem):
        self.send_sem, self.recv_sem, self.used = send_sem, recv_sem, 0

    def start(self, source, target, peer):
        slot = self.used
        self.used += 1
        copy = pltpu.make_async_remote_copy(
            src_ref=source,
            dst_ref=target,
            send_sem=self.send_sem.at[slot],
            recv_sem=self.recv_sem.at[slot],
            device_id=(peer,),
            device_id_type=MESH_ID,
        )
        copy.start()
        return copy


def wait_all(copies):
    for copy in copies:
        copy.wait()


def merge_stats(blocks):
    tops = [block[0] for block in blocks]
    top = functools.reduce(jnp.maximum, tops)
    total = sum(block[1] * jnp.exp(block[0] - top) for block in blocks)
    return top, total, sum(block[2] for block in blocks)


def head_kernel(
    grad_scale,
    head,
    table,
    bias,
    target_vecs,
    target_bias,
    table_grad,
    bias_grad,
    losses,
    total_loss,
    head_grad,
    heads,
    logits,
    expo,
    table_t,
    bias_col,
    part,
    land_pair,
    sum_pair,
    land_square,
    sum_square,
    land_line,
    stat,
    stat_pair,
    stat_square,
    stat_line,
    send_sem,
    recv_sem,
):
    grid = Grid()
    rows, wide = table.shape
    count = head.shape[0]
    total_mask = 32 * count
    grid.greet()
    sender = Sender(send_sem, recv_sem)
    line, square, core = grid.line, grid.square, grid.core
    flying = [sender.start(head, heads.at[line, square, core], peer) for peer, _ in grid.lines]
    heads[line, square, core] = head[...]

    def table_step(index, carry):
        at = pl.ds(pl.multiple_of(index * 128, 128), 128)
        table_t[:, at] = table[at].astype(jnp.float32).T.astype(jnp.bfloat16)
        return carry

    lax.fori_loop(0, rows // 128, table_step, 0)
    wait_all(flying)
    flying = [
        sender.start(heads.at[:, square, core], heads.at[:, square, core], peer)
        for peer, _ in grid.squares
    ]

    def bias_step(index, carry):
        at = pl.ds(pl.multiple_of(index * 128, 128), 128)
        bias_col[at] = jnp.broadcast_to(bias[:, at], (128, 128)).T
        return carry

    lax.fori_loop(0, rows // 128, bias_step, 0)
    wait_all(flying)
    sender.start(heads.at[:, :, core], heads.at[:, :, core], grid.twin).wait()

    all_heads = heads[...].reshape(total_mask, wide)
    slab = rows // 8

    def logit_step(index, carry):
        at = pl.ds(pl.multiple_of(index * slab, 16), slab)
        logits[at] = dot_right_t(table[at], all_heads)
        return carry

    lax.fori_loop(0, 8, logit_step, 0)
    tile = 64
    wide_copies = total_mask // 128

    def value_at(index):
        at = pl.ds(pl.multiple_of(index * tile, tile), tile)
        shift = bias_col[at]
        return at, logits[at] + jnp.concatenate([shift] * wide_copies, axis=1)

    def top_step(index, top):
        at, value = value_at(index)
        return jnp.maximum(top, jnp.max(value.reshape(tile // 8, 8, total_mask), axis=0))

    top = lax.fori_loop(
        0, rows // tile, top_step, jnp.full((8, total_mask), -jnp.inf, jnp.float32)
    )
    top = jnp.max(top, axis=0, keepdims=True)

    def exp_step(index, total):
        at, value = value_at(index)
        value = jnp.exp(value - top)
        expo[at] = value.astype(jnp.bfloat16)
        return total + jnp.sum(value.reshape(tile // 8, 8, total_mask), axis=0)

    total = lax.fori_loop(0, rows // tile, exp_step, jnp.zeros((8, total_mask), jnp.float32))
    total = jnp.sum(total, axis=0, keepdims=True)

    def fold(row):
        return jnp.concatenate([row[:, i * 128 : i * 128 + 128] for i in range(wide_copies)], axis=0)

    def unfold(block):
        return jnp.concatenate([block[i : i + 1] for i in range(wide_copies)], axis=1)

    own_top, own_total = fold(top), fold(total)
    target = (
        jnp.sum(head[...].astype(jnp.float32) * target_vecs[...], axis=1, keepdims=True)
        + target_bias[:, 0:1]
    )
    own_target = jnp.broadcast_to(jnp.sum(target, axis=0, keepdims=True), own_top.shape)
    stat[0, 0], stat[0, 1], stat[0, 2] = own_top, own_total, own_target
    copy = sender.start(stat.at[0], stat_pair, grid.twin)
    quarter = total_mask // 4
    parts = [dot_plain(table_t[...], expo[:, :quarter])]
    copy.wait()
    stat[1, 0], stat[1, 1], stat[1, 2] = merge_stats(
        [(own_top, own_total, own_target), (stat_pair[0], stat_pair[1], stat_pair[2])]
    )
    stat_square[square] = stat[1]
    flying = [sender.start(stat.at[1], stat_square.at[square], peer) for peer, _ in grid.squares]
    parts.append(dot_plain(table_t[...], expo[:, quarter : 2 * quarter]))
    wait_all(flying)
    stat[2, 0], stat[2, 1], stat[2, 2] = merge_stats(
        [(stat_square[i, 0], stat_square[i, 1], stat_square[i, 2]) for i in range(4)]
    )
    stat_line[line] = stat[2]
    flying = [sender.start(stat.at[2], stat_line.at[line], peer) for peer, _ in grid.lines]
    parts.append(dot_plain(table_t[...], expo[:, 2 * quarter : 3 * quarter]))
    parts.append(dot_plain(table_t[...], expo[:, 3 * quarter :]))
    wait_all(flying)
    full_top, full_total, full_target = merge_stats(
        [(stat_line[i, 0], stat_line[i, 1], stat_line[i, 2]) for i in range(4)]
    )
    lse = full_top + jnp.log(full_total)
    all_lse = jnp.sum(jnp.sum(lse, axis=1, keepdims=True), axis=0, keepdims=True)
    total_loss[...] = (all_lse - full_target[0:1]) * grad_scale
    mine = lax.broadcasted_iota(jnp.int32, (count, total_mask), 0) + lax.axis_index("dp") * count
    hit = mine == lax.broadcasted_iota(jnp.int32, (count, total_mask), 1)
    own_lse = jnp.sum(jnp.where(hit, unfold(lse), 0.0), axis=1, keepdims=True)
    losses[...] = jnp.broadcast_to(own_lse - target, losses.shape)
    scale = unfold(jnp.exp(own_top - lse) * grad_scale)
    per = 128 // count
    for index in range(total_mask // 128):
        at = slice(index * 128, index * 128 + 128)
        source = parts[index * 128 // quarter]
        begin = index * 128 % quarter
        piece = (source[:, begin : begin + 128] * scale[:, at]).T.astype(jnp.bfloat16)
        for inner in range(per):
            owner = index * per + inner
            part[owner // 8, owner // 2 % 4, owner % 2] = piece[inner * count : inner * count + count]
    copy = sender.start(part.at[:, :, 1 - core], land_pair, grid.twin)

    scaled = []
    for index in range(total_mask // 128):
        at = slice(index * 128, index * 128 + 128)
        column = jnp.broadcast_to(scale[:, at], (128, 128)).T
        column = jnp.concatenate([column] * (wide // 128), axis=1)
        scaled.append((all_heads[at].astype(jnp.float32) * column).astype(jnp.bfloat16))
    scaled = jnp.concatenate(scaled, axis=0)
    slab = rows // 4

    def grad_part(index):
        at = slice(index * slab, index * slab + slab)
        table_grad[at] = dot_plain(expo[at], scaled)

    grad_part(0)
    copy.wait()
    sum_pair[...] = (part[:, :, core].astype(jnp.float32) + land_pair[...].astype(jnp.float32)).astype(
        jnp.bfloat16
    )
    flying = [
        sender.start(sum_pair.at[:, other], land_square.at[square], peer)
        for peer, other in grid.squares
    ]
    land_square[square] = sum_pair[:, square]
    grad_part(1)
    wait_all(flying)
    sum_square[...] = sum(land_square[i].astype(jnp.float32) for i in range(4)).astype(jnp.bfloat16)
    flying = [
        sender.start(sum_square.at[other], land_line.at[line], peer) for peer, other in grid.lines
    ]
    land_line[line] = sum_square[line]
    grad_part(2)
    high = scale.astype(jnp.bfloat16)
    low = (scale - high.astype(jnp.float32)).astype(jnp.bfloat16)
    both = jnp.concatenate(
        [high.astype(jnp.float32), low.astype(jnp.float32), jnp.zeros((14, total_mask), jnp.float32)],
        axis=0,
    ).astype(jnp.bfloat16)
    sums = dot_right_t(both, expo[...])
    bias_grad[...] = sums[0:1] + sums[1:2]
    grad_part(3)
    wait_all(flying)
    head_grad[...] = sum(land_line[i].astype(jnp.float32) for i in range(4))


def head_and_table(
    head_low, entity_table, bias_row, target_vecs, target_bias, grad_scale, collective_id
):
    count, wide = head_low.shape
    rows = entity_table.shape[0]
    total_mask = 32 * count
    low, full = jnp.bfloat16, jnp.float32
    vmem = pl.BlockSpec(memory_space=pltpu.VMEM)
    folded = (total_mask // 128, 128)
    return pl.pallas_call(
        functools.partial(head_kernel, grad_scale),
        out_shape=[
            jax.ShapeDtypeStruct((rows, wide), full),
            jax.ShapeDtypeStruct((1, rows), full),
            jax.ShapeDtypeStruct((count, 128), full),
            jax.ShapeDtypeStruct((1, 128), full),
            jax.ShapeDtypeStruct((count, wide), full),
        ],
        in_specs=[vmem] * 5,
        out_specs=[vmem] * 5,
        scratch_shapes=[
            pltpu.VMEM((4, 4, 2, count, wide), low),
            pltpu.VMEM((rows, total_mask), full),
            pltpu.VMEM((rows, total_mask), low),
            pltpu.VMEM((wide, rows), low),
            pltpu.VMEM((rows, 128), full),
            pltpu.VMEM((4, 4, 2, count, wide), low),
            pltpu.VMEM((4, 4, count, wide), low),
            pltpu.VMEM((4, 4, count, wide), low),
            pltpu.VMEM((4, 4, count, wide), low),
            pltpu.VMEM((4, count, wide), low),
            pltpu.VMEM((4, count, wide), low),
            pltpu.VMEM((3, 3) + folded, full),
            pltpu.VMEM((3,) + folded, full),
            pltpu.VMEM((4, 3) + folded, full),
            pltpu.VMEM((4, 3) + folded, full),
            pltpu.SemaphoreType.DMA((24,)),
            pltpu.SemaphoreType.DMA((24,)),
        ],
        compiler_params=pltpu.CompilerParams(
            collective_id=collective_id, has_side_effects=True, vmem_limit_bytes=63 * 2**20
        ),
    )(head_low, entity_table, bias_row, target_vecs, target_bias)


def norm_slope(value, given, gain):
    scaled, rate = norm_parts(value)
    back = given * gain
    mean_back = jnp.mean(back, axis=-1, keepdims=True)
    mean_both = jnp.mean(back * scaled, axis=-1, keepdims=True)
    grad = rate * (back - mean_back - scaled * mean_both)
    return (
        grad,
        jnp.sum(given * scaled, axis=0, keepdims=True),
        jnp.sum(given, axis=0, keepdims=True),
    )


def split_low(value):
    high = value.astype(jnp.bfloat16)
    return high, (value - high.astype(jnp.float32)).astype(jnp.bfloat16)


def place_rows(source, order, count, store):
    owners = 2 ** len(order)
    for pair in range(owners // 2):
        one, two = place_owner(order, 2 * pair), place_owner(order, 2 * pair + 1)
        both = jnp.concatenate(
            [source[one * count : one * count + count], source[two * count : two * count + count]],
            axis=0,
        )
        store(slice(pair * 2 * count, (pair + 1) * 2 * count), both.astype(jnp.bfloat16))


def middle_back_kernel(
    orders,
    grad_scale,
    stage,
    head_grad,
    target_vecs,
    head_pre,
    gain_head,
    picked,
    head_w,
    choose,
    cotangent,
    resid_two,
    gain_two,
    normed_low,
    resid_one,
    gain_one,
    out_w,
    context,
    lse_lanes,
    active_hbm,
    slope_hbm,
    up_hbm,
    down_hbm,
    up_a,
    up_b,
    head_a,
    out_b,
    down_b,
    up_c,
    down_c,
    first_grad,
    context_grad,
    lse_delta,
    vectors,
    active,
    slope,
    up_w,
    down_w,
    flip,
    normed_t,
    context_t,
    down_in,
    acc,
    up_low,
    stage_a,
    stage_c,
    sems,
):
    seq_len, width = cotangent.shape
    slots = choose.shape[1]
    words = seq_len - slots
    cuts = down_w.shape[0] // width
    loads = []
    for index, (source, target) in enumerate(
        ((active_hbm, active), (down_hbm, down_w), (slope_hbm, slope), (up_hbm, up_w))
    ):
        for cut in range(cuts):
            at = pl.ds(cut * width, width)
            view = (at,) if index == 1 else (slice(None), at)
            loads.append(
                pltpu.make_async_copy(source.at[view], target.at[view], sems.at[index * cuts + cut])
            )
    for cut in range(cuts):
        for index in range(4):
            loads[index * cuts + cut].start()

    given = head_grad[...] - grad_scale * target_vecs[...]
    pre = head_pre[...]
    raised, change = gelu_parts(pre)
    back, gain_sum, bias_sum = norm_slope(raised, given, gain_head[...][None, :])
    sums = [gain_sum, bias_sum]
    pre_low = (back * change).astype(jnp.bfloat16)
    head_weight_grad = dot_left_t(picked[...], pre_low)
    count = width // 2 ** len(orders[0])

    def keep_head(at, value):
        head_a[0, at] = value

    flip[:, : head_a.shape[2]] = head_weight_grad
    place_rows(flip[:, : head_a.shape[2]], orders[0], count, keep_head)
    stage.need(5)
    picked_high, picked_rest = split_low(dot_right_t(pre_low, head_w[...]))
    placed = dot_left_t(choose[...], picked_high) + dot_left_t(choose[...], picked_rest)

    stage.need(7, 8)
    block = 128
    total_gain = jnp.zeros((1, width), jnp.float32)
    total_bias = jnp.zeros((1, width), jnp.float32)
    for begin in range(0, seq_len, block):
        at = slice(begin, begin + block)
        given = cotangent[at].astype(jnp.float32)
        if begin >= words:
            given = given + placed[begin - words : begin - words + block]
        grad, gain_sum, bias_sum = norm_slope(resid_two[at], given, gain_two[...][None, :])
        total_gain += gain_sum
        total_bias += bias_sum
        acc[at] = grad
        down_in[at] = grad.astype(jnp.bfloat16)
    sums += [total_gain, total_bias]

    def flip_into(source, target, order_list):
        def flip_step(index, carry):
            at = pl.ds(pl.multiple_of(index * block, block), block)
            flip[at] = source[:, at].astype(jnp.float32).T
            return carry

        lax.fori_loop(0, width // block, flip_step, 0)
        for slot, order in enumerate(order_list):

            def keep(at, value, slot=slot):
                target[slot, at] = value

            place_rows(flip, order, count, keep)

    stage.need(10, 14)
    flip_into(normed_low, normed_t, (orders[0], orders[2]))
    flip_into(context, context_t, (orders[1],))

    column = 384
    split = down_b.shape[2]
    owners = 2 ** len(orders[0])
    tall = down_w.shape[0] // owners
    spots = [
        {place_owner(order, place): place for place in range(owners)}
        for order in (orders[1], orders[2])
    ]
    stores = []
    for cut in range(cuts):
        at = slice(cut * width, cut * width + width)
        for index in range(4):
            loads[index * cuts + cut].wait()
        for begin in range(0, width, column):
            piece = dot_left_t(active[:, at], down_in[:, begin : begin + column])
            for inner in range(width // tall):
                owner = cut * (width // tall) + inner
                rows = piece[inner * tall : inner * tall + tall].astype(jnp.bfloat16)
                stop = min(begin + column, split)
                if begin < split:
                    place = spots[0][owner] * tall
                    stage_a[place : place + tall, begin:stop] = rows[:, : stop - begin]
                if begin + column > split:
                    start = max(begin, split)
                    place = spots[1][owner] * tall
                    stage_c[place : place + tall, start - split : begin + column - split] = rows[
                        :, start - begin :
                    ]

        def back_step(index, carry, at=at):
            span = seq_len // 4
            rows = pl.ds(pl.multiple_of(index * span, 16), span)
            grad = dot_right_t(down_in[rows], down_w[at]) * slope[rows, at].astype(jnp.float32)
            grad = grad.astype(jnp.bfloat16)
            up_low[rows] = grad
            acc[rows] = acc[rows] + dot_right_t(grad, up_w[:, at])
            return carry

        lax.fori_loop(0, 4, back_step, 0)
        target, slot, order_slot = ((up_a, 0, 0), (up_a, 1, 0), (up_b, 0, 0), (up_c, 0, 1))[cut]
        for begin in range(0, width, column):
            target[slot, :, begin : begin + column] = dot_plain(
                normed_t[order_slot], up_low[:, begin : begin + column]
            ).astype(jnp.bfloat16)
    stage.send(0, 1, 5)
    stage.need(11, 13)
    stores = [
        pltpu.make_async_copy(stage_a, down_b.at[0], sems.at[4 * cuts]),
        pltpu.make_async_copy(stage_c, down_c.at[0], sems.at[4 * cuts + 1]),
    ]
    for store in stores:
        store.start()

    total_gain = jnp.zeros((1, width), jnp.float32)
    total_bias = jnp.zeros((1, width), jnp.float32)
    row = lax.broadcasted_iota(jnp.int32, (width, 128), 0)
    lane = lax.broadcasted_iota(jnp.int32, (width, 128), 1)
    spot = 4 * lax.div(row, 128) + 2 + lax.div(lax.rem(row, 128), HD)
    pick = (spot == lane).astype(jnp.float32).astype(jnp.bfloat16)
    for begin in range(0, seq_len, block):
        at = slice(begin, begin + block)
        grad, gain_sum, bias_sum = norm_slope(resid_one[at], acc[at], gain_one[...][None, :])
        total_gain += gain_sum
        total_bias += bias_sum
        first_grad[at] = grad
        low = grad.astype(jnp.bfloat16)
        down_in[at] = low
        back = dot_right_t(low, out_w[...]).astype(jnp.bfloat16)
        context_grad[at] = back
        high, rest = split_low(back.astype(jnp.float32) * context[at].astype(jnp.float32))
        lse_delta[at] = lse_lanes[at] + dot_plain(high, pick) + dot_plain(rest, pick)
    stage.send(7, 8)
    sums += [total_gain, total_bias]
    tall, room = vectors.shape[1:]
    every = tall // owners
    placed = jnp.zeros((tall, room), jnp.float32)
    offset = 0
    for vector in sums:
        size = vector.shape[1]
        per = size // owners
        row = lax.broadcasted_iota(jnp.int32, (tall, size), 0)
        place = lax.div(row, every)
        owner = jnp.zeros((tall, size), jnp.int32)
        for spot, mask in enumerate(orders[0]):
            owner += lax.rem(lax.div(place, 2 ** (len(orders[0]) - 1 - spot)), 2) * mask
        column_at = lax.broadcasted_iota(jnp.int32, (tall, size), 1)
        mine = (lax.div(column_at, per) == owner) & (lax.rem(row, every) == 0)
        spread = jnp.where(mine, vector, 0.0).astype(jnp.bfloat16)
        source = lax.broadcasted_iota(jnp.int32, (size, room), 0)
        target = lax.broadcasted_iota(jnp.int32, (size, room), 1)
        move = (lax.rem(source, per) + offset == target).astype(jnp.float32).astype(jnp.bfloat16)
        placed += dot_plain(spread, move)
        offset += per
    vectors[0] = placed.astype(jnp.bfloat16)
    for begin in range(0, width, column):
        out_b[0, :, begin : begin + column] = dot_plain(
            context_t[0], down_in[:, begin : begin + column]
        ).astype(jnp.bfloat16)
    for store in stores:
        store.wait()


DOWN_SPLIT = 512


def middle_back(inputs, orders, grad_scale):
    seq_len, width = inputs[7].shape
    hidden_units = inputs[16].shape[1]
    head_width = inputs[0].shape[1]
    low, full = jnp.bfloat16, jnp.float32
    cuts = hidden_units // width
    vmem, hbm = pl.BlockSpec(memory_space=pltpu.VMEM), pl.BlockSpec(memory_space=pltpu.HBM)
    shapes = [
        ((2, width, width), low),
        ((1, width, width), low),
        ((1, width, head_width), low),
        ((1, width, width), low),
        ((1, hidden_units, DOWN_SPLIT), low),
        ((1, width, width), low),
        ((1, hidden_units, width - DOWN_SPLIT), low),
        ((seq_len, width), full),
        ((seq_len, width), low),
        ((seq_len, 128), full),
        ((1, 8 * 2 ** len(orders[0]), 256), low),
    ]
    outs = [jax.ShapeDtypeStruct(*shape) for shape in shapes]
    return staged_call(
        functools.partial(middle_back_kernel, orders, grad_scale),
        inputs,
        outs,
        [vmem] * 16 + [hbm] * 4,
        [hbm if index in (4, 6) else vmem for index in range(len(shapes))],
        (5, 7, 8, 10, 14, 11, 13),
        (0, 1, 3, 5, 7, 8),
        [
            pltpu.VMEM((seq_len, hidden_units), low),
            pltpu.VMEM((seq_len, hidden_units), low),
            pltpu.VMEM((width, hidden_units), low),
            pltpu.VMEM((hidden_units, width), low),
            pltpu.VMEM((width, seq_len), full),
            pltpu.VMEM((2, width, seq_len), low),
            pltpu.VMEM((1, width, seq_len), low),
            pltpu.VMEM((seq_len, width), low),
            pltpu.VMEM((seq_len, width), full),
            pltpu.VMEM((seq_len, width), low),
            pltpu.VMEM((hidden_units, DOWN_SPLIT), low),
            pltpu.VMEM((hidden_units, width - DOWN_SPLIT), low),
            pltpu.SemaphoreType.DMA((4 * cuts + 2,)),
        ],
        pltpu.CompilerParams(vmem_limit_bytes=63 * 2**20),
    )


def last_kernel(grad_scale, codes, back, table_hbm, bias_in, *refs):
    sums, refs = refs[:SUMS], refs[SUMS:]
    table_out, bias_out = refs[:2]
    outs, refs = refs[2 : 2 + SUMS - 3], refs[2 + SUMS - 3 :]
    table_in, result, sems, move_sems = refs
    rows = table_hbm.shape[0]
    entries = back.shape[0]
    step = 1024
    parts = [(begin, min(step, rows - begin)) for begin in range(0, rows, step)]
    loads = [
        pltpu.make_async_copy(
            table_hbm.at[pl.ds(begin, size)], table_in.at[pl.ds(begin, size)], sems.at[0, index]
        )
        for index, (begin, size) in enumerate(parts)
    ]
    stores = [
        pltpu.make_async_copy(
            result.at[pl.ds(begin, size)], table_out.at[pl.ds(begin, size)], sems.at[1, index]
        )
        for index, (begin, size) in enumerate(parts)
    ]
    for load in loads:
        load.start()
    up_two, down_a, up_last, down_b, up_third = sums[:5]
    up_out, down_out = outs[:2]
    width = up_last.shape[2]
    pairs = [
        (value, up_out.at[:, pl.ds(index * width, width)])
        for index, value in enumerate((up_two.at[0], up_two.at[1], up_third.at[0], up_last.at[0]))
    ]
    pairs.append((down_a.at[0], down_out.at[:, pl.ds(0, down_a.shape[2])]))
    pairs.append((down_b.at[0], down_out.at[:, pl.ds(down_a.shape[2], down_b.shape[2])]))
    pairs += [(source.at[0], target) for source, target in zip(sums[5:], outs[2:])]
    moves = [
        pltpu.make_async_copy(source, target, move_sems.at[index])
        for index, (source, target) in enumerate(pairs)
    ]
    for move in moves:
        move.start()
    code = codes[0:1]
    target = (code >= rows).astype(jnp.float32)
    flags = jnp.broadcast_to(target, (16, entries)).astype(jnp.bfloat16)
    code = jnp.where(code >= rows, code - rows, code)
    for index, (begin, size) in enumerate(parts):
        row = lax.broadcasted_iota(jnp.int32, (size, entries), 0) + begin
        match = (row == code).astype(jnp.float32).astype(jnp.bfloat16)
        at = slice(begin, begin + size)
        counts = dot_right_t(flags, match)
        bias_out[:, at] = bias_in[:, at] - grad_scale * counts[0:1]
        added = dot_plain(match, back[...])
        loads[index].wait()
        result[at] = table_in[at] + added
        stores[index].start()
    for copy in stores + moves:
        copy.wait()


SUMS = 15


def last_step(codes, back, table_grad, bias_grad, sums, grad_scale):
    vmem, hbm = pl.BlockSpec(memory_space=pltpu.VMEM), pl.BlockSpec(memory_space=pltpu.HBM)
    full = jnp.float32
    up_rows, width = sums[0].shape[1:]
    down_rows = sums[1].shape[1]
    shapes = [
        table_grad.shape,
        bias_grad.shape,
        (up_rows, 4 * width),
        (down_rows, width),
    ] + [value.shape[1:] for value in sums[5:]]
    return pl.pallas_call(
        functools.partial(last_kernel, grad_scale),
        out_shape=[jax.ShapeDtypeStruct(shape, full) for shape in shapes],
        in_specs=[vmem, vmem, hbm, vmem] + [vmem] * len(sums),
        out_specs=[hbm, vmem] + [hbm] * (len(shapes) - 2),
        scratch_shapes=[
            pltpu.VMEM(table_grad.shape, full),
            pltpu.VMEM(table_grad.shape, full),
            pltpu.SemaphoreType.DMA((2, 8)),
            pltpu.SemaphoreType.DMA((len(sums) + 1,)),
        ],
        compiler_params=pltpu.CompilerParams(vmem_limit_bytes=63 * 2**20),
    )(codes, back, table_grad, bias_grad, *sums)


def place_owner(order, place):
    bits = len(order)
    return sum(((place >> (bits - 1 - spot)) & 1) * mask for spot, mask in enumerate(order))


class Piece:
    def __init__(
        self, rows, stages, send, own, land, tail, pack, tail_land, out, send_sem, recv_sem
    ):
        self.rows, self.stages = rows, stages
        self.send, self.own, self.land = send, own, land
        self.tail, self.pack, self.tail_land, self.out = tail, pack, tail_land, out
        self.send_sem, self.recv_sem = send_sem, recv_sem
        self.sizes = [rows * 2 ** (stages - 1 - stage) for stage in range(stages)]
        self.spots = [sum(self.sizes[:stage]) for stage in range(stages)]

    def copy(self, stage, partner, bit):
        size = self.sizes[stage]
        away = (1 - bit) * size
        if stage < self.stages - 1:
            away = pl.multiple_of(away, 16)
        if stage == 0:
            source, target = self.send.at[:, pl.ds(away, size)], self.land.at[:, pl.ds(0, size)]
        elif stage < self.stages - 1:
            spot = pl.multiple_of(self.spots[stage - 1] + away, 16)
            source = self.land.at[:, pl.ds(spot, size)]
            target = self.land.at[:, pl.ds(self.spots[stage], size)]
        else:
            source, target = self.pack, self.tail_land
        return pltpu.make_async_remote_copy(
            src_ref=source,
            dst_ref=target,
            send_sem=self.send_sem.at[stage],
            recv_sem=self.recv_sem.at[stage],
            device_id=(partner,),
            device_id_type=MESH_ID,
        )

    def held(self, stage, bit):
        size = self.sizes[stage]
        if stage == 0 and self.own is not None:
            return self.own, 0
        if stage == 0:
            return self.send, pl.multiple_of(bit * size, 16)
        return self.land, pl.multiple_of(self.spots[stage - 1] + bit * size, 16)

    def add(self, stage, bit, half_index):
        size = self.sizes[stage]
        half = size // 2
        unit = 48 if half % 48 == 0 else 16
        start = half_index * half
        source, base = self.held(stage, bit)
        for slot in range(self.land.shape[0]):

            def step(index, carry, slot=slot):
                row = pl.multiple_of(start + index * unit, 16)
                mine = source[slot, pl.ds(pl.multiple_of(base + row, 16), unit)]
                spot = pl.ds(pl.multiple_of(self.spots[stage] + row, 16), unit)
                theirs = self.land[slot, spot]
                total = mine.astype(jnp.float32) + theirs.astype(jnp.float32)
                self.land[slot, spot] = total.astype(jnp.bfloat16)
                return carry

            lax.fori_loop(0, half // unit, step, 0)

    def add_tail(self, stage, bit, following):
        size = self.sizes[stage]
        half = size // 2
        middle = self.land.shape[2] // 2
        source, base = self.held(stage, bit)
        for slot in range(self.land.shape[0]):
            mine = source[slot, pl.ds(base, size)]
            theirs = self.land[slot, pl.ds(self.spots[stage], size)]
            self.tail[slot] = mine.astype(jnp.float32) + theirs.astype(jnp.float32)
            other = self.tail[slot, pl.ds(pl.multiple_of((1 - following) * half, 8), half)]
            self.pack[slot] = jnp.concatenate(
                [other[:, :middle], other[:, middle:]], axis=0
            ).astype(jnp.bfloat16)

    def finish(self, bit):
        size = self.sizes[-1]
        for slot in range(self.out.shape[0]):
            mine = self.tail[slot, pl.ds(pl.multiple_of(bit * size, 8), size)]
            theirs = self.tail_land[slot].astype(jnp.float32)
            self.out[slot] = mine + jnp.concatenate([theirs[:size], theirs[size:]], axis=1)


class Stream:
    def __init__(self, order, partner_of, pieces):
        self.order, self.partner_of, self.pieces = order, partner_of, pieces
        self.stages = len(order)

    def launch(self, stage):
        partner, bit = self.partner_of[self.order[stage]]
        for piece in self.pieces:
            piece.copy(stage, partner, bit).start()

    def advance(self, stage):
        partner, bit = self.partner_of[self.order[stage]]
        for piece in self.pieces:
            piece.copy(stage, partner, bit).wait()
        if stage == self.stages - 1:
            for piece in self.pieces:
                piece.finish(bit)
        elif stage == self.stages - 2:
            for piece in self.pieces:
                piece.add_tail(stage, bit, self.partner_of[self.order[stage + 1]][1])
            self.launch(stage + 1)
        else:
            following = self.partner_of[self.order[stage + 1]][1]
            for piece in self.pieces:
                piece.add(stage, bit, 1 - following)
            self.launch(stage + 1)
            for piece in self.pieces:
                piece.add(stage, bit, following)


def partners(me, masks):
    result = {}
    for mask in masks:
        bit = lax.rem(lax.div(me, mask), 2)
        result[mask] = (me + mask - 2 * mask * bit, bit)
    return result


EARLY = (
    (0, 2, 24, 768),
    (1, 1, 96, 512),
    (2, 1, 24, 768),
    (3, 1, 96, 256),
    (4, 1, 24, 768),
    (4, 1, 24, 256),
    (4, 1, 8, 256),
    (5, 1, 24, 768),
)
LATE = (
    (6, 1, 24, 768),
    (7, 1, 24, 768),
    (8, 1, 24, 768),
    (9, 1, 24, 768),
    (10, 1, 24, 768),
    (11, 1, 24, 768),
    (11, 1, 8, 768),
)
STREAM_ORDER = (0, 1, 2, 2, 0, 1, 1, 1, 2, 1, 0, 0)

WORD_POINTS = ("word0", "word1", "word2", "word3")

PLAN = {('p', 0): ((0, 0),), ('r', 1): ((1, 0), (2, 0)), ('p', 1): ((3, 0),), ('r', 2): ((4, 0), (5, 0)), ('r', 3): ((2, 1), (0, 1)), ('p', 4): ((3, 1),), ('r', 5): ((1, 1), (4, 1), (2, 2)), 'KV': ((5, 1),), 'ee': ((3, 2),), 'ww': ((6, 0), (7, 0), (8, 0), (0, 2), (1, 2)), 'ent': ((9, 0), (2, 3), (10, 0), (4, 2), (5, 2)), 'we': ((3, 3),), 'word0': ((8, 1),), 'word1': ((6, 1), (11, 0), (0, 3)), 'word3': ((10, 1),), 'end': ((1, 3), (6, 2), (7, 1), (4, 3), (5, 3), (8, 2), (9, 1), (0, 4), (2, 4), (11, 1), (3, 4), (1, 4), (6, 3), (7, 2), (10, 2), (4, 4), (5, 4), (8, 3), (6, 4), (7, 3), (11, 2), (9, 2), (8, 4), (10, 3), (7, 4), (11, 3), (9, 3), (10, 4), (11, 4), (9, 4))}


def piece_scratch(spec, stages, source, own):
    _, slots, rows, width = spec
    owners = 2**stages
    shapes = []
    if source:
        shapes.append(pltpu.VMEM((slots, rows * owners, width), jnp.bfloat16))
    if own:
        shapes.append(pltpu.VMEM((slots, rows * owners // 2, width), jnp.bfloat16))
    shapes += [
        pltpu.VMEM((slots, rows * (owners - 2), width), jnp.bfloat16),
        pltpu.VMEM((slots, 2 * rows, width), jnp.float32),
        pltpu.VMEM((slots, 2 * rows, width // 2), jnp.bfloat16),
        pltpu.VMEM((slots, 2 * rows, width // 2), jnp.bfloat16),
        pltpu.SemaphoreType.DMA((stages,)),
        pltpu.SemaphoreType.DMA((stages,)),
    ]
    return shapes


def attention_back_kernel(orders, grad_scale, *refs):
    stages = len(orders[0])
    refs = list(refs)

    def take(count):
        taken = refs[:count]
        del refs[:count]
        return taken

    early_send = take(len(EARLY))
    (hidden, qword, qent, keys, values, cgrad, feat_q, feat_k, lse_delta, first_grad, head_low, slot_row) = take(12)
    (w_ww, w_we, w_ew, w_ee, w_key, w_value, dense, entity_low) = take(8)
    early_out = take(len(EARLY))
    late_out = take(len(LATE))
    words_out, request_out = take(2)
    devices = request_out.shape[0]
    early_pieces = []
    own_copies = []
    me = lax.axis_index("dp")
    partner_of = partners(me, orders[0])
    own_sem = refs.pop()
    request_sems = refs.pop()
    request_send = refs.pop()
    word_weights = []
    dqw, dqe, dkey, dvalue, prob_s, grad_s, flip, hidden_t, hidden_te, entity_t = refs[-10:]
    del refs[-10:]
    pieces = [[] for _ in STREAM_ORDER]
    early_flat = []
    for index, spec in enumerate(EARLY):
        own, land, tail, pack, tail_land, send_sem, recv_sem = take(7)
        piece = Piece(
            spec[2], stages, early_send[index], own, land, tail, pack, tail_land,
            early_out[index], send_sem, recv_sem,
        )
        pieces[spec[0]].append(piece)
        early_flat.append(piece)
        bit = partner_of[orders[STREAM_ORDER[spec[0]]][0]][1]
        size = spec[2] * 2 ** (stages - 1)
        own_copies.append(
            pltpu.make_async_copy(
                early_send[index].at[:, pl.ds(pl.multiple_of(bit * size, 16), size)],
                own,
                own_sem.at[index],
            )
        )
    late_source = []
    for index, spec in enumerate(LATE):
        source, land, tail, pack, tail_land, send_sem, recv_sem = take(7)
        late_source.append(source)
        pieces[spec[0]].append(
            Piece(
                spec[2], stages, source, None, land, tail, pack, tail_land,
                late_out[index], send_sem, recv_sem,
            )
        )
    spare = (early_flat[1].own, early_flat[3].own)
    split = spare[0].shape[2]
    for index, weight in enumerate((w_ww, w_we)):
        rows = weight.shape[0]
        for part, at in enumerate((pl.ds(0, split), pl.ds(split, weight.shape[1] - split))):
            word_weights.append(
                pltpu.make_async_copy(
                    weight.at[:, at],
                    spare[part].at[0, pl.ds(index * rows, rows)],
                    own_sem.at[len(EARLY) + 2 * index + part],
                )
            )
    streams = [
        Stream(orders[order], partner_of, pieces[index])
        for index, order in enumerate(STREAM_ORDER)
    ]
    first_late = LATE[0][0]

    def go_on(point):
        for index, stage in PLAN.get(point, ()):
            if stage == 0 and index < first_late:
                for piece, spec in enumerate(EARLY):
                    if spec[0] == index:
                        own_copies[piece].wait()
            streams[index].advance(stage)
            if stage == 0 and index in (1, 3):
                for copy in word_weights[(index - 1) // 2 :: 2]:
                    copy.start()

    greet_all(me, devices)
    for stream in streams[:first_late]:
        stream.launch(0)
    for copy in own_copies:
        copy.start()

    width = hidden.shape[1]
    seq_len = hidden.shape[0]
    words = words_out.shape[0]
    block = 128
    lane = lax.broadcasted_iota(jnp.int32, (1, block), 1)
    low_half = (lane < HD).astype(jnp.float32).astype(jnp.bfloat16)
    high_half = (lane >= HD).astype(jnp.float32).astype(jnp.bfloat16)
    halves = (low_half, high_half)

    def flip_step(index, carry):
        at = pl.ds(pl.multiple_of(index * block, block), block)
        flip[at] = hidden[:, at].astype(jnp.float32).T
        return carry

    lax.fori_loop(0, width // block, flip_step, 0)
    owners = 2**stages
    rows = width // owners
    for slot, order in enumerate(orders):
        begin = words if slot == 2 else 0
        for pair in range(owners // 2):
            one, two = place_owner(order, 2 * pair), place_owner(order, 2 * pair + 1)
            both = jnp.concatenate(
                [flip[one * rows : one * rows + rows, begin:], flip[two * rows : two * rows + rows, begin:]],
                axis=0,
            ).astype(jnp.bfloat16)
            if slot == 2:
                hidden_te[pair * 2 * rows : (pair + 1) * 2 * rows] = both
            else:
                hidden_t[slot, pair * 2 * rows : (pair + 1) * 2 * rows] = both

    go_on("start")

    def go_on_in_loop(name, pair):
        for point in range(width // block):
            if (name, point) in PLAN:
                pl.when(pair == point)(functools.partial(go_on, (name, point)))

    def pair_step(pair, carry):
        lanes = pl.ds(pl.multiple_of(pair * block, block), block)
        key_pair = keys[:, lanes]
        value_pair = values[:, lanes]
        key_feat = [key_pair * halves[h] + feat_k[...] * halves[1 - h] for h in range(2)]
        key_only = [key_pair * halves[h] for h in range(2)]
        value_only = [value_pair * halves[h] for h in range(2)]

        def row_step(index, inner):
            at = pl.ds(pl.multiple_of(index * block, block), block)
            qw = qword[at, lanes]
            qe = qent[at, lanes]
            feats = feat_q[at]
            given = cgrad[at, lanes]
            stats = lse_delta[at]
            spot = lax.broadcasted_iota(jnp.int32, (1, block), 1) - 4 * pair
            total_w = jnp.zeros((block, block), jnp.float32)
            total_e = jnp.zeros((block, block), jnp.float32)
            for h in range(2):
                left_w = qw * halves[h] + feats * halves[1 - h]
                left_e = qe * halves[h] + feats * halves[1 - h]
                scores = jnp.concatenate(
                    [
                        dot_right_t(left_w, key_feat[h][:words]),
                        dot_right_t(left_e, key_feat[h][words:]),
                    ],
                    axis=1,
                )
                prob = jnp.exp(scores - jnp.sum(jnp.where(spot == h, stats, 0.0), axis=1, keepdims=True))
                pgrad = dot_right_t(given, value_only[h])
                sgrad = (prob * (pgrad - jnp.sum(jnp.where(spot == 2 + h, stats, 0.0), axis=1, keepdims=True))).astype(jnp.bfloat16)
                prob_s[h, at] = prob.astype(jnp.bfloat16)
                grad_s[h, at] = sgrad
                total_w += dot_plain(sgrad[:, :words], key_only[h][:words])
                total_e += dot_plain(sgrad[:, words:], key_only[h][words:])
            dqw[at, lanes] = total_w.astype(jnp.bfloat16)
            dqe[at, lanes] = total_e.astype(jnp.bfloat16)
            return inner

        lax.fori_loop(0, seq_len // block, row_step, 0)
        go_on_in_loop("r", pair)
        qw_all, qe_all, given_all = qword[:, lanes], qent[:, lanes], cgrad[:, lanes]
        dkey[:words, lanes] = (
            dot_left_t(grad_s[0, :, :words], qw_all * halves[0])
            + dot_left_t(grad_s[1, :, :words], qw_all * halves[1])
        ).astype(jnp.bfloat16)
        dkey[words:, lanes] = (
            dot_left_t(grad_s[0, :, words:], qe_all * halves[0])
            + dot_left_t(grad_s[1, :, words:], qe_all * halves[1])
        ).astype(jnp.bfloat16)
        dvalue[:, lanes] = (
            dot_left_t(prob_s[0], given_all * halves[0])
            + dot_left_t(prob_s[1], given_all * halves[1])
        ).astype(jnp.bfloat16)

        go_on_in_loop("p", pair)
        return carry

    lax.fori_loop(0, width // block, pair_step, 0)

    query_scale = HD ** (-0.5)
    column = 384

    def weight_grad(source, slot, order_slot, grad, begin, end, scale):
        for cut in range(0, width, column):
            left = hidden_te[...] if order_slot == 2 else hidden_t[order_slot, :, begin:end]
            piece = dot_plain(left, grad[begin:end, cut : cut + column])
            if scale:
                piece = piece * query_scale
            source[slot, :, cut : cut + column] = piece.astype(jnp.bfloat16)

    weight_grad(late_source[0], 0, 1, dkey, 0, seq_len, False)
    streams[6].launch(0)
    weight_grad(late_source[1], 0, 1, dvalue, 0, seq_len, False)
    streams[7].launch(0)
    go_on("KV")
    weight_grad(late_source[2], 0, 2, dqw, words, seq_len, True)
    streams[8].launch(0)
    go_on("ew")
    weight_grad(late_source[3], 0, 1, dqe, words, seq_len, True)
    streams[9].launch(0)
    go_on("ee")
    weight_grad(late_source[4], 0, 0, dqw, 0, words, True)
    streams[10].launch(0)
    go_on("ww")

    def data_grad(begin, size, queries):
        at = pl.ds(begin, size)
        return (
            first_grad[at]
            + query_scale * queries(at)
            + dot_right_t(dkey[at], w_key[...])
            + dot_right_t(dvalue[at], w_value[...])
        )

    def entity_queries(at):
        return dot_right_t(dqw[at], w_ew[...]) + dot_right_t(dqe[at], w_ee[...])

    def word_queries(at):
        total = 0.0
        for index, grad in enumerate((dqw, dqe)):
            rows_at = pl.ds(index * width, width)
            total += dot_right_t(grad[at, :split], spare[0][0, rows_at])
            total += dot_right_t(grad[at, split:], spare[1][0, rows_at])
        return total

    state_low = data_grad(words, seq_len - words, entity_queries).astype(jnp.bfloat16)
    vectors = jnp.concatenate(
        [dot_right_t(state_low, dense[...]).astype(jnp.bfloat16), (head_low[...].astype(jnp.float32) * -grad_scale).astype(jnp.bfloat16)], axis=0
    )
    entries = slot_row.shape[1]
    wanted = lax.broadcasted_iota(jnp.int32, (vectors.shape[0], entries), 0)
    placing = (wanted == slot_row[0:1]).astype(jnp.float32).astype(jnp.bfloat16)
    per_request = dot_left_t(placing, vectors).astype(jnp.bfloat16)
    request_send[...] = per_request.reshape(request_send.shape)

    def request_copy(step):
        peer = lax.rem(me + step, devices)
        return pltpu.make_async_remote_copy(
            src_ref=request_send.at[peer],
            dst_ref=request_out.at[me],
            send_sem=request_sems.at[0, step],
            recv_sem=request_sems.at[1, step],
            device_id=(peer,),
            device_id_type=MESH_ID,
        )

    def begin_request(step, carry):
        request_copy(step).start()
        return carry

    def finish_request(step, carry):
        request_copy(step).wait()
        return carry

    lax.fori_loop(1, devices, begin_request, 0)
    request_out[me] = request_send[me]
    entity_width = dense.shape[0]
    few = entity_width // owners
    for cut in range(0, entity_width, block):
        flip[cut : cut + block, :block] = entity_low[:, cut : cut + block].astype(jnp.float32).T
    for pair in range(owners // 2):
        one, two = place_owner(orders[0], 2 * pair), place_owner(orders[0], 2 * pair + 1)
        both = jnp.concatenate(
            [flip[one * few : one * few + few, :block], flip[two * few : two * few + few, :block]],
            axis=0,
        )
        entity_t[pair * 2 * few : (pair + 1) * 2 * few] = both.astype(jnp.bfloat16)
    late_source[6][0] = dot_plain(entity_t[...], state_low).astype(jnp.bfloat16)
    go_on("ent")
    weight_grad(late_source[5], 0, 0, dqe, 0, words, True)
    streams[11].launch(0)
    go_on("we")
    for copy in word_weights:
        copy.wait()

    def word_step(index, carry):
        begin = pl.multiple_of(index * block, block)
        words_out[pl.ds(begin, block)] = data_grad(begin, block, word_queries).astype(jnp.bfloat16)
        for point in range(words // block):
            name = WORD_POINTS[point]
            if name in PLAN:
                pl.when(index == point)(functools.partial(go_on, name))
        return carry

    lax.fori_loop(0, words // block, word_step, 0)
    go_on("end")
    lax.fori_loop(1, devices, finish_request, 0)


def in_order(grad, order):
    bits = len(order)
    owners = 2**bits
    view = grad.reshape((2,) * bits + (grad.shape[0] // owners, grad.shape[1]))
    spots = tuple(bits - mask.bit_length() for mask in order)
    return view.transpose(spots + (bits, bits + 1)).reshape(grad.shape)


def attention_back(early_grads, inputs, weights, grad_scale, collective_id):
    devices = lax.axis_size("dp")
    orders = stage_masks(devices)
    stages = len(orders[0])
    hidden = inputs[0]
    seq_len, width = hidden.shape
    slots = weights[-1].shape[0]
    words = seq_len - slots
    outs = [
        jax.ShapeDtypeStruct((count, rows, wide), jnp.float32)
        for _, count, rows, wide in EARLY + LATE
    ] + [
        jax.ShapeDtypeStruct((words, width), jnp.bfloat16),
        jax.ShapeDtypeStruct(
            (devices, inputs[11].shape[1] // devices, weights[-2].shape[0]), jnp.bfloat16
        ),
    ]
    scratch = []
    for spec in EARLY:
        scratch += piece_scratch(spec, stages, False, True)
    for spec in LATE:
        scratch += piece_scratch(spec, stages, True, False)
    scratch += [pltpu.VMEM((seq_len, width), jnp.bfloat16)] * 4
    scratch += [pltpu.VMEM((2, seq_len, seq_len), jnp.bfloat16)] * 2
    scratch += [
        pltpu.VMEM((width, seq_len), jnp.float32),
        pltpu.VMEM((2, width, seq_len), jnp.bfloat16),
        pltpu.VMEM((width, slots), jnp.bfloat16),
        pltpu.VMEM((weights[-2].shape[0], slots), jnp.bfloat16),
        pltpu.VMEM((devices, inputs[11].shape[1] // devices, weights[-2].shape[0]), jnp.bfloat16),
        pltpu.SemaphoreType.DMA((2, devices)),
        pltpu.SemaphoreType.DMA((len(EARLY) + 4,)),
    ]
    vmem = pl.BlockSpec(memory_space=pltpu.VMEM)
    return pl.pallas_call(
        functools.partial(attention_back_kernel, orders, grad_scale),
        out_shape=outs,
        in_specs=[pl.BlockSpec(memory_space=pltpu.HBM)] * len(EARLY)
        + [vmem] * len(inputs)
        + [pl.BlockSpec(memory_space=pltpu.HBM)] * 2
        + [vmem] * (len(weights) - 2),
        out_specs=[vmem] * len(outs),
        scratch_shapes=scratch,
        compiler_params=pltpu.CompilerParams(
            collective_id=collective_id, has_side_effects=True, vmem_limit_bytes=63 * 2**20
        ),
    )(*early_grads, *inputs, *weights)


def fused_body(
    word_states,
    word_segments,
    entity_segments,
    request_rows,
    request_slot,
    mask_slots,
    entity_table,
    vocab_bias,
    entity_dense,
    query_ww,
    query_we,
    query_ew,
    query_ee,
    key_weight,
    value_weight,
    out_weight,
    norm1_gain,
    norm1_bias,
    up_weight,
    down_weight,
    norm2_gain,
    norm2_bias,
    head_weight,
    head_gain,
    head_bias,
    cotangent,
):
    devices = lax.axis_size("dp")
    low = jnp.bfloat16
    slot_count = entity_segments.shape[1]
    mask_count = mask_slots.shape[1]
    request_count = slot_count + mask_count
    table_rows = entity_table.shape[0]
    grad_scale = 1.0 / (mask_count * devices)
    orders = stage_masks(devices)
    capacity = request_rows.shape[1]
    room = -(-capacity // 16) * 16 - capacity
    kind = jnp.where(request_slot >= slot_count, table_rows, 0)
    codes = jnp.where(request_slot < request_count, request_rows + kind, -1)
    codes = jnp.pad(codes, ((0, 0), (0, room)), constant_values=-1)
    codes = jnp.broadcast_to(codes[:, :, None], codes.shape + (128,))
    slot_row = jnp.pad(request_slot, ((0, 0), (0, room)), constant_values=request_count)
    slot_row = jnp.broadcast_to(slot_row.reshape(1, -1), (8, slot_row.size))
    bias_row = vocab_bias.astype(jnp.float32)[None, :]
    (
        entity_low,
        target_vecs,
        target_bias,
        code_row,
        word_q,
        word_e,
        word_k,
        word_v,
        feat_q,
        feat_k,
    ) = lookup(
        [
            codes,
            entity_table,
            bias_row,
            slot_row,
            word_states,
            query_ww,
            query_we,
            key_weight,
            value_weight,
            word_segments,
            entity_segments,
        ],
        slot_count,
        mask_count,
        0,
    )
    choose = (mask_slots[0][:, None] == jnp.arange(slot_count, dtype=jnp.int32)[None, :]).astype(low)
    (
        hidden_low,
        query_word,
        query_entity,
        key_rows,
        values,
        context_low,
        lse_lanes,
        residual_one,
        normed_low,
        activated,
        gelu_slope,
        residual_two,
        layer_low,
        picked_low,
        head_pre,
        head_low,
    ) = forward_pass(
        [
            word_states,
            entity_low,
            feat_q,
            feat_k,
            choose,
            entity_dense,
            word_q,
            word_e,
            word_k,
            word_v,
            query_ew,
            query_ee,
            key_weight,
            value_weight,
            out_weight,
            norm1_gain,
            norm1_bias,
            up_weight,
            down_weight,
            norm2_gain,
            norm2_bias,
            head_weight,
            head_gain,
            head_bias,
        ]
    )
    table_grad, bias_grad, losses, total_loss, head_grad = head_and_table(
        head_low,
        entity_table,
        bias_row,
        target_vecs,
        target_bias,
        grad_scale,
        1,
    )
    (
        up_a,
        up_b,
        head_a,
        out_b,
        down_b,
        up_c,
        down_c,
        first_grad,
        context_grad,
        lse_delta,
        vectors,
    ) = middle_back(
        [
            head_grad,
            target_vecs,
            head_pre,
            head_gain,
            picked_low,
            head_weight,
            choose,
            cotangent,
            residual_two,
            norm2_gain,
            normed_low,
            residual_one,
            norm1_gain,
            out_weight,
            context_low,
            lse_lanes,
            activated,
            gelu_slope,
            up_weight,
            down_weight,
        ],
        orders,
        grad_scale,
    )
    *sums, words_grad, back_rows = attention_back(
        [up_a, down_b, up_c, down_c, up_b, head_a, vectors, out_b],
        [
            hidden_low,
            query_word,
            query_entity,
            key_rows,
            values,
            context_grad,
            feat_q,
            feat_k,
            lse_delta,
            first_grad,
            head_low,
            slot_row,
        ],
        [
            query_ww,
            query_we,
            query_ew,
            query_ee,
            key_weight,
            value_weight,
            entity_dense,
            entity_low,
        ],
        grad_scale,
        2,
    )
    (
        table_grad,
        bias_grad,
        up_sum,
        down_sum,
        head_sum,
        vector_sum,
        out_sum,
        key_sum,
        value_sum,
        ew_sum,
        ee_sum,
        ww_sum,
        we_sum,
        dense_sum,
    ) = last_step(
        code_row, back_rows.reshape(-1, back_rows.shape[2]), table_grad, bias_grad, sums, grad_scale
    )
    row = vector_sum[0]
    few, many = head_gain.shape[0] // devices, norm1_gain.shape[0] // devices
    spots = [0, few, 2 * few] + [2 * few + many * (i + 1) for i in range(4)]
    vector_out = [row[spots[i] : spots[i + 1]] for i in range(6)]
    return (
        total_loss[0, 0],
        layer_low,
        words_grad,
        table_grad,
        bias_grad[0],
        dense_sum,
        ww_sum,
        we_sum,
        ew_sum,
        ee_sum,
        key_sum,
        value_sum,
        out_sum,
        vector_out[4],
        vector_out[5],
        up_sum,
        down_sum,
        vector_out[2],
        vector_out[3],
        head_sum,
        vector_out[0],
        vector_out[1],
        losses[:, 0],
    )


def solution(mesh):
    in_specs = (
        P("dp", None),
        P("dp", None),
        P("dp", None),
        P("dp", None),
        P("dp", None),
        P("dp", None),
        P("dp", None),
        P("dp"),
        P(),
        P(),
        P(),
        P(),
        P(),
        P(),
        P(),
        P(),
        P(),
        P(),
        P(),
        P(),
        P(),
        P(),
        P(),
        P(),
        P(),
        P("dp", None),
    )
    out_specs = (
        P(),
        P("dp", None),
        P("dp", None),
        P("dp", None),
        P("dp"),
        P("dp", None),
        P("dp", None),
        P("dp", None),
        P("dp", None),
        P("dp", None),
        P("dp", None),
        P("dp", None),
        P("dp", None),
        P("dp"),
        P("dp"),
        P("dp", None),
        P("dp", None),
        P("dp"),
        P("dp"),
        P("dp", None),
        P("dp"),
        P("dp"),
        P("dp"),
    )
    chosen = fused_body if mesh.shape["dp"] == 32 else body
    return jax.shard_map(chosen, mesh=mesh, in_specs=in_specs, out_specs=out_specs, check_vma=False)
```

```python
import functools

import jax
import jax.numpy as jnp
from jax import lax
from jax.experimental import pallas as pl
from jax.experimental.pallas import tpu as pltpu
from jax.sharding import PartitionSpec as P

MESH_ID = pl.DeviceIdType.MESH

HD = 64


EPSILON = 1e-05
MASKED = -1000000000.0


def dot_plain(left_side, right_side):
    return jnp.dot(left_side, right_side, preferred_element_type=jnp.float32)


def dot_left_t(left_side, right_side):
    return lax.dot_general(
        left_side, right_side, (((0,), (0,)), ((), ())), preferred_element_type=jnp.float32
    )


def dot_right_t(left_side, right_side):
    return lax.dot_general(
        left_side, right_side, (((1,), (1,)), ((), ())), preferred_element_type=jnp.float32
    )


def dot_exact(left_side, right_side):
    return jnp.dot(
        left_side, right_side, precision=lax.Precision.HIGHEST, preferred_element_type=jnp.float32
    )


def layer_norm(tensor, gain_vec, shift_vec):
    center = tensor - jnp.mean(tensor, axis=-1, keepdims=True)
    spread = jnp.mean(center * center, axis=-1, keepdims=True)
    return center * lax.rsqrt(spread + EPSILON) * gain_vec + shift_vec


def gelu_exact(tensor):
    return jax.nn.gelu(tensor, approximate=False)


def head_act(tensor, gain_vec, shift_vec):
    return layer_norm(gelu_exact(tensor), gain_vec, shift_vec)


def norm_back(tensor, gain_vec, shift_vec, grad_out):
    result, pullback = jax.vjp(layer_norm, tensor, gain_vec, shift_vec)
    return pullback(grad_out)


def attn_scores(query_word, query_entity, key_rows, allowed, word_count):
    to_words = jnp.einsum(
        "qhd,khd->hqk", query_word, key_rows[:word_count], preferred_element_type=jnp.float32
    )
    to_entities = jnp.einsum(
        "qhd,khd->hqk", query_entity, key_rows[word_count:], preferred_element_type=jnp.float32
    )
    return jnp.where(allowed[None], jnp.concatenate([to_words, to_entities], axis=2), MASKED)


def greet_all(me, devices):
    barrier = pltpu.get_barrier_semaphore()

    def greet(step, carry):
        pl.semaphore_signal(
            barrier, inc=1, device_id=(lax.rem(me + step, devices),), device_id_type=MESH_ID
        )
        return carry

    lax.fori_loop(1, devices, greet, 0)
    pl.semaphore_wait(barrier, devices - 1)


def swap_kernel(devices, gather, source, target, send_sem, recv_sem):
    me = lax.axis_index("dp")
    greet_all(me, devices)

    def piece(step):
        peer = lax.rem(me + step, devices)
        return pltpu.make_async_remote_copy(
            src_ref=source if gather else source.at[peer],
            dst_ref=target.at[me],
            send_sem=send_sem.at[step],
            recv_sem=recv_sem.at[step],
            device_id=(peer,),
            device_id_type=MESH_ID,
        )

    def begin(step, carry):
        piece(step).start()
        return carry

    def finish(step, carry):
        piece(step).wait()
        return carry

    lax.fori_loop(1, devices, begin, 0)
    target[me] = source[...] if gather else source[me]
    lax.fori_loop(1, devices, finish, 0)


def direct_swap(value, collective_id, gather=False):
    devices = lax.axis_size("dp")
    shape = (devices,) + value.shape if gather else value.shape
    return pl.pallas_call(
        functools.partial(swap_kernel, devices, gather),
        out_shape=jax.ShapeDtypeStruct(shape, value.dtype),
        in_specs=[pl.BlockSpec(memory_space=pltpu.VMEM)],
        out_specs=pl.BlockSpec(memory_space=pltpu.VMEM),
        scratch_shapes=[
            pltpu.SemaphoreType.DMA((devices,)),
            pltpu.SemaphoreType.DMA((devices,)),
        ],
        compiler_params=pltpu.CompilerParams(collective_id=collective_id, has_side_effects=True),
    )(value)


def stage_masks(devices):
    if devices == 32:
        axes = [[2], [4], [8, 16]]
    elif devices == 128:
        axes = [[2, 4], [8, 16], [32, 64]]
    else:
        axes = [[2**bit] for bit in range(1, devices.bit_length() - 1)]
        axes = axes + [[] for _ in range(3 - len(axes))]
    first, second, third = axes[0], axes[1], sum(axes[2:], [])
    return (
        [1] + first + second + third,
        [1] + second + first + third,
        [1] + third + first + second,
    )


def sum_kernel(masks, rows, *refs):
    parts = len(masks)
    stages = len(masks[0])
    sources, results = refs[:parts], refs[parts : 2 * parts]
    landing = refs[2 * parts : 3 * parts]
    send_sem, recv_sem = refs[3 * parts :]
    me = lax.axis_index("dp")
    barrier = pltpu.get_barrier_semaphore()
    partner_of = {}
    for mask in masks[0]:
        bit = lax.rem(lax.div(me, mask), 2)
        partner_of[mask] = (me + mask - 2 * mask * bit, bit)
    for mask in masks[0]:
        pl.semaphore_signal(
            barrier, inc=1, device_id=(partner_of[mask][0],), device_id_type=MESH_ID
        )
    pl.semaphore_wait(barrier, stages)
    sizes = [[rows[part] * 2 ** (stages - 1 - stage) for stage in range(stages)] for part in range(parts)]
    places = [[sum(size[:stage]) for stage in range(stages)] for size in sizes]

    def launch(part, stage):
        partner, bit = partner_of[masks[part][stage]]
        size = sizes[part][stage]
        away = (1 - bit) * size
        copy = pltpu.make_async_remote_copy(
            src_ref=sources[part].at[pl.ds(away, size)]
            if stage == 0
            else landing[part].at[pl.ds(places[part][stage - 1] + away, size)],
            dst_ref=landing[part].at[pl.ds(places[part][stage], size)],
            send_sem=send_sem.at[part, stage],
            recv_sem=recv_sem.at[part, stage],
            device_id=(partner,),
            device_id_type=MESH_ID,
        )
        copy.start()
        return copy

    flying = [launch(part, 0) for part in range(parts)]

    def add_rows(part, stage, start, count):
        keep = partner_of[masks[part][stage]][1] * sizes[part][stage] + start
        last = stage == stages - 1

        def step(index, carry):
            theirs = pl.ds(pl.multiple_of(places[part][stage] + start + index * 16, 16), 16)
            if stage == 0:
                mine = sources[part][pl.ds(pl.multiple_of(keep + index * 16, 16), 16)]
            else:
                mine = landing[part][
                    pl.ds(pl.multiple_of(places[part][stage - 1] + keep + index * 16, 16), 16)
                ]
            total = mine.astype(jnp.float32) + landing[part][theirs].astype(jnp.float32)
            if last:
                results[part][pl.ds(pl.multiple_of(index * 16, 16), 16)] = total
            else:
                landing[part][theirs] = total.astype(jnp.bfloat16)
            return carry

        lax.fori_loop(0, count // 16, step, 0, unroll=min(4, count // 16))

    for stage in range(stages):
        for part in range(parts):
            flying[part].wait()
            if stage == stages - 1:
                add_rows(part, stage, 0, sizes[part][stage])
                continue
            bit = partner_of[masks[part][stage + 1]][1]
            half = sizes[part][stage] // 2
            add_rows(part, stage, (1 - bit) * half, half)
            flying[part] = launch(part, stage + 1)
            add_rows(part, stage, bit * half, half)


def sum_scatter(parts, collective_id):
    devices = lax.axis_size("dp")
    masks = stage_masks(devices)
    rows = [part.shape[1] for part in parts]
    width = parts[0].shape[2]
    bits = devices.bit_length() - 1
    ordered = []
    for part, order in zip(parts, masks):
        view = part.reshape((2,) * bits + part.shape[1:])
        places = [bits - mask.bit_length() for mask in order]
        view = view.transpose(tuple(places) + (bits, bits + 1))
        ordered.append(view.reshape(devices * part.shape[1], width))
    return pl.pallas_call(
        functools.partial(sum_kernel, masks, rows),
        out_shape=[jax.ShapeDtypeStruct((count, width), jnp.float32) for count in rows],
        in_specs=[pl.BlockSpec(memory_space=pltpu.VMEM)] * len(parts),
        out_specs=[pl.BlockSpec(memory_space=pltpu.VMEM)] * len(parts),
        scratch_shapes=[pltpu.VMEM((devices * count, width), jnp.bfloat16) for count in rows]
        + [pltpu.SemaphoreType.DMA((len(parts), bits)), pltpu.SemaphoreType.DMA((len(parts), bits))],
        input_output_aliases={},
        compiler_params=pltpu.CompilerParams(
            collective_id=collective_id, has_side_effects=True, vmem_limit_bytes=56 * 2**20
        ),
    )(*ordered)


def by_owner(grad, width):
    devices = lax.axis_size("dp")
    rows = grad.shape[0] // devices
    blocks = grad.astype(jnp.bfloat16).reshape(devices, rows, grad.shape[1])
    if grad.shape[1] > width:
        cuts = grad.shape[1] // width
        return jnp.concatenate(jnp.split(blocks, cuts, axis=2), axis=1)
    if grad.shape[1] < width:
        return blocks.reshape(devices, rows * grad.shape[1] // width, width)
    return blocks


def from_owner(rows, shape):
    devices = lax.axis_size("dp")
    count, width = shape[0] // devices, shape[1]
    if width > rows.shape[1]:
        return jnp.concatenate(jnp.split(rows, width // rows.shape[1], axis=0), axis=1)
    return rows.reshape(count, width)


def sum_all(groups, collective_id):
    width = groups[0][0].shape[1]
    width = min(grad.shape[1] for group in groups for grad in group if grad.shape[1] >= 768)
    devices = lax.axis_size("dp")
    packed = []
    for group in groups:
        pieces = [by_owner(grad, width) for grad in group]
        count = sum(piece.shape[1] for piece in pieces)
        room = -(-count // 16) * 16 - count
        if room:
            pieces.append(jnp.zeros((devices, room, width), jnp.bfloat16))
        packed.append(jnp.concatenate(pieces, axis=1))
    sums = sum_scatter(packed, collective_id)
    results = []
    for group, total in zip(groups, sums):
        place, outs = 0, []
        for grad in group:
            count = grad.shape[0] // devices * grad.shape[1] // width
            outs.append(from_owner(total[place : place + count], grad.shape))
            place += count
        results.append(outs)
    return results


def body(
    word_states,
    word_segments,
    entity_segments,
    request_rows,
    request_slot,
    mask_slots,
    entity_table,
    vocab_bias,
    entity_dense,
    query_ww,
    query_we,
    query_ew,
    query_ee,
    key_weight,
    value_weight,
    out_weight,
    norm1_gain,
    norm1_bias,
    up_weight,
    down_weight,
    norm2_gain,
    norm2_bias,
    head_weight,
    head_gain,
    head_bias,
    cotangent,
):
    word_count = word_states.shape[0]
    model_width = word_states.shape[1]
    slot_count = entity_segments.shape[1]
    mask_count = mask_slots.shape[1]
    request_count = slot_count + mask_count
    seq_len = word_count + slot_count
    devices = lax.axis_size("dp")
    capacity = request_rows.shape[1]
    head_count = model_width // HD
    query_scale = HD ** (-0.5)
    emb_width = entity_table.shape[1]
    table_rows = entity_table.shape[0]
    total_mask = mask_count * devices
    grad_scale = 1.0 / total_mask
    id_block = jnp.pad(request_rows[:, None, :], ((0, 0), (0, 7), (0, 128 - capacity)))
    asked_ids = direct_swap(id_block, 0)[:, 0, :capacity]
    found_rows = jnp.take(entity_table, asked_ids, axis=0)
    found_bias = jnp.take(vocab_bias, asked_ids, axis=0)
    cap_room = -(-capacity // 16) * 16 - capacity
    found_all = jnp.concatenate(
        [found_rows, jnp.broadcast_to(found_bias[:, :, None], found_bias.shape + (128,))], axis=2
    )
    back_all = direct_swap(jnp.pad(found_all, ((0, 0), (0, cap_room), (0, 0))), 1)
    back_rows = back_all[:, :capacity, :emb_width]
    back_bias = back_all[:, :capacity, emb_width]
    got_rows = back_rows
    got_bias = back_bias
    slot_ids = request_slot.reshape(devices * capacity)
    placing = slot_ids[None, :] == jnp.arange(request_count, dtype=jnp.int32)[:, None]
    placing_low = placing.astype(jnp.bfloat16)
    request_vecs = dot_plain(placing_low, got_rows.reshape(devices * capacity, emb_width))
    request_bias = dot_plain(placing_low, got_bias.reshape(devices * capacity, 1))[:, 0]
    entity_low = request_vecs[:slot_count].astype(jnp.bfloat16)
    target_vecs = request_vecs[slot_count:]
    target_bias = request_bias[slot_count:]
    entity_states = dot_plain(entity_low, entity_dense)
    hidden = jnp.concatenate([word_states.astype(jnp.float32), entity_states], axis=0)
    hidden_low = hidden.astype(jnp.bfloat16)
    word_part = hidden_low[:word_count]
    entity_part = hidden_low[word_count:]
    query_word = (
        query_scale
        * jnp.concatenate(
            [dot_plain(word_part, query_ww), dot_plain(entity_part, query_ew)], axis=0
        )
    ).astype(jnp.bfloat16)
    query_entity = (
        query_scale
        * jnp.concatenate(
            [dot_plain(word_part, query_we), dot_plain(entity_part, query_ee)], axis=0
        )
    ).astype(jnp.bfloat16)
    key_rows = dot_plain(hidden_low, key_weight).astype(jnp.bfloat16)
    values = dot_plain(hidden_low, value_weight).astype(jnp.bfloat16)
    head_shape = (seq_len, head_count, HD)
    query_word_h = query_word.reshape(head_shape)
    query_entity_h = query_entity.reshape(head_shape)
    key_rows_h = key_rows.reshape(head_shape)
    values_h = values.reshape(head_shape)
    segment_row = jnp.concatenate([word_segments[0], entity_segments[0]])
    allowed = segment_row[:, None] == segment_row[None, :]
    scores = attn_scores(query_word_h, query_entity_h, key_rows_h, allowed, word_count)
    row_top = jnp.max(scores, axis=2, keepdims=True)
    exp_scores = jnp.exp(scores - row_top)
    row_total = jnp.sum(exp_scores, axis=2, keepdims=True)
    attn_low = (exp_scores / row_total).astype(jnp.bfloat16)
    row_lse = row_top + jnp.log(row_total)
    context = jnp.einsum("hqk,khd->qhd", attn_low, values_h, preferred_element_type=jnp.float32)
    context_low = context.reshape(seq_len, model_width).astype(jnp.bfloat16)
    attended = dot_plain(context_low, out_weight)
    residual_one = hidden + attended
    normed = layer_norm(residual_one, norm1_gain, norm1_bias)
    normed_low = normed.astype(jnp.bfloat16)
    up_value = dot_plain(normed_low, up_weight)
    activated = gelu_exact(up_value).astype(jnp.bfloat16)
    down_value = dot_plain(activated, down_weight)
    residual_two = normed + down_value
    layer_out = layer_norm(residual_two, norm2_gain, norm2_bias)
    choose = (mask_slots[0][:, None] == jnp.arange(slot_count, dtype=jnp.int32)[None, :]).astype(
        jnp.float32
    )
    picked_low = dot_exact(choose, layer_out[word_count:]).astype(jnp.bfloat16)
    head_pre = dot_plain(picked_low, head_weight)
    head_low = head_act(head_pre, head_gain, head_bias).astype(jnp.bfloat16)
    head_f32 = head_low.astype(jnp.float32)
    target_logit = jnp.sum(head_f32 * target_vecs, axis=1) + target_bias
    all_heads = direct_swap(head_low, 2, gather=True).reshape(total_mask, emb_width)
    block_rows = min(512, total_mask)
    block_count = total_mask // block_rows
    bias_f32 = vocab_bias.astype(jnp.float32)

    def block_logits(block_index):
        row_block = lax.dynamic_slice_in_dim(all_heads, block_index * block_rows, block_rows, 0)
        return (row_block, dot_right_t(row_block, entity_table) + bias_f32[None, :])

    def block_stats(block_index):
        row_block, logits = block_logits(block_index)
        top_value = jnp.max(logits, axis=1)
        return (top_value, jnp.sum(jnp.exp(logits - top_value[:, None]), axis=1))

    local_top, local_total = lax.map(block_stats, jnp.arange(block_count, dtype=jnp.int32))
    local_top = local_top.reshape(total_mask)
    local_total = local_total.reshape(total_mask)
    target_sum = jnp.sum(target_logit)
    stats = jnp.concatenate(
        [
            local_top.reshape(total_mask // 128, 128),
            local_total.reshape(total_mask // 128, 128),
            jnp.full((8, 128), target_sum),
        ],
        axis=0,
    )
    all_stats = direct_swap(stats, 3, gather=True)
    all_tops = all_stats[:, : total_mask // 128].reshape(devices, total_mask)
    all_totals = all_stats[:, total_mask // 128 : total_mask // 64].reshape(devices, total_mask)
    target_total = jnp.sum(all_stats[:, total_mask // 64, 0])
    global_top = jnp.max(all_tops, axis=0)
    global_total = jnp.sum(all_totals * jnp.exp(all_tops - global_top[None, :]), axis=0)
    lse_all = global_top + jnp.log(global_total)
    loss_value = (jnp.sum(lse_all) - target_total) * grad_scale
    own_lse = lax.dynamic_slice_in_dim(lse_all, lax.axis_index("dp") * mask_count, mask_count, 0)
    mask_loss = own_lse - target_logit

    def block_back(running, block_index):
        table_grad, bias_grad = running
        row_block, logits = block_logits(block_index)
        lse_block = lax.dynamic_slice_in_dim(lse_all, block_index * block_rows, block_rows, 0)
        logit_grad = (jnp.exp(logits - lse_block[:, None]) * grad_scale).astype(jnp.bfloat16)
        table_grad = table_grad + dot_left_t(logit_grad, row_block)
        bias_grad = bias_grad + jnp.sum(logit_grad.astype(jnp.float32), axis=0)
        return ((table_grad, bias_grad), dot_plain(logit_grad, entity_table))

    start_grads = (
        jnp.zeros((table_rows, emb_width), jnp.float32),
        jnp.zeros((table_rows,), jnp.float32),
    )
    (table_grad, bias_grad), head_terms = lax.scan(
        block_back, start_grads, jnp.arange(block_count, dtype=jnp.int32)
    )
    head_parts = direct_swap(head_terms.reshape(devices, mask_count, emb_width), 4)
    head_grad = jnp.sum(head_parts, axis=0)
    head_grad = head_grad - grad_scale * target_vecs
    target_grad = -grad_scale * head_f32
    pre_grad, head_gain_grad, head_bias_grad = jax.vjp(head_act, head_pre, head_gain, head_bias)[1](
        head_grad
    )
    pre_low = pre_grad.astype(jnp.bfloat16)
    head_weight_grad = dot_left_t(picked_low, pre_low)
    picked_grad = dot_right_t(pre_low, head_weight)
    out_grad = cotangent.astype(jnp.float32) + jnp.concatenate(
        [jnp.zeros((word_count, model_width), jnp.float32), dot_exact(choose.T, picked_grad)],
        axis=0,
    )
    resid_grad, norm2_gain_grad, norm2_bias_grad = norm_back(
        residual_two, norm2_gain, norm2_bias, out_grad
    )
    down_in = resid_grad.astype(jnp.bfloat16)
    down_grad = dot_left_t(activated, down_in)
    act_grad = dot_right_t(down_in, down_weight)
    up_grad = jax.vjp(gelu_exact, up_value)[1](act_grad)[0]
    up_low = up_grad.astype(jnp.bfloat16)
    up_weight_grad = dot_left_t(normed_low, up_low)
    normed_grad = resid_grad + dot_right_t(up_low, up_weight)
    first_grad, norm1_gain_grad, norm1_bias_grad = norm_back(
        residual_one, norm1_gain, norm1_bias, normed_grad
    )
    attn_in = first_grad.astype(jnp.bfloat16)
    out_weight_grad = dot_left_t(context_low, attn_in)
    context_grad = dot_right_t(attn_in, out_weight).astype(jnp.bfloat16).reshape(head_shape)
    scores_again = attn_scores(query_word_h, query_entity_h, key_rows_h, allowed, word_count)
    attn_prob = jnp.exp(scores_again - row_lse)
    prob_low = attn_prob.astype(jnp.bfloat16)
    prob_grad = jnp.einsum(
        "qhd,khd->hqk", context_grad, values_h, preferred_element_type=jnp.float32
    )
    values_grad = jnp.einsum(
        "hqk,qhd->khd", prob_low, context_grad, preferred_element_type=jnp.float32
    )
    values_grad = values_grad.reshape(seq_len, model_width).astype(jnp.bfloat16)
    row_delta = jnp.sum(attn_prob * prob_grad, axis=2, keepdims=True)
    score_grad = (attn_prob * (prob_grad - row_delta)).astype(jnp.bfloat16)
    qword_grad = jnp.einsum(
        "hqk,khd->qhd",
        score_grad[:, :, :word_count],
        key_rows_h[:word_count],
        preferred_element_type=jnp.float32,
    )
    qword_grad = qword_grad.reshape(seq_len, model_width).astype(jnp.bfloat16)
    qent_grad = jnp.einsum(
        "hqk,khd->qhd",
        score_grad[:, :, word_count:],
        key_rows_h[word_count:],
        preferred_element_type=jnp.float32,
    )
    qent_grad = qent_grad.reshape(seq_len, model_width).astype(jnp.bfloat16)
    keys_grad = jnp.concatenate(
        [
            jnp.einsum(
                "hqk,qhd->khd",
                score_grad[:, :, :word_count],
                query_word_h,
                preferred_element_type=jnp.float32,
            ),
            jnp.einsum(
                "hqk,qhd->khd",
                score_grad[:, :, word_count:],
                query_entity_h,
                preferred_element_type=jnp.float32,
            ),
        ],
        axis=0,
    )
    keys_grad = keys_grad.reshape(seq_len, model_width).astype(jnp.bfloat16)
    query_ww_grad = query_scale * dot_left_t(word_part, qword_grad[:word_count])
    query_ew_grad = query_scale * dot_left_t(entity_part, qword_grad[word_count:])
    query_we_grad = query_scale * dot_left_t(word_part, qent_grad[:word_count])
    query_ee_grad = query_scale * dot_left_t(entity_part, qent_grad[word_count:])
    key_weight_grad = dot_left_t(hidden_low, keys_grad)
    value_weight_grad = dot_left_t(hidden_low, values_grad)
    word_back = query_scale * (
        dot_right_t(qword_grad[:word_count], query_ww)
        + dot_right_t(qent_grad[:word_count], query_we)
    )
    entity_back = query_scale * (
        dot_right_t(qword_grad[word_count:], query_ew)
        + dot_right_t(qent_grad[word_count:], query_ee)
    )
    hidden_grad = (
        first_grad
        + jnp.concatenate([word_back, entity_back], axis=0)
        + dot_right_t(keys_grad, key_weight)
        + dot_right_t(values_grad, value_weight)
    )
    words_grad = hidden_grad[:word_count].astype(jnp.bfloat16)
    state_low = hidden_grad[word_count:].astype(jnp.bfloat16)
    dense_grad = dot_left_t(entity_low, state_low)
    entity_vec_grad = dot_right_t(state_low, entity_dense)
    vec_grad = jnp.concatenate([entity_vec_grad, target_grad], axis=0)
    bias_vec_grad = jnp.concatenate(
        [jnp.zeros((slot_count,), jnp.float32), jnp.full((mask_count,), -grad_scale, jnp.float32)]
    )
    placing_f32 = placing.astype(jnp.float32)
    per_request = dot_exact(placing_f32.T, vec_grad)
    bias_request = dot_exact(placing_f32.T, bias_vec_grad[:, None])[:, 0]
    back_block = jnp.concatenate(
        [
            per_request.reshape(devices, capacity, emb_width).astype(jnp.bfloat16),
            jnp.broadcast_to(
                bias_request.reshape(devices, capacity, 1).astype(jnp.bfloat16),
                (devices, capacity, 128),
            ),
        ],
        axis=2,
    )
    back_block = direct_swap(jnp.pad(back_block, ((0, 0), (0, cap_room), (0, 0))), 5)
    back_rows = back_block[:, :capacity, :emb_width].astype(jnp.float32)
    back_bias = back_block[:, :capacity, emb_width].astype(jnp.float32)
    flat_ids = asked_ids.reshape(devices * capacity)
    table_grad = table_grad + jax.ops.segment_sum(
        back_rows.reshape(devices * capacity, emb_width), flat_ids, num_segments=table_rows
    )
    bias_grad = bias_grad + jax.ops.segment_sum(
        back_bias.reshape(devices * capacity), flat_ids, num_segments=table_rows
    )
    vectors = [
        head_gain_grad,
        head_bias_grad,
        norm2_gain_grad,
        norm2_bias_grad,
        norm1_gain_grad,
        norm1_bias_grad,
    ]
    cuts = [vector.reshape(devices, -1) for vector in vectors]
    spots = [0]
    for cut in cuts:
        spots.append(spots[-1] + cut.shape[1])
    block = jnp.concatenate(cuts, axis=1)
    block = jnp.pad(block, ((0, 0), (0, 128 - spots[-1])))[:, None, :]
    vector_sums = jnp.sum(direct_swap(jnp.pad(block, ((0, 0), (0, 7), (0, 0))), 6)[:, 0], axis=0)
    vector_out = [vector_sums[spots[i] : spots[i + 1]] for i in range(len(cuts))]
    sums = sum_all(
        [
            [up_weight_grad, out_weight_grad, head_weight_grad],
            [down_grad, query_ww_grad, dense_grad],
            [query_we_grad, query_ew_grad, query_ee_grad, key_weight_grad, value_weight_grad],
        ],
        7,
    )
    all_sums = (
        sums[0][2],
        vector_out[0],
        vector_out[1],
        vector_out[2],
        vector_out[3],
        sums[0][0],
        sums[1][0],
        vector_out[4],
        vector_out[5],
        sums[0][1],
        sums[1][1],
        sums[2][0],
        sums[2][1],
        sums[2][2],
        sums[2][3],
        sums[2][4],
        sums[1][2],
    )
    return (
        loss_value,
        layer_out.astype(jnp.bfloat16),
        words_grad,
        table_grad,
        bias_grad,
        all_sums[16],
        all_sums[10],
        all_sums[11],
        all_sums[12],
        all_sums[13],
        all_sums[14],
        all_sums[15],
        all_sums[9],
        all_sums[7],
        all_sums[8],
        all_sums[5],
        all_sums[6],
        all_sums[3],
        all_sums[4],
        all_sums[0],
        all_sums[1],
        all_sums[2],
        mask_loss,
    )


class Stage:
    def __init__(self, loads, stores):
        self.loads, self.stores, self.waited, self.sent = loads, stores, set(), []

    def need(self, *indices):
        for index in indices:
            if index not in self.waited:
                self.waited.add(index)
                self.loads[index].wait()

    def send(self, *indices):
        for index in indices:
            self.sent.append(index)
            self.stores[index].start()

    def finish(self):
        self.need(*self.loads)
        self.send(*[index for index in self.stores if index not in self.sent])
        for copy in self.stores.values():
            copy.wait()


def staged_kernel(inner, counts, far_in, far_out, *refs):
    ins, outs = list(refs[: counts[0]]), list(refs[counts[0] : sum(counts)])
    rest = list(refs[sum(counts) :])
    out_sem, in_sem = rest.pop(), rest.pop()
    near = rest[len(rest) - len(far_in) - len(far_out) :]
    rest = rest[: len(rest) - len(near)]
    loads, stores = {}, {}
    for slot, index in enumerate(far_in):
        loads[index] = pltpu.make_async_copy(ins[index], near[slot], in_sem.at[slot])
        ins[index] = near[slot]
        loads[index].start()
    for slot, index in enumerate(far_out):
        close = near[len(far_in) + slot]
        stores[index] = pltpu.make_async_copy(close, outs[index], out_sem.at[slot])
        outs[index] = close
    stage = Stage(loads, stores)
    inner(stage, *ins, *outs, *rest)
    stage.finish()


def staged_call(inner, inputs, outs, in_specs, out_specs, far_in, far_out, scratch, params):
    hbm = pl.BlockSpec(memory_space=pltpu.HBM)
    in_specs, out_specs = list(in_specs), list(out_specs)
    extra = []
    for index in far_in:
        in_specs[index] = hbm
        extra.append(pltpu.VMEM(inputs[index].shape, inputs[index].dtype))
    for index in far_out:
        out_specs[index] = hbm
        extra.append(pltpu.VMEM(outs[index].shape, outs[index].dtype))
    return pl.pallas_call(
        functools.partial(staged_kernel, inner, (len(inputs), len(outs)), far_in, far_out),
        out_shape=outs,
        in_specs=in_specs,
        out_specs=out_specs,
        scratch_shapes=list(scratch)
        + extra
        + [
            pltpu.SemaphoreType.DMA((max(1, len(far_in)),)),
            pltpu.SemaphoreType.DMA((max(1, len(far_out)),)),
        ],
        compiler_params=params,
    )(*inputs)


def all_pairs(source, target, sems, me, devices):
    def piece(step):
        peer = lax.rem(me + step, devices)
        return pltpu.make_async_remote_copy(
            src_ref=source.at[peer],
            dst_ref=target.at[me],
            send_sem=sems.at[0, step],
            recv_sem=sems.at[1, step],
            device_id=(peer,),
            device_id_type=MESH_ID,
        )

    def begin(step, carry):
        piece(step).start()
        return carry

    def finish(step, carry):
        piece(step).wait()
        return carry

    lax.fori_loop(1, devices, begin, 0)
    target[me] = source[me]
    return lambda: lax.fori_loop(1, devices, finish, 0)


def lookup_kernel(
    stage,
    codes,
    table,
    bias,
    slot_row,
    word_states,
    w_ww,
    w_we,
    w_key,
    w_value,
    word_seg,
    entity_seg,
    entity_out,
    vec_out,
    bias_out,
    code_out,
    qword,
    qent,
    keys,
    values,
    feat_q,
    feat_k,
    codes_in,
    found,
    rows_in,
    bias_col,
    sems,
):
    devices, room, _ = codes.shape
    me = lax.axis_index("dp")
    rows, wide = table.shape
    entries = devices * room
    greet_all(me, devices)
    ended = all_pairs(codes, codes_in, sems.at[0], me, devices)
    width = word_states.shape[1]
    half = width // 2
    query_scale = HD ** (-0.5)

    def project(target, weight, scale):
        for cut in range(0, width, half):
            value = dot_plain(word_states[...], weight[:, cut : cut + half])
            if scale:
                value = value * query_scale
            target[:, cut : cut + half] = value.astype(jnp.bfloat16)

    def bias_step(index, carry):
        at = pl.ds(pl.multiple_of(index * 128, 128), 128)
        bias_col[at] = jnp.broadcast_to(bias[:, at], (128, 128)).T.astype(jnp.bfloat16)
        return carry

    lax.fori_loop(0, rows // 128, bias_step, 0)
    words = word_seg.shape[1]
    column = lax.rem(lax.broadcasted_iota(jnp.int32, (128, 128), 1), HD)
    for begin in range(0, words + entity_seg.shape[1], 128):
        seg = word_seg[:, begin : begin + 128] if begin < words else entity_seg[...]
        turned = jnp.broadcast_to(seg.astype(jnp.float32), (128, 128)).T
        same = turned == column.astype(jnp.float32)
        at = slice(begin, begin + 128)
        feat_q[at] = same.astype(jnp.float32).astype(jnp.bfloat16)
        feat_k[at] = jnp.where(same | (column >= 4), 0.0, MASKED).astype(jnp.bfloat16)
    stage.need(4, 5)
    project(qword, w_ww, True)
    stage.send(4)
    stage.need(1)
    ended()
    code = codes_in[...].reshape(entries, 128)
    for begin in range(0, entries, 128):
        turned = code[begin : begin + 128].astype(jnp.float32).T
        code_out[:, begin : begin + 128] = turned[0:8].astype(jnp.int32)
    code = jnp.where(code >= rows, code - rows, code)
    lane = lax.broadcasted_iota(jnp.int32, (entries, 128), 1)
    total = jnp.zeros((entries, wide), jnp.float32)
    shift = jnp.zeros((entries, 128), jnp.float32)
    step = 512
    for begin in range(0, rows, step):
        size = min(step, rows - begin)
        match = jnp.concatenate(
            [
                (code - (begin + inner) == lane).astype(jnp.float32)
                for inner in range(0, size, 128)
            ],
            axis=1,
        ).astype(jnp.bfloat16)
        total += dot_plain(match, table[begin : begin + size])
        shift += dot_plain(match, bias_col[begin : begin + size])
    both = jnp.concatenate([total, shift], axis=1).astype(jnp.bfloat16)
    found[...] = both.reshape(found.shape)
    ended = all_pairs(found, rows_in, sems.at[1], me, devices)
    stage.need(6)
    project(qent, w_we, True)
    stage.send(5)
    stage.need(7)
    project(keys, w_key, False)
    stage.send(6)
    stage.need(8)
    project(values, w_value, False)
    stage.send(7)
    ended()
    slots, masked = entity_out.shape[0], vec_out.shape[0]
    wanted = lax.broadcasted_iota(jnp.int32, (slots + masked, entries), 0)
    placing = (wanted == slot_row[0:1]).astype(jnp.float32).astype(jnp.bfloat16)
    placed = dot_plain(placing, rows_in[...].reshape(entries, wide + 128))
    entity_out[...] = placed[:slots, :wide].astype(jnp.bfloat16)
    vec_out[...] = placed[slots:, :wide]
    bias_out[...] = placed[slots:, wide:]


def lookup(inputs, slots, masked, collective_id):
    devices, room, _ = inputs[0].shape
    rows, wide = inputs[1].shape
    words, width = inputs[4].shape
    entries = devices * room
    low = jnp.bfloat16
    vmem = pl.BlockSpec(memory_space=pltpu.VMEM)
    outs = [
        jax.ShapeDtypeStruct((slots, wide), low),
        jax.ShapeDtypeStruct((masked, wide), jnp.float32),
        jax.ShapeDtypeStruct((masked, 128), jnp.float32),
        jax.ShapeDtypeStruct((8, entries), jnp.int32),
    ]
    outs += [jax.ShapeDtypeStruct((words, width), low)] * 4
    outs += [jax.ShapeDtypeStruct((words + slots, 128), low)] * 2
    return staged_call(
        lookup_kernel,
        inputs,
        outs,
        [vmem] * len(inputs),
        [vmem] * len(outs),
        (4, 5, 1, 6, 7, 8),
        (4, 5, 6, 7),
        [
            pltpu.VMEM(inputs[0].shape, jnp.int32),
            pltpu.VMEM((devices, room, wide + 128), low),
            pltpu.VMEM((devices, room, wide + 128), low),
            pltpu.VMEM((rows, 128), low),
            pltpu.SemaphoreType.DMA((2, 2, devices)),
        ],
        pltpu.CompilerParams(
            collective_id=collective_id, has_side_effects=True, vmem_limit_bytes=63 * 2**20
        ),
    )


def norm_parts(value):
    center = value - jnp.mean(value, axis=-1, keepdims=True)
    spread = jnp.mean(center * center, axis=-1, keepdims=True)
    rate = lax.rsqrt(spread + EPSILON)
    return center * rate, rate


def gelu_parts(value):
    chance = 0.5 + 0.5 * lax.erf(value * (0.5**0.5))
    slope = chance + value * (jnp.exp(-0.5 * value * value) * (0.5 / jnp.pi) ** 0.5)
    return value * chance, slope


def half_lanes(block):
    lane = lax.broadcasted_iota(jnp.int32, (1, block), 1)
    low_half = (lane < HD).astype(jnp.float32).astype(jnp.bfloat16)
    high_half = (lane >= HD).astype(jnp.float32).astype(jnp.bfloat16)
    return low_half, high_half


def forward_kernel(
    stage,
    word_states,
    entity_low,
    feat_q,
    feat_k,
    choose,
    dense,
    word_q,
    word_e,
    word_k,
    word_v,
    w_ew,
    w_ee,
    w_key,
    w_value,
    out_hbm,
    gain_one,
    shift_one,
    up_hbm,
    down_hbm,
    gain_two,
    shift_two,
    head_w,
    gain_head,
    shift_head,
    hidden,
    qword,
    qent,
    keys,
    values,
    context,
    lse_out,
    resid_one,
    normed_out,
    active_hbm,
    slope_hbm,
    resid_two,
    layer_low,
    picked_out,
    head_pre_out,
    head_out,
    state_scr,
    normed_scr,
    out_w,
    up_w,
    down_w,
    active,
    slope,
    sems,
):
    loads = [
        pltpu.make_async_copy(source, target, sems.at[index])
        for index, (source, target) in enumerate(
            ((out_hbm, out_w), (up_hbm, up_w), (down_hbm, down_w))
        )
    ]
    words, width = word_states.shape
    word_loads = [
        pltpu.make_async_copy(source, target.at[pl.ds(0, words)], sems.at[12 + index])
        for index, (source, target) in enumerate(
            ((word_q, qword), (word_e, qent), (word_k, keys), (word_v, values))
        )
    ]
    for load in word_loads + loads:
        load.start()
    stage.need(0, 1, 5)
    seq_len = hidden.shape[0]
    slots = seq_len - words
    block = 128
    tall = seq_len
    halves = half_lanes(block)
    query_scale = HD ** (-0.5)
    state_scr[...] = dot_plain(entity_low[...], dense[...])
    hidden[:words] = word_states[...]
    hidden[words:] = state_scr[...].astype(jnp.bfloat16)

    stage.send(0)
    ents = hidden[words:]
    stage.need(10, 11, 12, 13)
    for target, weight, scale in (
        (qword, w_ew, query_scale),
        (qent, w_ee, query_scale),
        (keys, w_key, None),
        (values, w_value, None),
    ):
        value = dot_plain(ents, weight[...])
        if scale is not None:
            value = value * scale
        target[words:] = value.astype(jnp.bfloat16)
    for load in word_loads:
        load.wait()
    stage.send(1, 2, 3, 4)
    stage.need(2, 3)
    lse_out[...] = jnp.zeros_like(lse_out)

    def pair_step(pair, carry):
        lanes = pl.ds(pl.multiple_of(pair * block, block), block)
        key_pair = keys[:, lanes]
        value_pair = values[:, lanes]
        key_feat = [key_pair * halves[h] + feat_k[...] * halves[1 - h] for h in range(2)]
        value_only = [value_pair * halves[h] for h in range(2)]
        spot = lax.broadcasted_iota(jnp.int32, (1, block), 1) - 4 * pair

        def row_step(index, inner):
            at = pl.ds(pl.multiple_of(index * tall, block), tall)
            qw = qword[at, lanes]
            qe = qent[at, lanes]
            feats = feat_q[at]
            result = jnp.zeros((tall, block), jnp.float32)
            stats = lse_out[at]
            for h in range(2):
                left_w = qw * halves[h] + feats * halves[1 - h]
                left_e = qe * halves[h] + feats * halves[1 - h]
                scores = jnp.concatenate(
                    [
                        dot_right_t(left_w, key_feat[h][:words]),
                        dot_right_t(left_e, key_feat[h][words:]),
                    ],
                    axis=1,
                )
                top = jnp.max(scores, axis=1, keepdims=True)
                expo = jnp.exp(scores - top)
                total = jnp.sum(expo, axis=1, keepdims=True)
                prob = (expo * (1.0 / total)).astype(jnp.bfloat16)
                result += dot_plain(prob, value_only[h])
                stats = jnp.where(spot == h, top + jnp.log(total), stats)
            context[at, lanes] = result.astype(jnp.bfloat16)
            lse_out[at] = stats
            return inner

        lax.fori_loop(0, seq_len // tall, row_step, 0)
        return carry

    lax.fori_loop(0, width // block, pair_step, 0)

    stage.send(5)
    loads[0].wait()
    for begin, size in ((0, words // 2), (words // 2, words // 2), (words, slots)):
        at = slice(begin, begin + size)
        start = (
            state_scr[...] if begin == words else word_states[at].astype(jnp.float32)
        )
        value = start + dot_plain(context[at], out_w[...])
        resid_one[at] = value
        normed = norm_parts(value)[0] * gain_one[...][None, :] + shift_one[...][None, :]
        normed_scr[at] = normed
        normed_out[at] = normed.astype(jnp.bfloat16)
    stage.send(7, 8)
    loads[1].wait()
    loads[2].wait()
    span = seq_len
    stores = []

    for slot in range(down_w.shape[0] // width):
        cols = slice(slot * width, slot * width + width)

        def up_step(index, carry, cols=cols):
            at = pl.ds(pl.multiple_of(index * span, 16), span)
            result, change = gelu_parts(dot_plain(normed_out[at], up_w[:, cols]))
            active[at, cols] = result.astype(jnp.bfloat16)
            slope[at, cols] = change.astype(jnp.bfloat16)
            return carry

        lax.fori_loop(0, seq_len // span, up_step, 0)
        for index, (source, target) in enumerate(((active, active_hbm), (slope, slope_hbm))):
            stores.append(
                pltpu.make_async_copy(
                    source.at[:, cols], target.at[:, cols], sems.at[3 + 2 * slot + index]
                )
            )
            stores[-1].start()

    def down_step(index, carry):
        at = pl.ds(pl.multiple_of(index * span, 16), span)
        value = normed_scr[at] + dot_plain(active[at], down_w[...])
        resid_two[at] = value
        layer_low[at] = (norm_parts(value)[0] * gain_two[...][None, :] + shift_two[...][None, :]).astype(jnp.bfloat16)
        return carry

    lax.fori_loop(0, seq_len // span, down_step, 0)
    stage.send(11, 12)
    stage.need(21)
    picked = dot_plain(choose[...], layer_low[words:]).astype(jnp.bfloat16)
    picked_out[...] = picked
    head_pre = dot_plain(picked, head_w[...])
    head_pre_out[...] = head_pre
    raised = gelu_parts(head_pre)[0]
    head_out[...] = (norm_parts(raised)[0] * gain_head[...][None, :] + shift_head[...][None, :]).astype(jnp.bfloat16)
    for store in stores:
        store.wait()


def forward_pass(inputs):
    words, width = inputs[0].shape
    slots = inputs[1].shape[0]
    seq_len = words + slots
    hidden_units = inputs[17].shape[1]
    mask_count = inputs[4].shape[0]
    head_width = inputs[21].shape[1]
    low, full = jnp.bfloat16, jnp.float32
    vmem, hbm = pl.BlockSpec(memory_space=pltpu.VMEM), pl.BlockSpec(memory_space=pltpu.HBM)
    far = (6, 7, 8, 9, 14, 17, 18)
    shapes = [
        ((seq_len, width), low),
        ((seq_len, width), low),
        ((seq_len, width), low),
        ((seq_len, width), low),
        ((seq_len, width), low),
        ((seq_len, width), low),
        ((seq_len, 128), full),
        ((seq_len, width), full),
        ((seq_len, width), low),
        ((seq_len, hidden_units), low),
        ((seq_len, hidden_units), low),
        ((seq_len, width), full),
        ((seq_len, width), low),
        ((mask_count, width), low),
        ((mask_count, head_width), full),
        ((mask_count, head_width), low),
    ]
    outs = [jax.ShapeDtypeStruct(*shape) for shape in shapes]
    return staged_call(
        forward_kernel,
        inputs,
        outs,
        [hbm if index in far else vmem for index in range(len(inputs))],
        [hbm if index in (9, 10) else vmem for index in range(len(shapes))],
        (0, 1, 5, 10, 11, 12, 13, 2, 3, 21),
        (0, 1, 2, 3, 4, 5, 7, 8, 11, 12),
        [
            pltpu.VMEM((slots, width), full),
            pltpu.VMEM((seq_len, width), full),
            pltpu.VMEM(inputs[14].shape, low),
            pltpu.VMEM(inputs[17].shape, low),
            pltpu.VMEM(inputs[18].shape, low),
            pltpu.VMEM((seq_len, hidden_units), low),
            pltpu.VMEM((seq_len, hidden_units), low),
            pltpu.SemaphoreType.DMA((16,)),
        ],
        pltpu.CompilerParams(vmem_limit_bytes=63 * 2**20),
    )


class Grid:
    def __init__(self):
        me = lax.axis_index("dp")
        self.core = lax.rem(me, 2)
        self.square = lax.rem(lax.div(me, 2), 4)
        self.line = lax.div(me, 8)
        self.twin = me + 1 - 2 * self.core
        self.squares = []
        self.lines = []
        for step in range(1, 4):
            other = lax.rem(self.square + step, 4)
            self.squares.append((me + 2 * (other - self.square), other))
            other = lax.rem(self.line + step, 4)
            self.lines.append((me + 8 * (other - self.line), other))

    def greet(self):
        barrier = pltpu.get_barrier_semaphore()
        peers = [self.twin] + [peer for peer, _ in self.squares + self.lines]
        for peer in peers:
            pl.semaphore_signal(barrier, inc=1, device_id=(peer,), device_id_type=MESH_ID)
        pl.semaphore_wait(barrier, len(peers))


class Sender:
    def __init__(self, send_sem, recv_sem):
        self.send_sem, self.recv_sem, self.used = send_sem, recv_sem, 0

    def start(self, source, target, peer):
        slot = self.used
        self.used += 1
        copy = pltpu.make_async_remote_copy(
            src_ref=source,
            dst_ref=target,
            send_sem=self.send_sem.at[slot],
            recv_sem=self.recv_sem.at[slot],
            device_id=(peer,),
            device_id_type=MESH_ID,
        )
        copy.start()
        return copy


def wait_all(copies):
    for copy in copies:
        copy.wait()


def merge_stats(blocks):
    tops = [block[0] for block in blocks]
    top = functools.reduce(jnp.maximum, tops)
    total = sum(block[1] * jnp.exp(block[0] - top) for block in blocks)
    return top, total, sum(block[2] for block in blocks)


def head_kernel(
    grad_scale,
    head,
    table,
    bias,
    target_vecs,
    target_bias,
    table_grad,
    bias_grad,
    losses,
    total_loss,
    head_grad,
    heads,
    logits,
    expo,
    table_t,
    bias_col,
    part,
    land_pair,
    sum_pair,
    land_square,
    sum_square,
    land_line,
    stat,
    stat_pair,
    stat_square,
    stat_line,
    send_sem,
    recv_sem,
):
    grid = Grid()
    rows, wide = table.shape
    count = head.shape[0]
    total_mask = 32 * count
    grid.greet()
    sender = Sender(send_sem, recv_sem)
    line, square, core = grid.line, grid.square, grid.core
    flying = [sender.start(head, heads.at[line, square, core], peer) for peer, _ in grid.lines]
    heads[line, square, core] = head[...]

    def table_step(index, carry):
        at = pl.ds(pl.multiple_of(index * 128, 128), 128)
        table_t[:, at] = table[at].astype(jnp.float32).T.astype(jnp.bfloat16)
        return carry

    lax.fori_loop(0, rows // 128, table_step, 0)
    wait_all(flying)
    flying = [
        sender.start(heads.at[:, square, core], heads.at[:, square, core], peer)
        for peer, _ in grid.squares
    ]

    def bias_step(index, carry):
        at = pl.ds(pl.multiple_of(index * 128, 128), 128)
        bias_col[at] = jnp.broadcast_to(bias[:, at], (128, 128)).T
        return carry

    lax.fori_loop(0, rows // 128, bias_step, 0)
    wait_all(flying)
    sender.start(heads.at[:, :, core], heads.at[:, :, core], grid.twin).wait()

    all_heads = heads[...].reshape(total_mask, wide)
    slab = rows // 2

    def logit_step(index, carry):
        at = pl.ds(pl.multiple_of(index * slab, 16), slab)
        logits[at] = dot_right_t(table[at], all_heads)
        return carry

    lax.fori_loop(0, rows // slab, logit_step, 0)
    tile = 64
    wide_copies = total_mask // 128

    def value_at(index):
        at = pl.ds(pl.multiple_of(index * tile, tile), tile)
        shift = bias_col[at]
        return at, logits[at] + jnp.concatenate([shift] * wide_copies, axis=1)

    def top_step(index, top):
        at, value = value_at(index)
        return jnp.maximum(top, jnp.max(value.reshape(tile // 8, 8, total_mask), axis=0))

    top = lax.fori_loop(
        0, rows // tile, top_step, jnp.full((8, total_mask), -jnp.inf, jnp.float32)
    )
    top = jnp.max(top, axis=0, keepdims=True)

    def exp_step(index, total):
        at, value = value_at(index)
        value = jnp.exp(value - top)
        expo[at] = value.astype(jnp.bfloat16)
        return total + jnp.sum(value.reshape(tile // 8, 8, total_mask), axis=0)

    total = lax.fori_loop(0, rows // tile, exp_step, jnp.zeros((8, total_mask), jnp.float32))
    total = jnp.sum(total, axis=0, keepdims=True)

    def fold(row):
        return jnp.concatenate([row[:, i * 128 : i * 128 + 128] for i in range(wide_copies)], axis=0)

    def unfold(block):
        return jnp.concatenate([block[i : i + 1] for i in range(wide_copies)], axis=1)

    own_top, own_total = fold(top), fold(total)
    target = (
        jnp.sum(head[...].astype(jnp.float32) * target_vecs[...], axis=1, keepdims=True)
        + target_bias[:, 0:1]
    )
    own_target = jnp.broadcast_to(jnp.sum(target, axis=0, keepdims=True), own_top.shape)
    stat[0, 0], stat[0, 1], stat[0, 2] = own_top, own_total, own_target
    copy = sender.start(stat.at[0], stat_pair, grid.twin)
    quarter = total_mask // 4
    parts = [dot_plain(table_t[...], expo[:, :quarter])]
    copy.wait()
    stat[1, 0], stat[1, 1], stat[1, 2] = merge_stats(
        [(own_top, own_total, own_target), (stat_pair[0], stat_pair[1], stat_pair[2])]
    )
    stat_square[square] = stat[1]
    flying = [sender.start(stat.at[1], stat_square.at[square], peer) for peer, _ in grid.squares]
    parts.append(dot_plain(table_t[...], expo[:, quarter : 2 * quarter]))
    wait_all(flying)
    stat[2, 0], stat[2, 1], stat[2, 2] = merge_stats(
        [(stat_square[i, 0], stat_square[i, 1], stat_square[i, 2]) for i in range(4)]
    )
    stat_line[line] = stat[2]
    flying = [sender.start(stat.at[2], stat_line.at[line], peer) for peer, _ in grid.lines]
    parts.append(dot_plain(table_t[...], expo[:, 2 * quarter : 3 * quarter]))
    parts.append(dot_plain(table_t[...], expo[:, 3 * quarter :]))
    wait_all(flying)
    full_top, full_total, full_target = merge_stats(
        [(stat_line[i, 0], stat_line[i, 1], stat_line[i, 2]) for i in range(4)]
    )
    lse = full_top + jnp.log(full_total)
    all_lse = jnp.sum(jnp.sum(lse, axis=1, keepdims=True), axis=0, keepdims=True)
    total_loss[...] = (all_lse - full_target[0:1]) * grad_scale
    mine = lax.broadcasted_iota(jnp.int32, (count, total_mask), 0) + lax.axis_index("dp") * count
    hit = mine == lax.broadcasted_iota(jnp.int32, (count, total_mask), 1)
    own_lse = jnp.sum(jnp.where(hit, unfold(lse), 0.0), axis=1, keepdims=True)
    losses[...] = jnp.broadcast_to(own_lse - target, losses.shape)
    scale = unfold(jnp.exp(own_top - lse) * grad_scale)
    per = 128 // count
    for index in range(total_mask // 128):
        at = slice(index * 128, index * 128 + 128)
        source = parts[index * 128 // quarter]
        begin = index * 128 % quarter
        piece = (source[:, begin : begin + 128] * scale[:, at]).T.astype(jnp.bfloat16)
        for inner in range(per):
            owner = index * per + inner
            part[owner // 8, owner // 2 % 4, owner % 2] = piece[inner * count : inner * count + count]
    copy = sender.start(part.at[:, :, 1 - core], land_pair, grid.twin)

    scaled = []
    for index in range(total_mask // 128):
        at = slice(index * 128, index * 128 + 128)
        column = jnp.broadcast_to(scale[:, at], (128, 128)).T
        column = jnp.concatenate([column] * (wide // 128), axis=1)
        scaled.append((all_heads[at].astype(jnp.float32) * column).astype(jnp.bfloat16))
    scaled = jnp.concatenate(scaled, axis=0)
    slab = rows // 4

    def grad_part(index):
        at = slice(index * slab, index * slab + slab)
        table_grad[at] = dot_plain(expo[at], scaled)

    grad_part(0)
    copy.wait()
    sum_pair[...] = (part[:, :, core].astype(jnp.float32) + land_pair[...].astype(jnp.float32)).astype(
        jnp.bfloat16
    )
    flying = [
        sender.start(sum_pair.at[:, other], land_square.at[square], peer)
        for peer, other in grid.squares
    ]
    land_square[square] = sum_pair[:, square]
    grad_part(1)
    wait_all(flying)
    sum_square[...] = sum(land_square[i].astype(jnp.float32) for i in range(4)).astype(jnp.bfloat16)
    flying = [
        sender.start(sum_square.at[other], land_line.at[line], peer) for peer, other in grid.lines
    ]
    land_line[line] = sum_square[line]
    grad_part(2)
    high = scale.astype(jnp.bfloat16)
    low = (scale - high.astype(jnp.float32)).astype(jnp.bfloat16)
    both = jnp.concatenate(
        [high.astype(jnp.float32), low.astype(jnp.float32), jnp.zeros((14, total_mask), jnp.float32)],
        axis=0,
    ).astype(jnp.bfloat16)
    sums = dot_right_t(both, expo[...])
    bias_grad[...] = sums[0:1] + sums[1:2]
    grad_part(3)
    wait_all(flying)
    head_grad[...] = sum(land_line[i].astype(jnp.float32) for i in range(4))


def head_and_table(
    head_low, entity_table, bias_row, target_vecs, target_bias, grad_scale, collective_id
):
    count, wide = head_low.shape
    rows = entity_table.shape[0]
    total_mask = 32 * count
    low, full = jnp.bfloat16, jnp.float32
    vmem = pl.BlockSpec(memory_space=pltpu.VMEM)
    folded = (total_mask // 128, 128)
    return pl.pallas_call(
        functools.partial(head_kernel, grad_scale),
        out_shape=[
            jax.ShapeDtypeStruct((rows, wide), full),
            jax.ShapeDtypeStruct((1, rows), full),
            jax.ShapeDtypeStruct((count, 128), full),
            jax.ShapeDtypeStruct((1, 128), full),
            jax.ShapeDtypeStruct((count, wide), full),
        ],
        in_specs=[vmem] * 5,
        out_specs=[vmem] * 5,
        scratch_shapes=[
            pltpu.VMEM((4, 4, 2, count, wide), low),
            pltpu.VMEM((rows, total_mask), full),
            pltpu.VMEM((rows, total_mask), low),
            pltpu.VMEM((wide, rows), low),
            pltpu.VMEM((rows, 128), full),
            pltpu.VMEM((4, 4, 2, count, wide), low),
            pltpu.VMEM((4, 4, count, wide), low),
            pltpu.VMEM((4, 4, count, wide), low),
            pltpu.VMEM((4, 4, count, wide), low),
            pltpu.VMEM((4, count, wide), low),
            pltpu.VMEM((4, count, wide), low),
            pltpu.VMEM((3, 3) + folded, full),
            pltpu.VMEM((3,) + folded, full),
            pltpu.VMEM((4, 3) + folded, full),
            pltpu.VMEM((4, 3) + folded, full),
            pltpu.SemaphoreType.DMA((24,)),
            pltpu.SemaphoreType.DMA((24,)),
        ],
        compiler_params=pltpu.CompilerParams(
            collective_id=collective_id, has_side_effects=True, vmem_limit_bytes=63 * 2**20
        ),
    )(head_low, entity_table, bias_row, target_vecs, target_bias)


def norm_slope(value, given, gain):
    scaled, rate = norm_parts(value)
    back = given * gain
    mean_back = jnp.mean(back, axis=-1, keepdims=True)
    mean_both = jnp.mean(back * scaled, axis=-1, keepdims=True)
    grad = rate * (back - mean_back - scaled * mean_both)
    return (
        grad,
        jnp.sum(given * scaled, axis=0, keepdims=True),
        jnp.sum(given, axis=0, keepdims=True),
    )


def split_low(value):
    high = value.astype(jnp.bfloat16)
    return high, (value - high.astype(jnp.float32)).astype(jnp.bfloat16)


def place_rows(source, order, count, store):
    owners = 2 ** len(order)
    for pair in range(owners // 2):
        one, two = place_owner(order, 2 * pair), place_owner(order, 2 * pair + 1)
        both = jnp.concatenate(
            [source[one * count : one * count + count], source[two * count : two * count + count]],
            axis=0,
        )
        store(slice(pair * 2 * count, (pair + 1) * 2 * count), both.astype(jnp.bfloat16))


def middle_back_kernel(
    orders,
    grad_scale,
    stage,
    head_grad,
    target_vecs,
    head_pre,
    gain_head,
    picked,
    head_w,
    choose,
    cotangent,
    resid_two,
    gain_two,
    normed_low,
    resid_one,
    gain_one,
    out_w,
    context,
    lse_lanes,
    active_hbm,
    slope_hbm,
    up_hbm,
    down_hbm,
    up_a,
    up_b,
    head_a,
    out_b,
    down_b,
    up_c,
    down_c,
    first_grad,
    context_grad,
    lse_delta,
    vectors,
    active,
    slope,
    up_w,
    down_w,
    flip,
    normed_t,
    context_t,
    down_in,
    acc,
    up_low,
    stage_a,
    stage_c,
    sems,
):
    seq_len, width = cotangent.shape
    slots = choose.shape[1]
    words = seq_len - slots
    cuts = down_w.shape[0] // width
    loads = []
    for index, (source, target) in enumerate(
        ((active_hbm, active), (down_hbm, down_w), (slope_hbm, slope), (up_hbm, up_w))
    ):
        for cut in range(cuts):
            at = pl.ds(cut * width, width)
            view = (at,) if index == 1 else (slice(None), at)
            loads.append(
                pltpu.make_async_copy(source.at[view], target.at[view], sems.at[index * cuts + cut])
            )
    for cut in range(cuts):
        for index in range(4):
            loads[index * cuts + cut].start()

    given = head_grad[...] - grad_scale * target_vecs[...]
    pre = head_pre[...]
    raised, change = gelu_parts(pre)
    back, gain_sum, bias_sum = norm_slope(raised, given, gain_head[...][None, :])
    sums = [gain_sum, bias_sum]
    pre_low = (back * change).astype(jnp.bfloat16)
    head_weight_grad = dot_left_t(picked[...], pre_low)
    count = width // 2 ** len(orders[0])

    def keep_head(at, value):
        head_a[0, at] = value

    flip[:, : head_a.shape[2]] = head_weight_grad
    place_rows(flip[:, : head_a.shape[2]], orders[0], count, keep_head)
    stage.need(5)
    picked_high, picked_rest = split_low(dot_right_t(pre_low, head_w[...]))
    placed = dot_left_t(choose[...], picked_high) + dot_left_t(choose[...], picked_rest)

    stage.need(7, 8)
    block = 128
    total_gain = jnp.zeros((1, width), jnp.float32)
    total_bias = jnp.zeros((1, width), jnp.float32)
    for begin in range(0, seq_len, block):
        at = slice(begin, begin + block)
        given = cotangent[at].astype(jnp.float32)
        if begin >= words:
            given = given + placed[begin - words : begin - words + block]
        grad, gain_sum, bias_sum = norm_slope(resid_two[at], given, gain_two[...][None, :])
        total_gain += gain_sum
        total_bias += bias_sum
        acc[at] = grad
        down_in[at] = grad.astype(jnp.bfloat16)
    sums += [total_gain, total_bias]

    def flip_into(source, target, order_list):
        def flip_step(index, carry):
            at = pl.ds(pl.multiple_of(index * block, block), block)
            flip[at] = source[:, at].astype(jnp.float32).T
            return carry

        lax.fori_loop(0, width // block, flip_step, 0)
        for slot, order in enumerate(order_list):

            def keep(at, value, slot=slot):
                target[slot, at] = value

            place_rows(flip, order, count, keep)

    stage.need(10, 14)
    flip_into(normed_low, normed_t, (orders[0], orders[2]))
    flip_into(context, context_t, (orders[1],))

    column = 384
    span = seq_len
    block_two = seq_len // 2
    split = down_b.shape[2]
    owners = 2 ** len(orders[0])
    tall = down_w.shape[0] // owners
    spots = [
        {place_owner(order, place): place for place in range(owners)}
        for order in (orders[1], orders[2])
    ]
    stores = []
    for cut in range(cuts):
        at = slice(cut * width, cut * width + width)
        for index in range(4):
            loads[index * cuts + cut].wait()
        for begin in range(0, width, column):
            piece = dot_left_t(active[:, at], down_in[:, begin : begin + column])
            for inner in range(width // tall):
                owner = cut * (width // tall) + inner
                rows = piece[inner * tall : inner * tall + tall].astype(jnp.bfloat16)
                stop = min(begin + column, split)
                if begin < split:
                    place = spots[0][owner] * tall
                    stage_a[place : place + tall, begin:stop] = rows[:, : stop - begin]
                if begin + column > split:
                    start = max(begin, split)
                    place = spots[1][owner] * tall
                    stage_c[place : place + tall, start - split : begin + column - split] = rows[
                        :, start - begin :
                    ]

        def back_step(index, carry, at=at):
            rows = pl.ds(pl.multiple_of(index * span, 16), span)
            grad = dot_right_t(down_in[rows], down_w[at]) * slope[rows, at].astype(jnp.float32)
            grad = grad.astype(jnp.bfloat16)
            up_low[rows] = grad
            acc[rows] = acc[rows] + dot_right_t(grad, up_w[:, at])
            return carry

        lax.fori_loop(0, seq_len // span, back_step, 0)
        target, slot, order_slot = ((up_a, 0, 0), (up_a, 1, 0), (up_b, 0, 0), (up_c, 0, 1))[cut]
        for begin in range(0, width, column):
            target[slot, :, begin : begin + column] = dot_plain(
                normed_t[order_slot], up_low[:, begin : begin + column]
            ).astype(jnp.bfloat16)
    stage.send(0, 1, 5)
    stage.need(11, 13)
    stores = [
        pltpu.make_async_copy(stage_a, down_b.at[0], sems.at[4 * cuts]),
        pltpu.make_async_copy(stage_c, down_c.at[0], sems.at[4 * cuts + 1]),
    ]
    for store in stores:
        store.start()

    total_gain = jnp.zeros((1, width), jnp.float32)
    total_bias = jnp.zeros((1, width), jnp.float32)
    row = lax.broadcasted_iota(jnp.int32, (width, 128), 0)
    lane = lax.broadcasted_iota(jnp.int32, (width, 128), 1)
    spot = 4 * lax.div(row, 128) + 2 + lax.div(lax.rem(row, 128), HD)
    pick = (spot == lane).astype(jnp.float32).astype(jnp.bfloat16)
    for begin in range(0, seq_len, block_two):
        at = slice(begin, begin + block_two)
        grad, gain_sum, bias_sum = norm_slope(resid_one[at], acc[at], gain_one[...][None, :])
        total_gain += gain_sum
        total_bias += bias_sum
        first_grad[at] = grad
        low = grad.astype(jnp.bfloat16)
        down_in[at] = low
        back = dot_right_t(low, out_w[...]).astype(jnp.bfloat16)
        context_grad[at] = back
        high, rest = split_low(back.astype(jnp.float32) * context[at].astype(jnp.float32))
        lse_delta[at] = lse_lanes[at] + dot_plain(high, pick) + dot_plain(rest, pick)
    stage.send(7, 8)
    sums += [total_gain, total_bias]
    tall, room = vectors.shape[1:]
    every = tall // owners
    placed = jnp.zeros((tall, room), jnp.float32)
    offset = 0
    for vector in sums:
        size = vector.shape[1]
        per = size // owners
        row = lax.broadcasted_iota(jnp.int32, (tall, size), 0)
        place = lax.div(row, every)
        owner = jnp.zeros((tall, size), jnp.int32)
        for spot, mask in enumerate(orders[0]):
            owner += lax.rem(lax.div(place, 2 ** (len(orders[0]) - 1 - spot)), 2) * mask
        column_at = lax.broadcasted_iota(jnp.int32, (tall, size), 1)
        mine = (lax.div(column_at, per) == owner) & (lax.rem(row, every) == 0)
        spread = jnp.where(mine, vector, 0.0).astype(jnp.bfloat16)
        source = lax.broadcasted_iota(jnp.int32, (size, room), 0)
        target = lax.broadcasted_iota(jnp.int32, (size, room), 1)
        move = (lax.rem(source, per) + offset == target).astype(jnp.float32).astype(jnp.bfloat16)
        placed += dot_plain(spread, move)
        offset += per
    vectors[0] = placed.astype(jnp.bfloat16)
    for begin in range(0, width, column):
        out_b[0, :, begin : begin + column] = dot_plain(
            context_t[0], down_in[:, begin : begin + column]
        ).astype(jnp.bfloat16)
    for store in stores:
        store.wait()


DOWN_SPLIT = 512


def middle_back(inputs, orders, grad_scale):
    seq_len, width = inputs[7].shape
    hidden_units = inputs[16].shape[1]
    head_width = inputs[0].shape[1]
    low, full = jnp.bfloat16, jnp.float32
    cuts = hidden_units // width
    vmem, hbm = pl.BlockSpec(memory_space=pltpu.VMEM), pl.BlockSpec(memory_space=pltpu.HBM)
    shapes = [
        ((2, width, width), low),
        ((1, width, width), low),
        ((1, width, head_width), low),
        ((1, width, width), low),
        ((1, hidden_units, DOWN_SPLIT), low),
        ((1, width, width), low),
        ((1, hidden_units, width - DOWN_SPLIT), low),
        ((seq_len, width), full),
        ((seq_len, width), low),
        ((seq_len, 128), full),
        ((1, 8 * 2 ** len(orders[0]), 256), low),
    ]
    outs = [jax.ShapeDtypeStruct(*shape) for shape in shapes]
    return staged_call(
        functools.partial(middle_back_kernel, orders, grad_scale),
        inputs,
        outs,
        [vmem] * 16 + [hbm] * 4,
        [hbm if index in (4, 6) else vmem for index in range(len(shapes))],
        (5, 7, 8, 10, 14, 11, 13),
        (0, 1, 3, 5, 7, 8),
        [
            pltpu.VMEM((seq_len, hidden_units), low),
            pltpu.VMEM((seq_len, hidden_units), low),
            pltpu.VMEM((width, hidden_units), low),
            pltpu.VMEM((hidden_units, width), low),
            pltpu.VMEM((width, seq_len), full),
            pltpu.VMEM((2, width, seq_len), low),
            pltpu.VMEM((1, width, seq_len), low),
            pltpu.VMEM((seq_len, width), low),
            pltpu.VMEM((seq_len, width), full),
            pltpu.VMEM((seq_len, width), low),
            pltpu.VMEM((hidden_units, DOWN_SPLIT), low),
            pltpu.VMEM((hidden_units, width - DOWN_SPLIT), low),
            pltpu.SemaphoreType.DMA((4 * cuts + 2,)),
        ],
        pltpu.CompilerParams(vmem_limit_bytes=63 * 2**20),
    )


def last_kernel(grad_scale, codes, back, table_hbm, bias_in, *refs):
    sums, refs = refs[:SUMS], refs[SUMS:]
    table_out, bias_out = refs[:2]
    outs, refs = refs[2 : 2 + SUMS - 3], refs[2 + SUMS - 3 :]
    table_in, result, sems, move_sems = refs
    rows = table_hbm.shape[0]
    entries = back.shape[0]
    step = 1024
    parts = [(begin, min(step, rows - begin)) for begin in range(0, rows, step)]
    loads = [
        pltpu.make_async_copy(
            table_hbm.at[pl.ds(begin, size)], table_in.at[pl.ds(begin, size)], sems.at[0, index]
        )
        for index, (begin, size) in enumerate(parts)
    ]
    stores = [
        pltpu.make_async_copy(
            result.at[pl.ds(begin, size)], table_out.at[pl.ds(begin, size)], sems.at[1, index]
        )
        for index, (begin, size) in enumerate(parts)
    ]
    for load in loads:
        load.start()
    up_two, down_a, up_last, down_b, up_third = sums[:5]
    up_out, down_out = outs[:2]
    width = up_last.shape[2]
    pairs = [
        (value, up_out.at[:, pl.ds(index * width, width)])
        for index, value in enumerate((up_two.at[0], up_two.at[1], up_third.at[0], up_last.at[0]))
    ]
    pairs.append((down_a.at[0], down_out.at[:, pl.ds(0, down_a.shape[2])]))
    pairs.append((down_b.at[0], down_out.at[:, pl.ds(down_a.shape[2], down_b.shape[2])]))
    pairs += [(source.at[0], target) for source, target in zip(sums[5:], outs[2:])]
    moves = [
        pltpu.make_async_copy(source, target, move_sems.at[index])
        for index, (source, target) in enumerate(pairs)
    ]
    for move in moves:
        move.start()
    code = codes[0:1]
    target = (code >= rows).astype(jnp.float32)
    flags = jnp.broadcast_to(target, (16, entries)).astype(jnp.bfloat16)
    code = jnp.where(code >= rows, code - rows, code)
    for index, (begin, size) in enumerate(parts):
        row = lax.broadcasted_iota(jnp.int32, (size, entries), 0) + begin
        match = (row == code).astype(jnp.float32).astype(jnp.bfloat16)
        at = slice(begin, begin + size)
        counts = dot_right_t(flags, match)
        bias_out[:, at] = bias_in[:, at] - grad_scale * counts[0:1]
        added = dot_plain(match, back[...])
        loads[index].wait()
        result[at] = table_in[at] + added
        stores[index].start()
    for copy in stores + moves:
        copy.wait()


SUMS = 15


def last_step(codes, back, table_grad, bias_grad, sums, grad_scale):
    vmem, hbm = pl.BlockSpec(memory_space=pltpu.VMEM), pl.BlockSpec(memory_space=pltpu.HBM)
    full = jnp.float32
    up_rows, width = sums[0].shape[1:]
    down_rows = sums[1].shape[1]
    shapes = [
        table_grad.shape,
        bias_grad.shape,
        (up_rows, 4 * width),
        (down_rows, width),
    ] + [value.shape[1:] for value in sums[5:]]
    return pl.pallas_call(
        functools.partial(last_kernel, grad_scale),
        out_shape=[jax.ShapeDtypeStruct(shape, full) for shape in shapes],
        in_specs=[vmem, vmem, hbm, vmem] + [vmem] * len(sums),
        out_specs=[hbm, vmem] + [hbm] * (len(shapes) - 2),
        scratch_shapes=[
            pltpu.VMEM(table_grad.shape, full),
            pltpu.VMEM(table_grad.shape, full),
            pltpu.SemaphoreType.DMA((2, 8)),
            pltpu.SemaphoreType.DMA((len(sums) + 1,)),
        ],
        compiler_params=pltpu.CompilerParams(vmem_limit_bytes=63 * 2**20),
    )(codes, back, table_grad, bias_grad, *sums)


def place_owner(order, place):
    bits = len(order)
    return sum(((place >> (bits - 1 - spot)) & 1) * mask for spot, mask in enumerate(order))


class Piece:
    def __init__(
        self, rows, stages, send, own, land, tail, pack, tail_land, out, send_sem, recv_sem
    ):
        self.rows, self.stages = rows, stages
        self.send, self.own, self.land = send, own, land
        self.tail, self.pack, self.tail_land, self.out = tail, pack, tail_land, out
        self.send_sem, self.recv_sem = send_sem, recv_sem
        self.sizes = [rows * 2 ** (stages - 1 - stage) for stage in range(stages)]
        self.spots = [sum(self.sizes[:stage]) for stage in range(stages)]

    def copy(self, stage, partner, bit):
        size = self.sizes[stage]
        away = (1 - bit) * size
        if stage < self.stages - 1:
            away = pl.multiple_of(away, 16)
        if stage == 0:
            source, target = self.send.at[:, pl.ds(away, size)], self.land.at[:, pl.ds(0, size)]
        elif stage < self.stages - 1:
            spot = pl.multiple_of(self.spots[stage - 1] + away, 16)
            source = self.land.at[:, pl.ds(spot, size)]
            target = self.land.at[:, pl.ds(self.spots[stage], size)]
        else:
            source, target = self.pack, self.tail_land
        return pltpu.make_async_remote_copy(
            src_ref=source,
            dst_ref=target,
            send_sem=self.send_sem.at[stage],
            recv_sem=self.recv_sem.at[stage],
            device_id=(partner,),
            device_id_type=MESH_ID,
        )

    def held(self, stage, bit):
        size = self.sizes[stage]
        if stage == 0 and self.own is not None:
            return self.own, 0
        if stage == 0:
            return self.send, pl.multiple_of(bit * size, 16)
        return self.land, pl.multiple_of(self.spots[stage - 1] + bit * size, 16)

    def add(self, stage, bit, half_index):
        size = self.sizes[stage]
        half = size // 2
        unit = 48 if half % 48 == 0 else 16
        start = half_index * half
        source, base = self.held(stage, bit)
        for slot in range(self.land.shape[0]):

            def step(index, carry, slot=slot):
                row = pl.multiple_of(start + index * unit, 16)
                mine = source[slot, pl.ds(pl.multiple_of(base + row, 16), unit)]
                spot = pl.ds(pl.multiple_of(self.spots[stage] + row, 16), unit)
                theirs = self.land[slot, spot]
                total = mine.astype(jnp.float32) + theirs.astype(jnp.float32)
                self.land[slot, spot] = total.astype(jnp.bfloat16)
                return carry

            lax.fori_loop(0, half // unit, step, 0)

    def add_tail(self, stage, bit, following):
        size = self.sizes[stage]
        half = size // 2
        middle = self.land.shape[2] // 2
        source, base = self.held(stage, bit)
        for slot in range(self.land.shape[0]):
            mine = source[slot, pl.ds(base, size)]
            theirs = self.land[slot, pl.ds(self.spots[stage], size)]
            self.tail[slot] = mine.astype(jnp.float32) + theirs.astype(jnp.float32)
            other = self.tail[slot, pl.ds(pl.multiple_of((1 - following) * half, 8), half)]
            self.pack[slot] = jnp.concatenate(
                [other[:, :middle], other[:, middle:]], axis=0
            ).astype(jnp.bfloat16)

    def finish(self, bit):
        size = self.sizes[-1]
        for slot in range(self.out.shape[0]):
            mine = self.tail[slot, pl.ds(pl.multiple_of(bit * size, 8), size)]
            theirs = self.tail_land[slot].astype(jnp.float32)
            self.out[slot] = mine + jnp.concatenate([theirs[:size], theirs[size:]], axis=1)


class Stream:
    def __init__(self, order, partner_of, pieces):
        self.order, self.partner_of, self.pieces = order, partner_of, pieces
        self.stages = len(order)

    def launch(self, stage):
        partner, bit = self.partner_of[self.order[stage]]
        for piece in self.pieces:
            piece.copy(stage, partner, bit).start()

    def advance(self, stage):
        partner, bit = self.partner_of[self.order[stage]]
        for piece in self.pieces:
            piece.copy(stage, partner, bit).wait()
        if stage == self.stages - 1:
            for piece in self.pieces:
                piece.finish(bit)
        elif stage == self.stages - 2:
            for piece in self.pieces:
                piece.add_tail(stage, bit, self.partner_of[self.order[stage + 1]][1])
            self.launch(stage + 1)
        else:
            following = self.partner_of[self.order[stage + 1]][1]
            for piece in self.pieces:
                piece.add(stage, bit, 1 - following)
            self.launch(stage + 1)
            for piece in self.pieces:
                piece.add(stage, bit, following)


def partners(me, masks):
    result = {}
    for mask in masks:
        bit = lax.rem(lax.div(me, mask), 2)
        result[mask] = (me + mask - 2 * mask * bit, bit)
    return result


EARLY = (
    (0, 2, 24, 768),
    (1, 1, 96, 512),
    (2, 1, 24, 768),
    (3, 1, 96, 256),
    (4, 1, 24, 768),
    (4, 1, 24, 256),
    (4, 1, 8, 256),
    (5, 1, 24, 768),
)
LATE = (
    (6, 1, 24, 768),
    (7, 1, 24, 768),
    (8, 1, 24, 768),
    (9, 1, 24, 768),
    (10, 1, 24, 768),
    (11, 1, 24, 768),
    (11, 1, 8, 768),
)
STREAM_ORDER = (0, 1, 2, 2, 0, 1, 1, 1, 2, 1, 0, 0)

WORD_POINTS = ("word0", "word1")

PLAN = {('p', 0): ((0, 0),), ('r', 1): ((1, 0), (2, 0)), ('p', 1): ((3, 0),), ('r', 2): ((4, 0), (5, 0)), ('r', 3): ((2, 1), (0, 1)), ('p', 4): ((3, 1),), ('r', 5): ((1, 1), (4, 1), (2, 2)), 'KV': ((5, 1),), 'ent': ((3, 2), (6, 0), (7, 0)), 'we': ((8, 0), (0, 2)), 'word0': ((1, 2), (9, 0), (2, 3), (10, 0)), 'word1': ((11, 0), (4, 2), (5, 2)), 'end': ((3, 3), (8, 1), (6, 1), (0, 3), (10, 1), (1, 3), (7, 1), (4, 3), (5, 3), (11, 1), (8, 2), (9, 1), (2, 4), (0, 4), (3, 4), (6, 2), (1, 4), (4, 4), (10, 2), (7, 2), (5, 4), (8, 3), (6, 3), (10, 3), (11, 2), (9, 2), (8, 4), (7, 3), (6, 4), (10, 4), (11, 3), (9, 3), (7, 4), (11, 4), (9, 4))}


def piece_scratch(spec, stages, source, own):
    _, slots, rows, width = spec
    owners = 2**stages
    shapes = []
    if source:
        shapes.append(pltpu.VMEM((slots, rows * owners, width), jnp.bfloat16))
    if own:
        shapes.append(pltpu.VMEM((slots, rows * owners // 2, width), jnp.bfloat16))
    shapes += [
        pltpu.VMEM((slots, rows * (owners - 2), width), jnp.bfloat16),
        pltpu.VMEM((slots, 2 * rows, width), jnp.float32),
        pltpu.VMEM((slots, 2 * rows, width // 2), jnp.bfloat16),
        pltpu.VMEM((slots, 2 * rows, width // 2), jnp.bfloat16),
        pltpu.SemaphoreType.DMA((stages,)),
        pltpu.SemaphoreType.DMA((stages,)),
    ]
    return shapes


def attention_back_kernel(orders, grad_scale, *refs):
    stages = len(orders[0])
    refs = list(refs)

    def take(count):
        taken = refs[:count]
        del refs[:count]
        return taken

    early_send = take(len(EARLY))
    (hidden, qword, qent, keys, values, cgrad, feat_q, feat_k, lse_delta, first_grad, head_low, slot_row) = take(12)
    (w_ww, w_we, w_ew, w_ee, w_key, w_value, dense, entity_low) = take(8)
    early_out = take(len(EARLY))
    late_out = take(len(LATE))
    words_out, request_out = take(2)
    devices = request_out.shape[0]
    early_pieces = []
    own_copies = []
    me = lax.axis_index("dp")
    partner_of = partners(me, orders[0])
    own_sem = refs.pop()
    request_sems = refs.pop()
    request_send = refs.pop()
    word_weights = []
    dqw, dqe, dkey, dvalue, prob_s, grad_s, flip, hidden_t, hidden_te, entity_t = refs[-10:]
    del refs[-10:]
    pieces = [[] for _ in STREAM_ORDER]
    early_flat = []
    for index, spec in enumerate(EARLY):
        own, land, tail, pack, tail_land, send_sem, recv_sem = take(7)
        piece = Piece(
            spec[2], stages, early_send[index], own, land, tail, pack, tail_land,
            early_out[index], send_sem, recv_sem,
        )
        pieces[spec[0]].append(piece)
        early_flat.append(piece)
        bit = partner_of[orders[STREAM_ORDER[spec[0]]][0]][1]
        size = spec[2] * 2 ** (stages - 1)
        own_copies.append(
            pltpu.make_async_copy(
                early_send[index].at[:, pl.ds(pl.multiple_of(bit * size, 16), size)],
                own,
                own_sem.at[index],
            )
        )
    late_source = []
    for index, spec in enumerate(LATE):
        source, land, tail, pack, tail_land, send_sem, recv_sem = take(7)
        late_source.append(source)
        pieces[spec[0]].append(
            Piece(
                spec[2], stages, source, None, land, tail, pack, tail_land,
                late_out[index], send_sem, recv_sem,
            )
        )
    spare = (early_flat[1].own, early_flat[3].own)
    split = spare[0].shape[2]
    for index, weight in enumerate((w_ww, w_we)):
        rows = weight.shape[0]
        for part, at in enumerate((pl.ds(0, split), pl.ds(split, weight.shape[1] - split))):
            word_weights.append(
                pltpu.make_async_copy(
                    weight.at[:, at],
                    spare[part].at[0, pl.ds(index * rows, rows)],
                    own_sem.at[len(EARLY) + 2 * index + part],
                )
            )
    streams = [
        Stream(orders[order], partner_of, pieces[index])
        for index, order in enumerate(STREAM_ORDER)
    ]
    first_late = LATE[0][0]

    def go_on(point):
        for index, stage in PLAN.get(point, ()):
            if stage == 0 and index < first_late:
                for piece, spec in enumerate(EARLY):
                    if spec[0] == index:
                        own_copies[piece].wait()
            streams[index].advance(stage)
            if stage == 0 and index in (1, 3):
                for copy in word_weights[(index - 1) // 2 :: 2]:
                    copy.start()

    greet_all(me, devices)
    for stream in streams[:first_late]:
        stream.launch(0)
    for copy in own_copies:
        copy.start()

    width = hidden.shape[1]
    seq_len = hidden.shape[0]
    words = words_out.shape[0]
    block = 128
    tall = seq_len // 2
    taller = words // len(WORD_POINTS)
    lane = lax.broadcasted_iota(jnp.int32, (1, block), 1)
    low_half = (lane < HD).astype(jnp.float32).astype(jnp.bfloat16)
    high_half = (lane >= HD).astype(jnp.float32).astype(jnp.bfloat16)
    halves = (low_half, high_half)

    def flip_step(index, carry):
        at = pl.ds(pl.multiple_of(index * block, block), block)
        flip[at] = hidden[:, at].astype(jnp.float32).T
        return carry

    lax.fori_loop(0, width // block, flip_step, 0)
    owners = 2**stages
    rows = width // owners
    for slot, order in enumerate(orders):
        begin = words if slot == 2 else 0
        for pair in range(owners // 2):
            one, two = place_owner(order, 2 * pair), place_owner(order, 2 * pair + 1)
            both = jnp.concatenate(
                [flip[one * rows : one * rows + rows, begin:], flip[two * rows : two * rows + rows, begin:]],
                axis=0,
            ).astype(jnp.bfloat16)
            if slot == 2:
                hidden_te[pair * 2 * rows : (pair + 1) * 2 * rows] = both
            else:
                hidden_t[slot, pair * 2 * rows : (pair + 1) * 2 * rows] = both

    go_on("start")

    def go_on_in_loop(name, pair):
        for point in range(width // block):
            if (name, point) in PLAN:
                pl.when(pair == point)(functools.partial(go_on, (name, point)))

    def pair_step(pair, carry):
        lanes = pl.ds(pl.multiple_of(pair * block, block), block)
        key_pair = keys[:, lanes]
        value_pair = values[:, lanes]
        key_feat = [key_pair * halves[h] + feat_k[...] * halves[1 - h] for h in range(2)]
        key_only = [key_pair * halves[h] for h in range(2)]
        value_only = [value_pair * halves[h] for h in range(2)]

        def row_step(index, inner):
            at = pl.ds(pl.multiple_of(index * tall, 16), tall)
            qw = qword[at, lanes]
            qe = qent[at, lanes]
            feats = feat_q[at]
            given = cgrad[at, lanes]
            stats = lse_delta[at]
            spot = lax.broadcasted_iota(jnp.int32, (1, block), 1) - 4 * pair
            total_w = jnp.zeros((tall, block), jnp.float32)
            total_e = jnp.zeros((tall, block), jnp.float32)
            for h in range(2):
                left_w = qw * halves[h] + feats * halves[1 - h]
                left_e = qe * halves[h] + feats * halves[1 - h]
                scores = jnp.concatenate(
                    [
                        dot_right_t(left_w, key_feat[h][:words]),
                        dot_right_t(left_e, key_feat[h][words:]),
                    ],
                    axis=1,
                )
                prob = jnp.exp(scores - jnp.sum(jnp.where(spot == h, stats, 0.0), axis=1, keepdims=True))
                pgrad = dot_right_t(given, value_only[h])
                sgrad = (prob * (pgrad - jnp.sum(jnp.where(spot == 2 + h, stats, 0.0), axis=1, keepdims=True))).astype(jnp.bfloat16)
                prob_s[h, at] = prob.astype(jnp.bfloat16)
                grad_s[h, at] = sgrad
                total_w += dot_plain(sgrad[:, :words], key_only[h][:words])
                total_e += dot_plain(sgrad[:, words:], key_only[h][words:])
            dqw[at, lanes] = total_w.astype(jnp.bfloat16)
            dqe[at, lanes] = total_e.astype(jnp.bfloat16)
            return inner

        lax.fori_loop(0, seq_len // tall, row_step, 0)
        go_on_in_loop("r", pair)
        qw_all, qe_all, given_all = qword[:, lanes], qent[:, lanes], cgrad[:, lanes]
        dkey[:words, lanes] = (
            dot_left_t(grad_s[0, :, :words], qw_all * halves[0])
            + dot_left_t(grad_s[1, :, :words], qw_all * halves[1])
        ).astype(jnp.bfloat16)
        dkey[words:, lanes] = (
            dot_left_t(grad_s[0, :, words:], qe_all * halves[0])
            + dot_left_t(grad_s[1, :, words:], qe_all * halves[1])
        ).astype(jnp.bfloat16)
        dvalue[:, lanes] = (
            dot_left_t(prob_s[0], given_all * halves[0])
            + dot_left_t(prob_s[1], given_all * halves[1])
        ).astype(jnp.bfloat16)

        go_on_in_loop("p", pair)
        return carry

    lax.fori_loop(0, width // block, pair_step, 0)

    query_scale = HD ** (-0.5)
    column = 384

    def weight_grad(source, slot, order_slot, grad, begin, end, scale):
        for cut in range(0, width, column):
            left = hidden_te[...] if order_slot == 2 else hidden_t[order_slot, :, begin:end]
            piece = dot_plain(left, grad[begin:end, cut : cut + column])
            if scale:
                piece = piece * query_scale
            source[slot, :, cut : cut + column] = piece.astype(jnp.bfloat16)

    weight_grad(late_source[0], 0, 1, dkey, 0, seq_len, False)
    streams[6].launch(0)
    weight_grad(late_source[1], 0, 1, dvalue, 0, seq_len, False)
    streams[7].launch(0)
    go_on("KV")
    weight_grad(late_source[2], 0, 2, dqw, words, seq_len, True)
    streams[8].launch(0)
    go_on("ew")
    weight_grad(late_source[3], 0, 1, dqe, words, seq_len, True)
    streams[9].launch(0)
    go_on("ee")
    weight_grad(late_source[4], 0, 0, dqw, 0, words, True)
    streams[10].launch(0)
    go_on("ww")

    def data_grad(begin, size, queries):
        at = pl.ds(begin, size)
        return (
            first_grad[at]
            + query_scale * queries(at)
            + dot_right_t(dkey[at], w_key[...])
            + dot_right_t(dvalue[at], w_value[...])
        )

    def entity_queries(at):
        return dot_right_t(dqw[at], w_ew[...]) + dot_right_t(dqe[at], w_ee[...])

    def word_queries(at):
        total = 0.0
        for index, grad in enumerate((dqw, dqe)):
            rows_at = pl.ds(index * width, width)
            total += dot_right_t(grad[at, :split], spare[0][0, rows_at])
            total += dot_right_t(grad[at, split:], spare[1][0, rows_at])
        return total

    state_low = data_grad(words, seq_len - words, entity_queries).astype(jnp.bfloat16)
    vectors = jnp.concatenate(
        [dot_right_t(state_low, dense[...]).astype(jnp.bfloat16), (head_low[...].astype(jnp.float32) * -grad_scale).astype(jnp.bfloat16)], axis=0
    )
    entries = slot_row.shape[1]
    wanted = lax.broadcasted_iota(jnp.int32, (vectors.shape[0], entries), 0)
    placing = (wanted == slot_row[0:1]).astype(jnp.float32).astype(jnp.bfloat16)
    per_request = dot_left_t(placing, vectors).astype(jnp.bfloat16)
    request_send[...] = per_request.reshape(request_send.shape)

    def request_copy(step):
        peer = lax.rem(me + step, devices)
        return pltpu.make_async_remote_copy(
            src_ref=request_send.at[peer],
            dst_ref=request_out.at[me],
            send_sem=request_sems.at[0, step],
            recv_sem=request_sems.at[1, step],
            device_id=(peer,),
            device_id_type=MESH_ID,
        )

    def begin_request(step, carry):
        request_copy(step).start()
        return carry

    def finish_request(step, carry):
        request_copy(step).wait()
        return carry

    lax.fori_loop(1, devices, begin_request, 0)
    request_out[me] = request_send[me]
    entity_width = dense.shape[0]
    few = entity_width // owners
    for cut in range(0, entity_width, block):
        flip[cut : cut + block, :block] = entity_low[:, cut : cut + block].astype(jnp.float32).T
    for pair in range(owners // 2):
        one, two = place_owner(orders[0], 2 * pair), place_owner(orders[0], 2 * pair + 1)
        both = jnp.concatenate(
            [flip[one * few : one * few + few, :block], flip[two * few : two * few + few, :block]],
            axis=0,
        )
        entity_t[pair * 2 * few : (pair + 1) * 2 * few] = both.astype(jnp.bfloat16)
    late_source[6][0] = dot_plain(entity_t[...], state_low).astype(jnp.bfloat16)
    go_on("ent")
    weight_grad(late_source[5], 0, 0, dqe, 0, words, True)
    streams[11].launch(0)
    go_on("we")
    for copy in word_weights:
        copy.wait()

    def word_step(index, carry):
        begin = pl.multiple_of(index * taller, 16)
        words_out[pl.ds(begin, taller)] = data_grad(begin, taller, word_queries).astype(jnp.bfloat16)
        for point in range(words // taller):
            name = WORD_POINTS[point]
            if name in PLAN:
                pl.when(index == point)(functools.partial(go_on, name))
        return carry

    lax.fori_loop(0, words // taller, word_step, 0)
    go_on("end")
    lax.fori_loop(1, devices, finish_request, 0)


def in_order(grad, order):
    bits = len(order)
    owners = 2**bits
    view = grad.reshape((2,) * bits + (grad.shape[0] // owners, grad.shape[1]))
    spots = tuple(bits - mask.bit_length() for mask in order)
    return view.transpose(spots + (bits, bits + 1)).reshape(grad.shape)


def attention_back(early_grads, inputs, weights, grad_scale, collective_id):
    devices = lax.axis_size("dp")
    orders = stage_masks(devices)
    stages = len(orders[0])
    hidden = inputs[0]
    seq_len, width = hidden.shape
    slots = weights[-1].shape[0]
    words = seq_len - slots
    outs = [
        jax.ShapeDtypeStruct((count, rows, wide), jnp.float32)
        for _, count, rows, wide in EARLY + LATE
    ] + [
        jax.ShapeDtypeStruct((words, width), jnp.bfloat16),
        jax.ShapeDtypeStruct(
            (devices, inputs[11].shape[1] // devices, weights[-2].shape[0]), jnp.bfloat16
        ),
    ]
    scratch = []
    for spec in EARLY:
        scratch += piece_scratch(spec, stages, False, True)
    for spec in LATE:
        scratch += piece_scratch(spec, stages, True, False)
    scratch += [pltpu.VMEM((seq_len, width), jnp.bfloat16)] * 4
    scratch += [pltpu.VMEM((2, seq_len, seq_len), jnp.bfloat16)] * 2
    scratch += [
        pltpu.VMEM((width, seq_len), jnp.float32),
        pltpu.VMEM((2, width, seq_len), jnp.bfloat16),
        pltpu.VMEM((width, slots), jnp.bfloat16),
        pltpu.VMEM((weights[-2].shape[0], slots), jnp.bfloat16),
        pltpu.VMEM((devices, inputs[11].shape[1] // devices, weights[-2].shape[0]), jnp.bfloat16),
        pltpu.SemaphoreType.DMA((2, devices)),
        pltpu.SemaphoreType.DMA((len(EARLY) + 4,)),
    ]
    vmem = pl.BlockSpec(memory_space=pltpu.VMEM)
    return pl.pallas_call(
        functools.partial(attention_back_kernel, orders, grad_scale),
        out_shape=outs,
        in_specs=[pl.BlockSpec(memory_space=pltpu.HBM)] * len(EARLY)
        + [vmem] * len(inputs)
        + [pl.BlockSpec(memory_space=pltpu.HBM)] * 2
        + [vmem] * (len(weights) - 2),
        out_specs=[vmem] * len(outs),
        scratch_shapes=scratch,
        compiler_params=pltpu.CompilerParams(
            collective_id=collective_id, has_side_effects=True, vmem_limit_bytes=63 * 2**20
        ),
    )(*early_grads, *inputs, *weights)


def fused_body(
    word_states,
    word_segments,
    entity_segments,
    request_rows,
    request_slot,
    mask_slots,
    entity_table,
    vocab_bias,
    entity_dense,
    query_ww,
    query_we,
    query_ew,
    query_ee,
    key_weight,
    value_weight,
    out_weight,
    norm1_gain,
    norm1_bias,
    up_weight,
    down_weight,
    norm2_gain,
    norm2_bias,
    head_weight,
    head_gain,
    head_bias,
    cotangent,
):
    devices = lax.axis_size("dp")
    low = jnp.bfloat16
    slot_count = entity_segments.shape[1]
    mask_count = mask_slots.shape[1]
    request_count = slot_count + mask_count
    table_rows = entity_table.shape[0]
    grad_scale = 1.0 / (mask_count * devices)
    orders = stage_masks(devices)
    capacity = request_rows.shape[1]
    room = -(-capacity // 16) * 16 - capacity
    kind = jnp.where(request_slot >= slot_count, table_rows, 0)
    codes = jnp.where(request_slot < request_count, request_rows + kind, -1)
    codes = jnp.pad(codes, ((0, 0), (0, room)), constant_values=-1)
    codes = jnp.broadcast_to(codes[:, :, None], codes.shape + (128,))
    slot_row = jnp.pad(request_slot, ((0, 0), (0, room)), constant_values=request_count)
    slot_row = jnp.broadcast_to(slot_row.reshape(1, -1), (8, slot_row.size))
    bias_row = vocab_bias.astype(jnp.float32)[None, :]
    (
        entity_low,
        target_vecs,
        target_bias,
        code_row,
        word_q,
        word_e,
        word_k,
        word_v,
        feat_q,
        feat_k,
    ) = lookup(
        [
            codes,
            entity_table,
            bias_row,
            slot_row,
            word_states,
            query_ww,
            query_we,
            key_weight,
            value_weight,
            word_segments,
            entity_segments,
        ],
        slot_count,
        mask_count,
        0,
    )
    choose = (mask_slots[0][:, None] == jnp.arange(slot_count, dtype=jnp.int32)[None, :]).astype(low)
    (
        hidden_low,
        query_word,
        query_entity,
        key_rows,
        values,
        context_low,
        lse_lanes,
        residual_one,
        normed_low,
        activated,
        gelu_slope,
        residual_two,
        layer_low,
        picked_low,
        head_pre,
        head_low,
    ) = forward_pass(
        [
            word_states,
            entity_low,
            feat_q,
            feat_k,
            choose,
            entity_dense,
            word_q,
            word_e,
            word_k,
            word_v,
            query_ew,
            query_ee,
            key_weight,
            value_weight,
            out_weight,
            norm1_gain,
            norm1_bias,
            up_weight,
            down_weight,
            norm2_gain,
            norm2_bias,
            head_weight,
            head_gain,
            head_bias,
        ]
    )
    table_grad, bias_grad, losses, total_loss, head_grad = head_and_table(
        head_low,
        entity_table,
        bias_row,
        target_vecs,
        target_bias,
        grad_scale,
        1,
    )
    (
        up_a,
        up_b,
        head_a,
        out_b,
        down_b,
        up_c,
        down_c,
        first_grad,
        context_grad,
        lse_delta,
        vectors,
    ) = middle_back(
        [
            head_grad,
            target_vecs,
            head_pre,
            head_gain,
            picked_low,
            head_weight,
            choose,
            cotangent,
            residual_two,
            norm2_gain,
            normed_low,
            residual_one,
            norm1_gain,
            out_weight,
            context_low,
            lse_lanes,
            activated,
            gelu_slope,
            up_weight,
            down_weight,
        ],
        orders,
        grad_scale,
    )
    *sums, words_grad, back_rows = attention_back(
        [up_a, down_b, up_c, down_c, up_b, head_a, vectors, out_b],
        [
            hidden_low,
            query_word,
            query_entity,
            key_rows,
            values,
            context_grad,
            feat_q,
            feat_k,
            lse_delta,
            first_grad,
            head_low,
            slot_row,
        ],
        [
            query_ww,
            query_we,
            query_ew,
            query_ee,
            key_weight,
            value_weight,
            entity_dense,
            entity_low,
        ],
        grad_scale,
        2,
    )
    (
        table_grad,
        bias_grad,
        up_sum,
        down_sum,
        head_sum,
        vector_sum,
        out_sum,
        key_sum,
        value_sum,
        ew_sum,
        ee_sum,
        ww_sum,
        we_sum,
        dense_sum,
    ) = last_step(
        code_row, back_rows.reshape(-1, back_rows.shape[2]), table_grad, bias_grad, sums, grad_scale
    )
    row = vector_sum[0]
    few, many = head_gain.shape[0] // devices, norm1_gain.shape[0] // devices
    spots = [0, few, 2 * few] + [2 * few + many * (i + 1) for i in range(4)]
    vector_out = [row[spots[i] : spots[i + 1]] for i in range(6)]
    return (
        total_loss[0, 0],
        layer_low,
        words_grad,
        table_grad,
        bias_grad[0],
        dense_sum,
        ww_sum,
        we_sum,
        ew_sum,
        ee_sum,
        key_sum,
        value_sum,
        out_sum,
        vector_out[4],
        vector_out[5],
        up_sum,
        down_sum,
        vector_out[2],
        vector_out[3],
        head_sum,
        vector_out[0],
        vector_out[1],
        losses[:, 0],
    )


def solution(mesh):
    in_specs = (
        P("dp", None),
        P("dp", None),
        P("dp", None),
        P("dp", None),
        P("dp", None),
        P("dp", None),
        P("dp", None),
        P("dp"),
        P(),
        P(),
        P(),
        P(),
        P(),
        P(),
        P(),
        P(),
        P(),
        P(),
        P(),
        P(),
        P(),
        P(),
        P(),
        P(),
        P(),
        P("dp", None),
    )
    out_specs = (
        P(),
        P("dp", None),
        P("dp", None),
        P("dp", None),
        P("dp"),
        P("dp", None),
        P("dp", None),
        P("dp", None),
        P("dp", None),
        P("dp", None),
        P("dp", None),
        P("dp", None),
        P("dp", None),
        P("dp"),
        P("dp"),
        P("dp", None),
        P("dp", None),
        P("dp"),
        P("dp"),
        P("dp", None),
        P("dp"),
        P("dp"),
        P("dp"),
    )
    chosen = fused_body if mesh.shape["dp"] == 32 else body
    return jax.shard_map(chosen, mesh=mesh, in_specs=in_specs, out_specs=out_specs, check_vma=False)
```

```python
import functools

import jax
import jax.numpy as jnp
from jax import lax
from jax.experimental import pallas as pl
from jax.experimental.pallas import tpu as pltpu
from jax.sharding import PartitionSpec as P

MESH_ID = pl.DeviceIdType.MESH

HD = 64


EPSILON = 1e-05
MASKED = -1000000000.0


def dot_plain(left_side, right_side):
    return jnp.dot(left_side, right_side, preferred_element_type=jnp.float32)


def dot_left_t(left_side, right_side):
    return lax.dot_general(
        left_side, right_side, (((0,), (0,)), ((), ())), preferred_element_type=jnp.float32
    )


def dot_right_t(left_side, right_side):
    return lax.dot_general(
        left_side, right_side, (((1,), (1,)), ((), ())), preferred_element_type=jnp.float32
    )


def dot_exact(left_side, right_side):
    return jnp.dot(
        left_side, right_side, precision=lax.Precision.HIGHEST, preferred_element_type=jnp.float32
    )


def layer_norm(tensor, gain_vec, shift_vec):
    center = tensor - jnp.mean(tensor, axis=-1, keepdims=True)
    spread = jnp.mean(center * center, axis=-1, keepdims=True)
    return center * lax.rsqrt(spread + EPSILON) * gain_vec + shift_vec


def gelu_exact(tensor):
    return jax.nn.gelu(tensor, approximate=False)


def head_act(tensor, gain_vec, shift_vec):
    return layer_norm(gelu_exact(tensor), gain_vec, shift_vec)


def norm_back(tensor, gain_vec, shift_vec, grad_out):
    result, pullback = jax.vjp(layer_norm, tensor, gain_vec, shift_vec)
    return pullback(grad_out)


def attn_scores(query_word, query_entity, key_rows, allowed, word_count):
    to_words = jnp.einsum(
        "qhd,khd->hqk", query_word, key_rows[:word_count], preferred_element_type=jnp.float32
    )
    to_entities = jnp.einsum(
        "qhd,khd->hqk", query_entity, key_rows[word_count:], preferred_element_type=jnp.float32
    )
    return jnp.where(allowed[None], jnp.concatenate([to_words, to_entities], axis=2), MASKED)


def greet_all(me, devices):
    barrier = pltpu.get_barrier_semaphore()

    def greet(step, carry):
        pl.semaphore_signal(
            barrier, inc=1, device_id=(lax.rem(me + step, devices),), device_id_type=MESH_ID
        )
        return carry

    lax.fori_loop(1, devices, greet, 0)
    pl.semaphore_wait(barrier, devices - 1)


def swap_kernel(devices, gather, source, target, send_sem, recv_sem):
    me = lax.axis_index("dp")
    greet_all(me, devices)

    def piece(step):
        peer = lax.rem(me + step, devices)
        return pltpu.make_async_remote_copy(
            src_ref=source if gather else source.at[peer],
            dst_ref=target.at[me],
            send_sem=send_sem.at[step],
            recv_sem=recv_sem.at[step],
            device_id=(peer,),
            device_id_type=MESH_ID,
        )

    def begin(step, carry):
        piece(step).start()
        return carry

    def finish(step, carry):
        piece(step).wait()
        return carry

    lax.fori_loop(1, devices, begin, 0)
    target[me] = source[...] if gather else source[me]
    lax.fori_loop(1, devices, finish, 0)


def direct_swap(value, collective_id, gather=False):
    devices = lax.axis_size("dp")
    shape = (devices,) + value.shape if gather else value.shape
    return pl.pallas_call(
        functools.partial(swap_kernel, devices, gather),
        out_shape=jax.ShapeDtypeStruct(shape, value.dtype),
        in_specs=[pl.BlockSpec(memory_space=pltpu.VMEM)],
        out_specs=pl.BlockSpec(memory_space=pltpu.VMEM),
        scratch_shapes=[
            pltpu.SemaphoreType.DMA((devices,)),
            pltpu.SemaphoreType.DMA((devices,)),
        ],
        compiler_params=pltpu.CompilerParams(collective_id=collective_id, has_side_effects=True),
    )(value)


def stage_masks(devices):
    if devices == 32:
        axes = [[2], [4], [8, 16]]
    elif devices == 128:
        axes = [[2, 4], [8, 16], [32, 64]]
    else:
        axes = [[2**bit] for bit in range(1, devices.bit_length() - 1)]
        axes = axes + [[] for _ in range(3 - len(axes))]
    first, second, third = axes[0], axes[1], sum(axes[2:], [])
    return (
        [1] + first + second + third,
        [1] + second + first + third,
        [1] + third + first + second,
    )


def sum_kernel(masks, rows, *refs):
    parts = len(masks)
    stages = len(masks[0])
    sources, results = refs[:parts], refs[parts : 2 * parts]
    landing = refs[2 * parts : 3 * parts]
    send_sem, recv_sem = refs[3 * parts :]
    me = lax.axis_index("dp")
    barrier = pltpu.get_barrier_semaphore()
    partner_of = {}
    for mask in masks[0]:
        bit = lax.rem(lax.div(me, mask), 2)
        partner_of[mask] = (me + mask - 2 * mask * bit, bit)
    for mask in masks[0]:
        pl.semaphore_signal(
            barrier, inc=1, device_id=(partner_of[mask][0],), device_id_type=MESH_ID
        )
    pl.semaphore_wait(barrier, stages)
    sizes = [[rows[part] * 2 ** (stages - 1 - stage) for stage in range(stages)] for part in range(parts)]
    places = [[sum(size[:stage]) for stage in range(stages)] for size in sizes]

    def launch(part, stage):
        partner, bit = partner_of[masks[part][stage]]
        size = sizes[part][stage]
        away = (1 - bit) * size
        copy = pltpu.make_async_remote_copy(
            src_ref=sources[part].at[pl.ds(away, size)]
            if stage == 0
            else landing[part].at[pl.ds(places[part][stage - 1] + away, size)],
            dst_ref=landing[part].at[pl.ds(places[part][stage], size)],
            send_sem=send_sem.at[part, stage],
            recv_sem=recv_sem.at[part, stage],
            device_id=(partner,),
            device_id_type=MESH_ID,
        )
        copy.start()
        return copy

    flying = [launch(part, 0) for part in range(parts)]

    def add_rows(part, stage, start, count):
        keep = partner_of[masks[part][stage]][1] * sizes[part][stage] + start
        last = stage == stages - 1

        def step(index, carry):
            theirs = pl.ds(pl.multiple_of(places[part][stage] + start + index * 16, 16), 16)
            if stage == 0:
                mine = sources[part][pl.ds(pl.multiple_of(keep + index * 16, 16), 16)]
            else:
                mine = landing[part][
                    pl.ds(pl.multiple_of(places[part][stage - 1] + keep + index * 16, 16), 16)
                ]
            total = mine.astype(jnp.float32) + landing[part][theirs].astype(jnp.float32)
            if last:
                results[part][pl.ds(pl.multiple_of(index * 16, 16), 16)] = total
            else:
                landing[part][theirs] = total.astype(jnp.bfloat16)
            return carry

        lax.fori_loop(0, count // 16, step, 0, unroll=min(4, count // 16))

    for stage in range(stages):
        for part in range(parts):
            flying[part].wait()
            if stage == stages - 1:
                add_rows(part, stage, 0, sizes[part][stage])
                continue
            bit = partner_of[masks[part][stage + 1]][1]
            half = sizes[part][stage] // 2
            add_rows(part, stage, (1 - bit) * half, half)
            flying[part] = launch(part, stage + 1)
            add_rows(part, stage, bit * half, half)


def sum_scatter(parts, collective_id):
    devices = lax.axis_size("dp")
    masks = stage_masks(devices)
    rows = [part.shape[1] for part in parts]
    width = parts[0].shape[2]
    bits = devices.bit_length() - 1
    ordered = []
    for part, order in zip(parts, masks):
        view = part.reshape((2,) * bits + part.shape[1:])
        places = [bits - mask.bit_length() for mask in order]
        view = view.transpose(tuple(places) + (bits, bits + 1))
        ordered.append(view.reshape(devices * part.shape[1], width))
    return pl.pallas_call(
        functools.partial(sum_kernel, masks, rows),
        out_shape=[jax.ShapeDtypeStruct((count, width), jnp.float32) for count in rows],
        in_specs=[pl.BlockSpec(memory_space=pltpu.VMEM)] * len(parts),
        out_specs=[pl.BlockSpec(memory_space=pltpu.VMEM)] * len(parts),
        scratch_shapes=[pltpu.VMEM((devices * count, width), jnp.bfloat16) for count in rows]
        + [pltpu.SemaphoreType.DMA((len(parts), bits)), pltpu.SemaphoreType.DMA((len(parts), bits))],
        input_output_aliases={},
        compiler_params=pltpu.CompilerParams(
            collective_id=collective_id, has_side_effects=True, vmem_limit_bytes=56 * 2**20
        ),
    )(*ordered)


def by_owner(grad, width):
    devices = lax.axis_size("dp")
    rows = grad.shape[0] // devices
    blocks = grad.astype(jnp.bfloat16).reshape(devices, rows, grad.shape[1])
    if grad.shape[1] > width:
        cuts = grad.shape[1] // width
        return jnp.concatenate(jnp.split(blocks, cuts, axis=2), axis=1)
    if grad.shape[1] < width:
        return blocks.reshape(devices, rows * grad.shape[1] // width, width)
    return blocks


def from_owner(rows, shape):
    devices = lax.axis_size("dp")
    count, width = shape[0] // devices, shape[1]
    if width > rows.shape[1]:
        return jnp.concatenate(jnp.split(rows, width // rows.shape[1], axis=0), axis=1)
    return rows.reshape(count, width)


def sum_all(groups, collective_id):
    width = groups[0][0].shape[1]
    width = min(grad.shape[1] for group in groups for grad in group if grad.shape[1] >= 768)
    devices = lax.axis_size("dp")
    packed = []
    for group in groups:
        pieces = [by_owner(grad, width) for grad in group]
        count = sum(piece.shape[1] for piece in pieces)
        room = -(-count // 16) * 16 - count
        if room:
            pieces.append(jnp.zeros((devices, room, width), jnp.bfloat16))
        packed.append(jnp.concatenate(pieces, axis=1))
    sums = sum_scatter(packed, collective_id)
    results = []
    for group, total in zip(groups, sums):
        place, outs = 0, []
        for grad in group:
            count = grad.shape[0] // devices * grad.shape[1] // width
            outs.append(from_owner(total[place : place + count], grad.shape))
            place += count
        results.append(outs)
    return results


def body(
    word_states,
    word_segments,
    entity_segments,
    request_rows,
    request_slot,
    mask_slots,
    entity_table,
    vocab_bias,
    entity_dense,
    query_ww,
    query_we,
    query_ew,
    query_ee,
    key_weight,
    value_weight,
    out_weight,
    norm1_gain,
    norm1_bias,
    up_weight,
    down_weight,
    norm2_gain,
    norm2_bias,
    head_weight,
    head_gain,
    head_bias,
    cotangent,
):
    word_count = word_states.shape[0]
    model_width = word_states.shape[1]
    slot_count = entity_segments.shape[1]
    mask_count = mask_slots.shape[1]
    request_count = slot_count + mask_count
    seq_len = word_count + slot_count
    devices = lax.axis_size("dp")
    capacity = request_rows.shape[1]
    head_count = model_width // HD
    query_scale = HD ** (-0.5)
    emb_width = entity_table.shape[1]
    table_rows = entity_table.shape[0]
    total_mask = mask_count * devices
    grad_scale = 1.0 / total_mask
    id_block = jnp.pad(request_rows[:, None, :], ((0, 0), (0, 7), (0, 128 - capacity)))
    asked_ids = direct_swap(id_block, 0)[:, 0, :capacity]
    found_rows = jnp.take(entity_table, asked_ids, axis=0)
    found_bias = jnp.take(vocab_bias, asked_ids, axis=0)
    cap_room = -(-capacity // 16) * 16 - capacity
    found_all = jnp.concatenate(
        [found_rows, jnp.broadcast_to(found_bias[:, :, None], found_bias.shape + (128,))], axis=2
    )
    back_all = direct_swap(jnp.pad(found_all, ((0, 0), (0, cap_room), (0, 0))), 1)
    back_rows = back_all[:, :capacity, :emb_width]
    back_bias = back_all[:, :capacity, emb_width]
    got_rows = back_rows
    got_bias = back_bias
    slot_ids = request_slot.reshape(devices * capacity)
    placing = slot_ids[None, :] == jnp.arange(request_count, dtype=jnp.int32)[:, None]
    placing_low = placing.astype(jnp.bfloat16)
    request_vecs = dot_plain(placing_low, got_rows.reshape(devices * capacity, emb_width))
    request_bias = dot_plain(placing_low, got_bias.reshape(devices * capacity, 1))[:, 0]
    entity_low = request_vecs[:slot_count].astype(jnp.bfloat16)
    target_vecs = request_vecs[slot_count:]
    target_bias = request_bias[slot_count:]
    entity_states = dot_plain(entity_low, entity_dense)
    hidden = jnp.concatenate([word_states.astype(jnp.float32), entity_states], axis=0)
    hidden_low = hidden.astype(jnp.bfloat16)
    word_part = hidden_low[:word_count]
    entity_part = hidden_low[word_count:]
    query_word = (
        query_scale
        * jnp.concatenate(
            [dot_plain(word_part, query_ww), dot_plain(entity_part, query_ew)], axis=0
        )
    ).astype(jnp.bfloat16)
    query_entity = (
        query_scale
        * jnp.concatenate(
            [dot_plain(word_part, query_we), dot_plain(entity_part, query_ee)], axis=0
        )
    ).astype(jnp.bfloat16)
    key_rows = dot_plain(hidden_low, key_weight).astype(jnp.bfloat16)
    values = dot_plain(hidden_low, value_weight).astype(jnp.bfloat16)
    head_shape = (seq_len, head_count, HD)
    query_word_h = query_word.reshape(head_shape)
    query_entity_h = query_entity.reshape(head_shape)
    key_rows_h = key_rows.reshape(head_shape)
    values_h = values.reshape(head_shape)
    segment_row = jnp.concatenate([word_segments[0], entity_segments[0]])
    allowed = segment_row[:, None] == segment_row[None, :]
    scores = attn_scores(query_word_h, query_entity_h, key_rows_h, allowed, word_count)
    row_top = jnp.max(scores, axis=2, keepdims=True)
    exp_scores = jnp.exp(scores - row_top)
    row_total = jnp.sum(exp_scores, axis=2, keepdims=True)
    attn_low = (exp_scores / row_total).astype(jnp.bfloat16)
    row_lse = row_top + jnp.log(row_total)
    context = jnp.einsum("hqk,khd->qhd", attn_low, values_h, preferred_element_type=jnp.float32)
    context_low = context.reshape(seq_len, model_width).astype(jnp.bfloat16)
    attended = dot_plain(context_low, out_weight)
    residual_one = hidden + attended
    normed = layer_norm(residual_one, norm1_gain, norm1_bias)
    normed_low = normed.astype(jnp.bfloat16)
    up_value = dot_plain(normed_low, up_weight)
    activated = gelu_exact(up_value).astype(jnp.bfloat16)
    down_value = dot_plain(activated, down_weight)
    residual_two = normed + down_value
    layer_out = layer_norm(residual_two, norm2_gain, norm2_bias)
    choose = (mask_slots[0][:, None] == jnp.arange(slot_count, dtype=jnp.int32)[None, :]).astype(
        jnp.float32
    )
    picked_low = dot_exact(choose, layer_out[word_count:]).astype(jnp.bfloat16)
    head_pre = dot_plain(picked_low, head_weight)
    head_low = head_act(head_pre, head_gain, head_bias).astype(jnp.bfloat16)
    head_f32 = head_low.astype(jnp.float32)
    target_logit = jnp.sum(head_f32 * target_vecs, axis=1) + target_bias
    all_heads = direct_swap(head_low, 2, gather=True).reshape(total_mask, emb_width)
    block_rows = min(512, total_mask)
    block_count = total_mask // block_rows
    bias_f32 = vocab_bias.astype(jnp.float32)

    def block_logits(block_index):
        row_block = lax.dynamic_slice_in_dim(all_heads, block_index * block_rows, block_rows, 0)
        return (row_block, dot_right_t(row_block, entity_table) + bias_f32[None, :])

    def block_stats(block_index):
        row_block, logits = block_logits(block_index)
        top_value = jnp.max(logits, axis=1)
        return (top_value, jnp.sum(jnp.exp(logits - top_value[:, None]), axis=1))

    local_top, local_total = lax.map(block_stats, jnp.arange(block_count, dtype=jnp.int32))
    local_top = local_top.reshape(total_mask)
    local_total = local_total.reshape(total_mask)
    target_sum = jnp.sum(target_logit)
    stats = jnp.concatenate(
        [
            local_top.reshape(total_mask // 128, 128),
            local_total.reshape(total_mask // 128, 128),
            jnp.full((8, 128), target_sum),
        ],
        axis=0,
    )
    all_stats = direct_swap(stats, 3, gather=True)
    all_tops = all_stats[:, : total_mask // 128].reshape(devices, total_mask)
    all_totals = all_stats[:, total_mask // 128 : total_mask // 64].reshape(devices, total_mask)
    target_total = jnp.sum(all_stats[:, total_mask // 64, 0])
    global_top = jnp.max(all_tops, axis=0)
    global_total = jnp.sum(all_totals * jnp.exp(all_tops - global_top[None, :]), axis=0)
    lse_all = global_top + jnp.log(global_total)
    loss_value = (jnp.sum(lse_all) - target_total) * grad_scale
    own_lse = lax.dynamic_slice_in_dim(lse_all, lax.axis_index("dp") * mask_count, mask_count, 0)
    mask_loss = own_lse - target_logit

    def block_back(running, block_index):
        table_grad, bias_grad = running
        row_block, logits = block_logits(block_index)
        lse_block = lax.dynamic_slice_in_dim(lse_all, block_index * block_rows, block_rows, 0)
        logit_grad = (jnp.exp(logits - lse_block[:, None]) * grad_scale).astype(jnp.bfloat16)
        table_grad = table_grad + dot_left_t(logit_grad, row_block)
        bias_grad = bias_grad + jnp.sum(logit_grad.astype(jnp.float32), axis=0)
        return ((table_grad, bias_grad), dot_plain(logit_grad, entity_table))

    start_grads = (
        jnp.zeros((table_rows, emb_width), jnp.float32),
        jnp.zeros((table_rows,), jnp.float32),
    )
    (table_grad, bias_grad), head_terms = lax.scan(
        block_back, start_grads, jnp.arange(block_count, dtype=jnp.int32)
    )
    head_parts = direct_swap(head_terms.reshape(devices, mask_count, emb_width), 4)
    head_grad = jnp.sum(head_parts, axis=0)
    head_grad = head_grad - grad_scale * target_vecs
    target_grad = -grad_scale * head_f32
    pre_grad, head_gain_grad, head_bias_grad = jax.vjp(head_act, head_pre, head_gain, head_bias)[1](
        head_grad
    )
    pre_low = pre_grad.astype(jnp.bfloat16)
    head_weight_grad = dot_left_t(picked_low, pre_low)
    picked_grad = dot_right_t(pre_low, head_weight)
    out_grad = cotangent.astype(jnp.float32) + jnp.concatenate(
        [jnp.zeros((word_count, model_width), jnp.float32), dot_exact(choose.T, picked_grad)],
        axis=0,
    )
    resid_grad, norm2_gain_grad, norm2_bias_grad = norm_back(
        residual_two, norm2_gain, norm2_bias, out_grad
    )
    down_in = resid_grad.astype(jnp.bfloat16)
    down_grad = dot_left_t(activated, down_in)
    act_grad = dot_right_t(down_in, down_weight)
    up_grad = jax.vjp(gelu_exact, up_value)[1](act_grad)[0]
    up_low = up_grad.astype(jnp.bfloat16)
    up_weight_grad = dot_left_t(normed_low, up_low)
    normed_grad = resid_grad + dot_right_t(up_low, up_weight)
    first_grad, norm1_gain_grad, norm1_bias_grad = norm_back(
        residual_one, norm1_gain, norm1_bias, normed_grad
    )
    attn_in = first_grad.astype(jnp.bfloat16)
    out_weight_grad = dot_left_t(context_low, attn_in)
    context_grad = dot_right_t(attn_in, out_weight).astype(jnp.bfloat16).reshape(head_shape)
    scores_again = attn_scores(query_word_h, query_entity_h, key_rows_h, allowed, word_count)
    attn_prob = jnp.exp(scores_again - row_lse)
    prob_low = attn_prob.astype(jnp.bfloat16)
    prob_grad = jnp.einsum(
        "qhd,khd->hqk", context_grad, values_h, preferred_element_type=jnp.float32
    )
    values_grad = jnp.einsum(
        "hqk,qhd->khd", prob_low, context_grad, preferred_element_type=jnp.float32
    )
    values_grad = values_grad.reshape(seq_len, model_width).astype(jnp.bfloat16)
    row_delta = jnp.sum(attn_prob * prob_grad, axis=2, keepdims=True)
    score_grad = (attn_prob * (prob_grad - row_delta)).astype(jnp.bfloat16)
    qword_grad = jnp.einsum(
        "hqk,khd->qhd",
        score_grad[:, :, :word_count],
        key_rows_h[:word_count],
        preferred_element_type=jnp.float32,
    )
    qword_grad = qword_grad.reshape(seq_len, model_width).astype(jnp.bfloat16)
    qent_grad = jnp.einsum(
        "hqk,khd->qhd",
        score_grad[:, :, word_count:],
        key_rows_h[word_count:],
        preferred_element_type=jnp.float32,
    )
    qent_grad = qent_grad.reshape(seq_len, model_width).astype(jnp.bfloat16)
    keys_grad = jnp.concatenate(
        [
            jnp.einsum(
                "hqk,qhd->khd",
                score_grad[:, :, :word_count],
                query_word_h,
                preferred_element_type=jnp.float32,
            ),
            jnp.einsum(
                "hqk,qhd->khd",
                score_grad[:, :, word_count:],
                query_entity_h,
                preferred_element_type=jnp.float32,
            ),
        ],
        axis=0,
    )
    keys_grad = keys_grad.reshape(seq_len, model_width).astype(jnp.bfloat16)
    query_ww_grad = query_scale * dot_left_t(word_part, qword_grad[:word_count])
    query_ew_grad = query_scale * dot_left_t(entity_part, qword_grad[word_count:])
    query_we_grad = query_scale * dot_left_t(word_part, qent_grad[:word_count])
    query_ee_grad = query_scale * dot_left_t(entity_part, qent_grad[word_count:])
    key_weight_grad = dot_left_t(hidden_low, keys_grad)
    value_weight_grad = dot_left_t(hidden_low, values_grad)
    word_back = query_scale * (
        dot_right_t(qword_grad[:word_count], query_ww)
        + dot_right_t(qent_grad[:word_count], query_we)
    )
    entity_back = query_scale * (
        dot_right_t(qword_grad[word_count:], query_ew)
        + dot_right_t(qent_grad[word_count:], query_ee)
    )
    hidden_grad = (
        first_grad
        + jnp.concatenate([word_back, entity_back], axis=0)
        + dot_right_t(keys_grad, key_weight)
        + dot_right_t(values_grad, value_weight)
    )
    words_grad = hidden_grad[:word_count].astype(jnp.bfloat16)
    state_low = hidden_grad[word_count:].astype(jnp.bfloat16)
    dense_grad = dot_left_t(entity_low, state_low)
    entity_vec_grad = dot_right_t(state_low, entity_dense)
    vec_grad = jnp.concatenate([entity_vec_grad, target_grad], axis=0)
    bias_vec_grad = jnp.concatenate(
        [jnp.zeros((slot_count,), jnp.float32), jnp.full((mask_count,), -grad_scale, jnp.float32)]
    )
    placing_f32 = placing.astype(jnp.float32)
    per_request = dot_exact(placing_f32.T, vec_grad)
    bias_request = dot_exact(placing_f32.T, bias_vec_grad[:, None])[:, 0]
    back_block = jnp.concatenate(
        [
            per_request.reshape(devices, capacity, emb_width).astype(jnp.bfloat16),
            jnp.broadcast_to(
                bias_request.reshape(devices, capacity, 1).astype(jnp.bfloat16),
                (devices, capacity, 128),
            ),
        ],
        axis=2,
    )
    back_block = direct_swap(jnp.pad(back_block, ((0, 0), (0, cap_room), (0, 0))), 5)
    back_rows = back_block[:, :capacity, :emb_width].astype(jnp.float32)
    back_bias = back_block[:, :capacity, emb_width].astype(jnp.float32)
    flat_ids = asked_ids.reshape(devices * capacity)
    table_grad = table_grad + jax.ops.segment_sum(
        back_rows.reshape(devices * capacity, emb_width), flat_ids, num_segments=table_rows
    )
    bias_grad = bias_grad + jax.ops.segment_sum(
        back_bias.reshape(devices * capacity), flat_ids, num_segments=table_rows
    )
    vectors = [
        head_gain_grad,
        head_bias_grad,
        norm2_gain_grad,
        norm2_bias_grad,
        norm1_gain_grad,
        norm1_bias_grad,
    ]
    cuts = [vector.reshape(devices, -1) for vector in vectors]
    spots = [0]
    for cut in cuts:
        spots.append(spots[-1] + cut.shape[1])
    block = jnp.concatenate(cuts, axis=1)
    block = jnp.pad(block, ((0, 0), (0, 128 - spots[-1])))[:, None, :]
    vector_sums = jnp.sum(direct_swap(jnp.pad(block, ((0, 0), (0, 7), (0, 0))), 6)[:, 0], axis=0)
    vector_out = [vector_sums[spots[i] : spots[i + 1]] for i in range(len(cuts))]
    sums = sum_all(
        [
            [up_weight_grad, out_weight_grad, head_weight_grad],
            [down_grad, query_ww_grad, dense_grad],
            [query_we_grad, query_ew_grad, query_ee_grad, key_weight_grad, value_weight_grad],
        ],
        7,
    )
    all_sums = (
        sums[0][2],
        vector_out[0],
        vector_out[1],
        vector_out[2],
        vector_out[3],
        sums[0][0],
        sums[1][0],
        vector_out[4],
        vector_out[5],
        sums[0][1],
        sums[1][1],
        sums[2][0],
        sums[2][1],
        sums[2][2],
        sums[2][3],
        sums[2][4],
        sums[1][2],
    )
    return (
        loss_value,
        layer_out.astype(jnp.bfloat16),
        words_grad,
        table_grad,
        bias_grad,
        all_sums[16],
        all_sums[10],
        all_sums[11],
        all_sums[12],
        all_sums[13],
        all_sums[14],
        all_sums[15],
        all_sums[9],
        all_sums[7],
        all_sums[8],
        all_sums[5],
        all_sums[6],
        all_sums[3],
        all_sums[4],
        all_sums[0],
        all_sums[1],
        all_sums[2],
        mask_loss,
    )


class Stage:
    def __init__(self, loads, stores):
        self.loads, self.stores, self.waited, self.sent = loads, stores, set(), []

    def need(self, *indices):
        for index in indices:
            if index not in self.waited:
                self.waited.add(index)
                self.loads[index].wait()

    def send(self, *indices):
        for index in indices:
            self.sent.append(index)
            self.stores[index].start()

    def finish(self):
        self.need(*self.loads)
        self.send(*[index for index in self.stores if index not in self.sent])
        for copy in self.stores.values():
            copy.wait()


def staged_kernel(inner, counts, far_in, far_out, *refs):
    ins, outs = list(refs[: counts[0]]), list(refs[counts[0] : sum(counts)])
    rest = list(refs[sum(counts) :])
    out_sem, in_sem = rest.pop(), rest.pop()
    near = rest[len(rest) - len(far_in) - len(far_out) :]
    rest = rest[: len(rest) - len(near)]
    loads, stores = {}, {}
    for slot, index in enumerate(far_in):
        loads[index] = pltpu.make_async_copy(ins[index], near[slot], in_sem.at[slot])
        ins[index] = near[slot]
        loads[index].start()
    for slot, index in enumerate(far_out):
        close = near[len(far_in) + slot]
        stores[index] = pltpu.make_async_copy(close, outs[index], out_sem.at[slot])
        outs[index] = close
    stage = Stage(loads, stores)
    inner(stage, *ins, *outs, *rest)
    stage.finish()


def staged_call(inner, inputs, outs, in_specs, out_specs, far_in, far_out, scratch, params):
    hbm = pl.BlockSpec(memory_space=pltpu.HBM)
    in_specs, out_specs = list(in_specs), list(out_specs)
    extra = []
    for index in far_in:
        in_specs[index] = hbm
        extra.append(pltpu.VMEM(inputs[index].shape, inputs[index].dtype))
    for index in far_out:
        out_specs[index] = hbm
        extra.append(pltpu.VMEM(outs[index].shape, outs[index].dtype))
    return pl.pallas_call(
        functools.partial(staged_kernel, inner, (len(inputs), len(outs)), far_in, far_out),
        out_shape=outs,
        in_specs=in_specs,
        out_specs=out_specs,
        scratch_shapes=list(scratch)
        + extra
        + [
            pltpu.SemaphoreType.DMA((max(1, len(far_in)),)),
            pltpu.SemaphoreType.DMA((max(1, len(far_out)),)),
        ],
        compiler_params=params,
    )(*inputs)


def all_pairs(source, target, sems, me, devices):
    def piece(step):
        peer = lax.rem(me + step, devices)
        return pltpu.make_async_remote_copy(
            src_ref=source.at[peer],
            dst_ref=target.at[me],
            send_sem=sems.at[0, step],
            recv_sem=sems.at[1, step],
            device_id=(peer,),
            device_id_type=MESH_ID,
        )

    def begin(step, carry):
        piece(step).start()
        return carry

    def finish(step, carry):
        piece(step).wait()
        return carry

    lax.fori_loop(1, devices, begin, 0)
    target[me] = source[me]
    return lambda: lax.fori_loop(1, devices, finish, 0)


def lookup_kernel(
    stage,
    request_rows,
    table,
    bias,
    request_slot,
    word_states,
    w_ww,
    w_we,
    w_key,
    w_value,
    word_seg,
    entity_seg,
    mask_slots,
    entity_out,
    vec_out,
    bias_out,
    code_out,
    qword,
    qent,
    keys,
    values,
    feat_q,
    feat_k,
    choose,
    slot_out,
    code_send,
    code_pad,
    slot_pad,
    codes_in,
    found,
    rows_in,
    bias_col,
    sems,
):
    devices, room, _ = found.shape
    me = lax.axis_index("dp")
    rows, wide = table.shape
    entries = devices * room
    slots, masked = entity_out.shape[0], vec_out.shape[0]
    slot = request_slot[...]
    code = request_rows[...] + jnp.where(slot >= slots, rows, 0)
    code = jnp.where(slot < slots + masked, code, -1)
    capacity = slot.shape[0]
    code_pad[...] = jnp.full(code_pad.shape, -1, jnp.int32).astype(jnp.float32)
    code_pad[0:capacity] = code.astype(jnp.float32)
    sent = code_pad[...].T.astype(jnp.int32)
    for owner in range(devices):
        code_send[owner] = sent[owner : owner + 1]
    slot_pad[...] = jnp.full(slot_pad.shape, slots + masked, jnp.int32).astype(jnp.float32)
    slot_pad[0:capacity] = slot.astype(jnp.float32)
    greet_all(me, devices)

    def in_column(turned):
        return jnp.concatenate(
            [
                jnp.broadcast_to(turned[0:room, one : one + 1], (room, 128))
                for one in range(devices)
            ],
            axis=0,
        )

    def in_row(column, target):
        for begin in range(0, entries, 128):
            turned = column[begin : begin + 128].T
            target[:, begin : begin + 128] = turned[0:8].astype(jnp.int32)

    ended = all_pairs(code_send, codes_in, sems.at[0], me, devices)
    width = word_states.shape[1]
    half = width // 2
    query_scale = HD ** (-0.5)

    def project(target, weight, scale):
        for cut in range(0, width, half):
            value = dot_plain(word_states[...], weight[:, cut : cut + half])
            if scale:
                value = value * query_scale
            target[:, cut : cut + half] = value.astype(jnp.bfloat16)

    def bias_step(index, carry):
        at = pl.ds(pl.multiple_of(index * 128, 128), 128)
        bias_col[at] = jnp.broadcast_to(bias[at].reshape(1, 128), (128, 128)).T.astype(jnp.bfloat16)
        return carry

    lax.fori_loop(0, rows // 128, bias_step, 0)
    words = word_seg.shape[1]
    column = lax.rem(lax.broadcasted_iota(jnp.int32, (128, 128), 1), HD)
    for begin in range(0, words + entity_seg.shape[1], 128):
        seg = word_seg[:, begin : begin + 128] if begin < words else entity_seg[...]
        turned = jnp.broadcast_to(seg.astype(jnp.float32), (128, 128)).T
        same = turned == column.astype(jnp.float32)
        at = slice(begin, begin + 128)
        feat_q[at] = same.astype(jnp.float32).astype(jnp.bfloat16)
        feat_k[at] = jnp.where(same | (column >= 4), 0.0, MASKED).astype(jnp.bfloat16)
    turned = jnp.broadcast_to(mask_slots[...].astype(jnp.float32), (128, masked)).T
    lanes = lax.broadcasted_iota(jnp.int32, (masked, 128), 1).astype(jnp.float32)
    choose[...] = (turned == lanes).astype(jnp.float32).astype(jnp.bfloat16)
    stage.need(4, 5)
    project(qword, w_ww, True)
    stage.send(4)
    stage.need(1)
    ended()
    code = in_column(
        jnp.concatenate([codes_in[one] for one in range(devices)], axis=0).astype(jnp.float32).T
    )
    in_row(code, code_out)
    code = code.astype(jnp.int32)
    code = jnp.where(code >= rows, code - rows, code)
    lane = lax.broadcasted_iota(jnp.int32, (entries, 128), 1)
    total = jnp.zeros((entries, wide), jnp.float32)
    shift = jnp.zeros((entries, 128), jnp.float32)
    step = 512
    for begin in range(0, rows, step):
        size = min(step, rows - begin)
        match = jnp.concatenate(
            [
                (code - (begin + inner) == lane).astype(jnp.float32)
                for inner in range(0, size, 128)
            ],
            axis=1,
        ).astype(jnp.bfloat16)
        total += dot_plain(match, table[begin : begin + size])
        shift += dot_plain(match, bias_col[begin : begin + size])
    both = jnp.concatenate([total, shift], axis=1).astype(jnp.bfloat16)
    found[...] = both.reshape(found.shape)
    ended = all_pairs(found, rows_in, sems.at[1], me, devices)
    in_row(in_column(slot_pad[...]), slot_out)
    stage.need(6)
    project(qent, w_we, True)
    stage.send(5)
    stage.need(7)
    project(keys, w_key, False)
    stage.send(6)
    stage.need(8)
    project(values, w_value, False)
    stage.send(7)
    ended()
    wanted = lax.broadcasted_iota(jnp.int32, (slots + masked, entries), 0)
    placing = (wanted == slot_out[0:1]).astype(jnp.float32).astype(jnp.bfloat16)
    placed = dot_plain(placing, rows_in[...].reshape(entries, wide + 128))
    entity_out[...] = placed[:slots, :wide].astype(jnp.bfloat16)
    vec_out[...] = placed[slots:, :wide]
    bias_out[...] = placed[slots:, wide:]


def lookup(inputs, slots, masked, collective_id):
    capacity, devices = inputs[0].shape
    room = -(-capacity // 16) * 16
    rows, wide = inputs[1].shape
    words, width = inputs[4].shape
    entries = devices * room
    low = jnp.bfloat16
    vmem = pl.BlockSpec(memory_space=pltpu.VMEM)
    outs = [
        jax.ShapeDtypeStruct((slots, wide), low),
        jax.ShapeDtypeStruct((masked, wide), jnp.float32),
        jax.ShapeDtypeStruct((masked, 128), jnp.float32),
        jax.ShapeDtypeStruct((8, entries), jnp.int32),
    ]
    outs += [jax.ShapeDtypeStruct((words, width), low)] * 4
    outs += [jax.ShapeDtypeStruct((words + slots, 128), low)] * 2
    outs += [jax.ShapeDtypeStruct((masked, slots), low)]
    outs += [jax.ShapeDtypeStruct((8, entries), jnp.int32)]
    return staged_call(
        lookup_kernel,
        inputs,
        outs,
        [vmem] * len(inputs),
        [vmem] * len(outs),
        (4, 5, 1, 6, 7, 8),
        (4, 5, 6, 7),
        [
            pltpu.VMEM((devices, 1, 128), jnp.int32),
            pltpu.VMEM((128, devices), jnp.float32),
            pltpu.VMEM((room, devices), jnp.float32),
            pltpu.VMEM((devices, 1, 128), jnp.int32),
            pltpu.VMEM((devices, room, wide + 128), low),
            pltpu.VMEM((devices, room, wide + 128), low),
            pltpu.VMEM((rows, 128), low),
            pltpu.SemaphoreType.DMA((2, 2, devices)),
        ],
        pltpu.CompilerParams(
            collective_id=collective_id, has_side_effects=True, vmem_limit_bytes=63 * 2**20
        ),
    )


def norm_parts(value):
    center = value - jnp.mean(value, axis=-1, keepdims=True)
    spread = jnp.mean(center * center, axis=-1, keepdims=True)
    rate = lax.rsqrt(spread + EPSILON)
    return center * rate, rate


def gelu_parts(value):
    chance = 0.5 + 0.5 * lax.erf(value * (0.5**0.5))
    slope = chance + value * (jnp.exp(-0.5 * value * value) * (0.5 / jnp.pi) ** 0.5)
    return value * chance, slope


def half_lanes(block):
    lane = lax.broadcasted_iota(jnp.int32, (1, block), 1)
    low_half = (lane < HD).astype(jnp.float32).astype(jnp.bfloat16)
    high_half = (lane >= HD).astype(jnp.float32).astype(jnp.bfloat16)
    return low_half, high_half


def forward_kernel(
    stage,
    word_states,
    entity_low,
    feat_q,
    feat_k,
    choose,
    dense,
    word_q,
    word_e,
    word_k,
    word_v,
    w_ew,
    w_ee,
    w_key,
    w_value,
    out_hbm,
    gain_one,
    shift_one,
    up_hbm,
    down_hbm,
    gain_two,
    shift_two,
    head_w,
    gain_head,
    shift_head,
    hidden,
    qword,
    qent,
    keys,
    values,
    context,
    lse_out,
    resid_one,
    normed_out,
    active_hbm,
    slope_hbm,
    resid_two,
    layer_low,
    picked_out,
    head_pre_out,
    head_out,
    state_scr,
    normed_scr,
    out_w,
    up_w,
    down_w,
    active,
    slope,
    sems,
):
    loads = [
        pltpu.make_async_copy(source, target, sems.at[index])
        for index, (source, target) in enumerate(
            ((out_hbm, out_w), (up_hbm, up_w), (down_hbm, down_w))
        )
    ]
    words, width = word_states.shape
    word_loads = [
        pltpu.make_async_copy(source, target.at[pl.ds(0, words)], sems.at[12 + index])
        for index, (source, target) in enumerate(
            ((word_q, qword), (word_e, qent), (word_k, keys), (word_v, values))
        )
    ]
    for load in word_loads + loads:
        load.start()
    stage.need(0, 1, 5)
    seq_len = hidden.shape[0]
    slots = seq_len - words
    block = 128
    tall = seq_len
    halves = half_lanes(block)
    query_scale = HD ** (-0.5)
    state_scr[...] = dot_plain(entity_low[...], dense[...])
    hidden[:words] = word_states[...]
    hidden[words:] = state_scr[...].astype(jnp.bfloat16)

    stage.send(0)
    ents = hidden[words:]
    stage.need(10, 11, 12, 13)
    for target, weight, scale in (
        (qword, w_ew, query_scale),
        (qent, w_ee, query_scale),
        (keys, w_key, None),
        (values, w_value, None),
    ):
        value = dot_plain(ents, weight[...])
        if scale is not None:
            value = value * scale
        target[words:] = value.astype(jnp.bfloat16)
    for load in word_loads:
        load.wait()
    stage.send(1, 2, 3, 4)
    stage.need(2, 3)
    lse_out[...] = jnp.zeros_like(lse_out)

    def pair_step(pair, carry):
        lanes = pl.ds(pl.multiple_of(pair * block, block), block)
        key_pair = keys[:, lanes]
        value_pair = values[:, lanes]
        key_feat = [key_pair * halves[h] + feat_k[...] * halves[1 - h] for h in range(2)]
        value_only = [value_pair * halves[h] for h in range(2)]
        spot = lax.broadcasted_iota(jnp.int32, (1, block), 1) - 4 * pair

        def row_step(index, inner):
            at = pl.ds(pl.multiple_of(index * tall, block), tall)
            qw = qword[at, lanes]
            qe = qent[at, lanes]
            feats = feat_q[at]
            result = jnp.zeros((tall, block), jnp.float32)
            stats = lse_out[at]
            for h in range(2):
                left_w = qw * halves[h] + feats * halves[1 - h]
                left_e = qe * halves[h] + feats * halves[1 - h]
                scores = jnp.concatenate(
                    [
                        dot_right_t(left_w, key_feat[h][:words]),
                        dot_right_t(left_e, key_feat[h][words:]),
                    ],
                    axis=1,
                )
                top = jnp.max(scores, axis=1, keepdims=True)
                expo = jnp.exp(scores - top)
                total = jnp.sum(expo, axis=1, keepdims=True)
                prob = (expo * (1.0 / total)).astype(jnp.bfloat16)
                result += dot_plain(prob, value_only[h])
                stats = jnp.where(spot == h, top + jnp.log(total), stats)
            context[at, lanes] = result.astype(jnp.bfloat16)
            lse_out[at] = stats
            return inner

        lax.fori_loop(0, seq_len // tall, row_step, 0)
        return carry

    lax.fori_loop(0, width // block, pair_step, 0)

    stage.send(5)
    loads[0].wait()
    for begin, size in ((0, words // 2), (words // 2, words // 2), (words, slots)):
        at = slice(begin, begin + size)
        start = (
            state_scr[...] if begin == words else word_states[at].astype(jnp.float32)
        )
        value = start + dot_plain(context[at], out_w[...])
        resid_one[at] = value
        normed = norm_parts(value)[0] * gain_one[...][None, :] + shift_one[...][None, :]
        normed_scr[at] = normed
        normed_out[at] = normed.astype(jnp.bfloat16)
    stage.send(7, 8)
    loads[1].wait()
    loads[2].wait()
    span = seq_len
    stores = []

    for slot in range(down_w.shape[0] // width):
        cols = slice(slot * width, slot * width + width)

        def up_step(index, carry, cols=cols):
            at = pl.ds(pl.multiple_of(index * span, 16), span)
            result, change = gelu_parts(dot_plain(normed_out[at], up_w[:, cols]))
            active[at, cols] = result.astype(jnp.bfloat16)
            slope[at, cols] = change.astype(jnp.bfloat16)
            return carry

        lax.fori_loop(0, seq_len // span, up_step, 0)
        for index, (source, target) in enumerate(((active, active_hbm), (slope, slope_hbm))):
            stores.append(
                pltpu.make_async_copy(
                    source.at[:, cols], target.at[:, cols], sems.at[3 + 2 * slot + index]
                )
            )
            stores[-1].start()

    def down_step(index, carry):
        at = pl.ds(pl.multiple_of(index * span, 16), span)
        value = normed_scr[at] + dot_plain(active[at], down_w[...])
        resid_two[at] = value
        layer_low[at] = (norm_parts(value)[0] * gain_two[...][None, :] + shift_two[...][None, :]).astype(jnp.bfloat16)
        return carry

    lax.fori_loop(0, seq_len // span, down_step, 0)
    stage.send(11, 12)
    stage.need(21)
    picked = dot_plain(choose[...], layer_low[words:]).astype(jnp.bfloat16)
    picked_out[...] = picked
    head_pre = dot_plain(picked, head_w[...])
    head_pre_out[...] = head_pre
    raised = gelu_parts(head_pre)[0]
    head_out[...] = (norm_parts(raised)[0] * gain_head[...][None, :] + shift_head[...][None, :]).astype(jnp.bfloat16)
    for store in stores:
        store.wait()


def forward_pass(inputs):
    words, width = inputs[0].shape
    slots = inputs[1].shape[0]
    seq_len = words + slots
    hidden_units = inputs[17].shape[1]
    mask_count = inputs[4].shape[0]
    head_width = inputs[21].shape[1]
    low, full = jnp.bfloat16, jnp.float32
    vmem, hbm = pl.BlockSpec(memory_space=pltpu.VMEM), pl.BlockSpec(memory_space=pltpu.HBM)
    far = (6, 7, 8, 9, 14, 17, 18)
    shapes = [
        ((seq_len, width), low),
        ((seq_len, width), low),
        ((seq_len, width), low),
        ((seq_len, width), low),
        ((seq_len, width), low),
        ((seq_len, width), low),
        ((seq_len, 128), full),
        ((seq_len, width), full),
        ((seq_len, width), low),
        ((seq_len, hidden_units), low),
        ((seq_len, hidden_units), low),
        ((seq_len, width), full),
        ((seq_len, width), low),
        ((mask_count, width), low),
        ((mask_count, head_width), full),
        ((mask_count, head_width), low),
    ]
    outs = [jax.ShapeDtypeStruct(*shape) for shape in shapes]
    return staged_call(
        forward_kernel,
        inputs,
        outs,
        [hbm if index in far else vmem for index in range(len(inputs))],
        [hbm if index in (9, 10) else vmem for index in range(len(shapes))],
        (0, 1, 5, 10, 11, 12, 13, 2, 3, 21),
        (0, 1, 2, 3, 4, 5, 7, 8, 11, 12),
        [
            pltpu.VMEM((slots, width), full),
            pltpu.VMEM((seq_len, width), full),
            pltpu.VMEM(inputs[14].shape, low),
            pltpu.VMEM(inputs[17].shape, low),
            pltpu.VMEM(inputs[18].shape, low),
            pltpu.VMEM((seq_len, hidden_units), low),
            pltpu.VMEM((seq_len, hidden_units), low),
            pltpu.SemaphoreType.DMA((16,)),
        ],
        pltpu.CompilerParams(vmem_limit_bytes=63 * 2**20),
    )


class Grid:
    def __init__(self):
        me = lax.axis_index("dp")
        self.core = lax.rem(me, 2)
        self.square = lax.rem(lax.div(me, 2), 4)
        self.line = lax.div(me, 8)
        self.twin = me + 1 - 2 * self.core
        self.squares = []
        self.lines = []
        for step in range(1, 4):
            other = lax.rem(self.square + step, 4)
            self.squares.append((me + 2 * (other - self.square), other))
            other = lax.rem(self.line + step, 4)
            self.lines.append((me + 8 * (other - self.line), other))

    def greet(self):
        barrier = pltpu.get_barrier_semaphore()
        peers = [self.twin] + [peer for peer, _ in self.squares + self.lines]
        for peer in peers:
            pl.semaphore_signal(barrier, inc=1, device_id=(peer,), device_id_type=MESH_ID)
        pl.semaphore_wait(barrier, len(peers))


class Sender:
    def __init__(self, send_sem, recv_sem):
        self.send_sem, self.recv_sem, self.used = send_sem, recv_sem, 0

    def start(self, source, target, peer):
        slot = self.used
        self.used += 1
        copy = pltpu.make_async_remote_copy(
            src_ref=source,
            dst_ref=target,
            send_sem=self.send_sem.at[slot],
            recv_sem=self.recv_sem.at[slot],
            device_id=(peer,),
            device_id_type=MESH_ID,
        )
        copy.start()
        return copy


def wait_all(copies):
    for copy in copies:
        copy.wait()


def merge_stats(blocks):
    tops = [block[0] for block in blocks]
    top = functools.reduce(jnp.maximum, tops)
    total = sum(block[1] * jnp.exp(block[0] - top) for block in blocks)
    return top, total, sum(block[2] for block in blocks)


def head_kernel(
    grad_scale,
    head,
    table,
    bias,
    target_vecs,
    target_bias,
    table_grad,
    bias_grad,
    losses,
    total_loss,
    head_grad,
    heads,
    logits,
    expo,
    table_t,
    bias_col,
    part,
    land_pair,
    sum_pair,
    land_square,
    sum_square,
    land_line,
    stat,
    stat_pair,
    stat_square,
    stat_line,
    send_sem,
    recv_sem,
):
    grid = Grid()
    rows, wide = table.shape
    count = head.shape[0]
    total_mask = 32 * count
    grid.greet()
    sender = Sender(send_sem, recv_sem)
    line, square, core = grid.line, grid.square, grid.core
    flying = [sender.start(head, heads.at[line, square, core], peer) for peer, _ in grid.lines]
    heads[line, square, core] = head[...]

    def table_step(index, carry):
        at = pl.ds(pl.multiple_of(index * 128, 128), 128)
        table_t[:, at] = table[at].astype(jnp.float32).T.astype(jnp.bfloat16)
        return carry

    lax.fori_loop(0, rows // 128, table_step, 0)
    wait_all(flying)
    flying = [
        sender.start(heads.at[:, square, core], heads.at[:, square, core], peer)
        for peer, _ in grid.squares
    ]

    def bias_step(index, carry):
        at = pl.ds(pl.multiple_of(index * 128, 128), 128)
        bias_col[at] = jnp.broadcast_to(bias[at].reshape(1, 128), (128, 128)).T
        return carry

    lax.fori_loop(0, rows // 128, bias_step, 0)
    wait_all(flying)
    sender.start(heads.at[:, :, core], heads.at[:, :, core], grid.twin).wait()

    all_heads = heads[...].reshape(total_mask, wide)
    slab = rows // 2

    def logit_step(index, carry):
        at = pl.ds(pl.multiple_of(index * slab, 16), slab)
        logits[at] = dot_right_t(table[at], all_heads)
        return carry

    lax.fori_loop(0, rows // slab, logit_step, 0)
    tile = 64
    wide_copies = total_mask // 128

    def value_at(index):
        at = pl.ds(pl.multiple_of(index * tile, tile), tile)
        shift = bias_col[at]
        return at, logits[at] + jnp.concatenate([shift] * wide_copies, axis=1)

    def top_step(index, top):
        at, value = value_at(index)
        return jnp.maximum(top, jnp.max(value.reshape(tile // 8, 8, total_mask), axis=0))

    top = lax.fori_loop(
        0, rows // tile, top_step, jnp.full((8, total_mask), -jnp.inf, jnp.float32)
    )
    top = jnp.max(top, axis=0, keepdims=True)

    def exp_step(index, total):
        at, value = value_at(index)
        value = jnp.exp(value - top)
        expo[at] = value.astype(jnp.bfloat16)
        return total + jnp.sum(value.reshape(tile // 8, 8, total_mask), axis=0)

    total = lax.fori_loop(0, rows // tile, exp_step, jnp.zeros((8, total_mask), jnp.float32))
    total = jnp.sum(total, axis=0, keepdims=True)

    def fold(row):
        return jnp.concatenate([row[:, i * 128 : i * 128 + 128] for i in range(wide_copies)], axis=0)

    def unfold(block):
        return jnp.concatenate([block[i : i + 1] for i in range(wide_copies)], axis=1)

    own_top, own_total = fold(top), fold(total)
    target = (
        jnp.sum(head[...].astype(jnp.float32) * target_vecs[...], axis=1, keepdims=True)
        + target_bias[:, 0:1]
    )
    own_target = jnp.broadcast_to(jnp.sum(target, axis=0, keepdims=True), own_top.shape)
    stat[0, 0], stat[0, 1], stat[0, 2] = own_top, own_total, own_target
    copy = sender.start(stat.at[0], stat_pair, grid.twin)
    quarter = total_mask // 4
    parts = [dot_plain(table_t[...], expo[:, :quarter])]
    copy.wait()
    stat[1, 0], stat[1, 1], stat[1, 2] = merge_stats(
        [(own_top, own_total, own_target), (stat_pair[0], stat_pair[1], stat_pair[2])]
    )
    stat_square[square] = stat[1]
    flying = [sender.start(stat.at[1], stat_square.at[square], peer) for peer, _ in grid.squares]
    parts.append(dot_plain(table_t[...], expo[:, quarter : 2 * quarter]))
    wait_all(flying)
    stat[2, 0], stat[2, 1], stat[2, 2] = merge_stats(
        [(stat_square[i, 0], stat_square[i, 1], stat_square[i, 2]) for i in range(4)]
    )
    stat_line[line] = stat[2]
    flying = [sender.start(stat.at[2], stat_line.at[line], peer) for peer, _ in grid.lines]
    parts.append(dot_plain(table_t[...], expo[:, 2 * quarter : 3 * quarter]))
    parts.append(dot_plain(table_t[...], expo[:, 3 * quarter :]))
    wait_all(flying)
    full_top, full_total, full_target = merge_stats(
        [(stat_line[i, 0], stat_line[i, 1], stat_line[i, 2]) for i in range(4)]
    )
    lse = full_top + jnp.log(full_total)
    all_lse = jnp.sum(jnp.sum(lse, axis=1, keepdims=True), axis=0, keepdims=True)
    total_loss[...] = (all_lse - full_target[0:1]) * grad_scale
    mine = lax.broadcasted_iota(jnp.int32, (count, total_mask), 0) + lax.axis_index("dp") * count
    hit = mine == lax.broadcasted_iota(jnp.int32, (count, total_mask), 1)
    own_lse = jnp.sum(jnp.where(hit, unfold(lse), 0.0), axis=1, keepdims=True)
    turned = jnp.broadcast_to(own_lse - target, (count, 128)).T
    losses[...] = turned[0:1].reshape(count)
    scale = unfold(jnp.exp(own_top - lse) * grad_scale)
    per = 128 // count
    for index in range(total_mask // 128):
        at = slice(index * 128, index * 128 + 128)
        source = parts[index * 128 // quarter]
        begin = index * 128 % quarter
        piece = (source[:, begin : begin + 128] * scale[:, at]).T.astype(jnp.bfloat16)
        for inner in range(per):
            owner = index * per + inner
            part[owner // 8, owner // 2 % 4, owner % 2] = piece[inner * count : inner * count + count]
    copy = sender.start(part.at[:, :, 1 - core], land_pair, grid.twin)

    scaled = []
    for index in range(total_mask // 128):
        at = slice(index * 128, index * 128 + 128)
        column = jnp.broadcast_to(scale[:, at], (128, 128)).T
        column = jnp.concatenate([column] * (wide // 128), axis=1)
        scaled.append((all_heads[at].astype(jnp.float32) * column).astype(jnp.bfloat16))
    scaled = jnp.concatenate(scaled, axis=0)
    slab = rows // 4

    def grad_part(index):
        at = slice(index * slab, index * slab + slab)
        table_grad[at] = dot_plain(expo[at], scaled)

    grad_part(0)
    copy.wait()
    sum_pair[...] = (part[:, :, core].astype(jnp.float32) + land_pair[...].astype(jnp.float32)).astype(
        jnp.bfloat16
    )
    flying = [
        sender.start(sum_pair.at[:, other], land_square.at[square], peer)
        for peer, other in grid.squares
    ]
    land_square[square] = sum_pair[:, square]
    grad_part(1)
    wait_all(flying)
    sum_square[...] = sum(land_square[i].astype(jnp.float32) for i in range(4)).astype(jnp.bfloat16)
    flying = [
        sender.start(sum_square.at[other], land_line.at[line], peer) for peer, other in grid.lines
    ]
    land_line[line] = sum_square[line]
    grad_part(2)
    high = scale.astype(jnp.bfloat16)
    low = (scale - high.astype(jnp.float32)).astype(jnp.bfloat16)
    both = jnp.concatenate(
        [high.astype(jnp.float32), low.astype(jnp.float32), jnp.zeros((14, total_mask), jnp.float32)],
        axis=0,
    ).astype(jnp.bfloat16)
    sums = dot_right_t(both, expo[...])
    bias_grad[...] = sums[0:1] + sums[1:2]
    grad_part(3)
    wait_all(flying)
    head_grad[...] = sum(land_line[i].astype(jnp.float32) for i in range(4))


def head_and_table(
    head_low, entity_table, bias_row, target_vecs, target_bias, grad_scale, collective_id
):
    count, wide = head_low.shape
    rows = entity_table.shape[0]
    total_mask = 32 * count
    low, full = jnp.bfloat16, jnp.float32
    vmem = pl.BlockSpec(memory_space=pltpu.VMEM)
    folded = (total_mask // 128, 128)
    return pl.pallas_call(
        functools.partial(head_kernel, grad_scale),
        out_shape=[
            jax.ShapeDtypeStruct((rows, wide), full),
            jax.ShapeDtypeStruct((1, rows), full),
            jax.ShapeDtypeStruct((count,), full),
            jax.ShapeDtypeStruct((1, 128), full),
            jax.ShapeDtypeStruct((count, wide), full),
        ],
        in_specs=[vmem] * 5,
        out_specs=[vmem] * 5,
        scratch_shapes=[
            pltpu.VMEM((4, 4, 2, count, wide), low),
            pltpu.VMEM((rows, total_mask), full),
            pltpu.VMEM((rows, total_mask), low),
            pltpu.VMEM((wide, rows), low),
            pltpu.VMEM((rows, 128), full),
            pltpu.VMEM((4, 4, 2, count, wide), low),
            pltpu.VMEM((4, 4, count, wide), low),
            pltpu.VMEM((4, 4, count, wide), low),
            pltpu.VMEM((4, 4, count, wide), low),
            pltpu.VMEM((4, count, wide), low),
            pltpu.VMEM((4, count, wide), low),
            pltpu.VMEM((3, 3) + folded, full),
            pltpu.VMEM((3,) + folded, full),
            pltpu.VMEM((4, 3) + folded, full),
            pltpu.VMEM((4, 3) + folded, full),
            pltpu.SemaphoreType.DMA((24,)),
            pltpu.SemaphoreType.DMA((24,)),
        ],
        compiler_params=pltpu.CompilerParams(
            collective_id=collective_id, has_side_effects=True, vmem_limit_bytes=63 * 2**20
        ),
    )(head_low, entity_table, bias_row, target_vecs, target_bias)


def norm_slope(value, given, gain):
    scaled, rate = norm_parts(value)
    back = given * gain
    mean_back = jnp.mean(back, axis=-1, keepdims=True)
    mean_both = jnp.mean(back * scaled, axis=-1, keepdims=True)
    grad = rate * (back - mean_back - scaled * mean_both)
    return (
        grad,
        jnp.sum(given * scaled, axis=0, keepdims=True),
        jnp.sum(given, axis=0, keepdims=True),
    )


def split_low(value):
    high = value.astype(jnp.bfloat16)
    return high, (value - high.astype(jnp.float32)).astype(jnp.bfloat16)


def place_rows(source, order, count, store):
    owners = 2 ** len(order)
    for pair in range(owners // 2):
        one, two = place_owner(order, 2 * pair), place_owner(order, 2 * pair + 1)
        both = jnp.concatenate(
            [source[one * count : one * count + count], source[two * count : two * count + count]],
            axis=0,
        )
        store(slice(pair * 2 * count, (pair + 1) * 2 * count), both.astype(jnp.bfloat16))


def middle_back_kernel(
    orders,
    grad_scale,
    stage,
    head_grad,
    target_vecs,
    head_pre,
    gain_head,
    picked,
    head_w,
    choose,
    cotangent,
    resid_two,
    gain_two,
    normed_low,
    resid_one,
    gain_one,
    out_w,
    context,
    lse_lanes,
    active_hbm,
    slope_hbm,
    up_hbm,
    down_hbm,
    up_a,
    up_b,
    head_a,
    out_b,
    down_b,
    up_c,
    down_c,
    first_grad,
    context_grad,
    lse_delta,
    vectors,
    active,
    slope,
    up_w,
    down_w,
    flip,
    normed_t,
    context_t,
    down_in,
    acc,
    up_low,
    stage_a,
    stage_c,
    sems,
):
    seq_len, width = cotangent.shape
    slots = choose.shape[1]
    words = seq_len - slots
    cuts = down_w.shape[0] // width
    loads = []
    for index, (source, target) in enumerate(
        ((active_hbm, active), (down_hbm, down_w), (slope_hbm, slope), (up_hbm, up_w))
    ):
        for cut in range(cuts):
            at = pl.ds(cut * width, width)
            view = (at,) if index == 1 else (slice(None), at)
            loads.append(
                pltpu.make_async_copy(source.at[view], target.at[view], sems.at[index * cuts + cut])
            )
    for cut in range(cuts):
        for index in range(4):
            loads[index * cuts + cut].start()

    given = head_grad[...] - grad_scale * target_vecs[...]
    pre = head_pre[...]
    raised, change = gelu_parts(pre)
    back, gain_sum, bias_sum = norm_slope(raised, given, gain_head[...][None, :])
    sums = [gain_sum, bias_sum]
    pre_low = (back * change).astype(jnp.bfloat16)
    head_weight_grad = dot_left_t(picked[...], pre_low)
    count = width // 2 ** len(orders[0])

    def keep_head(at, value):
        head_a[0, at] = value

    flip[:, : head_a.shape[2]] = head_weight_grad
    place_rows(flip[:, : head_a.shape[2]], orders[0], count, keep_head)
    stage.need(5)
    picked_high, picked_rest = split_low(dot_right_t(pre_low, head_w[...]))
    placed = dot_left_t(choose[...], picked_high) + dot_left_t(choose[...], picked_rest)

    stage.need(7, 8)
    block = 128
    total_gain = jnp.zeros((1, width), jnp.float32)
    total_bias = jnp.zeros((1, width), jnp.float32)
    for begin in range(0, seq_len, block):
        at = slice(begin, begin + block)
        given = cotangent[at].astype(jnp.float32)
        if begin >= words:
            given = given + placed[begin - words : begin - words + block]
        grad, gain_sum, bias_sum = norm_slope(resid_two[at], given, gain_two[...][None, :])
        total_gain += gain_sum
        total_bias += bias_sum
        acc[at] = grad
        down_in[at] = grad.astype(jnp.bfloat16)
    sums += [total_gain, total_bias]

    def flip_into(source, target, order_list):
        def flip_step(index, carry):
            at = pl.ds(pl.multiple_of(index * block, block), block)
            flip[at] = source[:, at].astype(jnp.float32).T
            return carry

        lax.fori_loop(0, width // block, flip_step, 0)
        for slot, order in enumerate(order_list):

            def keep(at, value, slot=slot):
                target[slot, at] = value

            place_rows(flip, order, count, keep)

    stage.need(10, 14)
    flip_into(normed_low, normed_t, (orders[0], orders[2]))
    flip_into(context, context_t, (orders[1],))

    column = 384
    span = seq_len
    block_two = seq_len // 2
    split = down_b.shape[2]
    owners = 2 ** len(orders[0])
    tall = down_w.shape[0] // owners
    spots = [
        {place_owner(order, place): place for place in range(owners)}
        for order in (orders[1], orders[2])
    ]
    stores = []
    for cut in range(cuts):
        at = slice(cut * width, cut * width + width)
        for index in range(4):
            loads[index * cuts + cut].wait()
        for begin in range(0, width, column):
            piece = dot_left_t(active[:, at], down_in[:, begin : begin + column])
            for inner in range(width // tall):
                owner = cut * (width // tall) + inner
                rows = piece[inner * tall : inner * tall + tall].astype(jnp.bfloat16)
                stop = min(begin + column, split)
                if begin < split:
                    place = spots[0][owner] * tall
                    stage_a[place : place + tall, begin:stop] = rows[:, : stop - begin]
                if begin + column > split:
                    start = max(begin, split)
                    place = spots[1][owner] * tall
                    stage_c[place : place + tall, start - split : begin + column - split] = rows[
                        :, start - begin :
                    ]

        def back_step(index, carry, at=at):
            rows = pl.ds(pl.multiple_of(index * span, 16), span)
            grad = dot_right_t(down_in[rows], down_w[at]) * slope[rows, at].astype(jnp.float32)
            grad = grad.astype(jnp.bfloat16)
            up_low[rows] = grad
            acc[rows] = acc[rows] + dot_right_t(grad, up_w[:, at])
            return carry

        lax.fori_loop(0, seq_len // span, back_step, 0)
        target, slot, order_slot = ((up_a, 0, 0), (up_a, 1, 0), (up_b, 0, 0), (up_c, 0, 1))[cut]
        for begin in range(0, width, column):
            target[slot, :, begin : begin + column] = dot_plain(
                normed_t[order_slot], up_low[:, begin : begin + column]
            ).astype(jnp.bfloat16)
    stage.send(0, 1, 5)
    stage.need(11, 13)
    stores = [
        pltpu.make_async_copy(stage_a, down_b.at[0], sems.at[4 * cuts]),
        pltpu.make_async_copy(stage_c, down_c.at[0], sems.at[4 * cuts + 1]),
    ]
    for store in stores:
        store.start()

    total_gain = jnp.zeros((1, width), jnp.float32)
    total_bias = jnp.zeros((1, width), jnp.float32)
    row = lax.broadcasted_iota(jnp.int32, (width, 128), 0)
    lane = lax.broadcasted_iota(jnp.int32, (width, 128), 1)
    spot = 4 * lax.div(row, 128) + 2 + lax.div(lax.rem(row, 128), HD)
    pick = (spot == lane).astype(jnp.float32).astype(jnp.bfloat16)
    for begin in range(0, seq_len, block_two):
        at = slice(begin, begin + block_two)
        grad, gain_sum, bias_sum = norm_slope(resid_one[at], acc[at], gain_one[...][None, :])
        total_gain += gain_sum
        total_bias += bias_sum
        first_grad[at] = grad
        low = grad.astype(jnp.bfloat16)
        down_in[at] = low
        back = dot_right_t(low, out_w[...]).astype(jnp.bfloat16)
        context_grad[at] = back
        high, rest = split_low(back.astype(jnp.float32) * context[at].astype(jnp.float32))
        lse_delta[at] = lse_lanes[at] + dot_plain(high, pick) + dot_plain(rest, pick)
    stage.send(7, 8)
    sums += [total_gain, total_bias]
    tall, room = vectors.shape[1:]
    every = tall // owners
    placed = jnp.zeros((tall, room), jnp.float32)
    offset = 0
    for vector in sums:
        size = vector.shape[1]
        per = size // owners
        row = lax.broadcasted_iota(jnp.int32, (tall, size), 0)
        place = lax.div(row, every)
        owner = jnp.zeros((tall, size), jnp.int32)
        for spot, mask in enumerate(orders[0]):
            owner += lax.rem(lax.div(place, 2 ** (len(orders[0]) - 1 - spot)), 2) * mask
        column_at = lax.broadcasted_iota(jnp.int32, (tall, size), 1)
        mine = (lax.div(column_at, per) == owner) & (lax.rem(row, every) == 0)
        spread = jnp.where(mine, vector, 0.0).astype(jnp.bfloat16)
        source = lax.broadcasted_iota(jnp.int32, (size, room), 0)
        target = lax.broadcasted_iota(jnp.int32, (size, room), 1)
        move = (lax.rem(source, per) + offset == target).astype(jnp.float32).astype(jnp.bfloat16)
        placed += dot_plain(spread, move)
        offset += per
    vectors[0] = placed.astype(jnp.bfloat16)
    for begin in range(0, width, column):
        out_b[0, :, begin : begin + column] = dot_plain(
            context_t[0], down_in[:, begin : begin + column]
        ).astype(jnp.bfloat16)
    for store in stores:
        store.wait()


DOWN_SPLIT = 512


def middle_back(inputs, orders, grad_scale):
    seq_len, width = inputs[7].shape
    hidden_units = inputs[16].shape[1]
    head_width = inputs[0].shape[1]
    low, full = jnp.bfloat16, jnp.float32
    cuts = hidden_units // width
    vmem, hbm = pl.BlockSpec(memory_space=pltpu.VMEM), pl.BlockSpec(memory_space=pltpu.HBM)
    shapes = [
        ((2, width, width), low),
        ((1, width, width), low),
        ((1, width, head_width), low),
        ((1, width, width), low),
        ((1, hidden_units, DOWN_SPLIT), low),
        ((1, width, width), low),
        ((1, hidden_units, width - DOWN_SPLIT), low),
        ((seq_len, width), full),
        ((seq_len, width), low),
        ((seq_len, 128), full),
        ((1, 8 * 2 ** len(orders[0]), 256), low),
    ]
    outs = [jax.ShapeDtypeStruct(*shape) for shape in shapes]
    return staged_call(
        functools.partial(middle_back_kernel, orders, grad_scale),
        inputs,
        outs,
        [vmem] * 16 + [hbm] * 4,
        [hbm if index in (4, 6) else vmem for index in range(len(shapes))],
        (5, 7, 8, 10, 14, 11, 13),
        (0, 1, 3, 5, 7, 8),
        [
            pltpu.VMEM((seq_len, hidden_units), low),
            pltpu.VMEM((seq_len, hidden_units), low),
            pltpu.VMEM((width, hidden_units), low),
            pltpu.VMEM((hidden_units, width), low),
            pltpu.VMEM((width, seq_len), full),
            pltpu.VMEM((2, width, seq_len), low),
            pltpu.VMEM((1, width, seq_len), low),
            pltpu.VMEM((seq_len, width), low),
            pltpu.VMEM((seq_len, width), full),
            pltpu.VMEM((seq_len, width), low),
            pltpu.VMEM((hidden_units, DOWN_SPLIT), low),
            pltpu.VMEM((hidden_units, width - DOWN_SPLIT), low),
            pltpu.SemaphoreType.DMA((4 * cuts + 2,)),
        ],
        pltpu.CompilerParams(vmem_limit_bytes=63 * 2**20),
    )


def last_kernel(grad_scale, codes, back, table_hbm, bias_in, *refs):
    sums, refs = refs[:SUMS], refs[SUMS:]
    table_out, bias_out = refs[:2]
    outs, refs = refs[2 : 2 + SUMS - 4], refs[2 + SUMS - 4 :]
    flats, refs = refs[: len(FLAT)], refs[len(FLAT) :]
    table_in, result, sems, move_sems = refs
    rows = table_hbm.shape[0]
    entries = back.shape[0]
    step = 1024
    parts = [(begin, min(step, rows - begin)) for begin in range(0, rows, step)]
    loads = [
        pltpu.make_async_copy(
            table_hbm.at[pl.ds(begin, size)], table_in.at[pl.ds(begin, size)], sems.at[0, index]
        )
        for index, (begin, size) in enumerate(parts)
    ]
    stores = [
        pltpu.make_async_copy(
            result.at[pl.ds(begin, size)], table_out.at[pl.ds(begin, size)], sems.at[1, index]
        )
        for index, (begin, size) in enumerate(parts)
    ]
    for load in loads:
        load.start()
    up_two, down_a, up_last, down_b, up_third = sums[:5]
    up_out, down_out = outs[:2]
    width = up_last.shape[2]
    pairs = [
        (value, up_out.at[:, pl.ds(index * width, width)])
        for index, value in enumerate((up_two.at[0], up_two.at[1], up_third.at[0], up_last.at[0]))
    ]
    pairs.append((down_a.at[0], down_out.at[:, pl.ds(0, down_a.shape[2])]))
    pairs.append((down_b.at[0], down_out.at[:, pl.ds(down_a.shape[2], down_b.shape[2])]))
    rest = [value for index, value in enumerate(sums) if index > 4 and index != VECTOR]
    pairs += [(source.at[0], target) for source, target in zip(rest, outs[2:])]
    moves = [
        pltpu.make_async_copy(source, target, move_sems.at[index])
        for index, (source, target) in enumerate(pairs)
    ]
    for move in moves:
        move.start()
    code = codes[0:1]
    target = (code >= rows).astype(jnp.float32)
    flags = jnp.broadcast_to(target, (16, entries)).astype(jnp.bfloat16)
    code = jnp.where(code >= rows, code - rows, code)
    for index, (begin, size) in enumerate(parts):
        row = lax.broadcasted_iota(jnp.int32, (size, entries), 0) + begin
        match = (row == code).astype(jnp.float32).astype(jnp.bfloat16)
        at = slice(begin, begin + size)
        counts = dot_right_t(flags, match)
        bias_out[at] = (bias_in[:, at] - grad_scale * counts[0:1]).reshape(size)
        added = dot_plain(match, back[...])
        loads[index].wait()
        result[at] = table_in[at] + added
        stores[index].start()
    offset = 0
    for target in flats:
        size = target.shape[0]
        target[...] = sums[VECTOR][0, 0:1, offset : offset + size].reshape(size)
        offset += size
    for copy in stores + moves:
        copy.wait()


SUMS = 15
VECTOR = 6
FLAT = (0, 0, 1, 1, 1, 1)


def last_step(codes, back, table_grad, bias_grad, sums, sizes, grad_scale):
    vmem, hbm = pl.BlockSpec(memory_space=pltpu.VMEM), pl.BlockSpec(memory_space=pltpu.HBM)
    full = jnp.float32
    up_rows, width = sums[0].shape[1:]
    down_rows = sums[1].shape[1]
    shapes = [
        table_grad.shape,
        (bias_grad.shape[1],),
        (up_rows, 4 * width),
        (down_rows, width),
    ] + [value.shape[1:] for index, value in enumerate(sums) if index > 4 and index != VECTOR]
    shapes += [(sizes[kind],) for kind in FLAT]
    return pl.pallas_call(
        functools.partial(last_kernel, grad_scale),
        out_shape=[jax.ShapeDtypeStruct(shape, full) for shape in shapes],
        in_specs=[vmem, vmem, hbm, vmem] + [vmem] * len(sums),
        out_specs=[hbm, vmem] + [hbm] * (len(shapes) - 2 - len(FLAT)) + [vmem] * len(FLAT),
        scratch_shapes=[
            pltpu.VMEM(table_grad.shape, full),
            pltpu.VMEM(table_grad.shape, full),
            pltpu.SemaphoreType.DMA((2, 8)),
            pltpu.SemaphoreType.DMA((len(sums) + 1,)),
        ],
        compiler_params=pltpu.CompilerParams(vmem_limit_bytes=63 * 2**20),
    )(codes, back, table_grad, bias_grad, *sums)


def place_owner(order, place):
    bits = len(order)
    return sum(((place >> (bits - 1 - spot)) & 1) * mask for spot, mask in enumerate(order))


class Piece:
    def __init__(
        self, rows, stages, send, own, land, tail, pack, tail_land, out, send_sem, recv_sem
    ):
        self.rows, self.stages = rows, stages
        self.send, self.own, self.land = send, own, land
        self.tail, self.pack, self.tail_land, self.out = tail, pack, tail_land, out
        self.send_sem, self.recv_sem = send_sem, recv_sem
        self.sizes = [rows * 2 ** (stages - 1 - stage) for stage in range(stages)]
        self.spots = [sum(self.sizes[:stage]) for stage in range(stages)]

    def copy(self, stage, partner, bit):
        size = self.sizes[stage]
        away = (1 - bit) * size
        if stage < self.stages - 1:
            away = pl.multiple_of(away, 16)
        if stage == 0:
            source, target = self.send.at[:, pl.ds(away, size)], self.land.at[:, pl.ds(0, size)]
        elif stage < self.stages - 1:
            spot = pl.multiple_of(self.spots[stage - 1] + away, 16)
            source = self.land.at[:, pl.ds(spot, size)]
            target = self.land.at[:, pl.ds(self.spots[stage], size)]
        else:
            source, target = self.pack, self.tail_land
        return pltpu.make_async_remote_copy(
            src_ref=source,
            dst_ref=target,
            send_sem=self.send_sem.at[stage],
            recv_sem=self.recv_sem.at[stage],
            device_id=(partner,),
            device_id_type=MESH_ID,
        )

    def held(self, stage, bit):
        size = self.sizes[stage]
        if stage == 0 and self.own is not None:
            return self.own, 0
        if stage == 0:
            return self.send, pl.multiple_of(bit * size, 16)
        return self.land, pl.multiple_of(self.spots[stage - 1] + bit * size, 16)

    def add(self, stage, bit, half_index):
        size = self.sizes[stage]
        half = size // 2
        unit = 48 if half % 48 == 0 else 16
        start = half_index * half
        source, base = self.held(stage, bit)
        for slot in range(self.land.shape[0]):

            def step(index, carry, slot=slot):
                row = pl.multiple_of(start + index * unit, 16)
                mine = source[slot, pl.ds(pl.multiple_of(base + row, 16), unit)]
                spot = pl.ds(pl.multiple_of(self.spots[stage] + row, 16), unit)
                theirs = self.land[slot, spot]
                total = mine.astype(jnp.float32) + theirs.astype(jnp.float32)
                self.land[slot, spot] = total.astype(jnp.bfloat16)
                return carry

            lax.fori_loop(0, half // unit, step, 0)

    def add_tail(self, stage, bit, following):
        size = self.sizes[stage]
        half = size // 2
        middle = self.land.shape[2] // 2
        source, base = self.held(stage, bit)
        for slot in range(self.land.shape[0]):
            mine = source[slot, pl.ds(base, size)]
            theirs = self.land[slot, pl.ds(self.spots[stage], size)]
            self.tail[slot] = mine.astype(jnp.float32) + theirs.astype(jnp.float32)
            other = self.tail[slot, pl.ds(pl.multiple_of((1 - following) * half, 8), half)]
            self.pack[slot] = jnp.concatenate(
                [other[:, :middle], other[:, middle:]], axis=0
            ).astype(jnp.bfloat16)

    def finish(self, bit):
        size = self.sizes[-1]
        for slot in range(self.out.shape[0]):
            mine = self.tail[slot, pl.ds(pl.multiple_of(bit * size, 8), size)]
            theirs = self.tail_land[slot].astype(jnp.float32)
            self.out[slot] = mine + jnp.concatenate([theirs[:size], theirs[size:]], axis=1)


class Stream:
    def __init__(self, order, partner_of, pieces):
        self.order, self.partner_of, self.pieces = order, partner_of, pieces
        self.stages = len(order)

    def launch(self, stage):
        partner, bit = self.partner_of[self.order[stage]]
        for piece in self.pieces:
            piece.copy(stage, partner, bit).start()

    def advance(self, stage):
        partner, bit = self.partner_of[self.order[stage]]
        for piece in self.pieces:
            piece.copy(stage, partner, bit).wait()
        if stage == self.stages - 1:
            for piece in self.pieces:
                piece.finish(bit)
        elif stage == self.stages - 2:
            for piece in self.pieces:
                piece.add_tail(stage, bit, self.partner_of[self.order[stage + 1]][1])
            self.launch(stage + 1)
        else:
            following = self.partner_of[self.order[stage + 1]][1]
            for piece in self.pieces:
                piece.add(stage, bit, 1 - following)
            self.launch(stage + 1)
            for piece in self.pieces:
                piece.add(stage, bit, following)


def partners(me, masks):
    result = {}
    for mask in masks:
        bit = lax.rem(lax.div(me, mask), 2)
        result[mask] = (me + mask - 2 * mask * bit, bit)
    return result


EARLY = (
    (0, 2, 24, 768),
    (1, 1, 96, 512),
    (2, 1, 24, 768),
    (3, 1, 96, 256),
    (4, 1, 24, 768),
    (4, 1, 24, 256),
    (4, 1, 8, 256),
    (5, 1, 24, 768),
)
LATE = (
    (6, 1, 24, 768),
    (7, 1, 24, 768),
    (8, 1, 24, 768),
    (9, 1, 24, 768),
    (10, 1, 24, 768),
    (11, 1, 24, 768),
    (11, 1, 8, 768),
)
STREAM_ORDER = (0, 1, 2, 2, 0, 1, 1, 1, 2, 1, 0, 0)

WORD_POINTS = ("word0", "word1")

PLAN = {('r', 1): ((0, 0),), ('p', 1): ((1, 0),), ('r', 2): ((2, 0), (3, 0)), ('p', 2): ((4, 0),), ('r', 3): ((5, 0),), ('r', 4): ((2, 1),), ('r', 5): ((0, 1),), 'KV': ((1, 1),), 'ew': ((3, 1),), 'ww': ((4, 1),), 'ent': ((6, 0), (2, 2), (7, 0), (5, 1), (8, 0)), 'we': ((9, 0),), 'word0': ((10, 0),), 'word1': ((1, 2), (11, 0), (3, 2), (0, 2), (2, 3)), 'end': ((8, 1), (5, 2), (4, 2), (1, 3), (10, 1), (0, 3), (6, 1), (8, 2), (5, 3), (7, 1), (4, 3), (11, 1), (1, 4), (3, 3), (0, 4), (5, 4), (4, 4), (9, 1), (6, 2), (2, 4), (8, 3), (10, 2), (6, 3), (7, 2), (10, 3), (11, 2), (9, 2), (6, 4), (3, 4), (8, 4), (7, 3), (10, 4), (11, 3), (9, 3), (7, 4), (11, 4), (9, 4))}


def piece_scratch(spec, stages, source, own):
    _, slots, rows, width = spec
    owners = 2**stages
    shapes = []
    if source:
        shapes.append(pltpu.VMEM((slots, rows * owners, width), jnp.bfloat16))
    if own:
        shapes.append(pltpu.VMEM((slots, rows * owners // 2, width), jnp.bfloat16))
    shapes += [
        pltpu.VMEM((slots, rows * (owners - 2), width), jnp.bfloat16),
        pltpu.VMEM((slots, 2 * rows, width), jnp.float32),
        pltpu.VMEM((slots, 2 * rows, width // 2), jnp.bfloat16),
        pltpu.VMEM((slots, 2 * rows, width // 2), jnp.bfloat16),
        pltpu.SemaphoreType.DMA((stages,)),
        pltpu.SemaphoreType.DMA((stages,)),
    ]
    return shapes


def attention_back_kernel(orders, grad_scale, *refs):
    stages = len(orders[0])
    refs = list(refs)

    def take(count):
        taken = refs[:count]
        del refs[:count]
        return taken

    early_send = take(len(EARLY))
    (hidden, qword, qent, keys, values, cgrad, feat_q, feat_k, lse_delta, first_grad, head_low, slot_row) = take(12)
    (w_ww, w_we, w_ew, w_ee, w_key, w_value, dense, entity_low) = take(8)
    early_out = take(len(EARLY))
    late_out = take(len(LATE))
    words_out, request_out = take(2)
    devices = request_out.shape[0]
    early_pieces = []
    own_copies = []
    me = lax.axis_index("dp")
    partner_of = partners(me, orders[0])
    own_sem = refs.pop()
    request_sems = refs.pop()
    request_send = refs.pop()
    word_weights = []
    dqw, dqe, dkey, dvalue, prob_s, grad_s, flip, hidden_t, hidden_te, entity_t = refs[-10:]
    del refs[-10:]
    pieces = [[] for _ in STREAM_ORDER]
    early_flat = []
    for index, spec in enumerate(EARLY):
        own, land, tail, pack, tail_land, send_sem, recv_sem = take(7)
        piece = Piece(
            spec[2], stages, early_send[index], own, land, tail, pack, tail_land,
            early_out[index], send_sem, recv_sem,
        )
        pieces[spec[0]].append(piece)
        early_flat.append(piece)
        bit = partner_of[orders[STREAM_ORDER[spec[0]]][0]][1]
        size = spec[2] * 2 ** (stages - 1)
        own_copies.append(
            pltpu.make_async_copy(
                early_send[index].at[:, pl.ds(pl.multiple_of(bit * size, 16), size)],
                own,
                own_sem.at[index],
            )
        )
    late_source = []
    for index, spec in enumerate(LATE):
        source, land, tail, pack, tail_land, send_sem, recv_sem = take(7)
        late_source.append(source)
        pieces[spec[0]].append(
            Piece(
                spec[2], stages, source, None, land, tail, pack, tail_land,
                late_out[index], send_sem, recv_sem,
            )
        )
    spare = (early_flat[1].own, early_flat[3].own)
    split = spare[0].shape[2]
    for index, weight in enumerate((w_ww, w_we)):
        rows = weight.shape[0]
        for part, at in enumerate((pl.ds(0, split), pl.ds(split, weight.shape[1] - split))):
            word_weights.append(
                pltpu.make_async_copy(
                    weight.at[:, at],
                    spare[part].at[0, pl.ds(index * rows, rows)],
                    own_sem.at[len(EARLY) + 2 * index + part],
                )
            )
    streams = [
        Stream(orders[order], partner_of, pieces[index])
        for index, order in enumerate(STREAM_ORDER)
    ]
    first_late = LATE[0][0]

    def go_on(point):
        for index, stage in PLAN.get(point, ()):
            if stage == 0 and index < first_late:
                for piece, spec in enumerate(EARLY):
                    if spec[0] == index:
                        own_copies[piece].wait()
            streams[index].advance(stage)
            if stage == 0 and index in (1, 3):
                for copy in word_weights[(index - 1) // 2 :: 2]:
                    copy.start()

    greet_all(me, devices)
    for stream in streams[:first_late]:
        stream.launch(0)
    for copy in own_copies:
        copy.start()

    width = hidden.shape[1]
    seq_len = hidden.shape[0]
    words = words_out.shape[0]
    block = 128
    tall = seq_len // 2
    taller = words // len(WORD_POINTS)
    lane = lax.broadcasted_iota(jnp.int32, (1, block), 1)
    low_half = (lane < HD).astype(jnp.float32).astype(jnp.bfloat16)
    high_half = (lane >= HD).astype(jnp.float32).astype(jnp.bfloat16)
    halves = (low_half, high_half)

    def flip_step(index, carry):
        at = pl.ds(pl.multiple_of(index * block, block), block)
        flip[at] = hidden[:, at].astype(jnp.float32).T
        return carry

    lax.fori_loop(0, width // block, flip_step, 0)
    owners = 2**stages
    rows = width // owners
    for slot, order in enumerate(orders):
        begin = words if slot == 2 else 0
        for pair in range(owners // 2):
            one, two = place_owner(order, 2 * pair), place_owner(order, 2 * pair + 1)
            both = jnp.concatenate(
                [flip[one * rows : one * rows + rows, begin:], flip[two * rows : two * rows + rows, begin:]],
                axis=0,
            ).astype(jnp.bfloat16)
            if slot == 2:
                hidden_te[pair * 2 * rows : (pair + 1) * 2 * rows] = both
            else:
                hidden_t[slot, pair * 2 * rows : (pair + 1) * 2 * rows] = both

    go_on("start")

    def go_on_in_loop(name, pair):
        for point in range(width // block):
            if (name, point) in PLAN:
                pl.when(pair == point)(functools.partial(go_on, (name, point)))

    def pair_step(pair, carry):
        lanes = pl.ds(pl.multiple_of(pair * block, block), block)
        key_pair = keys[:, lanes]
        value_pair = values[:, lanes]
        key_feat = [key_pair * halves[h] + feat_k[...] * halves[1 - h] for h in range(2)]
        key_only = [key_pair * halves[h] for h in range(2)]
        value_only = [value_pair * halves[h] for h in range(2)]

        def row_step(index, inner):
            at = pl.ds(pl.multiple_of(index * tall, 16), tall)
            qw = qword[at, lanes]
            qe = qent[at, lanes]
            feats = feat_q[at]
            given = cgrad[at, lanes]
            stats = lse_delta[at]
            spot = lax.broadcasted_iota(jnp.int32, (1, block), 1) - 4 * pair
            total_w = jnp.zeros((tall, block), jnp.float32)
            total_e = jnp.zeros((tall, block), jnp.float32)
            for h in range(2):
                left_w = qw * halves[h] + feats * halves[1 - h]
                left_e = qe * halves[h] + feats * halves[1 - h]
                scores = jnp.concatenate(
                    [
                        dot_right_t(left_w, key_feat[h][:words]),
                        dot_right_t(left_e, key_feat[h][words:]),
                    ],
                    axis=1,
                )
                prob = jnp.exp(scores - jnp.sum(jnp.where(spot == h, stats, 0.0), axis=1, keepdims=True))
                pgrad = dot_right_t(given, value_only[h])
                sgrad = (prob * (pgrad - jnp.sum(jnp.where(spot == 2 + h, stats, 0.0), axis=1, keepdims=True))).astype(jnp.bfloat16)
                prob_s[h, at] = prob.astype(jnp.bfloat16)
                grad_s[h, at] = sgrad
                total_w += dot_plain(sgrad[:, :words], key_only[h][:words])
                total_e += dot_plain(sgrad[:, words:], key_only[h][words:])
            dqw[at, lanes] = total_w.astype(jnp.bfloat16)
            dqe[at, lanes] = total_e.astype(jnp.bfloat16)
            return inner

        lax.fori_loop(0, seq_len // tall, row_step, 0)
        go_on_in_loop("r", pair)
        qw_all, qe_all, given_all = qword[:, lanes], qent[:, lanes], cgrad[:, lanes]
        dkey[:words, lanes] = (
            dot_left_t(grad_s[0, :, :words], qw_all * halves[0])
            + dot_left_t(grad_s[1, :, :words], qw_all * halves[1])
        ).astype(jnp.bfloat16)
        dkey[words:, lanes] = (
            dot_left_t(grad_s[0, :, words:], qe_all * halves[0])
            + dot_left_t(grad_s[1, :, words:], qe_all * halves[1])
        ).astype(jnp.bfloat16)
        dvalue[:, lanes] = (
            dot_left_t(prob_s[0], given_all * halves[0])
            + dot_left_t(prob_s[1], given_all * halves[1])
        ).astype(jnp.bfloat16)

        go_on_in_loop("p", pair)
        return carry

    lax.fori_loop(0, width // block, pair_step, 0)

    query_scale = HD ** (-0.5)
    column = 384

    def weight_grad(source, slot, order_slot, grad, begin, end, scale):
        for cut in range(0, width, column):
            left = hidden_te[...] if order_slot == 2 else hidden_t[order_slot, :, begin:end]
            piece = dot_plain(left, grad[begin:end, cut : cut + column])
            if scale:
                piece = piece * query_scale
            source[slot, :, cut : cut + column] = piece.astype(jnp.bfloat16)

    weight_grad(late_source[0], 0, 1, dkey, 0, seq_len, False)
    streams[6].launch(0)
    weight_grad(late_source[1], 0, 1, dvalue, 0, seq_len, False)
    streams[7].launch(0)
    go_on("KV")
    weight_grad(late_source[2], 0, 2, dqw, words, seq_len, True)
    streams[8].launch(0)
    go_on("ew")
    weight_grad(late_source[3], 0, 1, dqe, words, seq_len, True)
    streams[9].launch(0)
    go_on("ee")
    weight_grad(late_source[4], 0, 0, dqw, 0, words, True)
    streams[10].launch(0)
    go_on("ww")

    def data_grad(begin, size, queries):
        at = pl.ds(begin, size)
        return (
            first_grad[at]
            + query_scale * queries(at)
            + dot_right_t(dkey[at], w_key[...])
            + dot_right_t(dvalue[at], w_value[...])
        )

    def entity_queries(at):
        return dot_right_t(dqw[at], w_ew[...]) + dot_right_t(dqe[at], w_ee[...])

    def word_queries(at):
        total = 0.0
        for index, grad in enumerate((dqw, dqe)):
            rows_at = pl.ds(index * width, width)
            total += dot_right_t(grad[at, :split], spare[0][0, rows_at])
            total += dot_right_t(grad[at, split:], spare[1][0, rows_at])
        return total

    state_low = data_grad(words, seq_len - words, entity_queries).astype(jnp.bfloat16)
    vectors = jnp.concatenate(
        [dot_right_t(state_low, dense[...]).astype(jnp.bfloat16), (head_low[...].astype(jnp.float32) * -grad_scale).astype(jnp.bfloat16)], axis=0
    )
    entries = slot_row.shape[1]
    wanted = lax.broadcasted_iota(jnp.int32, (vectors.shape[0], entries), 0)
    placing = (wanted == slot_row[0:1]).astype(jnp.float32).astype(jnp.bfloat16)
    per_request = dot_left_t(placing, vectors).astype(jnp.bfloat16)
    request_send[...] = per_request.reshape(request_send.shape)

    def request_copy(step):
        peer = lax.rem(me + step, devices)
        return pltpu.make_async_remote_copy(
            src_ref=request_send.at[peer],
            dst_ref=request_out.at[me],
            send_sem=request_sems.at[0, step],
            recv_sem=request_sems.at[1, step],
            device_id=(peer,),
            device_id_type=MESH_ID,
        )

    def begin_request(step, carry):
        request_copy(step).start()
        return carry

    def finish_request(step, carry):
        request_copy(step).wait()
        return carry

    lax.fori_loop(1, devices, begin_request, 0)
    request_out[me] = request_send[me]
    entity_width = dense.shape[0]
    few = entity_width // owners
    for cut in range(0, entity_width, block):
        flip[cut : cut + block, :block] = entity_low[:, cut : cut + block].astype(jnp.float32).T
    for pair in range(owners // 2):
        one, two = place_owner(orders[0], 2 * pair), place_owner(orders[0], 2 * pair + 1)
        both = jnp.concatenate(
            [flip[one * few : one * few + few, :block], flip[two * few : two * few + few, :block]],
            axis=0,
        )
        entity_t[pair * 2 * few : (pair + 1) * 2 * few] = both.astype(jnp.bfloat16)
    late_source[6][0] = dot_plain(entity_t[...], state_low).astype(jnp.bfloat16)
    go_on("ent")
    weight_grad(late_source[5], 0, 0, dqe, 0, words, True)
    streams[11].launch(0)
    go_on("we")
    for copy in word_weights:
        copy.wait()

    def word_step(index, carry):
        begin = pl.multiple_of(index * taller, 16)
        words_out[pl.ds(begin, taller)] = data_grad(begin, taller, word_queries).astype(jnp.bfloat16)
        for point in range(words // taller):
            name = WORD_POINTS[point]
            if name in PLAN:
                pl.when(index == point)(functools.partial(go_on, name))
        return carry

    lax.fori_loop(0, words // taller, word_step, 0)
    go_on("end")
    lax.fori_loop(1, devices, finish_request, 0)


def in_order(grad, order):
    bits = len(order)
    owners = 2**bits
    view = grad.reshape((2,) * bits + (grad.shape[0] // owners, grad.shape[1]))
    spots = tuple(bits - mask.bit_length() for mask in order)
    return view.transpose(spots + (bits, bits + 1)).reshape(grad.shape)


def attention_back(early_grads, inputs, weights, grad_scale, collective_id):
    devices = lax.axis_size("dp")
    orders = stage_masks(devices)
    stages = len(orders[0])
    hidden = inputs[0]
    seq_len, width = hidden.shape
    slots = weights[-1].shape[0]
    words = seq_len - slots
    outs = [
        jax.ShapeDtypeStruct((count, rows, wide), jnp.float32)
        for _, count, rows, wide in EARLY + LATE
    ] + [
        jax.ShapeDtypeStruct((words, width), jnp.bfloat16),
        jax.ShapeDtypeStruct(
            (devices, inputs[11].shape[1] // devices, weights[-2].shape[0]), jnp.bfloat16
        ),
    ]
    scratch = []
    for spec in EARLY:
        scratch += piece_scratch(spec, stages, False, True)
    for spec in LATE:
        scratch += piece_scratch(spec, stages, True, False)
    scratch += [pltpu.VMEM((seq_len, width), jnp.bfloat16)] * 4
    scratch += [pltpu.VMEM((2, seq_len, seq_len), jnp.bfloat16)] * 2
    scratch += [
        pltpu.VMEM((width, seq_len), jnp.float32),
        pltpu.VMEM((2, width, seq_len), jnp.bfloat16),
        pltpu.VMEM((width, slots), jnp.bfloat16),
        pltpu.VMEM((weights[-2].shape[0], slots), jnp.bfloat16),
        pltpu.VMEM((devices, inputs[11].shape[1] // devices, weights[-2].shape[0]), jnp.bfloat16),
        pltpu.SemaphoreType.DMA((2, devices)),
        pltpu.SemaphoreType.DMA((len(EARLY) + 4,)),
    ]
    vmem = pl.BlockSpec(memory_space=pltpu.VMEM)
    return pl.pallas_call(
        functools.partial(attention_back_kernel, orders, grad_scale),
        out_shape=outs,
        in_specs=[pl.BlockSpec(memory_space=pltpu.HBM)] * len(EARLY)
        + [vmem] * len(inputs)
        + [pl.BlockSpec(memory_space=pltpu.HBM)] * 2
        + [vmem] * (len(weights) - 2),
        out_specs=[vmem] * len(outs),
        scratch_shapes=scratch,
        compiler_params=pltpu.CompilerParams(
            collective_id=collective_id, has_side_effects=True, vmem_limit_bytes=63 * 2**20
        ),
    )(*early_grads, *inputs, *weights)


def fused_body(
    word_states,
    word_segments,
    entity_segments,
    request_rows,
    request_slot,
    mask_slots,
    entity_table,
    vocab_bias,
    entity_dense,
    query_ww,
    query_we,
    query_ew,
    query_ee,
    key_weight,
    value_weight,
    out_weight,
    norm1_gain,
    norm1_bias,
    up_weight,
    down_weight,
    norm2_gain,
    norm2_bias,
    head_weight,
    head_gain,
    head_bias,
    cotangent,
):
    devices = lax.axis_size("dp")
    low = jnp.bfloat16
    slot_count = entity_segments.shape[1]
    mask_count = mask_slots.shape[1]
    grad_scale = 1.0 / (mask_count * devices)
    orders = stage_masks(devices)
    bias_row = vocab_bias.astype(jnp.float32)
    (
        entity_low,
        target_vecs,
        target_bias,
        code_row,
        word_q,
        word_e,
        word_k,
        word_v,
        feat_q,
        feat_k,
        choose,
        slot_row,
    ) = lookup(
        [
            request_rows.T,
            entity_table,
            bias_row,
            request_slot.T,
            word_states,
            query_ww,
            query_we,
            key_weight,
            value_weight,
            word_segments,
            entity_segments,
            mask_slots,
        ],
        slot_count,
        mask_count,
        0,
    )
    (
        hidden_low,
        query_word,
        query_entity,
        key_rows,
        values,
        context_low,
        lse_lanes,
        residual_one,
        normed_low,
        activated,
        gelu_slope,
        residual_two,
        layer_low,
        picked_low,
        head_pre,
        head_low,
    ) = forward_pass(
        [
            word_states,
            entity_low,
            feat_q,
            feat_k,
            choose,
            entity_dense,
            word_q,
            word_e,
            word_k,
            word_v,
            query_ew,
            query_ee,
            key_weight,
            value_weight,
            out_weight,
            norm1_gain,
            norm1_bias,
            up_weight,
            down_weight,
            norm2_gain,
            norm2_bias,
            head_weight,
            head_gain,
            head_bias,
        ]
    )
    table_grad, bias_grad, losses, total_loss, head_grad = head_and_table(
        head_low,
        entity_table,
        bias_row,
        target_vecs,
        target_bias,
        grad_scale,
        1,
    )
    (
        up_a,
        up_b,
        head_a,
        out_b,
        down_b,
        up_c,
        down_c,
        first_grad,
        context_grad,
        lse_delta,
        vectors,
    ) = middle_back(
        [
            head_grad,
            target_vecs,
            head_pre,
            head_gain,
            picked_low,
            head_weight,
            choose,
            cotangent,
            residual_two,
            norm2_gain,
            normed_low,
            residual_one,
            norm1_gain,
            out_weight,
            context_low,
            lse_lanes,
            activated,
            gelu_slope,
            up_weight,
            down_weight,
        ],
        orders,
        grad_scale,
    )
    *sums, words_grad, back_rows = attention_back(
        [up_a, down_b, up_c, down_c, up_b, head_a, vectors, out_b],
        [
            hidden_low,
            query_word,
            query_entity,
            key_rows,
            values,
            context_grad,
            feat_q,
            feat_k,
            lse_delta,
            first_grad,
            head_low,
            slot_row,
        ],
        [
            query_ww,
            query_we,
            query_ew,
            query_ee,
            key_weight,
            value_weight,
            entity_dense,
            entity_low,
        ],
        grad_scale,
        2,
    )
    (
        table_grad,
        bias_grad,
        up_sum,
        down_sum,
        head_sum,
        out_sum,
        key_sum,
        value_sum,
        ew_sum,
        ee_sum,
        ww_sum,
        we_sum,
        dense_sum,
        *vector_out,
    ) = last_step(
        code_row,
        back_rows.reshape(-1, back_rows.shape[2]),
        table_grad,
        bias_grad,
        sums,
        (head_gain.shape[0] // devices, norm1_gain.shape[0] // devices),
        grad_scale,
    )
    return (
        total_loss[0, 0],
        layer_low,
        words_grad,
        table_grad,
        bias_grad,
        dense_sum,
        ww_sum,
        we_sum,
        ew_sum,
        ee_sum,
        key_sum,
        value_sum,
        out_sum,
        vector_out[4],
        vector_out[5],
        up_sum,
        down_sum,
        vector_out[2],
        vector_out[3],
        head_sum,
        vector_out[0],
        vector_out[1],
        losses,
    )


def solution(mesh):
    in_specs = (
        P("dp", None),
        P("dp", None),
        P("dp", None),
        P("dp", None),
        P("dp", None),
        P("dp", None),
        P("dp", None),
        P("dp"),
        P(),
        P(),
        P(),
        P(),
        P(),
        P(),
        P(),
        P(),
        P(),
        P(),
        P(),
        P(),
        P(),
        P(),
        P(),
        P(),
        P(),
        P("dp", None),
    )
    out_specs = (
        P(),
        P("dp", None),
        P("dp", None),
        P("dp", None),
        P("dp"),
        P("dp", None),
        P("dp", None),
        P("dp", None),
        P("dp", None),
        P("dp", None),
        P("dp", None),
        P("dp", None),
        P("dp", None),
        P("dp"),
        P("dp"),
        P("dp", None),
        P("dp", None),
        P("dp"),
        P("dp"),
        P("dp", None),
        P("dp"),
        P("dp"),
        P("dp"),
    )
    chosen = fused_body if mesh.shape["dp"] == 32 else body
    return jax.shard_map(chosen, mesh=mesh, in_specs=in_specs, out_specs=out_specs, check_vma=False)
```

```python
import functools

import jax
import jax.numpy as jnp
from jax import lax
from jax.experimental import pallas as pl
from jax.experimental.pallas import tpu as pltpu
from jax.sharding import PartitionSpec as P

MESH_ID = pl.DeviceIdType.MESH

HD = 64


EPSILON = 1e-05
MASKED = -1000000000.0


def dot_plain(left_side, right_side):
    return jnp.dot(left_side, right_side, preferred_element_type=jnp.float32)


def dot_left_t(left_side, right_side):
    return lax.dot_general(
        left_side, right_side, (((0,), (0,)), ((), ())), preferred_element_type=jnp.float32
    )


def dot_right_t(left_side, right_side):
    return lax.dot_general(
        left_side, right_side, (((1,), (1,)), ((), ())), preferred_element_type=jnp.float32
    )


def dot_exact(left_side, right_side):
    return jnp.dot(
        left_side, right_side, precision=lax.Precision.HIGHEST, preferred_element_type=jnp.float32
    )


def layer_norm(tensor, gain_vec, shift_vec):
    center = tensor - jnp.mean(tensor, axis=-1, keepdims=True)
    spread = jnp.mean(center * center, axis=-1, keepdims=True)
    return center * lax.rsqrt(spread + EPSILON) * gain_vec + shift_vec


def gelu_exact(tensor):
    return jax.nn.gelu(tensor, approximate=False)


def head_act(tensor, gain_vec, shift_vec):
    return layer_norm(gelu_exact(tensor), gain_vec, shift_vec)


def norm_back(tensor, gain_vec, shift_vec, grad_out):
    result, pullback = jax.vjp(layer_norm, tensor, gain_vec, shift_vec)
    return pullback(grad_out)


def attn_scores(query_word, query_entity, key_rows, allowed, word_count):
    to_words = jnp.einsum(
        "qhd,khd->hqk", query_word, key_rows[:word_count], preferred_element_type=jnp.float32
    )
    to_entities = jnp.einsum(
        "qhd,khd->hqk", query_entity, key_rows[word_count:], preferred_element_type=jnp.float32
    )
    return jnp.where(allowed[None], jnp.concatenate([to_words, to_entities], axis=2), MASKED)


def greet_all(me, devices):
    barrier = pltpu.get_barrier_semaphore()

    def greet(step, carry):
        pl.semaphore_signal(
            barrier, inc=1, device_id=(lax.rem(me + step, devices),), device_id_type=MESH_ID
        )
        return carry

    lax.fori_loop(1, devices, greet, 0)
    pl.semaphore_wait(barrier, devices - 1)


def swap_kernel(devices, gather, source, target, send_sem, recv_sem):
    me = lax.axis_index("dp")
    greet_all(me, devices)

    def piece(step):
        peer = lax.rem(me + step, devices)
        return pltpu.make_async_remote_copy(
            src_ref=source if gather else source.at[peer],
            dst_ref=target.at[me],
            send_sem=send_sem.at[step],
            recv_sem=recv_sem.at[step],
            device_id=(peer,),
            device_id_type=MESH_ID,
        )

    def begin(step, carry):
        piece(step).start()
        return carry

    def finish(step, carry):
        piece(step).wait()
        return carry

    lax.fori_loop(1, devices, begin, 0)
    target[me] = source[...] if gather else source[me]
    lax.fori_loop(1, devices, finish, 0)


def direct_swap(value, collective_id, gather=False):
    devices = lax.axis_size("dp")
    shape = (devices,) + value.shape if gather else value.shape
    return pl.pallas_call(
        functools.partial(swap_kernel, devices, gather),
        out_shape=jax.ShapeDtypeStruct(shape, value.dtype),
        in_specs=[pl.BlockSpec(memory_space=pltpu.VMEM)],
        out_specs=pl.BlockSpec(memory_space=pltpu.VMEM),
        scratch_shapes=[
            pltpu.SemaphoreType.DMA((devices,)),
            pltpu.SemaphoreType.DMA((devices,)),
        ],
        compiler_params=pltpu.CompilerParams(collective_id=collective_id, has_side_effects=True),
    )(value)


def stage_masks(devices):
    if devices == 32:
        axes = [[2], [4], [8, 16]]
    elif devices == 128:
        axes = [[2, 4], [8, 16], [32, 64]]
    else:
        axes = [[2**bit] for bit in range(1, devices.bit_length() - 1)]
        axes = axes + [[] for _ in range(3 - len(axes))]
    first, second, third = axes[0], axes[1], sum(axes[2:], [])
    return (
        [1] + first + second + third,
        [1] + second + first + third,
        [1] + third + first + second,
    )


def sum_kernel(masks, rows, *refs):
    parts = len(masks)
    stages = len(masks[0])
    sources, results = refs[:parts], refs[parts : 2 * parts]
    landing = refs[2 * parts : 3 * parts]
    send_sem, recv_sem = refs[3 * parts :]
    me = lax.axis_index("dp")
    barrier = pltpu.get_barrier_semaphore()
    partner_of = {}
    for mask in masks[0]:
        bit = lax.rem(lax.div(me, mask), 2)
        partner_of[mask] = (me + mask - 2 * mask * bit, bit)
    for mask in masks[0]:
        pl.semaphore_signal(
            barrier, inc=1, device_id=(partner_of[mask][0],), device_id_type=MESH_ID
        )
    pl.semaphore_wait(barrier, stages)
    sizes = [[rows[part] * 2 ** (stages - 1 - stage) for stage in range(stages)] for part in range(parts)]
    places = [[sum(size[:stage]) for stage in range(stages)] for size in sizes]

    def launch(part, stage):
        partner, bit = partner_of[masks[part][stage]]
        size = sizes[part][stage]
        away = (1 - bit) * size
        copy = pltpu.make_async_remote_copy(
            src_ref=sources[part].at[pl.ds(away, size)]
            if stage == 0
            else landing[part].at[pl.ds(places[part][stage - 1] + away, size)],
            dst_ref=landing[part].at[pl.ds(places[part][stage], size)],
            send_sem=send_sem.at[part, stage],
            recv_sem=recv_sem.at[part, stage],
            device_id=(partner,),
            device_id_type=MESH_ID,
        )
        copy.start()
        return copy

    flying = [launch(part, 0) for part in range(parts)]

    def add_rows(part, stage, start, count):
        keep = partner_of[masks[part][stage]][1] * sizes[part][stage] + start
        last = stage == stages - 1

        def step(index, carry):
            theirs = pl.ds(pl.multiple_of(places[part][stage] + start + index * 16, 16), 16)
            if stage == 0:
                mine = sources[part][pl.ds(pl.multiple_of(keep + index * 16, 16), 16)]
            else:
                mine = landing[part][
                    pl.ds(pl.multiple_of(places[part][stage - 1] + keep + index * 16, 16), 16)
                ]
            total = mine.astype(jnp.float32) + landing[part][theirs].astype(jnp.float32)
            if last:
                results[part][pl.ds(pl.multiple_of(index * 16, 16), 16)] = total
            else:
                landing[part][theirs] = total.astype(jnp.bfloat16)
            return carry

        lax.fori_loop(0, count // 16, step, 0, unroll=min(4, count // 16))

    for stage in range(stages):
        for part in range(parts):
            flying[part].wait()
            if stage == stages - 1:
                add_rows(part, stage, 0, sizes[part][stage])
                continue
            bit = partner_of[masks[part][stage + 1]][1]
            half = sizes[part][stage] // 2
            add_rows(part, stage, (1 - bit) * half, half)
            flying[part] = launch(part, stage + 1)
            add_rows(part, stage, bit * half, half)


def sum_scatter(parts, collective_id):
    devices = lax.axis_size("dp")
    masks = stage_masks(devices)
    rows = [part.shape[1] for part in parts]
    width = parts[0].shape[2]
    bits = devices.bit_length() - 1
    ordered = []
    for part, order in zip(parts, masks):
        view = part.reshape((2,) * bits + part.shape[1:])
        places = [bits - mask.bit_length() for mask in order]
        view = view.transpose(tuple(places) + (bits, bits + 1))
        ordered.append(view.reshape(devices * part.shape[1], width))
    return pl.pallas_call(
        functools.partial(sum_kernel, masks, rows),
        out_shape=[jax.ShapeDtypeStruct((count, width), jnp.float32) for count in rows],
        in_specs=[pl.BlockSpec(memory_space=pltpu.VMEM)] * len(parts),
        out_specs=[pl.BlockSpec(memory_space=pltpu.VMEM)] * len(parts),
        scratch_shapes=[pltpu.VMEM((devices * count, width), jnp.bfloat16) for count in rows]
        + [pltpu.SemaphoreType.DMA((len(parts), bits)), pltpu.SemaphoreType.DMA((len(parts), bits))],
        input_output_aliases={},
        compiler_params=pltpu.CompilerParams(
            collective_id=collective_id, has_side_effects=True, vmem_limit_bytes=56 * 2**20
        ),
    )(*ordered)


def by_owner(grad, width):
    devices = lax.axis_size("dp")
    rows = grad.shape[0] // devices
    blocks = grad.astype(jnp.bfloat16).reshape(devices, rows, grad.shape[1])
    if grad.shape[1] > width:
        cuts = grad.shape[1] // width
        return jnp.concatenate(jnp.split(blocks, cuts, axis=2), axis=1)
    if grad.shape[1] < width:
        return blocks.reshape(devices, rows * grad.shape[1] // width, width)
    return blocks


def from_owner(rows, shape):
    devices = lax.axis_size("dp")
    count, width = shape[0] // devices, shape[1]
    if width > rows.shape[1]:
        return jnp.concatenate(jnp.split(rows, width // rows.shape[1], axis=0), axis=1)
    return rows.reshape(count, width)


def sum_all(groups, collective_id):
    width = groups[0][0].shape[1]
    width = min(grad.shape[1] for group in groups for grad in group if grad.shape[1] >= 768)
    devices = lax.axis_size("dp")
    packed = []
    for group in groups:
        pieces = [by_owner(grad, width) for grad in group]
        count = sum(piece.shape[1] for piece in pieces)
        room = -(-count // 16) * 16 - count
        if room:
            pieces.append(jnp.zeros((devices, room, width), jnp.bfloat16))
        packed.append(jnp.concatenate(pieces, axis=1))
    sums = sum_scatter(packed, collective_id)
    results = []
    for group, total in zip(groups, sums):
        place, outs = 0, []
        for grad in group:
            count = grad.shape[0] // devices * grad.shape[1] // width
            outs.append(from_owner(total[place : place + count], grad.shape))
            place += count
        results.append(outs)
    return results


def body(
    word_states,
    word_segments,
    entity_segments,
    request_rows,
    request_slot,
    mask_slots,
    entity_table,
    vocab_bias,
    entity_dense,
    query_ww,
    query_we,
    query_ew,
    query_ee,
    key_weight,
    value_weight,
    out_weight,
    norm1_gain,
    norm1_bias,
    up_weight,
    down_weight,
    norm2_gain,
    norm2_bias,
    head_weight,
    head_gain,
    head_bias,
    cotangent,
):
    word_count = word_states.shape[0]
    model_width = word_states.shape[1]
    slot_count = entity_segments.shape[1]
    mask_count = mask_slots.shape[1]
    request_count = slot_count + mask_count
    seq_len = word_count + slot_count
    devices = lax.axis_size("dp")
    capacity = request_rows.shape[1]
    head_count = model_width // HD
    query_scale = HD ** (-0.5)
    emb_width = entity_table.shape[1]
    table_rows = entity_table.shape[0]
    total_mask = mask_count * devices
    grad_scale = 1.0 / total_mask
    id_block = jnp.pad(request_rows[:, None, :], ((0, 0), (0, 7), (0, 128 - capacity)))
    asked_ids = direct_swap(id_block, 0)[:, 0, :capacity]
    found_rows = jnp.take(entity_table, asked_ids, axis=0)
    found_bias = jnp.take(vocab_bias, asked_ids, axis=0)
    cap_room = -(-capacity // 16) * 16 - capacity
    found_all = jnp.concatenate(
        [found_rows, jnp.broadcast_to(found_bias[:, :, None], found_bias.shape + (128,))], axis=2
    )
    back_all = direct_swap(jnp.pad(found_all, ((0, 0), (0, cap_room), (0, 0))), 1)
    back_rows = back_all[:, :capacity, :emb_width]
    back_bias = back_all[:, :capacity, emb_width]
    got_rows = back_rows
    got_bias = back_bias
    slot_ids = request_slot.reshape(devices * capacity)
    placing = slot_ids[None, :] == jnp.arange(request_count, dtype=jnp.int32)[:, None]
    placing_low = placing.astype(jnp.bfloat16)
    request_vecs = dot_plain(placing_low, got_rows.reshape(devices * capacity, emb_width))
    request_bias = dot_plain(placing_low, got_bias.reshape(devices * capacity, 1))[:, 0]
    entity_low = request_vecs[:slot_count].astype(jnp.bfloat16)
    target_vecs = request_vecs[slot_count:]
    target_bias = request_bias[slot_count:]
    entity_states = dot_plain(entity_low, entity_dense)
    hidden = jnp.concatenate([word_states.astype(jnp.float32), entity_states], axis=0)
    hidden_low = hidden.astype(jnp.bfloat16)
    word_part = hidden_low[:word_count]
    entity_part = hidden_low[word_count:]
    query_word = (
        query_scale
        * jnp.concatenate(
            [dot_plain(word_part, query_ww), dot_plain(entity_part, query_ew)], axis=0
        )
    ).astype(jnp.bfloat16)
    query_entity = (
        query_scale
        * jnp.concatenate(
            [dot_plain(word_part, query_we), dot_plain(entity_part, query_ee)], axis=0
        )
    ).astype(jnp.bfloat16)
    key_rows = dot_plain(hidden_low, key_weight).astype(jnp.bfloat16)
    values = dot_plain(hidden_low, value_weight).astype(jnp.bfloat16)
    head_shape = (seq_len, head_count, HD)
    query_word_h = query_word.reshape(head_shape)
    query_entity_h = query_entity.reshape(head_shape)
    key_rows_h = key_rows.reshape(head_shape)
    values_h = values.reshape(head_shape)
    segment_row = jnp.concatenate([word_segments[0], entity_segments[0]])
    allowed = segment_row[:, None] == segment_row[None, :]
    scores = attn_scores(query_word_h, query_entity_h, key_rows_h, allowed, word_count)
    row_top = jnp.max(scores, axis=2, keepdims=True)
    exp_scores = jnp.exp(scores - row_top)
    row_total = jnp.sum(exp_scores, axis=2, keepdims=True)
    attn_low = (exp_scores / row_total).astype(jnp.bfloat16)
    row_lse = row_top + jnp.log(row_total)
    context = jnp.einsum("hqk,khd->qhd", attn_low, values_h, preferred_element_type=jnp.float32)
    context_low = context.reshape(seq_len, model_width).astype(jnp.bfloat16)
    attended = dot_plain(context_low, out_weight)
    residual_one = hidden + attended
    normed = layer_norm(residual_one, norm1_gain, norm1_bias)
    normed_low = normed.astype(jnp.bfloat16)
    up_value = dot_plain(normed_low, up_weight)
    activated = gelu_exact(up_value).astype(jnp.bfloat16)
    down_value = dot_plain(activated, down_weight)
    residual_two = normed + down_value
    layer_out = layer_norm(residual_two, norm2_gain, norm2_bias)
    choose = (mask_slots[0][:, None] == jnp.arange(slot_count, dtype=jnp.int32)[None, :]).astype(
        jnp.float32
    )
    picked_low = dot_exact(choose, layer_out[word_count:]).astype(jnp.bfloat16)
    head_pre = dot_plain(picked_low, head_weight)
    head_low = head_act(head_pre, head_gain, head_bias).astype(jnp.bfloat16)
    head_f32 = head_low.astype(jnp.float32)
    target_logit = jnp.sum(head_f32 * target_vecs, axis=1) + target_bias
    all_heads = direct_swap(head_low, 2, gather=True).reshape(total_mask, emb_width)
    block_rows = min(512, total_mask)
    block_count = total_mask // block_rows
    bias_f32 = vocab_bias.astype(jnp.float32)

    def block_logits(block_index):
        row_block = lax.dynamic_slice_in_dim(all_heads, block_index * block_rows, block_rows, 0)
        return (row_block, dot_right_t(row_block, entity_table) + bias_f32[None, :])

    def block_stats(block_index):
        row_block, logits = block_logits(block_index)
        top_value = jnp.max(logits, axis=1)
        return (top_value, jnp.sum(jnp.exp(logits - top_value[:, None]), axis=1))

    local_top, local_total = lax.map(block_stats, jnp.arange(block_count, dtype=jnp.int32))
    local_top = local_top.reshape(total_mask)
    local_total = local_total.reshape(total_mask)
    target_sum = jnp.sum(target_logit)
    stats = jnp.concatenate(
        [
            local_top.reshape(total_mask // 128, 128),
            local_total.reshape(total_mask // 128, 128),
            jnp.full((8, 128), target_sum),
        ],
        axis=0,
    )
    all_stats = direct_swap(stats, 3, gather=True)
    all_tops = all_stats[:, : total_mask // 128].reshape(devices, total_mask)
    all_totals = all_stats[:, total_mask // 128 : total_mask // 64].reshape(devices, total_mask)
    target_total = jnp.sum(all_stats[:, total_mask // 64, 0])
    global_top = jnp.max(all_tops, axis=0)
    global_total = jnp.sum(all_totals * jnp.exp(all_tops - global_top[None, :]), axis=0)
    lse_all = global_top + jnp.log(global_total)
    loss_value = (jnp.sum(lse_all) - target_total) * grad_scale
    own_lse = lax.dynamic_slice_in_dim(lse_all, lax.axis_index("dp") * mask_count, mask_count, 0)
    mask_loss = own_lse - target_logit

    def block_back(running, block_index):
        table_grad, bias_grad = running
        row_block, logits = block_logits(block_index)
        lse_block = lax.dynamic_slice_in_dim(lse_all, block_index * block_rows, block_rows, 0)
        logit_grad = (jnp.exp(logits - lse_block[:, None]) * grad_scale).astype(jnp.bfloat16)
        table_grad = table_grad + dot_left_t(logit_grad, row_block)
        bias_grad = bias_grad + jnp.sum(logit_grad.astype(jnp.float32), axis=0)
        return ((table_grad, bias_grad), dot_plain(logit_grad, entity_table))

    start_grads = (
        jnp.zeros((table_rows, emb_width), jnp.float32),
        jnp.zeros((table_rows,), jnp.float32),
    )
    (table_grad, bias_grad), head_terms = lax.scan(
        block_back, start_grads, jnp.arange(block_count, dtype=jnp.int32)
    )
    head_parts = direct_swap(head_terms.reshape(devices, mask_count, emb_width), 4)
    head_grad = jnp.sum(head_parts, axis=0)
    head_grad = head_grad - grad_scale * target_vecs
    target_grad = -grad_scale * head_f32
    pre_grad, head_gain_grad, head_bias_grad = jax.vjp(head_act, head_pre, head_gain, head_bias)[1](
        head_grad
    )
    pre_low = pre_grad.astype(jnp.bfloat16)
    head_weight_grad = dot_left_t(picked_low, pre_low)
    picked_grad = dot_right_t(pre_low, head_weight)
    out_grad = cotangent.astype(jnp.float32) + jnp.concatenate(
        [jnp.zeros((word_count, model_width), jnp.float32), dot_exact(choose.T, picked_grad)],
        axis=0,
    )
    resid_grad, norm2_gain_grad, norm2_bias_grad = norm_back(
        residual_two, norm2_gain, norm2_bias, out_grad
    )
    down_in = resid_grad.astype(jnp.bfloat16)
    down_grad = dot_left_t(activated, down_in)
    act_grad = dot_right_t(down_in, down_weight)
    up_grad = jax.vjp(gelu_exact, up_value)[1](act_grad)[0]
    up_low = up_grad.astype(jnp.bfloat16)
    up_weight_grad = dot_left_t(normed_low, up_low)
    normed_grad = resid_grad + dot_right_t(up_low, up_weight)
    first_grad, norm1_gain_grad, norm1_bias_grad = norm_back(
        residual_one, norm1_gain, norm1_bias, normed_grad
    )
    attn_in = first_grad.astype(jnp.bfloat16)
    out_weight_grad = dot_left_t(context_low, attn_in)
    context_grad = dot_right_t(attn_in, out_weight).astype(jnp.bfloat16).reshape(head_shape)
    scores_again = attn_scores(query_word_h, query_entity_h, key_rows_h, allowed, word_count)
    attn_prob = jnp.exp(scores_again - row_lse)
    prob_low = attn_prob.astype(jnp.bfloat16)
    prob_grad = jnp.einsum(
        "qhd,khd->hqk", context_grad, values_h, preferred_element_type=jnp.float32
    )
    values_grad = jnp.einsum(
        "hqk,qhd->khd", prob_low, context_grad, preferred_element_type=jnp.float32
    )
    values_grad = values_grad.reshape(seq_len, model_width).astype(jnp.bfloat16)
    row_delta = jnp.sum(attn_prob * prob_grad, axis=2, keepdims=True)
    score_grad = (attn_prob * (prob_grad - row_delta)).astype(jnp.bfloat16)
    qword_grad = jnp.einsum(
        "hqk,khd->qhd",
        score_grad[:, :, :word_count],
        key_rows_h[:word_count],
        preferred_element_type=jnp.float32,
    )
    qword_grad = qword_grad.reshape(seq_len, model_width).astype(jnp.bfloat16)
    qent_grad = jnp.einsum(
        "hqk,khd->qhd",
        score_grad[:, :, word_count:],
        key_rows_h[word_count:],
        preferred_element_type=jnp.float32,
    )
    qent_grad = qent_grad.reshape(seq_len, model_width).astype(jnp.bfloat16)
    keys_grad = jnp.concatenate(
        [
            jnp.einsum(
                "hqk,qhd->khd",
                score_grad[:, :, :word_count],
                query_word_h,
                preferred_element_type=jnp.float32,
            ),
            jnp.einsum(
                "hqk,qhd->khd",
                score_grad[:, :, word_count:],
                query_entity_h,
                preferred_element_type=jnp.float32,
            ),
        ],
        axis=0,
    )
    keys_grad = keys_grad.reshape(seq_len, model_width).astype(jnp.bfloat16)
    query_ww_grad = query_scale * dot_left_t(word_part, qword_grad[:word_count])
    query_ew_grad = query_scale * dot_left_t(entity_part, qword_grad[word_count:])
    query_we_grad = query_scale * dot_left_t(word_part, qent_grad[:word_count])
    query_ee_grad = query_scale * dot_left_t(entity_part, qent_grad[word_count:])
    key_weight_grad = dot_left_t(hidden_low, keys_grad)
    value_weight_grad = dot_left_t(hidden_low, values_grad)
    word_back = query_scale * (
        dot_right_t(qword_grad[:word_count], query_ww)
        + dot_right_t(qent_grad[:word_count], query_we)
    )
    entity_back = query_scale * (
        dot_right_t(qword_grad[word_count:], query_ew)
        + dot_right_t(qent_grad[word_count:], query_ee)
    )
    hidden_grad = (
        first_grad
        + jnp.concatenate([word_back, entity_back], axis=0)
        + dot_right_t(keys_grad, key_weight)
        + dot_right_t(values_grad, value_weight)
    )
    words_grad = hidden_grad[:word_count].astype(jnp.bfloat16)
    state_low = hidden_grad[word_count:].astype(jnp.bfloat16)
    dense_grad = dot_left_t(entity_low, state_low)
    entity_vec_grad = dot_right_t(state_low, entity_dense)
    vec_grad = jnp.concatenate([entity_vec_grad, target_grad], axis=0)
    bias_vec_grad = jnp.concatenate(
        [jnp.zeros((slot_count,), jnp.float32), jnp.full((mask_count,), -grad_scale, jnp.float32)]
    )
    placing_f32 = placing.astype(jnp.float32)
    per_request = dot_exact(placing_f32.T, vec_grad)
    bias_request = dot_exact(placing_f32.T, bias_vec_grad[:, None])[:, 0]
    back_block = jnp.concatenate(
        [
            per_request.reshape(devices, capacity, emb_width).astype(jnp.bfloat16),
            jnp.broadcast_to(
                bias_request.reshape(devices, capacity, 1).astype(jnp.bfloat16),
                (devices, capacity, 128),
            ),
        ],
        axis=2,
    )
    back_block = direct_swap(jnp.pad(back_block, ((0, 0), (0, cap_room), (0, 0))), 5)
    back_rows = back_block[:, :capacity, :emb_width].astype(jnp.float32)
    back_bias = back_block[:, :capacity, emb_width].astype(jnp.float32)
    flat_ids = asked_ids.reshape(devices * capacity)
    table_grad = table_grad + jax.ops.segment_sum(
        back_rows.reshape(devices * capacity, emb_width), flat_ids, num_segments=table_rows
    )
    bias_grad = bias_grad + jax.ops.segment_sum(
        back_bias.reshape(devices * capacity), flat_ids, num_segments=table_rows
    )
    vectors = [
        head_gain_grad,
        head_bias_grad,
        norm2_gain_grad,
        norm2_bias_grad,
        norm1_gain_grad,
        norm1_bias_grad,
    ]
    cuts = [vector.reshape(devices, -1) for vector in vectors]
    spots = [0]
    for cut in cuts:
        spots.append(spots[-1] + cut.shape[1])
    block = jnp.concatenate(cuts, axis=1)
    block = jnp.pad(block, ((0, 0), (0, 128 - spots[-1])))[:, None, :]
    vector_sums = jnp.sum(direct_swap(jnp.pad(block, ((0, 0), (0, 7), (0, 0))), 6)[:, 0], axis=0)
    vector_out = [vector_sums[spots[i] : spots[i + 1]] for i in range(len(cuts))]
    sums = sum_all(
        [
            [up_weight_grad, out_weight_grad, head_weight_grad],
            [down_grad, query_ww_grad, dense_grad],
            [query_we_grad, query_ew_grad, query_ee_grad, key_weight_grad, value_weight_grad],
        ],
        7,
    )
    all_sums = (
        sums[0][2],
        vector_out[0],
        vector_out[1],
        vector_out[2],
        vector_out[3],
        sums[0][0],
        sums[1][0],
        vector_out[4],
        vector_out[5],
        sums[0][1],
        sums[1][1],
        sums[2][0],
        sums[2][1],
        sums[2][2],
        sums[2][3],
        sums[2][4],
        sums[1][2],
    )
    return (
        loss_value,
        layer_out.astype(jnp.bfloat16),
        words_grad,
        table_grad,
        bias_grad,
        all_sums[16],
        all_sums[10],
        all_sums[11],
        all_sums[12],
        all_sums[13],
        all_sums[14],
        all_sums[15],
        all_sums[9],
        all_sums[7],
        all_sums[8],
        all_sums[5],
        all_sums[6],
        all_sums[3],
        all_sums[4],
        all_sums[0],
        all_sums[1],
        all_sums[2],
        mask_loss,
    )


class Stage:
    def __init__(self, loads, stores):
        self.loads, self.stores, self.waited, self.sent = loads, stores, set(), []

    def need(self, *indices):
        for index in indices:
            if index not in self.waited:
                self.waited.add(index)
                self.loads[index].wait()

    def send(self, *indices):
        for index in indices:
            self.sent.append(index)
            self.stores[index].start()

    def finish(self):
        self.need(*self.loads)
        self.send(*[index for index in self.stores if index not in self.sent])
        for copy in self.stores.values():
            copy.wait()


def staged_kernel(inner, counts, far_in, far_out, *refs):
    ins, outs = list(refs[: counts[0]]), list(refs[counts[0] : sum(counts)])
    rest = list(refs[sum(counts) :])
    out_sem, in_sem = rest.pop(), rest.pop()
    near = rest[len(rest) - len(far_in) - len(far_out) :]
    rest = rest[: len(rest) - len(near)]
    loads, stores = {}, {}
    for slot, index in enumerate(far_in):
        loads[index] = pltpu.make_async_copy(ins[index], near[slot], in_sem.at[slot])
        ins[index] = near[slot]
        loads[index].start()
    for slot, index in enumerate(far_out):
        close = near[len(far_in) + slot]
        stores[index] = pltpu.make_async_copy(close, outs[index], out_sem.at[slot])
        outs[index] = close
    stage = Stage(loads, stores)
    inner(stage, *ins, *outs, *rest)
    stage.finish()


def staged_call(inner, inputs, outs, in_specs, out_specs, far_in, far_out, scratch, params):
    hbm = pl.BlockSpec(memory_space=pltpu.HBM)
    in_specs, out_specs = list(in_specs), list(out_specs)
    extra = []
    for index in far_in:
        in_specs[index] = hbm
        extra.append(pltpu.VMEM(inputs[index].shape, inputs[index].dtype))
    for index in far_out:
        out_specs[index] = hbm
        extra.append(pltpu.VMEM(outs[index].shape, outs[index].dtype))
    return pl.pallas_call(
        functools.partial(staged_kernel, inner, (len(inputs), len(outs)), far_in, far_out),
        out_shape=outs,
        in_specs=in_specs,
        out_specs=out_specs,
        scratch_shapes=list(scratch)
        + extra
        + [
            pltpu.SemaphoreType.DMA((max(1, len(far_in)),)),
            pltpu.SemaphoreType.DMA((max(1, len(far_out)),)),
        ],
        compiler_params=params,
    )(*inputs)


def all_pairs(source, target, sems, me, devices):
    def piece(step):
        peer = lax.rem(me + step, devices)
        return pltpu.make_async_remote_copy(
            src_ref=source.at[peer],
            dst_ref=target.at[me],
            send_sem=sems.at[0, step],
            recv_sem=sems.at[1, step],
            device_id=(peer,),
            device_id_type=MESH_ID,
        )

    def begin(step, carry):
        piece(step).start()
        return carry

    def finish(step, carry):
        piece(step).wait()
        return carry

    lax.fori_loop(1, devices, begin, 0)
    target[me] = source[me]
    return lambda: lax.fori_loop(1, devices, finish, 0)


def lookup_kernel(
    stage,
    request_rows,
    table,
    bias,
    request_slot,
    word_states,
    w_ww,
    w_we,
    w_key,
    w_value,
    word_seg,
    entity_seg,
    mask_slots,
    entity_out,
    vec_out,
    bias_out,
    code_out,
    qword,
    qent,
    keys,
    values,
    feat_q,
    feat_k,
    choose,
    slot_out,
    code_send,
    code_pad,
    slot_pad,
    codes_in,
    found,
    rows_in,
    bias_col,
    sems,
):
    devices, room, _ = found.shape
    me = lax.axis_index("dp")
    rows, wide = table.shape
    entries = devices * room
    slots, masked = entity_out.shape[0], vec_out.shape[0]
    slot = request_slot[...]
    code = request_rows[...] + jnp.where(slot >= slots, rows, 0)
    code = jnp.where(slot < slots + masked, code, -1)
    capacity = slot.shape[0]
    code_pad[...] = jnp.full(code_pad.shape, -1, jnp.int32).astype(jnp.float32)
    code_pad[0:capacity] = code.astype(jnp.float32)
    sent = code_pad[...].T.astype(jnp.int32)
    for owner in range(devices):
        code_send[owner] = sent[owner : owner + 1]
    slot_pad[...] = jnp.full(slot_pad.shape, slots + masked, jnp.int32).astype(jnp.float32)
    slot_pad[0:capacity] = slot.astype(jnp.float32)
    greet_all(me, devices)

    def in_column(turned):
        return jnp.concatenate(
            [
                jnp.broadcast_to(turned[0:room, one : one + 1], (room, 128))
                for one in range(devices)
            ],
            axis=0,
        )

    def in_row(column, target):
        for begin in range(0, entries, 128):
            turned = column[begin : begin + 128].T
            target[:, begin : begin + 128] = turned[0:8].astype(jnp.int32)

    ended = all_pairs(code_send, codes_in, sems.at[0], me, devices)
    width = word_states.shape[1]
    half = width // 2
    query_scale = HD ** (-0.5)

    def project(target, weight, scale):
        for cut in range(0, width, half):
            value = dot_plain(word_states[...], weight[:, cut : cut + half])
            if scale:
                value = value * query_scale
            target[:, cut : cut + half] = value.astype(jnp.bfloat16)

    def bias_step(index, carry):
        at = pl.ds(pl.multiple_of(index * 128, 128), 128)
        bias_col[at] = jnp.broadcast_to(bias[at].reshape(1, 128), (128, 128)).T.astype(jnp.bfloat16)
        return carry

    lax.fori_loop(0, rows // 128, bias_step, 0)
    words = word_seg.shape[1]
    column = lax.rem(lax.broadcasted_iota(jnp.int32, (128, 128), 1), HD)
    for begin in range(0, words + entity_seg.shape[1], 128):
        seg = word_seg[:, begin : begin + 128] if begin < words else entity_seg[...]
        turned = jnp.broadcast_to(seg.astype(jnp.float32), (128, 128)).T
        same = turned == column.astype(jnp.float32)
        at = slice(begin, begin + 128)
        feat_q[at] = same.astype(jnp.float32).astype(jnp.bfloat16)
        feat_k[at] = jnp.where(same | (column >= 4), 0.0, MASKED).astype(jnp.bfloat16)
    turned = jnp.broadcast_to(mask_slots[...].astype(jnp.float32), (128, masked)).T
    lanes = lax.broadcasted_iota(jnp.int32, (masked, 128), 1).astype(jnp.float32)
    choose[...] = (turned == lanes).astype(jnp.float32).astype(jnp.bfloat16)
    stage.need(4, 5)
    project(qword, w_ww, True)
    stage.send(4)
    stage.need(1)
    ended()
    code = in_column(
        jnp.concatenate([codes_in[one] for one in range(devices)], axis=0).astype(jnp.float32).T
    )
    in_row(code, code_out)
    code = code.astype(jnp.int32)
    code = jnp.where(code >= rows, code - rows, code)
    lane = lax.broadcasted_iota(jnp.int32, (entries, 128), 1)
    total = jnp.zeros((entries, wide), jnp.float32)
    shift = jnp.zeros((entries, 128), jnp.float32)
    step = 512
    for begin in range(0, rows, step):
        size = min(step, rows - begin)
        match = jnp.concatenate(
            [
                (code - (begin + inner) == lane).astype(jnp.float32)
                for inner in range(0, size, 128)
            ],
            axis=1,
        ).astype(jnp.bfloat16)
        total += dot_plain(match, table[begin : begin + size])
        shift += dot_plain(match, bias_col[begin : begin + size])
    both = jnp.concatenate([total, shift], axis=1).astype(jnp.bfloat16)
    found[...] = both.reshape(found.shape)
    ended = all_pairs(found, rows_in, sems.at[1], me, devices)
    in_row(in_column(slot_pad[...]), slot_out)
    stage.need(6)
    project(qent, w_we, True)
    stage.send(5)
    stage.need(7)
    project(keys, w_key, False)
    stage.send(6)
    stage.need(8)
    project(values, w_value, False)
    stage.send(7)
    ended()
    wanted = lax.broadcasted_iota(jnp.int32, (slots + masked, entries), 0)
    placing = (wanted == slot_out[0:1]).astype(jnp.float32).astype(jnp.bfloat16)
    placed = dot_plain(placing, rows_in[...].reshape(entries, wide + 128))
    entity_out[...] = placed[:slots, :wide].astype(jnp.bfloat16)
    vec_out[...] = placed[slots:, :wide]
    bias_out[...] = placed[slots:, wide:]


def lookup(inputs, slots, masked, collective_id):
    capacity, devices = inputs[0].shape
    room = -(-capacity // 16) * 16
    rows, wide = inputs[1].shape
    words, width = inputs[4].shape
    entries = devices * room
    low = jnp.bfloat16
    vmem = pl.BlockSpec(memory_space=pltpu.VMEM)
    outs = [
        jax.ShapeDtypeStruct((slots, wide), low),
        jax.ShapeDtypeStruct((masked, wide), jnp.float32),
        jax.ShapeDtypeStruct((masked, 128), jnp.float32),
        jax.ShapeDtypeStruct((8, entries), jnp.int32),
    ]
    outs += [jax.ShapeDtypeStruct((words, width), low)] * 4
    outs += [jax.ShapeDtypeStruct((words + slots, 128), low)] * 2
    outs += [jax.ShapeDtypeStruct((masked, slots), low)]
    outs += [jax.ShapeDtypeStruct((8, entries), jnp.int32)]
    return staged_call(
        lookup_kernel,
        inputs,
        outs,
        [vmem] * len(inputs),
        [vmem] * len(outs),
        (4, 5, 1, 6, 7, 8),
        (4, 5, 6, 7),
        [
            pltpu.VMEM((devices, 1, 128), jnp.int32),
            pltpu.VMEM((128, devices), jnp.float32),
            pltpu.VMEM((room, devices), jnp.float32),
            pltpu.VMEM((devices, 1, 128), jnp.int32),
            pltpu.VMEM((devices, room, wide + 128), low),
            pltpu.VMEM((devices, room, wide + 128), low),
            pltpu.VMEM((rows, 128), low),
            pltpu.SemaphoreType.DMA((2, 2, devices)),
        ],
        pltpu.CompilerParams(
            collective_id=collective_id, has_side_effects=True, vmem_limit_bytes=63 * 2**20
        ),
    )


def norm_parts(value):
    center = value - jnp.mean(value, axis=-1, keepdims=True)
    spread = jnp.mean(center * center, axis=-1, keepdims=True)
    rate = lax.rsqrt(spread + EPSILON)
    return center * rate, rate


def gelu_parts(value):
    chance = 0.5 + 0.5 * lax.erf(value * (0.5**0.5))
    slope = chance + value * (jnp.exp(-0.5 * value * value) * (0.5 / jnp.pi) ** 0.5)
    return value * chance, slope


def half_lanes(block):
    lane = lax.broadcasted_iota(jnp.int32, (1, block), 1)
    low_half = (lane < HD).astype(jnp.float32).astype(jnp.bfloat16)
    high_half = (lane >= HD).astype(jnp.float32).astype(jnp.bfloat16)
    return low_half, high_half


def forward_kernel(
    stage,
    word_states,
    entity_low,
    feat_q,
    feat_k,
    choose,
    dense,
    word_q,
    word_e,
    word_k,
    word_v,
    w_ew,
    w_ee,
    w_key,
    w_value,
    out_hbm,
    gain_one,
    shift_one,
    up_hbm,
    down_hbm,
    gain_two,
    shift_two,
    head_w,
    gain_head,
    shift_head,
    hidden,
    qword,
    qent,
    keys,
    values,
    context,
    lse_out,
    resid_one,
    normed_out,
    active_hbm,
    slope_hbm,
    resid_two,
    layer_low,
    picked_out,
    head_pre_out,
    head_out,
    state_scr,
    normed_scr,
    out_w,
    up_w,
    down_w,
    active,
    slope,
    sems,
):
    loads = [
        pltpu.make_async_copy(source, target, sems.at[index])
        for index, (source, target) in enumerate(
            ((out_hbm, out_w), (up_hbm, up_w), (down_hbm, down_w))
        )
    ]
    words, width = word_states.shape
    word_loads = [
        pltpu.make_async_copy(source, target.at[pl.ds(0, words)], sems.at[12 + index])
        for index, (source, target) in enumerate(
            ((word_q, qword), (word_e, qent), (word_k, keys), (word_v, values))
        )
    ]
    for load in word_loads + loads:
        load.start()
    stage.need(0, 1, 5)
    seq_len = hidden.shape[0]
    slots = seq_len - words
    block = 128
    tall = seq_len
    halves = half_lanes(block)
    query_scale = HD ** (-0.5)
    state_scr[...] = dot_plain(entity_low[...], dense[...])
    hidden[:words] = word_states[...]
    hidden[words:] = state_scr[...].astype(jnp.bfloat16)

    stage.send(0)
    ents = hidden[words:]
    stage.need(10, 11, 12, 13)
    for target, weight, scale in (
        (qword, w_ew, query_scale),
        (qent, w_ee, query_scale),
        (keys, w_key, None),
        (values, w_value, None),
    ):
        value = dot_plain(ents, weight[...])
        if scale is not None:
            value = value * scale
        target[words:] = value.astype(jnp.bfloat16)
    for load in word_loads:
        load.wait()
    stage.send(1, 2, 3, 4)
    stage.need(2, 3)
    lse_out[...] = jnp.zeros_like(lse_out)

    def pair_step(pair, carry):
        lanes = pl.ds(pl.multiple_of(pair * block, block), block)
        key_pair = keys[:, lanes]
        value_pair = values[:, lanes]
        key_feat = [key_pair * halves[h] + feat_k[...] * halves[1 - h] for h in range(2)]
        value_only = [value_pair * halves[h] for h in range(2)]
        spot = lax.broadcasted_iota(jnp.int32, (1, block), 1) - 4 * pair

        def row_step(index, inner):
            at = pl.ds(pl.multiple_of(index * tall, block), tall)
            qw = qword[at, lanes]
            qe = qent[at, lanes]
            feats = feat_q[at]
            result = jnp.zeros((tall, block), jnp.float32)
            stats = lse_out[at]
            for h in range(2):
                left_w = qw * halves[h] + feats * halves[1 - h]
                left_e = qe * halves[h] + feats * halves[1 - h]
                scores = jnp.concatenate(
                    [
                        dot_right_t(left_w, key_feat[h][:words]),
                        dot_right_t(left_e, key_feat[h][words:]),
                    ],
                    axis=1,
                )
                top = jnp.max(scores, axis=1, keepdims=True)
                expo = jnp.exp(scores - top)
                total = jnp.sum(expo, axis=1, keepdims=True)
                prob = (expo * (1.0 / total)).astype(jnp.bfloat16)
                result += dot_plain(prob, value_only[h])
                stats = jnp.where(spot == h, top + jnp.log(total), stats)
            context[at, lanes] = result.astype(jnp.bfloat16)
            lse_out[at] = stats
            return inner

        lax.fori_loop(0, seq_len // tall, row_step, 0)
        return carry

    lax.fori_loop(0, width // block, pair_step, 0)

    stage.send(5)
    loads[0].wait()
    for begin, size in ((0, words // 2), (words // 2, words // 2), (words, slots)):
        at = slice(begin, begin + size)
        start = (
            state_scr[...] if begin == words else word_states[at].astype(jnp.float32)
        )
        value = start + dot_plain(context[at], out_w[...])
        resid_one[at] = value
        normed = norm_parts(value)[0] * gain_one[...][None, :] + shift_one[...][None, :]
        normed_scr[at] = normed
        normed_out[at] = normed.astype(jnp.bfloat16)
    stage.send(7, 8)
    loads[1].wait()
    loads[2].wait()
    span = seq_len
    stores = []

    for slot in range(down_w.shape[0] // width):
        cols = slice(slot * width, slot * width + width)

        def up_step(index, carry, cols=cols):
            at = pl.ds(pl.multiple_of(index * span, 16), span)
            result, change = gelu_parts(dot_plain(normed_out[at], up_w[:, cols]))
            active[at, cols] = result.astype(jnp.bfloat16)
            slope[at, cols] = change.astype(jnp.bfloat16)
            return carry

        lax.fori_loop(0, seq_len // span, up_step, 0)
        for index, (source, target) in enumerate(((active, active_hbm), (slope, slope_hbm))):
            stores.append(
                pltpu.make_async_copy(
                    source.at[:, cols], target.at[:, cols], sems.at[3 + 2 * slot + index]
                )
            )
            stores[-1].start()

    def down_step(index, carry):
        at = pl.ds(pl.multiple_of(index * span, 16), span)
        value = normed_scr[at] + dot_plain(active[at], down_w[...])
        resid_two[at] = value
        layer_low[at] = (norm_parts(value)[0] * gain_two[...][None, :] + shift_two[...][None, :]).astype(jnp.bfloat16)
        return carry

    lax.fori_loop(0, seq_len // span, down_step, 0)
    stage.send(11, 12)
    stage.need(21)
    picked = dot_plain(choose[...], layer_low[words:]).astype(jnp.bfloat16)
    picked_out[...] = picked
    head_pre = dot_plain(picked, head_w[...])
    head_pre_out[...] = head_pre
    raised = gelu_parts(head_pre)[0]
    head_out[...] = (norm_parts(raised)[0] * gain_head[...][None, :] + shift_head[...][None, :]).astype(jnp.bfloat16)
    for store in stores:
        store.wait()


def forward_pass(inputs):
    words, width = inputs[0].shape
    slots = inputs[1].shape[0]
    seq_len = words + slots
    hidden_units = inputs[17].shape[1]
    mask_count = inputs[4].shape[0]
    head_width = inputs[21].shape[1]
    low, full = jnp.bfloat16, jnp.float32
    vmem, hbm = pl.BlockSpec(memory_space=pltpu.VMEM), pl.BlockSpec(memory_space=pltpu.HBM)
    far = (6, 7, 8, 9, 14, 17, 18)
    shapes = [
        ((seq_len, width), low),
        ((seq_len, width), low),
        ((seq_len, width), low),
        ((seq_len, width), low),
        ((seq_len, width), low),
        ((seq_len, width), low),
        ((seq_len, 128), full),
        ((seq_len, width), full),
        ((seq_len, width), low),
        ((seq_len, hidden_units), low),
        ((seq_len, hidden_units), low),
        ((seq_len, width), full),
        ((seq_len, width), low),
        ((mask_count, width), low),
        ((mask_count, head_width), full),
        ((mask_count, head_width), low),
    ]
    outs = [jax.ShapeDtypeStruct(*shape) for shape in shapes]
    return staged_call(
        forward_kernel,
        inputs,
        outs,
        [hbm if index in far else vmem for index in range(len(inputs))],
        [hbm if index in (9, 10) else vmem for index in range(len(shapes))],
        (0, 1, 5, 10, 11, 12, 13, 2, 3, 21),
        (0, 1, 2, 3, 4, 5, 7, 8, 11, 12),
        [
            pltpu.VMEM((slots, width), full),
            pltpu.VMEM((seq_len, width), full),
            pltpu.VMEM(inputs[14].shape, low),
            pltpu.VMEM(inputs[17].shape, low),
            pltpu.VMEM(inputs[18].shape, low),
            pltpu.VMEM((seq_len, hidden_units), low),
            pltpu.VMEM((seq_len, hidden_units), low),
            pltpu.SemaphoreType.DMA((16,)),
        ],
        pltpu.CompilerParams(vmem_limit_bytes=63 * 2**20),
    )


class Grid:
    def __init__(self):
        me = lax.axis_index("dp")
        self.core = lax.rem(me, 2)
        self.square = lax.rem(lax.div(me, 2), 4)
        self.line = lax.div(me, 8)
        self.twin = me + 1 - 2 * self.core
        self.squares = []
        self.lines = []
        for step in range(1, 4):
            other = lax.rem(self.square + step, 4)
            self.squares.append((me + 2 * (other - self.square), other))
            other = lax.rem(self.line + step, 4)
            self.lines.append((me + 8 * (other - self.line), other))

    def greet(self):
        barrier = pltpu.get_barrier_semaphore()
        peers = [self.twin] + [peer for peer, _ in self.squares + self.lines]
        for peer in peers:
            pl.semaphore_signal(barrier, inc=1, device_id=(peer,), device_id_type=MESH_ID)
        pl.semaphore_wait(barrier, len(peers))


class Sender:
    def __init__(self, send_sem, recv_sem):
        self.send_sem, self.recv_sem, self.used = send_sem, recv_sem, 0

    def start(self, source, target, peer):
        slot = self.used
        self.used += 1
        copy = pltpu.make_async_remote_copy(
            src_ref=source,
            dst_ref=target,
            send_sem=self.send_sem.at[slot],
            recv_sem=self.recv_sem.at[slot],
            device_id=(peer,),
            device_id_type=MESH_ID,
        )
        copy.start()
        return copy


def wait_all(copies):
    for copy in copies:
        copy.wait()


def merge_stats(blocks):
    tops = [block[0] for block in blocks]
    top = functools.reduce(jnp.maximum, tops)
    total = sum(block[1] * jnp.exp(block[0] - top) for block in blocks)
    return top, total, sum(block[2] for block in blocks)


def head_kernel(
    grad_scale,
    stage,
    head,
    table,
    bias,
    target_vecs,
    target_bias,
    table_grad,
    bias_grad,
    losses,
    total_loss,
    head_grad,
    heads,
    logits,
    expo,
    table_t,
    bias_col,
    part,
    land_pair,
    sum_pair,
    land_square,
    sum_square,
    land_line,
    stat,
    stat_pair,
    stat_square,
    stat_line,
    send_sem,
    recv_sem,
):
    grid = Grid()
    rows, wide = table.shape
    count = head.shape[0]
    total_mask = 32 * count
    grid.greet()
    sender = Sender(send_sem, recv_sem)
    line, square, core = grid.line, grid.square, grid.core
    flying = [sender.start(head, heads.at[line, square, core], peer) for peer, _ in grid.lines]
    heads[line, square, core] = head[...]

    def table_step(index, carry):
        at = pl.ds(pl.multiple_of(index * 128, 128), 128)
        table_t[:, at] = table[at].astype(jnp.float32).T.astype(jnp.bfloat16)
        return carry

    stage.need(1)
    lax.fori_loop(0, rows // 128, table_step, 0)
    wait_all(flying)
    flying = [
        sender.start(heads.at[:, square, core], heads.at[:, square, core], peer)
        for peer, _ in grid.squares
    ]

    def bias_step(index, carry):
        at = pl.ds(pl.multiple_of(index * 128, 128), 128)
        bias_col[at] = jnp.broadcast_to(bias[at].reshape(1, 128), (128, 128)).T
        return carry

    lax.fori_loop(0, rows // 128, bias_step, 0)
    wait_all(flying)
    sender.start(heads.at[:, :, core], heads.at[:, :, core], grid.twin).wait()

    all_heads = heads[...].reshape(total_mask, wide)
    slab = rows // 2

    def logit_step(index, carry):
        at = pl.ds(pl.multiple_of(index * slab, 16), slab)
        logits[at] = dot_right_t(table[at], all_heads)
        return carry

    lax.fori_loop(0, rows // slab, logit_step, 0)
    tile = 64
    wide_copies = total_mask // 128

    def value_at(index):
        at = pl.ds(pl.multiple_of(index * tile, tile), tile)
        shift = bias_col[at]
        return at, logits[at] + jnp.concatenate([shift] * wide_copies, axis=1)

    def top_step(index, top):
        at, value = value_at(index)
        return jnp.maximum(top, jnp.max(value.reshape(tile // 8, 8, total_mask), axis=0))

    top = lax.fori_loop(
        0, rows // tile, top_step, jnp.full((8, total_mask), -jnp.inf, jnp.float32)
    )
    top = jnp.max(top, axis=0, keepdims=True)

    def exp_step(index, total):
        at, value = value_at(index)
        value = jnp.exp(value - top)
        expo[at] = value.astype(jnp.bfloat16)
        return total + jnp.sum(value.reshape(tile // 8, 8, total_mask), axis=0)

    total = lax.fori_loop(0, rows // tile, exp_step, jnp.zeros((8, total_mask), jnp.float32))
    total = jnp.sum(total, axis=0, keepdims=True)

    def fold(row):
        return jnp.concatenate([row[:, i * 128 : i * 128 + 128] for i in range(wide_copies)], axis=0)

    def unfold(block):
        return jnp.concatenate([block[i : i + 1] for i in range(wide_copies)], axis=1)

    own_top, own_total = fold(top), fold(total)
    target = (
        jnp.sum(head[...].astype(jnp.float32) * target_vecs[...], axis=1, keepdims=True)
        + target_bias[:, 0:1]
    )
    own_target = jnp.broadcast_to(jnp.sum(target, axis=0, keepdims=True), own_top.shape)
    stat[0, 0], stat[0, 1], stat[0, 2] = own_top, own_total, own_target
    copy = sender.start(stat.at[0], stat_pair, grid.twin)
    quarter = total_mask // 4
    parts = [dot_plain(table_t[...], expo[:, :quarter])]
    copy.wait()
    stat[1, 0], stat[1, 1], stat[1, 2] = merge_stats(
        [(own_top, own_total, own_target), (stat_pair[0], stat_pair[1], stat_pair[2])]
    )
    stat_square[square] = stat[1]
    flying = [sender.start(stat.at[1], stat_square.at[square], peer) for peer, _ in grid.squares]
    parts.append(dot_plain(table_t[...], expo[:, quarter : 2 * quarter]))
    wait_all(flying)
    stat[2, 0], stat[2, 1], stat[2, 2] = merge_stats(
        [(stat_square[i, 0], stat_square[i, 1], stat_square[i, 2]) for i in range(4)]
    )
    stat_line[line] = stat[2]
    flying = [sender.start(stat.at[2], stat_line.at[line], peer) for peer, _ in grid.lines]
    parts.append(dot_plain(table_t[...], expo[:, 2 * quarter : 3 * quarter]))
    parts.append(dot_plain(table_t[...], expo[:, 3 * quarter :]))
    wait_all(flying)
    full_top, full_total, full_target = merge_stats(
        [(stat_line[i, 0], stat_line[i, 1], stat_line[i, 2]) for i in range(4)]
    )
    lse = full_top + jnp.log(full_total)
    all_lse = jnp.sum(jnp.sum(lse, axis=1, keepdims=True), axis=0, keepdims=True)
    total_loss[...] = (all_lse - full_target[0:1]) * grad_scale
    mine = lax.broadcasted_iota(jnp.int32, (count, total_mask), 0) + lax.axis_index("dp") * count
    hit = mine == lax.broadcasted_iota(jnp.int32, (count, total_mask), 1)
    own_lse = jnp.sum(jnp.where(hit, unfold(lse), 0.0), axis=1, keepdims=True)
    turned = jnp.broadcast_to(own_lse - target, (count, 128)).T
    losses[...] = turned[0:1].reshape(count)
    scale = unfold(jnp.exp(own_top - lse) * grad_scale)
    per = 128 // count
    for index in range(total_mask // 128):
        at = slice(index * 128, index * 128 + 128)
        source = parts[index * 128 // quarter]
        begin = index * 128 % quarter
        piece = (source[:, begin : begin + 128] * scale[:, at]).T.astype(jnp.bfloat16)
        for inner in range(per):
            owner = index * per + inner
            part[owner // 8, owner // 2 % 4, owner % 2] = piece[inner * count : inner * count + count]
    copy = sender.start(part.at[:, :, 1 - core], land_pair, grid.twin)

    scaled = []
    for index in range(total_mask // 128):
        at = slice(index * 128, index * 128 + 128)
        column = jnp.broadcast_to(scale[:, at], (128, 128)).T
        column = jnp.concatenate([column] * (wide // 128), axis=1)
        scaled.append((all_heads[at].astype(jnp.float32) * column).astype(jnp.bfloat16))
    scaled = jnp.concatenate(scaled, axis=0)
    slab = rows // 4

    def grad_part(index):
        at = slice(index * slab, index * slab + slab)
        table_grad[at] = dot_plain(expo[at], scaled)

    grad_part(0)
    copy.wait()
    sum_pair[...] = (part[:, :, core].astype(jnp.float32) + land_pair[...].astype(jnp.float32)).astype(
        jnp.bfloat16
    )
    flying = [
        sender.start(sum_pair.at[:, other], land_square.at[square], peer)
        for peer, other in grid.squares
    ]
    land_square[square] = sum_pair[:, square]
    grad_part(1)
    wait_all(flying)
    sum_square[...] = sum(land_square[i].astype(jnp.float32) for i in range(4)).astype(jnp.bfloat16)
    flying = [
        sender.start(sum_square.at[other], land_line.at[line], peer) for peer, other in grid.lines
    ]
    land_line[line] = sum_square[line]
    grad_part(2)
    high = scale.astype(jnp.bfloat16)
    low = (scale - high.astype(jnp.float32)).astype(jnp.bfloat16)
    both = jnp.concatenate(
        [high.astype(jnp.float32), low.astype(jnp.float32), jnp.zeros((14, total_mask), jnp.float32)],
        axis=0,
    ).astype(jnp.bfloat16)
    sums = dot_right_t(both, expo[...])
    bias_grad[...] = sums[0:1] + sums[1:2]
    grad_part(3)
    stage.send(0)
    wait_all(flying)
    head_grad[...] = sum(land_line[i].astype(jnp.float32) for i in range(4))


def head_and_table(
    head_low, entity_table, bias_row, target_vecs, target_bias, grad_scale, collective_id
):
    count, wide = head_low.shape
    rows = entity_table.shape[0]
    total_mask = 32 * count
    low, full = jnp.bfloat16, jnp.float32
    vmem = pl.BlockSpec(memory_space=pltpu.VMEM)
    folded = (total_mask // 128, 128)
    inputs = [head_low, entity_table, bias_row, target_vecs, target_bias]
    outs = [
        jax.ShapeDtypeStruct((rows, wide), full),
        jax.ShapeDtypeStruct((1, rows), full),
        jax.ShapeDtypeStruct((count,), full),
        jax.ShapeDtypeStruct((1, 128), full),
        jax.ShapeDtypeStruct((count, wide), full),
    ]
    return staged_call(
        functools.partial(head_kernel, grad_scale),
        inputs,
        outs,
        [vmem] * 5,
        [vmem] * 5,
        (1,),
        (0,),
        [
            pltpu.VMEM((4, 4, 2, count, wide), low),
            pltpu.VMEM((rows, total_mask), full),
            pltpu.VMEM((rows, total_mask), low),
            pltpu.VMEM((wide, rows), low),
            pltpu.VMEM((rows, 128), full),
            pltpu.VMEM((4, 4, 2, count, wide), low),
            pltpu.VMEM((4, 4, count, wide), low),
            pltpu.VMEM((4, 4, count, wide), low),
            pltpu.VMEM((4, 4, count, wide), low),
            pltpu.VMEM((4, count, wide), low),
            pltpu.VMEM((4, count, wide), low),
            pltpu.VMEM((3, 3) + folded, full),
            pltpu.VMEM((3,) + folded, full),
            pltpu.VMEM((4, 3) + folded, full),
            pltpu.VMEM((4, 3) + folded, full),
            pltpu.SemaphoreType.DMA((24,)),
            pltpu.SemaphoreType.DMA((24,)),
        ],
        pltpu.CompilerParams(
            collective_id=collective_id, has_side_effects=True, vmem_limit_bytes=63 * 2**20
        ),
    )


def norm_slope(value, given, gain):
    scaled, rate = norm_parts(value)
    back = given * gain
    mean_back = jnp.mean(back, axis=-1, keepdims=True)
    mean_both = jnp.mean(back * scaled, axis=-1, keepdims=True)
    grad = rate * (back - mean_back - scaled * mean_both)
    return (
        grad,
        jnp.sum(given * scaled, axis=0, keepdims=True),
        jnp.sum(given, axis=0, keepdims=True),
    )


def split_low(value):
    high = value.astype(jnp.bfloat16)
    return high, (value - high.astype(jnp.float32)).astype(jnp.bfloat16)


def place_rows(source, order, count, store):
    owners = 2 ** len(order)
    for pair in range(owners // 2):
        one, two = place_owner(order, 2 * pair), place_owner(order, 2 * pair + 1)
        both = jnp.concatenate(
            [source[one * count : one * count + count], source[two * count : two * count + count]],
            axis=0,
        )
        store(slice(pair * 2 * count, (pair + 1) * 2 * count), both.astype(jnp.bfloat16))


def middle_back_kernel(
    orders,
    grad_scale,
    stage,
    head_grad,
    target_vecs,
    head_pre,
    gain_head,
    picked,
    head_w,
    choose,
    cotangent,
    resid_two,
    gain_two,
    normed_low,
    resid_one,
    gain_one,
    out_w,
    context,
    lse_lanes,
    active_hbm,
    slope_hbm,
    up_hbm,
    down_hbm,
    up_a,
    up_b,
    head_a,
    out_b,
    down_b,
    up_c,
    down_c,
    first_grad,
    context_grad,
    lse_delta,
    vectors,
    active,
    slope,
    up_w,
    down_w,
    flip,
    normed_t,
    context_t,
    down_in,
    acc,
    up_low,
    stage_a,
    stage_c,
    sems,
):
    seq_len, width = cotangent.shape
    slots = choose.shape[1]
    words = seq_len - slots
    cuts = down_w.shape[0] // width
    loads = []
    for index, (source, target) in enumerate(
        ((active_hbm, active), (down_hbm, down_w), (slope_hbm, slope), (up_hbm, up_w))
    ):
        for cut in range(cuts):
            at = pl.ds(cut * width, width)
            view = (at,) if index == 1 else (slice(None), at)
            loads.append(
                pltpu.make_async_copy(source.at[view], target.at[view], sems.at[index * cuts + cut])
            )
    for cut in range(cuts):
        for index in range(4):
            loads[index * cuts + cut].start()

    given = head_grad[...] - grad_scale * target_vecs[...]
    pre = head_pre[...]
    raised, change = gelu_parts(pre)
    back, gain_sum, bias_sum = norm_slope(raised, given, gain_head[...][None, :])
    sums = [gain_sum, bias_sum]
    pre_low = (back * change).astype(jnp.bfloat16)
    head_weight_grad = dot_left_t(picked[...], pre_low)
    count = width // 2 ** len(orders[0])

    def keep_head(at, value):
        head_a[0, at] = value

    flip[:, : head_a.shape[2]] = head_weight_grad
    place_rows(flip[:, : head_a.shape[2]], orders[0], count, keep_head)
    stage.need(5)
    picked_high, picked_rest = split_low(dot_right_t(pre_low, head_w[...]))
    placed = dot_left_t(choose[...], picked_high) + dot_left_t(choose[...], picked_rest)

    stage.need(7, 8)
    block = 128
    total_gain = jnp.zeros((1, width), jnp.float32)
    total_bias = jnp.zeros((1, width), jnp.float32)
    for begin in range(0, seq_len, block):
        at = slice(begin, begin + block)
        given = cotangent[at].astype(jnp.float32)
        if begin >= words:
            given = given + placed[begin - words : begin - words + block]
        grad, gain_sum, bias_sum = norm_slope(resid_two[at], given, gain_two[...][None, :])
        total_gain += gain_sum
        total_bias += bias_sum
        acc[at] = grad
        down_in[at] = grad.astype(jnp.bfloat16)
    sums += [total_gain, total_bias]

    def flip_into(source, target, order_list):
        def flip_step(index, carry):
            at = pl.ds(pl.multiple_of(index * block, block), block)
            flip[at] = source[:, at].astype(jnp.float32).T
            return carry

        lax.fori_loop(0, width // block, flip_step, 0)
        for slot, order in enumerate(order_list):

            def keep(at, value, slot=slot):
                target[slot, at] = value

            place_rows(flip, order, count, keep)

    stage.need(10, 14)
    flip_into(normed_low, normed_t, (orders[0], orders[2]))
    flip_into(context, context_t, (orders[1],))

    column = 384
    span = seq_len
    block_two = seq_len // 2
    split = down_b.shape[2]
    owners = 2 ** len(orders[0])
    tall = down_w.shape[0] // owners
    spots = [
        {place_owner(order, place): place for place in range(owners)}
        for order in (orders[1], orders[2])
    ]
    stores = []
    for cut in range(cuts):
        at = slice(cut * width, cut * width + width)
        for index in range(4):
            loads[index * cuts + cut].wait()
        for begin in range(0, width, column):
            piece = dot_left_t(active[:, at], down_in[:, begin : begin + column])
            for inner in range(width // tall):
                owner = cut * (width // tall) + inner
                rows = piece[inner * tall : inner * tall + tall].astype(jnp.bfloat16)
                stop = min(begin + column, split)
                if begin < split:
                    place = spots[0][owner] * tall
                    stage_a[place : place + tall, begin:stop] = rows[:, : stop - begin]
                if begin + column > split:
                    start = max(begin, split)
                    place = spots[1][owner] * tall
                    stage_c[place : place + tall, start - split : begin + column - split] = rows[
                        :, start - begin :
                    ]

        def back_step(index, carry, at=at):
            rows = pl.ds(pl.multiple_of(index * span, 16), span)
            grad = dot_right_t(down_in[rows], down_w[at]) * slope[rows, at].astype(jnp.float32)
            grad = grad.astype(jnp.bfloat16)
            up_low[rows] = grad
            acc[rows] = acc[rows] + dot_right_t(grad, up_w[:, at])
            return carry

        lax.fori_loop(0, seq_len // span, back_step, 0)
        target, slot, order_slot = ((up_a, 0, 0), (up_a, 1, 0), (up_b, 0, 0), (up_c, 0, 1))[cut]
        for begin in range(0, width, column):
            target[slot, :, begin : begin + column] = dot_plain(
                normed_t[order_slot], up_low[:, begin : begin + column]
            ).astype(jnp.bfloat16)
    stage.send(0, 1, 5)
    stage.need(11, 13)
    stores = [
        pltpu.make_async_copy(stage_a, down_b.at[0], sems.at[4 * cuts]),
        pltpu.make_async_copy(stage_c, down_c.at[0], sems.at[4 * cuts + 1]),
    ]
    for store in stores:
        store.start()

    total_gain = jnp.zeros((1, width), jnp.float32)
    total_bias = jnp.zeros((1, width), jnp.float32)
    row = lax.broadcasted_iota(jnp.int32, (width, 128), 0)
    lane = lax.broadcasted_iota(jnp.int32, (width, 128), 1)
    spot = 4 * lax.div(row, 128) + 2 + lax.div(lax.rem(row, 128), HD)
    pick = (spot == lane).astype(jnp.float32).astype(jnp.bfloat16)
    for begin in range(0, seq_len, block_two):
        at = slice(begin, begin + block_two)
        grad, gain_sum, bias_sum = norm_slope(resid_one[at], acc[at], gain_one[...][None, :])
        total_gain += gain_sum
        total_bias += bias_sum
        first_grad[at] = grad
        low = grad.astype(jnp.bfloat16)
        down_in[at] = low
        back = dot_right_t(low, out_w[...]).astype(jnp.bfloat16)
        context_grad[at] = back
        high, rest = split_low(back.astype(jnp.float32) * context[at].astype(jnp.float32))
        lse_delta[at] = lse_lanes[at] + dot_plain(high, pick) + dot_plain(rest, pick)
    stage.send(7, 8)
    sums += [total_gain, total_bias]
    tall, room = vectors.shape[1:]
    every = tall // owners
    placed = jnp.zeros((tall, room), jnp.float32)
    offset = 0
    for vector in sums:
        size = vector.shape[1]
        per = size // owners
        row = lax.broadcasted_iota(jnp.int32, (tall, size), 0)
        place = lax.div(row, every)
        owner = jnp.zeros((tall, size), jnp.int32)
        for spot, mask in enumerate(orders[0]):
            owner += lax.rem(lax.div(place, 2 ** (len(orders[0]) - 1 - spot)), 2) * mask
        column_at = lax.broadcasted_iota(jnp.int32, (tall, size), 1)
        mine = (lax.div(column_at, per) == owner) & (lax.rem(row, every) == 0)
        spread = jnp.where(mine, vector, 0.0).astype(jnp.bfloat16)
        source = lax.broadcasted_iota(jnp.int32, (size, room), 0)
        target = lax.broadcasted_iota(jnp.int32, (size, room), 1)
        move = (lax.rem(source, per) + offset == target).astype(jnp.float32).astype(jnp.bfloat16)
        placed += dot_plain(spread, move)
        offset += per
    vectors[0] = placed.astype(jnp.bfloat16)
    for begin in range(0, width, column):
        out_b[0, :, begin : begin + column] = dot_plain(
            context_t[0], down_in[:, begin : begin + column]
        ).astype(jnp.bfloat16)
    for store in stores:
        store.wait()


DOWN_SPLIT = 512


def middle_back(inputs, orders, grad_scale):
    seq_len, width = inputs[7].shape
    hidden_units = inputs[16].shape[1]
    head_width = inputs[0].shape[1]
    low, full = jnp.bfloat16, jnp.float32
    cuts = hidden_units // width
    vmem, hbm = pl.BlockSpec(memory_space=pltpu.VMEM), pl.BlockSpec(memory_space=pltpu.HBM)
    shapes = [
        ((2, width, width), low),
        ((1, width, width), low),
        ((1, width, head_width), low),
        ((1, width, width), low),
        ((1, hidden_units, DOWN_SPLIT), low),
        ((1, width, width), low),
        ((1, hidden_units, width - DOWN_SPLIT), low),
        ((seq_len, width), full),
        ((seq_len, width), low),
        ((seq_len, 128), full),
        ((1, 8 * 2 ** len(orders[0]), 256), low),
    ]
    outs = [jax.ShapeDtypeStruct(*shape) for shape in shapes]
    return staged_call(
        functools.partial(middle_back_kernel, orders, grad_scale),
        inputs,
        outs,
        [vmem] * 16 + [hbm] * 4,
        [hbm if index in (4, 6) else vmem for index in range(len(shapes))],
        (5, 7, 8, 10, 14, 11, 13),
        (0, 1, 3, 5, 7, 8),
        [
            pltpu.VMEM((seq_len, hidden_units), low),
            pltpu.VMEM((seq_len, hidden_units), low),
            pltpu.VMEM((width, hidden_units), low),
            pltpu.VMEM((hidden_units, width), low),
            pltpu.VMEM((width, seq_len), full),
            pltpu.VMEM((2, width, seq_len), low),
            pltpu.VMEM((1, width, seq_len), low),
            pltpu.VMEM((seq_len, width), low),
            pltpu.VMEM((seq_len, width), full),
            pltpu.VMEM((seq_len, width), low),
            pltpu.VMEM((hidden_units, DOWN_SPLIT), low),
            pltpu.VMEM((hidden_units, width - DOWN_SPLIT), low),
            pltpu.SemaphoreType.DMA((4 * cuts + 2,)),
        ],
        pltpu.CompilerParams(vmem_limit_bytes=63 * 2**20),
    )


def last_kernel(grad_scale, codes, back, table_hbm, bias_in, *refs):
    sums, refs = refs[:SUMS], refs[SUMS:]
    table_out, bias_out = refs[:2]
    outs, refs = refs[2 : 2 + SUMS - 4], refs[2 + SUMS - 4 :]
    flats, refs = refs[: len(FLAT)], refs[len(FLAT) :]
    table_in, result, sems, move_sems = refs
    rows = table_hbm.shape[0]
    entries = back.shape[0]
    step = 1024
    parts = [(begin, min(step, rows - begin)) for begin in range(0, rows, step)]
    loads = [
        pltpu.make_async_copy(
            table_hbm.at[pl.ds(begin, size)], table_in.at[pl.ds(begin, size)], sems.at[0, index]
        )
        for index, (begin, size) in enumerate(parts)
    ]
    stores = [
        pltpu.make_async_copy(
            result.at[pl.ds(begin, size)], table_out.at[pl.ds(begin, size)], sems.at[1, index]
        )
        for index, (begin, size) in enumerate(parts)
    ]
    for load in loads:
        load.start()
    up_two, down_a, up_last, down_b, up_third = sums[:5]
    up_out, down_out = outs[:2]
    width = up_last.shape[2]
    pairs = [
        (value, up_out.at[:, pl.ds(index * width, width)])
        for index, value in enumerate((up_two.at[0], up_two.at[1], up_third.at[0], up_last.at[0]))
    ]
    pairs.append((down_a.at[0], down_out.at[:, pl.ds(0, down_a.shape[2])]))
    pairs.append((down_b.at[0], down_out.at[:, pl.ds(down_a.shape[2], down_b.shape[2])]))
    rest = [value for index, value in enumerate(sums) if index > 4 and index != VECTOR]
    pairs += [(source.at[0], target) for source, target in zip(rest, outs[2:])]
    moves = [
        pltpu.make_async_copy(source, target, move_sems.at[index])
        for index, (source, target) in enumerate(pairs)
    ]
    for move in moves:
        move.start()
    code = codes[0:1]
    target = (code >= rows).astype(jnp.float32)
    flags = jnp.broadcast_to(target, (16, entries)).astype(jnp.bfloat16)
    code = jnp.where(code >= rows, code - rows, code)
    for index, (begin, size) in enumerate(parts):
        row = lax.broadcasted_iota(jnp.int32, (size, entries), 0) + begin
        match = (row == code).astype(jnp.float32).astype(jnp.bfloat16)
        at = slice(begin, begin + size)
        counts = dot_right_t(flags, match)
        bias_out[at] = (bias_in[:, at] - grad_scale * counts[0:1]).reshape(size)
        added = dot_plain(match, back[...])
        loads[index].wait()
        result[at] = table_in[at] + added
        stores[index].start()
    offset = 0
    for target in flats:
        size = target.shape[0]
        target[...] = sums[VECTOR][0, 0:1, offset : offset + size].reshape(size)
        offset += size
    for copy in stores + moves:
        copy.wait()


SUMS = 15
VECTOR = 6
FLAT = (0, 0, 1, 1, 1, 1)


def last_step(codes, back, table_grad, bias_grad, sums, sizes, grad_scale):
    vmem, hbm = pl.BlockSpec(memory_space=pltpu.VMEM), pl.BlockSpec(memory_space=pltpu.HBM)
    full = jnp.float32
    up_rows, width = sums[0].shape[1:]
    down_rows = sums[1].shape[1]
    shapes = [
        table_grad.shape,
        (bias_grad.shape[1],),
        (up_rows, 4 * width),
        (down_rows, width),
    ] + [value.shape[1:] for index, value in enumerate(sums) if index > 4 and index != VECTOR]
    shapes += [(sizes[kind],) for kind in FLAT]
    return pl.pallas_call(
        functools.partial(last_kernel, grad_scale),
        out_shape=[jax.ShapeDtypeStruct(shape, full) for shape in shapes],
        in_specs=[vmem, vmem, hbm, vmem] + [vmem] * len(sums),
        out_specs=[hbm, vmem] + [hbm] * (len(shapes) - 2 - len(FLAT)) + [vmem] * len(FLAT),
        scratch_shapes=[
            pltpu.VMEM(table_grad.shape, full),
            pltpu.VMEM(table_grad.shape, full),
            pltpu.SemaphoreType.DMA((2, 8)),
            pltpu.SemaphoreType.DMA((len(sums) + 1,)),
        ],
        compiler_params=pltpu.CompilerParams(vmem_limit_bytes=63 * 2**20),
    )(codes, back, table_grad, bias_grad, *sums)


def place_owner(order, place):
    bits = len(order)
    return sum(((place >> (bits - 1 - spot)) & 1) * mask for spot, mask in enumerate(order))


class Piece:
    def __init__(
        self, rows, stages, send, own, land, tail, pack, tail_land, out, send_sem, recv_sem
    ):
        self.rows, self.stages = rows, stages
        self.send, self.own, self.land = send, own, land
        self.tail, self.pack, self.tail_land, self.out = tail, pack, tail_land, out
        self.send_sem, self.recv_sem = send_sem, recv_sem
        self.sizes = [rows * 2 ** (stages - 1 - stage) for stage in range(stages)]
        self.spots = [sum(self.sizes[:stage]) for stage in range(stages)]

    def copy(self, stage, partner, bit):
        size = self.sizes[stage]
        away = (1 - bit) * size
        if stage < self.stages - 1:
            away = pl.multiple_of(away, 16)
        if stage == 0:
            source, target = self.send.at[:, pl.ds(away, size)], self.land.at[:, pl.ds(0, size)]
        elif stage < self.stages - 1:
            spot = pl.multiple_of(self.spots[stage - 1] + away, 16)
            source = self.land.at[:, pl.ds(spot, size)]
            target = self.land.at[:, pl.ds(self.spots[stage], size)]
        else:
            source, target = self.pack, self.tail_land
        return pltpu.make_async_remote_copy(
            src_ref=source,
            dst_ref=target,
            send_sem=self.send_sem.at[stage],
            recv_sem=self.recv_sem.at[stage],
            device_id=(partner,),
            device_id_type=MESH_ID,
        )

    def held(self, stage, bit):
        size = self.sizes[stage]
        if stage == 0 and self.own is not None:
            return self.own, 0
        if stage == 0:
            return self.send, pl.multiple_of(bit * size, 16)
        return self.land, pl.multiple_of(self.spots[stage - 1] + bit * size, 16)

    def add(self, stage, bit, half_index):
        size = self.sizes[stage]
        half = size // 2
        unit = 48 if half % 48 == 0 else 16
        start = half_index * half
        source, base = self.held(stage, bit)
        for slot in range(self.land.shape[0]):

            def step(index, carry, slot=slot):
                row = pl.multiple_of(start + index * unit, 16)
                mine = source[slot, pl.ds(pl.multiple_of(base + row, 16), unit)]
                spot = pl.ds(pl.multiple_of(self.spots[stage] + row, 16), unit)
                theirs = self.land[slot, spot]
                total = mine.astype(jnp.float32) + theirs.astype(jnp.float32)
                self.land[slot, spot] = total.astype(jnp.bfloat16)
                return carry

            lax.fori_loop(0, half // unit, step, 0)

    def add_tail(self, stage, bit, following):
        size = self.sizes[stage]
        half = size // 2
        middle = self.land.shape[2] // 2
        source, base = self.held(stage, bit)
        for slot in range(self.land.shape[0]):
            mine = source[slot, pl.ds(base, size)]
            theirs = self.land[slot, pl.ds(self.spots[stage], size)]
            self.tail[slot] = mine.astype(jnp.float32) + theirs.astype(jnp.float32)
            other = self.tail[slot, pl.ds(pl.multiple_of((1 - following) * half, 8), half)]
            self.pack[slot] = jnp.concatenate(
                [other[:, :middle], other[:, middle:]], axis=0
            ).astype(jnp.bfloat16)

    def finish(self, bit):
        size = self.sizes[-1]
        for slot in range(self.out.shape[0]):
            mine = self.tail[slot, pl.ds(pl.multiple_of(bit * size, 8), size)]
            theirs = self.tail_land[slot].astype(jnp.float32)
            self.out[slot] = mine + jnp.concatenate([theirs[:size], theirs[size:]], axis=1)


class Stream:
    def __init__(self, order, partner_of, pieces):
        self.order, self.partner_of, self.pieces = order, partner_of, pieces
        self.stages = len(order)

    def launch(self, stage):
        partner, bit = self.partner_of[self.order[stage]]
        for piece in self.pieces:
            piece.copy(stage, partner, bit).start()

    def advance(self, stage):
        partner, bit = self.partner_of[self.order[stage]]
        for piece in self.pieces:
            piece.copy(stage, partner, bit).wait()
        if stage == self.stages - 1:
            for piece in self.pieces:
                piece.finish(bit)
        elif stage == self.stages - 2:
            for piece in self.pieces:
                piece.add_tail(stage, bit, self.partner_of[self.order[stage + 1]][1])
            self.launch(stage + 1)
        else:
            following = self.partner_of[self.order[stage + 1]][1]
            for piece in self.pieces:
                piece.add(stage, bit, 1 - following)
            self.launch(stage + 1)
            for piece in self.pieces:
                piece.add(stage, bit, following)


def partners(me, masks):
    result = {}
    for mask in masks:
        bit = lax.rem(lax.div(me, mask), 2)
        result[mask] = (me + mask - 2 * mask * bit, bit)
    return result


EARLY = (
    (0, 2, 24, 768),
    (1, 1, 96, 512),
    (2, 1, 24, 768),
    (3, 1, 96, 256),
    (4, 1, 24, 768),
    (4, 1, 24, 256),
    (4, 1, 8, 256),
    (5, 1, 24, 768),
)
LATE = (
    (6, 1, 24, 768),
    (7, 1, 24, 768),
    (8, 1, 24, 768),
    (9, 1, 24, 768),
    (10, 1, 24, 768),
    (11, 1, 24, 768),
    (11, 1, 8, 768),
)
STREAM_ORDER = (0, 1, 2, 2, 0, 1, 1, 1, 2, 1, 0, 0)

WORD_POINTS = ("word0", "word1")

PLAN = {('r', 1): ((0, 0),), ('p', 1): ((1, 0),), ('r', 2): ((2, 0), (3, 0)), ('p', 2): ((4, 0),), ('r', 3): ((5, 0),), ('r', 4): ((2, 1),), ('r', 5): ((0, 1),), 'KV': ((1, 1),), 'ew': ((3, 1),), 'ww': ((4, 1),), 'ent': ((6, 0), (2, 2), (7, 0), (5, 1), (8, 0)), 'we': ((9, 0),), 'word0': ((10, 0),), 'word1': ((1, 2), (11, 0), (3, 2), (0, 2), (2, 3)), 'end': ((8, 1), (5, 2), (4, 2), (1, 3), (10, 1), (0, 3), (6, 1), (8, 2), (5, 3), (7, 1), (4, 3), (11, 1), (1, 4), (3, 3), (0, 4), (5, 4), (4, 4), (9, 1), (6, 2), (2, 4), (8, 3), (10, 2), (6, 3), (7, 2), (10, 3), (11, 2), (9, 2), (6, 4), (3, 4), (8, 4), (7, 3), (10, 4), (11, 3), (9, 3), (7, 4), (11, 4), (9, 4))}


def piece_scratch(spec, stages, source, own):
    _, slots, rows, width = spec
    owners = 2**stages
    shapes = []
    if source:
        shapes.append(pltpu.VMEM((slots, rows * owners, width), jnp.bfloat16))
    if own:
        shapes.append(pltpu.VMEM((slots, rows * owners // 2, width), jnp.bfloat16))
    shapes += [
        pltpu.VMEM((slots, rows * (owners - 2), width), jnp.bfloat16),
        pltpu.VMEM((slots, 2 * rows, width), jnp.float32),
        pltpu.VMEM((slots, 2 * rows, width // 2), jnp.bfloat16),
        pltpu.VMEM((slots, 2 * rows, width // 2), jnp.bfloat16),
        pltpu.SemaphoreType.DMA((stages,)),
        pltpu.SemaphoreType.DMA((stages,)),
    ]
    return shapes


def attention_back_kernel(orders, grad_scale, stage, *refs):
    stages = len(orders[0])
    refs = list(refs)

    def take(count):
        taken = refs[:count]
        del refs[:count]
        return taken

    early_send = take(len(EARLY))
    (hidden, qword, qent, keys, values, cgrad, feat_q, feat_k, lse_delta, first_grad, head_low, slot_row) = take(12)
    (w_ww, w_we, w_ew, w_ee, w_key, w_value, dense, entity_low) = take(8)
    early_out = take(len(EARLY))
    late_out = take(len(LATE))
    words_out, request_out = take(2)
    devices = request_out.shape[0]
    early_pieces = []
    own_copies = []
    me = lax.axis_index("dp")
    partner_of = partners(me, orders[0])
    own_sem = refs.pop()
    request_sems = refs.pop()
    request_send = refs.pop()
    word_weights = []
    dqw, dqe, dkey, dvalue, prob_s, grad_s, flip, hidden_t, hidden_te, entity_t = refs[-10:]
    del refs[-10:]
    pieces = [[] for _ in STREAM_ORDER]
    early_flat = []
    for index, spec in enumerate(EARLY):
        own, land, tail, pack, tail_land, send_sem, recv_sem = take(7)
        piece = Piece(
            spec[2], stages, early_send[index], own, land, tail, pack, tail_land,
            early_out[index], send_sem, recv_sem,
        )
        pieces[spec[0]].append(piece)
        early_flat.append(piece)
        bit = partner_of[orders[STREAM_ORDER[spec[0]]][0]][1]
        size = spec[2] * 2 ** (stages - 1)
        own_copies.append(
            pltpu.make_async_copy(
                early_send[index].at[:, pl.ds(pl.multiple_of(bit * size, 16), size)],
                own,
                own_sem.at[index],
            )
        )
    late_source = []
    for index, spec in enumerate(LATE):
        source, land, tail, pack, tail_land, send_sem, recv_sem = take(7)
        late_source.append(source)
        pieces[spec[0]].append(
            Piece(
                spec[2], stages, source, None, land, tail, pack, tail_land,
                late_out[index], send_sem, recv_sem,
            )
        )
    spare = (early_flat[1].own, early_flat[3].own)
    split = spare[0].shape[2]
    for index, weight in enumerate((w_ww, w_we)):
        rows = weight.shape[0]
        for part, at in enumerate((pl.ds(0, split), pl.ds(split, weight.shape[1] - split))):
            word_weights.append(
                pltpu.make_async_copy(
                    weight.at[:, at],
                    spare[part].at[0, pl.ds(index * rows, rows)],
                    own_sem.at[len(EARLY) + 2 * index + part],
                )
            )
    streams = [
        Stream(orders[order], partner_of, pieces[index])
        for index, order in enumerate(STREAM_ORDER)
    ]
    first_late = LATE[0][0]

    def go_on(point):
        for index, stage in PLAN.get(point, ()):
            if stage == 0 and index < first_late:
                for piece, spec in enumerate(EARLY):
                    if spec[0] == index:
                        own_copies[piece].wait()
            streams[index].advance(stage)
            if stage == 0 and index in (1, 3):
                for copy in word_weights[(index - 1) // 2 :: 2]:
                    copy.start()

    greet_all(me, devices)
    for stream in streams[:first_late]:
        stream.launch(0)
    for copy in own_copies:
        copy.start()

    width = hidden.shape[1]
    seq_len = hidden.shape[0]
    words = words_out.shape[0]
    block = 128
    tall = seq_len // 2
    taller = words // len(WORD_POINTS)
    lane = lax.broadcasted_iota(jnp.int32, (1, block), 1)
    low_half = (lane < HD).astype(jnp.float32).astype(jnp.bfloat16)
    high_half = (lane >= HD).astype(jnp.float32).astype(jnp.bfloat16)
    halves = (low_half, high_half)

    stage.need(8)
    def flip_step(index, carry):
        at = pl.ds(pl.multiple_of(index * block, block), block)
        flip[at] = hidden[:, at].astype(jnp.float32).T
        return carry

    lax.fori_loop(0, width // block, flip_step, 0)
    owners = 2**stages
    rows = width // owners
    for slot, order in enumerate(orders):
        begin = words if slot == 2 else 0
        for pair in range(owners // 2):
            one, two = place_owner(order, 2 * pair), place_owner(order, 2 * pair + 1)
            both = jnp.concatenate(
                [flip[one * rows : one * rows + rows, begin:], flip[two * rows : two * rows + rows, begin:]],
                axis=0,
            ).astype(jnp.bfloat16)
            if slot == 2:
                hidden_te[pair * 2 * rows : (pair + 1) * 2 * rows] = both
            else:
                hidden_t[slot, pair * 2 * rows : (pair + 1) * 2 * rows] = both

    stage.need(*range(9, 17))
    go_on("start")

    def go_on_in_loop(name, pair):
        for point in range(width // block):
            if (name, point) in PLAN:
                pl.when(pair == point)(functools.partial(go_on, (name, point)))

    def pair_step(pair, carry):
        lanes = pl.ds(pl.multiple_of(pair * block, block), block)
        key_pair = keys[:, lanes]
        value_pair = values[:, lanes]
        key_feat = [key_pair * halves[h] + feat_k[...] * halves[1 - h] for h in range(2)]
        key_only = [key_pair * halves[h] for h in range(2)]
        value_only = [value_pair * halves[h] for h in range(2)]

        def row_step(index, inner):
            at = pl.ds(pl.multiple_of(index * tall, 16), tall)
            qw = qword[at, lanes]
            qe = qent[at, lanes]
            feats = feat_q[at]
            given = cgrad[at, lanes]
            stats = lse_delta[at]
            spot = lax.broadcasted_iota(jnp.int32, (1, block), 1) - 4 * pair
            total_w = jnp.zeros((tall, block), jnp.float32)
            total_e = jnp.zeros((tall, block), jnp.float32)
            for h in range(2):
                left_w = qw * halves[h] + feats * halves[1 - h]
                left_e = qe * halves[h] + feats * halves[1 - h]
                scores = jnp.concatenate(
                    [
                        dot_right_t(left_w, key_feat[h][:words]),
                        dot_right_t(left_e, key_feat[h][words:]),
                    ],
                    axis=1,
                )
                prob = jnp.exp(scores - jnp.sum(jnp.where(spot == h, stats, 0.0), axis=1, keepdims=True))
                pgrad = dot_right_t(given, value_only[h])
                sgrad = (prob * (pgrad - jnp.sum(jnp.where(spot == 2 + h, stats, 0.0), axis=1, keepdims=True))).astype(jnp.bfloat16)
                prob_s[h, at] = prob.astype(jnp.bfloat16)
                grad_s[h, at] = sgrad
                total_w += dot_plain(sgrad[:, :words], key_only[h][:words])
                total_e += dot_plain(sgrad[:, words:], key_only[h][words:])
            dqw[at, lanes] = total_w.astype(jnp.bfloat16)
            dqe[at, lanes] = total_e.astype(jnp.bfloat16)
            return inner

        lax.fori_loop(0, seq_len // tall, row_step, 0)
        go_on_in_loop("r", pair)
        qw_all, qe_all, given_all = qword[:, lanes], qent[:, lanes], cgrad[:, lanes]
        dkey[:words, lanes] = (
            dot_left_t(grad_s[0, :, :words], qw_all * halves[0])
            + dot_left_t(grad_s[1, :, :words], qw_all * halves[1])
        ).astype(jnp.bfloat16)
        dkey[words:, lanes] = (
            dot_left_t(grad_s[0, :, words:], qe_all * halves[0])
            + dot_left_t(grad_s[1, :, words:], qe_all * halves[1])
        ).astype(jnp.bfloat16)
        dvalue[:, lanes] = (
            dot_left_t(prob_s[0], given_all * halves[0])
            + dot_left_t(prob_s[1], given_all * halves[1])
        ).astype(jnp.bfloat16)

        go_on_in_loop("p", pair)
        return carry

    lax.fori_loop(0, width // block, pair_step, 0)

    query_scale = HD ** (-0.5)
    column = 384

    def weight_grad(source, slot, order_slot, grad, begin, end, scale):
        for cut in range(0, width, column):
            left = hidden_te[...] if order_slot == 2 else hidden_t[order_slot, :, begin:end]
            piece = dot_plain(left, grad[begin:end, cut : cut + column])
            if scale:
                piece = piece * query_scale
            source[slot, :, cut : cut + column] = piece.astype(jnp.bfloat16)

    weight_grad(late_source[0], 0, 1, dkey, 0, seq_len, False)
    streams[6].launch(0)
    weight_grad(late_source[1], 0, 1, dvalue, 0, seq_len, False)
    streams[7].launch(0)
    go_on("KV")
    weight_grad(late_source[2], 0, 2, dqw, words, seq_len, True)
    streams[8].launch(0)
    go_on("ew")
    weight_grad(late_source[3], 0, 1, dqe, words, seq_len, True)
    streams[9].launch(0)
    go_on("ee")
    weight_grad(late_source[4], 0, 0, dqw, 0, words, True)
    streams[10].launch(0)
    go_on("ww")

    stage.need(17, *range(22, 27))

    def data_grad(begin, size, queries):
        at = pl.ds(begin, size)
        return (
            first_grad[at]
            + query_scale * queries(at)
            + dot_right_t(dkey[at], w_key[...])
            + dot_right_t(dvalue[at], w_value[...])
        )

    def entity_queries(at):
        return dot_right_t(dqw[at], w_ew[...]) + dot_right_t(dqe[at], w_ee[...])

    def word_queries(at):
        total = 0.0
        for index, grad in enumerate((dqw, dqe)):
            rows_at = pl.ds(index * width, width)
            total += dot_right_t(grad[at, :split], spare[0][0, rows_at])
            total += dot_right_t(grad[at, split:], spare[1][0, rows_at])
        return total

    state_low = data_grad(words, seq_len - words, entity_queries).astype(jnp.bfloat16)
    vectors = jnp.concatenate(
        [dot_right_t(state_low, dense[...]).astype(jnp.bfloat16), (head_low[...].astype(jnp.float32) * -grad_scale).astype(jnp.bfloat16)], axis=0
    )
    entries = slot_row.shape[1]
    wanted = lax.broadcasted_iota(jnp.int32, (vectors.shape[0], entries), 0)
    placing = (wanted == slot_row[0:1]).astype(jnp.float32).astype(jnp.bfloat16)
    per_request = dot_left_t(placing, vectors).astype(jnp.bfloat16)
    request_send[...] = per_request.reshape(request_send.shape)

    def request_copy(step):
        peer = lax.rem(me + step, devices)
        return pltpu.make_async_remote_copy(
            src_ref=request_send.at[peer],
            dst_ref=request_out.at[me],
            send_sem=request_sems.at[0, step],
            recv_sem=request_sems.at[1, step],
            device_id=(peer,),
            device_id_type=MESH_ID,
        )

    def begin_request(step, carry):
        request_copy(step).start()
        return carry

    def finish_request(step, carry):
        request_copy(step).wait()
        return carry

    lax.fori_loop(1, devices, begin_request, 0)
    request_out[me] = request_send[me]
    entity_width = dense.shape[0]
    few = entity_width // owners
    for cut in range(0, entity_width, block):
        flip[cut : cut + block, :block] = entity_low[:, cut : cut + block].astype(jnp.float32).T
    for pair in range(owners // 2):
        one, two = place_owner(orders[0], 2 * pair), place_owner(orders[0], 2 * pair + 1)
        both = jnp.concatenate(
            [flip[one * few : one * few + few, :block], flip[two * few : two * few + few, :block]],
            axis=0,
        )
        entity_t[pair * 2 * few : (pair + 1) * 2 * few] = both.astype(jnp.bfloat16)
    late_source[6][0] = dot_plain(entity_t[...], state_low).astype(jnp.bfloat16)
    go_on("ent")
    weight_grad(late_source[5], 0, 0, dqe, 0, words, True)
    streams[11].launch(0)
    go_on("we")
    for copy in word_weights:
        copy.wait()

    def word_step(index, carry):
        begin = pl.multiple_of(index * taller, 16)
        words_out[pl.ds(begin, taller)] = data_grad(begin, taller, word_queries).astype(jnp.bfloat16)
        for point in range(words // taller):
            name = WORD_POINTS[point]
            if name in PLAN:
                pl.when(index == point)(functools.partial(go_on, name))
        return carry

    lax.fori_loop(0, words // taller, word_step, 0)
    go_on("end")
    lax.fori_loop(1, devices, finish_request, 0)


def in_order(grad, order):
    bits = len(order)
    owners = 2**bits
    view = grad.reshape((2,) * bits + (grad.shape[0] // owners, grad.shape[1]))
    spots = tuple(bits - mask.bit_length() for mask in order)
    return view.transpose(spots + (bits, bits + 1)).reshape(grad.shape)


def attention_back(early_grads, inputs, weights, grad_scale, collective_id):
    devices = lax.axis_size("dp")
    orders = stage_masks(devices)
    stages = len(orders[0])
    hidden = inputs[0]
    seq_len, width = hidden.shape
    slots = weights[-1].shape[0]
    words = seq_len - slots
    outs = [
        jax.ShapeDtypeStruct((count, rows, wide), jnp.float32)
        for _, count, rows, wide in EARLY + LATE
    ] + [
        jax.ShapeDtypeStruct((words, width), jnp.bfloat16),
        jax.ShapeDtypeStruct(
            (devices, inputs[11].shape[1] // devices, weights[-2].shape[0]), jnp.bfloat16
        ),
    ]
    scratch = []
    for spec in EARLY:
        scratch += piece_scratch(spec, stages, False, True)
    for spec in LATE:
        scratch += piece_scratch(spec, stages, True, False)
    scratch += [pltpu.VMEM((seq_len, width), jnp.bfloat16)] * 4
    scratch += [pltpu.VMEM((2, seq_len, seq_len), jnp.bfloat16)] * 2
    scratch += [
        pltpu.VMEM((width, seq_len), jnp.float32),
        pltpu.VMEM((2, width, seq_len), jnp.bfloat16),
        pltpu.VMEM((width, slots), jnp.bfloat16),
        pltpu.VMEM((weights[-2].shape[0], slots), jnp.bfloat16),
        pltpu.VMEM((devices, inputs[11].shape[1] // devices, weights[-2].shape[0]), jnp.bfloat16),
        pltpu.SemaphoreType.DMA((2, devices)),
        pltpu.SemaphoreType.DMA((len(EARLY) + 4,)),
    ]
    vmem = pl.BlockSpec(memory_space=pltpu.VMEM)
    return staged_call(
        functools.partial(attention_back_kernel, orders, grad_scale),
        [*early_grads, *inputs, *weights],
        outs,
        [pl.BlockSpec(memory_space=pltpu.HBM)] * len(EARLY)
        + [vmem] * len(inputs)
        + [pl.BlockSpec(memory_space=pltpu.HBM)] * 2
        + [vmem] * (len(weights) - 2),
        [vmem] * len(outs),
        (8, 11, 12, 9, 10, 13, 14, 15, 16, 17, 22, 23, 24, 25, 26),
        (),
        scratch,
        pltpu.CompilerParams(
            collective_id=collective_id, has_side_effects=True, vmem_limit_bytes=63 * 2**20
        ),
    )


def fused_body(
    word_states,
    word_segments,
    entity_segments,
    request_rows,
    request_slot,
    mask_slots,
    entity_table,
    vocab_bias,
    entity_dense,
    query_ww,
    query_we,
    query_ew,
    query_ee,
    key_weight,
    value_weight,
    out_weight,
    norm1_gain,
    norm1_bias,
    up_weight,
    down_weight,
    norm2_gain,
    norm2_bias,
    head_weight,
    head_gain,
    head_bias,
    cotangent,
):
    devices = lax.axis_size("dp")
    low = jnp.bfloat16
    slot_count = entity_segments.shape[1]
    mask_count = mask_slots.shape[1]
    grad_scale = 1.0 / (mask_count * devices)
    orders = stage_masks(devices)
    bias_row = vocab_bias.astype(jnp.float32)
    (
        entity_low,
        target_vecs,
        target_bias,
        code_row,
        word_q,
        word_e,
        word_k,
        word_v,
        feat_q,
        feat_k,
        choose,
        slot_row,
    ) = lookup(
        [
            request_rows.T,
            entity_table,
            bias_row,
            request_slot.T,
            word_states,
            query_ww,
            query_we,
            key_weight,
            value_weight,
            word_segments,
            entity_segments,
            mask_slots,
        ],
        slot_count,
        mask_count,
        0,
    )
    (
        hidden_low,
        query_word,
        query_entity,
        key_rows,
        values,
        context_low,
        lse_lanes,
        residual_one,
        normed_low,
        activated,
        gelu_slope,
        residual_two,
        layer_low,
        picked_low,
        head_pre,
        head_low,
    ) = forward_pass(
        [
            word_states,
            entity_low,
            feat_q,
            feat_k,
            choose,
            entity_dense,
            word_q,
            word_e,
            word_k,
            word_v,
            query_ew,
            query_ee,
            key_weight,
            value_weight,
            out_weight,
            norm1_gain,
            norm1_bias,
            up_weight,
            down_weight,
            norm2_gain,
            norm2_bias,
            head_weight,
            head_gain,
            head_bias,
        ]
    )
    table_grad, bias_grad, losses, total_loss, head_grad = head_and_table(
        head_low,
        entity_table,
        bias_row,
        target_vecs,
        target_bias,
        grad_scale,
        1,
    )
    (
        up_a,
        up_b,
        head_a,
        out_b,
        down_b,
        up_c,
        down_c,
        first_grad,
        context_grad,
        lse_delta,
        vectors,
    ) = middle_back(
        [
            head_grad,
            target_vecs,
            head_pre,
            head_gain,
            picked_low,
            head_weight,
            choose,
            cotangent,
            residual_two,
            norm2_gain,
            normed_low,
            residual_one,
            norm1_gain,
            out_weight,
            context_low,
            lse_lanes,
            activated,
            gelu_slope,
            up_weight,
            down_weight,
        ],
        orders,
        grad_scale,
    )
    *sums, words_grad, back_rows = attention_back(
        [up_a, down_b, up_c, down_c, up_b, head_a, vectors, out_b],
        [
            hidden_low,
            query_word,
            query_entity,
            key_rows,
            values,
            context_grad,
            feat_q,
            feat_k,
            lse_delta,
            first_grad,
            head_low,
            slot_row,
        ],
        [
            query_ww,
            query_we,
            query_ew,
            query_ee,
            key_weight,
            value_weight,
            entity_dense,
            entity_low,
        ],
        grad_scale,
        2,
    )
    (
        table_grad,
        bias_grad,
        up_sum,
        down_sum,
        head_sum,
        out_sum,
        key_sum,
        value_sum,
        ew_sum,
        ee_sum,
        ww_sum,
        we_sum,
        dense_sum,
        *vector_out,
    ) = last_step(
        code_row,
        back_rows.reshape(-1, back_rows.shape[2]),
        table_grad,
        bias_grad,
        sums,
        (head_gain.shape[0] // devices, norm1_gain.shape[0] // devices),
        grad_scale,
    )
    return (
        total_loss[0, 0],
        layer_low,
        words_grad,
        table_grad,
        bias_grad,
        dense_sum,
        ww_sum,
        we_sum,
        ew_sum,
        ee_sum,
        key_sum,
        value_sum,
        out_sum,
        vector_out[4],
        vector_out[5],
        up_sum,
        down_sum,
        vector_out[2],
        vector_out[3],
        head_sum,
        vector_out[0],
        vector_out[1],
        losses,
    )


def solution(mesh):
    in_specs = (
        P("dp", None),
        P("dp", None),
        P("dp", None),
        P("dp", None),
        P("dp", None),
        P("dp", None),
        P("dp", None),
        P("dp"),
        P(),
        P(),
        P(),
        P(),
        P(),
        P(),
        P(),
        P(),
        P(),
        P(),
        P(),
        P(),
        P(),
        P(),
        P(),
        P(),
        P(),
        P("dp", None),
    )
    out_specs = (
        P(),
        P("dp", None),
        P("dp", None),
        P("dp", None),
        P("dp"),
        P("dp", None),
        P("dp", None),
        P("dp", None),
        P("dp", None),
        P("dp", None),
        P("dp", None),
        P("dp", None),
        P("dp", None),
        P("dp"),
        P("dp"),
        P("dp", None),
        P("dp", None),
        P("dp"),
        P("dp"),
        P("dp", None),
        P("dp"),
        P("dp"),
        P("dp"),
    )
    chosen = fused_body if mesh.shape["dp"] == 32 else body
    return jax.shard_map(chosen, mesh=mesh, in_specs=in_specs, out_specs=out_specs, check_vma=False)
```

```python
import functools

import jax
import jax.numpy as jnp
from jax import lax
from jax.experimental import pallas as pl
from jax.experimental.pallas import tpu as pltpu
from jax.sharding import PartitionSpec as P

MESH_ID = pl.DeviceIdType.MESH

HD = 64


EPSILON = 1e-05
MASKED = -1000000000.0


def dot_plain(left_side, right_side):
    return jnp.dot(left_side, right_side, preferred_element_type=jnp.float32)


def dot_left_t(left_side, right_side):
    return lax.dot_general(
        left_side, right_side, (((0,), (0,)), ((), ())), preferred_element_type=jnp.float32
    )


def dot_right_t(left_side, right_side):
    return lax.dot_general(
        left_side, right_side, (((1,), (1,)), ((), ())), preferred_element_type=jnp.float32
    )


def dot_exact(left_side, right_side):
    return jnp.dot(
        left_side, right_side, precision=lax.Precision.HIGHEST, preferred_element_type=jnp.float32
    )


def layer_norm(tensor, gain_vec, shift_vec):
    center = tensor - jnp.mean(tensor, axis=-1, keepdims=True)
    spread = jnp.mean(center * center, axis=-1, keepdims=True)
    return center * lax.rsqrt(spread + EPSILON) * gain_vec + shift_vec


def gelu_exact(tensor):
    return jax.nn.gelu(tensor, approximate=False)


def head_act(tensor, gain_vec, shift_vec):
    return layer_norm(gelu_exact(tensor), gain_vec, shift_vec)


def norm_back(tensor, gain_vec, shift_vec, grad_out):
    result, pullback = jax.vjp(layer_norm, tensor, gain_vec, shift_vec)
    return pullback(grad_out)


def attn_scores(query_word, query_entity, key_rows, allowed, word_count):
    to_words = jnp.einsum(
        "qhd,khd->hqk", query_word, key_rows[:word_count], preferred_element_type=jnp.float32
    )
    to_entities = jnp.einsum(
        "qhd,khd->hqk", query_entity, key_rows[word_count:], preferred_element_type=jnp.float32
    )
    return jnp.where(allowed[None], jnp.concatenate([to_words, to_entities], axis=2), MASKED)


def greet_all(me, devices):
    barrier = pltpu.get_barrier_semaphore()

    def greet(step, carry):
        pl.semaphore_signal(
            barrier, inc=1, device_id=(lax.rem(me + step, devices),), device_id_type=MESH_ID
        )
        return carry

    lax.fori_loop(1, devices, greet, 0)
    pl.semaphore_wait(barrier, devices - 1)


def swap_kernel(devices, gather, source, target, send_sem, recv_sem):
    me = lax.axis_index("dp")
    greet_all(me, devices)

    def piece(step):
        peer = lax.rem(me + step, devices)
        return pltpu.make_async_remote_copy(
            src_ref=source if gather else source.at[peer],
            dst_ref=target.at[me],
            send_sem=send_sem.at[step],
            recv_sem=recv_sem.at[step],
            device_id=(peer,),
            device_id_type=MESH_ID,
        )

    def begin(step, carry):
        piece(step).start()
        return carry

    def finish(step, carry):
        piece(step).wait()
        return carry

    lax.fori_loop(1, devices, begin, 0)
    target[me] = source[...] if gather else source[me]
    lax.fori_loop(1, devices, finish, 0)


def direct_swap(value, collective_id, gather=False):
    devices = lax.axis_size("dp")
    shape = (devices,) + value.shape if gather else value.shape
    return pl.pallas_call(
        functools.partial(swap_kernel, devices, gather),
        out_shape=jax.ShapeDtypeStruct(shape, value.dtype),
        in_specs=[pl.BlockSpec(memory_space=pltpu.VMEM)],
        out_specs=pl.BlockSpec(memory_space=pltpu.VMEM),
        scratch_shapes=[
            pltpu.SemaphoreType.DMA((devices,)),
            pltpu.SemaphoreType.DMA((devices,)),
        ],
        compiler_params=pltpu.CompilerParams(collective_id=collective_id, has_side_effects=True),
    )(value)


def stage_masks(devices):
    if devices == 32:
        axes = [[2], [4], [8, 16]]
    elif devices == 128:
        axes = [[2, 4], [8, 16], [32, 64]]
    else:
        axes = [[2**bit] for bit in range(1, devices.bit_length() - 1)]
        axes = axes + [[] for _ in range(3 - len(axes))]
    first, second, third = axes[0], axes[1], sum(axes[2:], [])
    return (
        [1] + first + second + third,
        [1] + second + first + third,
        [1] + third + first + second,
    )


def sum_kernel(masks, rows, *refs):
    parts = len(masks)
    stages = len(masks[0])
    sources, results = refs[:parts], refs[parts : 2 * parts]
    landing = refs[2 * parts : 3 * parts]
    send_sem, recv_sem = refs[3 * parts :]
    me = lax.axis_index("dp")
    barrier = pltpu.get_barrier_semaphore()
    partner_of = {}
    for mask in masks[0]:
        bit = lax.rem(lax.div(me, mask), 2)
        partner_of[mask] = (me + mask - 2 * mask * bit, bit)
    for mask in masks[0]:
        pl.semaphore_signal(
            barrier, inc=1, device_id=(partner_of[mask][0],), device_id_type=MESH_ID
        )
    pl.semaphore_wait(barrier, stages)
    sizes = [[rows[part] * 2 ** (stages - 1 - stage) for stage in range(stages)] for part in range(parts)]
    places = [[sum(size[:stage]) for stage in range(stages)] for size in sizes]

    def launch(part, stage):
        partner, bit = partner_of[masks[part][stage]]
        size = sizes[part][stage]
        away = (1 - bit) * size
        copy = pltpu.make_async_remote_copy(
            src_ref=sources[part].at[pl.ds(away, size)]
            if stage == 0
            else landing[part].at[pl.ds(places[part][stage - 1] + away, size)],
            dst_ref=landing[part].at[pl.ds(places[part][stage], size)],
            send_sem=send_sem.at[part, stage],
            recv_sem=recv_sem.at[part, stage],
            device_id=(partner,),
            device_id_type=MESH_ID,
        )
        copy.start()
        return copy

    flying = [launch(part, 0) for part in range(parts)]

    def add_rows(part, stage, start, count):
        keep = partner_of[masks[part][stage]][1] * sizes[part][stage] + start
        last = stage == stages - 1

        def step(index, carry):
            theirs = pl.ds(pl.multiple_of(places[part][stage] + start + index * 16, 16), 16)
            if stage == 0:
                mine = sources[part][pl.ds(pl.multiple_of(keep + index * 16, 16), 16)]
            else:
                mine = landing[part][
                    pl.ds(pl.multiple_of(places[part][stage - 1] + keep + index * 16, 16), 16)
                ]
            total = mine.astype(jnp.float32) + landing[part][theirs].astype(jnp.float32)
            if last:
                results[part][pl.ds(pl.multiple_of(index * 16, 16), 16)] = total
            else:
                landing[part][theirs] = total.astype(jnp.bfloat16)
            return carry

        lax.fori_loop(0, count // 16, step, 0, unroll=min(4, count // 16))

    for stage in range(stages):
        for part in range(parts):
            flying[part].wait()
            if stage == stages - 1:
                add_rows(part, stage, 0, sizes[part][stage])
                continue
            bit = partner_of[masks[part][stage + 1]][1]
            half = sizes[part][stage] // 2
            add_rows(part, stage, (1 - bit) * half, half)
            flying[part] = launch(part, stage + 1)
            add_rows(part, stage, bit * half, half)


def sum_scatter(parts, collective_id):
    devices = lax.axis_size("dp")
    masks = stage_masks(devices)
    rows = [part.shape[1] for part in parts]
    width = parts[0].shape[2]
    bits = devices.bit_length() - 1
    ordered = []
    for part, order in zip(parts, masks):
        view = part.reshape((2,) * bits + part.shape[1:])
        places = [bits - mask.bit_length() for mask in order]
        view = view.transpose(tuple(places) + (bits, bits + 1))
        ordered.append(view.reshape(devices * part.shape[1], width))
    return pl.pallas_call(
        functools.partial(sum_kernel, masks, rows),
        out_shape=[jax.ShapeDtypeStruct((count, width), jnp.float32) for count in rows],
        in_specs=[pl.BlockSpec(memory_space=pltpu.VMEM)] * len(parts),
        out_specs=[pl.BlockSpec(memory_space=pltpu.VMEM)] * len(parts),
        scratch_shapes=[pltpu.VMEM((devices * count, width), jnp.bfloat16) for count in rows]
        + [pltpu.SemaphoreType.DMA((len(parts), bits)), pltpu.SemaphoreType.DMA((len(parts), bits))],
        input_output_aliases={},
        compiler_params=pltpu.CompilerParams(
            collective_id=collective_id, has_side_effects=True, vmem_limit_bytes=56 * 2**20
        ),
    )(*ordered)


def by_owner(grad, width):
    devices = lax.axis_size("dp")
    rows = grad.shape[0] // devices
    blocks = grad.astype(jnp.bfloat16).reshape(devices, rows, grad.shape[1])
    if grad.shape[1] > width:
        cuts = grad.shape[1] // width
        return jnp.concatenate(jnp.split(blocks, cuts, axis=2), axis=1)
    if grad.shape[1] < width:
        return blocks.reshape(devices, rows * grad.shape[1] // width, width)
    return blocks


def from_owner(rows, shape):
    devices = lax.axis_size("dp")
    count, width = shape[0] // devices, shape[1]
    if width > rows.shape[1]:
        return jnp.concatenate(jnp.split(rows, width // rows.shape[1], axis=0), axis=1)
    return rows.reshape(count, width)


def sum_all(groups, collective_id):
    width = groups[0][0].shape[1]
    width = min(grad.shape[1] for group in groups for grad in group if grad.shape[1] >= 768)
    devices = lax.axis_size("dp")
    packed = []
    for group in groups:
        pieces = [by_owner(grad, width) for grad in group]
        count = sum(piece.shape[1] for piece in pieces)
        room = -(-count // 16) * 16 - count
        if room:
            pieces.append(jnp.zeros((devices, room, width), jnp.bfloat16))
        packed.append(jnp.concatenate(pieces, axis=1))
    sums = sum_scatter(packed, collective_id)
    results = []
    for group, total in zip(groups, sums):
        place, outs = 0, []
        for grad in group:
            count = grad.shape[0] // devices * grad.shape[1] // width
            outs.append(from_owner(total[place : place + count], grad.shape))
            place += count
        results.append(outs)
    return results


def body(
    word_states,
    word_segments,
    entity_segments,
    request_rows,
    request_slot,
    mask_slots,
    entity_table,
    vocab_bias,
    entity_dense,
    query_ww,
    query_we,
    query_ew,
    query_ee,
    key_weight,
    value_weight,
    out_weight,
    norm1_gain,
    norm1_bias,
    up_weight,
    down_weight,
    norm2_gain,
    norm2_bias,
    head_weight,
    head_gain,
    head_bias,
    cotangent,
):
    word_count = word_states.shape[0]
    model_width = word_states.shape[1]
    slot_count = entity_segments.shape[1]
    mask_count = mask_slots.shape[1]
    request_count = slot_count + mask_count
    seq_len = word_count + slot_count
    devices = lax.axis_size("dp")
    capacity = request_rows.shape[1]
    head_count = model_width // HD
    query_scale = HD ** (-0.5)
    emb_width = entity_table.shape[1]
    table_rows = entity_table.shape[0]
    total_mask = mask_count * devices
    grad_scale = 1.0 / total_mask
    id_block = jnp.pad(request_rows[:, None, :], ((0, 0), (0, 7), (0, 128 - capacity)))
    asked_ids = direct_swap(id_block, 0)[:, 0, :capacity]
    found_rows = jnp.take(entity_table, asked_ids, axis=0)
    found_bias = jnp.take(vocab_bias, asked_ids, axis=0)
    cap_room = -(-capacity // 16) * 16 - capacity
    found_all = jnp.concatenate(
        [found_rows, jnp.broadcast_to(found_bias[:, :, None], found_bias.shape + (128,))], axis=2
    )
    back_all = direct_swap(jnp.pad(found_all, ((0, 0), (0, cap_room), (0, 0))), 1)
    back_rows = back_all[:, :capacity, :emb_width]
    back_bias = back_all[:, :capacity, emb_width]
    got_rows = back_rows
    got_bias = back_bias
    slot_ids = request_slot.reshape(devices * capacity)
    placing = slot_ids[None, :] == jnp.arange(request_count, dtype=jnp.int32)[:, None]
    placing_low = placing.astype(jnp.bfloat16)
    request_vecs = dot_plain(placing_low, got_rows.reshape(devices * capacity, emb_width))
    request_bias = dot_plain(placing_low, got_bias.reshape(devices * capacity, 1))[:, 0]
    entity_low = request_vecs[:slot_count].astype(jnp.bfloat16)
    target_vecs = request_vecs[slot_count:]
    target_bias = request_bias[slot_count:]
    entity_states = dot_plain(entity_low, entity_dense)
    hidden = jnp.concatenate([word_states.astype(jnp.float32), entity_states], axis=0)
    hidden_low = hidden.astype(jnp.bfloat16)
    word_part = hidden_low[:word_count]
    entity_part = hidden_low[word_count:]
    query_word = (
        query_scale
        * jnp.concatenate(
            [dot_plain(word_part, query_ww), dot_plain(entity_part, query_ew)], axis=0
        )
    ).astype(jnp.bfloat16)
    query_entity = (
        query_scale
        * jnp.concatenate(
            [dot_plain(word_part, query_we), dot_plain(entity_part, query_ee)], axis=0
        )
    ).astype(jnp.bfloat16)
    key_rows = dot_plain(hidden_low, key_weight).astype(jnp.bfloat16)
    values = dot_plain(hidden_low, value_weight).astype(jnp.bfloat16)
    head_shape = (seq_len, head_count, HD)
    query_word_h = query_word.reshape(head_shape)
    query_entity_h = query_entity.reshape(head_shape)
    key_rows_h = key_rows.reshape(head_shape)
    values_h = values.reshape(head_shape)
    segment_row = jnp.concatenate([word_segments[0], entity_segments[0]])
    allowed = segment_row[:, None] == segment_row[None, :]
    scores = attn_scores(query_word_h, query_entity_h, key_rows_h, allowed, word_count)
    row_top = jnp.max(scores, axis=2, keepdims=True)
    exp_scores = jnp.exp(scores - row_top)
    row_total = jnp.sum(exp_scores, axis=2, keepdims=True)
    attn_low = (exp_scores / row_total).astype(jnp.bfloat16)
    row_lse = row_top + jnp.log(row_total)
    context = jnp.einsum("hqk,khd->qhd", attn_low, values_h, preferred_element_type=jnp.float32)
    context_low = context.reshape(seq_len, model_width).astype(jnp.bfloat16)
    attended = dot_plain(context_low, out_weight)
    residual_one = hidden + attended
    normed = layer_norm(residual_one, norm1_gain, norm1_bias)
    normed_low = normed.astype(jnp.bfloat16)
    up_value = dot_plain(normed_low, up_weight)
    activated = gelu_exact(up_value).astype(jnp.bfloat16)
    down_value = dot_plain(activated, down_weight)
    residual_two = normed + down_value
    layer_out = layer_norm(residual_two, norm2_gain, norm2_bias)
    choose = (mask_slots[0][:, None] == jnp.arange(slot_count, dtype=jnp.int32)[None, :]).astype(
        jnp.float32
    )
    picked_low = dot_exact(choose, layer_out[word_count:]).astype(jnp.bfloat16)
    head_pre = dot_plain(picked_low, head_weight)
    head_low = head_act(head_pre, head_gain, head_bias).astype(jnp.bfloat16)
    head_f32 = head_low.astype(jnp.float32)
    target_logit = jnp.sum(head_f32 * target_vecs, axis=1) + target_bias
    all_heads = direct_swap(head_low, 2, gather=True).reshape(total_mask, emb_width)
    block_rows = min(512, total_mask)
    block_count = total_mask // block_rows
    bias_f32 = vocab_bias.astype(jnp.float32)

    def block_logits(block_index):
        row_block = lax.dynamic_slice_in_dim(all_heads, block_index * block_rows, block_rows, 0)
        return (row_block, dot_right_t(row_block, entity_table) + bias_f32[None, :])

    def block_stats(block_index):
        row_block, logits = block_logits(block_index)
        top_value = jnp.max(logits, axis=1)
        return (top_value, jnp.sum(jnp.exp(logits - top_value[:, None]), axis=1))

    local_top, local_total = lax.map(block_stats, jnp.arange(block_count, dtype=jnp.int32))
    local_top = local_top.reshape(total_mask)
    local_total = local_total.reshape(total_mask)
    target_sum = jnp.sum(target_logit)
    stats = jnp.concatenate(
        [
            local_top.reshape(total_mask // 128, 128),
            local_total.reshape(total_mask // 128, 128),
            jnp.full((8, 128), target_sum),
        ],
        axis=0,
    )
    all_stats = direct_swap(stats, 3, gather=True)
    all_tops = all_stats[:, : total_mask // 128].reshape(devices, total_mask)
    all_totals = all_stats[:, total_mask // 128 : total_mask // 64].reshape(devices, total_mask)
    target_total = jnp.sum(all_stats[:, total_mask // 64, 0])
    global_top = jnp.max(all_tops, axis=0)
    global_total = jnp.sum(all_totals * jnp.exp(all_tops - global_top[None, :]), axis=0)
    lse_all = global_top + jnp.log(global_total)
    loss_value = (jnp.sum(lse_all) - target_total) * grad_scale
    own_lse = lax.dynamic_slice_in_dim(lse_all, lax.axis_index("dp") * mask_count, mask_count, 0)
    mask_loss = own_lse - target_logit

    def block_back(running, block_index):
        table_grad, bias_grad = running
        row_block, logits = block_logits(block_index)
        lse_block = lax.dynamic_slice_in_dim(lse_all, block_index * block_rows, block_rows, 0)
        logit_grad = (jnp.exp(logits - lse_block[:, None]) * grad_scale).astype(jnp.bfloat16)
        table_grad = table_grad + dot_left_t(logit_grad, row_block)
        bias_grad = bias_grad + jnp.sum(logit_grad.astype(jnp.float32), axis=0)
        return ((table_grad, bias_grad), dot_plain(logit_grad, entity_table))

    start_grads = (
        jnp.zeros((table_rows, emb_width), jnp.float32),
        jnp.zeros((table_rows,), jnp.float32),
    )
    (table_grad, bias_grad), head_terms = lax.scan(
        block_back, start_grads, jnp.arange(block_count, dtype=jnp.int32)
    )
    head_parts = direct_swap(head_terms.reshape(devices, mask_count, emb_width), 4)
    head_grad = jnp.sum(head_parts, axis=0)
    head_grad = head_grad - grad_scale * target_vecs
    target_grad = -grad_scale * head_f32
    pre_grad, head_gain_grad, head_bias_grad = jax.vjp(head_act, head_pre, head_gain, head_bias)[1](
        head_grad
    )
    pre_low = pre_grad.astype(jnp.bfloat16)
    head_weight_grad = dot_left_t(picked_low, pre_low)
    picked_grad = dot_right_t(pre_low, head_weight)
    out_grad = cotangent.astype(jnp.float32) + jnp.concatenate(
        [jnp.zeros((word_count, model_width), jnp.float32), dot_exact(choose.T, picked_grad)],
        axis=0,
    )
    resid_grad, norm2_gain_grad, norm2_bias_grad = norm_back(
        residual_two, norm2_gain, norm2_bias, out_grad
    )
    down_in = resid_grad.astype(jnp.bfloat16)
    down_grad = dot_left_t(activated, down_in)
    act_grad = dot_right_t(down_in, down_weight)
    up_grad = jax.vjp(gelu_exact, up_value)[1](act_grad)[0]
    up_low = up_grad.astype(jnp.bfloat16)
    up_weight_grad = dot_left_t(normed_low, up_low)
    normed_grad = resid_grad + dot_right_t(up_low, up_weight)
    first_grad, norm1_gain_grad, norm1_bias_grad = norm_back(
        residual_one, norm1_gain, norm1_bias, normed_grad
    )
    attn_in = first_grad.astype(jnp.bfloat16)
    out_weight_grad = dot_left_t(context_low, attn_in)
    context_grad = dot_right_t(attn_in, out_weight).astype(jnp.bfloat16).reshape(head_shape)
    scores_again = attn_scores(query_word_h, query_entity_h, key_rows_h, allowed, word_count)
    attn_prob = jnp.exp(scores_again - row_lse)
    prob_low = attn_prob.astype(jnp.bfloat16)
    prob_grad = jnp.einsum(
        "qhd,khd->hqk", context_grad, values_h, preferred_element_type=jnp.float32
    )
    values_grad = jnp.einsum(
        "hqk,qhd->khd", prob_low, context_grad, preferred_element_type=jnp.float32
    )
    values_grad = values_grad.reshape(seq_len, model_width).astype(jnp.bfloat16)
    row_delta = jnp.sum(attn_prob * prob_grad, axis=2, keepdims=True)
    score_grad = (attn_prob * (prob_grad - row_delta)).astype(jnp.bfloat16)
    qword_grad = jnp.einsum(
        "hqk,khd->qhd",
        score_grad[:, :, :word_count],
        key_rows_h[:word_count],
        preferred_element_type=jnp.float32,
    )
    qword_grad = qword_grad.reshape(seq_len, model_width).astype(jnp.bfloat16)
    qent_grad = jnp.einsum(
        "hqk,khd->qhd",
        score_grad[:, :, word_count:],
        key_rows_h[word_count:],
        preferred_element_type=jnp.float32,
    )
    qent_grad = qent_grad.reshape(seq_len, model_width).astype(jnp.bfloat16)
    keys_grad = jnp.concatenate(
        [
            jnp.einsum(
                "hqk,qhd->khd",
                score_grad[:, :, :word_count],
                query_word_h,
                preferred_element_type=jnp.float32,
            ),
            jnp.einsum(
                "hqk,qhd->khd",
                score_grad[:, :, word_count:],
                query_entity_h,
                preferred_element_type=jnp.float32,
            ),
        ],
        axis=0,
    )
    keys_grad = keys_grad.reshape(seq_len, model_width).astype(jnp.bfloat16)
    query_ww_grad = query_scale * dot_left_t(word_part, qword_grad[:word_count])
    query_ew_grad = query_scale * dot_left_t(entity_part, qword_grad[word_count:])
    query_we_grad = query_scale * dot_left_t(word_part, qent_grad[:word_count])
    query_ee_grad = query_scale * dot_left_t(entity_part, qent_grad[word_count:])
    key_weight_grad = dot_left_t(hidden_low, keys_grad)
    value_weight_grad = dot_left_t(hidden_low, values_grad)
    word_back = query_scale * (
        dot_right_t(qword_grad[:word_count], query_ww)
        + dot_right_t(qent_grad[:word_count], query_we)
    )
    entity_back = query_scale * (
        dot_right_t(qword_grad[word_count:], query_ew)
        + dot_right_t(qent_grad[word_count:], query_ee)
    )
    hidden_grad = (
        first_grad
        + jnp.concatenate([word_back, entity_back], axis=0)
        + dot_right_t(keys_grad, key_weight)
        + dot_right_t(values_grad, value_weight)
    )
    words_grad = hidden_grad[:word_count].astype(jnp.bfloat16)
    state_low = hidden_grad[word_count:].astype(jnp.bfloat16)
    dense_grad = dot_left_t(entity_low, state_low)
    entity_vec_grad = dot_right_t(state_low, entity_dense)
    vec_grad = jnp.concatenate([entity_vec_grad, target_grad], axis=0)
    bias_vec_grad = jnp.concatenate(
        [jnp.zeros((slot_count,), jnp.float32), jnp.full((mask_count,), -grad_scale, jnp.float32)]
    )
    placing_f32 = placing.astype(jnp.float32)
    per_request = dot_exact(placing_f32.T, vec_grad)
    bias_request = dot_exact(placing_f32.T, bias_vec_grad[:, None])[:, 0]
    back_block = jnp.concatenate(
        [
            per_request.reshape(devices, capacity, emb_width).astype(jnp.bfloat16),
            jnp.broadcast_to(
                bias_request.reshape(devices, capacity, 1).astype(jnp.bfloat16),
                (devices, capacity, 128),
            ),
        ],
        axis=2,
    )
    back_block = direct_swap(jnp.pad(back_block, ((0, 0), (0, cap_room), (0, 0))), 5)
    back_rows = back_block[:, :capacity, :emb_width].astype(jnp.float32)
    back_bias = back_block[:, :capacity, emb_width].astype(jnp.float32)
    flat_ids = asked_ids.reshape(devices * capacity)
    table_grad = table_grad + jax.ops.segment_sum(
        back_rows.reshape(devices * capacity, emb_width), flat_ids, num_segments=table_rows
    )
    bias_grad = bias_grad + jax.ops.segment_sum(
        back_bias.reshape(devices * capacity), flat_ids, num_segments=table_rows
    )
    vectors = [
        head_gain_grad,
        head_bias_grad,
        norm2_gain_grad,
        norm2_bias_grad,
        norm1_gain_grad,
        norm1_bias_grad,
    ]
    cuts = [vector.reshape(devices, -1) for vector in vectors]
    spots = [0]
    for cut in cuts:
        spots.append(spots[-1] + cut.shape[1])
    block = jnp.concatenate(cuts, axis=1)
    block = jnp.pad(block, ((0, 0), (0, 128 - spots[-1])))[:, None, :]
    vector_sums = jnp.sum(direct_swap(jnp.pad(block, ((0, 0), (0, 7), (0, 0))), 6)[:, 0], axis=0)
    vector_out = [vector_sums[spots[i] : spots[i + 1]] for i in range(len(cuts))]
    sums = sum_all(
        [
            [up_weight_grad, out_weight_grad, head_weight_grad],
            [down_grad, query_ww_grad, dense_grad],
            [query_we_grad, query_ew_grad, query_ee_grad, key_weight_grad, value_weight_grad],
        ],
        7,
    )
    all_sums = (
        sums[0][2],
        vector_out[0],
        vector_out[1],
        vector_out[2],
        vector_out[3],
        sums[0][0],
        sums[1][0],
        vector_out[4],
        vector_out[5],
        sums[0][1],
        sums[1][1],
        sums[2][0],
        sums[2][1],
        sums[2][2],
        sums[2][3],
        sums[2][4],
        sums[1][2],
    )
    return (
        loss_value,
        layer_out.astype(jnp.bfloat16),
        words_grad,
        table_grad,
        bias_grad,
        all_sums[16],
        all_sums[10],
        all_sums[11],
        all_sums[12],
        all_sums[13],
        all_sums[14],
        all_sums[15],
        all_sums[9],
        all_sums[7],
        all_sums[8],
        all_sums[5],
        all_sums[6],
        all_sums[3],
        all_sums[4],
        all_sums[0],
        all_sums[1],
        all_sums[2],
        mask_loss,
    )


class Stage:
    def __init__(self, loads, stores):
        self.loads, self.stores, self.waited, self.sent = loads, stores, set(), []

    def need(self, *indices):
        for index in indices:
            if index not in self.waited:
                self.waited.add(index)
                self.loads[index].wait()

    def send(self, *indices):
        for index in indices:
            self.sent.append(index)
            self.stores[index].start()

    def finish(self):
        self.need(*self.loads)
        self.send(*[index for index in self.stores if index not in self.sent])
        for copy in self.stores.values():
            copy.wait()


def staged_kernel(inner, counts, far_in, far_out, *refs):
    ins, outs = list(refs[: counts[0]]), list(refs[counts[0] : sum(counts)])
    rest = list(refs[sum(counts) :])
    out_sem, in_sem = rest.pop(), rest.pop()
    near = rest[len(rest) - len(far_in) - len(far_out) :]
    rest = rest[: len(rest) - len(near)]
    loads, stores = {}, {}
    for slot, index in enumerate(far_in):
        loads[index] = pltpu.make_async_copy(ins[index], near[slot], in_sem.at[slot])
        ins[index] = near[slot]
        loads[index].start()
    for slot, index in enumerate(far_out):
        close = near[len(far_in) + slot]
        stores[index] = pltpu.make_async_copy(close, outs[index], out_sem.at[slot])
        outs[index] = close
    stage = Stage(loads, stores)
    inner(stage, *ins, *outs, *rest)
    stage.finish()


def staged_call(inner, inputs, outs, in_specs, out_specs, far_in, far_out, scratch, params):
    hbm = pl.BlockSpec(memory_space=pltpu.HBM)
    in_specs, out_specs = list(in_specs), list(out_specs)
    extra = []
    for index in far_in:
        in_specs[index] = hbm
        extra.append(pltpu.VMEM(inputs[index].shape, inputs[index].dtype))
    for index in far_out:
        out_specs[index] = hbm
        extra.append(pltpu.VMEM(outs[index].shape, outs[index].dtype))
    return pl.pallas_call(
        functools.partial(staged_kernel, inner, (len(inputs), len(outs)), far_in, far_out),
        out_shape=outs,
        in_specs=in_specs,
        out_specs=out_specs,
        scratch_shapes=list(scratch)
        + extra
        + [
            pltpu.SemaphoreType.DMA((max(1, len(far_in)),)),
            pltpu.SemaphoreType.DMA((max(1, len(far_out)),)),
        ],
        compiler_params=params,
    )(*inputs)


def all_pairs(source, target, sems, me, devices):
    def piece(step):
        peer = lax.rem(me + step, devices)
        return pltpu.make_async_remote_copy(
            src_ref=source.at[peer],
            dst_ref=target.at[me],
            send_sem=sems.at[0, step],
            recv_sem=sems.at[1, step],
            device_id=(peer,),
            device_id_type=MESH_ID,
        )

    def begin(step, carry):
        piece(step).start()
        return carry

    def finish(step, carry):
        piece(step).wait()
        return carry

    lax.fori_loop(1, devices, begin, 0)
    target[me] = source[me]
    return lambda: lax.fori_loop(1, devices, finish, 0)


def lookup_kernel(
    stage,
    request_rows,
    table,
    bias,
    request_slot,
    word_states,
    w_ww,
    w_we,
    w_key,
    w_value,
    word_seg,
    entity_seg,
    mask_slots,
    entity_out,
    vec_out,
    bias_out,
    code_out,
    qword,
    qent,
    keys,
    values,
    feat_q,
    feat_k,
    choose,
    slot_out,
    code_send,
    code_pad,
    slot_pad,
    codes_in,
    found,
    rows_in,
    bias_col,
    sems,
):
    devices, room, _ = found.shape
    me = lax.axis_index("dp")
    rows, wide = table.shape
    entries = devices * room
    slots, masked = entity_out.shape[0], vec_out.shape[0]
    slot = request_slot[...]
    code = request_rows[...] + jnp.where(slot >= slots, rows, 0)
    code = jnp.where(slot < slots + masked, code, -1)
    capacity = slot.shape[0]
    code_pad[...] = jnp.full(code_pad.shape, -1, jnp.int32).astype(jnp.float32)
    code_pad[0:capacity] = code.astype(jnp.float32)
    sent = code_pad[...].T.astype(jnp.int32)
    for owner in range(devices):
        code_send[owner] = sent[owner : owner + 1]
    slot_pad[...] = jnp.full(slot_pad.shape, slots + masked, jnp.int32).astype(jnp.float32)
    slot_pad[0:capacity] = slot.astype(jnp.float32)
    greet_all(me, devices)

    def in_column(turned):
        return jnp.concatenate(
            [
                jnp.broadcast_to(turned[0:room, one : one + 1], (room, 128))
                for one in range(devices)
            ],
            axis=0,
        )

    def in_row(column, target):
        for begin in range(0, entries, 128):
            turned = column[begin : begin + 128].T
            target[:, begin : begin + 128] = turned[0:8].astype(jnp.int32)

    ended = all_pairs(code_send, codes_in, sems.at[0], me, devices)
    width = word_states.shape[1]
    half = width // 2
    query_scale = HD ** (-0.5)

    def project(target, weight, scale):
        for cut in range(0, width, half):
            value = dot_plain(word_states[...], weight[:, cut : cut + half])
            if scale:
                value = value * query_scale
            target[:, cut : cut + half] = value.astype(jnp.bfloat16)

    def bias_step(index, carry):
        at = pl.ds(pl.multiple_of(index * 128, 128), 128)
        bias_col[at] = jnp.broadcast_to(bias[at].reshape(1, 128), (128, 128)).T.astype(jnp.bfloat16)
        return carry

    lax.fori_loop(0, rows // 128, bias_step, 0)
    words = word_seg.shape[1]
    column = lax.rem(lax.broadcasted_iota(jnp.int32, (128, 128), 1), HD)
    for begin in range(0, words + entity_seg.shape[1], 128):
        seg = word_seg[:, begin : begin + 128] if begin < words else entity_seg[...]
        turned = jnp.broadcast_to(seg.astype(jnp.float32), (128, 128)).T
        same = turned == column.astype(jnp.float32)
        at = slice(begin, begin + 128)
        feat_q[at] = same.astype(jnp.float32).astype(jnp.bfloat16)
        feat_k[at] = jnp.where(same | (column >= 4), 0.0, MASKED).astype(jnp.bfloat16)
    turned = jnp.broadcast_to(mask_slots[...].astype(jnp.float32), (128, masked)).T
    lanes = lax.broadcasted_iota(jnp.int32, (masked, 128), 1).astype(jnp.float32)
    choose[...] = (turned == lanes).astype(jnp.float32).astype(jnp.bfloat16)
    stage.need(4, 5)
    project(qword, w_ww, True)
    stage.send(4)
    stage.need(1)
    ended()
    code = in_column(
        jnp.concatenate([codes_in[one] for one in range(devices)], axis=0).astype(jnp.float32).T
    )
    in_row(code, code_out)
    code = code.astype(jnp.int32)
    code = jnp.where(code >= rows, code - rows, code)
    lane = lax.broadcasted_iota(jnp.int32, (entries, 128), 1)
    total = jnp.zeros((entries, wide), jnp.float32)
    shift = jnp.zeros((entries, 128), jnp.float32)
    step = 512
    for begin in range(0, rows, step):
        size = min(step, rows - begin)
        match = jnp.concatenate(
            [
                (code - (begin + inner) == lane).astype(jnp.float32)
                for inner in range(0, size, 128)
            ],
            axis=1,
        ).astype(jnp.bfloat16)
        total += dot_plain(match, table[begin : begin + size])
        shift += dot_plain(match, bias_col[begin : begin + size])
    both = jnp.concatenate([total, shift], axis=1).astype(jnp.bfloat16)
    found[...] = both.reshape(found.shape)
    ended = all_pairs(found, rows_in, sems.at[1], me, devices)
    in_row(in_column(slot_pad[...]), slot_out)
    stage.need(6)
    project(qent, w_we, True)
    stage.send(5)
    stage.need(7)
    project(keys, w_key, False)
    stage.send(6)
    stage.need(8)
    project(values, w_value, False)
    stage.send(7)
    ended()
    wanted = lax.broadcasted_iota(jnp.int32, (slots + masked, entries), 0)
    placing = (wanted == slot_out[0:1]).astype(jnp.float32).astype(jnp.bfloat16)
    placed = dot_plain(placing, rows_in[...].reshape(entries, wide + 128))
    entity_out[...] = placed[:slots, :wide].astype(jnp.bfloat16)
    vec_out[...] = placed[slots:, :wide]
    bias_out[...] = placed[slots:, wide:]


def lookup(inputs, slots, masked, collective_id):
    capacity, devices = inputs[0].shape
    room = -(-capacity // 16) * 16
    rows, wide = inputs[1].shape
    words, width = inputs[4].shape
    entries = devices * room
    low = jnp.bfloat16
    vmem = pl.BlockSpec(memory_space=pltpu.VMEM)
    outs = [
        jax.ShapeDtypeStruct((slots, wide), low),
        jax.ShapeDtypeStruct((masked, wide), jnp.float32),
        jax.ShapeDtypeStruct((masked, 128), jnp.float32),
        jax.ShapeDtypeStruct((8, entries), jnp.int32),
    ]
    outs += [jax.ShapeDtypeStruct((words, width), low)] * 4
    outs += [jax.ShapeDtypeStruct((words + slots, 128), low)] * 2
    outs += [jax.ShapeDtypeStruct((masked, slots), low)]
    outs += [jax.ShapeDtypeStruct((8, entries), jnp.int32)]
    return staged_call(
        lookup_kernel,
        inputs,
        outs,
        [vmem] * len(inputs),
        [vmem] * len(outs),
        (4, 5, 1, 6, 7, 8),
        (4, 5, 6, 7),
        [
            pltpu.VMEM((devices, 1, 128), jnp.int32),
            pltpu.VMEM((128, devices), jnp.float32),
            pltpu.VMEM((room, devices), jnp.float32),
            pltpu.VMEM((devices, 1, 128), jnp.int32),
            pltpu.VMEM((devices, room, wide + 128), low),
            pltpu.VMEM((devices, room, wide + 128), low),
            pltpu.VMEM((rows, 128), low),
            pltpu.SemaphoreType.DMA((2, 2, devices)),
        ],
        pltpu.CompilerParams(
            collective_id=collective_id, has_side_effects=True, vmem_limit_bytes=63 * 2**20
        ),
    )


def norm_parts(value):
    center = value - jnp.mean(value, axis=-1, keepdims=True)
    spread = jnp.mean(center * center, axis=-1, keepdims=True)
    rate = lax.rsqrt(spread + EPSILON)
    return center * rate, rate


def gelu_parts(value):
    chance = 0.5 + 0.5 * lax.erf(value * (0.5**0.5))
    slope = chance + value * (jnp.exp(-0.5 * value * value) * (0.5 / jnp.pi) ** 0.5)
    return value * chance, slope


def half_lanes(block):
    lane = lax.broadcasted_iota(jnp.int32, (1, block), 1)
    low_half = (lane < HD).astype(jnp.float32).astype(jnp.bfloat16)
    high_half = (lane >= HD).astype(jnp.float32).astype(jnp.bfloat16)
    return low_half, high_half


def forward_kernel(
    stage,
    word_states,
    entity_low,
    feat_q,
    feat_k,
    choose,
    dense,
    word_q,
    word_e,
    word_k,
    word_v,
    w_ew,
    w_ee,
    w_key,
    w_value,
    out_hbm,
    gain_one,
    shift_one,
    up_hbm,
    down_hbm,
    gain_two,
    shift_two,
    head_w,
    gain_head,
    shift_head,
    hidden,
    qword,
    qent,
    keys,
    values,
    context,
    lse_out,
    resid_one,
    normed_out,
    active_hbm,
    slope_hbm,
    resid_two,
    layer_low,
    picked_out,
    head_pre_out,
    head_out,
    state_scr,
    normed_scr,
    out_w,
    up_w,
    down_w,
    active,
    slope,
    sems,
):
    loads = [
        pltpu.make_async_copy(source, target, sems.at[index])
        for index, (source, target) in enumerate(
            ((out_hbm, out_w), (up_hbm, up_w), (down_hbm, down_w))
        )
    ]
    words, width = word_states.shape
    word_loads = [
        pltpu.make_async_copy(source, target.at[pl.ds(0, words)], sems.at[12 + index])
        for index, (source, target) in enumerate(
            ((word_q, qword), (word_e, qent), (word_k, keys), (word_v, values))
        )
    ]
    for load in word_loads + loads:
        load.start()
    stage.need(0, 1, 5)
    seq_len = hidden.shape[0]
    slots = seq_len - words
    block = 128
    tall = seq_len
    halves = half_lanes(block)
    query_scale = HD ** (-0.5)
    state_scr[...] = dot_plain(entity_low[...], dense[...])
    hidden[:words] = word_states[...]
    hidden[words:] = state_scr[...].astype(jnp.bfloat16)

    stage.send(0)
    ents = hidden[words:]
    stage.need(10, 11, 12, 13)
    for target, weight, scale in (
        (qword, w_ew, query_scale),
        (qent, w_ee, query_scale),
        (keys, w_key, None),
        (values, w_value, None),
    ):
        value = dot_plain(ents, weight[...])
        if scale is not None:
            value = value * scale
        target[words:] = value.astype(jnp.bfloat16)
    for load in word_loads:
        load.wait()
    stage.send(1, 2, 3, 4)
    stage.need(2, 3)
    lse_out[...] = jnp.zeros_like(lse_out)

    def pair_step(pair, carry):
        lanes = pl.ds(pl.multiple_of(pair * block, block), block)
        key_pair = keys[:, lanes]
        value_pair = values[:, lanes]
        key_feat = [key_pair * halves[h] + feat_k[...] * halves[1 - h] for h in range(2)]
        value_only = [value_pair * halves[h] for h in range(2)]
        spot = lax.broadcasted_iota(jnp.int32, (1, block), 1) - 4 * pair

        def row_step(index, inner):
            at = pl.ds(pl.multiple_of(index * tall, block), tall)
            qw = qword[at, lanes]
            qe = qent[at, lanes]
            feats = feat_q[at]
            result = jnp.zeros((tall, block), jnp.float32)
            stats = lse_out[at]
            for h in range(2):
                left_w = qw * halves[h] + feats * halves[1 - h]
                left_e = qe * halves[h] + feats * halves[1 - h]
                scores = jnp.concatenate(
                    [
                        dot_right_t(left_w, key_feat[h][:words]),
                        dot_right_t(left_e, key_feat[h][words:]),
                    ],
                    axis=1,
                )
                top = jnp.max(scores, axis=1, keepdims=True)
                expo = jnp.exp(scores - top)
                total = jnp.sum(expo, axis=1, keepdims=True)
                prob = (expo * (1.0 / total)).astype(jnp.bfloat16)
                result += dot_plain(prob, value_only[h])
                stats = jnp.where(spot == h, top + jnp.log(total), stats)
            context[at, lanes] = result.astype(jnp.bfloat16)
            lse_out[at] = stats
            return inner

        lax.fori_loop(0, seq_len // tall, row_step, 0)
        return carry

    lax.fori_loop(0, width // block, pair_step, 0)

    stage.send(5)
    loads[0].wait()
    for begin, size in ((0, words // 2), (words // 2, words // 2), (words, slots)):
        at = slice(begin, begin + size)
        start = (
            state_scr[...] if begin == words else word_states[at].astype(jnp.float32)
        )
        value = start + dot_plain(context[at], out_w[...])
        resid_one[at] = value
        normed = norm_parts(value)[0] * gain_one[...][None, :] + shift_one[...][None, :]
        normed_scr[at] = normed
        normed_out[at] = normed.astype(jnp.bfloat16)
    stage.send(7, 8)
    loads[1].wait()
    loads[2].wait()
    span = seq_len
    stores = []

    for slot in range(down_w.shape[0] // width):
        cols = slice(slot * width, slot * width + width)

        def up_step(index, carry, cols=cols):
            at = pl.ds(pl.multiple_of(index * span, 16), span)
            result, change = gelu_parts(dot_plain(normed_out[at], up_w[:, cols]))
            active[at, cols] = result.astype(jnp.bfloat16)
            slope[at, cols] = change.astype(jnp.bfloat16)
            return carry

        lax.fori_loop(0, seq_len // span, up_step, 0)
        for index, (source, target) in enumerate(((active, active_hbm), (slope, slope_hbm))):
            stores.append(
                pltpu.make_async_copy(
                    source.at[:, cols], target.at[:, cols], sems.at[3 + 2 * slot + index]
                )
            )
            stores[-1].start()

    def down_step(index, carry):
        at = pl.ds(pl.multiple_of(index * span, 16), span)
        value = normed_scr[at] + dot_plain(active[at], down_w[...])
        resid_two[at] = value
        layer_low[at] = (norm_parts(value)[0] * gain_two[...][None, :] + shift_two[...][None, :]).astype(jnp.bfloat16)
        return carry

    lax.fori_loop(0, seq_len // span, down_step, 0)
    stage.send(11, 12)
    stage.need(21)
    picked = dot_plain(choose[...], layer_low[words:]).astype(jnp.bfloat16)
    picked_out[...] = picked
    head_pre = dot_plain(picked, head_w[...])
    head_pre_out[...] = head_pre
    raised = gelu_parts(head_pre)[0]
    head_out[...] = (norm_parts(raised)[0] * gain_head[...][None, :] + shift_head[...][None, :]).astype(jnp.bfloat16)
    for store in stores:
        store.wait()


def forward_pass(inputs):
    words, width = inputs[0].shape
    slots = inputs[1].shape[0]
    seq_len = words + slots
    hidden_units = inputs[17].shape[1]
    mask_count = inputs[4].shape[0]
    head_width = inputs[21].shape[1]
    low, full = jnp.bfloat16, jnp.float32
    vmem, hbm = pl.BlockSpec(memory_space=pltpu.VMEM), pl.BlockSpec(memory_space=pltpu.HBM)
    far = (6, 7, 8, 9, 14, 17, 18)
    shapes = [
        ((seq_len, width), low),
        ((seq_len, width), low),
        ((seq_len, width), low),
        ((seq_len, width), low),
        ((seq_len, width), low),
        ((seq_len, width), low),
        ((seq_len, 128), full),
        ((seq_len, width), full),
        ((seq_len, width), low),
        ((seq_len, hidden_units), low),
        ((seq_len, hidden_units), low),
        ((seq_len, width), full),
        ((seq_len, width), low),
        ((mask_count, width), low),
        ((mask_count, head_width), full),
        ((mask_count, head_width), low),
    ]
    outs = [jax.ShapeDtypeStruct(*shape) for shape in shapes]
    return staged_call(
        forward_kernel,
        inputs,
        outs,
        [hbm if index in far else vmem for index in range(len(inputs))],
        [hbm if index in (9, 10) else vmem for index in range(len(shapes))],
        (0, 1, 5, 10, 11, 12, 13, 2, 3, 21),
        (0, 1, 2, 3, 4, 5, 7, 8, 11, 12),
        [
            pltpu.VMEM((slots, width), full),
            pltpu.VMEM((seq_len, width), full),
            pltpu.VMEM(inputs[14].shape, low),
            pltpu.VMEM(inputs[17].shape, low),
            pltpu.VMEM(inputs[18].shape, low),
            pltpu.VMEM((seq_len, hidden_units), low),
            pltpu.VMEM((seq_len, hidden_units), low),
            pltpu.SemaphoreType.DMA((16,)),
        ],
        pltpu.CompilerParams(vmem_limit_bytes=63 * 2**20),
    )


class Grid:
    def __init__(self):
        me = lax.axis_index("dp")
        self.core = lax.rem(me, 2)
        self.square = lax.rem(lax.div(me, 2), 4)
        self.line = lax.div(me, 8)
        self.twin = me + 1 - 2 * self.core
        self.squares = []
        self.lines = []
        for step in range(1, 4):
            other = lax.rem(self.square + step, 4)
            self.squares.append((me + 2 * (other - self.square), other))
            other = lax.rem(self.line + step, 4)
            self.lines.append((me + 8 * (other - self.line), other))

    def greet(self):
        barrier = pltpu.get_barrier_semaphore()
        peers = [self.twin] + [peer for peer, _ in self.squares + self.lines]
        for peer in peers:
            pl.semaphore_signal(barrier, inc=1, device_id=(peer,), device_id_type=MESH_ID)
        pl.semaphore_wait(barrier, len(peers))


class Sender:
    def __init__(self, send_sem, recv_sem):
        self.send_sem, self.recv_sem, self.used = send_sem, recv_sem, 0

    def start(self, source, target, peer):
        slot = self.used
        self.used += 1
        copy = pltpu.make_async_remote_copy(
            src_ref=source,
            dst_ref=target,
            send_sem=self.send_sem.at[slot],
            recv_sem=self.recv_sem.at[slot],
            device_id=(peer,),
            device_id_type=MESH_ID,
        )
        copy.start()
        return copy


def wait_all(copies):
    for copy in copies:
        copy.wait()


def merge_stats(blocks):
    tops = [block[0] for block in blocks]
    top = functools.reduce(jnp.maximum, tops)
    total = sum(block[1] * jnp.exp(block[0] - top) for block in blocks)
    return top, total, sum(block[2] for block in blocks)


def head_kernel(
    grad_scale,
    stage,
    head,
    table,
    bias,
    target_vecs,
    target_bias,
    table_grad,
    bias_grad,
    losses,
    total_loss,
    head_grad,
    heads,
    logits,
    expo,
    table_t,
    bias_col,
    part,
    land_pair,
    sum_pair,
    land_square,
    sum_square,
    land_line,
    stat,
    stat_pair,
    stat_square,
    stat_line,
    send_sem,
    recv_sem,
):
    grid = Grid()
    rows, wide = table.shape
    count = head.shape[0]
    total_mask = 32 * count
    grid.greet()
    sender = Sender(send_sem, recv_sem)
    line, square, core = grid.line, grid.square, grid.core
    flying = [sender.start(head, heads.at[line, square, core], peer) for peer, _ in grid.lines]
    heads[line, square, core] = head[...]

    def table_step(index, carry):
        at = pl.ds(pl.multiple_of(index * 128, 128), 128)
        table_t[:, at] = table[at].astype(jnp.float32).T.astype(jnp.bfloat16)
        return carry

    stage.need(1)
    lax.fori_loop(0, rows // 128, table_step, 0)
    wait_all(flying)
    flying = [
        sender.start(heads.at[:, square, core], heads.at[:, square, core], peer)
        for peer, _ in grid.squares
    ]

    def bias_step(index, carry):
        at = pl.ds(pl.multiple_of(index * 128, 128), 128)
        bias_col[at] = jnp.broadcast_to(bias[at].reshape(1, 128), (128, 128)).T
        return carry

    lax.fori_loop(0, rows // 128, bias_step, 0)
    wait_all(flying)
    sender.start(heads.at[:, :, core], heads.at[:, :, core], grid.twin).wait()

    all_heads = heads[...].reshape(total_mask, wide)
    slab = rows // 2

    def logit_step(index, carry):
        at = pl.ds(pl.multiple_of(index * slab, 16), slab)
        logits[at] = dot_right_t(table[at], all_heads)
        return carry

    lax.fori_loop(0, rows // slab, logit_step, 0)
    tile = 64
    wide_copies = total_mask // 128

    def value_at(index):
        at = pl.ds(pl.multiple_of(index * tile, tile), tile)
        shift = bias_col[at]
        return at, logits[at] + jnp.concatenate([shift] * wide_copies, axis=1)

    def top_step(index, top):
        at, value = value_at(index)
        return jnp.maximum(top, jnp.max(value.reshape(tile // 8, 8, total_mask), axis=0))

    top = lax.fori_loop(
        0, rows // tile, top_step, jnp.full((8, total_mask), -jnp.inf, jnp.float32)
    )
    top = jnp.max(top, axis=0, keepdims=True)

    def exp_step(index, total):
        at, value = value_at(index)
        value = jnp.exp(value - top)
        expo[at] = value.astype(jnp.bfloat16)
        return total + jnp.sum(value.reshape(tile // 8, 8, total_mask), axis=0)

    total = lax.fori_loop(0, rows // tile, exp_step, jnp.zeros((8, total_mask), jnp.float32))
    total = jnp.sum(total, axis=0, keepdims=True)

    def fold(row):
        return jnp.concatenate([row[:, i * 128 : i * 128 + 128] for i in range(wide_copies)], axis=0)

    def unfold(block):
        return jnp.concatenate([block[i : i + 1] for i in range(wide_copies)], axis=1)

    own_top, own_total = fold(top), fold(total)
    target = (
        jnp.sum(head[...].astype(jnp.float32) * target_vecs[...], axis=1, keepdims=True)
        + target_bias[:, 0:1]
    )
    own_target = jnp.broadcast_to(jnp.sum(target, axis=0, keepdims=True), own_top.shape)
    stat[0, 0], stat[0, 1], stat[0, 2] = own_top, own_total, own_target
    copy = sender.start(stat.at[0], stat_pair, grid.twin)
    quarter = total_mask // 4
    parts = [dot_plain(table_t[...], expo[:, :quarter])]
    copy.wait()
    stat[1, 0], stat[1, 1], stat[1, 2] = merge_stats(
        [(own_top, own_total, own_target), (stat_pair[0], stat_pair[1], stat_pair[2])]
    )
    stat_square[square] = stat[1]
    flying = [sender.start(stat.at[1], stat_square.at[square], peer) for peer, _ in grid.squares]
    parts.append(dot_plain(table_t[...], expo[:, quarter : 2 * quarter]))
    wait_all(flying)
    stat[2, 0], stat[2, 1], stat[2, 2] = merge_stats(
        [(stat_square[i, 0], stat_square[i, 1], stat_square[i, 2]) for i in range(4)]
    )
    stat_line[line] = stat[2]
    flying = [sender.start(stat.at[2], stat_line.at[line], peer) for peer, _ in grid.lines]
    parts.append(dot_plain(table_t[...], expo[:, 2 * quarter : 3 * quarter]))
    parts.append(dot_plain(table_t[...], expo[:, 3 * quarter :]))
    wait_all(flying)
    full_top, full_total, full_target = merge_stats(
        [(stat_line[i, 0], stat_line[i, 1], stat_line[i, 2]) for i in range(4)]
    )
    lse = full_top + jnp.log(full_total)
    all_lse = jnp.sum(jnp.sum(lse, axis=1, keepdims=True), axis=0, keepdims=True)
    total_loss[...] = (all_lse - full_target[0:1]) * grad_scale
    mine = lax.broadcasted_iota(jnp.int32, (count, total_mask), 0) + lax.axis_index("dp") * count
    hit = mine == lax.broadcasted_iota(jnp.int32, (count, total_mask), 1)
    own_lse = jnp.sum(jnp.where(hit, unfold(lse), 0.0), axis=1, keepdims=True)
    turned = jnp.broadcast_to(own_lse - target, (count, 128)).T
    losses[...] = turned[0:1].reshape(count)
    scale = unfold(jnp.exp(own_top - lse) * grad_scale)
    per = 128 // count
    for index in range(total_mask // 128):
        at = slice(index * 128, index * 128 + 128)
        source = parts[index * 128 // quarter]
        begin = index * 128 % quarter
        piece = (source[:, begin : begin + 128] * scale[:, at]).T.astype(jnp.bfloat16)
        for inner in range(per):
            owner = index * per + inner
            part[owner // 8, owner // 2 % 4, owner % 2] = piece[inner * count : inner * count + count]
    copy = sender.start(part.at[:, :, 1 - core], land_pair, grid.twin)

    scaled = []
    for index in range(total_mask // 128):
        at = slice(index * 128, index * 128 + 128)
        column = jnp.broadcast_to(scale[:, at], (128, 128)).T
        column = jnp.concatenate([column] * (wide // 128), axis=1)
        scaled.append((all_heads[at].astype(jnp.float32) * column).astype(jnp.bfloat16))
    scaled = jnp.concatenate(scaled, axis=0)
    slab = rows // 4

    def grad_part(index):
        at = slice(index * slab, index * slab + slab)
        table_grad[at] = dot_plain(expo[at], scaled)

    grad_part(0)
    copy.wait()
    sum_pair[...] = (part[:, :, core].astype(jnp.float32) + land_pair[...].astype(jnp.float32)).astype(
        jnp.bfloat16
    )
    flying = [
        sender.start(sum_pair.at[:, other], land_square.at[square], peer)
        for peer, other in grid.squares
    ]
    land_square[square] = sum_pair[:, square]
    grad_part(1)
    wait_all(flying)
    sum_square[...] = sum(land_square[i].astype(jnp.float32) for i in range(4)).astype(jnp.bfloat16)
    flying = [
        sender.start(sum_square.at[other], land_line.at[line], peer) for peer, other in grid.lines
    ]
    land_line[line] = sum_square[line]
    grad_part(2)
    high = scale.astype(jnp.bfloat16)
    low = (scale - high.astype(jnp.float32)).astype(jnp.bfloat16)
    both = jnp.concatenate(
        [high.astype(jnp.float32), low.astype(jnp.float32), jnp.zeros((14, total_mask), jnp.float32)],
        axis=0,
    ).astype(jnp.bfloat16)
    sums = dot_right_t(both, expo[...])
    bias_grad[...] = sums[0:1] + sums[1:2]
    grad_part(3)
    stage.send(0)
    wait_all(flying)
    head_grad[...] = sum(land_line[i].astype(jnp.float32) for i in range(4))


def head_and_table(
    head_low, entity_table, bias_row, target_vecs, target_bias, grad_scale, collective_id
):
    count, wide = head_low.shape
    rows = entity_table.shape[0]
    total_mask = 32 * count
    low, full = jnp.bfloat16, jnp.float32
    vmem = pl.BlockSpec(memory_space=pltpu.VMEM)
    folded = (total_mask // 128, 128)
    inputs = [head_low, entity_table, bias_row, target_vecs, target_bias]
    outs = [
        jax.ShapeDtypeStruct((rows, wide), full),
        jax.ShapeDtypeStruct((1, rows), full),
        jax.ShapeDtypeStruct((count,), full),
        jax.ShapeDtypeStruct((1, 128), full),
        jax.ShapeDtypeStruct((count, wide), full),
    ]
    return staged_call(
        functools.partial(head_kernel, grad_scale),
        inputs,
        outs,
        [vmem] * 5,
        [vmem] * 5,
        (1,),
        (0,),
        [
            pltpu.VMEM((4, 4, 2, count, wide), low),
            pltpu.VMEM((rows, total_mask), full),
            pltpu.VMEM((rows, total_mask), low),
            pltpu.VMEM((wide, rows), low),
            pltpu.VMEM((rows, 128), full),
            pltpu.VMEM((4, 4, 2, count, wide), low),
            pltpu.VMEM((4, 4, count, wide), low),
            pltpu.VMEM((4, 4, count, wide), low),
            pltpu.VMEM((4, 4, count, wide), low),
            pltpu.VMEM((4, count, wide), low),
            pltpu.VMEM((4, count, wide), low),
            pltpu.VMEM((3, 3) + folded, full),
            pltpu.VMEM((3,) + folded, full),
            pltpu.VMEM((4, 3) + folded, full),
            pltpu.VMEM((4, 3) + folded, full),
            pltpu.SemaphoreType.DMA((24,)),
            pltpu.SemaphoreType.DMA((24,)),
        ],
        pltpu.CompilerParams(
            collective_id=collective_id, has_side_effects=True, vmem_limit_bytes=63 * 2**20
        ),
    )


def norm_slope(value, given, gain):
    scaled, rate = norm_parts(value)
    back = given * gain
    mean_back = jnp.mean(back, axis=-1, keepdims=True)
    mean_both = jnp.mean(back * scaled, axis=-1, keepdims=True)
    grad = rate * (back - mean_back - scaled * mean_both)
    return (
        grad,
        jnp.sum(given * scaled, axis=0, keepdims=True),
        jnp.sum(given, axis=0, keepdims=True),
    )


def split_low(value):
    high = value.astype(jnp.bfloat16)
    return high, (value - high.astype(jnp.float32)).astype(jnp.bfloat16)


def place_rows(source, order, count, store):
    owners = 2 ** len(order)
    for pair in range(owners // 2):
        one, two = place_owner(order, 2 * pair), place_owner(order, 2 * pair + 1)
        both = jnp.concatenate(
            [source[one * count : one * count + count], source[two * count : two * count + count]],
            axis=0,
        )
        store(slice(pair * 2 * count, (pair + 1) * 2 * count), both.astype(jnp.bfloat16))


def middle_back_kernel(
    orders,
    grad_scale,
    stage,
    head_grad,
    target_vecs,
    head_pre,
    gain_head,
    picked,
    head_w,
    choose,
    cotangent,
    resid_two,
    gain_two,
    normed_low,
    resid_one,
    gain_one,
    out_w,
    context,
    lse_lanes,
    active_hbm,
    slope_hbm,
    up_hbm,
    down_hbm,
    up_a,
    up_b,
    head_a,
    out_b,
    down_b,
    up_c,
    down_c,
    first_grad,
    context_grad,
    lse_delta,
    vectors,
    active,
    slope,
    up_w,
    down_w,
    flip,
    normed_t,
    context_t,
    down_in,
    acc,
    up_low,
    stage_a,
    stage_c,
    sems,
):
    seq_len, width = cotangent.shape
    slots = choose.shape[1]
    words = seq_len - slots
    cuts = down_w.shape[0] // width
    loads = []
    for index, (source, target) in enumerate(
        ((active_hbm, active), (down_hbm, down_w), (slope_hbm, slope), (up_hbm, up_w))
    ):
        for cut in range(cuts):
            at = pl.ds(cut * width, width)
            view = (at,) if index == 1 else (slice(None), at)
            loads.append(
                pltpu.make_async_copy(source.at[view], target.at[view], sems.at[index * cuts + cut])
            )
    for cut in range(cuts):
        for index in range(4):
            loads[index * cuts + cut].start()

    given = head_grad[...] - grad_scale * target_vecs[...]
    pre = head_pre[...]
    raised, change = gelu_parts(pre)
    back, gain_sum, bias_sum = norm_slope(raised, given, gain_head[...][None, :])
    sums = [gain_sum, bias_sum]
    pre_low = (back * change).astype(jnp.bfloat16)
    head_weight_grad = dot_left_t(picked[...], pre_low)
    count = width // 2 ** len(orders[0])

    def keep_head(at, value):
        head_a[0, at] = value

    flip[:, : head_a.shape[2]] = head_weight_grad
    place_rows(flip[:, : head_a.shape[2]], orders[0], count, keep_head)
    stage.need(5)
    picked_high, picked_rest = split_low(dot_right_t(pre_low, head_w[...]))
    placed = dot_left_t(choose[...], picked_high) + dot_left_t(choose[...], picked_rest)

    stage.need(7, 8)
    block = 128
    total_gain = jnp.zeros((1, width), jnp.float32)
    total_bias = jnp.zeros((1, width), jnp.float32)
    for begin in range(0, seq_len, block):
        at = slice(begin, begin + block)
        given = cotangent[at].astype(jnp.float32)
        if begin >= words:
            given = given + placed[begin - words : begin - words + block]
        grad, gain_sum, bias_sum = norm_slope(resid_two[at], given, gain_two[...][None, :])
        total_gain += gain_sum
        total_bias += bias_sum
        acc[at] = grad
        down_in[at] = grad.astype(jnp.bfloat16)
    sums += [total_gain, total_bias]

    def flip_into(source, target, order_list):
        def flip_step(index, carry):
            at = pl.ds(pl.multiple_of(index * block, block), block)
            flip[at] = source[:, at].astype(jnp.float32).T
            return carry

        lax.fori_loop(0, width // block, flip_step, 0)
        for slot, order in enumerate(order_list):

            def keep(at, value, slot=slot):
                target[slot, at] = value

            place_rows(flip, order, count, keep)

    stage.need(10, 14)
    flip_into(normed_low, normed_t, (orders[0], orders[2]))
    flip_into(context, context_t, (orders[1],))

    column = 384
    span = seq_len
    block_two = seq_len // 2
    split = down_b.shape[2]
    owners = 2 ** len(orders[0])
    tall = down_w.shape[0] // owners
    spots = [
        {place_owner(order, place): place for place in range(owners)}
        for order in (orders[1], orders[2])
    ]
    stores = []
    for cut in range(cuts):
        at = slice(cut * width, cut * width + width)
        for index in range(4):
            loads[index * cuts + cut].wait()
        for begin in range(0, width, column):
            piece = dot_left_t(active[:, at], down_in[:, begin : begin + column])
            for inner in range(width // tall):
                owner = cut * (width // tall) + inner
                rows = piece[inner * tall : inner * tall + tall].astype(jnp.bfloat16)
                stop = min(begin + column, split)
                if begin < split:
                    place = spots[0][owner] * tall
                    stage_a[place : place + tall, begin:stop] = rows[:, : stop - begin]
                if begin + column > split:
                    start = max(begin, split)
                    place = spots[1][owner] * tall
                    stage_c[place : place + tall, start - split : begin + column - split] = rows[
                        :, start - begin :
                    ]

        def back_step(index, carry, at=at):
            rows = pl.ds(pl.multiple_of(index * span, 16), span)
            grad = dot_right_t(down_in[rows], down_w[at]) * slope[rows, at].astype(jnp.float32)
            grad = grad.astype(jnp.bfloat16)
            up_low[rows] = grad
            acc[rows] = acc[rows] + dot_right_t(grad, up_w[:, at])
            return carry

        lax.fori_loop(0, seq_len // span, back_step, 0)
        target, slot, order_slot = ((up_a, 0, 0), (up_a, 1, 0), (up_b, 0, 0), (up_c, 0, 1))[cut]
        for begin in range(0, width, column):
            target[slot, :, begin : begin + column] = dot_plain(
                normed_t[order_slot], up_low[:, begin : begin + column]
            ).astype(jnp.bfloat16)
    stage.send(0, 1, 5)
    stage.need(11, 13)
    stores = [
        pltpu.make_async_copy(stage_a, down_b.at[0], sems.at[4 * cuts]),
        pltpu.make_async_copy(stage_c, down_c.at[0], sems.at[4 * cuts + 1]),
    ]
    for store in stores:
        store.start()

    total_gain = jnp.zeros((1, width), jnp.float32)
    total_bias = jnp.zeros((1, width), jnp.float32)
    row = lax.broadcasted_iota(jnp.int32, (width, 128), 0)
    lane = lax.broadcasted_iota(jnp.int32, (width, 128), 1)
    spot = 4 * lax.div(row, 128) + 2 + lax.div(lax.rem(row, 128), HD)
    pick = (spot == lane).astype(jnp.float32).astype(jnp.bfloat16)
    for begin in range(0, seq_len, block_two):
        at = slice(begin, begin + block_two)
        grad, gain_sum, bias_sum = norm_slope(resid_one[at], acc[at], gain_one[...][None, :])
        total_gain += gain_sum
        total_bias += bias_sum
        first_grad[at] = grad
        low = grad.astype(jnp.bfloat16)
        down_in[at] = low
        back = dot_right_t(low, out_w[...]).astype(jnp.bfloat16)
        context_grad[at] = back
        high, rest = split_low(back.astype(jnp.float32) * context[at].astype(jnp.float32))
        lse_delta[at] = lse_lanes[at] + dot_plain(high, pick) + dot_plain(rest, pick)
    stage.send(7, 8)
    sums += [total_gain, total_bias]
    tall, room = vectors.shape[1:]
    every = tall // owners
    placed = jnp.zeros((tall, room), jnp.float32)
    offset = 0
    for vector in sums:
        size = vector.shape[1]
        per = size // owners
        row = lax.broadcasted_iota(jnp.int32, (tall, size), 0)
        place = lax.div(row, every)
        owner = jnp.zeros((tall, size), jnp.int32)
        for spot, mask in enumerate(orders[0]):
            owner += lax.rem(lax.div(place, 2 ** (len(orders[0]) - 1 - spot)), 2) * mask
        column_at = lax.broadcasted_iota(jnp.int32, (tall, size), 1)
        mine = (lax.div(column_at, per) == owner) & (lax.rem(row, every) == 0)
        spread = jnp.where(mine, vector, 0.0).astype(jnp.bfloat16)
        source = lax.broadcasted_iota(jnp.int32, (size, room), 0)
        target = lax.broadcasted_iota(jnp.int32, (size, room), 1)
        move = (lax.rem(source, per) + offset == target).astype(jnp.float32).astype(jnp.bfloat16)
        placed += dot_plain(spread, move)
        offset += per
    vectors[0] = placed.astype(jnp.bfloat16)
    for begin in range(0, width, column):
        out_b[0, :, begin : begin + column] = dot_plain(
            context_t[0], down_in[:, begin : begin + column]
        ).astype(jnp.bfloat16)
    for store in stores:
        store.wait()


DOWN_SPLIT = 512


def middle_back(inputs, orders, grad_scale):
    seq_len, width = inputs[7].shape
    hidden_units = inputs[16].shape[1]
    head_width = inputs[0].shape[1]
    low, full = jnp.bfloat16, jnp.float32
    cuts = hidden_units // width
    vmem, hbm = pl.BlockSpec(memory_space=pltpu.VMEM), pl.BlockSpec(memory_space=pltpu.HBM)
    shapes = [
        ((2, width, width), low),
        ((1, width, width), low),
        ((1, width, head_width), low),
        ((1, width, width), low),
        ((1, hidden_units, DOWN_SPLIT), low),
        ((1, width, width), low),
        ((1, hidden_units, width - DOWN_SPLIT), low),
        ((seq_len, width), full),
        ((seq_len, width), low),
        ((seq_len, 128), full),
        ((1, 8 * 2 ** len(orders[0]), 256), low),
    ]
    outs = [jax.ShapeDtypeStruct(*shape) for shape in shapes]
    return staged_call(
        functools.partial(middle_back_kernel, orders, grad_scale),
        inputs,
        outs,
        [vmem] * 16 + [hbm] * 4,
        [hbm if index in (4, 6) else vmem for index in range(len(shapes))],
        (5, 7, 8, 10, 14, 11, 13),
        (0, 1, 3, 5, 7, 8),
        [
            pltpu.VMEM((seq_len, hidden_units), low),
            pltpu.VMEM((seq_len, hidden_units), low),
            pltpu.VMEM((width, hidden_units), low),
            pltpu.VMEM((hidden_units, width), low),
            pltpu.VMEM((width, seq_len), full),
            pltpu.VMEM((2, width, seq_len), low),
            pltpu.VMEM((1, width, seq_len), low),
            pltpu.VMEM((seq_len, width), low),
            pltpu.VMEM((seq_len, width), full),
            pltpu.VMEM((seq_len, width), low),
            pltpu.VMEM((hidden_units, DOWN_SPLIT), low),
            pltpu.VMEM((hidden_units, width - DOWN_SPLIT), low),
            pltpu.SemaphoreType.DMA((4 * cuts + 2,)),
        ],
        pltpu.CompilerParams(vmem_limit_bytes=63 * 2**20),
    )


def last_kernel(grad_scale, stage, codes, back, table_hbm, bias_in, *refs):
    sums, refs = refs[:SUMS], refs[SUMS:]
    table_out, bias_out = refs[:2]
    outs, refs = refs[2 : 2 + SUMS - 4], refs[2 + SUMS - 4 :]
    flats, refs = refs[: len(FLAT)], refs[len(FLAT) :]
    table_in, result, sems, move_sems = refs
    rows = table_hbm.shape[0]
    entries = back.shape[0]
    step = 1024
    parts = [(begin, min(step, rows - begin)) for begin in range(0, rows, step)]
    loads = [
        pltpu.make_async_copy(
            table_hbm.at[pl.ds(begin, size)], table_in.at[pl.ds(begin, size)], sems.at[0, index]
        )
        for index, (begin, size) in enumerate(parts)
    ]
    stores = [
        pltpu.make_async_copy(
            result.at[pl.ds(begin, size)], table_out.at[pl.ds(begin, size)], sems.at[1, index]
        )
        for index, (begin, size) in enumerate(parts)
    ]
    for load in loads:
        load.start()
    up_two, down_a, up_last, down_b, up_third = sums[:5]
    up_out, down_out = outs[:2]
    width = up_last.shape[2]
    pairs = [
        (value, up_out.at[:, pl.ds(index * width, width)])
        for index, value in enumerate((up_two.at[0], up_two.at[1], up_third.at[0], up_last.at[0]))
    ]
    pairs.append((down_a.at[0], down_out.at[:, pl.ds(0, down_a.shape[2])]))
    pairs.append((down_b.at[0], down_out.at[:, pl.ds(down_a.shape[2], down_b.shape[2])]))
    rest = [value for index, value in enumerate(sums) if index > 4 and index != VECTOR]
    pairs += [(source.at[0], target) for source, target in zip(rest, outs[2:])]
    moves = [
        pltpu.make_async_copy(source, target, move_sems.at[index])
        for index, (source, target) in enumerate(pairs)
    ]
    code = codes[0:1]
    target = (code >= rows).astype(jnp.float32)
    flags = jnp.broadcast_to(target, (16, entries)).astype(jnp.bfloat16)
    code = jnp.where(code >= rows, code - rows, code)
    for index, (begin, size) in enumerate(parts):
        row = lax.broadcasted_iota(jnp.int32, (size, entries), 0) + begin
        match = (row == code).astype(jnp.float32).astype(jnp.bfloat16)
        at = slice(begin, begin + size)
        counts = dot_right_t(flags, match)
        bias_out[at] = (bias_in[:, at] - grad_scale * counts[0:1]).reshape(size)
        added = dot_plain(match, back[...])
        loads[index].wait()
        result[at] = table_in[at] + added
        stores[index].start()
    stage.need(*range(4, 4 + SUMS))
    for move in moves:
        move.start()
    offset = 0
    for target in flats:
        size = target.shape[0]
        target[...] = sums[VECTOR][0, 0:1, offset : offset + size].reshape(size)
        offset += size
    for copy in stores + moves:
        copy.wait()


SUMS = 15
VECTOR = 6
FLAT = (0, 0, 1, 1, 1, 1)


def last_step(codes, back, table_grad, bias_grad, sums, sizes, grad_scale):
    vmem, hbm = pl.BlockSpec(memory_space=pltpu.VMEM), pl.BlockSpec(memory_space=pltpu.HBM)
    full = jnp.float32
    up_rows, width = sums[0].shape[1:]
    down_rows = sums[1].shape[1]
    shapes = [
        table_grad.shape,
        (bias_grad.shape[1],),
        (up_rows, 4 * width),
        (down_rows, width),
    ] + [value.shape[1:] for index, value in enumerate(sums) if index > 4 and index != VECTOR]
    shapes += [(sizes[kind],) for kind in FLAT]
    return staged_call(
        functools.partial(last_kernel, grad_scale),
        [codes, back, table_grad, bias_grad, *sums],
        [jax.ShapeDtypeStruct(shape, full) for shape in shapes],
        [vmem, vmem, hbm, vmem] + [vmem] * len(sums),
        [hbm, vmem] + [hbm] * (len(shapes) - 2 - len(FLAT)) + [vmem] * len(FLAT),
        tuple(range(4, 4 + len(sums))),
        (),
        [
            pltpu.VMEM(table_grad.shape, full),
            pltpu.VMEM(table_grad.shape, full),
            pltpu.SemaphoreType.DMA((2, 8)),
            pltpu.SemaphoreType.DMA((len(sums) + 1,)),
        ],
        pltpu.CompilerParams(vmem_limit_bytes=63 * 2**20),
    )


def place_owner(order, place):
    bits = len(order)
    return sum(((place >> (bits - 1 - spot)) & 1) * mask for spot, mask in enumerate(order))


class Piece:
    def __init__(
        self, rows, stages, send, own, land, tail, pack, tail_land, out, send_sem, recv_sem
    ):
        self.rows, self.stages = rows, stages
        self.send, self.own, self.land = send, own, land
        self.tail, self.pack, self.tail_land, self.out = tail, pack, tail_land, out
        self.send_sem, self.recv_sem = send_sem, recv_sem
        self.sizes = [rows * 2 ** (stages - 1 - stage) for stage in range(stages)]
        self.spots = [sum(self.sizes[:stage]) for stage in range(stages)]

    def copy(self, stage, partner, bit):
        size = self.sizes[stage]
        away = (1 - bit) * size
        if stage < self.stages - 1:
            away = pl.multiple_of(away, 16)
        if stage == 0:
            source, target = self.send.at[:, pl.ds(away, size)], self.land.at[:, pl.ds(0, size)]
        elif stage < self.stages - 1:
            spot = pl.multiple_of(self.spots[stage - 1] + away, 16)
            source = self.land.at[:, pl.ds(spot, size)]
            target = self.land.at[:, pl.ds(self.spots[stage], size)]
        else:
            source, target = self.pack, self.tail_land
        return pltpu.make_async_remote_copy(
            src_ref=source,
            dst_ref=target,
            send_sem=self.send_sem.at[stage],
            recv_sem=self.recv_sem.at[stage],
            device_id=(partner,),
            device_id_type=MESH_ID,
        )

    def held(self, stage, bit):
        size = self.sizes[stage]
        if stage == 0 and self.own is not None:
            return self.own, 0
        if stage == 0:
            return self.send, pl.multiple_of(bit * size, 16)
        return self.land, pl.multiple_of(self.spots[stage - 1] + bit * size, 16)

    def add(self, stage, bit, half_index):
        size = self.sizes[stage]
        half = size // 2
        unit = 48 if half % 48 == 0 else 16
        start = half_index * half
        source, base = self.held(stage, bit)
        for slot in range(self.land.shape[0]):

            def step(index, carry, slot=slot):
                row = pl.multiple_of(start + index * unit, 16)
                mine = source[slot, pl.ds(pl.multiple_of(base + row, 16), unit)]
                spot = pl.ds(pl.multiple_of(self.spots[stage] + row, 16), unit)
                theirs = self.land[slot, spot]
                total = mine.astype(jnp.float32) + theirs.astype(jnp.float32)
                self.land[slot, spot] = total.astype(jnp.bfloat16)
                return carry

            lax.fori_loop(0, half // unit, step, 0)

    def add_tail(self, stage, bit, following):
        size = self.sizes[stage]
        half = size // 2
        middle = self.land.shape[2] // 2
        source, base = self.held(stage, bit)
        for slot in range(self.land.shape[0]):
            mine = source[slot, pl.ds(base, size)]
            theirs = self.land[slot, pl.ds(self.spots[stage], size)]
            self.tail[slot] = mine.astype(jnp.float32) + theirs.astype(jnp.float32)
            other = self.tail[slot, pl.ds(pl.multiple_of((1 - following) * half, 8), half)]
            self.pack[slot] = jnp.concatenate(
                [other[:, :middle], other[:, middle:]], axis=0
            ).astype(jnp.bfloat16)

    def finish(self, bit):
        size = self.sizes[-1]
        for slot in range(self.out.shape[0]):
            mine = self.tail[slot, pl.ds(pl.multiple_of(bit * size, 8), size)]
            theirs = self.tail_land[slot].astype(jnp.float32)
            self.out[slot] = mine + jnp.concatenate([theirs[:size], theirs[size:]], axis=1)


class Stream:
    def __init__(self, order, partner_of, pieces):
        self.order, self.partner_of, self.pieces = order, partner_of, pieces
        self.stages = len(order)

    def launch(self, stage):
        partner, bit = self.partner_of[self.order[stage]]
        for piece in self.pieces:
            piece.copy(stage, partner, bit).start()

    def advance(self, stage):
        partner, bit = self.partner_of[self.order[stage]]
        for piece in self.pieces:
            piece.copy(stage, partner, bit).wait()
        if stage == self.stages - 1:
            for piece in self.pieces:
                piece.finish(bit)
        elif stage == self.stages - 2:
            for piece in self.pieces:
                piece.add_tail(stage, bit, self.partner_of[self.order[stage + 1]][1])
            self.launch(stage + 1)
        else:
            following = self.partner_of[self.order[stage + 1]][1]
            for piece in self.pieces:
                piece.add(stage, bit, 1 - following)
            self.launch(stage + 1)
            for piece in self.pieces:
                piece.add(stage, bit, following)


def partners(me, masks):
    result = {}
    for mask in masks:
        bit = lax.rem(lax.div(me, mask), 2)
        result[mask] = (me + mask - 2 * mask * bit, bit)
    return result


EARLY = (
    (0, 2, 24, 768),
    (1, 1, 96, 512),
    (2, 1, 24, 768),
    (3, 1, 96, 256),
    (4, 1, 24, 768),
    (4, 1, 24, 256),
    (4, 1, 8, 256),
    (5, 1, 24, 768),
)
LATE = (
    (6, 1, 24, 768),
    (7, 1, 24, 768),
    (8, 1, 24, 768),
    (9, 1, 24, 768),
    (10, 1, 24, 768),
    (11, 1, 24, 768),
    (11, 1, 8, 768),
)
STREAM_ORDER = (0, 1, 2, 2, 0, 1, 1, 1, 2, 1, 0, 0)

WORD_POINTS = ("word0", "word1")

PLAN = {('r', 1): ((0, 0),), ('p', 1): ((1, 0),), ('r', 2): ((2, 0), (3, 0)), ('p', 2): ((4, 0),), ('r', 3): ((5, 0),), ('r', 4): ((2, 1),), ('r', 5): ((0, 1),), 'KV': ((1, 1),), 'ew': ((3, 1),), 'ww': ((4, 1),), 'ent': ((6, 0), (2, 2), (7, 0), (5, 1), (8, 0)), 'we': ((9, 0),), 'word0': ((10, 0),), 'word1': ((1, 2), (11, 0), (3, 2), (0, 2), (2, 3)), 'end': ((8, 1), (5, 2), (4, 2), (1, 3), (10, 1), (0, 3), (6, 1), (8, 2), (5, 3), (7, 1), (4, 3), (11, 1), (1, 4), (3, 3), (0, 4), (5, 4), (4, 4), (9, 1), (6, 2), (2, 4), (8, 3), (10, 2), (6, 3), (7, 2), (10, 3), (11, 2), (9, 2), (6, 4), (3, 4), (8, 4), (7, 3), (10, 4), (11, 3), (9, 3), (7, 4), (11, 4), (9, 4))}


def piece_scratch(spec, stages, source, own):
    _, slots, rows, width = spec
    owners = 2**stages
    shapes = []
    if source:
        shapes.append(pltpu.VMEM((slots, rows * owners, width), jnp.bfloat16))
    if own:
        shapes.append(pltpu.VMEM((slots, rows * owners // 2, width), jnp.bfloat16))
    shapes += [
        pltpu.VMEM((slots, rows * (owners - 2), width), jnp.bfloat16),
        pltpu.VMEM((slots, 2 * rows, width), jnp.float32),
        pltpu.VMEM((slots, 2 * rows, width // 2), jnp.bfloat16),
        pltpu.VMEM((slots, 2 * rows, width // 2), jnp.bfloat16),
        pltpu.SemaphoreType.DMA((stages,)),
        pltpu.SemaphoreType.DMA((stages,)),
    ]
    return shapes


def attention_back_kernel(orders, grad_scale, stage, *refs):
    stages = len(orders[0])
    refs = list(refs)

    def take(count):
        taken = refs[:count]
        del refs[:count]
        return taken

    early_send = take(len(EARLY))
    (hidden, qword, qent, keys, values, cgrad, feat_q, feat_k, lse_delta, first_grad, head_low, slot_row) = take(12)
    (w_ww, w_we, w_ew, w_ee, w_key, w_value, dense, entity_low) = take(8)
    early_out = take(len(EARLY))
    late_out = take(len(LATE))
    words_out, request_out = take(2)
    devices = request_out.shape[0]
    early_pieces = []
    own_copies = []
    me = lax.axis_index("dp")
    partner_of = partners(me, orders[0])
    own_sem = refs.pop()
    request_sems = refs.pop()
    request_send = refs.pop()
    word_weights = []
    dqw, dqe, dkey, dvalue, prob_s, grad_s, flip, hidden_t, hidden_te, entity_t = refs[-10:]
    del refs[-10:]
    pieces = [[] for _ in STREAM_ORDER]
    early_flat = []
    for index, spec in enumerate(EARLY):
        own, land, tail, pack, tail_land, send_sem, recv_sem = take(7)
        piece = Piece(
            spec[2], stages, early_send[index], own, land, tail, pack, tail_land,
            early_out[index], send_sem, recv_sem,
        )
        pieces[spec[0]].append(piece)
        early_flat.append(piece)
        bit = partner_of[orders[STREAM_ORDER[spec[0]]][0]][1]
        size = spec[2] * 2 ** (stages - 1)
        own_copies.append(
            pltpu.make_async_copy(
                early_send[index].at[:, pl.ds(pl.multiple_of(bit * size, 16), size)],
                own,
                own_sem.at[index],
            )
        )
    late_source = []
    for index, spec in enumerate(LATE):
        source, land, tail, pack, tail_land, send_sem, recv_sem = take(7)
        late_source.append(source)
        pieces[spec[0]].append(
            Piece(
                spec[2], stages, source, None, land, tail, pack, tail_land,
                late_out[index], send_sem, recv_sem,
            )
        )
    spare = (early_flat[1].own, early_flat[3].own)
    split = spare[0].shape[2]
    for index, weight in enumerate((w_ww, w_we)):
        rows = weight.shape[0]
        for part, at in enumerate((pl.ds(0, split), pl.ds(split, weight.shape[1] - split))):
            word_weights.append(
                pltpu.make_async_copy(
                    weight.at[:, at],
                    spare[part].at[0, pl.ds(index * rows, rows)],
                    own_sem.at[len(EARLY) + 2 * index + part],
                )
            )
    streams = [
        Stream(orders[order], partner_of, pieces[index])
        for index, order in enumerate(STREAM_ORDER)
    ]
    first_late = LATE[0][0]

    def go_on(point):
        for index, stage in PLAN.get(point, ()):
            if stage == 0 and index < first_late:
                for piece, spec in enumerate(EARLY):
                    if spec[0] == index:
                        own_copies[piece].wait()
            streams[index].advance(stage)
            if stage == 0 and index in (1, 3):
                for copy in word_weights[(index - 1) // 2 :: 2]:
                    copy.start()

    greet_all(me, devices)
    for stream in streams[:first_late]:
        stream.launch(0)
    for copy in own_copies:
        copy.start()

    width = hidden.shape[1]
    seq_len = hidden.shape[0]
    words = words_out.shape[0]
    block = 128
    tall = seq_len // 2
    taller = words // len(WORD_POINTS)
    lane = lax.broadcasted_iota(jnp.int32, (1, block), 1)
    low_half = (lane < HD).astype(jnp.float32).astype(jnp.bfloat16)
    high_half = (lane >= HD).astype(jnp.float32).astype(jnp.bfloat16)
    halves = (low_half, high_half)

    stage.need(8)
    def flip_step(index, carry):
        at = pl.ds(pl.multiple_of(index * block, block), block)
        flip[at] = hidden[:, at].astype(jnp.float32).T
        return carry

    lax.fori_loop(0, width // block, flip_step, 0)
    owners = 2**stages
    rows = width // owners
    for slot, order in enumerate(orders):
        begin = words if slot == 2 else 0
        for pair in range(owners // 2):
            one, two = place_owner(order, 2 * pair), place_owner(order, 2 * pair + 1)
            both = jnp.concatenate(
                [flip[one * rows : one * rows + rows, begin:], flip[two * rows : two * rows + rows, begin:]],
                axis=0,
            ).astype(jnp.bfloat16)
            if slot == 2:
                hidden_te[pair * 2 * rows : (pair + 1) * 2 * rows] = both
            else:
                hidden_t[slot, pair * 2 * rows : (pair + 1) * 2 * rows] = both

    stage.need(*range(9, 17))
    go_on("start")

    def go_on_in_loop(name, pair):
        for point in range(width // block):
            if (name, point) in PLAN:
                pl.when(pair == point)(functools.partial(go_on, (name, point)))

    def pair_step(pair, carry):
        lanes = pl.ds(pl.multiple_of(pair * block, block), block)
        key_pair = keys[:, lanes]
        value_pair = values[:, lanes]
        key_feat = [key_pair * halves[h] + feat_k[...] * halves[1 - h] for h in range(2)]
        key_only = [key_pair * halves[h] for h in range(2)]
        value_only = [value_pair * halves[h] for h in range(2)]

        def row_step(index, inner):
            at = pl.ds(pl.multiple_of(index * tall, 16), tall)
            qw = qword[at, lanes]
            qe = qent[at, lanes]
            feats = feat_q[at]
            given = cgrad[at, lanes]
            stats = lse_delta[at]
            spot = lax.broadcasted_iota(jnp.int32, (1, block), 1) - 4 * pair
            total_w = jnp.zeros((tall, block), jnp.float32)
            total_e = jnp.zeros((tall, block), jnp.float32)
            for h in range(2):
                left_w = qw * halves[h] + feats * halves[1 - h]
                left_e = qe * halves[h] + feats * halves[1 - h]
                scores = jnp.concatenate(
                    [
                        dot_right_t(left_w, key_feat[h][:words]),
                        dot_right_t(left_e, key_feat[h][words:]),
                    ],
                    axis=1,
                )
                prob = jnp.exp(scores - jnp.sum(jnp.where(spot == h, stats, 0.0), axis=1, keepdims=True))
                pgrad = dot_right_t(given, value_only[h])
                sgrad = (prob * (pgrad - jnp.sum(jnp.where(spot == 2 + h, stats, 0.0), axis=1, keepdims=True))).astype(jnp.bfloat16)
                prob_s[h, at] = prob.astype(jnp.bfloat16)
                grad_s[h, at] = sgrad
                total_w += dot_plain(sgrad[:, :words], key_only[h][:words])
                total_e += dot_plain(sgrad[:, words:], key_only[h][words:])
            dqw[at, lanes] = total_w.astype(jnp.bfloat16)
            dqe[at, lanes] = total_e.astype(jnp.bfloat16)
            return inner

        lax.fori_loop(0, seq_len // tall, row_step, 0)
        go_on_in_loop("r", pair)
        qw_all, qe_all, given_all = qword[:, lanes], qent[:, lanes], cgrad[:, lanes]
        dkey[:words, lanes] = (
            dot_left_t(grad_s[0, :, :words], qw_all * halves[0])
            + dot_left_t(grad_s[1, :, :words], qw_all * halves[1])
        ).astype(jnp.bfloat16)
        dkey[words:, lanes] = (
            dot_left_t(grad_s[0, :, words:], qe_all * halves[0])
            + dot_left_t(grad_s[1, :, words:], qe_all * halves[1])
        ).astype(jnp.bfloat16)
        dvalue[:, lanes] = (
            dot_left_t(prob_s[0], given_all * halves[0])
            + dot_left_t(prob_s[1], given_all * halves[1])
        ).astype(jnp.bfloat16)

        go_on_in_loop("p", pair)
        return carry

    lax.fori_loop(0, width // block, pair_step, 0)

    query_scale = HD ** (-0.5)
    column = 384

    def weight_grad(source, slot, order_slot, grad, begin, end, scale):
        for cut in range(0, width, column):
            left = hidden_te[...] if order_slot == 2 else hidden_t[order_slot, :, begin:end]
            piece = dot_plain(left, grad[begin:end, cut : cut + column])
            if scale:
                piece = piece * query_scale
            source[slot, :, cut : cut + column] = piece.astype(jnp.bfloat16)

    weight_grad(late_source[0], 0, 1, dkey, 0, seq_len, False)
    streams[6].launch(0)
    weight_grad(late_source[1], 0, 1, dvalue, 0, seq_len, False)
    streams[7].launch(0)
    go_on("KV")
    weight_grad(late_source[2], 0, 2, dqw, words, seq_len, True)
    streams[8].launch(0)
    go_on("ew")
    weight_grad(late_source[3], 0, 1, dqe, words, seq_len, True)
    streams[9].launch(0)
    go_on("ee")
    weight_grad(late_source[4], 0, 0, dqw, 0, words, True)
    streams[10].launch(0)
    go_on("ww")

    stage.need(17, *range(22, 27))

    def data_grad(begin, size, queries):
        at = pl.ds(begin, size)
        return (
            first_grad[at]
            + query_scale * queries(at)
            + dot_right_t(dkey[at], w_key[...])
            + dot_right_t(dvalue[at], w_value[...])
        )

    def entity_queries(at):
        return dot_right_t(dqw[at], w_ew[...]) + dot_right_t(dqe[at], w_ee[...])

    def word_queries(at):
        total = 0.0
        for index, grad in enumerate((dqw, dqe)):
            rows_at = pl.ds(index * width, width)
            total += dot_right_t(grad[at, :split], spare[0][0, rows_at])
            total += dot_right_t(grad[at, split:], spare[1][0, rows_at])
        return total

    state_low = data_grad(words, seq_len - words, entity_queries).astype(jnp.bfloat16)
    vectors = jnp.concatenate(
        [dot_right_t(state_low, dense[...]).astype(jnp.bfloat16), (head_low[...].astype(jnp.float32) * -grad_scale).astype(jnp.bfloat16)], axis=0
    )
    entries = slot_row.shape[1]
    wanted = lax.broadcasted_iota(jnp.int32, (vectors.shape[0], entries), 0)
    placing = (wanted == slot_row[0:1]).astype(jnp.float32).astype(jnp.bfloat16)
    per_request = dot_left_t(placing, vectors).astype(jnp.bfloat16)
    request_send[...] = per_request.reshape(request_send.shape)

    def request_copy(step):
        peer = lax.rem(me + step, devices)
        return pltpu.make_async_remote_copy(
            src_ref=request_send.at[peer],
            dst_ref=request_out.at[me],
            send_sem=request_sems.at[0, step],
            recv_sem=request_sems.at[1, step],
            device_id=(peer,),
            device_id_type=MESH_ID,
        )

    def begin_request(step, carry):
        request_copy(step).start()
        return carry

    def finish_request(step, carry):
        request_copy(step).wait()
        return carry

    lax.fori_loop(1, devices, begin_request, 0)
    request_out[me] = request_send[me]
    entity_width = dense.shape[0]
    few = entity_width // owners
    for cut in range(0, entity_width, block):
        flip[cut : cut + block, :block] = entity_low[:, cut : cut + block].astype(jnp.float32).T
    for pair in range(owners // 2):
        one, two = place_owner(orders[0], 2 * pair), place_owner(orders[0], 2 * pair + 1)
        both = jnp.concatenate(
            [flip[one * few : one * few + few, :block], flip[two * few : two * few + few, :block]],
            axis=0,
        )
        entity_t[pair * 2 * few : (pair + 1) * 2 * few] = both.astype(jnp.bfloat16)
    late_source[6][0] = dot_plain(entity_t[...], state_low).astype(jnp.bfloat16)
    go_on("ent")
    weight_grad(late_source[5], 0, 0, dqe, 0, words, True)
    streams[11].launch(0)
    go_on("we")
    for copy in word_weights:
        copy.wait()

    def word_step(index, carry):
        begin = pl.multiple_of(index * taller, 16)
        words_out[pl.ds(begin, taller)] = data_grad(begin, taller, word_queries).astype(jnp.bfloat16)
        for point in range(words // taller):
            name = WORD_POINTS[point]
            if name in PLAN:
                pl.when(index == point)(functools.partial(go_on, name))
        return carry

    lax.fori_loop(0, words // taller, word_step, 0)
    go_on("end")
    lax.fori_loop(1, devices, finish_request, 0)


def in_order(grad, order):
    bits = len(order)
    owners = 2**bits
    view = grad.reshape((2,) * bits + (grad.shape[0] // owners, grad.shape[1]))
    spots = tuple(bits - mask.bit_length() for mask in order)
    return view.transpose(spots + (bits, bits + 1)).reshape(grad.shape)


def attention_back(early_grads, inputs, weights, grad_scale, collective_id):
    devices = lax.axis_size("dp")
    orders = stage_masks(devices)
    stages = len(orders[0])
    hidden = inputs[0]
    seq_len, width = hidden.shape
    slots = weights[-1].shape[0]
    words = seq_len - slots
    outs = [
        jax.ShapeDtypeStruct((count, rows, wide), jnp.float32)
        for _, count, rows, wide in EARLY + LATE
    ] + [
        jax.ShapeDtypeStruct((words, width), jnp.bfloat16),
        jax.ShapeDtypeStruct(
            (devices, inputs[11].shape[1] // devices, weights[-2].shape[0]), jnp.bfloat16
        ),
    ]
    scratch = []
    for spec in EARLY:
        scratch += piece_scratch(spec, stages, False, True)
    for spec in LATE:
        scratch += piece_scratch(spec, stages, True, False)
    scratch += [pltpu.VMEM((seq_len, width), jnp.bfloat16)] * 4
    scratch += [pltpu.VMEM((2, seq_len, seq_len), jnp.bfloat16)] * 2
    scratch += [
        pltpu.VMEM((width, seq_len), jnp.float32),
        pltpu.VMEM((2, width, seq_len), jnp.bfloat16),
        pltpu.VMEM((width, slots), jnp.bfloat16),
        pltpu.VMEM((weights[-2].shape[0], slots), jnp.bfloat16),
        pltpu.VMEM((devices, inputs[11].shape[1] // devices, weights[-2].shape[0]), jnp.bfloat16),
        pltpu.SemaphoreType.DMA((2, devices)),
        pltpu.SemaphoreType.DMA((len(EARLY) + 4,)),
    ]
    vmem = pl.BlockSpec(memory_space=pltpu.VMEM)
    return staged_call(
        functools.partial(attention_back_kernel, orders, grad_scale),
        [*early_grads, *inputs, *weights],
        outs,
        [pl.BlockSpec(memory_space=pltpu.HBM)] * len(EARLY)
        + [vmem] * len(inputs)
        + [pl.BlockSpec(memory_space=pltpu.HBM)] * 2
        + [vmem] * (len(weights) - 2),
        [vmem] * len(outs),
        (8, 11, 12, 9, 10, 13, 14, 15, 16, 17, 22, 23, 24, 25, 26),
        (),
        scratch,
        pltpu.CompilerParams(
            collective_id=collective_id, has_side_effects=True, vmem_limit_bytes=63 * 2**20
        ),
    )


def fused_body(
    word_states,
    word_segments,
    entity_segments,
    request_rows,
    request_slot,
    mask_slots,
    entity_table,
    vocab_bias,
    entity_dense,
    query_ww,
    query_we,
    query_ew,
    query_ee,
    key_weight,
    value_weight,
    out_weight,
    norm1_gain,
    norm1_bias,
    up_weight,
    down_weight,
    norm2_gain,
    norm2_bias,
    head_weight,
    head_gain,
    head_bias,
    cotangent,
):
    devices = lax.axis_size("dp")
    low = jnp.bfloat16
    slot_count = entity_segments.shape[1]
    mask_count = mask_slots.shape[1]
    grad_scale = 1.0 / (mask_count * devices)
    orders = stage_masks(devices)
    bias_row = vocab_bias.astype(jnp.float32)
    (
        entity_low,
        target_vecs,
        target_bias,
        code_row,
        word_q,
        word_e,
        word_k,
        word_v,
        feat_q,
        feat_k,
        choose,
        slot_row,
    ) = lookup(
        [
            request_rows.T,
            entity_table,
            bias_row,
            request_slot.T,
            word_states,
            query_ww,
            query_we,
            key_weight,
            value_weight,
            word_segments,
            entity_segments,
            mask_slots,
        ],
        slot_count,
        mask_count,
        0,
    )
    (
        hidden_low,
        query_word,
        query_entity,
        key_rows,
        values,
        context_low,
        lse_lanes,
        residual_one,
        normed_low,
        activated,
        gelu_slope,
        residual_two,
        layer_low,
        picked_low,
        head_pre,
        head_low,
    ) = forward_pass(
        [
            word_states,
            entity_low,
            feat_q,
            feat_k,
            choose,
            entity_dense,
            word_q,
            word_e,
            word_k,
            word_v,
            query_ew,
            query_ee,
            key_weight,
            value_weight,
            out_weight,
            norm1_gain,
            norm1_bias,
            up_weight,
            down_weight,
            norm2_gain,
            norm2_bias,
            head_weight,
            head_gain,
            head_bias,
        ]
    )
    table_grad, bias_grad, losses, total_loss, head_grad = head_and_table(
        head_low,
        entity_table,
        bias_row,
        target_vecs,
        target_bias,
        grad_scale,
        1,
    )
    (
        up_a,
        up_b,
        head_a,
        out_b,
        down_b,
        up_c,
        down_c,
        first_grad,
        context_grad,
        lse_delta,
        vectors,
    ) = middle_back(
        [
            head_grad,
            target_vecs,
            head_pre,
            head_gain,
            picked_low,
            head_weight,
            choose,
            cotangent,
            residual_two,
            norm2_gain,
            normed_low,
            residual_one,
            norm1_gain,
            out_weight,
            context_low,
            lse_lanes,
            activated,
            gelu_slope,
            up_weight,
            down_weight,
        ],
        orders,
        grad_scale,
    )
    *sums, words_grad, back_rows = attention_back(
        [up_a, down_b, up_c, down_c, up_b, head_a, vectors, out_b],
        [
            hidden_low,
            query_word,
            query_entity,
            key_rows,
            values,
            context_grad,
            feat_q,
            feat_k,
            lse_delta,
            first_grad,
            head_low,
            slot_row,
        ],
        [
            query_ww,
            query_we,
            query_ew,
            query_ee,
            key_weight,
            value_weight,
            entity_dense,
            entity_low,
        ],
        grad_scale,
        2,
    )
    (
        table_grad,
        bias_grad,
        up_sum,
        down_sum,
        head_sum,
        out_sum,
        key_sum,
        value_sum,
        ew_sum,
        ee_sum,
        ww_sum,
        we_sum,
        dense_sum,
        *vector_out,
    ) = last_step(
        code_row,
        back_rows.reshape(-1, back_rows.shape[2]),
        table_grad,
        bias_grad,
        sums,
        (head_gain.shape[0] // devices, norm1_gain.shape[0] // devices),
        grad_scale,
    )
    return (
        total_loss[0, 0],
        layer_low,
        words_grad,
        table_grad,
        bias_grad,
        dense_sum,
        ww_sum,
        we_sum,
        ew_sum,
        ee_sum,
        key_sum,
        value_sum,
        out_sum,
        vector_out[4],
        vector_out[5],
        up_sum,
        down_sum,
        vector_out[2],
        vector_out[3],
        head_sum,
        vector_out[0],
        vector_out[1],
        losses,
    )


def solution(mesh):
    in_specs = (
        P("dp", None),
        P("dp", None),
        P("dp", None),
        P("dp", None),
        P("dp", None),
        P("dp", None),
        P("dp", None),
        P("dp"),
        P(),
        P(),
        P(),
        P(),
        P(),
        P(),
        P(),
        P(),
        P(),
        P(),
        P(),
        P(),
        P(),
        P(),
        P(),
        P(),
        P(),
        P("dp", None),
    )
    out_specs = (
        P(),
        P("dp", None),
        P("dp", None),
        P("dp", None),
        P("dp"),
        P("dp", None),
        P("dp", None),
        P("dp", None),
        P("dp", None),
        P("dp", None),
        P("dp", None),
        P("dp", None),
        P("dp", None),
        P("dp"),
        P("dp"),
        P("dp", None),
        P("dp", None),
        P("dp"),
        P("dp"),
        P("dp", None),
        P("dp"),
        P("dp"),
        P("dp"),
    )
    chosen = fused_body if mesh.shape["dp"] == 32 else body
    return jax.shard_map(chosen, mesh=mesh, in_specs=in_specs, out_specs=out_specs, check_vma=False)
```
